32 devices in a mesh: pipe: 2 (over y), ctx: 4 (over x, core), tp: 4 (over z).
Axes of the slice: x: 2, y: 2, z: 4, core: 2. Of those that a mesh axis runs over, the one named last changes fastest.
Arguments:
- block_input: bfloat16 [3, 1024, 2048], P(None, ('ctx', 'tp')), may hold values from -6 to 6
- out_grad: bfloat16 [3, 1024, 2048], P(None, ('ctx', 'tp')), may hold values from -6 to 6
- triple_weight: bfloat16 [2, 2048, 8, 3, 256], P('pipe', 'ctx', 'tp'), may hold values from -0.125 to 0.125
- output_weight: bfloat16 [2, 8, 256, 2048], P('pipe', 'tp', None, 'ctx'), may hold values from -0.75 to 0.75
- expand_weight: bfloat16 [2, 2048, 8192], P('pipe', 'ctx', 'tp'), may hold values from -0.125 to 0.125
- contract_weight: bfloat16 [2, 8192, 2048], P('pipe', 'tp', 'ctx'), may hold values from -0.0625 to 0.0625
- norm_gains: bfloat16 [2, 2, 2048], P('pipe', None, 'ctx'), may hold values from 0.5 to 1.5
- norm_biases: bfloat16 [2, 2, 2048], P('pipe', None, 'ctx'), may hold values from -3 to 3
Outputs:
- layer_outputs: bfloat16 [2, 3, 1024, 2048], P('pipe', None, ('ctx', 'tp'))
- entry_grads: bfloat16 [2, 3, 1024, 2048], P('pipe', None, ('ctx', 'tp'))
- triple_grads: float32 [2, 2048, 8, 3, 256], P('pipe', 'ctx', 'tp')
- output_grads: float32 [2, 8, 256, 2048], P('pipe', 'tp', None, 'ctx')
- expand_grads: float32 [2, 2048, 8192], P('pipe', 'ctx', 'tp')
- contract_grads: float32 [2, 8192, 2048], P('pipe', 'tp', 'ctx')
- gain_grads: float32 [2, 2, 2048], P('pipe', None, 'ctx')
- bias_grads: float32 [2, 2, 2048], P('pipe', None, 'ctx')
The draws below stay inside these ranges and needn't reach their ends.
All inputs are finite; a program needn't handle non-finite values.
Results may differ from the reference program's by a relative error of at most 0.029.
Values may be sent and summed in bfloat16 or wider, within the bound.
No kernel may reach another device: no remote copies, remote signals or barrier semaphores. Data moves between devices by JAX's collectives and lax.ppermute only.
A program may use at most 320 MiB of HBM per device.

```python
import jax
import jax.numpy as jnp
from jax import lax

D = 2048
H = 8
HD = 256
FF = 8192
ROT = 64
MICRO = 3
SEQ = 1024


def steps_of(own_key, dims, split, least, high):
    level, own = 1.0, jax.random.fold_in(own_key, 6)
    for axis_at, blocks in split:
        draws = jnp.exp(jax.random.uniform(jax.random.fold_in(own, axis_at), (blocks,), jnp.float32, least / len(split), high / len(split)))
        level = level * jnp.repeat(draws, dims[axis_at] // blocks).reshape([-1 if axis == axis_at else 1 for axis in range(len(dims))])
    return level


def noise(key, shape, scale, most, cuts=(), held_as=jnp.bfloat16):
    loudness = steps_of(key, shape, cuts, -0.22, 0.18) if cuts else 1.0
    drawn = jax.random.normal(key, shape, jnp.float32) * scale * loudness
    return jnp.minimum(jnp.maximum(drawn, -most), most).astype(held_as)


def setup_inputs(seed: int = 0) -> dict:
    keys = jax.random.split(jax.random.key(seed), 9)
    return {
        "block_input": noise(keys[0], (MICRO, SEQ, D), 1.0, 6.0, ((1, 16),)),
        "out_grad": noise(keys[1], (MICRO, SEQ, D), 1.0, 6.0, ((1, 16),)),
        "triple_weight": noise(keys[2], (2, D, H, 3, HD), D ** -0.5, 0.125, ((0, 2), (1, 4), (2, 4))),
        "output_weight": noise(keys[3], (2, H, HD, D), (H * HD // 32) ** -0.5, 0.75, ((0, 2), (1, 4), (3, 4))),
        "expand_weight": noise(keys[4], (2, D, FF), D ** -0.5, 0.125, ((0, 2), (1, 4), (2, 4))),
        "contract_weight": noise(keys[5], (2, FF, D), FF ** -0.5, 0.0625, ((0, 2), (1, 4), (2, 4))),
        "norm_gains": jnp.clip(1.0 + 0.1 * jax.random.normal(keys[6], (2, 2, D), jnp.float32), 0.5, 1.5).astype(jnp.bfloat16),
        "norm_biases": noise(keys[7], (2, 2, D), 0.3, 3.0, ((0, 2), (2, 4))),
    }


@jax.custom_vjp
def low(v):
    return lax.optimization_barrier(v.astype(jnp.bfloat16)).astype(jnp.float32)

@jax.custom_vjp
def low_back(v):
    return v

def low_keep(v):
    return (low(v), None)

def low_pass(kept, grad):
    return (grad,)

def back_keep(v):
    return (v, None)

def back_low(kept, grad):
    return (low(grad),)
low.defvjp(low_keep, low_pass)
low_back.defvjp(back_keep, back_low)
highest = lax.Precision.HIGHEST
epsilon = 1e-05

def layer_norm(values, gain_row, shift_bias):
    center = values - lax.optimization_barrier(jnp.mean(values, axis=-1, keepdims=True))
    spread = lax.optimization_barrier(jnp.mean(center * center, axis=-1, keepdims=True))
    return center * lax.rsqrt(spread + epsilon) * gain_row + shift_bias

def rotate(values, cosine, sine_table):
    half_rot = ROT // 2
    first_part = values[..., :half_rot]
    second_part = values[..., half_rot:ROT]
    return jnp.concatenate([first_part * cosine - second_part * sine_table, second_part * cosine + first_part * sine_table, values[..., ROT:]], axis=-1)

def attention(query_rows, key_part, value_part):
    block_rows = min(512, SEQ)
    score_scale = HD ** (-0.5)
    key_pos = jnp.arange(SEQ, dtype=jnp.int32)

    def one_block(row_start):
        block_query = lax.dynamic_slice_in_dim(query_rows, row_start, block_rows, 0)
        scores = low_back(jnp.einsum('qhe,khe->hqk', block_query, key_part, precision=highest) * score_scale)
        query_pos = row_start + jnp.arange(block_rows, dtype=jnp.int32)
        allowed = key_pos[None, :] <= query_pos[:, None]
        scores = jnp.where(allowed[None], scores, -1e+30)
        probs = jax.nn.softmax(scores, axis=-1)
        return jnp.einsum('hqk,khe->qhe', low(probs), value_part, precision=highest)
    starts = jnp.arange(0, SEQ, block_rows, dtype=jnp.int32)
    pieces = lax.map(jax.checkpoint(one_block), starts)
    return pieces.reshape(SEQ, H, HD)

def block_layer(inputs, layer_weights, cosine, sine_table):
    triple, output_w, expand, contract, gain_rows, biases = layer_weights
    first_norm = low(layer_norm(inputs, gain_rows[0], biases[0]))
    second_norm = low(layer_norm(inputs, gain_rows[1], biases[1]))
    projected = jnp.einsum('td,dhce->thce', first_norm, triple, precision=highest)
    query_rows = low(rotate(low_back(projected[:, :, 0]), cosine, sine_table))
    key_part = low(rotate(low_back(projected[:, :, 1]), cosine, sine_table))
    value_part = low(low_back(projected[:, :, 2]))
    attended = low_back(low(attention(query_rows, key_part, value_part)))
    attn_branch = jnp.einsum('the,hed->td', attended, output_w, precision=highest)
    hidden_pre = low_back(jnp.dot(second_norm, expand, precision=highest))
    activated = low(jax.nn.gelu(hidden_pre, approximate=False))
    mlp_branch = jnp.dot(activated, contract, precision=highest)
    return inputs + attn_branch + mlp_branch

def reference(block_input, out_grad, triple_weight, output_weight, expand_weight, contract_weight, norm_gains, norm_biases):
    positions = jnp.arange(SEQ, dtype=jnp.float32)
    frequency = 10000.0 ** (-jnp.arange(0, ROT, 2, dtype=jnp.float32) / ROT)
    angles = positions[:, None] * frequency[None, :]
    cosine = jnp.cos(angles)[:, None, :]
    sine_table = jnp.sin(angles)[:, None, :]
    inputs = block_input.astype(jnp.float32)
    relay_zero = jnp.zeros_like(inputs)
    weights = tuple((weight_piece.astype(jnp.float32) for weight_piece in (triple_weight, output_weight, expand_weight, contract_weight, norm_gains, norm_biases)))

    def forward(inputs, relay_zero, weights):

        def one_micro(scan_carry, micro_pair):
            start_in, relay_in = micro_pair
            first_in = low_back(start_in)
            first_out = block_layer(first_in, [weight_piece[0] for weight_piece in weights], cosine, sine_table)
            second_in = low_back(low(first_out) + relay_in)
            second_out = block_layer(second_in, [weight_piece[1] for weight_piece in weights], cosine, sine_table)
            return (scan_carry, (second_out, low(first_out), low(second_out)))
        scan_carry, (final_out, first_low, second_low) = lax.scan(one_micro, jnp.zeros((), jnp.float32), (inputs, relay_zero))
        return (final_out, (first_low, second_low))
    final_out, pullback, (first_low, second_low) = jax.vjp(forward, inputs, relay_zero, weights, has_aux=True)
    grad_inputs, grad_relay, grad_weights = pullback(out_grad.astype(jnp.float32))
    layer_outputs = jnp.stack([first_low, second_low]).astype(jnp.bfloat16)
    entry_grads = jnp.stack([grad_inputs, grad_relay]).astype(jnp.bfloat16)
    return (layer_outputs, entry_grads, grad_weights[0], grad_weights[1], grad_weights[2], grad_weights[3], grad_weights[4], grad_weights[5])
```

```python
import jax
import jax.numpy as jnp
from jax import lax
from jax.sharding import PartitionSpec as P

ROT = 64
epsilon = 1e-05
masked_score = -1e30
f32 = jnp.float32
bf16 = jnp.bfloat16


def dot(a, b, dims):
    return lax.dot_general(a, b, (dims, ((), ())), preferred_element_type=f32)


def xor_blocks(values, index, count):
    width = values.shape[-1] // count
    step = 1
    while step < count:
        order = [k ^ step for k in range(count)]
        swapped = jnp.concatenate([values[..., k * width : (k + 1) * width] for k in order], axis=-1)
        values = jnp.where((index & step) != 0, swapped, values)
        step *= 2
    return values


def rope_tables(positions):
    frequency = 10000.0 ** (-jnp.arange(0, ROT, 2, dtype=f32) / ROT)
    angles = positions.astype(f32)[:, None] * frequency[None, :]
    return (jnp.cos(angles)[:, None, :], jnp.sin(angles)[:, None, :])


def rotate(values, cosine, sine_table):
    half = cosine.shape[-1]
    first = values[..., :half]
    second = values[..., half : 2 * half]
    return jnp.concatenate(
        [
            first * cosine - second * sine_table,
            second * cosine + first * sine_table,
            values[..., 2 * half :],
        ],
        axis=-1,
    )


def normalize(values):
    center = values - jnp.mean(values, axis=-1, keepdims=True)
    inverse = lax.rsqrt(jnp.mean(center * center, axis=-1, keepdims=True) + epsilon)
    return (center * inverse, inverse)


def gelu_slope(pre):
    return (
        0.5 * (1.0 + lax.erf(pre * 0.7071067811865476))
        + pre * jnp.exp(-0.5 * pre * pre) * 0.3989422804014327
    )


def shards(
    block_input,
    out_grad,
    triple_weight,
    output_weight,
    expand_weight,
    contract_weight,
    norm_gains,
    norm_biases,
):
    section = lax.axis_index("pipe")
    span = lax.axis_index("ctx")
    lane = lax.axis_index("tp")
    spans = lax.axis_size("ctx")
    lanes = lax.axis_size("tp")
    micros, rows, width = block_input.shape
    span_rows = rows * lanes
    heads = triple_weight.shape[2]
    head_dim = triple_weight.shape[4]
    scale = head_dim ** (-0.5)
    first_section = section == 0

    def over_ctx(array, j):
        return lax.ppermute(array, "ctx", [(a, a ^ j) for a in range(spans)])

    def over_tp(array, j, sections):
        pairs = [(s * lanes + a, s * lanes + (a ^ j)) for s in sections for a in range(lanes)]
        return lax.ppermute(array, ("pipe", "tp"), pairs)

    def across(array, j, source):
        pairs = [(source * lanes + a, (1 - source) * lanes + (a ^ j)) for a in range(lanes)]
        return lax.ppermute(array, ("pipe", "tp"), pairs)

    def gather_ctx(array):
        held = {0: array}
        step = spans // 2
        while step:
            for k in list(held):
                held[k ^ step] = over_ctx(held[k], step)
            step //= 2
        return [held[k] for k in range(spans)]

    def gather_tp(array, axis, sections):
        return jnp.concatenate(
            [array] + [over_tp(array, j, sections) for j in range(1, lanes)], axis=axis
        )

    def swap_slices(array):
        size = width // spans
        return [array[..., :size]] + [
            over_ctx(array[..., j * size : (j + 1) * size], j) for j in range(1, spans)
        ]

    small = jnp.concatenate([norm_gains[0], norm_biases[0]], axis=0)
    small_full = jnp.concatenate(gather_ctx(small), axis=1).astype(f32)
    gains, biases = small_full[:2], small_full[2:]
    own_triple = triple_weight[0].reshape(width // spans, heads * 3 * head_dim)
    own_output = output_weight[0].reshape(heads * head_dim, width // spans)
    own_expand = expand_weight[0]
    own_contract = contract_weight[0]
    inputs = xor_blocks(block_input, span, spans)
    cotangent = xor_blocks(out_grad, span, spans)
    early = jnp.where(first_section, inputs, cotangent)
    early_rows = gather_tp(early, 1, (0, 1))
    triple = jnp.concatenate(gather_ctx(own_triple), axis=0)
    output = jnp.concatenate(gather_ctx(own_output), axis=1)
    expand = jnp.concatenate(gather_ctx(own_expand), axis=0)
    contract = jnp.concatenate(gather_ctx(own_contract), axis=1)

    in_row = jnp.arange(rows, dtype=jnp.int32)
    in_span = jnp.concatenate([(lane ^ j) * rows + in_row for j in range(lanes)])
    positions = span * span_rows + in_span
    key_positions = jnp.concatenate([(span ^ k) * span_rows + in_span for k in range(spans)])
    allowed = key_positions[None, :] <= positions[:, None]
    cosine, sine_table = rope_tables(positions)

    def forward(row_block):
        count = row_block.shape[0]
        normalized, _ = normalize(row_block.astype(f32))
        first = (normalized * gains[0] + biases[0]).astype(bf16).reshape(-1, width)
        second = (normalized * gains[1] + biases[1]).astype(bf16).reshape(-1, width)
        projected = dot(first, triple, ((1,), (0,))).reshape(
            count, span_rows, heads, 3, head_dim
        )
        queries = rotate(projected[:, :, :, 0], cosine, sine_table).astype(bf16)
        keys = rotate(projected[:, :, :, 1], cosine, sine_table).astype(bf16)
        values = projected[:, :, :, 2].astype(bf16)
        pairs = gather_ctx(jnp.stack([keys, values]))
        key_all = jnp.concatenate([pair[0] for pair in pairs], axis=1)
        value_all = jnp.concatenate([pair[1] for pair in pairs], axis=1)
        hidden_pre = dot(second, expand, ((1,), (0,)))
        activated = jax.nn.gelu(hidden_pre, approximate=False).astype(bf16)
        scores = (
            jnp.einsum("mqhe,mkhe->mhqk", queries, key_all, preferred_element_type=f32) * scale
        )
        scores = jnp.where(allowed, scores, masked_score)
        probs = jax.nn.softmax(scores, axis=-1)
        attended = jnp.einsum(
            "mhqk,mkhe->mqhe", probs.astype(bf16), value_all, preferred_element_type=f32
        ).astype(bf16)
        branch = dot(activated, contract, ((1,), (0,))) + dot(
            attended.reshape(-1, heads * head_dim), output, ((1,), (0,))
        )
        kept = dict(
            queries=queries,
            keys=key_all,
            values=value_all,
            probs=probs,
            attended=attended,
            hidden_pre=hidden_pre.reshape(count, span_rows, -1),
            activated=activated.reshape(count, span_rows, -1),
            normalized=normalized.astype(bf16),
        )
        return branch.astype(bf16).reshape(count, span_rows, width), kept

    def backward(upstream, kept):
        queries, keys, values = kept["queries"], kept["keys"], kept["values"]
        probs, attended = kept["probs"], kept["attended"]
        grad_attended = (
            dot(upstream, output, ((1,), (1,)))
            .astype(bf16)
            .reshape(span_rows, heads, head_dim)
        )
        delta = jnp.einsum("qhe,qhe->hq", grad_attended.astype(f32), attended.astype(f32))
        grad_probs = jnp.einsum(
            "qhe,khe->hqk", grad_attended, values, preferred_element_type=f32
        )
        grad_scores = (probs * (grad_probs - delta[..., None])).astype(bf16)
        grad_query = (
            jnp.einsum("hqk,khe->qhe", grad_scores, keys, preferred_element_type=f32) * scale
        )
        grad_keys = (
            jnp.einsum("hqk,qhe->khe", grad_scores, queries, preferred_element_type=f32) * scale
        )
        grad_values = jnp.einsum(
            "hqk,qhe->khe", probs.astype(bf16), grad_attended, preferred_element_type=f32
        )
        pair = jnp.stack([grad_keys.astype(bf16), grad_values.astype(bf16)])
        held = {
            k: pair[:, k * span_rows : (k + 1) * span_rows] for k in range(spans)
        }
        step = 1
        while step < spans:
            going = [k for k in held if k & step]
            came = over_ctx(jnp.stack([held[k] for k in going]), step)
            held = {
                k ^ step: (held[k ^ step].astype(f32) + came[at].astype(f32)).astype(
                    bf16 if 2 * step < spans else f32
                )
                for at, k in enumerate(going)
            }
            step *= 2
        own_pair = held[0].astype(f32)
        grad_hidden = (
            dot(upstream, contract, ((1,), (1,))) * gelu_slope(kept["hidden_pre"])
        ).astype(bf16)
        grad_second = dot(grad_hidden, expand, ((1,), (1,)))
        grad_projected = (
            jnp.stack(
                [
                    rotate(grad_query, cosine, -sine_table),
                    rotate(own_pair[0], cosine, -sine_table),
                    own_pair[1],
                ],
                axis=2,
            )
            .astype(bf16)
            .reshape(span_rows, heads * 3 * head_dim)
        )
        grad_first = dot(grad_projected, triple, ((1,), (1,)))
        combined = (grad_first * gains[0] + grad_second * gains[1]).astype(bf16)
        return combined, grad_hidden, grad_projected

    def block(array, j):
        return array[j * rows : (j + 1) * rows]

    def norm_back(upstream, combined, entering):
        normalized, inverse = normalize(entering.astype(f32))
        return (
            upstream.astype(f32)
            + inverse
            * (
                combined
                - jnp.mean(combined, axis=-1, keepdims=True)
                - normalized * jnp.mean(combined * normalized, axis=-1, keepdims=True)
            )
        ).astype(bf16)

    def one(kept, m):
        return {name: array[m] for name, array in kept.items()}

    parts, kept_first = forward(early_rows)
    middle, middle_rows, middle_back = [], [], []
    for m in range(micros):
        total = inputs[m].astype(f32)
        for j in range(lanes):
            total = total + across(block(parts[m], j), j, 0).astype(f32)
        middle.append(total.astype(bf16))
        middle_rows.append(gather_tp(middle[m], 0, (1,)))
        middle_back.append(lax.ppermute(middle[m], "pipe", [(1, 0)]))

    kept_second, finals = [], []
    for m in range(micros):
        parts, kept = forward(middle_rows[m][None])
        total = middle[m].astype(f32) + block(parts[0], 0).astype(f32)
        for j in range(1, lanes):
            total = total + over_tp(block(parts[0], j), j, (1,)).astype(f32)
        finals.append(total.astype(bf16))
        kept_second.append(one(kept, 0))
    layer_outputs = jnp.where(first_section, jnp.stack(middle_back), jnp.stack(finals))

    relay, relay_rows, relay_back, grads_second = [], [], [], []
    for m in range(micros):
        combined, grad_hidden, grad_projected = backward(early_rows[m], kept_second[m])
        grads_second.append((grad_hidden, grad_projected))
        total = jnp.zeros((rows, width), f32)
        for j in range(lanes):
            total = total + across(block(combined, j), j, 1).astype(f32)
        relay.append(norm_back(cotangent[m], total, middle_back[m]))
        relay_rows.append(gather_tp(relay[m], 0, (0,)))
        relay_back.append(lax.ppermute(relay[m], "pipe", [(0, 1)]))

    entries, hidden_sides, projected_sides, upstream_sides = [], [], [], []
    normal_sides, active_sides, attended_sides = [], [], []
    for m in range(micros):
        kept = one(kept_first, m)
        other = kept_second[m]

        def chosen(name):
            return jnp.where(first_section, kept[name], other[name])

        normal_sides.append(swap_slices(chosen("normalized")))
        active_sides.append(gather_ctx(chosen("activated")))
        attended_sides.append(
            gather_ctx(chosen("attended").reshape(span_rows, heads * head_dim))
        )
        upstream_sides.append(
            swap_slices(jnp.where(first_section, relay_rows[m], early_rows[m]))
        )
        combined, grad_hidden, grad_projected = backward(relay_rows[m], kept)
        hidden_sides.append(
            gather_ctx(jnp.where(first_section, grad_hidden, grads_second[m][0]))
        )
        projected_sides.append(
            gather_ctx(jnp.where(first_section, grad_projected, grads_second[m][1]))
        )
        total = block(combined, 0).astype(f32)
        for j in range(1, lanes):
            total = total + over_tp(block(combined, j), j, (0,)).astype(f32)
        entries.append(norm_back(relay[m], total, inputs[m]))
    entry_grads = jnp.where(first_section, jnp.stack(entries), jnp.stack(relay_back))

    def joined(sides):
        return jnp.concatenate([piece for side in sides for piece in side], axis=0)

    normal = joined(normal_sides)
    upstream = joined(upstream_sides)
    tokens = ((0,), (0,))
    contract_grads = dot(joined(active_sides), upstream, tokens)
    output_grads = dot(joined(attended_sides), upstream, tokens)
    own_gains = norm_gains[0].astype(f32)[:, :, None]
    own_biases = norm_biases[0].astype(f32)[:, :, None]

    def normed_grads(c, sides, weight):
        grads = joined(sides)
        product = dot(normal, grads, tokens)
        column = jnp.sum(grads.astype(f32), axis=0)
        weight_grad = own_gains[c] * product + own_biases[c] * column
        wide = weight.astype(f32)
        return weight_grad, jnp.sum(wide * product, axis=1), jnp.sum(wide * column, axis=1)

    expand_grads, gain_second, bias_second = normed_grads(1, hidden_sides, own_expand)
    triple_grads, gain_first, bias_first = normed_grads(0, projected_sides, own_triple)
    side = jnp.stack([gain_first, gain_second, bias_first, bias_second])
    side_total = side
    for j in range(1, lanes):
        side_total = side_total + over_tp(side, j, (0, 1))
    return (
        xor_blocks(layer_outputs, span, spans)[None],
        xor_blocks(entry_grads, span, spans)[None],
        triple_grads.reshape(triple_weight.shape),
        output_grads.reshape(output_weight.shape),
        expand_grads[None],
        contract_grads[None],
        side_total[:2][None],
        side_total[2:][None],
    )


def solution(mesh):
    return jax.shard_map(
        shards,
        mesh=mesh,
        in_specs=(
            P(None, ("ctx", "tp"), None),
            P(None, ("ctx", "tp"), None),
            P("pipe", "ctx", "tp", None, None),
            P("pipe", "tp", None, "ctx"),
            P("pipe", "ctx", "tp"),
            P("pipe", "tp", "ctx"),
            P("pipe", None, "ctx"),
            P("pipe", None, "ctx"),
        ),
        out_specs=(
            P("pipe", None, ("ctx", "tp"), None),
            P("pipe", None, ("ctx", "tp"), None),
            P("pipe", "ctx", "tp", None, None),
            P("pipe", "tp", None, "ctx"),
            P("pipe", "ctx", "tp"),
            P("pipe", "tp", "ctx"),
            P("pipe", None, "ctx"),
            P("pipe", None, "ctx"),
        ),
        check_vma=False,
    )
```

```python
import functools

import jax
import jax.numpy as jnp
from jax import lax
from jax.experimental import pallas as pl
from jax.experimental.pallas import tpu as pltpu
from jax.sharding import PartitionSpec as P

ROT = 64
LANES = 128
epsilon = 1e-05
masked_score = -1e30
f32 = jnp.float32
bf16 = jnp.bfloat16
vmem_bytes = 56 * 1024 * 1024
half_root = 0.7071067811865476
bell = 0.3989422804014327


def dot(a, b, dims):
    return lax.dot_general(a, b, (dims, ((), ())), preferred_element_type=f32)


def plain(a, b):
    return dot(a, b, ((1,), (0,)))


def turned(a, b):
    return dot(a, b, ((1,), (1,)))


def doubling(count):
    order, step = [0], count // 2
    while step:
        order += [k ^ step for k in order]
        step //= 2
    return order


def xor_blocks(values, index, count, inverse=False):
    width = values.shape[-1] // count
    order = doubling(count)

    def taken(places):
        return jnp.concatenate(
            [values[..., k * width : (k + 1) * width] for k in places], axis=-1
        )

    if inverse:
        values = taken([order.index(k) for k in range(count)])
    step = 1
    while step < count:
        swapped = taken([k ^ step for k in range(count)])
        values = jnp.where((index & step) != 0, swapped, values)
        step *= 2
    return values if inverse else taken(order)


def rope_tables(positions):
    half = ROT // 2
    frequency = 10000.0 ** (-jnp.arange(0, ROT, 2, dtype=f32) / ROT)
    angles = positions.astype(f32)[:, None] * frequency[None, :]
    cosine, sine = jnp.cos(angles), jnp.sin(angles)
    count = positions.shape[0]
    rest = jnp.zeros((count, LANES - ROT), f32)
    none = jnp.zeros((count, half), f32)
    return jnp.stack(
        [
            jnp.concatenate([cosine, cosine, rest + 1.0], axis=1),
            jnp.concatenate([-sine, none, rest], axis=1),
            jnp.concatenate([none, sine, rest], axis=1),
        ]
    )


def turn(values, tables, sign):
    half = ROT // 2
    part = values[:, :LANES]
    moved = (
        pltpu.roll(part, LANES - half, 1) * tables[1] + pltpu.roll(part, half, 1) * tables[2]
    )
    part = part * tables[0] + (moved if sign > 0 else -moved)
    return jnp.concatenate([part, values[:, LANES:]], axis=1)


def normalize(values):
    center = values - jnp.mean(values, axis=-1, keepdims=True)
    inverse = lax.rsqrt(jnp.mean(center * center, axis=-1, keepdims=True) + epsilon)
    return (center * inverse, inverse)


def whole(array):
    zeros = (0,) * array.ndim
    return pl.BlockSpec(array.shape, lambda *_: zeros)


def at(block, place):
    return pl.BlockSpec(block, lambda *_: place)


kept_out = pl.BlockSpec(memory_space=pl.ANY)


def shape(dims, dtype=bf16):
    return jax.ShapeDtypeStruct(dims, dtype)


def run(kernel, ins, outs, scratch, flops, moved, name, grid=(1,)):
    arrays = [array for array, _ in ins]
    return pl.pallas_call(
        kernel,
        grid=grid,
        in_specs=[spec for _, spec in ins],
        out_specs=[spec for _, spec in outs],
        out_shape=[struct for struct, _ in outs],
        scratch_shapes=scratch,
        compiler_params=pltpu.CompilerParams(vmem_limit_bytes=vmem_bytes),
        cost_estimate=pl.CostEstimate(
            flops=int(flops), bytes_accessed=int(moved), transcendentals=0
        ),
        name=name,
    )(*arrays)


def full_out(dims, dtype=bf16):
    zeros = (0,) * len(dims)
    return (shape(dims, dtype), pl.BlockSpec(dims, lambda *_: zeros))


def copies(sources, targets, sems):
    started = []
    for source, target, sem in zip(sources, targets, sems):
        copy = pltpu.make_async_copy(source, target, sem)
        copy.start()
        started.append(copy)
    return started


def project(pieces, gains, biases, tables, weights, head_dim):
    count, _, width = pieces[0].shape
    span_rows = sum(piece.shape[1] for piece in pieces)
    rows = count * span_rows
    chunk = pieces[0].shape[1]
    depth, columns = weights[0].shape
    spans = len(weights)
    heads = columns // (3 * head_dim)
    wide = 3 * head_dim

    def kernel(*refs):
        piece_refs = refs[: len(pieces)]
        gain_ref, bias_ref, table_ref = refs[len(pieces) : len(pieces) + 3]
        weight_refs = refs[len(pieces) + 3 : len(pieces) + 3 + spans]
        first, second, normal, queries, pair, held, sems = refs[len(pieces) + 3 + spans :]
        started = []
        for h in range(heads):
            started.append(
                copies(
                    [w.at[:, h * wide : (h + 1) * wide] for w in weight_refs],
                    [held.at[h, k * depth : (k + 1) * depth] for k in range(spans)],
                    [sems.at[h, k] for k in range(spans)],
                )
            )
        start = 0
        for piece_ref in piece_refs:
            chunks = piece_ref.shape[1] // chunk

            def one(i, _, piece_ref=piece_ref, start=start, chunks=chunks):
                m, c = i // chunks, i % chunks
                values = piece_ref[m, pl.ds(pl.multiple_of(c * chunk, chunk), chunk), :]
                normed, _ = normalize(values.astype(f32))
                to = pl.ds(
                    pl.multiple_of(m * span_rows + start + c * chunk, chunk), chunk
                )
                normal[to, :] = normed.astype(bf16)
                first[to, :] = (normed * gain_ref[0:1] + bias_ref[0:1]).astype(bf16)
                second[to, :] = (normed * gain_ref[1:2] + bias_ref[1:2]).astype(bf16)
                return 0

            lax.fori_loop(0, count * chunks, one, 0)
            start += piece_ref.shape[1]
        for h in range(heads):
            for copy in started[h]:
                copy.wait()

            def two(m, _, h=h):
                to = pl.ds(pl.multiple_of(m * span_rows, span_rows), span_rows)
                made = plain(first[to, :], held[h])
                queries[h, to, :] = turn(made[:, :head_dim], table_ref, 1).astype(bf16)
                pair[0, h, to, :] = turn(
                    made[:, head_dim : 2 * head_dim], table_ref, 1
                ).astype(bf16)
                pair[1, h, to, :] = made[:, 2 * head_dim :].astype(bf16)
                return 0

            lax.fori_loop(0, count, two, 0)

    ins = [(piece, whole(piece)) for piece in pieces]
    ins += [(array, whole(array)) for array in (gains, biases, tables)]
    ins += [(w, kept_out) for w in weights]
    outs = [full_out((rows, width))] * 3 + [
        full_out((heads, rows, head_dim)),
        full_out((2, heads, rows, head_dim)),
    ]
    scratch = [
        pltpu.VMEM((heads, width, wide), bf16),
        pltpu.SemaphoreType.DMA((heads, spans)),
    ]
    flops = 2 * rows * width * columns
    return run(kernel, ins, outs, scratch, flops, 2 * width * (4 * rows + columns), "project")


def expand_up(second, weights, span_rows):
    rows, width = second.shape
    depth, hidden = weights[0].shape
    spans = len(weights)
    tile = min(512, hidden)
    tiles = hidden // tile

    def kernel(*refs):
        second_ref, weight_refs = refs[0], refs[1 : 1 + spans]
        active, slope, held, sems = refs[1 + spans :]
        started = []
        for t in range(tiles):
            started.append(
                copies(
                    [w.at[:, t * tile : (t + 1) * tile] for w in weight_refs],
                    [held.at[t, k * depth : (k + 1) * depth] for k in range(spans)],
                    [sems.at[t, k] for k in range(spans)],
                )
            )
        for t in range(tiles):
            for copy in started[t]:
                copy.wait()

            def one(m, _, t=t):
                to = pl.ds(pl.multiple_of(m * span_rows, span_rows), span_rows)
                pre = plain(second_ref[to, :], held[t])
                risen = 0.5 * (1.0 + lax.erf(pre * half_root))
                columns = slice(t * tile, (t + 1) * tile)
                active[to, columns] = (pre * risen).astype(bf16)
                slope[to, columns] = (
                    risen + pre * jnp.exp(-0.5 * pre * pre) * bell
                ).astype(bf16)
                return 0

            lax.fori_loop(0, rows // span_rows, one, 0)

    ins = [(second, whole(second))] + [(w, kept_out) for w in weights]
    outs = [full_out((rows, hidden))] * 2
    scratch = [
        pltpu.VMEM((tiles, width, tile), bf16),
        pltpu.SemaphoreType.DMA((tiles, spans)),
    ]
    flops = 2 * rows * width * hidden
    moved = 2 * (rows * width + 2 * rows * hidden + width * hidden)
    return run(kernel, ins, outs, scratch, flops, moved, "expand")


def attend(queries, pairs, positions, key_positions, scale, span_rows):
    heads, rows, head_dim = queries.shape
    count = rows // span_rows
    spans = len(pairs)

    def kernel(*refs):
        query_ref, pair_refs = refs[0], refs[1 : 1 + spans]
        row_ref, key_ref, attended, probs = refs[1 + spans :]
        here = query_ref[0]
        scores = []
        for k in range(spans):
            raw = turned(here, pair_refs[k][0, 0]) * scale
            allowed = key_ref[k] <= row_ref[...]
            scores.append(jnp.where(allowed, raw, masked_score))
        top = functools.reduce(
            jnp.maximum, [jnp.max(part, axis=1, keepdims=True) for part in scores]
        )
        scores = [jnp.exp(part - top) for part in scores]
        total = sum(jnp.sum(part, axis=1, keepdims=True) for part in scores)
        inverse = 1.0 / total
        summed = None
        for k in range(spans):
            part = (scores[k] * inverse).astype(bf16)
            probs[k, 0] = part
            term = plain(part, pair_refs[k][1, 0])
            summed = term if summed is None else summed + term
        attended[...] = summed.astype(bf16)

    ins = [(queries, pl.BlockSpec((1, span_rows, head_dim), lambda m, h: (h, m, 0)))]
    ins += [
        (pair, pl.BlockSpec((2, 1, span_rows, head_dim), lambda m, h: (0, h, m, 0)))
        for pair in pairs
    ]
    ins += [(positions, whole(positions)), (key_positions, whole(key_positions))]
    outs = [
        (
            shape((rows, heads * head_dim)),
            pl.BlockSpec((span_rows, head_dim), lambda m, h: (m, h)),
        ),
        (
            shape((spans, heads, rows, span_rows)),
            pl.BlockSpec((spans, 1, span_rows, span_rows), lambda m, h: (0, h, m, 0)),
        ),
    ]
    work = heads * rows * spans * span_rows
    return run(
        kernel, ins, outs, [], 4 * work * head_dim, 8 * work, "attend", grid=(count, heads)
    )


def branch_out(active, attended, contract, output, m, span_rows):
    hidden, depth = contract[0].shape
    across = attended.shape[1]
    spans = len(contract)
    width = depth * spans
    half = span_rows // 2

    def kernel(*refs):
        active_ref, attended_ref = refs[:2]
        contract_refs, output_refs = refs[2 : 2 + spans], refs[2 + spans : 2 + 2 * spans]
        low, high, held, held_out, sems = refs[2 + 2 * spans :]
        started = copies(
            [ref for k in range(spans) for ref in (output_refs[k], contract_refs[k])],
            [ref for k in range(spans) for ref in (held_out.at[k], held.at[k])],
            [sems.at[j] for j in range(2 * spans)],
        )
        for k in range(spans):
            started[2 * k].wait()
            started[2 * k + 1].wait()
            made = plain(attended_ref[...], held_out[k]) + plain(active_ref[...], held[k])
            columns = slice(k * depth, (k + 1) * depth)
            low[:, columns] = made[:half].astype(bf16)
            high[:, columns] = made[half:].astype(bf16)

    ins = [
        (active, at((span_rows, hidden), (m, 0))),
        (attended, at((span_rows, across), (m, 0))),
    ]
    ins += [(w, kept_out) for w in contract] + [(w, kept_out) for w in output]
    outs = [full_out((half, width))] * 2
    scratch = [
        pltpu.VMEM((spans, hidden, depth), bf16),
        pltpu.VMEM((spans, across, depth), bf16),
        pltpu.SemaphoreType.DMA((2 * spans,)),
    ]
    flops = 2 * span_rows * width * (hidden + across)
    moved = 2 * width * (hidden + across + span_rows)
    return run(kernel, ins, outs, scratch, flops, moved, "branch")


def attend_back(pieces, output, queries, pairs, probs, tables, scale, m, at_piece):
    span_rows = sum(piece.shape[1] for piece in pieces)
    width = pieces[0].shape[2]
    heads, _, head_dim = queries.shape
    spans = len(pairs)
    across, depth = output[0].shape
    half = spans // 2

    def kernel(*refs):
        piece_refs = refs[: len(pieces)]
        refs = refs[len(pieces) :]
        output_refs, refs = refs[:spans], refs[spans:]
        query_ref, refs = refs[0], refs[1:]
        pair_refs, refs = refs[:spans], refs[spans:]
        prob_ref, table_ref, rows_out, turned_back, keep, send, held, sems = refs
        started = copies(
            output_refs,
            [held.at[:, k * depth : (k + 1) * depth] for k in range(spans)],
            [sems.at[k] for k in range(spans)],
        )
        start = 0
        for piece_ref in piece_refs:
            size = piece_ref.shape[1]
            rows_out[start : start + size, :] = piece_ref[0]
            start += size
        for copy in started:
            copy.wait()
        grad_attended = turned(rows_out[...], held[...]).astype(bf16)
        for h in range(heads):
            grad = grad_attended[:, h * head_dim : (h + 1) * head_dim]
            here = query_ref[h]
            grad_probs = [turned(grad, pair_refs[k][1, h]) for k in range(spans)]
            parts = [prob_ref[k, h] for k in range(spans)]
            delta = sum(
                jnp.sum(parts[k].astype(f32) * grad_probs[k], axis=1, keepdims=True)
                for k in range(spans)
            )
            query_grad = None
            for k in range(spans):
                slopes = (parts[k].astype(f32) * (grad_probs[k] - delta)).astype(bf16)
                term = plain(slopes, pair_refs[k][0, h])
                query_grad = term if query_grad is None else query_grad + term
                side = keep if k < half else send
                side[k % half, 0, h] = (
                    dot(slopes, here, ((0,), (0,))) * scale
                ).astype(bf16)
                side[k % half, 1, h] = dot(parts[k], grad, ((0,), (0,))).astype(bf16)
            turned_back[h] = turn(query_grad * scale, table_ref, -1).astype(bf16)

    ins = [(piece, at((1,) + piece.shape[1:], (at_piece, 0, 0))) for piece in pieces]
    ins += [(w, kept_out) for w in output]
    ins += [(queries, at((heads, span_rows, head_dim), (0, m, 0)))]
    ins += [(pair, at((2, heads, span_rows, head_dim), (0, 0, m, 0))) for pair in pairs]
    ins += [(probs, at((spans, heads, span_rows, span_rows), (0, 0, m, 0)))]
    ins += [(tables, whole(tables))]
    outs = [full_out((span_rows, width)), full_out((heads, span_rows, head_dim))]
    outs += [full_out((half, 2, heads, span_rows, head_dim))] * 2
    scratch = [pltpu.VMEM((across, width), bf16), pltpu.SemaphoreType.DMA((spans,))]
    work = heads * span_rows * spans * span_rows * head_dim
    flops = 8 * work + 2 * span_rows * width * across
    moved = 2 * width * (across + 2 * span_rows) + 8 * span_rows * spans * across
    return run(kernel, ins, outs, scratch, flops, moved, "attend_back")


def hidden_back(upstream, contract, expand, slope, normal, gains, m):
    span_rows, width = upstream.shape
    hidden, depth = contract[0].shape
    spans = len(contract)
    tile = min(512, hidden)
    tiles = hidden // tile

    def kernel(*refs):
        upstream_ref, refs = refs[0], refs[1:]
        contract_refs, refs = refs[:spans], refs[spans:]
        expand_refs, refs = refs[:spans], refs[spans:]
        slope_ref, normal_ref, gain_ref, grads, part, side, held, held_up, sems, sems_up = refs
        started = [
            copies(
                [w.at[t * tile : (t + 1) * tile, :] for w in contract_refs],
                [held.at[t, :, k * depth : (k + 1) * depth] for k in range(spans)],
                [sems.at[t, k] for k in range(spans)],
            )
            for t in range(tiles)
        ]
        started_up = copies(
            expand_refs, [held_up.at[k] for k in range(spans)], [sems_up.at[k] for k in range(spans)]
        )
        for t in range(tiles):
            for copy in started[t]:
                copy.wait()
            columns = slice(t * tile, (t + 1) * tile)
            grads[:, columns] = (
                turned(upstream_ref[...], held[t]) * slope_ref[:, columns].astype(f32)
            ).astype(bf16)
        for k in range(spans):
            started_up[k].wait()
            made = turned(grads[...], held_up[k])
            columns = slice(k * depth, (k + 1) * depth)
            side[0:1, columns] = jnp.sum(
                made * normal_ref[:, columns].astype(f32), axis=0, keepdims=True
            )
            side[1:2, columns] = jnp.sum(made, axis=0, keepdims=True)
            part[:, columns] = made * gain_ref[1:2, columns]

    ins = [(upstream, whole(upstream))]
    ins += [(w, kept_out) for w in contract] + [(w, kept_out) for w in expand]
    ins += [
        (slope, at((span_rows, hidden), (m, 0))),
        (normal, at((span_rows, width), (m, 0))),
        (gains, whole(gains)),
    ]
    outs = [
        full_out((span_rows, hidden)),
        full_out((span_rows, width), f32),
        full_out((2, width), f32),
    ]
    scratch = [
        pltpu.VMEM((tiles, tile, width), bf16),
        pltpu.VMEM((spans, depth, hidden), bf16),
        pltpu.SemaphoreType.DMA((tiles, spans)),
        pltpu.SemaphoreType.DMA((spans,)),
    ]
    flops = 4 * span_rows * width * hidden
    moved = 4 * width * hidden + 8 * span_rows * width
    return run(kernel, ins, outs, scratch, flops, moved, "hidden_back")


def project_back(turned_back, own, came, weights, part, normal, gains, tables, m):
    heads, span_rows, head_dim = turned_back.shape
    depth, columns = weights[0].shape
    spans = len(weights)
    width = depth * spans
    half = span_rows // 2

    def kernel(*refs):
        query_ref, own_ref, came_ref, refs = refs[0], refs[1], refs[2], refs[3:]
        weight_refs, refs = refs[:spans], refs[spans:]
        part_ref, normal_ref, gain_ref, table_ref, grads, low, high, side, held, sems = refs
        started = copies(
            weight_refs, [held.at[k] for k in range(spans)], [sems.at[k] for k in range(spans)]
        )
        for h in range(heads):
            at_column = h * 3 * head_dim
            keys = own_ref[0, h].astype(f32) + came_ref[0, h].astype(f32)
            values = own_ref[1, h].astype(f32) + came_ref[1, h].astype(f32)
            grads[:, at_column : at_column + head_dim] = query_ref[h]
            grads[:, at_column + head_dim : at_column + 2 * head_dim] = turn(
                keys, table_ref, -1
            ).astype(bf16)
            grads[:, at_column + 2 * head_dim : at_column + 3 * head_dim] = values.astype(bf16)
        for k in range(spans):
            started[k].wait()
            made = turned(grads[...], held[k])
            span_columns = slice(k * depth, (k + 1) * depth)
            side[0:1, span_columns] = jnp.sum(
                made * normal_ref[:, span_columns].astype(f32), axis=0, keepdims=True
            )
            side[1:2, span_columns] = jnp.sum(made, axis=0, keepdims=True)
            both = (made * gain_ref[0:1, span_columns] + part_ref[:, span_columns]).astype(bf16)
            low[:, span_columns] = both[:half]
            high[:, span_columns] = both[half:]

    ins = [(array, whole(array)) for array in (turned_back, own, came)]
    ins += [(w, kept_out) for w in weights]
    ins += [(part, whole(part)), (normal, at((span_rows, width), (m, 0)))]
    ins += [(gains, whole(gains)), (tables, whole(tables))]
    outs = [full_out((span_rows, columns))] + [full_out((half, width))] * 2
    outs += [full_out((2, width), f32)]
    scratch = [pltpu.VMEM((spans, depth, columns), bf16), pltpu.SemaphoreType.DMA((spans,))]
    flops = 2 * span_rows * width * columns
    moved = 2 * width * columns + 10 * span_rows * width
    return run(kernel, ins, outs, scratch, flops, moved, "project_back")


def shards(
    block_input,
    out_grad,
    triple_weight,
    output_weight,
    expand_weight,
    contract_weight,
    norm_gains,
    norm_biases,
):
    section = lax.axis_index("pipe")
    span = lax.axis_index("ctx")
    lane = lax.axis_index("tp")
    spans = lax.axis_size("ctx")
    lanes = lax.axis_size("tp")
    micros, rows, width = block_input.shape
    span_rows = rows * lanes
    heads = triple_weight.shape[2]
    head_dim = triple_weight.shape[4]
    across = heads * head_dim
    scale = head_dim ** (-0.5)
    first_section = section == 0
    both = (0, 1)

    def hop(array, axis, step, sections):
        size = lax.axis_size(axis)
        pairs = [(s * size + a, s * size + (a ^ step)) for s in sections for a in range(size)]
        return lax.ppermute(array, ("pipe", axis), pairs)

    def gather_ctx(array, sections=both):
        held, step = {0: array}, spans // 2
        while step:
            for k in list(held):
                held[k ^ step] = hop(held[k], "ctx", step, sections)
            step //= 2
        return [held[k] for k in doubling(spans)]

    def gather_tp(array, axis, sections):
        pieces, step = [array], lanes // 2
        while step:
            going = jnp.concatenate(pieces, axis=axis) if len(pieces) > 1 else array
            pieces.append(hop(going, "tp", step, sections))
            step //= 2
        return pieces

    def scatter(keep, send, axis_name, dim, sections):
        step, size = 1, lax.axis_size(axis_name)
        while True:
            came = hop(send, axis_name, step, sections)
            step *= 2
            if step == size:
                return keep, came
            middle = keep.shape[dim] // 2
            total = keep.astype(f32) + came.astype(f32)
            keep = lax.slice_in_dim(total, 0, middle, axis=dim).astype(bf16)
            send = lax.slice_in_dim(total, middle, 2 * middle, axis=dim).astype(bf16)

    small = jnp.concatenate([norm_gains[0], norm_biases[0]], axis=0)
    small_full = jnp.concatenate(gather_ctx(small), axis=1).astype(f32)
    gains, biases = small_full[:2], small_full[2:]
    inputs = xor_blocks(block_input, span, spans)
    cotangent = xor_blocks(out_grad, span, spans)
    early = jnp.where(first_section, inputs, cotangent)
    early_pieces = gather_tp(early, 1, both)
    output = gather_ctx(output_weight[0].reshape(across, width // spans))
    triple = gather_ctx(triple_weight[0].reshape(width // spans, 3 * across))
    expand = gather_ctx(expand_weight[0])

    in_row = jnp.arange(rows, dtype=jnp.int32)
    in_span = jnp.concatenate([(lane ^ j) * rows + in_row for j in doubling(lanes)])
    positions = span * span_rows + in_span
    key_positions = jnp.stack([(span ^ k) * span_rows + in_span for k in doubling(spans)])
    tables = rope_tables(positions)
    position_column = positions[:, None]
    key_positions = key_positions[:, None, :]

    def forward_head(pieces, sections):
        first, second, normal, queries, pair = project(
            pieces, gains, biases, tables, triple, head_dim
        )
        pairs = gather_ctx(pair, sections)
        active, slope = expand_up(second, expand, span_rows)
        attended, probs = attend(
            queries, pairs, position_column, key_positions, scale, span_rows
        )
        return dict(
            first=first,
            second=second,
            normal=normal,
            queries=queries,
            pairs=pairs,
            active=active,
            slope=slope,
            attended=attended,
            probs=probs,
        )

    def forward_tail(kept, m, sections):
        low, high = branch_out(kept["active"], kept["attended"], contract, output, m, span_rows)
        return scatter(low, high, "tp", 0, sections)

    def backward(pieces, at_piece, kept, m, sections):
        upstream, turned_back, keep, send = attend_back(
            pieces,
            output,
            kept["queries"],
            kept["pairs"],
            kept["probs"],
            tables,
            scale,
            m,
            at_piece,
        )
        own, came = scatter(keep, send, "ctx", 0, sections)
        hidden_grads, part, side_second = hidden_back(
            upstream, contract, expand, kept["slope"], kept["normal"], gains, m
        )
        own, came = own.reshape(own.shape[1:]), came.reshape(came.shape[1:])
        stacked, low, high, side_first = project_back(
            turned_back, own, came, triple, part, kept["normal"], gains, tables, m
        )
        summed = scatter(low, high, "tp", 0, sections)
        side = jnp.concatenate([side_first, side_second], axis=0)
        return summed, dict(upstream=upstream, hidden=hidden_grads, stacked=stacked, side=side)

    def total_of(pair):
        return pair[0].astype(f32) + pair[1].astype(f32)

    def norm_back(upstream, combined, entering):
        normalized, inverse = normalize(entering.astype(f32))
        return (
            upstream.astype(f32)
            + inverse
            * (
                combined
                - jnp.mean(combined, axis=-1, keepdims=True)
                - normalized * jnp.mean(combined * normalized, axis=-1, keepdims=True)
            )
        ).astype(bf16)

    kept_first = forward_head(early_pieces, (0,))
    contract = gather_ctx(contract_weight[0])
    middle, arrived = [], []
    for m in range(micros):
        total = total_of(forward_tail(kept_first, m, (0,)))
        middle.append((inputs[m].astype(f32) + total).astype(bf16))
        arrived.append(lax.ppermute(middle[m], "pipe", [(0, 1)]))

    kept_second, finals = [], []
    for m in range(micros):
        pieces = gather_tp(arrived[m], 0, (1,))
        kept = forward_head([piece[None] for piece in pieces], (1,))
        total = total_of(forward_tail(kept, 0, (1,)))
        finals.append((arrived[m].astype(f32) + total).astype(bf16))
        kept_second.append(kept)
    layer_outputs = jnp.where(first_section, jnp.stack(middle), jnp.stack(finals))

    relay, made_second, own_entries = [], [], []
    for m in range(micros):
        summed, made = backward(early_pieces, m, kept_second[m], 0, (1,))
        made_second.append(made)
        own_entries.append(norm_back(cotangent[m], total_of(summed), arrived[m]))
        relay.append(lax.ppermute(own_entries[m], "pipe", [(1, 0)]))

    def weight_grads(kepts, mades, sections):
        def joined(dicts, name):
            parts = [d[name] for d in dicts]
            return parts[0] if len(parts) == 1 else jnp.concatenate(parts, axis=0)

        upstream = joined(mades, "upstream")
        tokens = ((0,), (0,))
        half = width // 2

        def by_columns(left):
            send = dot(left, upstream[:, half:], tokens).astype(bf16)
            keep = dot(left, upstream[:, :half], tokens).astype(bf16)
            return scatter(keep, send, "ctx", 1, sections)

        def by_rows(left, right):
            send = dot(left[:, half:], right, tokens).astype(bf16)
            keep = dot(left[:, :half], right, tokens).astype(bf16)
            return scatter(keep, send, "ctx", 0, sections)

        contract_sum = by_columns(joined(kepts, "active"))
        output_sum = by_columns(joined(kepts, "attended"))
        expand_sum = by_rows(joined(kepts, "second"), joined(mades, "hidden"))
        triple_sum = by_rows(joined(kepts, "first"), joined(mades, "stacked"))
        side = sum(made["side"] for made in mades)
        return [triple_sum, output_sum, expand_sum, contract_sum], side

    sums_second, side_second = weight_grads(kept_second, made_second, (1,))

    made_first, entries = [], []
    for m in range(micros):
        pieces = [piece[None] for piece in gather_tp(relay[m], 0, (0,))]
        summed, made = backward(pieces, 0, kept_first, m, (0,))
        made_first.append(made)
        entries.append(norm_back(relay[m], total_of(summed), inputs[m]))
    entry_grads = jnp.where(first_section, jnp.stack(entries), jnp.stack(own_entries))
    sums_first, side_first = weight_grads([kept_first], made_first, (0,))

    triple_grads, output_grads, expand_grads, contract_grads = [
        jnp.where(first_section, total_of(a), total_of(b))
        for a, b in zip(sums_first, sums_second)
    ]
    side = jnp.where(first_section, side_first, side_second)
    step = 1
    while step < spans:
        middle_column = side.shape[1] // 2
        side = side[:, :middle_column] + hop(side[:, middle_column:], "ctx", step, both)
        step *= 2
    step = 1
    while step < lanes:
        side = side + hop(side, "tp", step, both)
        step *= 2
    gain_grads = jnp.stack([side[0], side[2]])
    bias_grads = jnp.stack([side[1], side[3]])
    return (
        xor_blocks(layer_outputs, span, spans, inverse=True)[None],
        xor_blocks(entry_grads, span, spans, inverse=True)[None],
        triple_grads.reshape(triple_weight.shape),
        output_grads.reshape(output_weight.shape),
        expand_grads[None],
        contract_grads[None],
        gain_grads[None],
        bias_grads[None],
    )


def solution(mesh):
    return jax.shard_map(
        shards,
        mesh=mesh,
        in_specs=(
            P(None, ("ctx", "tp"), None),
            P(None, ("ctx", "tp"), None),
            P("pipe", "ctx", "tp", None, None),
            P("pipe", "tp", None, "ctx"),
            P("pipe", "ctx", "tp"),
            P("pipe", "tp", "ctx"),
            P("pipe", None, "ctx"),
            P("pipe", None, "ctx"),
        ),
        out_specs=(
            P("pipe", None, ("ctx", "tp"), None),
            P("pipe", None, ("ctx", "tp"), None),
            P("pipe", "ctx", "tp", None, None),
            P("pipe", "tp", None, "ctx"),
            P("pipe", "ctx", "tp"),
            P("pipe", "tp", "ctx"),
            P("pipe", None, "ctx"),
            P("pipe", None, "ctx"),
        ),
        check_vma=False,
    )
```

```python
import functools

import jax
import jax.numpy as jnp
from jax import lax
from jax.experimental import pallas as pl
from jax.experimental.pallas import tpu as pltpu
from jax.sharding import PartitionSpec as P

ROT = 64
LANES = 128
epsilon = 1e-05
masked_score = -1e30
f32 = jnp.float32
bf16 = jnp.bfloat16
vmem_bytes = 56 * 1024 * 1024
half_root = 0.7071067811865476
bell = 0.3989422804014327


def dot(a, b, dims):
    return lax.dot_general(a, b, (dims, ((), ())), preferred_element_type=f32)


def plain(a, b):
    return dot(a, b, ((1,), (0,)))


def turned(a, b):
    return dot(a, b, ((1,), (1,)))


def doubling(count):
    order, step = [0], count // 2
    while step:
        order += [k ^ step for k in order]
        step //= 2
    return order


def xor_blocks(values, index, count, inverse=False):
    width = values.shape[-1] // count
    order = doubling(count)

    def taken(places):
        return jnp.concatenate(
            [values[..., k * width : (k + 1) * width] for k in places], axis=-1
        )

    if inverse:
        values = taken([order.index(k) for k in range(count)])
    step = 1
    while step < count:
        swapped = taken([k ^ step for k in range(count)])
        values = jnp.where((index & step) != 0, swapped, values)
        step *= 2
    return values if inverse else taken(order)


def rope_tables(positions):
    half = ROT // 2
    frequency = 10000.0 ** (-jnp.arange(0, ROT, 2, dtype=f32) / ROT)
    angles = positions.astype(f32)[:, None] * frequency[None, :]
    cosine, sine = jnp.cos(angles), jnp.sin(angles)
    count = positions.shape[0]
    rest = jnp.zeros((count, LANES - ROT), f32)
    none = jnp.zeros((count, half), f32)
    return jnp.stack(
        [
            jnp.concatenate([cosine, cosine, rest + 1.0], axis=1),
            jnp.concatenate([-sine, none, rest], axis=1),
            jnp.concatenate([none, sine, rest], axis=1),
        ]
    )


def turn(values, tables, sign):
    half = ROT // 2
    part = values[:, :LANES]
    moved = (
        pltpu.roll(part, LANES - half, 1) * tables[1] + pltpu.roll(part, half, 1) * tables[2]
    )
    part = part * tables[0] + (moved if sign > 0 else -moved)
    return jnp.concatenate([part, values[:, LANES:]], axis=1)


def normalize(values):
    center = values - jnp.mean(values, axis=-1, keepdims=True)
    inverse = lax.rsqrt(jnp.mean(center * center, axis=-1, keepdims=True) + epsilon)
    return (center * inverse, inverse)


def whole(array):
    zeros = (0,) * array.ndim
    return pl.BlockSpec(array.shape, lambda *_: zeros)


def at(block, place):
    return pl.BlockSpec(block, lambda *_: place)


kept_out = pl.BlockSpec(memory_space=pl.ANY)


def shape(dims, dtype=bf16):
    return jax.ShapeDtypeStruct(dims, dtype)


class Order:
    def __init__(self):
        self.last = []

    def follow(self, results):
        self.last = [min(results, key=lambda array: array.size * array.dtype.itemsize)]


def run(order, kernel, ins, outs, scratch, flops, moved, name, grid=(1,)):
    before = order.last if order else []
    taken = len(ins)
    ins = list(ins) + [(array, kept_out) for array in before]
    arrays = [array for array, _ in ins]

    def body(*refs):
        kernel(*refs[:taken], *refs[len(ins) :])

    results = pl.pallas_call(
        body,
        grid=grid,
        in_specs=[spec for _, spec in ins],
        out_specs=[spec for _, spec in outs],
        out_shape=[struct for struct, _ in outs],
        scratch_shapes=scratch,
        compiler_params=pltpu.CompilerParams(vmem_limit_bytes=vmem_bytes),
        cost_estimate=pl.CostEstimate(
            flops=int(flops), bytes_accessed=int(moved), transcendentals=0
        ),
        name=name,
    )(*arrays)
    if order:
        order.follow(results)
    return results


def full_out(dims, dtype=bf16):
    zeros = (0,) * len(dims)
    return (shape(dims, dtype), pl.BlockSpec(dims, lambda *_: zeros))


def copies(sources, targets, sems):
    started = []
    for source, target, sem in zip(sources, targets, sems):
        copy = pltpu.make_async_copy(source, target, sem)
        copy.start()
        started.append(copy)
    return started


def project(order, pieces, gains, biases, tables, weights, head_dim):
    count, _, width = pieces[0].shape
    span_rows = sum(piece.shape[1] for piece in pieces)
    rows = count * span_rows
    chunk = pieces[0].shape[1]
    depth, columns = weights[0].shape
    spans = len(weights)
    heads = columns // (3 * head_dim)
    wide = 3 * head_dim

    def kernel(*refs):
        piece_refs = refs[: len(pieces)]
        gain_ref, bias_ref, table_ref = refs[len(pieces) : len(pieces) + 3]
        weight_refs = refs[len(pieces) + 3 : len(pieces) + 3 + spans]
        first, second, normal, queries, pair, held, sems = refs[len(pieces) + 3 + spans :]
        started = []
        for h in range(heads):
            started.append(
                copies(
                    [w.at[:, h * wide : (h + 1) * wide] for w in weight_refs],
                    [held.at[h, k * depth : (k + 1) * depth] for k in range(spans)],
                    [sems.at[h, k] for k in range(spans)],
                )
            )
        start = 0
        for piece_ref in piece_refs:
            chunks = piece_ref.shape[1] // chunk

            def one(i, _, piece_ref=piece_ref, start=start, chunks=chunks):
                m, c = i // chunks, i % chunks
                values = piece_ref[m, pl.ds(pl.multiple_of(c * chunk, chunk), chunk), :]
                normed, _ = normalize(values.astype(f32))
                to = pl.ds(
                    pl.multiple_of(m * span_rows + start + c * chunk, chunk), chunk
                )
                normal[to, :] = normed.astype(bf16)
                first[to, :] = (normed * gain_ref[0:1] + bias_ref[0:1]).astype(bf16)
                second[to, :] = (normed * gain_ref[1:2] + bias_ref[1:2]).astype(bf16)
                return 0

            lax.fori_loop(0, count * chunks, one, 0)
            start += piece_ref.shape[1]
        for h in range(heads):
            for copy in started[h]:
                copy.wait()

            def two(m, _, h=h):
                to = pl.ds(pl.multiple_of(m * span_rows, span_rows), span_rows)
                made = plain(first[to, :], held[h])
                queries[h, to, :] = turn(made[:, :head_dim], table_ref, 1).astype(bf16)
                pair[0, h, to, :] = turn(
                    made[:, head_dim : 2 * head_dim], table_ref, 1
                ).astype(bf16)
                pair[1, h, to, :] = made[:, 2 * head_dim :].astype(bf16)
                return 0

            lax.fori_loop(0, count, two, 0)

    ins = [(piece, whole(piece)) for piece in pieces]
    ins += [(array, whole(array)) for array in (gains, biases, tables)]
    ins += [(w, kept_out) for w in weights]
    outs = [full_out((rows, width))] * 3 + [
        full_out((heads, rows, head_dim)),
        full_out((2, heads, rows, head_dim)),
    ]
    scratch = [
        pltpu.VMEM((heads, width, wide), bf16),
        pltpu.SemaphoreType.DMA((heads, spans)),
    ]
    flops = 2 * rows * width * columns
    return run(order, kernel, ins, outs, scratch, flops, 2 * width * (4 * rows + columns), "project")


def expand_up(order, second, weights, span_rows):
    rows, width = second.shape
    depth, hidden = weights[0].shape
    spans = len(weights)
    tile = min(512, hidden)
    tiles = hidden // tile

    def kernel(*refs):
        second_ref, weight_refs = refs[0], refs[1 : 1 + spans]
        active, slope, held, sems = refs[1 + spans :]
        started = []
        for t in range(tiles):
            started.append(
                copies(
                    [w.at[:, t * tile : (t + 1) * tile] for w in weight_refs],
                    [held.at[t, k * depth : (k + 1) * depth] for k in range(spans)],
                    [sems.at[t, k] for k in range(spans)],
                )
            )
        for t in range(tiles):
            for copy in started[t]:
                copy.wait()

            def one(m, _, t=t):
                to = pl.ds(pl.multiple_of(m * span_rows, span_rows), span_rows)
                pre = plain(second_ref[to, :], held[t])
                risen = 0.5 * (1.0 + lax.erf(pre * half_root))
                columns = slice(t * tile, (t + 1) * tile)
                active[to, columns] = (pre * risen).astype(bf16)
                slope[to, columns] = (
                    risen + pre * jnp.exp(-0.5 * pre * pre) * bell
                ).astype(bf16)
                return 0

            lax.fori_loop(0, rows // span_rows, one, 0)

    ins = [(second, whole(second))] + [(w, kept_out) for w in weights]
    outs = [full_out((rows, hidden))] * 2
    scratch = [
        pltpu.VMEM((tiles, width, tile), bf16),
        pltpu.SemaphoreType.DMA((tiles, spans)),
    ]
    flops = 2 * rows * width * hidden
    moved = 2 * (rows * width + 2 * rows * hidden + width * hidden)
    return run(order, kernel, ins, outs, scratch, flops, moved, "expand")


def attend(order, queries, pairs, positions, key_positions, scale, span_rows):
    heads, rows, head_dim = queries.shape
    count = rows // span_rows
    spans = len(pairs)

    def kernel(*refs):
        query_ref, pair_refs = refs[0], refs[1 : 1 + spans]
        row_ref, key_ref, attended, probs = refs[1 + spans :]
        here = query_ref[0]
        scores = []
        for k in range(spans):
            raw = turned(here, pair_refs[k][0, 0]) * scale
            allowed = key_ref[k] <= row_ref[...]
            scores.append(jnp.where(allowed, raw, masked_score))
        top = functools.reduce(
            jnp.maximum, [jnp.max(part, axis=1, keepdims=True) for part in scores]
        )
        scores = [jnp.exp(part - top) for part in scores]
        total = sum(jnp.sum(part, axis=1, keepdims=True) for part in scores)
        inverse = 1.0 / total
        summed = None
        for k in range(spans):
            part = (scores[k] * inverse).astype(bf16)
            probs[k, 0] = part
            term = plain(part, pair_refs[k][1, 0])
            summed = term if summed is None else summed + term
        attended[...] = summed.astype(bf16)

    ins = [(queries, pl.BlockSpec((1, span_rows, head_dim), lambda m, h: (h, m, 0)))]
    ins += [
        (pair, pl.BlockSpec((2, 1, span_rows, head_dim), lambda m, h: (0, h, m, 0)))
        for pair in pairs
    ]
    ins += [(positions, whole(positions)), (key_positions, whole(key_positions))]
    outs = [
        (
            shape((rows, heads * head_dim)),
            pl.BlockSpec((span_rows, head_dim), lambda m, h: (m, h)),
        ),
        (
            shape((spans, heads, rows, span_rows)),
            pl.BlockSpec((spans, 1, span_rows, span_rows), lambda m, h: (0, h, m, 0)),
        ),
    ]
    work = heads * rows * spans * span_rows
    return run(
        order, kernel, ins, outs, [], 4 * work * head_dim, 8 * work, "attend", grid=(count, heads)
    )


def branch_out(order, active, attended, contract, output, m, span_rows):
    hidden, depth = contract[0].shape
    across = attended.shape[1]
    spans = len(contract)
    width = depth * spans
    half = span_rows // 2

    def kernel(*refs):
        active_ref, attended_ref = refs[:2]
        contract_refs, output_refs = refs[2 : 2 + spans], refs[2 + spans : 2 + 2 * spans]
        low, high, held, held_out, sems = refs[2 + 2 * spans :]
        started = copies(
            [ref for k in range(spans) for ref in (output_refs[k], contract_refs[k])],
            [ref for k in range(spans) for ref in (held_out.at[k], held.at[k])],
            [sems.at[j] for j in range(2 * spans)],
        )
        for k in range(spans):
            started[2 * k].wait()
            started[2 * k + 1].wait()
            made = plain(attended_ref[...], held_out[k]) + plain(active_ref[...], held[k])
            columns = slice(k * depth, (k + 1) * depth)
            low[:, columns] = made[:half].astype(bf16)
            high[:, columns] = made[half:].astype(bf16)

    ins = [
        (active, at((span_rows, hidden), (m, 0))),
        (attended, at((span_rows, across), (m, 0))),
    ]
    ins += [(w, kept_out) for w in contract] + [(w, kept_out) for w in output]
    outs = [full_out((half, width))] * 2
    scratch = [
        pltpu.VMEM((spans, hidden, depth), bf16),
        pltpu.VMEM((spans, across, depth), bf16),
        pltpu.SemaphoreType.DMA((2 * spans,)),
    ]
    flops = 2 * span_rows * width * (hidden + across)
    moved = 2 * width * (hidden + across + span_rows)
    return run(order, kernel, ins, outs, scratch, flops, moved, "branch")


def attend_back(order, pieces, output, queries, pairs, probs, tables, scale, m, at_piece):
    span_rows = sum(piece.shape[1] for piece in pieces)
    width = pieces[0].shape[2]
    heads, _, head_dim = queries.shape
    spans = len(pairs)
    across, depth = output[0].shape
    half = spans // 2

    def kernel(*refs):
        piece_refs = refs[: len(pieces)]
        refs = refs[len(pieces) :]
        output_refs, refs = refs[:spans], refs[spans:]
        query_ref, refs = refs[0], refs[1:]
        pair_refs, refs = refs[:spans], refs[spans:]
        prob_ref, table_ref, rows_out, turned_back, keep, send, held, sems = refs
        started = copies(
            output_refs,
            [held.at[:, k * depth : (k + 1) * depth] for k in range(spans)],
            [sems.at[k] for k in range(spans)],
        )
        start = 0
        for piece_ref in piece_refs:
            size = piece_ref.shape[1]
            rows_out[start : start + size, :] = piece_ref[0]
            start += size
        for copy in started:
            copy.wait()
        grad_attended = turned(rows_out[...], held[...]).astype(bf16)
        for h in range(heads):
            grad = grad_attended[:, h * head_dim : (h + 1) * head_dim]
            here = query_ref[h]
            grad_probs = [turned(grad, pair_refs[k][1, h]) for k in range(spans)]
            parts = [prob_ref[k, h] for k in range(spans)]
            delta = sum(
                jnp.sum(parts[k].astype(f32) * grad_probs[k], axis=1, keepdims=True)
                for k in range(spans)
            )
            query_grad = None
            for k in range(spans):
                slopes = (parts[k].astype(f32) * (grad_probs[k] - delta)).astype(bf16)
                term = plain(slopes, pair_refs[k][0, h])
                query_grad = term if query_grad is None else query_grad + term
                side = keep if k < half else send
                side[k % half, 0, h] = (
                    dot(slopes, here, ((0,), (0,))) * scale
                ).astype(bf16)
                side[k % half, 1, h] = dot(parts[k], grad, ((0,), (0,))).astype(bf16)
            turned_back[h] = turn(query_grad * scale, table_ref, -1).astype(bf16)

    ins = [(piece, at((1,) + piece.shape[1:], (at_piece, 0, 0))) for piece in pieces]
    ins += [(w, kept_out) for w in output]
    ins += [(queries, at((heads, span_rows, head_dim), (0, m, 0)))]
    ins += [(pair, at((2, heads, span_rows, head_dim), (0, 0, m, 0))) for pair in pairs]
    ins += [(probs, at((spans, heads, span_rows, span_rows), (0, 0, m, 0)))]
    ins += [(tables, whole(tables))]
    outs = [full_out((span_rows, width)), full_out((heads, span_rows, head_dim))]
    outs += [full_out((half, 2, heads, span_rows, head_dim))] * 2
    scratch = [pltpu.VMEM((across, width), bf16), pltpu.SemaphoreType.DMA((spans,))]
    work = heads * span_rows * spans * span_rows * head_dim
    flops = 8 * work + 2 * span_rows * width * across
    moved = 2 * width * (across + 2 * span_rows) + 8 * span_rows * spans * across
    return run(order, kernel, ins, outs, scratch, flops, moved, "attend_back")


def hidden_back(order, upstream, contract, expand, slope, normal, gains, m):
    span_rows, width = upstream.shape
    hidden, depth = contract[0].shape
    spans = len(contract)
    tile = min(512, hidden)
    tiles = hidden // tile

    def kernel(*refs):
        upstream_ref, refs = refs[0], refs[1:]
        contract_refs, refs = refs[:spans], refs[spans:]
        expand_refs, refs = refs[:spans], refs[spans:]
        slope_ref, normal_ref, gain_ref, grads, part, side, held, held_up, sems, sems_up = refs
        started = [
            copies(
                [w.at[t * tile : (t + 1) * tile, :] for w in contract_refs],
                [held.at[t, :, k * depth : (k + 1) * depth] for k in range(spans)],
                [sems.at[t, k] for k in range(spans)],
            )
            for t in range(tiles)
        ]
        started_up = copies(
            expand_refs, [held_up.at[k] for k in range(spans)], [sems_up.at[k] for k in range(spans)]
        )
        for t in range(tiles):
            for copy in started[t]:
                copy.wait()
            columns = slice(t * tile, (t + 1) * tile)
            grads[:, columns] = (
                turned(upstream_ref[...], held[t]) * slope_ref[:, columns].astype(f32)
            ).astype(bf16)
        for k in range(spans):
            started_up[k].wait()
            made = turned(grads[...], held_up[k])
            columns = slice(k * depth, (k + 1) * depth)
            side[0:1, columns] = jnp.sum(
                made * normal_ref[:, columns].astype(f32), axis=0, keepdims=True
            )
            side[1:2, columns] = jnp.sum(made, axis=0, keepdims=True)
            part[:, columns] = made * gain_ref[1:2, columns]

    ins = [(upstream, whole(upstream))]
    ins += [(w, kept_out) for w in contract] + [(w, kept_out) for w in expand]
    ins += [
        (slope, at((span_rows, hidden), (m, 0))),
        (normal, at((span_rows, width), (m, 0))),
        (gains, whole(gains)),
    ]
    outs = [
        full_out((span_rows, hidden)),
        full_out((span_rows, width), f32),
        full_out((2, width), f32),
    ]
    scratch = [
        pltpu.VMEM((tiles, tile, width), bf16),
        pltpu.VMEM((spans, depth, hidden), bf16),
        pltpu.SemaphoreType.DMA((tiles, spans)),
        pltpu.SemaphoreType.DMA((spans,)),
    ]
    flops = 4 * span_rows * width * hidden
    moved = 4 * width * hidden + 8 * span_rows * width
    return run(order, kernel, ins, outs, scratch, flops, moved, "hidden_back")


def project_back(order, turned_back, own, came, weights, part, normal, gains, tables, m):
    heads, span_rows, head_dim = turned_back.shape
    depth, columns = weights[0].shape
    spans = len(weights)
    width = depth * spans
    half = span_rows // 2

    def kernel(*refs):
        query_ref, own_ref, came_ref, refs = refs[0], refs[1], refs[2], refs[3:]
        weight_refs, refs = refs[:spans], refs[spans:]
        part_ref, normal_ref, gain_ref, table_ref, grads, low, high, side, held, sems = refs
        started = copies(
            weight_refs, [held.at[k] for k in range(spans)], [sems.at[k] for k in range(spans)]
        )
        for h in range(heads):
            at_column = h * 3 * head_dim
            keys = own_ref[0, h].astype(f32) + came_ref[0, h].astype(f32)
            values = own_ref[1, h].astype(f32) + came_ref[1, h].astype(f32)
            grads[:, at_column : at_column + head_dim] = query_ref[h]
            grads[:, at_column + head_dim : at_column + 2 * head_dim] = turn(
                keys, table_ref, -1
            ).astype(bf16)
            grads[:, at_column + 2 * head_dim : at_column + 3 * head_dim] = values.astype(bf16)
        for k in range(spans):
            started[k].wait()
            made = turned(grads[...], held[k])
            span_columns = slice(k * depth, (k + 1) * depth)
            side[0:1, span_columns] = jnp.sum(
                made * normal_ref[:, span_columns].astype(f32), axis=0, keepdims=True
            )
            side[1:2, span_columns] = jnp.sum(made, axis=0, keepdims=True)
            both = (made * gain_ref[0:1, span_columns] + part_ref[:, span_columns]).astype(bf16)
            low[:, span_columns] = both[:half]
            high[:, span_columns] = both[half:]

    ins = [(array, whole(array)) for array in (turned_back, own, came)]
    ins += [(w, kept_out) for w in weights]
    ins += [(part, whole(part)), (normal, at((span_rows, width), (m, 0)))]
    ins += [(gains, whole(gains)), (tables, whole(tables))]
    outs = [full_out((span_rows, columns))] + [full_out((half, width))] * 2
    outs += [full_out((2, width), f32)]
    scratch = [pltpu.VMEM((spans, depth, columns), bf16), pltpu.SemaphoreType.DMA((spans,))]
    flops = 2 * span_rows * width * columns
    moved = 2 * width * columns + 10 * span_rows * width
    return run(order, kernel, ins, outs, scratch, flops, moved, "project_back")


def weight_sums(order, section, lefts, rights, by_rows, spans):
    rows = sum(piece.shape[0] for piece in lefts[0][0])
    left_width = sum(group[0].shape[1] for group in lefts[0])
    right_width = sum(group[0].shape[1] for group in rights[0])
    if by_rows:
        tile = left_width // spans
        steps, block = spans // 2, (tile, right_width)
    else:
        tile = min(512, left_width)
        while left_width % tile:
            tile //= 2
        steps, block = left_width // tile, (tile, right_width // 2)
    chunk = min(512, block[1])
    pieces = [
        [piece for groups in (lefts[s], rights[s]) for group in groups for piece in group]
        for s in (0, 1)
    ]
    most = max(len(p) for p in pieces)

    def kernel(section_ref, *refs):
        piece_refs = (refs[: len(pieces[0])], refs[len(pieces[0]) : len(pieces[0]) + len(pieces[1])])
        keep, send, left, right, flipped, sems = refs[len(pieces[0]) + len(pieces[1]) :]
        g = pl.program_id(0)
        for s in (0, 1):

            @pl.when((g == 0) & (section_ref[0] == s))
            def _(s=s):
                targets = []
                for held, groups in ((left, lefts[s]), (right, rights[s])):
                    column = 0
                    for group in groups:
                        row, wide = 0, group[0].shape[1]
                        for piece in group:
                            targets.append(
                                held.at[row : row + piece.shape[0], column : column + wide]
                            )
                            row += piece.shape[0]
                        column += wide
                started = copies(
                    piece_refs[s], targets, [sems.at[j] for j in range(len(targets))]
                )
                for copy in started:
                    copy.wait()

        def product(column, store):
            flipped[...] = left[:, pl.ds(pl.multiple_of(column, LANES), tile)].T

            def one(c, _):
                columns = pl.ds(pl.multiple_of(c * chunk, chunk), chunk)
                store(c, plain(flipped[...], right[:, columns]).astype(bf16))
                return 0

            lax.fori_loop(0, right_width // chunk, one, 0)

        if by_rows:

            def to(target):
                def store(c, made):
                    target[:, pl.ds(pl.multiple_of(c * chunk, chunk), chunk)] = made

                return store

            product(g * tile, to(keep))
            product((g + steps) * tile, to(send))
        else:
            half = right_width // 2 // chunk

            def store(c, made):
                @pl.when(c < half)
                def _():
                    keep[:, pl.ds(pl.multiple_of(c * chunk, chunk), chunk)] = made

                @pl.when(c >= half)
                def _():
                    send[:, pl.ds(pl.multiple_of((c - half) * chunk, chunk), chunk)] = made

            product(g * tile, store)

    ins = [(section, pl.BlockSpec(memory_space=pltpu.SMEM))]
    ins += [(piece, kept_out) for s in (0, 1) for piece in pieces[s]]
    dims = (steps * tile, block[1])
    outs = [(shape(dims), pl.BlockSpec(block, lambda g: (g, 0)))] * 2
    scratch = [
        pltpu.VMEM((rows, left_width), bf16),
        pltpu.VMEM((rows, right_width), bf16),
        pltpu.VMEM((tile, rows), bf16),
        pltpu.SemaphoreType.DMA((most,)),
    ]
    flops = 2 * rows * left_width * right_width
    moved = 2 * (rows * (left_width + right_width) + left_width * right_width)
    return run(
        order, kernel, ins, outs, scratch, flops, moved, "weight_sums", grid=(steps,)
    )


def fold(keep, came, dim):
    rows, columns = keep.shape
    if dim == 0:
        tile = min(256, rows // 2)
        steps, block = rows // 2 // tile, (tile, columns)
        places = [lambda g: (g, 0), lambda g: (g + steps, 0)]
        half = (rows // 2, columns)
    else:
        tile = min(256, rows)
        steps, block = rows // tile, (tile, columns // 2)
        places = [lambda g: (g, 0), lambda g: (g, 1)]
        half = (rows, columns // 2)

    def kernel(keep_low, keep_high, came_low, came_high, low, high):
        low[...] = (keep_low[...].astype(f32) + came_low[...].astype(f32)).astype(bf16)
        high[...] = (keep_high[...].astype(f32) + came_high[...].astype(f32)).astype(bf16)

    ins = [(array, pl.BlockSpec(block, place)) for array in (keep, came) for place in places]
    outs = [(shape(half), pl.BlockSpec(block, lambda g: (g, 0)))] * 2
    return run(
        None, kernel, ins, outs, [], keep.size, 6 * keep.size, "fold", grid=(steps,)
    )


def shards(
    block_input,
    out_grad,
    triple_weight,
    output_weight,
    expand_weight,
    contract_weight,
    norm_gains,
    norm_biases,
):
    section = lax.axis_index("pipe")
    span = lax.axis_index("ctx")
    lane = lax.axis_index("tp")
    spans = lax.axis_size("ctx")
    lanes = lax.axis_size("tp")
    micros, rows, width = block_input.shape
    span_rows = rows * lanes
    heads = triple_weight.shape[2]
    head_dim = triple_weight.shape[4]
    across = heads * head_dim
    scale = head_dim ** (-0.5)
    first_section = section == 0
    both = (0, 1)

    def hop(array, axis, step, sections):
        size = lax.axis_size(axis)
        pairs = [(s * size + a, s * size + (a ^ step)) for s in sections for a in range(size)]
        return lax.ppermute(array, ("pipe", axis), pairs)

    def gather_ctx(array, sections=both):
        held, step = {0: array}, spans // 2
        while step:
            for k in list(held):
                held[k ^ step] = hop(held[k], "ctx", step, sections)
            step //= 2
        return [held[k] for k in doubling(spans)]

    def gather_tp(array, axis, sections):
        pieces, step = [array], lanes // 2
        while step:
            going = jnp.concatenate(pieces, axis=axis) if len(pieces) > 1 else array
            pieces.append(hop(going, "tp", step, sections))
            step //= 2
        return pieces

    def scatter(keep, send, axis_name, dim, sections):
        step, size = 1, lax.axis_size(axis_name)
        while True:
            came = hop(send, axis_name, step, sections)
            step *= 2
            if step == size:
                return keep, came
            middle = keep.shape[dim] // 2
            total = keep.astype(f32) + came.astype(f32)
            keep = lax.slice_in_dim(total, 0, middle, axis=dim).astype(bf16)
            send = lax.slice_in_dim(total, middle, 2 * middle, axis=dim).astype(bf16)

    small = jnp.concatenate([norm_gains[0], norm_biases[0]], axis=0)
    small_full = jnp.concatenate(gather_ctx(small), axis=1).astype(f32)
    gains, biases = small_full[:2], small_full[2:]
    inputs = xor_blocks(block_input, span, spans)
    cotangent = xor_blocks(out_grad, span, spans)
    early = jnp.where(first_section, inputs, cotangent)
    early_pieces = gather_tp(early, 1, both)
    output = gather_ctx(output_weight[0].reshape(across, width // spans))
    triple = gather_ctx(triple_weight[0].reshape(width // spans, 3 * across))
    expand = gather_ctx(expand_weight[0])

    in_row = jnp.arange(rows, dtype=jnp.int32)
    in_span = jnp.concatenate([(lane ^ j) * rows + in_row for j in doubling(lanes)])
    positions = span * span_rows + in_span
    key_positions = jnp.stack([(span ^ k) * span_rows + in_span for k in doubling(spans)])
    tables = rope_tables(positions)
    position_column = positions[:, None]
    key_positions = key_positions[:, None, :]

    order = Order()

    def scatter_wide(keep, send, dim):
        step = 1
        while True:
            came = hop(send, "ctx", step, both)
            step *= 2
            if step == spans:
                return keep.astype(f32) + came.astype(f32)
            keep, send = fold(keep, came, dim)

    def start_forward(pieces, sections):
        first, second, normal, queries, pair = project(
            order, pieces, gains, biases, tables, triple, head_dim
        )
        pairs = gather_ctx(pair, sections)
        return dict(first=first, second=second, normal=normal, queries=queries, pairs=pairs)

    def run_expand(kept):
        kept["active"], kept["slope"] = expand_up(order, kept["second"], expand, span_rows)

    def run_attend(kept):
        kept["attended"], kept["probs"] = attend(
            order,
            kept["queries"],
            kept["pairs"],
            position_column,
            key_positions,
            scale,
            span_rows,
        )

    def run_branch(kept, m, sections):
        low, high = branch_out(
            order, kept["active"], kept["attended"], contract, output, m, span_rows
        )
        return total_of(scatter(low, high, "tp", 0, sections))

    def run_attend_back(pieces, at_piece, kept, m, sections):
        upstream, turned_back, keep, send = attend_back(
            order,
            pieces,
            output,
            kept["queries"],
            kept["pairs"],
            kept["probs"],
            tables,
            scale,
            m,
            at_piece,
        )
        own, came = scatter(keep, send, "ctx", 0, sections)
        return dict(
            upstream=upstream,
            turned_back=turned_back,
            own=own.reshape(own.shape[1:]),
            came=came.reshape(came.shape[1:]),
        )

    def run_hidden_back(kept, made, m):
        made["hidden"], made["part"], made["side_second"] = hidden_back(
            order, made["upstream"], contract, expand, kept["slope"], kept["normal"], gains, m
        )

    def run_project_back(kept, made, m, sections):
        made["stacked"], low, high, made["side_first"] = project_back(
            order,
            made["turned_back"],
            made["own"],
            made["came"],
            triple,
            made["part"],
            kept["normal"],
            gains,
            tables,
            m,
        )
        return total_of(scatter(low, high, "tp", 0, sections))

    def total_of(pair):
        return pair[0].astype(f32) + pair[1].astype(f32)

    def norm_back(upstream, combined, entering):
        normalized, inverse = normalize(entering.astype(f32))
        return (
            upstream.astype(f32)
            + inverse
            * (
                combined
                - jnp.mean(combined, axis=-1, keepdims=True)
                - normalized * jnp.mean(combined * normalized, axis=-1, keepdims=True)
            )
        ).astype(bf16)

    kept_first = start_forward(early_pieces, (0,))
    contract = gather_ctx(contract_weight[0])
    run_expand(kept_first)
    run_attend(kept_first)
    middle, arrived, arrived_pieces = [], [], []
    for m in range(micros):
        total = run_branch(kept_first, m, (0,))
        middle.append((inputs[m].astype(f32) + total).astype(bf16))
        arrived.append(lax.ppermute(middle[m], "pipe", [(0, 1)]))
        arrived_pieces.append([piece[None] for piece in gather_tp(arrived[m], 0, (1,))])

    kept_second = [None] * micros
    made_second = [None] * micros
    own_entries, relay, relay_pieces = [], [], []

    def second_project(m):
        kept_second[m] = start_forward(arrived_pieces[m], (1,))

    def second_expand(m):
        run_expand(kept_second[m])

    def second_attend(m):
        run_attend(kept_second[m])

    def second_attend_back(m):
        made_second[m] = run_attend_back(early_pieces, m, kept_second[m], 0, (1,))

    def second_hidden_back(m):
        run_hidden_back(kept_second[m], made_second[m], 0)

    def second_project_back(m):
        total = run_project_back(kept_second[m], made_second[m], 0, (1,))
        own_entries.append(norm_back(cotangent[m], total, arrived[m]))
        relay.append(lax.ppermute(own_entries[m], "pipe", [(1, 0)]))
        relay_pieces.append([piece[None] for piece in gather_tp(relay[m], 0, (0,))])

    steps = [second_project, second_expand, second_attend, second_attend_back]
    steps += [second_hidden_back, second_project_back]
    plan = sorted(
        (3 * m + s, m, s) for m in range(micros) for s in range(len(steps))
    )
    for _, m, s in plan:
        steps[s](m)

    made_first, entries, finals = [], [], []

    def finish(m):
        total = run_branch(kept_second[m], 0, (1,))
        finals.append((arrived[m].astype(f32) + total).astype(bf16))

    section_index = jnp.reshape(section, (1,)).astype(jnp.int32)

    def sums(lefts, rights, by_rows):
        def groups(names, kepts):
            return [[kept[name] for kept in kepts] for name in names]

        sides = [
            (groups(lefts, [kept_first]), groups(rights, made_first)),
            (groups(lefts, kept_second), groups(rights, made_second)),
        ]
        keep, send = weight_sums(
            order,
            section_index,
            [side[0] for side in sides],
            [side[1] for side in sides],
            by_rows,
            spans,
        )
        return scatter_wide(keep, send, 0 if by_rows else 1)

    for m in range(micros):
        if m == micros - 1:
            finish(m)
        made_first.append(run_attend_back(relay_pieces[m], 0, kept_first, m, (0,)))
        if m == micros - 1:
            branch_grads = sums(["active", "attended"], ["upstream"], False)
        run_hidden_back(kept_first, made_first[m], m)
        if m == micros - 1:
            expand_grads = sums(["second"], ["hidden"], True)
        else:
            finish(m)
        total = run_project_back(kept_first, made_first[m], m, (0,))
        entries.append(norm_back(relay[m], total, inputs[m]))
    triple_grads = sums(["first"], ["stacked"], True)
    hidden = expand_weight.shape[2]
    contract_grads, output_grads = branch_grads[:hidden], branch_grads[hidden:]
    layer_outputs = jnp.where(first_section, jnp.stack(middle), jnp.stack(finals))
    entry_grads = jnp.where(first_section, jnp.stack(entries), jnp.stack(own_entries))

    def side_of(mades):
        return sum(
            jnp.concatenate([made["side_first"], made["side_second"]], axis=0) for made in mades
        )

    side_first, side_second = side_of(made_first), side_of(made_second)
    side = jnp.where(first_section, side_first, side_second)
    step = 1
    while step < spans:
        middle_column = side.shape[1] // 2
        side = side[:, :middle_column] + hop(side[:, middle_column:], "ctx", step, both)
        step *= 2
    step = 1
    while step < lanes:
        side = side + hop(side, "tp", step, both)
        step *= 2
    gain_grads = jnp.stack([side[0], side[2]])
    bias_grads = jnp.stack([side[1], side[3]])
    return (
        xor_blocks(layer_outputs, span, spans, inverse=True)[None],
        xor_blocks(entry_grads, span, spans, inverse=True)[None],
        triple_grads.reshape(triple_weight.shape),
        output_grads.reshape(output_weight.shape),
        expand_grads[None],
        contract_grads[None],
        gain_grads[None],
        bias_grads[None],
    )


def solution(mesh):
    return jax.shard_map(
        shards,
        mesh=mesh,
        in_specs=(
            P(None, ("ctx", "tp"), None),
            P(None, ("ctx", "tp"), None),
            P("pipe", "ctx", "tp", None, None),
            P("pipe", "tp", None, "ctx"),
            P("pipe", "ctx", "tp"),
            P("pipe", "tp", "ctx"),
            P("pipe", None, "ctx"),
            P("pipe", None, "ctx"),
        ),
        out_specs=(
            P("pipe", None, ("ctx", "tp"), None),
            P("pipe", None, ("ctx", "tp"), None),
            P("pipe", "ctx", "tp", None, None),
            P("pipe", "tp", None, "ctx"),
            P("pipe", "ctx", "tp"),
            P("pipe", "tp", "ctx"),
            P("pipe", None, "ctx"),
            P("pipe", None, "ctx"),
        ),
        check_vma=False,
    )
```

```python
import functools

import jax
import jax.numpy as jnp
from jax import lax
from jax.experimental import pallas as pl
from jax.experimental.pallas import tpu as pltpu
from jax.sharding import PartitionSpec as P

ROT = 64
LANES = 128
epsilon = 1e-05
masked_score = -1e30
f32 = jnp.float32
bf16 = jnp.bfloat16
vmem_bytes = 56 * 1024 * 1024
half_root = 0.7071067811865476
bell = 0.3989422804014327


def dot(a, b, dims):
    return lax.dot_general(a, b, (dims, ((), ())), preferred_element_type=f32)


def plain(a, b):
    return dot(a, b, ((1,), (0,)))


def turned(a, b):
    return dot(a, b, ((1,), (1,)))


def doubling(count):
    order, step = [0], count // 2
    while step:
        order += [k ^ step for k in order]
        step //= 2
    return order


def xor_blocks(values, index, count, inverse=False):
    width = values.shape[-1] // count
    order = doubling(count)

    def taken(places):
        return jnp.concatenate(
            [values[..., k * width : (k + 1) * width] for k in places], axis=-1
        )

    if inverse:
        values = taken([order.index(k) for k in range(count)])
    step = 1
    while step < count:
        swapped = taken([k ^ step for k in range(count)])
        values = jnp.where((index & step) != 0, swapped, values)
        step *= 2
    return values if inverse else taken(order)


def rope_tables(positions):
    half = ROT // 2
    frequency = 10000.0 ** (-jnp.arange(0, ROT, 2, dtype=f32) / ROT)
    angles = positions.astype(f32)[:, None] * frequency[None, :]
    cosine, sine = jnp.cos(angles), jnp.sin(angles)
    count = positions.shape[0]
    rest = jnp.zeros((count, LANES - ROT), f32)
    none = jnp.zeros((count, half), f32)
    return jnp.stack(
        [
            jnp.concatenate([cosine, cosine, rest + 1.0], axis=1),
            jnp.concatenate([-sine, none, rest], axis=1),
            jnp.concatenate([none, sine, rest], axis=1),
        ]
    )


def turn(values, tables, sign):
    half = ROT // 2
    part = values[:, :LANES]
    moved = (
        pltpu.roll(part, LANES - half, 1) * tables[1] + pltpu.roll(part, half, 1) * tables[2]
    )
    part = part * tables[0] + (moved if sign > 0 else -moved)
    return jnp.concatenate([part, values[:, LANES:]], axis=1)


def normalize(values):
    center = values - jnp.mean(values, axis=-1, keepdims=True)
    inverse = lax.rsqrt(jnp.mean(center * center, axis=-1, keepdims=True) + epsilon)
    return (center * inverse, inverse)


def whole(array):
    zeros = (0,) * array.ndim
    return pl.BlockSpec(array.shape, lambda *_: zeros)


def at(block, place):
    return pl.BlockSpec(block, lambda *_: place)


kept_out = pl.BlockSpec(memory_space=pl.ANY)


def shape(dims, dtype=bf16):
    return jax.ShapeDtypeStruct(dims, dtype)


class Order:
    def __init__(self):
        self.last = []

    def follow(self, results):
        self.last = [min(results, key=lambda array: array.size * array.dtype.itemsize)]

    def also(self, array):
        self.last = self.last + [array]


def run(order, flags, kernel, ins, outs, scratch, flops, moved, name, grid=(1,)):
    taken = len(ins)
    ins = [(flags, pl.BlockSpec(memory_space=pltpu.SMEM))] + list(ins)
    ins += [(array, kept_out) for array in order.last]
    arrays = [array for array, _ in ins]

    def body(flag_ref, *refs):
        @pl.when(flag_ref[0] == 1)
        def _():
            kernel(flag_ref, *refs[:taken], *refs[len(ins) - 1 :])

    results = pl.pallas_call(
        body,
        grid=grid,
        in_specs=[spec for _, spec in ins],
        out_specs=[spec for _, spec in outs],
        out_shape=[struct for struct, _ in outs],
        scratch_shapes=scratch,
        compiler_params=pltpu.CompilerParams(vmem_limit_bytes=vmem_bytes),
        cost_estimate=pl.CostEstimate(
            flops=int(flops), bytes_accessed=int(moved), transcendentals=0
        ),
        name=name,
    )(*arrays)
    order.follow(results)
    return results


def full_out(dims, dtype=bf16):
    zeros = (0,) * len(dims)
    return (shape(dims, dtype), pl.BlockSpec(dims, lambda *_: zeros))


def copies(sources, targets, sems):
    started = []
    for source, target, sem in zip(sources, targets, sems):
        copy = pltpu.make_async_copy(source, target, sem)
        copy.start()
        started.append(copy)
    return started


def project(order, flags, pieces, gains, biases, tables, weights, heads, head_dim):
    count, _, width = pieces[0].shape
    span_rows = sum(piece.shape[1] for piece in pieces)
    rows = count * span_rows
    chunk = pieces[0].shape[1]
    spans = len(weights)
    depth = width // spans
    wide = 3 * head_dim
    columns = heads * wide

    def kernel(flag_ref, *refs):
        piece_refs = refs[: len(pieces)]
        gain_ref, bias_ref, table_ref = refs[len(pieces) : len(pieces) + 3]
        weight_refs = refs[len(pieces) + 3 : len(pieces) + 3 + spans]
        first, second, normal, queries, pair, held, sems = refs[len(pieces) + 3 + spans :]
        started = []
        for h in range(heads):
            started.append(
                copies(
                    [w.at[:depth, h * wide : (h + 1) * wide] for w in weight_refs],
                    [held.at[h, k * depth : (k + 1) * depth] for k in range(spans)],
                    [sems.at[h, k] for k in range(spans)],
                )
            )
        start = 0
        for piece_ref in piece_refs:
            chunks = piece_ref.shape[1] // chunk

            def one(i, _, piece_ref=piece_ref, start=start, chunks=chunks):
                m, c = i // chunks, i % chunks
                values = piece_ref[m, pl.ds(pl.multiple_of(c * chunk, chunk), chunk), :]
                normed, _ = normalize(values.astype(f32))
                to = pl.ds(
                    pl.multiple_of(m * span_rows + start + c * chunk, chunk), chunk
                )
                normal[to, :] = normed.astype(bf16)
                first[to, :] = (normed * gain_ref[0:1] + bias_ref[0:1]).astype(bf16)
                second[to, :] = (normed * gain_ref[1:2] + bias_ref[1:2]).astype(bf16)
                return 0

            lax.fori_loop(0, count * chunks, one, 0)
            start += piece_ref.shape[1]
        for h in range(heads):
            for copy in started[h]:
                copy.wait()

            def two(m, _, h=h):
                to = pl.ds(pl.multiple_of(m * span_rows, span_rows), span_rows)
                made = plain(first[to, :], held[h])
                queries[h, to, :] = turn(made[:, :head_dim], table_ref, 1).astype(bf16)
                pair[0, h, to, :] = turn(
                    made[:, head_dim : 2 * head_dim], table_ref, 1
                ).astype(bf16)
                pair[1, h, to, :] = made[:, 2 * head_dim :].astype(bf16)
                return 0

            lax.fori_loop(0, count, two, 0)

    ins = [(piece, whole(piece)) for piece in pieces]
    ins += [(array, whole(array)) for array in (gains, biases, tables)]
    ins += [(w, kept_out) for w in weights]
    outs = [full_out((rows, width))] * 3 + [
        full_out((heads, rows, head_dim)),
        full_out((2, heads, rows, head_dim)),
    ]
    scratch = [
        pltpu.VMEM((heads, width, wide), bf16),
        pltpu.SemaphoreType.DMA((heads, spans)),
    ]
    flops = 2 * rows * width * columns
    return run(order, flags, kernel, ins, outs, scratch, flops, 2 * width * (4 * rows + columns), "project")


def expand_up(order, flags, second, weights, span_rows):
    rows, width = second.shape
    depth, hidden = weights[0].shape
    spans = len(weights)
    tile = min(512, hidden)
    tiles = hidden // tile

    def kernel(flag_ref, *refs):
        second_ref, weight_refs = refs[0], refs[1 : 1 + spans]
        active, slope, held, sems = refs[1 + spans :]
        started = []
        for t in range(tiles):
            started.append(
                copies(
                    [w.at[:, t * tile : (t + 1) * tile] for w in weight_refs],
                    [held.at[t, k * depth : (k + 1) * depth] for k in range(spans)],
                    [sems.at[t, k] for k in range(spans)],
                )
            )
        for t in range(tiles):
            for copy in started[t]:
                copy.wait()

            def one(m, _, t=t):
                to = pl.ds(pl.multiple_of(m * span_rows, span_rows), span_rows)
                pre = plain(second_ref[to, :], held[t])
                risen = 0.5 * (1.0 + lax.erf(pre * half_root))
                columns = slice(t * tile, (t + 1) * tile)
                active[to, columns] = (pre * risen).astype(bf16)
                slope[to, columns] = (
                    risen + pre * jnp.exp(-0.5 * pre * pre) * bell
                ).astype(bf16)
                return 0

            lax.fori_loop(0, rows // span_rows, one, 0)

    ins = [(second, whole(second))] + [(w, kept_out) for w in weights]
    outs = [full_out((rows, hidden))] * 2
    scratch = [
        pltpu.VMEM((tiles, width, tile), bf16),
        pltpu.SemaphoreType.DMA((tiles, spans)),
    ]
    flops = 2 * rows * width * hidden
    moved = 2 * (rows * width + 2 * rows * hidden + width * hidden)
    return run(order, flags, kernel, ins, outs, scratch, flops, moved, "expand")


def attend(order, flags, queries, pairs, positions, key_positions, scale, span_rows):
    heads, rows, head_dim = queries.shape
    count = rows // span_rows
    spans = pairs.shape[0]

    def kernel(flag_ref, query_ref, pair_ref, row_ref, key_ref, attended, probs):
        here = query_ref[0]
        scores = []
        for k in range(spans):
            raw = turned(here, pair_ref[k, 0, 0]) * scale
            allowed = key_ref[k] <= row_ref[...]
            scores.append(jnp.where(allowed, raw, masked_score))
        top = functools.reduce(
            jnp.maximum, [jnp.max(part, axis=1, keepdims=True) for part in scores]
        )
        scores = [jnp.exp(part - top) for part in scores]
        total = sum(jnp.sum(part, axis=1, keepdims=True) for part in scores)
        inverse = 1.0 / total
        summed = None
        for k in range(spans):
            part = (scores[k] * inverse).astype(bf16)
            probs[k, 0] = part
            term = plain(part, pair_ref[k, 1, 0])
            summed = term if summed is None else summed + term
        attended[...] = summed.astype(bf16)

    ins = [
        (queries, pl.BlockSpec((1, span_rows, head_dim), lambda m, h: (h, m, 0))),
        (
            pairs,
            pl.BlockSpec((spans, 2, 1, span_rows, head_dim), lambda m, h: (0, 0, h, m, 0)),
        ),
        (positions, whole(positions)),
        (key_positions, whole(key_positions)),
    ]
    outs = [
        (
            shape((rows, heads * head_dim)),
            pl.BlockSpec((span_rows, head_dim), lambda m, h: (m, h)),
        ),
        (
            shape((spans, heads, rows, span_rows)),
            pl.BlockSpec((spans, 1, span_rows, span_rows), lambda m, h: (0, h, m, 0)),
        ),
    ]
    work = heads * rows * spans * span_rows
    return run(
        order,
        flags,
        kernel,
        ins,
        outs,
        [],
        4 * work * head_dim,
        8 * work,
        "attend",
        grid=(count, heads),
    )


def branch_out(order, flags, groups, contract, packed, span_rows):
    hidden, depth = contract[0].shape
    across = groups[0][1].shape[1]
    spans = len(contract)
    width = depth * spans
    half = span_rows // 2
    count = len(groups)

    def kernel(flag_ref, *refs):
        group_refs, refs = refs[: 2 * count], refs[2 * count :]
        contract_refs, packed_refs = refs[:spans], refs[spans : 2 * spans]
        low, high, held, held_out, sems = refs[2 * spans :]
        outputs = [w.at[:across, 3 * across : 3 * across + depth] for w in packed_refs]
        started = copies(
            [ref for k in range(spans) for ref in (outputs[k], contract_refs[k])],
            [ref for k in range(spans) for ref in (held_out.at[k], held.at[k])],
            [sems.at[j] for j in range(2 * spans)],
        )
        for k in range(spans):
            started[2 * k].wait()
            started[2 * k + 1].wait()
            columns = slice(k * depth, (k + 1) * depth)
            for c in range(count):
                made = plain(group_refs[2 * c + 1][...], held_out[k])
                made = made + plain(group_refs[2 * c][...], held[k])
                low[c, :, columns] = made[:half].astype(bf16)
                high[c, :, columns] = made[half:].astype(bf16)

    ins = []
    for active, attended, m in groups:
        ins += [
            (active, at((span_rows, hidden), (m, 0))),
            (attended, at((span_rows, across), (m, 0))),
        ]
    ins += [(w, kept_out) for w in contract] + [(w, kept_out) for w in packed]
    outs = [full_out((count, half, width))] * 2
    scratch = [
        pltpu.VMEM((spans, hidden, depth), bf16),
        pltpu.VMEM((spans, across, depth), bf16),
        pltpu.SemaphoreType.DMA((2 * spans,)),
    ]
    flops = 2 * count * span_rows * width * (hidden + across)
    moved = 2 * width * (hidden + across + count * span_rows)
    return run(order, flags, kernel, ins, outs, scratch, flops, moved, "branch")


def attend_back(order, flags, pieces, packed, queries, pairs, probs, tables, scale, m, at_piece):
    span_rows = sum(piece.shape[1] for piece in pieces)
    width = pieces[0].shape[2]
    heads, _, head_dim = queries.shape
    spans = len(packed)
    across, depth = heads * head_dim, width // spans
    half = spans // 2
    offsets = doubling(spans)

    def kernel(flag_ref, *refs):
        piece_refs = refs[: len(pieces)]
        refs = refs[len(pieces) :]
        packed_refs, refs = refs[:spans], refs[spans:]
        query_ref, pair_ref, prob_ref, table_ref, *refs = refs
        rows_out, turned_back, keep, send, held, sems = refs
        places = [jnp.bitwise_xor(flag_ref[1], offset) for offset in offsets]
        started = copies(
            [w.at[:across, 3 * across : 3 * across + depth] for w in packed_refs],
            [held.at[:, k * depth : (k + 1) * depth] for k in range(spans)],
            [sems.at[k] for k in range(spans)],
        )
        start = 0
        for piece_ref in piece_refs:
            size = piece_ref.shape[1]
            rows_out[start : start + size, :] = piece_ref[0]
            start += size
        for copy in started:
            copy.wait()
        grad_attended = turned(rows_out[...], held[...]).astype(bf16)
        for h in range(heads):
            grad = grad_attended[:, h * head_dim : (h + 1) * head_dim]
            here = query_ref[h]
            grad_probs = [turned(grad, pair_ref[places[k], 1, h]) for k in range(spans)]
            parts = [prob_ref[places[k], h] for k in range(spans)]
            delta = sum(
                jnp.sum(parts[k].astype(f32) * grad_probs[k], axis=1, keepdims=True)
                for k in range(spans)
            )
            query_grad = None
            for k in range(spans):
                slopes = (parts[k].astype(f32) * (grad_probs[k] - delta)).astype(bf16)
                term = plain(slopes, pair_ref[places[k], 0, h])
                query_grad = term if query_grad is None else query_grad + term
                side = keep if k < half else send
                side[k % half, 0, h] = (
                    dot(slopes, here, ((0,), (0,))) * scale
                ).astype(bf16)
                side[k % half, 1, h] = dot(parts[k], grad, ((0,), (0,))).astype(bf16)
            turned_back[h] = turn(query_grad * scale, table_ref, -1).astype(bf16)

    ins = [(piece, at((1,) + piece.shape[1:], (at_piece, 0, 0))) for piece in pieces]
    ins += [(w, kept_out) for w in packed]
    ins += [(queries, at((heads, span_rows, head_dim), (0, m, 0)))]
    ins += [(pairs, at((spans, 2, heads, span_rows, head_dim), (0, 0, 0, m, 0)))]
    ins += [(probs, at((spans, heads, span_rows, span_rows), (0, 0, m, 0)))]
    ins += [(tables, whole(tables))]
    outs = [full_out((span_rows, width)), full_out((heads, span_rows, head_dim))]
    outs += [full_out((half, 2, heads, span_rows, head_dim))] * 2
    scratch = [pltpu.VMEM((across, width), bf16), pltpu.SemaphoreType.DMA((spans,))]
    work = heads * span_rows * spans * span_rows * head_dim
    flops = 8 * work + 2 * span_rows * width * across
    moved = 2 * width * (across + 2 * span_rows) + 8 * span_rows * spans * across
    return run(order, flags, kernel, ins, outs, scratch, flops, moved, "attend_back")


def hidden_back(order, flags, upstream, contract, expand, slope, normal, gains, m):
    span_rows, width = upstream.shape
    hidden, depth = contract[0].shape
    spans = len(contract)
    tile = min(512, hidden)
    tiles = hidden // tile

    def kernel(flag_ref, *refs):
        upstream_ref, refs = refs[0], refs[1:]
        contract_refs, refs = refs[:spans], refs[spans:]
        expand_refs, refs = refs[:spans], refs[spans:]
        slope_ref, normal_ref, gain_ref, grads, part, side, held, held_up, sems, sems_up = refs
        started = [
            copies(
                [w.at[t * tile : (t + 1) * tile, :] for w in contract_refs],
                [held.at[t, :, k * depth : (k + 1) * depth] for k in range(spans)],
                [sems.at[t, k] for k in range(spans)],
            )
            for t in range(tiles)
        ]
        started_up = copies(
            expand_refs, [held_up.at[k] for k in range(spans)], [sems_up.at[k] for k in range(spans)]
        )
        for t in range(tiles):
            for copy in started[t]:
                copy.wait()
            columns = slice(t * tile, (t + 1) * tile)
            grads[:, columns] = (
                turned(upstream_ref[...], held[t]) * slope_ref[:, columns].astype(f32)
            ).astype(bf16)
        for k in range(spans):
            started_up[k].wait()
            made = turned(grads[...], held_up[k])
            columns = slice(k * depth, (k + 1) * depth)
            side[0:1, columns] = jnp.sum(
                made * normal_ref[:, columns].astype(f32), axis=0, keepdims=True
            )
            side[1:2, columns] = jnp.sum(made, axis=0, keepdims=True)
            part[:, columns] = made * gain_ref[1:2, columns]

    ins = [(upstream, whole(upstream))]
    ins += [(w, kept_out) for w in contract] + [(w, kept_out) for w in expand]
    ins += [
        (slope, at((span_rows, hidden), (m, 0))),
        (normal, at((span_rows, width), (m, 0))),
        (gains, whole(gains)),
    ]
    outs = [
        full_out((span_rows, hidden)),
        full_out((span_rows, width), f32),
        full_out((2, width), f32),
    ]
    scratch = [
        pltpu.VMEM((tiles, tile, width), bf16),
        pltpu.VMEM((spans, depth, hidden), bf16),
        pltpu.SemaphoreType.DMA((tiles, spans)),
        pltpu.SemaphoreType.DMA((spans,)),
    ]
    flops = 4 * span_rows * width * hidden
    moved = 4 * width * hidden + 8 * span_rows * width
    return run(order, flags, kernel, ins, outs, scratch, flops, moved, "hidden_back")


def project_back(order, flags, turned_back, own, came, weights, part, normal, gains, tables, m):
    heads, span_rows, head_dim = turned_back.shape
    spans = len(weights)
    width = part.shape[1]
    depth, columns = width // spans, 3 * heads * head_dim
    half = span_rows // 2

    def kernel(flag_ref, *refs):
        query_ref, own_ref, came_ref, refs = refs[0], refs[1], refs[2], refs[3:]
        weight_refs, refs = refs[:spans], refs[spans:]
        part_ref, normal_ref, gain_ref, table_ref, grads, low, high, side, held, sems = refs
        started = copies(
            [w.at[:depth, :columns] for w in weight_refs],
            [held.at[k] for k in range(spans)],
            [sems.at[k] for k in range(spans)],
        )
        for h in range(heads):
            at_column = h * 3 * head_dim
            keys = own_ref[0, h].astype(f32) + came_ref[0, h].astype(f32)
            values = own_ref[1, h].astype(f32) + came_ref[1, h].astype(f32)
            grads[:, at_column : at_column + head_dim] = query_ref[h]
            grads[:, at_column + head_dim : at_column + 2 * head_dim] = turn(
                keys, table_ref, -1
            ).astype(bf16)
            grads[:, at_column + 2 * head_dim : at_column + 3 * head_dim] = values.astype(bf16)
        for k in range(spans):
            started[k].wait()
            made = turned(grads[...], held[k])
            span_columns = slice(k * depth, (k + 1) * depth)
            side[0:1, span_columns] = jnp.sum(
                made * normal_ref[:, span_columns].astype(f32), axis=0, keepdims=True
            )
            side[1:2, span_columns] = jnp.sum(made, axis=0, keepdims=True)
            both = (made * gain_ref[0:1, span_columns] + part_ref[:, span_columns]).astype(bf16)
            low[:, span_columns] = both[:half]
            high[:, span_columns] = both[half:]

    ins = [(array, whole(array)) for array in (turned_back, own, came)]
    ins += [(w, kept_out) for w in weights]
    ins += [(part, whole(part)), (normal, at((span_rows, width), (m, 0)))]
    ins += [(gains, whole(gains)), (tables, whole(tables))]
    outs = [full_out((span_rows, columns))] + [full_out((half, width))] * 2
    outs += [full_out((2, width), f32)]
    scratch = [pltpu.VMEM((spans, depth, columns), bf16), pltpu.SemaphoreType.DMA((spans,))]
    flops = 2 * span_rows * width * columns
    moved = 2 * width * columns + 10 * span_rows * width
    return run(order, flags, kernel, ins, outs, scratch, flops, moved, "project_back")


def weight_sums(order, flags, lefts, rights, by_rows, spans):
    rows = sum(piece.shape[0] for piece in lefts[0][0])
    left_width = sum(group[0].shape[1] for group in lefts[0])
    right_width = sum(group[0].shape[1] for group in rights[0])
    if by_rows:
        tile = left_width // spans
        steps, block = spans // 2, (tile, right_width)
    else:
        tile = min(512, left_width)
        while left_width % tile:
            tile //= 2
        steps, block = left_width // tile, (tile, right_width // 2)
    chunk = min(1024, block[1])
    while right_width % chunk:
        chunk //= 2
    pieces = [
        [piece for groups in (lefts[s], rights[s]) for group in groups for piece in group]
        for s in (0, 1)
    ]
    most = max(len(p) for p in pieces)

    def kernel(flag_ref, *refs):
        piece_refs = (refs[: len(pieces[0])], refs[len(pieces[0]) : len(pieces[0]) + len(pieces[1])])
        keep, send, left, right, flipped, sems = refs[len(pieces[0]) + len(pieces[1]) :]
        g = pl.program_id(0)
        for s in (0, 1):

            @pl.when((g == 0) & (flag_ref[2] == s))
            def _(s=s):
                targets = []
                for held, groups in ((left, lefts[s]), (right, rights[s])):
                    column = 0
                    for group in groups:
                        row, wide = 0, group[0].shape[1]
                        for piece in group:
                            targets.append(
                                held.at[row : row + piece.shape[0], column : column + wide]
                            )
                            row += piece.shape[0]
                        column += wide
                started = copies(
                    piece_refs[s], targets, [sems.at[j] for j in range(len(targets))]
                )
                for copy in started:
                    copy.wait()

        def product(column, store):
            flipped[...] = left[:, pl.ds(pl.multiple_of(column, LANES), tile)].T

            def one(c, _):
                columns = pl.ds(pl.multiple_of(c * chunk, chunk), chunk)
                store(c, plain(flipped[...], right[:, columns]).astype(bf16))
                return 0

            lax.fori_loop(0, right_width // chunk, one, 0)

        if by_rows:

            def to(target):
                def store(c, made):
                    target[:, pl.ds(pl.multiple_of(c * chunk, chunk), chunk)] = made

                return store

            product(g * tile, to(keep))
            product((g + steps) * tile, to(send))
        else:
            half = right_width // 2 // chunk

            def store(c, made):
                @pl.when(c < half)
                def _():
                    keep[:, pl.ds(pl.multiple_of(c * chunk, chunk), chunk)] = made

                @pl.when(c >= half)
                def _():
                    send[:, pl.ds(pl.multiple_of((c - half) * chunk, chunk), chunk)] = made

            product(g * tile, store)

    ins = [(piece, kept_out) for s in (0, 1) for piece in pieces[s]]
    dims = (steps * tile, block[1])
    outs = [(shape(dims), pl.BlockSpec(block, lambda g: (g, 0)))] * 2
    scratch = [
        pltpu.VMEM((rows, left_width), bf16),
        pltpu.VMEM((rows, right_width), bf16),
        pltpu.VMEM((tile, rows), bf16),
        pltpu.SemaphoreType.DMA((most,)),
    ]
    flops = 2 * rows * left_width * right_width
    moved = 2 * (rows * (left_width + right_width) + left_width * right_width)
    return run(
        order, flags, kernel, ins, outs, scratch, flops, moved, "weight_sums", grid=(steps,)
    )


def fold(order, flags, keep, came, dim):
    rows, columns = keep.shape
    if dim == 0:
        tile = min(256, rows // 2)
        steps, block = rows // 2 // tile, (tile, columns)
        places = [lambda g: (g, 0), lambda g: (g + steps, 0)]
        half = (rows // 2, columns)
    else:
        tile = min(256, rows)
        steps, block = rows // tile, (tile, columns // 2)
        places = [lambda g: (g, 0), lambda g: (g, 1)]
        half = (rows, columns // 2)

    def kernel(flag_ref, keep_low, keep_high, came_low, came_high, low, high):
        low[...] = (keep_low[...].astype(f32) + came_low[...].astype(f32)).astype(bf16)
        high[...] = (keep_high[...].astype(f32) + came_high[...].astype(f32)).astype(bf16)

    ins = [(array, pl.BlockSpec(block, place)) for array in (keep, came) for place in places]
    outs = [(shape(half), pl.BlockSpec(block, lambda g: (g, 0)))] * 2
    return run(
        order, flags, kernel, ins, outs, [], keep.size, 6 * keep.size, "fold", grid=(steps,)
    )


def shards(
    block_input,
    out_grad,
    triple_weight,
    output_weight,
    expand_weight,
    contract_weight,
    norm_gains,
    norm_biases,
):
    section = lax.axis_index("pipe")
    span = lax.axis_index("ctx")
    lane = lax.axis_index("tp")
    spans = lax.axis_size("ctx")
    lanes = lax.axis_size("tp")
    micros, rows, width = block_input.shape
    span_rows = rows * lanes
    heads = triple_weight.shape[2]
    head_dim = triple_weight.shape[4]
    across = heads * head_dim
    scale = head_dim ** (-0.5)
    first_section = section == 0
    both = (0, 1)

    def hop(array, axis, step, sections):
        size = lax.axis_size(axis)
        pairs = [(s * size + a, s * size + (a ^ step)) for s in sections for a in range(size)]
        return lax.ppermute(array, ("pipe", axis), pairs)

    def gather_ctx(array, sections=both):
        held, step = {0: array}, spans // 2
        while step:
            for k in list(held):
                held[k ^ step] = hop(held[k], "ctx", step, sections)
            step //= 2
        return [held[k] for k in doubling(spans)]

    def gather_tp(array, axis, sections):
        pieces, step = [array], lanes // 2
        while step:
            going = jnp.concatenate(pieces, axis=axis) if len(pieces) > 1 else array
            pieces.append(hop(going, "tp", step, sections))
            step //= 2
        return pieces

    def scatter(keep, send, axis_name, dim, sections, order=None):
        step, size = 1, lax.axis_size(axis_name)
        while True:
            came = hop(send, axis_name, step, sections)
            if order and step == 1:
                order.also(came)
            step *= 2
            if step == size:
                return keep, came
            middle = keep.shape[dim] // 2
            total = keep.astype(f32) + came.astype(f32)
            keep = lax.slice_in_dim(total, 0, middle, axis=dim).astype(bf16)
            send = lax.slice_in_dim(total, middle, 2 * middle, axis=dim).astype(bf16)

    order = Order()

    def flags_for(wanted):
        return jnp.stack([jnp.asarray(wanted), span, section]).astype(jnp.int32)

    flags = [flags_for(section == s) for s in both]
    always = flags_for(1)

    depth = width // spans
    assert depth == across
    small = jnp.concatenate([norm_gains[0], norm_biases[0]], axis=0)
    packed = jnp.concatenate(
        [triple_weight[0].reshape(depth, 3 * across), output_weight[0].reshape(across, depth)],
        axis=1,
    )
    packed = jnp.pad(packed, ((0, 16), (0, 0)))
    packed = lax.dynamic_update_slice(packed, small, (depth, 0))
    packed = gather_ctx(packed)
    small_full = jnp.concatenate(
        [piece[depth : depth + 4, :depth] for piece in packed], axis=1
    ).astype(f32)
    gains, biases = small_full[:2], small_full[2:]
    inputs = xor_blocks(block_input, span, spans)
    cotangent = xor_blocks(out_grad, span, spans)
    early = jnp.where(first_section, inputs, cotangent)
    early_pieces = gather_tp(early, 1, both)
    expand = gather_ctx(expand_weight[0])
    contract = gather_ctx(contract_weight[0])

    in_row = jnp.arange(rows, dtype=jnp.int32)
    in_span = jnp.concatenate([(lane ^ j) * rows + in_row for j in doubling(lanes)])
    positions = span * span_rows + in_span
    key_positions = jnp.stack([k * span_rows + in_span for k in range(spans)])
    tables = rope_tables(positions)
    position_column = positions[:, None]
    key_positions = key_positions[:, None, :]

    def scatter_wide(keep, send, dim):
        came = hop(send, "ctx", 1, both)

        def finished():
            held, arrived, step = keep, came, 2
            while step < spans:
                held, going = fold(order, always, held, arrived, dim)
                arrived = hop(going, "ctx", step, both)
                step *= 2
            return held.astype(f32) + arrived.astype(f32)

        return finished

    def start_forward(pieces, s):
        first, second, normal, queries, pair = project(
            order, flags[s], pieces, gains, biases, tables, packed, heads, head_dim
        )
        pairs = lax.all_gather(pair, "ctx", axis=0, tiled=False)
        return dict(first=first, second=second, normal=normal, queries=queries, pairs=pairs)

    def run_expand(kept, s):
        kept["active"], kept["slope"] = expand_up(
            order, flags[s], kept["second"], expand, span_rows
        )

    def run_attend(kept, s):
        kept["attended"], kept["probs"] = attend(
            order,
            flags[s],
            kept["queries"],
            kept["pairs"],
            position_column,
            key_positions,
            scale,
            span_rows,
        )

    def run_attend_back(pieces, at_piece, kept, m, s):
        upstream, turned_back, keep, send = attend_back(
            order,
            flags[s],
            pieces,
            packed,
            kept["queries"],
            kept["pairs"],
            kept["probs"],
            tables,
            scale,
            m,
            at_piece,
        )
        own, came = scatter(keep, send, "ctx", 0, (s,))
        return dict(
            upstream=upstream,
            turned_back=turned_back,
            own=own.reshape(own.shape[1:]),
            came=came.reshape(came.shape[1:]),
        )

    def run_hidden_back(kept, made, m, s):
        made["hidden"], made["part"], made["side_second"] = hidden_back(
            order,
            flags[s],
            made["upstream"],
            contract,
            expand,
            kept["slope"],
            kept["normal"],
            gains,
            m,
        )

    def run_project_back(kept, made, m, s):
        made["stacked"], low, high, made["side_first"] = project_back(
            order,
            flags[s],
            made["turned_back"],
            made["own"],
            made["came"],
            packed,
            made["part"],
            kept["normal"],
            gains,
            tables,
            m,
        )
        return low, high

    def total_of(pair):
        return pair[0].astype(f32) + pair[1].astype(f32)

    def norm_back(upstream, combined, entering):
        normalized, inverse = normalize(entering.astype(f32))
        return (
            upstream.astype(f32)
            + inverse
            * (
                combined
                - jnp.mean(combined, axis=-1, keepdims=True)
                - normalized * jnp.mean(combined * normalized, axis=-1, keepdims=True)
            )
        ).astype(bf16)

    kept_first = start_forward(early_pieces, 0)
    run_expand(kept_first, 0)
    run_attend(kept_first, 0)
    middle, arrived, arrived_pieces = [], [], []
    for m in range(micros):
        low, high = branch_out(
            order,
            flags[0],
            [(kept_first["active"], kept_first["attended"], m)],
            contract,
            packed,
            span_rows,
        )
        keep, came = scatter(low[0], high[0], "tp", 0, (0,), order)
        middle.append((inputs[m].astype(f32) + total_of((keep, came))).astype(bf16))
        arrived.append(lax.ppermute(middle[m], "pipe", [(0, 1)]))
        arrived_pieces.append([piece[None] for piece in gather_tp(arrived[m], 0, (1,))])

    kept_second = [None] * micros
    made_second = [None] * micros
    own_entries, relay, relay_pieces = [], [], []

    def second_project(m):
        kept_second[m] = start_forward(arrived_pieces[m], 1)

    def second_expand(m):
        run_expand(kept_second[m], 1)

    def second_attend(m):
        run_attend(kept_second[m], 1)

    def second_attend_back(m):
        made_second[m] = run_attend_back(early_pieces, m, kept_second[m], 0, 1)

    def second_hidden_back(m):
        run_hidden_back(kept_second[m], made_second[m], 0, 1)

    def second_project_back(m):
        low, high = run_project_back(kept_second[m], made_second[m], 0, 1)
        total = total_of(scatter(low, high, "tp", 0, (1,)))
        own_entries.append(norm_back(cotangent[m], total, arrived[m]))
        relay.append(lax.ppermute(own_entries[m], "pipe", [(1, 0)]))
        relay_pieces.append([piece[None] for piece in gather_tp(relay[m], 0, (0,))])

    steps = [second_project, second_expand, second_attend, second_attend_back]
    steps += [second_hidden_back, second_project_back]
    plan = sorted((3 * m + s, m, s) for m in range(micros) for s in range(len(steps)))
    for _, m, s in plan:
        steps[s](m)

    made_first, ends = [], []

    def sums(lefts, rights, by_rows):
        keep, send = weight_sums(order, always, lefts, rights, by_rows, spans)
        return scatter_wide(keep, send, 0 if by_rows else 1)

    def of(name, kepts):
        return [kept[name] for kept in kepts]

    for m in range(micros):
        last = m == micros - 1
        if last:
            lows, highs = branch_out(
                order,
                flags[1],
                [(kept["active"], kept["attended"], 0) for kept in kept_second],
                contract,
                packed,
                span_rows,
            )
            final_sum = total_of(scatter(lows, highs, "tp", 1, (1,)))
            pieces = [piece[0] for piece in relay_pieces[m]]
            branch_grads = sums(
                [
                    [of("active", [kept_first]), of("attended", [kept_first])],
                    [of("active", kept_second), of("attended", kept_second)],
                ],
                [[of("upstream", made_first) + pieces], [of("upstream", made_second)]],
                False,
            )
        made_first.append(run_attend_back(relay_pieces[m], 0, kept_first, m, 0))
        if last:
            branch_grads = branch_grads()
        run_hidden_back(kept_first, made_first[m], m, 0)
        if last:
            expand_grads = sums(
                [[of("second", [kept_first])], [of("second", kept_second)]],
                [[of("hidden", made_first)], [of("hidden", made_second)]],
                True,
            )
        ends.append(run_project_back(kept_first, made_first[m], m, 0))
    expand_grads = expand_grads()
    triple_grads = sums(
        [[of("first", [kept_first])], [of("first", kept_second)]],
        [[of("stacked", made_first)], [of("stacked", made_second)]],
        True,
    )()
    end_sum = total_of(
        scatter(
            jnp.stack([low for low, _ in ends]),
            jnp.stack([high for _, high in ends]),
            "tp",
            1,
            (0,),
        )
    )
    hidden = expand_weight.shape[2]
    contract_grads, output_grads = branch_grads[:hidden], branch_grads[hidden:]
    entering = jnp.stack(arrived).astype(f32)
    layer_outputs = jnp.where(
        first_section, jnp.stack(middle), (entering + final_sum).astype(bf16)
    )
    entry_grads = jnp.where(
        first_section, norm_back(jnp.stack(relay), end_sum, inputs), jnp.stack(own_entries)
    )

    def side_of(mades):
        return sum(
            jnp.concatenate([made["side_first"], made["side_second"]], axis=0) for made in mades
        )

    side_first, side_second = side_of(made_first), side_of(made_second)
    side = jnp.where(first_section, side_first, side_second)
    step = 1
    while step < spans:
        middle_column = side.shape[1] // 2
        side = side[:, :middle_column] + hop(side[:, middle_column:], "ctx", step, both)
        step *= 2
    step = 1
    while step < lanes:
        side = side + hop(side, "tp", step, both)
        step *= 2
    gain_grads = jnp.stack([side[0], side[2]])
    bias_grads = jnp.stack([side[1], side[3]])
    return (
        xor_blocks(layer_outputs, span, spans, inverse=True)[None],
        xor_blocks(entry_grads, span, spans, inverse=True)[None],
        triple_grads.reshape(triple_weight.shape),
        output_grads.reshape(output_weight.shape),
        expand_grads[None],
        contract_grads[None],
        gain_grads[None],
        bias_grads[None],
    )


def solution(mesh):
    return jax.shard_map(
        shards,
        mesh=mesh,
        in_specs=(
            P(None, ("ctx", "tp"), None),
            P(None, ("ctx", "tp"), None),
            P("pipe", "ctx", "tp", None, None),
            P("pipe", "tp", None, "ctx"),
            P("pipe", "ctx", "tp"),
            P("pipe", "tp", "ctx"),
            P("pipe", None, "ctx"),
            P("pipe", None, "ctx"),
        ),
        out_specs=(
            P("pipe", None, ("ctx", "tp"), None),
            P("pipe", None, ("ctx", "tp"), None),
            P("pipe", "ctx", "tp", None, None),
            P("pipe", "tp", None, "ctx"),
            P("pipe", "ctx", "tp"),
            P("pipe", "tp", "ctx"),
            P("pipe", None, "ctx"),
            P("pipe", None, "ctx"),
        ),
        check_vma=False,
    )
```

```python
import functools
from types import SimpleNamespace

import jax
import jax.numpy as jnp
from jax import lax
from jax.experimental import pallas as pl
from jax.experimental.pallas import tpu as pltpu
from jax.sharding import PartitionSpec as P

ROT = 64
LANES = 128
epsilon = 1e-05
masked_score = -1e30
f32 = jnp.float32
bf16 = jnp.bfloat16
vmem_bytes = 56 * 1024 * 1024
half_root = 0.7071067811865476
bell = 0.3989422804014327


def dot(a, b, dims):
    return lax.dot_general(a, b, (dims, ((), ())), preferred_element_type=f32)


def plain(a, b):
    return dot(a, b, ((1,), (0,)))


def turned(a, b):
    return dot(a, b, ((1,), (1,)))


def doubling(count):
    order, step = [0], count // 2
    while step:
        order += [k ^ step for k in order]
        step //= 2
    return order


def xor_blocks(values, index, count, inverse=False):
    width = values.shape[-1] // count
    order = doubling(count)

    def taken(places):
        return jnp.concatenate(
            [values[..., k * width : (k + 1) * width] for k in places], axis=-1
        )

    if inverse:
        values = taken([order.index(k) for k in range(count)])
    step = 1
    while step < count:
        swapped = taken([k ^ step for k in range(count)])
        values = jnp.where((index & step) != 0, swapped, values)
        step *= 2
    return values if inverse else taken(order)


def rope_tables(positions):
    half = ROT // 2
    frequency = 10000.0 ** (-jnp.arange(0, ROT, 2, dtype=f32) / ROT)
    angles = positions.astype(f32)[:, None] * frequency[None, :]
    cosine, sine = jnp.cos(angles), jnp.sin(angles)
    count = positions.shape[0]
    rest = jnp.zeros((count, LANES - ROT), f32)
    none = jnp.zeros((count, half), f32)
    return jnp.stack(
        [
            jnp.concatenate([cosine, cosine, rest + 1.0], axis=1),
            jnp.concatenate([-sine, none, rest], axis=1),
            jnp.concatenate([none, sine, rest], axis=1),
        ]
    )


def turn(values, tables, sign):
    half = ROT // 2
    part = values[:, :LANES]
    moved = (
        pltpu.roll(part, LANES - half, 1) * tables[1] + pltpu.roll(part, half, 1) * tables[2]
    )
    part = part * tables[0] + (moved if sign > 0 else -moved)
    return jnp.concatenate([part, values[:, LANES:]], axis=1)


def normalize(values):
    center = values - jnp.mean(values, axis=-1, keepdims=True)
    inverse = lax.rsqrt(jnp.mean(center * center, axis=-1, keepdims=True) + epsilon)
    return (center * inverse, inverse)


def whole(array):
    zeros = (0,) * array.ndim
    return pl.BlockSpec(array.shape, lambda *_: zeros)


def at(block, place):
    return pl.BlockSpec(block, lambda *_: place)


kept_out = pl.BlockSpec(memory_space=pl.ANY)


def shape(dims, dtype=bf16):
    return jax.ShapeDtypeStruct(dims, dtype)


class Order:
    def __init__(self):
        self.last = []

    def follow(self, results):
        self.last = [min(results, key=lambda array: array.size * array.dtype.itemsize)]

    def also(self, array):
        self.last = self.last + [array]


took = dict(
    project=7,
    expand=8,
    attend=5,
    branch=8,
    hidden_both=14,
    attend_both=11,
    attend_back=8,
    hidden_back=13,
    project_back=8,
    weight_sums=16,
    fold=7,
)
peak = 1.15e9


def run(order, flags, kernel, ins, outs, scratch, name, grid=(1,)):
    taken = len(ins)
    ins = [(flags, pl.BlockSpec(memory_space=pltpu.SMEM))] + list(ins)
    ins += [(array, kept_out) for array in order.last]
    arrays = [array for array, _ in ins]

    def body(flag_ref, *refs):
        @pl.when(flag_ref[0] == 1)
        def _():
            kernel(flag_ref, *refs[:taken], *refs[len(ins) - 1 :])

    results = pl.pallas_call(
        body,
        grid=grid,
        in_specs=[spec for _, spec in ins],
        out_specs=[spec for _, spec in outs],
        out_shape=[struct for struct, _ in outs],
        scratch_shapes=scratch,
        compiler_params=pltpu.CompilerParams(vmem_limit_bytes=vmem_bytes),
        cost_estimate=pl.CostEstimate(
            flops=int(took[name] * peak), bytes_accessed=0, transcendentals=0
        ),
        name=name,
    )(*arrays)
    order.follow(results)
    return results


def fence(through, waits):
    count = len(through)

    def kernel(*refs):
        pass

    return pl.pallas_call(
        kernel,
        in_specs=[kept_out] * (count + len(waits)),
        out_specs=[kept_out] * count,
        out_shape=[shape(array.shape, array.dtype) for array in through],
        input_output_aliases={j: j for j in range(count)},
        compiler_params=pltpu.CompilerParams(vmem_limit_bytes=vmem_bytes),
        cost_estimate=pl.CostEstimate(flops=1, bytes_accessed=1, transcendentals=0),
        name="fence",
    )(*through, *waits)


def full_out(dims, dtype=bf16):
    zeros = (0,) * len(dims)
    return (shape(dims, dtype), pl.BlockSpec(dims, lambda *_: zeros))


def copies(sources, targets, sems):
    started = []
    for source, target, sem in zip(sources, targets, sems):
        copy = pltpu.make_async_copy(source, target, sem)
        copy.start()
        started.append(copy)
    return started


def project(order, flags, pieces, at_piece, gains, biases, tables, weights, heads, head_dim):
    count, width = 1, pieces[0].shape[2]
    span_rows = sum(piece.shape[1] for piece in pieces)
    rows = count * span_rows
    chunk = pieces[0].shape[1]
    spans = len(weights)
    depth = width // spans
    wide = 3 * head_dim
    columns = heads * wide

    def kernel(flag_ref, *refs):
        piece_refs = refs[: len(pieces)]
        gain_ref, bias_ref, table_ref = refs[len(pieces) : len(pieces) + 3]
        weight_refs = refs[len(pieces) + 3 : len(pieces) + 3 + spans]
        first, second, normal, queries, pair, held, sems = refs[len(pieces) + 3 + spans :]
        started = []
        for h in range(heads):
            started.append(
                copies(
                    [w.at[:depth, h * wide : (h + 1) * wide] for w in weight_refs],
                    [held.at[h, k * depth : (k + 1) * depth] for k in range(spans)],
                    [sems.at[h, k] for k in range(spans)],
                )
            )
        start = 0
        for piece_ref in piece_refs:
            chunks = piece_ref.shape[1] // chunk

            def one(i, _, piece_ref=piece_ref, start=start, chunks=chunks):
                m, c = i // chunks, i % chunks
                values = piece_ref[m, pl.ds(pl.multiple_of(c * chunk, chunk), chunk), :]
                normed, _ = normalize(values.astype(f32))
                to = pl.ds(
                    pl.multiple_of(m * span_rows + start + c * chunk, chunk), chunk
                )
                normal[to, :] = normed.astype(bf16)
                first[to, :] = (normed * gain_ref[0:1] + bias_ref[0:1]).astype(bf16)
                second[to, :] = (normed * gain_ref[1:2] + bias_ref[1:2]).astype(bf16)
                return 0

            lax.fori_loop(0, count * chunks, one, 0)
            start += piece_ref.shape[1]
        for h in range(heads):
            for copy in started[h]:
                copy.wait()

            def two(m, _, h=h):
                to = pl.ds(pl.multiple_of(m * span_rows, span_rows), span_rows)
                made = plain(first[to, :], held[h])
                queries[h, to, :] = turn(made[:, :head_dim], table_ref, 1).astype(bf16)
                pair[0, h, to, :] = turn(
                    made[:, head_dim : 2 * head_dim], table_ref, 1
                ).astype(bf16)
                pair[1, h, to, :] = made[:, 2 * head_dim :].astype(bf16)
                return 0

            lax.fori_loop(0, count, two, 0)

    ins = [(piece, at((1,) + piece.shape[1:], (at_piece, 0, 0))) for piece in pieces]
    ins += [(array, whole(array)) for array in (gains, biases, tables)]
    ins += [(w, kept_out) for w in weights]
    outs = [full_out((rows, width))] * 3 + [
        full_out((heads, rows, head_dim)),
        full_out((2, heads, rows, head_dim)),
    ]
    scratch = [
        pltpu.VMEM((heads, width, wide), bf16),
        pltpu.SemaphoreType.DMA((heads, spans)),
    ]
    return run(order, flags, kernel, ins, outs, scratch, "project")


def expand_up(order, flags, second, weights, span_rows):
    rows, width = second.shape
    depth, hidden = weights[0].shape
    spans = len(weights)
    tile = min(512, hidden)
    tiles = hidden // tile

    def kernel(flag_ref, *refs):
        second_ref, weight_refs = refs[0], refs[1 : 1 + spans]
        active, slope, held, sems = refs[1 + spans :]
        started = []
        for t in range(tiles):
            started.append(
                copies(
                    [w.at[:, t * tile : (t + 1) * tile] for w in weight_refs],
                    [held.at[t, k * depth : (k + 1) * depth] for k in range(spans)],
                    [sems.at[t, k] for k in range(spans)],
                )
            )
        for t in range(tiles):
            for copy in started[t]:
                copy.wait()

            def one(m, _, t=t):
                to = pl.ds(pl.multiple_of(m * span_rows, span_rows), span_rows)
                pre = plain(second_ref[to, :], held[t])
                risen = 0.5 * (1.0 + lax.erf(pre * half_root))
                columns = slice(t * tile, (t + 1) * tile)
                active[to, columns] = (pre * risen).astype(bf16)
                slope[to, columns] = (
                    risen + pre * jnp.exp(-0.5 * pre * pre) * bell
                ).astype(bf16)
                return 0

            lax.fori_loop(0, rows // span_rows, one, 0)

    ins = [(second, whole(second))] + [(w, kept_out) for w in weights]
    outs = [full_out((rows, hidden))] * 2
    scratch = [
        pltpu.VMEM((tiles, width, tile), bf16),
        pltpu.SemaphoreType.DMA((tiles, spans)),
    ]
    return run(order, flags, kernel, ins, outs, scratch, "expand")


def spread(refs):
    return [ref.at[j] for ref in refs for j in range(ref.shape[0])]


def attention(here, pairs, head, row_ref, key_ref, scale):
    scores = []
    for k, pair in enumerate(pairs):
        raw = turned(here, pair[0, head]) * scale
        scores.append(jnp.where(key_ref[k] <= row_ref[...], raw, masked_score))
    top = functools.reduce(
        jnp.maximum, [jnp.max(part, axis=1, keepdims=True) for part in scores]
    )
    scores = [jnp.exp(part - top) for part in scores]
    inverse = 1.0 / sum(jnp.sum(part, axis=1, keepdims=True) for part in scores)
    return [part * inverse for part in scores]


def attend(order, flags, queries, pairs, positions, key_positions, scale):
    heads, rows, head_dim = queries.shape
    spans = sum(pair.shape[0] for pair in pairs)

    def kernel(flag_ref, query_ref, *refs):
        views, refs = spread(refs[: len(pairs)]), refs[len(pairs) :]
        row_ref, key_ref, attended, probs = refs
        for h in range(heads):
            parts = attention(query_ref[h], views, h, row_ref, key_ref, scale)
            summed = None
            for k in range(spans):
                part = parts[k].astype(bf16)
                probs[k, h] = part
                term = plain(part, views[k][1, h])
                summed = term if summed is None else summed + term
            attended[:, h * head_dim : (h + 1) * head_dim] = summed.astype(bf16)

    ins = [
        (array, whole(array)) for array in (queries, *pairs, positions, key_positions)
    ]
    outs = [full_out((rows, heads * head_dim)), full_out((spans, heads, rows, rows))]
    return run(order, flags, kernel, ins, outs, [], "attend")


def attention_grads(grad, here, parts, views, head, keep, send, scale):
    half = keep.shape[0]
    grad_probs = [turned(grad, view[1, head]) for view in views]
    delta = sum(
        jnp.sum(part.astype(f32) * slope, axis=1, keepdims=True)
        for part, slope in zip(parts, grad_probs)
    )
    query_grad = None
    for k, view in enumerate(views):
        slopes = (parts[k].astype(f32) * (grad_probs[k] - delta)).astype(bf16)
        term = plain(slopes, view[0, head])
        query_grad = term if query_grad is None else query_grad + term
        side = keep if k < half else send
        side[k % half, 0, head] = (dot(slopes, here, ((0,), (0,))) * scale).astype(bf16)
        side[k % half, 1, head] = dot(parts[k].astype(bf16), grad, ((0,), (0,))).astype(bf16)
    return query_grad * scale


def attend_both(
    order, flags, rows_in, packed, queries, pairs, positions, key_positions, tables, scale
):
    heads, rows, head_dim = queries.shape
    width = rows_in.shape[1]
    spans = len(packed)
    across, depth = heads * head_dim, width // spans
    half = spans // 2

    def kernel(flag_ref, rows_ref, *refs):
        packed_refs, refs = refs[:spans], refs[spans:]
        query_ref, refs = refs[0], refs[1:]
        views, refs = spread(refs[: len(pairs)]), refs[len(pairs) :]
        row_ref, key_ref, table_ref, attended, turned_back, keep, send, held, sems = refs
        started = copies(
            [w.at[:across, 3 * across : 3 * across + depth] for w in packed_refs],
            [held.at[:, k * depth : (k + 1) * depth] for k in range(spans)],
            [sems.at[k] for k in range(spans)],
        )
        all_parts = []
        for h in range(heads):
            parts = attention(query_ref[h], views, h, row_ref, key_ref, scale)
            summed = None
            for k in range(spans):
                term = plain(parts[k].astype(bf16), views[k][1, h])
                summed = term if summed is None else summed + term
            attended[:, h * head_dim : (h + 1) * head_dim] = summed.astype(bf16)
            all_parts.append(parts)
        for copy in started:
            copy.wait()
        grads = turned(rows_ref[...], held[...]).astype(bf16)
        for h in range(heads):
            made = attention_grads(
                grads[:, h * head_dim : (h + 1) * head_dim],
                query_ref[h],
                all_parts[h],
                views,
                h,
                keep,
                send,
                scale,
            )
            turned_back[h] = turn(made, table_ref, -1).astype(bf16)

    ins = [(rows_in, whole(rows_in))] + [(w, kept_out) for w in packed]
    ins += [
        (array, whole(array)) for array in (queries, *pairs, positions, key_positions, tables)
    ]
    outs = [full_out((rows, across)), full_out((heads, rows, head_dim))]
    outs += [full_out((half, 2, heads, rows, head_dim))] * 2
    scratch = [pltpu.VMEM((across, width), bf16), pltpu.SemaphoreType.DMA((spans,))]
    return run(order, flags, kernel, ins, outs, scratch, "attend_both")


def hidden_both(order, flags, second, pieces, at_piece, expand, contract, normal, gains):
    rows, width = second.shape
    hidden, depth = contract[0].shape
    spans = len(contract)
    tile = min(512, hidden)
    tiles = hidden // tile

    def kernel(flag_ref, second_ref, *refs):
        piece_refs, refs = refs[: len(pieces)], refs[len(pieces) :]
        expand_refs, refs = refs[:spans], refs[spans:]
        contract_refs, refs = refs[:spans], refs[spans:]
        normal_ref, gain_ref, rows_out, active, grads, part, side, *refs = refs
        held_up, held_down, sems_up, sems_down = refs
        started = []
        for t in range(tiles):
            block = slice(t * tile, (t + 1) * tile)
            places = [slice(k * depth, (k + 1) * depth) for k in range(spans)]
            up = copies(
                [w.at[:, block] for w in expand_refs],
                [held_up.at[place, block] for place in places],
                [sems_up.at[t, k] for k in range(spans)],
            )
            down = copies(
                [w.at[block, :] for w in contract_refs],
                [held_down.at[block, place] for place in places],
                [sems_down.at[t, k] for k in range(spans)],
            )
            started.append((up, down))
        start = 0
        for piece_ref in piece_refs:
            size = piece_ref.shape[1]
            rows_out[start : start + size, :] = piece_ref[0]
            start += size
        for t in range(tiles):
            block = slice(t * tile, (t + 1) * tile)
            for copy in started[t][0] + started[t][1]:
                copy.wait()
            pre = plain(second_ref[...], held_up[:, block])
            risen = 0.5 * (1.0 + lax.erf(pre * half_root))
            active[:, block] = (pre * risen).astype(bf16)
            slope = risen + pre * jnp.exp(-0.5 * pre * pre) * bell
            grads[:, block] = (turned(rows_out[...], held_down[block, :]) * slope).astype(bf16)
        for k in range(spans):
            place = slice(k * depth, (k + 1) * depth)
            made = turned(grads[...], held_up[place, :])
            side[0:1, place] = jnp.sum(
                made * normal_ref[:, place].astype(f32), axis=0, keepdims=True
            )
            side[1:2, place] = jnp.sum(made, axis=0, keepdims=True)
            part[:, place] = made * gain_ref[1:2, place]

    ins = [(second, whole(second))]
    ins += [(piece, at((1,) + piece.shape[1:], (at_piece, 0, 0))) for piece in pieces]
    ins += [(w, kept_out) for w in expand] + [(w, kept_out) for w in contract]
    ins += [(normal, whole(normal)), (gains, whole(gains))]
    outs = [
        full_out((rows, width)),
        full_out((rows, hidden)),
        full_out((rows, hidden)),
        full_out((rows, width), f32),
        full_out((2, width), f32),
    ]
    scratch = [
        pltpu.VMEM((width, hidden), bf16),
        pltpu.VMEM((hidden, width), bf16),
        pltpu.SemaphoreType.DMA((tiles, spans)),
        pltpu.SemaphoreType.DMA((tiles, spans)),
    ]
    return run(order, flags, kernel, ins, outs, scratch, "hidden_both")


def branch_out(order, flags, groups, contract, packed, span_rows):
    hidden, depth = contract[0].shape
    across = groups[0][1].shape[1]
    spans = len(contract)
    width = depth * spans
    half = span_rows // 2
    count = len(groups)

    def kernel(flag_ref, *refs):
        group_refs, refs = refs[: 2 * count], refs[2 * count :]
        contract_refs, packed_refs = refs[:spans], refs[spans : 2 * spans]
        low, high, held, held_out, sems = refs[2 * spans :]
        outputs = [w.at[:across, 3 * across : 3 * across + depth] for w in packed_refs]
        started = copies(
            [ref for k in range(spans) for ref in (outputs[k], contract_refs[k])],
            [ref for k in range(spans) for ref in (held_out.at[k], held.at[k])],
            [sems.at[j] for j in range(2 * spans)],
        )
        for k in range(spans):
            started[2 * k].wait()
            started[2 * k + 1].wait()
            columns = slice(k * depth, (k + 1) * depth)
            for c in range(count):
                made = plain(group_refs[2 * c + 1][...], held_out[k])
                made = made + plain(group_refs[2 * c][...], held[k])
                low[c, :, columns] = made[:half].astype(bf16)
                high[c, :, columns] = made[half:].astype(bf16)

    ins = []
    for active, attended, m in groups:
        ins += [
            (active, at((span_rows, hidden), (m, 0))),
            (attended, at((span_rows, across), (m, 0))),
        ]
    ins += [(w, kept_out) for w in contract] + [(w, kept_out) for w in packed]
    outs = [full_out((count, half, width))] * 2
    scratch = [
        pltpu.VMEM((spans, hidden, depth), bf16),
        pltpu.VMEM((spans, across, depth), bf16),
        pltpu.SemaphoreType.DMA((2 * spans,)),
    ]
    return run(order, flags, kernel, ins, outs, scratch, "branch")


def attend_back(order, flags, pieces, packed, queries, pairs, probs, tables, scale):
    rows = sum(piece.shape[1] for piece in pieces)
    width = pieces[0].shape[2]
    heads, _, head_dim = queries.shape
    spans = len(packed)
    across, depth = heads * head_dim, width // spans
    half = spans // 2

    def kernel(flag_ref, *refs):
        piece_refs, refs = refs[: len(pieces)], refs[len(pieces) :]
        packed_refs, refs = refs[:spans], refs[spans:]
        query_ref, refs = refs[0], refs[1:]
        views, refs = spread(refs[: len(pairs)]), refs[len(pairs) :]
        prob_ref, table_ref, rows_out, turned_back, keep, send, held, sems = refs
        started = copies(
            [w.at[:across, 3 * across : 3 * across + depth] for w in packed_refs],
            [held.at[:, k * depth : (k + 1) * depth] for k in range(spans)],
            [sems.at[k] for k in range(spans)],
        )
        start = 0
        for piece_ref in piece_refs:
            size = piece_ref.shape[1]
            rows_out[start : start + size, :] = piece_ref[0]
            start += size
        for copy in started:
            copy.wait()
        grads = turned(rows_out[...], held[...]).astype(bf16)
        for h in range(heads):
            made = attention_grads(
                grads[:, h * head_dim : (h + 1) * head_dim],
                query_ref[h],
                [prob_ref[k, h] for k in range(spans)],
                views,
                h,
                keep,
                send,
                scale,
            )
            turned_back[h] = turn(made, table_ref, -1).astype(bf16)

    ins = [(piece, whole(piece)) for piece in pieces] + [(w, kept_out) for w in packed]
    ins += [(array, whole(array)) for array in (queries, *pairs, probs, tables)]
    outs = [full_out((rows, width)), full_out((heads, rows, head_dim))]
    outs += [full_out((half, 2, heads, rows, head_dim))] * 2
    scratch = [pltpu.VMEM((across, width), bf16), pltpu.SemaphoreType.DMA((spans,))]
    return run(order, flags, kernel, ins, outs, scratch, "attend_back")


def hidden_back(order, flags, upstream, contract, expand, slope, normal, gains):
    span_rows, width = upstream.shape
    hidden, depth = contract[0].shape
    spans = len(contract)
    tile = min(512, hidden)
    tiles = hidden // tile

    def kernel(flag_ref, *refs):
        upstream_ref, refs = refs[0], refs[1:]
        contract_refs, refs = refs[:spans], refs[spans:]
        expand_refs, refs = refs[:spans], refs[spans:]
        slope_ref, normal_ref, gain_ref, grads, part, side, held, held_up, sems, sems_up = refs
        started = [
            copies(
                [w.at[t * tile : (t + 1) * tile, :] for w in contract_refs],
                [held.at[t, :, k * depth : (k + 1) * depth] for k in range(spans)],
                [sems.at[t, k] for k in range(spans)],
            )
            for t in range(tiles)
        ]
        started_up = copies(
            expand_refs, [held_up.at[k] for k in range(spans)], [sems_up.at[k] for k in range(spans)]
        )
        for t in range(tiles):
            for copy in started[t]:
                copy.wait()
            columns = slice(t * tile, (t + 1) * tile)
            grads[:, columns] = (
                turned(upstream_ref[...], held[t]) * slope_ref[:, columns].astype(f32)
            ).astype(bf16)
        for k in range(spans):
            started_up[k].wait()
            made = turned(grads[...], held_up[k])
            columns = slice(k * depth, (k + 1) * depth)
            side[0:1, columns] = jnp.sum(
                made * normal_ref[:, columns].astype(f32), axis=0, keepdims=True
            )
            side[1:2, columns] = jnp.sum(made, axis=0, keepdims=True)
            part[:, columns] = made * gain_ref[1:2, columns]

    ins = [(upstream, whole(upstream))]
    ins += [(w, kept_out) for w in contract] + [(w, kept_out) for w in expand]
    ins += [
        (slope, whole(slope)),
        (normal, whole(normal)),
        (gains, whole(gains)),
    ]
    outs = [
        full_out((span_rows, hidden)),
        full_out((span_rows, width), f32),
        full_out((2, width), f32),
    ]
    scratch = [
        pltpu.VMEM((tiles, tile, width), bf16),
        pltpu.VMEM((spans, depth, hidden), bf16),
        pltpu.SemaphoreType.DMA((tiles, spans)),
        pltpu.SemaphoreType.DMA((spans,)),
    ]
    return run(order, flags, kernel, ins, outs, scratch, "hidden_back")


def project_back(order, flags, turned_back, own, came, weights, part, normal, gains, tables):
    heads, span_rows, head_dim = turned_back.shape
    spans = len(weights)
    width = part.shape[1]
    depth, columns = width // spans, 3 * heads * head_dim
    half = span_rows // 2

    def kernel(flag_ref, *refs):
        query_ref, own_ref, came_ref, refs = refs[0], refs[1], refs[2], refs[3:]
        weight_refs, refs = refs[:spans], refs[spans:]
        part_ref, normal_ref, gain_ref, table_ref, grads, low, high, side, held, sems = refs
        started = copies(
            [w.at[:depth, :columns] for w in weight_refs],
            [held.at[k] for k in range(spans)],
            [sems.at[k] for k in range(spans)],
        )
        for h in range(heads):
            at_column = h * 3 * head_dim
            keys = own_ref[0, h].astype(f32) + came_ref[0, h].astype(f32)
            values = own_ref[1, h].astype(f32) + came_ref[1, h].astype(f32)
            grads[:, at_column : at_column + head_dim] = query_ref[h]
            grads[:, at_column + head_dim : at_column + 2 * head_dim] = turn(
                keys, table_ref, -1
            ).astype(bf16)
            grads[:, at_column + 2 * head_dim : at_column + 3 * head_dim] = values.astype(bf16)
        for k in range(spans):
            started[k].wait()
            made = turned(grads[...], held[k])
            span_columns = slice(k * depth, (k + 1) * depth)
            side[0:1, span_columns] = jnp.sum(
                made * normal_ref[:, span_columns].astype(f32), axis=0, keepdims=True
            )
            side[1:2, span_columns] = jnp.sum(made, axis=0, keepdims=True)
            both = (made * gain_ref[0:1, span_columns] + part_ref[:, span_columns]).astype(bf16)
            low[:, span_columns] = both[:half]
            high[:, span_columns] = both[half:]

    ins = [(array, whole(array)) for array in (turned_back, own, came)]
    ins += [(w, kept_out) for w in weights]
    ins += [(part, whole(part)), (normal, whole(normal))]
    ins += [(gains, whole(gains)), (tables, whole(tables))]
    outs = [full_out((span_rows, columns))] + [full_out((half, width))] * 2
    outs += [full_out((2, width), f32)]
    scratch = [pltpu.VMEM((spans, depth, columns), bf16), pltpu.SemaphoreType.DMA((spans,))]
    return run(order, flags, kernel, ins, outs, scratch, "project_back")


def weight_sums(order, flags, lefts, rights, by_rows, spans):
    rows = sum(piece.shape[0] for piece in lefts[0][0])
    left_width = sum(group[0].shape[1] for group in lefts[0])
    right_width = sum(group[0].shape[1] for group in rights[0])
    if by_rows:
        tile = left_width // spans
        steps, block = spans // 2, (tile, right_width)
    else:
        tile = min(512, left_width)
        while left_width % tile:
            tile //= 2
        steps, block = left_width // tile, (tile, right_width // 2)
    chunk = min(1024, block[1])
    while right_width % chunk:
        chunk //= 2
    pieces = [
        [piece for groups in (lefts[s], rights[s]) for group in groups for piece in group]
        for s in (0, 1)
    ]
    most = max(len(p) for p in pieces)

    def kernel(flag_ref, *refs):
        piece_refs = (refs[: len(pieces[0])], refs[len(pieces[0]) : len(pieces[0]) + len(pieces[1])])
        keep, send, left, right, flipped, sems = refs[len(pieces[0]) + len(pieces[1]) :]
        g = pl.program_id(0)
        for s in (0, 1):

            @pl.when((g == 0) & (flag_ref[2] == s))
            def _(s=s):
                targets = []
                for held, groups in ((left, lefts[s]), (right, rights[s])):
                    column = 0
                    for group in groups:
                        row, wide = 0, group[0].shape[1]
                        for piece in group:
                            targets.append(
                                held.at[row : row + piece.shape[0], column : column + wide]
                            )
                            row += piece.shape[0]
                        column += wide
                started = copies(
                    piece_refs[s], targets, [sems.at[j] for j in range(len(targets))]
                )
                for copy in started:
                    copy.wait()

        def product(column, store):
            flipped[...] = left[:, pl.ds(pl.multiple_of(column, LANES), tile)].T

            def one(c, _):
                columns = pl.ds(pl.multiple_of(c * chunk, chunk), chunk)
                store(c, plain(flipped[...], right[:, columns]).astype(bf16))
                return 0

            lax.fori_loop(0, right_width // chunk, one, 0)

        if by_rows:

            def to(target):
                def store(c, made):
                    target[:, pl.ds(pl.multiple_of(c * chunk, chunk), chunk)] = made

                return store

            product(g * tile, to(keep))
            product((g + steps) * tile, to(send))
        else:
            half = right_width // 2 // chunk

            def store(c, made):
                @pl.when(c < half)
                def _():
                    keep[:, pl.ds(pl.multiple_of(c * chunk, chunk), chunk)] = made

                @pl.when(c >= half)
                def _():
                    send[:, pl.ds(pl.multiple_of((c - half) * chunk, chunk), chunk)] = made

            product(g * tile, store)

    ins = [(piece, kept_out) for s in (0, 1) for piece in pieces[s]]
    dims = (steps * tile, block[1])
    outs = [(shape(dims), pl.BlockSpec(block, lambda g: (g, 0)))] * 2
    scratch = [
        pltpu.VMEM((rows, left_width), bf16),
        pltpu.VMEM((rows, right_width), bf16),
        pltpu.VMEM((tile, rows), bf16),
        pltpu.SemaphoreType.DMA((most,)),
    ]
    return run(
        order, flags, kernel, ins, outs, scratch, "weight_sums", grid=(steps,)
    )


def fold(order, flags, keep, came, dim):
    rows, columns = keep.shape
    if dim == 0:
        tile = min(256, rows // 2)
        steps, block = rows // 2 // tile, (tile, columns)
        places = [lambda g: (g, 0), lambda g: (g + steps, 0)]
        half = (rows // 2, columns)
    else:
        tile = min(256, rows)
        steps, block = rows // tile, (tile, columns // 2)
        places = [lambda g: (g, 0), lambda g: (g, 1)]
        half = (rows, columns // 2)

    def kernel(flag_ref, keep_low, keep_high, came_low, came_high, low, high):
        low[...] = (keep_low[...].astype(f32) + came_low[...].astype(f32)).astype(bf16)
        high[...] = (keep_high[...].astype(f32) + came_high[...].astype(f32)).astype(bf16)

    ins = [(array, pl.BlockSpec(block, place)) for array in (keep, came) for place in places]
    outs = [(shape(half), pl.BlockSpec(block, lambda g: (g, 0)))] * 2
    return run(order, flags, kernel, ins, outs, [], "fold", grid=(steps,))


def shards(
    block_input,
    out_grad,
    triple_weight,
    output_weight,
    expand_weight,
    contract_weight,
    norm_gains,
    norm_biases,
):
    section = lax.axis_index("pipe")
    span = lax.axis_index("ctx")
    lane = lax.axis_index("tp")
    spans = lax.axis_size("ctx")
    lanes = lax.axis_size("tp")
    micros, rows, width = block_input.shape
    span_rows = rows * lanes
    heads = triple_weight.shape[2]
    head_dim = triple_weight.shape[4]
    across = heads * head_dim
    scale = head_dim ** (-0.5)
    first_section = section == 0
    both = (0, 1)

    def hop(array, axis, step, sections):
        size = lax.axis_size(axis)
        pairs = [(s * size + a, s * size + (a ^ step)) for s in sections for a in range(size)]
        return lax.ppermute(array, ("pipe", axis), pairs)

    def gather_ctx(array, first_came):
        held, step = {0: array, spans // 2: first_came}, spans // 4
        while step:
            for k in list(held):
                held[k ^ step] = hop(held[k], "ctx", step, both)
            step //= 2
        return [held[k] for k in doubling(spans)]

    def gather(array, axis, axis_name, sections, first_came=None):
        pieces, step = [array], lax.axis_size(axis_name) // 2
        if first_came is not None:
            pieces, step = [array, first_came], step // 2
        while step:
            going = jnp.concatenate(pieces, axis=axis) if len(pieces) > 1 else array
            pieces.append(hop(going, axis_name, step, sections))
            step //= 2
        return pieces

    def scatter(keep, send, axis_name, dim, sections, noted=None, name=None, gate=None):
        step, size = 1, lax.axis_size(axis_name)
        while True:
            came = hop(send, axis_name, step, sections)
            if noted is not None:
                setattr(noted, name + ("1" if step == 1 else "2"), came)
            if gate is not None and step == 1:
                came = fence([came], [gate])[0]
            step *= 2
            if step == size:
                return keep, came
            middle = keep.shape[dim] // 2
            total = keep.astype(f32) + came.astype(f32)
            keep = lax.slice_in_dim(total, 0, middle, axis=dim).astype(bf16)
            send = lax.slice_in_dim(total, middle, 2 * middle, axis=dim).astype(bf16)

    order = Order()

    def flags_for(wanted):
        return jnp.stack([jnp.asarray(wanted), span, section]).astype(jnp.int32)

    flags = [flags_for(section == s) for s in both]
    always = flags_for(1)

    depth = width // spans
    assert depth == across
    small = jnp.concatenate([norm_gains[0], norm_biases[0]], axis=0)
    packed = jnp.concatenate(
        [triple_weight[0].reshape(depth, 3 * across), output_weight[0].reshape(across, depth)],
        axis=1,
    )
    packed = jnp.pad(packed, ((0, 16), (0, 0)))
    packed = lax.dynamic_update_slice(packed, small, (depth, 0))
    inputs = xor_blocks(block_input, span, spans)
    cotangent = xor_blocks(out_grad, span, spans)
    early_pieces = gather(jnp.where(first_section, inputs, cotangent), 1, "tp", both)
    far = spans // 2
    packed_came, expand_came = fence(
        [hop(packed, "ctx", far, both), hop(expand_weight[0], "ctx", far, both)],
        early_pieces[-1:],
    )
    packed = gather_ctx(packed, packed_came)
    small_full = jnp.concatenate(
        [piece[depth : depth + 4, :depth] for piece in packed], axis=1
    ).astype(f32)
    gains, biases = small_full[:2], small_full[2:]
    expand = gather_ctx(expand_weight[0], expand_came)

    in_row = jnp.arange(rows, dtype=jnp.int32)
    in_span = jnp.concatenate([(lane ^ j) * rows + in_row for j in doubling(lanes)])
    positions = span * span_rows + in_span
    key_positions = jnp.stack([(span ^ k) * span_rows + in_span for k in doubling(spans)])
    tables = rope_tables(positions)
    position_column = positions[:, None]
    key_positions = key_positions[:, None, :]

    def scatter_wide(keep, send, dim):
        came = hop(send, "ctx", 1, both)

        def finished():
            held, arrived, step = keep, came, 2
            while step < spans:
                held, going = fold(order, always, held, arrived, dim)
                arrived = hop(going, "ctx", step, both)
                step *= 2
            return held.astype(f32) + arrived.astype(f32), arrived

        return finished

    def total_of(pair):
        return pair[0].astype(f32) + pair[1].astype(f32)

    def norm_back(upstream, combined, entering):
        normalized, inverse = normalize(entering.astype(f32))
        return (
            upstream.astype(f32)
            + inverse
            * (
                combined
                - jnp.mean(combined, axis=-1, keepdims=True)
                - normalized * jnp.mean(combined * normalized, axis=-1, keepdims=True)
            )
        ).astype(bf16)

    kept = [[SimpleNamespace() for _ in range(micros)] for _ in both]
    came = [[SimpleNamespace() for _ in range(micros)] for _ in both]

    def wait(s, m, name):
        if 0 <= m < micros:
            order.also(getattr(came[s][m], name))

    def run_project(s, m):
        k = kept[s][m]
        pieces, place = (early_pieces, m) if s == 0 else (k.arrived_pieces, 0)
        k.first, k.second, k.normal, k.queries, pair = project(
            order, flags[s], pieces, place, gains, biases, tables, packed, heads, head_dim
        )
        if s == 0:
            k.pairs = gather(pair[None], 0, "ctx", (s,))
        else:
            k.pair = pair[None]
            k.pair_came = hop(pair[None], "ctx", far, (s,))

    def run_expand(m):
        k = kept[0][m]
        k.active, k.slope = expand_up(order, flags[0], k.second, expand, span_rows)

    def run_attend(m):
        k = kept[0][m]
        k.attended, k.probs = attend(
            order, flags[0], k.queries, k.pairs, position_column, key_positions, scale
        )

    def run_branch(m):
        k = kept[0][m]
        low, high = branch_out(
            order, flags[0], [(k.active, k.attended, 0)], contract, packed, span_rows
        )
        total = total_of(scatter(low[0], high[0], "tp", 0, (0,), came[0][m], "sum"))
        k.middle = (inputs[m].astype(f32) + total).astype(bf16)

    def run_arrive(m, after=None):
        middle = kept[0][m].middle
        if after is not None:
            middle = fence([middle], [after])[0]
        arrived = lax.ppermute(middle, "pipe", [(0, 1)])
        kept[1][m].arrived = came[1][m].arrived = arrived
        pieces = gather(arrived, 0, "tp", (1,))
        came[1][m].arrived_far = pieces[1]
        kept[1][m].arrived_pieces = [piece[None] for piece in pieces]

    def run_hidden_both(m):
        k = kept[1][m]
        k.upstream, k.active, k.hidden, k.part, k.side_second = hidden_both(
            order, flags[1], k.second, early_pieces, m, expand, contract, k.normal, gains
        )
        pair_came = fence([k.pair_came], [k.side_second])[0]
        k.pairs = gather(k.pair, 0, "ctx", (1,), pair_came)

    def pair_grads(s, m, keep, send):
        own, arrived = scatter(keep, send, "ctx", 0, (s,), came[s][m], "pair_grad")
        kept[s][m].own = own.reshape(own.shape[1:])
        kept[s][m].came = arrived.reshape(arrived.shape[1:])

    def run_attend_both(m):
        k = kept[1][m]
        k.attended, k.turned_back, keep, send = attend_both(
            order,
            flags[1],
            k.upstream,
            packed,
            k.queries,
            k.pairs,
            position_column,
            key_positions,
            tables,
            scale,
        )
        pair_grads(1, m, keep, send)

    def run_attend_back(m):
        k = kept[0][m]
        k.upstream, k.turned_back, keep, send = attend_back(
            order,
            flags[0],
            k.relay_pieces,
            packed,
            k.queries,
            k.pairs,
            k.probs,
            tables,
            scale,
        )
        pair_grads(0, m, keep, send)

    def run_hidden_back(m):
        k = kept[0][m]
        k.hidden, k.part, k.side_second = hidden_back(
            order,
            flags[0],
            k.upstream,
            contract,
            expand,
            k.slope,
            k.normal,
            gains,
        )

    def run_project_back(s, m):
        k = kept[s][m]
        k.stacked, k.low, k.high, k.side_first = project_back(
            order,
            flags[s],
            k.turned_back,
            k.own,
            k.came,
            packed,
            k.part,
            k.normal,
            gains,
            tables,
        )

    def run_hand_back(m, before=None, gate=None):
        k = kept[1][m]
        send = k.high if before is None else fence([k.high], [before])[0]
        total = total_of(scatter(k.low, send, "tp", 0, (1,), came[1][m], "sum", gate))
        k.entry = norm_back(cotangent[m], total, k.arrived)
        relay = lax.ppermute(k.entry, "pipe", [(1, 0)])
        kept[0][m].relay = came[0][m].relay = relay
        pieces = gather(relay, 0, "tp", (0,))
        came[0][m].relay_far = pieces[1]
        kept[0][m].relay_pieces = [piece[None] for piece in pieces]

    def sums(lefts, rights, by_rows):
        keep, send = weight_sums(order, always, lefts, rights, by_rows, spans)
        return scatter_wide(keep, send, 0 if by_rows else 1)

    def of(name, s, count=micros):
        return [getattr(kept[s][m], name) for m in range(count)]

    contract_came = hop(contract_weight[0], "ctx", far, both)
    run_project(0, 0)
    run_expand(0)
    contract_came = fence([contract_came], [kept[0][0].slope])[0]
    contract = gather_ctx(contract_weight[0], contract_came)
    run_attend(0)
    run_branch(0)
    for m in range(1, micros + 1):
        wait(0, m - 1, "sum1")
        if m < micros:
            run_project(0, m)
            run_expand(m)
        if m >= 2:
            run_project(1, m - 2)
        wait(0, m - 1, "sum2")
        if m < micros:
            run_attend(m)
        if m >= 2:
            run_hidden_both(m - 2)
        run_arrive(m - 1, kept[1][m - 2].side_second if m >= 3 else None)
        wait(1, m - 1, "arrived")
        if m < micros:
            run_branch(m)
        if m >= 3:
            wait(1, m - 3, "pair_grad2")
            run_project_back(1, m - 3)
        if m != 2:
            wait(1, m - 1, "arrived_far")
        if m >= 2:
            run_attend_both(m - 2)
            wait(1, m - 2, "pair_grad1")
        if m >= 3:
            run_hand_back(m - 3, kept[1][m - 2].turned_back)
            wait(1, m - 3, "sum1")
    for m in range(micros - 1, micros + 1):
        if m < micros:
            run_project(1, m)
            wait(1, m - 2, "sum2")
            run_hidden_both(m)
            wait(0, m - 2, "relay")
        else:
            wait(1, m - 2, "sum2")
        run_project_back(1, m - 1)
        if m < micros:
            wait(0, m - 2, "relay_far")
            run_attend_both(m)
            wait(1, m, "pair_grad1")
            run_hand_back(m - 1, kept[1][m].turned_back)
            wait(1, m - 1, "sum1")
        else:
            run_hand_back(m - 1, gate=came[0][m - 2].relay)
    wait(0, micros - 2, "relay")
    last = micros - 1
    for m in range(last):
        run_attend_back(m)
        if m == 0:
            wait(1, last, "sum1")
            wait(0, 1, "relay_far")
        else:
            wait(0, m + 1, "relay_far")
        run_hidden_back(m)
        run_project_back(0, m)
        if m == 0:
            wait(1, last, "sum2")
            wait(0, last, "relay")
    lows, highs = branch_out(
        order,
        flags[1],
        [(k.active, k.attended, 0) for k in kept[1]],
        contract,
        packed,
        span_rows,
    )
    final_sum = total_of(scatter(lows, highs, "tp", 1, (1,)))
    branch_grads = sums(
        [[of("active", s), of("attended", s)] for s in both],
        [
            [of("upstream", 0, last) + [piece[0] for piece in kept[0][last].relay_pieces]],
            [of("upstream", 1)],
        ],
        False,
    )
    run_attend_back(last)
    branch_grads, branch_came = branch_grads()
    run_hidden_back(last)
    expand_grads = sums(
        [[of("second", s)] for s in both], [[of("hidden", s)] for s in both], True
    )
    expand_grads, expand_came = expand_grads()
    order.also(branch_came)
    run_project_back(0, last)
    triple_grads = sums(
        [[of("first", s)] for s in both], [[of("stacked", s)] for s in both], True
    )
    order.also(expand_came)
    triple_grads, _ = triple_grads()
    end_sum = total_of(
        scatter(jnp.stack(of("low", 0)), jnp.stack(of("high", 0)), "tp", 1, (0,))
    )
    hidden = expand_weight.shape[2]
    contract_grads, output_grads = branch_grads[:hidden], branch_grads[hidden:]
    entering = jnp.stack(of("arrived", 1)).astype(f32)
    layer_outputs = jnp.where(
        first_section, jnp.stack(of("middle", 0)), (entering + final_sum).astype(bf16)
    )
    entry_grads = jnp.where(
        first_section,
        norm_back(jnp.stack(of("relay", 0)), end_sum, inputs),
        jnp.stack(of("entry", 1)),
    )

    def side_of(mades):
        return sum(
            jnp.concatenate([k.side_first, k.side_second], axis=0) for k in mades
        )

    side_first, side_second = side_of(kept[0]), side_of(kept[1])
    side = jnp.where(first_section, side_first, side_second)
    step = 1
    while step < spans:
        middle_column = side.shape[1] // 2
        side = side[:, :middle_column] + hop(side[:, middle_column:], "ctx", step, both)
        step *= 2
    step = 1
    while step < lanes:
        side = side + hop(side, "tp", step, both)
        step *= 2
    gain_grads = jnp.stack([side[0], side[2]])
    bias_grads = jnp.stack([side[1], side[3]])
    return (
        xor_blocks(layer_outputs, span, spans, inverse=True)[None],
        xor_blocks(entry_grads, span, spans, inverse=True)[None],
        triple_grads.reshape(triple_weight.shape),
        output_grads.reshape(output_weight.shape),
        expand_grads[None],
        contract_grads[None],
        gain_grads[None],
        bias_grads[None],
    )


def solution(mesh):
    return jax.shard_map(
        shards,
        mesh=mesh,
        in_specs=(
            P(None, ("ctx", "tp"), None),
            P(None, ("ctx", "tp"), None),
            P("pipe", "ctx", "tp", None, None),
            P("pipe", "tp", None, "ctx"),
            P("pipe", "ctx", "tp"),
            P("pipe", "tp", "ctx"),
            P("pipe", None, "ctx"),
            P("pipe", None, "ctx"),
        ),
        out_specs=(
            P("pipe", None, ("ctx", "tp"), None),
            P("pipe", None, ("ctx", "tp"), None),
            P("pipe", "ctx", "tp", None, None),
            P("pipe", "tp", None, "ctx"),
            P("pipe", "ctx", "tp"),
            P("pipe", "tp", "ctx"),
            P("pipe", None, "ctx"),
            P("pipe", None, "ctx"),
        ),
        check_vma=False,
    )
```

```python
import functools
from types import SimpleNamespace

import jax
import jax.numpy as jnp
from jax import lax
from jax.experimental import pallas as pl
from jax.experimental.pallas import tpu as pltpu
from jax.sharding import PartitionSpec as P

ROT = 64
LANES = 128
epsilon = 1e-05
masked_score = -1e30
f32 = jnp.float32
bf16 = jnp.bfloat16
vmem_bytes = 56 * 1024 * 1024
half_root = 0.7071067811865476
bell = 0.3989422804014327


def dot(a, b, dims):
    return lax.dot_general(a, b, (dims, ((), ())), preferred_element_type=f32)


def plain(a, b):
    return dot(a, b, ((1,), (0,)))


def turned(a, b):
    return dot(a, b, ((1,), (1,)))


def doubling(count):
    order, step = [0], count // 2
    while step:
        order += [k ^ step for k in order]
        step //= 2
    return order


def xor_blocks(values, index, count, inverse=False):
    width = values.shape[-1] // count
    order = doubling(count)

    def taken(places):
        return jnp.concatenate(
            [values[..., k * width : (k + 1) * width] for k in places], axis=-1
        )

    if inverse:
        values = taken([order.index(k) for k in range(count)])
    step = 1
    while step < count:
        swapped = taken([k ^ step for k in range(count)])
        values = jnp.where((index & step) != 0, swapped, values)
        step *= 2
    return values if inverse else taken(order)


def rope_tables(positions):
    half = ROT // 2
    frequency = 10000.0 ** (-jnp.arange(0, ROT, 2, dtype=f32) / ROT)
    angles = positions.astype(f32)[:, None] * frequency[None, :]
    cosine, sine = jnp.cos(angles), jnp.sin(angles)
    count = positions.shape[0]
    rest = jnp.zeros((count, LANES - ROT), f32)
    none = jnp.zeros((count, half), f32)
    return jnp.stack(
        [
            jnp.concatenate([cosine, cosine, rest + 1.0], axis=1),
            jnp.concatenate([-sine, none, rest], axis=1),
            jnp.concatenate([none, sine, rest], axis=1),
        ]
    )


def turn(values, tables, sign):
    half = ROT // 2
    part = values[:, :LANES]
    moved = (
        pltpu.roll(part, LANES - half, 1) * tables[1] + pltpu.roll(part, half, 1) * tables[2]
    )
    part = part * tables[0] + (moved if sign > 0 else -moved)
    return jnp.concatenate([part, values[:, LANES:]], axis=1)


def normalize(values):
    center = values - jnp.mean(values, axis=-1, keepdims=True)
    inverse = lax.rsqrt(jnp.mean(center * center, axis=-1, keepdims=True) + epsilon)
    return (center * inverse, inverse)


def whole(array):
    zeros = (0,) * array.ndim
    return pl.BlockSpec(array.shape, lambda *_: zeros)


def at(block, place):
    return pl.BlockSpec(block, lambda *_: place)


kept_out = pl.BlockSpec(memory_space=pl.ANY)


def shape(dims, dtype=bf16):
    return jax.ShapeDtypeStruct(dims, dtype)


class Order:
    def __init__(self):
        self.last = []

    def follow(self, results):
        self.last = [min(results, key=lambda array: array.size * array.dtype.itemsize)]

    def also(self, array):
        self.last = self.last + [array]


took = dict(
    project=7,
    expand=8,
    attend=5,
    branch=8,
    hidden_both=14,
    attend_both=11,
    attend_back=8,
    hidden_back=13,
    project_back=8,
    weight_sums=16,
    fold=7,
)
peak = 1.15e9


def run(order, flags, kernel, ins, outs, scratch, name, grid=(1,)):
    taken = len(ins)
    ins = [(flags, pl.BlockSpec(memory_space=pltpu.SMEM))] + list(ins)
    ins += [(array, kept_out) for array in order.last]
    arrays = [array for array, _ in ins]

    def body(flag_ref, *refs):
        @pl.when(flag_ref[0] == 1)
        def _():
            kernel(flag_ref, *refs[:taken], *refs[len(ins) - 1 :])

    results = pl.pallas_call(
        body,
        grid=grid,
        in_specs=[spec for _, spec in ins],
        out_specs=[spec for _, spec in outs],
        out_shape=[struct for struct, _ in outs],
        scratch_shapes=scratch,
        compiler_params=pltpu.CompilerParams(vmem_limit_bytes=vmem_bytes),
        cost_estimate=pl.CostEstimate(
            flops=int(took[name] * peak), bytes_accessed=0, transcendentals=0
        ),
        name=name,
    )(*arrays)
    order.follow(results)
    return results


def fence(through, waits):
    count = len(through)

    def kernel(*refs):
        pass

    return pl.pallas_call(
        kernel,
        in_specs=[kept_out] * (count + len(waits)),
        out_specs=[kept_out] * count,
        out_shape=[shape(array.shape, array.dtype) for array in through],
        input_output_aliases={j: j for j in range(count)},
        compiler_params=pltpu.CompilerParams(vmem_limit_bytes=vmem_bytes),
        cost_estimate=pl.CostEstimate(flops=1, bytes_accessed=1, transcendentals=0),
        name="fence",
    )(*through, *waits)


def full_out(dims, dtype=bf16):
    zeros = (0,) * len(dims)
    return (shape(dims, dtype), pl.BlockSpec(dims, lambda *_: zeros))


def copies(sources, targets, sems):
    started = []
    for source, target, sem in zip(sources, targets, sems):
        copy = pltpu.make_async_copy(source, target, sem)
        copy.start()
        started.append(copy)
    return started


def project(order, flags, pieces, at_piece, gains, biases, tables, weights, heads, head_dim):
    count, width = 1, pieces[0].shape[2]
    span_rows = sum(piece.shape[1] for piece in pieces)
    rows = count * span_rows
    chunk = pieces[0].shape[1]
    spans = len(weights)
    depth = width // spans
    wide = 3 * head_dim
    columns = heads * wide

    def kernel(flag_ref, *refs):
        piece_refs = refs[: len(pieces)]
        gain_ref, bias_ref, table_ref = refs[len(pieces) : len(pieces) + 3]
        weight_refs = refs[len(pieces) + 3 : len(pieces) + 3 + spans]
        first, second, normal, queries, pair, held, sems = refs[len(pieces) + 3 + spans :]
        started = []
        for h in range(heads):
            started.append(
                copies(
                    [w.at[:depth, h * wide : (h + 1) * wide] for w in weight_refs],
                    [held.at[h, k * depth : (k + 1) * depth] for k in range(spans)],
                    [sems.at[h, k] for k in range(spans)],
                )
            )
        start = 0
        for piece_ref in piece_refs:
            chunks = piece_ref.shape[1] // chunk

            def one(i, _, piece_ref=piece_ref, start=start, chunks=chunks):
                m, c = i // chunks, i % chunks
                values = piece_ref[m, pl.ds(pl.multiple_of(c * chunk, chunk), chunk), :]
                normed, _ = normalize(values.astype(f32))
                to = pl.ds(
                    pl.multiple_of(m * span_rows + start + c * chunk, chunk), chunk
                )
                normal[to, :] = normed.astype(bf16)
                first[to, :] = (normed * gain_ref[0:1] + bias_ref[0:1]).astype(bf16)
                second[to, :] = (normed * gain_ref[1:2] + bias_ref[1:2]).astype(bf16)
                return 0

            lax.fori_loop(0, count * chunks, one, 0)
            start += piece_ref.shape[1]
        for h in range(heads):
            for copy in started[h]:
                copy.wait()

            def two(m, _, h=h):
                to = pl.ds(pl.multiple_of(m * span_rows, span_rows), span_rows)
                made = plain(first[to, :], held[h])
                queries[h, to, :] = turn(made[:, :head_dim], table_ref, 1).astype(bf16)
                pair[0, h, to, :] = turn(
                    made[:, head_dim : 2 * head_dim], table_ref, 1
                ).astype(bf16)
                pair[1, h, to, :] = made[:, 2 * head_dim :].astype(bf16)
                return 0

            lax.fori_loop(0, count, two, 0)

    ins = [(piece, at((1,) + piece.shape[1:], (at_piece, 0, 0))) for piece in pieces]
    ins += [(array, whole(array)) for array in (gains, biases, tables)]
    ins += [(w, kept_out) for w in weights]
    outs = [full_out((rows, width))] * 3 + [
        full_out((heads, rows, head_dim)),
        full_out((2, heads, rows, head_dim)),
    ]
    scratch = [
        pltpu.VMEM((heads, width, wide), bf16),
        pltpu.SemaphoreType.DMA((heads, spans)),
    ]
    return run(order, flags, kernel, ins, outs, scratch, "project")


def expand_up(order, flags, second, weights, span_rows):
    rows, width = second.shape
    depth, hidden = weights[0].shape
    spans = len(weights)
    tile = min(512, hidden)
    tiles = hidden // tile

    def kernel(flag_ref, *refs):
        second_ref, weight_refs = refs[0], refs[1 : 1 + spans]
        active, slope, held, sems = refs[1 + spans :]
        started = []
        for t in range(tiles):
            started.append(
                copies(
                    [w.at[:, t * tile : (t + 1) * tile] for w in weight_refs],
                    [held.at[t, k * depth : (k + 1) * depth] for k in range(spans)],
                    [sems.at[t, k] for k in range(spans)],
                )
            )
        for t in range(tiles):
            for copy in started[t]:
                copy.wait()

            def one(m, _, t=t):
                to = pl.ds(pl.multiple_of(m * span_rows, span_rows), span_rows)
                pre = plain(second_ref[to, :], held[t])
                risen = 0.5 * (1.0 + lax.erf(pre * half_root))
                columns = slice(t * tile, (t + 1) * tile)
                active[to, columns] = (pre * risen).astype(bf16)
                slope[to, columns] = (
                    risen + pre * jnp.exp(-0.5 * pre * pre) * bell
                ).astype(bf16)
                return 0

            lax.fori_loop(0, rows // span_rows, one, 0)

    ins = [(second, whole(second))] + [(w, kept_out) for w in weights]
    outs = [full_out((rows, hidden))] * 2
    scratch = [
        pltpu.VMEM((tiles, width, tile), bf16),
        pltpu.SemaphoreType.DMA((tiles, spans)),
    ]
    return run(order, flags, kernel, ins, outs, scratch, "expand")


def spread(refs):
    return [ref.at[j] for ref in refs for j in range(ref.shape[0])]


def attention(here, pairs, head, row_ref, key_ref, scale):
    scores = []
    for k, pair in enumerate(pairs):
        raw = turned(here, pair[0, head]) * scale
        scores.append(jnp.where(key_ref[k] <= row_ref[...], raw, masked_score))
    top = functools.reduce(
        jnp.maximum, [jnp.max(part, axis=1, keepdims=True) for part in scores]
    )
    scores = [jnp.exp(part - top) for part in scores]
    inverse = 1.0 / sum(jnp.sum(part, axis=1, keepdims=True) for part in scores)
    return [part * inverse for part in scores]


def attend(order, flags, queries, pairs, positions, key_positions, scale):
    heads, rows, head_dim = queries.shape
    spans = sum(pair.shape[0] for pair in pairs)

    def kernel(flag_ref, query_ref, *refs):
        views, refs = spread(refs[: len(pairs)]), refs[len(pairs) :]
        row_ref, key_ref, attended, probs = refs
        for h in range(heads):
            parts = attention(query_ref[h], views, h, row_ref, key_ref, scale)
            summed = None
            for k in range(spans):
                part = parts[k].astype(bf16)
                probs[k, h] = part
                term = plain(part, views[k][1, h])
                summed = term if summed is None else summed + term
            attended[:, h * head_dim : (h + 1) * head_dim] = summed.astype(bf16)

    ins = [
        (array, whole(array)) for array in (queries, *pairs, positions, key_positions)
    ]
    outs = [full_out((rows, heads * head_dim)), full_out((spans, heads, rows, rows))]
    return run(order, flags, kernel, ins, outs, [], "attend")


def attention_grads(grad, here, parts, views, head, keep, send, scale):
    half = keep.shape[0]
    grad_probs = [turned(grad, view[1, head]) for view in views]
    delta = sum(
        jnp.sum(part.astype(f32) * slope, axis=1, keepdims=True)
        for part, slope in zip(parts, grad_probs)
    )
    query_grad = None
    for k, view in enumerate(views):
        slopes = (parts[k].astype(f32) * (grad_probs[k] - delta)).astype(bf16)
        term = plain(slopes, view[0, head])
        query_grad = term if query_grad is None else query_grad + term
        side = keep if k < half else send
        side[k % half, 0, head] = (dot(slopes, here, ((0,), (0,))) * scale).astype(bf16)
        side[k % half, 1, head] = dot(parts[k].astype(bf16), grad, ((0,), (0,))).astype(bf16)
    return query_grad * scale


def attend_both(
    order, flags, rows_in, packed, queries, pairs, positions, key_positions, tables, scale
):
    heads, rows, head_dim = queries.shape
    width = rows_in.shape[1]
    spans = len(packed)
    across, depth = heads * head_dim, width // spans
    half = spans // 2

    def kernel(flag_ref, rows_ref, *refs):
        packed_refs, refs = refs[:spans], refs[spans:]
        query_ref, refs = refs[0], refs[1:]
        views, refs = spread(refs[: len(pairs)]), refs[len(pairs) :]
        row_ref, key_ref, table_ref, attended, turned_back, keep, send, held, sems = refs
        started = copies(
            [w.at[:across, 3 * across : 3 * across + depth] for w in packed_refs],
            [held.at[:, k * depth : (k + 1) * depth] for k in range(spans)],
            [sems.at[k] for k in range(spans)],
        )
        all_parts = []
        for h in range(heads):
            parts = attention(query_ref[h], views, h, row_ref, key_ref, scale)
            summed = None
            for k in range(spans):
                term = plain(parts[k].astype(bf16), views[k][1, h])
                summed = term if summed is None else summed + term
            attended[:, h * head_dim : (h + 1) * head_dim] = summed.astype(bf16)
            all_parts.append(parts)
        for copy in started:
            copy.wait()
        grads = turned(rows_ref[...], held[...]).astype(bf16)
        for h in range(heads):
            made = attention_grads(
                grads[:, h * head_dim : (h + 1) * head_dim],
                query_ref[h],
                all_parts[h],
                views,
                h,
                keep,
                send,
                scale,
            )
            turned_back[h] = turn(made, table_ref, -1).astype(bf16)

    ins = [(rows_in, whole(rows_in))] + [(w, kept_out) for w in packed]
    ins += [
        (array, whole(array)) for array in (queries, *pairs, positions, key_positions, tables)
    ]
    outs = [full_out((rows, across)), full_out((heads, rows, head_dim))]
    outs += [full_out((half, 2, heads, rows, head_dim))] * 2
    scratch = [pltpu.VMEM((across, width), bf16), pltpu.SemaphoreType.DMA((spans,))]
    return run(order, flags, kernel, ins, outs, scratch, "attend_both")


def hidden_both(order, flags, second, pieces, at_piece, expand, contract, normal, gains):
    rows, width = second.shape
    hidden, depth = contract[0].shape
    spans = len(contract)
    tile = min(512, hidden)
    tiles = hidden // tile

    def kernel(flag_ref, second_ref, *refs):
        piece_refs, refs = refs[: len(pieces)], refs[len(pieces) :]
        expand_refs, refs = refs[:spans], refs[spans:]
        contract_refs, refs = refs[:spans], refs[spans:]
        normal_ref, gain_ref, rows_out, active, grads, part, side, *refs = refs
        held_up, held_down, sems_up, sems_down = refs
        started = []
        for t in range(tiles):
            block = slice(t * tile, (t + 1) * tile)
            places = [slice(k * depth, (k + 1) * depth) for k in range(spans)]
            up = copies(
                [w.at[:, block] for w in expand_refs],
                [held_up.at[place, block] for place in places],
                [sems_up.at[t, k] for k in range(spans)],
            )
            down = copies(
                [w.at[block, :] for w in contract_refs],
                [held_down.at[block, place] for place in places],
                [sems_down.at[t, k] for k in range(spans)],
            )
            started.append((up, down))
        start = 0
        for piece_ref in piece_refs:
            size = piece_ref.shape[1]
            rows_out[start : start + size, :] = piece_ref[0]
            start += size
        for t in range(tiles):
            block = slice(t * tile, (t + 1) * tile)
            for copy in started[t][0] + started[t][1]:
                copy.wait()
            pre = plain(second_ref[...], held_up[:, block])
            risen = 0.5 * (1.0 + lax.erf(pre * half_root))
            active[:, block] = (pre * risen).astype(bf16)
            slope = risen + pre * jnp.exp(-0.5 * pre * pre) * bell
            grads[:, block] = (turned(rows_out[...], held_down[block, :]) * slope).astype(bf16)
        for k in range(spans):
            place = slice(k * depth, (k + 1) * depth)
            made = turned(grads[...], held_up[place, :])
            side[0:1, place] = jnp.sum(
                made * normal_ref[:, place].astype(f32), axis=0, keepdims=True
            )
            side[1:2, place] = jnp.sum(made, axis=0, keepdims=True)
            part[:, place] = made * gain_ref[1:2, place]

    ins = [(second, whole(second))]
    ins += [(piece, at((1,) + piece.shape[1:], (at_piece, 0, 0))) for piece in pieces]
    ins += [(w, kept_out) for w in expand] + [(w, kept_out) for w in contract]
    ins += [(normal, whole(normal)), (gains, whole(gains))]
    outs = [
        full_out((rows, width)),
        full_out((rows, hidden)),
        full_out((rows, hidden)),
        full_out((rows, width), f32),
        full_out((2, width), f32),
    ]
    scratch = [
        pltpu.VMEM((width, hidden), bf16),
        pltpu.VMEM((hidden, width), bf16),
        pltpu.SemaphoreType.DMA((tiles, spans)),
        pltpu.SemaphoreType.DMA((tiles, spans)),
    ]
    return run(order, flags, kernel, ins, outs, scratch, "hidden_both")


def branch_out(order, flags, groups, contract, packed, span_rows):
    hidden, depth = contract[0].shape
    across = groups[0][1].shape[1]
    spans = len(contract)
    width = depth * spans
    half = span_rows // 2
    count = len(groups)

    def kernel(flag_ref, *refs):
        group_refs, refs = refs[: 2 * count], refs[2 * count :]
        contract_refs, packed_refs = refs[:spans], refs[spans : 2 * spans]
        low, high, held, held_out, sems = refs[2 * spans :]
        outputs = [w.at[:across, 3 * across : 3 * across + depth] for w in packed_refs]
        started = copies(
            [ref for k in range(spans) for ref in (outputs[k], contract_refs[k])],
            [ref for k in range(spans) for ref in (held_out.at[k], held.at[k])],
            [sems.at[j] for j in range(2 * spans)],
        )
        for k in range(spans):
            started[2 * k].wait()
            started[2 * k + 1].wait()
            columns = slice(k * depth, (k + 1) * depth)
            for c in range(count):
                made = plain(group_refs[2 * c + 1][...], held_out[k])
                made = made + plain(group_refs[2 * c][...], held[k])
                low[c, :, columns] = made[:half].astype(bf16)
                high[c, :, columns] = made[half:].astype(bf16)

    ins = []
    for active, attended, m in groups:
        ins += [
            (active, at((span_rows, hidden), (m, 0))),
            (attended, at((span_rows, across), (m, 0))),
        ]
    ins += [(w, kept_out) for w in contract] + [(w, kept_out) for w in packed]
    outs = [full_out((count, half, width))] * 2
    scratch = [
        pltpu.VMEM((spans, hidden, depth), bf16),
        pltpu.VMEM((spans, across, depth), bf16),
        pltpu.SemaphoreType.DMA((2 * spans,)),
    ]
    return run(order, flags, kernel, ins, outs, scratch, "branch")


def attend_back(order, flags, pieces, packed, queries, pairs, probs, tables, scale):
    rows = sum(piece.shape[1] for piece in pieces)
    width = pieces[0].shape[2]
    heads, _, head_dim = queries.shape
    spans = len(packed)
    across, depth = heads * head_dim, width // spans
    half = spans // 2

    def kernel(flag_ref, *refs):
        piece_refs, refs = refs[: len(pieces)], refs[len(pieces) :]
        packed_refs, refs = refs[:spans], refs[spans:]
        query_ref, refs = refs[0], refs[1:]
        views, refs = spread(refs[: len(pairs)]), refs[len(pairs) :]
        prob_ref, table_ref, rows_out, turned_back, keep, send, held, sems = refs
        started = copies(
            [w.at[:across, 3 * across : 3 * across + depth] for w in packed_refs],
            [held.at[:, k * depth : (k + 1) * depth] for k in range(spans)],
            [sems.at[k] for k in range(spans)],
        )
        start = 0
        for piece_ref in piece_refs:
            size = piece_ref.shape[1]
            rows_out[start : start + size, :] = piece_ref[0]
            start += size
        for copy in started:
            copy.wait()
        grads = turned(rows_out[...], held[...]).astype(bf16)
        for h in range(heads):
            made = attention_grads(
                grads[:, h * head_dim : (h + 1) * head_dim],
                query_ref[h],
                [prob_ref[k, h] for k in range(spans)],
                views,
                h,
                keep,
                send,
                scale,
            )
            turned_back[h] = turn(made, table_ref, -1).astype(bf16)

    ins = [(piece, whole(piece)) for piece in pieces] + [(w, kept_out) for w in packed]
    ins += [(array, whole(array)) for array in (queries, *pairs, probs, tables)]
    outs = [full_out((rows, width)), full_out((heads, rows, head_dim))]
    outs += [full_out((half, 2, heads, rows, head_dim))] * 2
    scratch = [pltpu.VMEM((across, width), bf16), pltpu.SemaphoreType.DMA((spans,))]
    return run(order, flags, kernel, ins, outs, scratch, "attend_back")


def hidden_back(order, flags, upstream, contract, expand, slope, normal, gains):
    span_rows, width = upstream.shape
    hidden, depth = contract[0].shape
    spans = len(contract)
    tile = min(512, hidden)
    tiles = hidden // tile

    def kernel(flag_ref, *refs):
        upstream_ref, refs = refs[0], refs[1:]
        contract_refs, refs = refs[:spans], refs[spans:]
        expand_refs, refs = refs[:spans], refs[spans:]
        slope_ref, normal_ref, gain_ref, grads, part, side, held, held_up, sems, sems_up = refs
        started = [
            copies(
                [w.at[t * tile : (t + 1) * tile, :] for w in contract_refs],
                [held.at[t, :, k * depth : (k + 1) * depth] for k in range(spans)],
                [sems.at[t, k] for k in range(spans)],
            )
            for t in range(tiles)
        ]
        started_up = copies(
            expand_refs, [held_up.at[k] for k in range(spans)], [sems_up.at[k] for k in range(spans)]
        )
        for t in range(tiles):
            for copy in started[t]:
                copy.wait()
            columns = slice(t * tile, (t + 1) * tile)
            grads[:, columns] = (
                turned(upstream_ref[...], held[t]) * slope_ref[:, columns].astype(f32)
            ).astype(bf16)
        for k in range(spans):
            started_up[k].wait()
            made = turned(grads[...], held_up[k])
            columns = slice(k * depth, (k + 1) * depth)
            side[0:1, columns] = jnp.sum(
                made * normal_ref[:, columns].astype(f32), axis=0, keepdims=True
            )
            side[1:2, columns] = jnp.sum(made, axis=0, keepdims=True)
            part[:, columns] = made * gain_ref[1:2, columns]

    ins = [(upstream, whole(upstream))]
    ins += [(w, kept_out) for w in contract] + [(w, kept_out) for w in expand]
    ins += [
        (slope, whole(slope)),
        (normal, whole(normal)),
        (gains, whole(gains)),
    ]
    outs = [
        full_out((span_rows, hidden)),
        full_out((span_rows, width), f32),
        full_out((2, width), f32),
    ]
    scratch = [
        pltpu.VMEM((tiles, tile, width), bf16),
        pltpu.VMEM((spans, depth, hidden), bf16),
        pltpu.SemaphoreType.DMA((tiles, spans)),
        pltpu.SemaphoreType.DMA((spans,)),
    ]
    return run(order, flags, kernel, ins, outs, scratch, "hidden_back")


def project_back(order, flags, turned_back, own, came, weights, part, normal, gains, tables):
    heads, span_rows, head_dim = turned_back.shape
    spans = len(weights)
    width = part.shape[1]
    depth, columns = width // spans, 3 * heads * head_dim
    half = span_rows // 2

    def kernel(flag_ref, *refs):
        query_ref, own_ref, came_ref, refs = refs[0], refs[1], refs[2], refs[3:]
        weight_refs, refs = refs[:spans], refs[spans:]
        part_ref, normal_ref, gain_ref, table_ref, grads, low, high, side, held, sems = refs
        started = copies(
            [w.at[:depth, :columns] for w in weight_refs],
            [held.at[k] for k in range(spans)],
            [sems.at[k] for k in range(spans)],
        )
        for h in range(heads):
            at_column = h * 3 * head_dim
            keys = own_ref[0, h].astype(f32) + came_ref[0, h].astype(f32)
            values = own_ref[1, h].astype(f32) + came_ref[1, h].astype(f32)
            grads[:, at_column : at_column + head_dim] = query_ref[h]
            grads[:, at_column + head_dim : at_column + 2 * head_dim] = turn(
                keys, table_ref, -1
            ).astype(bf16)
            grads[:, at_column + 2 * head_dim : at_column + 3 * head_dim] = values.astype(bf16)
        for k in range(spans):
            started[k].wait()
            made = turned(grads[...], held[k])
            span_columns = slice(k * depth, (k + 1) * depth)
            side[0:1, span_columns] = jnp.sum(
                made * normal_ref[:, span_columns].astype(f32), axis=0, keepdims=True
            )
            side[1:2, span_columns] = jnp.sum(made, axis=0, keepdims=True)
            both = (made * gain_ref[0:1, span_columns] + part_ref[:, span_columns]).astype(bf16)
            low[:, span_columns] = both[:half]
            high[:, span_columns] = both[half:]

    ins = [(array, whole(array)) for array in (turned_back, own, came)]
    ins += [(w, kept_out) for w in weights]
    ins += [(part, whole(part)), (normal, whole(normal))]
    ins += [(gains, whole(gains)), (tables, whole(tables))]
    outs = [full_out((span_rows, columns))] + [full_out((half, width))] * 2
    outs += [full_out((2, width), f32)]
    scratch = [pltpu.VMEM((spans, depth, columns), bf16), pltpu.SemaphoreType.DMA((spans,))]
    return run(order, flags, kernel, ins, outs, scratch, "project_back")


def weight_sums(order, flags, lefts, rights, by_rows, spans):
    rows = sum(piece.shape[0] for piece in lefts[0][0])
    left_width = sum(group[0].shape[1] for group in lefts[0])
    right_width = sum(group[0].shape[1] for group in rights[0])
    if by_rows:
        tile = left_width // spans
        steps, block = spans // 2, (tile, right_width)
    else:
        tile = min(512, left_width)
        while left_width % tile:
            tile //= 2
        steps, block = left_width // tile, (tile, right_width // 2)
    chunk = min(1024, block[1])
    while right_width % chunk:
        chunk //= 2
    pieces = [
        [piece for groups in (lefts[s], rights[s]) for group in groups for piece in group]
        for s in (0, 1)
    ]
    most = max(len(p) for p in pieces)

    def kernel(flag_ref, *refs):
        piece_refs = (refs[: len(pieces[0])], refs[len(pieces[0]) : len(pieces[0]) + len(pieces[1])])
        keep, send, left, right, flipped, sems = refs[len(pieces[0]) + len(pieces[1]) :]
        g = pl.program_id(0)
        for s in (0, 1):

            @pl.when((g == 0) & (flag_ref[2] == s))
            def _(s=s):
                targets = []
                for held, groups in ((left, lefts[s]), (right, rights[s])):
                    column = 0
                    for group in groups:
                        row, wide = 0, group[0].shape[1]
                        for piece in group:
                            targets.append(
                                held.at[row : row + piece.shape[0], column : column + wide]
                            )
                            row += piece.shape[0]
                        column += wide
                started = copies(
                    piece_refs[s], targets, [sems.at[j] for j in range(len(targets))]
                )
                for copy in started:
                    copy.wait()

        def product(column, store):
            flipped[...] = left[:, pl.ds(pl.multiple_of(column, LANES), tile)].T

            def one(c, _):
                columns = pl.ds(pl.multiple_of(c * chunk, chunk), chunk)
                store(c, plain(flipped[...], right[:, columns]).astype(bf16))
                return 0

            lax.fori_loop(0, right_width // chunk, one, 0)

        if by_rows:

            def to(target):
                def store(c, made):
                    target[:, pl.ds(pl.multiple_of(c * chunk, chunk), chunk)] = made

                return store

            product(g * tile, to(keep))
            product((g + steps) * tile, to(send))
        else:
            half = right_width // 2 // chunk

            def store(c, made):
                @pl.when(c < half)
                def _():
                    keep[:, pl.ds(pl.multiple_of(c * chunk, chunk), chunk)] = made

                @pl.when(c >= half)
                def _():
                    send[:, pl.ds(pl.multiple_of((c - half) * chunk, chunk), chunk)] = made

            product(g * tile, store)

    ins = [(piece, kept_out) for s in (0, 1) for piece in pieces[s]]
    dims = (steps * tile, block[1])
    outs = [(shape(dims), pl.BlockSpec(block, lambda g: (g, 0)))] * 2
    scratch = [
        pltpu.VMEM((rows, left_width), bf16),
        pltpu.VMEM((rows, right_width), bf16),
        pltpu.VMEM((tile, rows), bf16),
        pltpu.SemaphoreType.DMA((most,)),
    ]
    return run(
        order, flags, kernel, ins, outs, scratch, "weight_sums", grid=(steps,)
    )


def fold(order, flags, keep, came, dim):
    rows, columns = keep.shape
    if dim == 0:
        tile = min(256, rows // 2)
        steps, block = rows // 2 // tile, (tile, columns)
        places = [lambda g: (g, 0), lambda g: (g + steps, 0)]
        half = (rows // 2, columns)
    else:
        tile = min(256, rows)
        steps, block = rows // tile, (tile, columns // 2)
        places = [lambda g: (g, 0), lambda g: (g, 1)]
        half = (rows, columns // 2)

    def kernel(flag_ref, keep_low, keep_high, came_low, came_high, low, high):
        low[...] = (keep_low[...].astype(f32) + came_low[...].astype(f32)).astype(bf16)
        high[...] = (keep_high[...].astype(f32) + came_high[...].astype(f32)).astype(bf16)

    ins = [(array, pl.BlockSpec(block, place)) for array in (keep, came) for place in places]
    outs = [(shape(half), pl.BlockSpec(block, lambda g: (g, 0)))] * 2
    return run(order, flags, kernel, ins, outs, [], "fold", grid=(steps,))


def shards(
    block_input,
    out_grad,
    triple_weight,
    output_weight,
    expand_weight,
    contract_weight,
    norm_gains,
    norm_biases,
):
    section = lax.axis_index("pipe")
    span = lax.axis_index("ctx")
    lane = lax.axis_index("tp")
    spans = lax.axis_size("ctx")
    lanes = lax.axis_size("tp")
    micros, rows, width = block_input.shape
    span_rows = rows * lanes
    heads = triple_weight.shape[2]
    head_dim = triple_weight.shape[4]
    across = heads * head_dim
    scale = head_dim ** (-0.5)
    first_section = section == 0
    both = (0, 1)

    def hop(array, axis, step, sections):
        size = lax.axis_size(axis)
        pairs = [(s * size + a, s * size + (a ^ step)) for s in sections for a in range(size)]
        return lax.ppermute(array, ("pipe", axis), pairs)

    order = Order()

    def flags_for(wanted):
        return jnp.stack([jnp.asarray(wanted), span, section]).astype(jnp.int32)

    flags = [flags_for(section == s) for s in both]
    always = flags_for(1)

    kept = [[SimpleNamespace() for _ in range(micros)] for _ in both]
    due = {}
    slot_index = [0]

    def slot(hops, kernels=()):
        now = slot_index[0]
        slot_index[0] += 1
        ready = due.pop(now, [])
        hops = [h if len(h) == 3 else h + (1,) for h in hops]
        if hops:
            gated = fence([operand for operand, _, _ in hops], order.last + ready)
            order.last = [min(gated, key=lambda array: array.size)]
            for passed, (_, go, slots) in zip(gated, hops):
                due.setdefault(now + slots, []).append(go(passed))
        else:
            order.last = order.last + ready
        for kernel in kernels:
            kernel()

    def halved(keep, came, dim):
        middle = keep.shape[dim] // 2
        total = keep.astype(f32) + came.astype(f32)
        return (
            lax.slice_in_dim(total, 0, middle, axis=dim).astype(bf16),
            lax.slice_in_dim(total, middle, 2 * middle, axis=dim).astype(bf16),
        )

    def spread_hops(pieces, axis, axis_name, sections, first):
        step = lax.axis_size(axis_name) // 4
        going = first
        while step:
            pieces.append(hop(going, axis_name, step, sections))
            going = jnp.concatenate(pieces, axis=axis)
            step //= 2
        return pieces[-1]

    def fold_hops(k, first, axis_name, dim, sections):
        step, size = 1, lax.axis_size(axis_name)
        while 2 * step < size:
            came = hop(first, axis_name, step, sections)
            k.keep, k.send = halved(k.keep, came, dim)
            first = k.send
            step *= 2
        return came

    depth = width // spans
    far = spans // 2
    assert depth == across
    small = jnp.concatenate([norm_gains[0], norm_biases[0]], axis=0)
    packed = jnp.concatenate(
        [triple_weight[0].reshape(depth, 3 * across), output_weight[0].reshape(across, depth)],
        axis=1,
    )
    packed = jnp.pad(packed, ((0, 16), (0, 0)))
    packed = lax.dynamic_update_slice(packed, small, (depth, 0))
    own_expand, own_contract = expand_weight[0], contract_weight[0]
    hidden = own_expand.shape[1]
    half_hidden = hidden // 2
    inputs = xor_blocks(block_input, span, spans)
    cotangent = xor_blocks(out_grad, span, spans)
    early = jnp.where(first_section, inputs, cotangent)

    def blocks_of(own, came):
        held, step = {0: own, far: came}, far // 2
        while step:
            for k in list(held):
                held[k ^ step] = hop(held[k], "ctx", step, both)
            step //= 2
        return [held[k] for k in doubling(spans)]

    packed_came = hop(packed, "ctx", far, both)
    expand_came = hop(own_expand, "ctx", far, both)
    early_pieces = [early, hop(early, "tp", lanes // 2, both)]
    spread_hops(early_pieces, 1, "tp", both, jnp.concatenate(early_pieces, axis=1))

    in_row = jnp.arange(rows, dtype=jnp.int32)
    in_span = jnp.concatenate([(lane ^ j) * rows + in_row for j in doubling(lanes)])
    positions = span * span_rows + in_span
    key_positions = jnp.stack([(span ^ k) * span_rows + in_span for k in doubling(spans)])
    tables = rope_tables(positions)
    position_column = positions[:, None]
    key_positions = key_positions[:, None, :]

    def rows_far(s, m):
        k = kept[s][m]

        def go(passed):
            k.rows = passed
            k.pieces = [passed, hop(passed, "tp", lanes // 2, (s,))]
            return k.pieces[1]

        return k.rows, go

    def rows_near(s, m):
        k = kept[s][m]

        def go(passed):
            last_piece = spread_hops(k.pieces, 0, "tp", (s,), passed)
            k.row_pieces = [piece[None] for piece in k.pieces]
            return last_piece

        return jnp.concatenate(k.pieces, axis=0), go

    def pair_far(s, m):
        k = kept[s][m]

        def go(passed):
            k.pairs = [passed, hop(passed, "ctx", far, (s,))]
            return k.pairs[1]

        return k.pair, go

    def pair_near(s, m):
        k = kept[s][m]

        def go(passed):
            return spread_hops(k.pairs, 0, "ctx", (s,), passed)

        return jnp.concatenate(k.pairs, axis=0), go

    def pair_grad_near(s, m):
        k = kept[s][m].pair_grad
        return k.send, lambda passed: fold_hops(k, passed, "ctx", 0, (s,))

    def pair_grad_far(s, m):
        k = kept[s][m].pair_grad

        def go(passed):
            k.came = hop(passed, "ctx", far, (s,))
            return k.came

        return k.send, go

    def sum_near(s, k, dim=0):
        return k.send, lambda passed: fold_hops(k, passed, "tp", dim, (s,))

    def sum_far(s, k):
        def go(passed):
            k.came = hop(passed, "tp", lanes // 2, (s,))
            return k.came

        return k.send, go

    def total_of(k):
        return k.keep.astype(f32) + k.came.astype(f32)

    def norm_back(upstream, combined, entering):
        normalized, inverse = normalize(entering.astype(f32))
        return (
            upstream.astype(f32)
            + inverse
            * (
                combined
                - jnp.mean(combined, axis=-1, keepdims=True)
                - normalized * jnp.mean(combined * normalized, axis=-1, keepdims=True)
            )
        ).astype(bf16)

    def hand_over(m):
        k = kept[0][m]

        def go(passed):
            k.middle = passed
            kept[1][m].rows = lax.ppermute(passed, "pipe", [(0, 1)])
            return kept[1][m].rows

        return (inputs[m].astype(f32) + total_of(k.summed)).astype(bf16), go

    def hand_back(m):
        k = kept[1][m]

        def go(passed):
            k.entry = passed
            kept[0][m].rows = lax.ppermute(passed, "pipe", [(1, 0)])
            return kept[0][m].rows

        return norm_back(cotangent[m], total_of(k.summed), k.rows), go

    def run_project(s, m):
        k = kept[s][m]
        pieces, place = (early_pieces, m) if s == 0 else (k.row_pieces, 0)
        k.first, k.second, k.normal, k.queries, pair = project(
            order, flags[s], pieces, place, gains, biases, tables, packed, heads, head_dim
        )
        k.pair = pair[None]

    def run_expand(m):
        k = kept[0][m]
        k.active, k.slope = expand_up(order, flags[0], k.second, expand, span_rows)

    def run_attend(m):
        k = kept[0][m]
        k.attended, k.probs = attend(
            order, flags[0], k.queries, k.pairs, position_column, key_positions, scale
        )

    def run_branch(m):
        k = kept[0][m]
        low, high = branch_out(
            order, flags[0], [(k.active, k.attended, 0)], contract, packed, span_rows
        )
        k.summed = SimpleNamespace(keep=low[0], send=high[0])

    def run_hidden_both(m):
        k = kept[1][m]
        k.upstream, k.active, k.hidden, k.part, k.side_second = hidden_both(
            order, flags[1], k.second, early_pieces, m, expand, contract, k.normal, gains
        )

    def run_attend_both(m):
        k = kept[1][m]
        k.attended, k.turned_back, keep, send = attend_both(
            order,
            flags[1],
            k.upstream,
            packed,
            k.queries,
            k.pairs,
            position_column,
            key_positions,
            tables,
            scale,
        )
        k.pair_grad = SimpleNamespace(keep=keep, send=send)

    def run_attend_back(m):
        k = kept[0][m]
        k.upstream, k.turned_back, keep, send = attend_back(
            order,
            flags[0],
            k.row_pieces,
            packed,
            k.queries,
            k.pairs,
            k.probs,
            tables,
            scale,
        )
        k.pair_grad = SimpleNamespace(keep=keep, send=send)

    def run_hidden_back(m):
        k = kept[0][m]
        k.hidden, k.part, k.side_second = hidden_back(
            order,
            flags[0],
            k.upstream,
            contract,
            expand,
            k.slope,
            k.normal,
            gains,
        )

    def run_project_back(s, m):
        k = kept[s][m]
        own, arrived = k.pair_grad.keep, k.pair_grad.came
        k.stacked, low, high, k.side_first = project_back(
            order,
            flags[s],
            k.turned_back,
            own.reshape(own.shape[1:]),
            arrived.reshape(arrived.shape[1:]),
            packed,
            k.part,
            k.normal,
            gains,
            tables,
        )
        k.summed = SimpleNamespace(keep=low, send=high)

    def of(name, s, count=micros):
        return [getattr(kept[s][m], name) for m in range(count)]

    branch_sums, expand_sums, triple_sums = (SimpleNamespace(parts=[]) for _ in range(3))

    def run_sums(w, lefts, rights, by_rows):
        w.dim = 0 if by_rows else 1
        w.keep, w.send = weight_sums(order, always, lefts, rights, by_rows, spans)

    def wide_near(w):
        def go(passed):
            w.came = hop(passed, "ctx", 1, both)
            return w.came

        return w.send, go

    def run_fold(w):
        step = 2
        w.keep, w.send = fold(order, always, w.keep, w.came, w.dim)
        while 2 * step < spans:
            w.came = hop(w.send, "ctx", step, both)
            w.keep, w.send = fold(order, always, w.keep, w.came, w.dim)
            step *= 2

    def wide_far(w, start, stop):
        def go(passed):
            w.parts.append(hop(passed, "ctx", far, both))
            return w.parts[-1]

        return w.send[start:stop], go

    contract_parts = []

    def contract_far(start, stop):
        def go(passed):
            contract_parts.append(hop(passed, "ctx", far, both))
            return contract_parts[-1]

        return own_contract[start:stop], go

    weights = SimpleNamespace()

    def packed_near(passed):
        weights.packed = blocks_of(packed, passed)
        return weights.packed[-1]

    def expand_near(passed):
        weights.expand = blocks_of(own_expand, passed)
        return weights.expand[-1]

    def contract_near(passed):
        weights.contract = blocks_of(own_contract, passed)
        return weights.contract[-1]

    due[0] = [early_pieces[-1]]
    slot(
        [
            (packed_came, packed_near),
            contract_far(0, half_hidden) + (2,),
            (expand_came, expand_near, 2),
        ]
    )
    packed = weights.packed
    small_full = jnp.concatenate(
        [piece[depth : depth + 4, :depth] for piece in packed], axis=1
    ).astype(f32)
    gains, biases = small_full[:2], small_full[2:]
    slot([], [lambda m=m: run_project(0, m) for m in range(micros)])
    expand = weights.expand
    slot(
        [pair_far(0, 0), contract_far(half_hidden, hidden)],
        [lambda m=m: run_expand(m) for m in range(micros)],
    )
    slot([(jnp.concatenate(contract_parts, axis=0), contract_near), pair_near(0, 0)])
    contract = weights.contract

    def ks(s, m):
        return kept[s][m].summed

    slot([pair_far(0, 1)], [lambda: run_attend(0), lambda: run_branch(0)])
    slot([sum_near(0, ks(0, 0)), pair_near(0, 1), pair_far(0, 2)])
    slot(
        [sum_far(0, ks(0, 0)), pair_near(0, 2)],
        [lambda: run_attend(1), lambda: run_branch(1)],
    )
    slot(
        [hand_over(0), sum_near(0, ks(0, 1))], [lambda: run_attend(2), lambda: run_branch(2)]
    )
    slot([rows_far(1, 0), sum_far(0, ks(0, 1)), sum_near(0, ks(0, 2))])
    slot([rows_near(1, 0), hand_over(1), sum_far(0, ks(0, 2))])
    slot([rows_far(1, 1), hand_over(2)], [lambda: run_project(1, 0)])
    slot(
        [pair_far(1, 0), rows_near(1, 1), rows_far(1, 2)], [lambda: run_hidden_both(0)]
    )
    slot([pair_near(1, 0), rows_near(1, 2)], [lambda: run_project(1, 1)])
    slot([pair_far(1, 1)], [lambda: run_attend_both(0), lambda: run_hidden_both(1)])
    slot([pair_grad_near(1, 0), pair_near(1, 1)], [lambda: run_project(1, 2)])
    slot(
        [pair_grad_far(1, 0), pair_far(1, 2)],
        [lambda: run_attend_both(1), lambda: run_hidden_both(2)],
    )
    slot([pair_grad_near(1, 1), pair_near(1, 2)], [lambda: run_project_back(1, 0)])
    slot(
        [sum_near(1, ks(1, 0)), pair_grad_far(1, 1)], [lambda: run_attend_both(2)]
    )
    slot(
        [sum_far(1, ks(1, 0)), pair_grad_near(1, 2)], [lambda: run_project_back(1, 1)]
    )
    slot([hand_back(0), sum_near(1, ks(1, 1)), pair_grad_far(1, 2)])
    slot([sum_far(1, ks(1, 1)), rows_far(0, 0)], [lambda: run_project_back(1, 2)])
    slot([sum_near(1, ks(1, 2)), hand_back(1), rows_near(0, 0)])
    slot([sum_far(1, ks(1, 2)), rows_far(0, 1)], [lambda: run_attend_back(0)])
    ends = SimpleNamespace()

    def run_final_branch():
        ends.low, ends.high = branch_out(
            order,
            flags[1],
            [(k.active, k.attended, 0) for k in kept[1]],
            contract,
            packed,
            span_rows,
        )

    slot(
        [hand_back(2), rows_near(0, 1), pair_grad_near(0, 0)],
        [lambda: run_hidden_back(0), run_final_branch],
    )
    finals = SimpleNamespace(keep=ends.low, send=ends.high)
    slot([rows_far(0, 2), pair_grad_far(0, 0)], [lambda: run_attend_back(1)])
    slot(
        [rows_near(0, 2), pair_grad_near(0, 1), sum_near(1, finals, 1) + (2,)],
        [lambda: run_hidden_back(1), lambda: run_project_back(0, 0)],
    )
    last = micros - 1
    slot(
        [pair_grad_far(0, 1)],
        [
            lambda: run_sums(
                branch_sums,
                [[of("active", s), of("attended", s)] for s in both],
                [
                    [of("upstream", 0, last) + [piece[0] for piece in kept[0][last].row_pieces]],
                    [of("upstream", 1)],
                ],
                False,
            )
        ],
    )
    slot(
        [wide_near(branch_sums), sum_far(1, finals) + (2,)],
        [lambda: run_project_back(0, 1), lambda: run_attend_back(2)],
    )
    slot([pair_grad_near(0, 2)], [lambda: run_fold(branch_sums)])
    slot(
        [wide_far(branch_sums, 0, half_hidden), pair_grad_far(0, 2)],
        [
            lambda: run_hidden_back(2),
            lambda: run_sums(
                expand_sums,
                [[of("second", s)] for s in both],
                [[of("hidden", s)] for s in both],
                True,
            ),
        ],
    )
    slot(
        [wide_far(branch_sums, hidden, hidden + across), wide_near(expand_sums)],
        [lambda: run_project_back(0, 2)],
    )
    outs = SimpleNamespace(
        keep=jnp.stack([k.summed.keep for k in kept[0]]),
        send=jnp.stack([k.summed.send for k in kept[0]]),
    )

    def side_of(mades):
        return sum(
            jnp.concatenate([k.side_first, k.side_second], axis=0) for k in mades
        )

    side = SimpleNamespace(
        all=jnp.where(first_section, side_of(kept[0]), side_of(kept[1])), step=1
    )

    def side_ctx():
        middle = side.all.shape[1] // 2

        def go(passed):
            came = hop(passed, "ctx", side.step, both)
            side.all = side.all[:, :middle] + came
            side.step *= 2
            return came

        return side.all[:, middle:], go

    def side_tp(passed):
        step = 1
        while step < lanes:
            came = hop(passed, "tp", step, both)
            passed = passed + came
            step *= 2
        side.all = passed
        return came

    slot(
        [wide_far(branch_sums, half_hidden, hidden), sum_near(0, outs, 1) + (2,), side_ctx()],
        [
            lambda: run_fold(expand_sums),
            lambda: run_sums(
                triple_sums,
                [[of("first", s)] for s in both],
                [[of("stacked", s)] for s in both],
                True,
            ),
        ],
    )
    half_rows = depth // 2
    slot([wide_far(expand_sums, 0, half_rows), wide_near(triple_sums), side_ctx()])
    while side.step < spans:
        slot([side_ctx()])
    slot(
        [wide_far(expand_sums, half_rows, depth), sum_far(0, outs) + (2,)],
        [lambda: run_fold(triple_sums)],
    )
    slot([wide_far(triple_sums, 0, depth), (side.all, side_tp)])

    def wide_total(keep, parts):
        came = jnp.concatenate(parts, axis=0) if len(parts) > 1 else parts[0]
        return keep.astype(f32) + came.astype(f32)

    low_part, output_part, high_part = branch_sums.parts
    contract_grads = wide_total(branch_sums.keep[:hidden], [low_part, high_part])
    output_grads = wide_total(branch_sums.keep[hidden:], [output_part])
    expand_grads = wide_total(expand_sums.keep, expand_sums.parts)
    triple_grads = wide_total(triple_sums.keep, triple_sums.parts)
    layer_outputs = jnp.where(
        first_section,
        jnp.stack(of("middle", 0)),
        (jnp.stack(of("rows", 1)).astype(f32) + total_of(finals)).astype(bf16),
    )
    entry_grads = jnp.where(
        first_section,
        norm_back(jnp.stack(of("rows", 0)), total_of(outs), inputs),
        jnp.stack(of("entry", 1)),
    )
    gain_grads = jnp.stack([side.all[0], side.all[2]])
    bias_grads = jnp.stack([side.all[1], side.all[3]])
    return (
        xor_blocks(layer_outputs, span, spans, inverse=True)[None],
        xor_blocks(entry_grads, span, spans, inverse=True)[None],
        triple_grads.reshape(triple_weight.shape),
        output_grads.reshape(output_weight.shape),
        expand_grads[None],
        contract_grads[None],
        gain_grads[None],
        bias_grads[None],
    )


def solution(mesh):
    return jax.shard_map(
        shards,
        mesh=mesh,
        in_specs=(
            P(None, ("ctx", "tp"), None),
            P(None, ("ctx", "tp"), None),
            P("pipe", "ctx", "tp", None, None),
            P("pipe", "tp", None, "ctx"),
            P("pipe", "ctx", "tp"),
            P("pipe", "tp", "ctx"),
            P("pipe", None, "ctx"),
            P("pipe", None, "ctx"),
        ),
        out_specs=(
            P("pipe", None, ("ctx", "tp"), None),
            P("pipe", None, ("ctx", "tp"), None),
            P("pipe", "ctx", "tp", None, None),
            P("pipe", "tp", None, "ctx"),
            P("pipe", "ctx", "tp"),
            P("pipe", "tp", "ctx"),
            P("pipe", None, "ctx"),
            P("pipe", None, "ctx"),
        ),
        check_vma=False,
    )
```

```python
import functools
from types import SimpleNamespace

import jax
import jax.numpy as jnp
from jax import lax
from jax.experimental import pallas as pl
from jax.experimental.pallas import tpu as pltpu
from jax.sharding import PartitionSpec as P

ROT = 64
LANES = 128
epsilon = 1e-05
masked_score = -1e30
f32 = jnp.float32
bf16 = jnp.bfloat16
vmem_bytes = 56 * 1024 * 1024
half_root = 0.7071067811865476
bell = 0.3989422804014327


def dot(a, b, dims):
    return lax.dot_general(a, b, (dims, ((), ())), preferred_element_type=f32)


def plain(a, b):
    return dot(a, b, ((1,), (0,)))


def turned(a, b):
    return dot(a, b, ((1,), (1,)))


def doubling(count):
    order, step = [0], count // 2
    while step:
        order += [k ^ step for k in order]
        step //= 2
    return order


def xor_blocks(values, index, count, inverse=False):
    width = values.shape[-1] // count
    order = doubling(count)

    def taken(places):
        return jnp.concatenate(
            [values[..., k * width : (k + 1) * width] for k in places], axis=-1
        )

    if inverse:
        values = taken([order.index(k) for k in range(count)])
    step = 1
    while step < count:
        swapped = taken([k ^ step for k in range(count)])
        values = jnp.where((index & step) != 0, swapped, values)
        step *= 2
    return values if inverse else taken(order)


def rope_tables(positions):
    half = ROT // 2
    frequency = 10000.0 ** (-jnp.arange(0, ROT, 2, dtype=f32) / ROT)
    angles = positions.astype(f32)[:, None] * frequency[None, :]
    cosine, sine = jnp.cos(angles), jnp.sin(angles)
    count = positions.shape[0]
    rest = jnp.zeros((count, LANES - ROT), f32)
    none = jnp.zeros((count, half), f32)
    return jnp.stack(
        [
            jnp.concatenate([cosine, cosine, rest + 1.0], axis=1),
            jnp.concatenate([-sine, none, rest], axis=1),
            jnp.concatenate([none, sine, rest], axis=1),
        ]
    )


def turn(values, tables, sign):
    half = ROT // 2
    part = values[:, :LANES]
    moved = (
        pltpu.roll(part, LANES - half, 1) * tables[1] + pltpu.roll(part, half, 1) * tables[2]
    )
    part = part * tables[0] + (moved if sign > 0 else -moved)
    return jnp.concatenate([part, values[:, LANES:]], axis=1)


def normalize(values):
    center = values - jnp.mean(values, axis=-1, keepdims=True)
    inverse = lax.rsqrt(jnp.mean(center * center, axis=-1, keepdims=True) + epsilon)
    return (center * inverse, inverse)


def whole(array):
    zeros = (0,) * array.ndim
    return pl.BlockSpec(array.shape, lambda *_: zeros)


def at(block, place):
    return pl.BlockSpec(block, lambda *_: place)


kept_out = pl.BlockSpec(memory_space=pl.ANY)


def shape(dims, dtype=bf16):
    return jax.ShapeDtypeStruct(dims, dtype)


class Order:
    def __init__(self):
        self.last = []

    def follow(self, results):
        self.last = [min(results, key=lambda array: array.size * array.dtype.itemsize)]

    def also(self, array):
        self.last = self.last + [array]


took = dict(
    project=7,
    expand=8,
    attend=5,
    branch=8,
    hidden_both=14,
    attend_both=11,
    attend_back=8,
    hidden_back=13,
    project_back=8,
    weight_sums=16,
    fold=7,
)
peak = 1.15e9


def run(order, flags, kernel, ins, outs, scratch, name, grid=(1,)):
    taken = len(ins)
    ins = [(flags, pl.BlockSpec(memory_space=pltpu.SMEM))] + list(ins)
    ins += [(array, kept_out) for array in order.last]
    arrays = [array for array, _ in ins]

    def body(flag_ref, *refs):
        @pl.when(flag_ref[0] == 1)
        def _():
            kernel(flag_ref, *refs[:taken], *refs[len(ins) - 1 :])

    results = pl.pallas_call(
        body,
        grid=grid,
        in_specs=[spec for _, spec in ins],
        out_specs=[spec for _, spec in outs],
        out_shape=[struct for struct, _ in outs],
        scratch_shapes=scratch,
        compiler_params=pltpu.CompilerParams(vmem_limit_bytes=vmem_bytes),
        cost_estimate=pl.CostEstimate(
            flops=int(took[name] * peak), bytes_accessed=0, transcendentals=0
        ),
        name=name,
    )(*arrays)
    order.follow(results)
    return results


def fence(through, waits):
    count = len(through)

    def kernel(*refs):
        pass

    return pl.pallas_call(
        kernel,
        in_specs=[kept_out] * (count + len(waits)),
        out_specs=[kept_out] * count,
        out_shape=[shape(array.shape, array.dtype) for array in through],
        input_output_aliases={j: j for j in range(count)},
        compiler_params=pltpu.CompilerParams(vmem_limit_bytes=vmem_bytes),
        cost_estimate=pl.CostEstimate(flops=1, bytes_accessed=1, transcendentals=0),
        name="fence",
    )(*through, *waits)


def full_out(dims, dtype=bf16):
    zeros = (0,) * len(dims)
    return (shape(dims, dtype), pl.BlockSpec(dims, lambda *_: zeros))


def copies(sources, targets, sems):
    started = []
    for source, target, sem in zip(sources, targets, sems):
        copy = pltpu.make_async_copy(source, target, sem)
        copy.start()
        started.append(copy)
    return started


def project(order, flags, pieces, at_piece, gains, biases, tables, weights, heads, head_dim):
    count, width = 1, pieces[0].shape[2]
    span_rows = sum(piece.shape[1] for piece in pieces)
    rows = count * span_rows
    chunk = pieces[0].shape[1]
    spans = len(weights)
    depth = width // spans
    wide = 3 * head_dim
    columns = heads * wide

    def kernel(flag_ref, *refs):
        piece_refs = refs[: len(pieces)]
        gain_ref, bias_ref, table_ref = refs[len(pieces) : len(pieces) + 3]
        weight_refs = refs[len(pieces) + 3 : len(pieces) + 3 + spans]
        first, second, normal, queries, pair, held, sems = refs[len(pieces) + 3 + spans :]
        started = []
        for h in range(heads):
            started.append(
                copies(
                    [w.at[:depth, h * wide : (h + 1) * wide] for w in weight_refs],
                    [held.at[h, k * depth : (k + 1) * depth] for k in range(spans)],
                    [sems.at[h, k] for k in range(spans)],
                )
            )
        start = 0
        for piece_ref in piece_refs:
            chunks = piece_ref.shape[1] // chunk

            def one(i, _, piece_ref=piece_ref, start=start, chunks=chunks):
                m, c = i // chunks, i % chunks
                values = piece_ref[m, pl.ds(pl.multiple_of(c * chunk, chunk), chunk), :]
                normed, _ = normalize(values.astype(f32))
                to = pl.ds(
                    pl.multiple_of(m * span_rows + start + c * chunk, chunk), chunk
                )
                normal[to, :] = normed.astype(bf16)
                first[to, :] = (normed * gain_ref[0:1] + bias_ref[0:1]).astype(bf16)
                second[to, :] = (normed * gain_ref[1:2] + bias_ref[1:2]).astype(bf16)
                return 0

            lax.fori_loop(0, count * chunks, one, 0)
            start += piece_ref.shape[1]
        for h in range(heads):
            for copy in started[h]:
                copy.wait()

            def two(m, _, h=h):
                to = pl.ds(pl.multiple_of(m * span_rows, span_rows), span_rows)
                made = plain(first[to, :], held[h])
                queries[h, to, :] = turn(made[:, :head_dim], table_ref, 1).astype(bf16)
                pair[0, h, to, :] = turn(
                    made[:, head_dim : 2 * head_dim], table_ref, 1
                ).astype(bf16)
                pair[1, h, to, :] = made[:, 2 * head_dim :].astype(bf16)
                return 0

            lax.fori_loop(0, count, two, 0)

    ins = [(piece, at((1,) + piece.shape[1:], (at_piece, 0, 0))) for piece in pieces]
    ins += [(array, whole(array)) for array in (gains, biases, tables)]
    ins += [(w, kept_out) for w in weights]
    outs = [full_out((rows, width))] * 3 + [
        full_out((heads, rows, head_dim)),
        full_out((2, heads, rows, head_dim)),
    ]
    scratch = [
        pltpu.VMEM((heads, width, wide), bf16),
        pltpu.SemaphoreType.DMA((heads, spans)),
    ]
    return run(order, flags, kernel, ins, outs, scratch, "project")


def expand_up(order, flags, second, weights, span_rows):
    rows, width = second.shape
    depth, hidden = weights[0].shape
    spans = len(weights)
    tile = min(512, hidden)
    tiles = hidden // tile

    def kernel(flag_ref, *refs):
        second_ref, weight_refs = refs[0], refs[1 : 1 + spans]
        active, slope, held, sems = refs[1 + spans :]
        started = []
        for t in range(tiles):
            started.append(
                copies(
                    [w.at[:, t * tile : (t + 1) * tile] for w in weight_refs],
                    [held.at[t, k * depth : (k + 1) * depth] for k in range(spans)],
                    [sems.at[t, k] for k in range(spans)],
                )
            )
        for t in range(tiles):
            for copy in started[t]:
                copy.wait()

            def one(m, _, t=t):
                to = pl.ds(pl.multiple_of(m * span_rows, span_rows), span_rows)
                pre = plain(second_ref[to, :], held[t])
                risen = 0.5 * (1.0 + lax.erf(pre * half_root))
                columns = slice(t * tile, (t + 1) * tile)
                active[to, columns] = (pre * risen).astype(bf16)
                slope[to, columns] = (
                    risen + pre * jnp.exp(-0.5 * pre * pre) * bell
                ).astype(bf16)
                return 0

            lax.fori_loop(0, rows // span_rows, one, 0)

    ins = [(second, whole(second))] + [(w, kept_out) for w in weights]
    outs = [full_out((rows, hidden))] * 2
    scratch = [
        pltpu.VMEM((tiles, width, tile), bf16),
        pltpu.SemaphoreType.DMA((tiles, spans)),
    ]
    return run(order, flags, kernel, ins, outs, scratch, "expand")


def spread(refs):
    return [ref.at[j] for ref in refs for j in range(ref.shape[0])]


def attention(here, pairs, head, row_ref, key_ref, scale):
    scores = []
    for k, pair in enumerate(pairs):
        raw = turned(here, pair[0, head]) * scale
        scores.append(jnp.where(key_ref[k] <= row_ref[...], raw, masked_score))
    top = functools.reduce(
        jnp.maximum, [jnp.max(part, axis=1, keepdims=True) for part in scores]
    )
    scores = [jnp.exp(part - top) for part in scores]
    inverse = 1.0 / sum(jnp.sum(part, axis=1, keepdims=True) for part in scores)
    return [part * inverse for part in scores]


def attend(order, flags, queries, pairs, positions, key_positions, scale):
    heads, rows, head_dim = queries.shape
    spans = sum(pair.shape[0] for pair in pairs)

    def kernel(flag_ref, query_ref, *refs):
        views, refs = spread(refs[: len(pairs)]), refs[len(pairs) :]
        row_ref, key_ref, attended, probs = refs
        for h in range(heads):
            parts = attention(query_ref[h], views, h, row_ref, key_ref, scale)
            summed = None
            for k in range(spans):
                part = parts[k].astype(bf16)
                probs[k, h] = part
                term = plain(part, views[k][1, h])
                summed = term if summed is None else summed + term
            attended[:, h * head_dim : (h + 1) * head_dim] = summed.astype(bf16)

    ins = [
        (array, whole(array)) for array in (queries, *pairs, positions, key_positions)
    ]
    outs = [full_out((rows, heads * head_dim)), full_out((spans, heads, rows, rows))]
    return run(order, flags, kernel, ins, outs, [], "attend")


def attention_grads(grad, here, parts, views, head, keep, send, scale):
    half = keep.shape[0]
    grad_probs = [turned(grad, view[1, head]) for view in views]
    delta = sum(
        jnp.sum(part.astype(f32) * slope, axis=1, keepdims=True)
        for part, slope in zip(parts, grad_probs)
    )
    query_grad = None
    for k, view in enumerate(views):
        slopes = (parts[k].astype(f32) * (grad_probs[k] - delta)).astype(bf16)
        term = plain(slopes, view[0, head])
        query_grad = term if query_grad is None else query_grad + term
        side = keep if k < half else send
        side[k % half, 0, head] = (dot(slopes, here, ((0,), (0,))) * scale).astype(bf16)
        side[k % half, 1, head] = dot(parts[k].astype(bf16), grad, ((0,), (0,))).astype(bf16)
    return query_grad * scale


def attend_both(
    order, flags, rows_in, packed, queries, pairs, positions, key_positions, tables, scale
):
    heads, rows, head_dim = queries.shape
    width = rows_in.shape[1]
    spans = len(packed)
    across, depth = heads * head_dim, width // spans
    half = spans // 2

    def kernel(flag_ref, rows_ref, *refs):
        packed_refs, refs = refs[:spans], refs[spans:]
        query_ref, refs = refs[0], refs[1:]
        views, refs = spread(refs[: len(pairs)]), refs[len(pairs) :]
        row_ref, key_ref, table_ref, attended, turned_back, keep, send, held, sems = refs
        started = copies(
            [w.at[:across, 3 * across : 3 * across + depth] for w in packed_refs],
            [held.at[:, k * depth : (k + 1) * depth] for k in range(spans)],
            [sems.at[k] for k in range(spans)],
        )
        all_parts = []
        for h in range(heads):
            parts = attention(query_ref[h], views, h, row_ref, key_ref, scale)
            summed = None
            for k in range(spans):
                term = plain(parts[k].astype(bf16), views[k][1, h])
                summed = term if summed is None else summed + term
            attended[:, h * head_dim : (h + 1) * head_dim] = summed.astype(bf16)
            all_parts.append(parts)
        for copy in started:
            copy.wait()
        grads = turned(rows_ref[...], held[...]).astype(bf16)
        for h in range(heads):
            made = attention_grads(
                grads[:, h * head_dim : (h + 1) * head_dim],
                query_ref[h],
                all_parts[h],
                views,
                h,
                keep,
                send,
                scale,
            )
            turned_back[h] = turn(made, table_ref, -1).astype(bf16)

    ins = [(rows_in, whole(rows_in))] + [(w, kept_out) for w in packed]
    ins += [
        (array, whole(array)) for array in (queries, *pairs, positions, key_positions, tables)
    ]
    outs = [full_out((rows, across)), full_out((heads, rows, head_dim))]
    outs += [full_out((half, 2, heads, rows, head_dim))] * 2
    scratch = [pltpu.VMEM((across, width), bf16), pltpu.SemaphoreType.DMA((spans,))]
    return run(order, flags, kernel, ins, outs, scratch, "attend_both")


def hidden_both(order, flags, second, pieces, at_piece, expand, contract, normal, gains):
    rows, width = second.shape
    hidden, depth = contract[0].shape
    spans = len(contract)
    tile = min(512, hidden)
    tiles = hidden // tile

    def kernel(flag_ref, second_ref, *refs):
        piece_refs, refs = refs[: len(pieces)], refs[len(pieces) :]
        expand_refs, refs = refs[:spans], refs[spans:]
        contract_refs, refs = refs[:spans], refs[spans:]
        normal_ref, gain_ref, rows_out, active, grads, part, side, *refs = refs
        held_up, held_down, sems_up, sems_down = refs
        started = []
        for t in range(tiles):
            block = slice(t * tile, (t + 1) * tile)
            places = [slice(k * depth, (k + 1) * depth) for k in range(spans)]
            up = copies(
                [w.at[:, block] for w in expand_refs],
                [held_up.at[place, block] for place in places],
                [sems_up.at[t, k] for k in range(spans)],
            )
            down = copies(
                [w.at[block, :] for w in contract_refs],
                [held_down.at[block, place] for place in places],
                [sems_down.at[t, k] for k in range(spans)],
            )
            started.append((up, down))
        start = 0
        for piece_ref in piece_refs:
            size = piece_ref.shape[1]
            rows_out[start : start + size, :] = piece_ref[0]
            start += size
        for t in range(tiles):
            block = slice(t * tile, (t + 1) * tile)
            for copy in started[t][0] + started[t][1]:
                copy.wait()
            pre = plain(second_ref[...], held_up[:, block])
            risen = 0.5 * (1.0 + lax.erf(pre * half_root))
            active[:, block] = (pre * risen).astype(bf16)
            slope = risen + pre * jnp.exp(-0.5 * pre * pre) * bell
            grads[:, block] = (turned(rows_out[...], held_down[block, :]) * slope).astype(bf16)
        for k in range(spans):
            place = slice(k * depth, (k + 1) * depth)
            made = turned(grads[...], held_up[place, :])
            side[0:1, place] = jnp.sum(
                made * normal_ref[:, place].astype(f32), axis=0, keepdims=True
            )
            side[1:2, place] = jnp.sum(made, axis=0, keepdims=True)
            part[:, place] = made * gain_ref[1:2, place]

    ins = [(second, whole(second))]
    ins += [(piece, at((1,) + piece.shape[1:], (at_piece, 0, 0))) for piece in pieces]
    ins += [(w, kept_out) for w in expand] + [(w, kept_out) for w in contract]
    ins += [(normal, whole(normal)), (gains, whole(gains))]
    outs = [
        full_out((rows, width)),
        full_out((rows, hidden)),
        full_out((rows, hidden)),
        full_out((rows, width), f32),
        full_out((2, width), f32),
    ]
    scratch = [
        pltpu.VMEM((width, hidden), bf16),
        pltpu.VMEM((hidden, width), bf16),
        pltpu.SemaphoreType.DMA((tiles, spans)),
        pltpu.SemaphoreType.DMA((tiles, spans)),
    ]
    return run(order, flags, kernel, ins, outs, scratch, "hidden_both")


def branch_out(order, flags, groups, contract, packed, lanes):
    hidden, depth = contract[0].shape
    across = groups[0][1].shape[1]
    spans = len(contract)
    width = depth * spans
    span_rows = groups[0][0].shape[0]
    block = span_rows // lanes
    count = len(groups)

    def kernel(flag_ref, *refs):
        group_refs, refs = refs[: 2 * count], refs[2 * count :]
        contract_refs, packed_refs = refs[:spans], refs[spans : 2 * spans]
        blocks, refs = refs[2 * spans : 2 * spans + count * lanes], refs[2 * spans + count * lanes :]
        held, held_out, sems = refs
        outputs = [w.at[:across, 3 * across : 3 * across + depth] for w in packed_refs]
        started = copies(
            [ref for k in range(spans) for ref in (outputs[k], contract_refs[k])],
            [ref for k in range(spans) for ref in (held_out.at[k], held.at[k])],
            [sems.at[j] for j in range(2 * spans)],
        )
        for k in range(spans):
            started[2 * k].wait()
            started[2 * k + 1].wait()
            columns = slice(k * depth, (k + 1) * depth)
            for c in range(count):
                made = plain(group_refs[2 * c + 1][...], held_out[k])
                made = made + plain(group_refs[2 * c][...], held[k])
                for j in range(lanes):
                    rows = made[j * block : (j + 1) * block]
                    blocks[c * lanes + j][:, columns] = rows.astype(bf16)

    ins = []
    for active, attended in groups:
        ins += [(active, whole(active)), (attended, whole(attended))]
    ins += [(w, kept_out) for w in contract] + [(w, kept_out) for w in packed]
    outs = [full_out((block, width))] * (count * lanes)
    scratch = [
        pltpu.VMEM((spans, hidden, depth), bf16),
        pltpu.VMEM((spans, across, depth), bf16),
        pltpu.SemaphoreType.DMA((2 * spans,)),
    ]
    return run(order, flags, kernel, ins, outs, scratch, "branch")


def attend_back(order, flags, pieces, packed, queries, pairs, probs, tables, scale):
    rows = sum(piece.shape[1] for piece in pieces)
    width = pieces[0].shape[2]
    heads, _, head_dim = queries.shape
    spans = len(packed)
    across, depth = heads * head_dim, width // spans
    half = spans // 2

    def kernel(flag_ref, *refs):
        piece_refs, refs = refs[: len(pieces)], refs[len(pieces) :]
        packed_refs, refs = refs[:spans], refs[spans:]
        query_ref, refs = refs[0], refs[1:]
        views, refs = spread(refs[: len(pairs)]), refs[len(pairs) :]
        prob_ref, table_ref, rows_out, turned_back, keep, send, held, sems = refs
        started = copies(
            [w.at[:across, 3 * across : 3 * across + depth] for w in packed_refs],
            [held.at[:, k * depth : (k + 1) * depth] for k in range(spans)],
            [sems.at[k] for k in range(spans)],
        )
        start = 0
        for piece_ref in piece_refs:
            size = piece_ref.shape[1]
            rows_out[start : start + size, :] = piece_ref[0]
            start += size
        for copy in started:
            copy.wait()
        grads = turned(rows_out[...], held[...]).astype(bf16)
        for h in range(heads):
            made = attention_grads(
                grads[:, h * head_dim : (h + 1) * head_dim],
                query_ref[h],
                [prob_ref[k, h] for k in range(spans)],
                views,
                h,
                keep,
                send,
                scale,
            )
            turned_back[h] = turn(made, table_ref, -1).astype(bf16)

    ins = [(piece, whole(piece)) for piece in pieces] + [(w, kept_out) for w in packed]
    ins += [(array, whole(array)) for array in (queries, *pairs, probs, tables)]
    outs = [full_out((rows, width)), full_out((heads, rows, head_dim))]
    outs += [full_out((half, 2, heads, rows, head_dim))] * 2
    scratch = [pltpu.VMEM((across, width), bf16), pltpu.SemaphoreType.DMA((spans,))]
    return run(order, flags, kernel, ins, outs, scratch, "attend_back")


def hidden_back(order, flags, upstream, contract, expand, slope, normal, gains):
    span_rows, width = upstream.shape
    hidden, depth = contract[0].shape
    spans = len(contract)
    tile = min(512, hidden)
    tiles = hidden // tile

    def kernel(flag_ref, *refs):
        upstream_ref, refs = refs[0], refs[1:]
        contract_refs, refs = refs[:spans], refs[spans:]
        expand_refs, refs = refs[:spans], refs[spans:]
        slope_ref, normal_ref, gain_ref, grads, part, side, held, held_up, sems, sems_up = refs
        started = [
            copies(
                [w.at[t * tile : (t + 1) * tile, :] for w in contract_refs],
                [held.at[t, :, k * depth : (k + 1) * depth] for k in range(spans)],
                [sems.at[t, k] for k in range(spans)],
            )
            for t in range(tiles)
        ]
        started_up = copies(
            expand_refs, [held_up.at[k] for k in range(spans)], [sems_up.at[k] for k in range(spans)]
        )
        for t in range(tiles):
            for copy in started[t]:
                copy.wait()
            columns = slice(t * tile, (t + 1) * tile)
            grads[:, columns] = (
                turned(upstream_ref[...], held[t]) * slope_ref[:, columns].astype(f32)
            ).astype(bf16)
        for k in range(spans):
            started_up[k].wait()
            made = turned(grads[...], held_up[k])
            columns = slice(k * depth, (k + 1) * depth)
            side[0:1, columns] = jnp.sum(
                made * normal_ref[:, columns].astype(f32), axis=0, keepdims=True
            )
            side[1:2, columns] = jnp.sum(made, axis=0, keepdims=True)
            part[:, columns] = made * gain_ref[1:2, columns]

    ins = [(upstream, whole(upstream))]
    ins += [(w, kept_out) for w in contract] + [(w, kept_out) for w in expand]
    ins += [
        (slope, whole(slope)),
        (normal, whole(normal)),
        (gains, whole(gains)),
    ]
    outs = [
        full_out((span_rows, hidden)),
        full_out((span_rows, width), f32),
        full_out((2, width), f32),
    ]
    scratch = [
        pltpu.VMEM((tiles, tile, width), bf16),
        pltpu.VMEM((spans, depth, hidden), bf16),
        pltpu.SemaphoreType.DMA((tiles, spans)),
        pltpu.SemaphoreType.DMA((spans,)),
    ]
    return run(order, flags, kernel, ins, outs, scratch, "hidden_back")


def project_back(
    order, flags, turned_back, own, came, weights, part, normal, gains, tables, lanes
):
    heads, span_rows, head_dim = turned_back.shape
    spans = len(weights)
    width = part.shape[1]
    depth, columns = width // spans, 3 * heads * head_dim
    block = span_rows // lanes

    def kernel(flag_ref, *refs):
        query_ref, own_ref, came_ref, refs = refs[0], refs[1], refs[2], refs[3:]
        weight_refs, refs = refs[:spans], refs[spans:]
        part_ref, normal_ref, gain_ref, table_ref, grads, side, *refs = refs
        blocks, (held, sems) = refs[:lanes], refs[lanes:]
        started = copies(
            [w.at[:depth, :columns] for w in weight_refs],
            [held.at[k] for k in range(spans)],
            [sems.at[k] for k in range(spans)],
        )
        for h in range(heads):
            at_column = h * 3 * head_dim
            keys = own_ref[0, h].astype(f32) + came_ref[0, h].astype(f32)
            values = own_ref[1, h].astype(f32) + came_ref[1, h].astype(f32)
            grads[:, at_column : at_column + head_dim] = query_ref[h]
            grads[:, at_column + head_dim : at_column + 2 * head_dim] = turn(
                keys, table_ref, -1
            ).astype(bf16)
            grads[:, at_column + 2 * head_dim : at_column + 3 * head_dim] = values.astype(bf16)
        for k in range(spans):
            started[k].wait()
            made = turned(grads[...], held[k])
            span_columns = slice(k * depth, (k + 1) * depth)
            side[0:1, span_columns] = jnp.sum(
                made * normal_ref[:, span_columns].astype(f32), axis=0, keepdims=True
            )
            side[1:2, span_columns] = jnp.sum(made, axis=0, keepdims=True)
            both = (made * gain_ref[0:1, span_columns] + part_ref[:, span_columns]).astype(bf16)
            for j in range(lanes):
                blocks[j][:, span_columns] = both[j * block : (j + 1) * block]

    ins = [(array, whole(array)) for array in (turned_back, own, came)]
    ins += [(w, kept_out) for w in weights]
    ins += [(part, whole(part)), (normal, whole(normal))]
    ins += [(gains, whole(gains)), (tables, whole(tables))]
    outs = [full_out((span_rows, columns)), full_out((2, width), f32)]
    outs += [full_out((block, width))] * lanes
    scratch = [pltpu.VMEM((spans, depth, columns), bf16), pltpu.SemaphoreType.DMA((spans,))]
    return run(order, flags, kernel, ins, outs, scratch, "project_back")


def weight_sums(order, flags, lefts, rights, by_rows, spans):
    rows = sum(piece.shape[0] for piece in lefts[0][0])
    left_width = sum(group[0].shape[1] for group in lefts[0])
    right_width = sum(group[0].shape[1] for group in rights[0])
    if by_rows:
        tile = left_width // spans
        steps, block = spans // 2, (tile, right_width)
    else:
        tile = min(512, left_width)
        while left_width % tile:
            tile //= 2
        steps, block = left_width // tile, (tile, right_width // 2)
    chunk = min(1024, block[1])
    while right_width % chunk:
        chunk //= 2
    pieces = [
        [piece for groups in (lefts[s], rights[s]) for group in groups for piece in group]
        for s in (0, 1)
    ]
    most = max(len(p) for p in pieces)

    def kernel(flag_ref, *refs):
        piece_refs = (refs[: len(pieces[0])], refs[len(pieces[0]) : len(pieces[0]) + len(pieces[1])])
        keep, send, left, right, flipped, sems = refs[len(pieces[0]) + len(pieces[1]) :]
        g = pl.program_id(0)
        for s in (0, 1):

            @pl.when((g == 0) & (flag_ref[2] == s))
            def _(s=s):
                targets = []
                for held, groups in ((left, lefts[s]), (right, rights[s])):
                    column = 0
                    for group in groups:
                        row, wide = 0, group[0].shape[1]
                        for piece in group:
                            targets.append(
                                held.at[row : row + piece.shape[0], column : column + wide]
                            )
                            row += piece.shape[0]
                        column += wide
                started = copies(
                    piece_refs[s], targets, [sems.at[j] for j in range(len(targets))]
                )
                for copy in started:
                    copy.wait()

        def product(column, store):
            flipped[...] = left[:, pl.ds(pl.multiple_of(column, LANES), tile)].T

            def one(c, _):
                columns = pl.ds(pl.multiple_of(c * chunk, chunk), chunk)
                store(c, plain(flipped[...], right[:, columns]).astype(bf16))
                return 0

            lax.fori_loop(0, right_width // chunk, one, 0)

        if by_rows:

            def to(target):
                def store(c, made):
                    target[:, pl.ds(pl.multiple_of(c * chunk, chunk), chunk)] = made

                return store

            product(g * tile, to(keep))
            product((g + steps) * tile, to(send))
        else:
            half = right_width // 2 // chunk

            def store(c, made):
                @pl.when(c < half)
                def _():
                    keep[:, pl.ds(pl.multiple_of(c * chunk, chunk), chunk)] = made

                @pl.when(c >= half)
                def _():
                    send[:, pl.ds(pl.multiple_of((c - half) * chunk, chunk), chunk)] = made

            product(g * tile, store)

    ins = [(piece, kept_out) for s in (0, 1) for piece in pieces[s]]
    dims = (steps * tile, block[1])
    outs = [(shape(dims), pl.BlockSpec(block, lambda g: (g, 0)))] * 2
    scratch = [
        pltpu.VMEM((rows, left_width), bf16),
        pltpu.VMEM((rows, right_width), bf16),
        pltpu.VMEM((tile, rows), bf16),
        pltpu.SemaphoreType.DMA((most,)),
    ]
    return run(
        order, flags, kernel, ins, outs, scratch, "weight_sums", grid=(steps,)
    )


def fold(order, flags, keep, came, dim):
    rows, columns = keep.shape
    if dim == 0:
        tile = rows // 4
        steps, block = rows // 2 // tile, (tile, columns)
        places = [lambda g: (g, 0), lambda g: (g + steps, 0)]
        half = (rows // 2, columns)
    else:
        tile = rows // 4
        steps, block = rows // tile, (tile, columns // 2)
        places = [lambda g: (g, 0), lambda g: (g, 1)]
        half = (rows, columns // 2)

    def kernel(flag_ref, keep_low, keep_high, came_low, came_high, low, high):
        low[...] = (keep_low[...].astype(f32) + came_low[...].astype(f32)).astype(bf16)
        high[...] = (keep_high[...].astype(f32) + came_high[...].astype(f32)).astype(bf16)

    ins = [(array, pl.BlockSpec(block, place)) for array in (keep, came) for place in places]
    outs = [(shape(half), pl.BlockSpec(block, lambda g: (g, 0)))] * 2
    return run(order, flags, kernel, ins, outs, [], "fold", grid=(steps,))


def shards(
    block_input,
    out_grad,
    triple_weight,
    output_weight,
    expand_weight,
    contract_weight,
    norm_gains,
    norm_biases,
):
    section = lax.axis_index("pipe")
    span = lax.axis_index("ctx")
    lane = lax.axis_index("tp")
    spans = lax.axis_size("ctx")
    lanes = lax.axis_size("tp")
    micros, rows, width = block_input.shape
    span_rows = rows * lanes
    heads = triple_weight.shape[2]
    head_dim = triple_weight.shape[4]
    across_units = heads * head_dim
    scale = head_dim ** (-0.5)
    first_section = section == 0
    both = (0, 1)

    def hop(array, axis, step, sections):
        size = lax.axis_size(axis)
        pairs = [(s * size + a, s * size + (a ^ step)) for s in sections for a in range(size)]
        return lax.ppermute(array, ("pipe", axis), pairs)

    order = Order()

    def flags_for(wanted):
        return jnp.stack([jnp.asarray(wanted), span, section]).astype(jnp.int32)

    flags = [flags_for(section == s) for s in both]
    always = flags_for(1)

    kept = [[SimpleNamespace() for _ in range(micros)] for _ in both]
    due = {}
    slot_index = [0]

    def slot(hops, kernels=()):
        now = slot_index[0]
        slot_index[0] += 1
        ready = due.pop(now, [])
        hops = [h if len(h) == 3 else h + (1,) for h in hops]
        if hops:
            gated = fence([operand for operand, _, _ in hops], order.last + ready)
            order.last = [min(gated, key=lambda array: array.size)]
            for passed, (_, go, slots) in zip(gated, hops):
                results = go(passed)
                results = results if isinstance(results, list) else [results]
                due.setdefault(now + slots, []).extend(results)
        else:
            order.last = order.last + ready
        for kernel in kernels:
            kernel()

    def halved(keep, came, dim):
        middle = keep.shape[dim] // 2
        total = keep.astype(f32) + came.astype(f32)
        return (
            lax.slice_in_dim(total, 0, middle, axis=dim).astype(bf16),
            lax.slice_in_dim(total, middle, 2 * middle, axis=dim).astype(bf16),
        )

    def spread_hops(pieces, axis, axis_name, sections, first):
        step = lax.axis_size(axis_name) // 4
        going = first
        while step:
            pieces.append(hop(going, axis_name, step, sections))
            going = jnp.concatenate(pieces, axis=axis)
            step //= 2
        return pieces[-1]

    def fold_hops(k, first, axis_name, dim, sections):
        step, size = 1, lax.axis_size(axis_name)
        while 2 * step < size:
            came = hop(first, axis_name, step, sections)
            k.keep, k.send = halved(k.keep, came, dim)
            first = k.send
            step *= 2
        return came

    depth = width // spans
    far = spans // 2
    assert depth == across_units
    small = jnp.concatenate([norm_gains[0], norm_biases[0]], axis=0)
    packed = jnp.concatenate(
        [triple_weight[0].reshape(depth, -1), output_weight[0].reshape(-1, depth)],
        axis=1,
    )
    packed = jnp.pad(packed, ((0, 16), (0, 0)))
    packed = lax.dynamic_update_slice(packed, small, (depth, 0))
    own_expand, own_contract = expand_weight[0], contract_weight[0]
    hidden = own_expand.shape[1]
    inputs = xor_blocks(block_input, span, spans)
    cotangent = xor_blocks(out_grad, span, spans)
    early = jnp.where(first_section, inputs, cotangent)

    in_row = jnp.arange(rows, dtype=jnp.int32)
    in_span = jnp.concatenate([(lane ^ j) * rows + in_row for j in doubling(lanes)])
    positions = span * span_rows + in_span
    key_positions = jnp.stack([(span ^ k) * span_rows + in_span for k in doubling(spans)])
    tables = rope_tables(positions)
    position_column = positions[:, None]
    key_positions = key_positions[:, None, :]

    def blocks_of(own, came):
        held, step = {0: own, far: came}, far // 2
        while step:
            for k in list(held):
                held[k ^ step] = hop(held[k], "ctx", step, both)
            step //= 2
        return [held[k] for k in doubling(spans)]

    lane_offsets = doubling(lanes)

    def across(array, j, source):
        pairs = [(source * lanes + a, (1 - source) * lanes + (a ^ j)) for a in range(lanes)]
        return lax.ppermute(array, ("pipe", "tp"), pairs)

    def rows_far(s, m):
        k = kept[s][m]

        def go(passed):
            k.rows = passed
            k.pieces = [passed, hop(passed, "tp", lanes // 2, (s,))]
            return k.pieces[1]

        return k.rows, go

    def rows_near(s, m):
        k = kept[s][m]

        def go(passed):
            last_piece = spread_hops(k.pieces, 0, "tp", (s,), passed)
            k.row_pieces = [piece[None] for piece in k.pieces]
            return last_piece

        return jnp.concatenate(k.pieces, axis=0), go

    def pair_far(s, m):
        k = kept[s][m]

        def go(passed):
            k.pairs = [passed, hop(passed, "ctx", far, (s,))]
            return k.pairs[1]

        return k.pair, go

    def pair_near(s, m):
        k = kept[s][m]

        def go(passed):
            return spread_hops(k.pairs, 0, "ctx", (s,), passed)

        return jnp.concatenate(k.pairs, axis=0), go

    def pair_grad_near(s, m):
        k = kept[s][m].pair_grad
        return k.send, lambda passed: fold_hops(k, passed, "ctx", 0, (s,))

    def pair_grad_far(s, m):
        k = kept[s][m].pair_grad

        def go(passed):
            k.came = hop(passed, "ctx", far, (s,))
            return k.came

        return k.send, go

    def sum_hops(s, m):
        blocks = kept[s][m].blocks
        arrived = kept[s][m].arrived = []

        def one(j):
            def go(passed):
                arrived.append(hop(passed, "tp", lane_offsets[j], (s,)))
                return arrived[-1]

            return blocks[j], go

        return [one(j) for j in range(1, lanes)]

    def sum_near(s, m):
        k = kept[s][m]
        k.keep = jnp.concatenate(k.blocks[: lanes // 2], axis=0)
        going = jnp.concatenate(k.blocks[lanes // 2 :], axis=0)
        return going, lambda passed: fold_hops(k, passed, "tp", 0, (s,))

    def sum_far(s, m):
        k = kept[s][m]

        def go(passed):
            k.blocks, k.arrived = [k.keep], [hop(passed, "tp", lanes // 2, (s,))]
            return k.arrived[0]

        return k.send, go

    def total_of(k):
        return sum(array.astype(f32) for array in [k.blocks[0], *k.arrived])

    def norm_back(upstream, combined, entering):
        normalized, inverse = normalize(entering.astype(f32))
        return (
            upstream.astype(f32)
            + inverse
            * (
                combined
                - jnp.mean(combined, axis=-1, keepdims=True)
                - normalized * jnp.mean(combined * normalized, axis=-1, keepdims=True)
            )
        ).astype(bf16)

    def middle_of(m):
        return (inputs[m].astype(f32) + total_of(kept[0][m])).astype(bf16)

    def entry_of(m):
        k = kept[1][m]
        return norm_back(cotangent[m], total_of(k), k.rows)

    def hand(s, m):
        k, other = kept[s][m], kept[1 - s][m]
        k.given = middle_of(m) if s == 0 else entry_of(m)

        def go(passed):
            k.given = passed
            pieces = [across(passed, j, s) for j in lane_offsets]
            other.rows = pieces[0]
            other.row_pieces = [piece[None] for piece in pieces]
            return pieces

        return k.given, go

    def hand_one(s, m):
        k, other = kept[s][m], kept[1 - s][m]
        k.given = middle_of(m) if s == 0 else entry_of(m)

        def go(passed):
            k.given = passed
            other.rows = across(passed, 0, s)
            return other.rows

        return k.given, go

    def run_project(s, m):
        k = kept[s][m]
        pieces, place = (early_pieces, m) if s == 0 else (k.row_pieces, 0)
        k.first, k.second, k.normal, k.queries, pair = project(
            order, flags[s], pieces, place, gains, biases, tables, packed, heads, head_dim
        )
        k.pair = pair[None]

    def run_expand(m):
        k = kept[0][m]
        k.active, k.slope = expand_up(order, flags[0], k.second, expand, span_rows)

    def run_attend(m):
        k = kept[0][m]
        k.attended, k.probs = attend(
            order, flags[0], k.queries, k.pairs, position_column, key_positions, scale
        )

    def run_branch(m):
        k = kept[0][m]
        k.blocks = branch_out(
            order, flags[0], [(k.active, k.attended)], contract, packed, lanes
        )

    def run_hidden_both(m):
        k = kept[1][m]
        k.upstream, k.active, k.hidden, k.part, k.side_second = hidden_both(
            order, flags[1], k.second, early_pieces, m, expand, contract, k.normal, gains
        )

    def run_attend_both(m):
        k = kept[1][m]
        k.attended, k.turned_back, keep, send = attend_both(
            order,
            flags[1],
            k.upstream,
            packed,
            k.queries,
            k.pairs,
            position_column,
            key_positions,
            tables,
            scale,
        )
        k.pair_grad = SimpleNamespace(keep=keep, send=send)

    def run_attend_back(m):
        k = kept[0][m]
        k.upstream, k.turned_back, keep, send = attend_back(
            order,
            flags[0],
            k.row_pieces,
            packed,
            k.queries,
            k.pairs,
            k.probs,
            tables,
            scale,
        )
        k.pair_grad = SimpleNamespace(keep=keep, send=send)

    def run_hidden_back(m):
        k = kept[0][m]
        k.hidden, k.part, k.side_second = hidden_back(
            order,
            flags[0],
            k.upstream,
            contract,
            expand,
            k.slope,
            k.normal,
            gains,
        )

    def run_project_back(s, m):
        k = kept[s][m]
        own, arrived = k.pair_grad.keep, k.pair_grad.came
        k.stacked, k.side_first, *k.blocks = project_back(
            order,
            flags[s],
            k.turned_back,
            own.reshape(own.shape[1:]),
            arrived.reshape(arrived.shape[1:]),
            packed,
            k.part,
            k.normal,
            gains,
            tables,
            lanes,
        )

    def of(name, s, count=micros):
        return [getattr(kept[s][m], name) for m in range(count)]

    branch_sums, expand_sums, triple_sums = (SimpleNamespace(parts=[]) for _ in range(3))

    def run_sums(w, lefts, rights, by_rows):
        w.dim = 0 if by_rows else 1
        w.keep, w.send = weight_sums(order, always, lefts, rights, by_rows, spans)

    def wide_near(w):
        def go(passed):
            w.came = hop(passed, "ctx", 1, both)
            return w.came

        return w.send, go

    def run_fold(w):
        step = 2
        w.keep, w.send = fold(order, always, w.keep, w.came, w.dim)
        while 2 * step < spans:
            w.came = hop(w.send, "ctx", step, both)
            w.keep, w.send = fold(order, always, w.keep, w.came, w.dim)
            step *= 2

    def wide_far(w, start, stop):
        def go(passed):
            w.parts.append(hop(passed, "ctx", far, both))
            return w.parts[-1]

        return w.send[start:stop], go

    weights = SimpleNamespace(expand_came=[], contract_came=[])
    half_depth = depth // 2

    def expand_far(start, stop):
        def go(passed):
            weights.expand_came.append(hop(passed, "ctx", far, both))
            return weights.expand_came[-1]

        return own_expand[start:stop], go

    def packed_far(passed):
        weights.packed_came = hop(passed, "ctx", far, both)
        return weights.packed_came

    def packed_near(passed):
        weights.packed = blocks_of(packed, passed)
        return weights.packed[1:]

    def expand_near(passed):
        weights.expand = blocks_of(own_expand, passed)
        return weights.expand[1:]

    def contract_far(start, stop):
        def go(passed):
            weights.contract_came.append(hop(passed, "ctx", far, both))
            return weights.contract_came[-1]

        return own_contract[start:stop], go

    def contract_near(passed):
        weights.contract = blocks_of(own_contract, passed)
        return weights.contract[1:]

    def early_hops(passed):
        weights.early = [passed] + [hop(passed, "tp", j, both) for j in lane_offsets[1:]]
        return weights.early[1:]

    due[0] = [expand_far(0, half_depth)[1](own_expand[:half_depth])]
    slot([(packed, packed_far), expand_far(half_depth, depth), (early, early_hops)])
    early_pieces = weights.early
    slot(
        [
            (weights.packed_came, packed_near),
            (jnp.concatenate(weights.expand_came, axis=0), expand_near, 2),
        ]
    )
    packed, expand = weights.packed, weights.expand
    small_full = jnp.concatenate(
        [piece[depth : depth + 4, :depth] for piece in packed], axis=1
    ).astype(f32)
    gains, biases = small_full[:2], small_full[2:]
    slot(
        [contract_far(0, hidden // 2)],
        [lambda m=m: run_project(0, m) for m in range(micros)],
    )
    slot(
        [pair_far(0, 0), contract_far(hidden // 2, hidden)],
        [lambda m=m: run_expand(m) for m in range(micros)],
    )
    contract_came = jnp.concatenate(weights.contract_came, axis=0)
    slot([(contract_came, contract_near), pair_near(0, 0)])
    contract = weights.contract
    slot([pair_far(0, 1)], [lambda: run_attend(0), lambda: run_branch(0)])
    slot(sum_hops(0, 0) + [pair_near(0, 1), pair_far(0, 2)])
    slot([hand(0, 0), pair_near(0, 2)], [lambda: run_attend(1), lambda: run_branch(1)])
    slot(
        sum_hops(0, 1),
        [lambda: run_project(1, 0), lambda: run_attend(2), lambda: run_branch(2)],
    )
    slot([pair_far(1, 0)], [lambda: run_hidden_both(0)])
    slot([pair_near(1, 0)])
    slot([hand(0, 1)], [lambda: run_attend_both(0)])
    slot([pair_grad_near(1, 0)] + sum_hops(0, 2), [lambda: run_project(1, 1)])
    slot([pair_far(1, 1), pair_grad_far(1, 0)], [lambda: run_hidden_both(1)])
    slot([pair_near(1, 1)], [lambda: run_project_back(1, 0)])
    slot([hand(0, 2)], [lambda: run_attend_both(1)])
    slot([pair_grad_near(1, 1)], [lambda: run_project(1, 2)])
    slot(
        [pair_far(1, 2), pair_grad_far(1, 1), sum_near(1, 0)], [lambda: run_hidden_both(2)]
    )
    slot([pair_near(1, 2), sum_far(1, 0)], [lambda: run_project_back(1, 1)])
    slot([hand_one(1, 0)], [lambda: run_attend_both(2)])
    slot([pair_grad_near(1, 2), rows_far(0, 0)])
    slot([pair_grad_far(1, 2), rows_near(0, 0)] + sum_hops(1, 1))
    slot([hand_one(1, 1)], [lambda: run_project_back(1, 2), lambda: run_attend_back(0)])
    finals = [SimpleNamespace(arrived=[]) for _ in range(micros)]

    def run_final_branch():
        blocks = branch_out(
            order,
            flags[1],
            [(k.active, k.attended) for k in kept[1]],
            contract,
            packed,
            lanes,
        )
        for m in range(micros):
            finals[m].blocks = blocks[m * lanes : (m + 1) * lanes]

    def final_hops(m):
        def one(j):
            def go(passed):
                finals[m].arrived.append(hop(passed, "tp", lane_offsets[j], (1,)))
                return finals[m].arrived[-1]

            return finals[m].blocks[j], go

        return [one(j) for j in range(1, lanes)]

    slot(
        sum_hops(1, 2) + [rows_far(0, 1), pair_grad_near(0, 0)],
        [lambda: run_hidden_back(0), run_final_branch],
    )
    slot([hand(1, 2), rows_near(0, 1)])
    last = micros - 1
    slot(
        [pair_grad_far(0, 0)] + final_hops(0),
        [
            lambda: run_sums(
                branch_sums,
                [[of("active", s), of("attended", s)] for s in both],
                [
                    [
                        of("upstream", 0, 1)
                        + [piece[0] for k in kept[0][1:] for piece in k.row_pieces]
                    ],
                    [of("upstream", 1)],
                ],
                False,
            )
        ],
    )
    slot(
        [wide_near(branch_sums)] + final_hops(1),
        [lambda: run_attend_back(2), lambda: run_attend_back(1)],
    )
    slot(
        [pair_grad_near(0, 2), pair_grad_near(0, 1)] + final_hops(2),
        [lambda: run_fold(branch_sums)],
    )
    cut = [0, hidden // 2, 3 * hidden // 4, hidden, hidden + across_units]
    slot(
        [wide_far(branch_sums, cut[0], cut[1]), pair_grad_far(0, 2), pair_grad_far(0, 1)],
        [lambda: run_hidden_back(2), lambda: run_hidden_back(1)],
    )
    slot(
        [wide_far(branch_sums, cut[1], cut[2])],
        [lambda m=m: run_project_back(0, m) for m in range(micros)],
    )
    slot(
        [wide_far(branch_sums, cut[2], cut[3])] + sum_hops(0, 0),
        [
            lambda: run_sums(
                triple_sums,
                [[of("first", s)] for s in both],
                [[of("stacked", s)] for s in both],
                True,
            )
        ],
    )
    slot(
        [wide_far(branch_sums, cut[3], cut[4]), wide_near(triple_sums)],
        [
            lambda: run_sums(
                expand_sums,
                [[of("second", s)] for s in both],
                [[of("hidden", s)] for s in both],
                True,
            )
        ],
    )

    def side_of(mades):
        return sum(
            jnp.concatenate([k.side_first, k.side_second], axis=0) for k in mades
        )

    side = SimpleNamespace(
        all=jnp.where(first_section, side_of(kept[0]), side_of(kept[1])), step=1
    )

    def side_ctx():
        middle = side.all.shape[1] // 2

        def go(passed):
            came = hop(passed, "ctx", side.step, both)
            side.all = side.all[:, :middle] + came
            side.step *= 2
            return came

        return side.all[:, middle:], go

    def side_tp(passed):
        step = 1
        while step < lanes:
            came = hop(passed, "tp", step, both)
            passed = passed + came
            step *= 2
        side.all = passed
        return came

    slot([wide_near(expand_sums), side_ctx()], [lambda: run_fold(triple_sums)])
    slot(
        [wide_far(triple_sums, 0, depth), side_ctx()] + sum_hops(0, 1),
        [lambda: run_fold(expand_sums)],
    )
    while side.step < spans:
        slot([side_ctx()])
    slot([wide_far(expand_sums, 0, half_depth), (side.all, side_tp)] + sum_hops(0, 2))
    slot([wide_far(expand_sums, half_depth, depth)])

    def wide_total(keep, parts):
        came = jnp.concatenate(parts, axis=0) if len(parts) > 1 else parts[0]
        return keep.astype(f32) + came.astype(f32)

    contract_grads = wide_total(branch_sums.keep[:hidden], branch_sums.parts[:3])
    output_grads = wide_total(branch_sums.keep[hidden:], branch_sums.parts[3:])
    expand_grads = wide_total(expand_sums.keep, expand_sums.parts)
    triple_grads = wide_total(triple_sums.keep, triple_sums.parts)
    layer_outputs = jnp.stack(
        [
            jnp.where(
                first_section,
                kept[0][m].given,
                (kept[1][m].rows.astype(f32) + total_of(finals[m])).astype(bf16),
            )
            for m in range(micros)
        ]
    )
    entry_grads = jnp.stack(
        [
            jnp.where(
                first_section,
                norm_back(kept[0][m].rows, total_of(kept[0][m]), inputs[m]),
                kept[1][m].given,
            )
            for m in range(micros)
        ]
    )
    gain_grads = jnp.stack([side.all[0], side.all[2]])
    bias_grads = jnp.stack([side.all[1], side.all[3]])
    return (
        xor_blocks(layer_outputs, span, spans, inverse=True)[None],
        xor_blocks(entry_grads, span, spans, inverse=True)[None],
        triple_grads.reshape(triple_weight.shape),
        output_grads.reshape(output_weight.shape),
        expand_grads[None],
        contract_grads[None],
        gain_grads[None],
        bias_grads[None],
    )


def solution(mesh):
    return jax.shard_map(
        shards,
        mesh=mesh,
        in_specs=(
            P(None, ("ctx", "tp"), None),
            P(None, ("ctx", "tp"), None),
            P("pipe", "ctx", "tp", None, None),
            P("pipe", "tp", None, "ctx"),
            P("pipe", "ctx", "tp"),
            P("pipe", "tp", "ctx"),
            P("pipe", None, "ctx"),
            P("pipe", None, "ctx"),
        ),
        out_specs=(
            P("pipe", None, ("ctx", "tp"), None),
            P("pipe", None, ("ctx", "tp"), None),
            P("pipe", "ctx", "tp", None, None),
            P("pipe", "tp", None, "ctx"),
            P("pipe", "ctx", "tp"),
            P("pipe", "tp", "ctx"),
            P("pipe", None, "ctx"),
            P("pipe", None, "ctx"),
        ),
        check_vma=False,
    )
```

```python
import functools
from types import SimpleNamespace

import jax
import jax.numpy as jnp
from jax import lax
from jax.experimental import pallas as pl
from jax.experimental.pallas import tpu as pltpu
from jax.sharding import PartitionSpec as P

ROT = 64
LANES = 128
epsilon = 1e-05
masked_score = -1e30
f32 = jnp.float32
bf16 = jnp.bfloat16
vmem_bytes = 56 * 1024 * 1024
half_root = 0.7071067811865476
bell = 0.3989422804014327


def dot(a, b, dims):
    return lax.dot_general(a, b, (dims, ((), ())), preferred_element_type=f32)


def plain(a, b):
    return dot(a, b, ((1,), (0,)))


def turned(a, b):
    return dot(a, b, ((1,), (1,)))


def doubling(count):
    order, step = [0], count // 2
    while step:
        order += [k ^ step for k in order]
        step //= 2
    return order


def xor_blocks(values, index, count, inverse=False):
    width = values.shape[-1] // count
    order = doubling(count)

    def taken(places):
        return jnp.concatenate(
            [values[..., k * width : (k + 1) * width] for k in places], axis=-1
        )

    if inverse:
        values = taken([order.index(k) for k in range(count)])
    step = 1
    while step < count:
        swapped = taken([k ^ step for k in range(count)])
        values = jnp.where((index & step) != 0, swapped, values)
        step *= 2
    return values if inverse else taken(order)


def rope_tables(positions):
    half = ROT // 2
    frequency = 10000.0 ** (-jnp.arange(0, ROT, 2, dtype=f32) / ROT)
    angles = positions.astype(f32)[:, None] * frequency[None, :]
    cosine, sine = jnp.cos(angles), jnp.sin(angles)
    count = positions.shape[0]
    rest = jnp.zeros((count, LANES - ROT), f32)
    none = jnp.zeros((count, half), f32)
    return jnp.stack(
        [
            jnp.concatenate([cosine, cosine, rest + 1.0], axis=1),
            jnp.concatenate([-sine, none, rest], axis=1),
            jnp.concatenate([none, sine, rest], axis=1),
        ]
    )


def turn(values, tables, sign):
    half = ROT // 2
    part = values[:, :LANES]
    moved = (
        pltpu.roll(part, LANES - half, 1) * tables[1] + pltpu.roll(part, half, 1) * tables[2]
    )
    part = part * tables[0] + (moved if sign > 0 else -moved)
    return jnp.concatenate([part, values[:, LANES:]], axis=1)


def normalize(values):
    center = values - jnp.mean(values, axis=-1, keepdims=True)
    inverse = lax.rsqrt(jnp.mean(center * center, axis=-1, keepdims=True) + epsilon)
    return (center * inverse, inverse)


def whole(array):
    zeros = (0,) * array.ndim
    return pl.BlockSpec(array.shape, lambda *_: zeros)


def at(block, place):
    return pl.BlockSpec(block, lambda *_: place)


kept_out = pl.BlockSpec(memory_space=pl.ANY)


def shape(dims, dtype=bf16):
    return jax.ShapeDtypeStruct(dims, dtype)


class Order:
    def __init__(self):
        self.last = []

    def follow(self, results):
        self.last = [min(results, key=lambda array: array.size * array.dtype.itemsize)]

    def also(self, array):
        self.last = self.last + [array]


took = dict(
    project=7,
    expand=8,
    attend=5,
    branch=8,
    hidden_both=14,
    attend_both=11,
    attend_back=8,
    hidden_back=13,
    project_back=8,
    weight_sums=16,
    fold=6,
    owner_sums=14,
)
peak = 1.15e9


def run(order, flags, kernel, ins, outs, scratch, name, grid=(1,), in_place={}):
    taken = len(ins)
    ins = [(flags, pl.BlockSpec(memory_space=pltpu.SMEM))] + list(ins)
    ins += [(array, kept_out) for array in order.last]
    arrays = [array for array, _ in ins]

    def body(flag_ref, *refs):
        @pl.when(flag_ref[0] == 1)
        def _():
            kernel(flag_ref, *refs[:taken], *refs[len(ins) - 1 :])

    results = pl.pallas_call(
        body,
        grid=grid,
        in_specs=[spec for _, spec in ins],
        out_specs=[spec for _, spec in outs],
        out_shape=[struct for struct, _ in outs],
        scratch_shapes=scratch,
        input_output_aliases=in_place,
        compiler_params=pltpu.CompilerParams(vmem_limit_bytes=vmem_bytes),
        cost_estimate=pl.CostEstimate(
            flops=int(took[name] * peak), bytes_accessed=0, transcendentals=0
        ),
        name=name,
    )(*arrays)
    order.follow(results)
    return results


def fence(through, waits):
    count = len(through)

    def kernel(*refs):
        pass

    return pl.pallas_call(
        kernel,
        in_specs=[kept_out] * (count + len(waits)),
        out_specs=[kept_out] * count,
        out_shape=[shape(array.shape, array.dtype) for array in through],
        input_output_aliases={j: j for j in range(count)},
        compiler_params=pltpu.CompilerParams(vmem_limit_bytes=vmem_bytes),
        cost_estimate=pl.CostEstimate(flops=1, bytes_accessed=1, transcendentals=0),
        name="fence",
    )(*through, *waits)


def full_out(dims, dtype=bf16):
    zeros = (0,) * len(dims)
    return (shape(dims, dtype), pl.BlockSpec(dims, lambda *_: zeros))


def copies(sources, targets, sems):
    started = []
    for source, target, sem in zip(sources, targets, sems):
        copy = pltpu.make_async_copy(source, target, sem)
        copy.start()
        started.append(copy)
    return started


def project(order, flags, pieces, at_piece, gains, biases, tables, weights, heads, head_dim):
    count, width = 1, pieces[0].shape[2]
    span_rows = sum(piece.shape[1] for piece in pieces)
    rows = count * span_rows
    chunk = pieces[0].shape[1]
    spans = len(weights)
    depth = width // spans
    wide = 3 * head_dim
    columns = heads * wide

    def kernel(flag_ref, *refs):
        piece_refs = refs[: len(pieces)]
        gain_ref, bias_ref, table_ref = refs[len(pieces) : len(pieces) + 3]
        weight_refs = refs[len(pieces) + 3 : len(pieces) + 3 + spans]
        first, second, normal, queries, pair, held, sems = refs[len(pieces) + 3 + spans :]
        started = []
        for h in range(heads):
            started.append(
                copies(
                    [w.at[:depth, h * wide : (h + 1) * wide] for w in weight_refs],
                    [held.at[h, k * depth : (k + 1) * depth] for k in range(spans)],
                    [sems.at[h, k] for k in range(spans)],
                )
            )
        start = 0
        for piece_ref in piece_refs:
            chunks = piece_ref.shape[1] // chunk

            def one(i, _, piece_ref=piece_ref, start=start, chunks=chunks):
                m, c = i // chunks, i % chunks
                values = piece_ref[m, pl.ds(pl.multiple_of(c * chunk, chunk), chunk), :]
                normed, _ = normalize(values.astype(f32))
                to = pl.ds(
                    pl.multiple_of(m * span_rows + start + c * chunk, chunk), chunk
                )
                normal[to, :] = normed.astype(bf16)
                first[to, :] = (normed * gain_ref[0:1] + bias_ref[0:1]).astype(bf16)
                second[to, :] = (normed * gain_ref[1:2] + bias_ref[1:2]).astype(bf16)
                return 0

            lax.fori_loop(0, count * chunks, one, 0)
            start += piece_ref.shape[1]
        for h in range(heads):
            for copy in started[h]:
                copy.wait()

            def two(m, _, h=h):
                to = pl.ds(pl.multiple_of(m * span_rows, span_rows), span_rows)
                made = plain(first[to, :], held[h])
                queries[h, to, :] = turn(made[:, :head_dim], table_ref, 1).astype(bf16)
                pair[0, h, to, :] = turn(
                    made[:, head_dim : 2 * head_dim], table_ref, 1
                ).astype(bf16)
                pair[1, h, to, :] = made[:, 2 * head_dim :].astype(bf16)
                return 0

            lax.fori_loop(0, count, two, 0)

    ins = [(piece, at((1,) + piece.shape[1:], (at_piece, 0, 0))) for piece in pieces]
    ins += [(array, whole(array)) for array in (gains, biases, tables)]
    ins += [(w, kept_out) for w in weights]
    outs = [full_out((rows, width))] * 3 + [
        full_out((heads, rows, head_dim)),
        full_out((2, heads, rows, head_dim)),
    ]
    scratch = [
        pltpu.VMEM((heads, width, wide), bf16),
        pltpu.SemaphoreType.DMA((heads, spans)),
    ]
    return run(order, flags, kernel, ins, outs, scratch, "project")


def expand_up(order, flags, second, weights, span_rows, room):
    rows, width = second.shape
    depth, hidden = weights[0].shape
    spans = len(weights)
    tile = min(512, hidden)
    tiles = hidden // tile

    def kernel(flag_ref, *refs):
        second_ref, weight_refs = refs[0], refs[1 : 1 + spans]
        active, slope, held, sems = refs[1 + spans :]
        started = []
        for t in range(tiles):
            started.append(
                copies(
                    [w.at[:, t * tile : (t + 1) * tile] for w in weight_refs],
                    [held.at[t, k * depth : (k + 1) * depth] for k in range(spans)],
                    [sems.at[t, k] for k in range(spans)],
                )
            )
        for t in range(tiles):
            for copy in started[t]:
                copy.wait()

            def one(m, _, t=t):
                to = pl.ds(pl.multiple_of(m * span_rows, span_rows), span_rows)
                pre = plain(second_ref[to, :], held[t])
                risen = 0.5 * (1.0 + lax.erf(pre * half_root))
                columns = slice(t * tile, (t + 1) * tile)
                active[to, columns] = (pre * risen).astype(bf16)
                slope[to, columns] = (
                    risen + pre * jnp.exp(-0.5 * pre * pre) * bell
                ).astype(bf16)
                return 0

            lax.fori_loop(0, rows // span_rows, one, 0)

    ins = [(second, whole(second))] + [(w, kept_out) for w in weights]
    outs = [
        (shape((rows, hidden + room)), at((rows, hidden), (0, 0))),
        full_out((rows, hidden)),
    ]
    scratch = [
        pltpu.VMEM((tiles, width, tile), bf16),
        pltpu.SemaphoreType.DMA((tiles, spans)),
    ]
    return run(order, flags, kernel, ins, outs, scratch, "expand")


def spread(refs):
    return [ref.at[j] for ref in refs for j in range(ref.shape[0])]


def attention(here, pairs, head, row_ref, key_ref, scale):
    scores = []
    for k, pair in enumerate(pairs):
        raw = turned(here, pair[0, head]) * scale
        scores.append(jnp.where(key_ref[k] <= row_ref[...], raw, masked_score))
    top = functools.reduce(
        jnp.maximum, [jnp.max(part, axis=1, keepdims=True) for part in scores]
    )
    scores = [jnp.exp(part - top) for part in scores]
    inverse = 1.0 / sum(jnp.sum(part, axis=1, keepdims=True) for part in scores)
    return [part * inverse for part in scores]


def attend(order, flags, units, queries, pairs, positions, key_positions, scale):
    heads, rows, head_dim = queries.shape
    spans = sum(pair.shape[0] for pair in pairs)
    across = heads * head_dim

    def kernel(flag_ref, units_ref, query_ref, *refs):
        views, refs = spread(refs[: len(pairs)]), refs[len(pairs) :]
        row_ref, key_ref, attended, probs = refs
        for h in range(heads):
            parts = attention(query_ref[h], views, h, row_ref, key_ref, scale)
            summed = None
            for k in range(spans):
                part = parts[k].astype(bf16)
                probs[k, h] = part
                term = plain(part, views[k][1, h])
                summed = term if summed is None else summed + term
            attended[:, h * head_dim : (h + 1) * head_dim] = summed.astype(bf16)

    ins = [(units, kept_out)]
    ins += [(array, whole(array)) for array in (queries, *pairs, positions, key_positions)]
    outs = [
        (shape(units.shape), at((rows, across), (0, units.shape[1] // across - 1))),
        full_out((spans, heads, rows, rows)),
    ]
    return run(order, flags, kernel, ins, outs, [], "attend", in_place={1: 0})


def attention_grads(grad, here, parts, views, head, keep, send, scale):
    half = keep.shape[0]
    grad_probs = [turned(grad, view[1, head]) for view in views]
    delta = sum(
        jnp.sum(part.astype(f32) * slope, axis=1, keepdims=True)
        for part, slope in zip(parts, grad_probs)
    )
    query_grad = None
    for k, view in enumerate(views):
        slopes = (parts[k].astype(f32) * (grad_probs[k] - delta)).astype(bf16)
        term = plain(slopes, view[0, head])
        query_grad = term if query_grad is None else query_grad + term
        side = keep if k < half else send
        side[k % half, 0, head] = (dot(slopes, here, ((0,), (0,))) * scale).astype(bf16)
        side[k % half, 1, head] = dot(parts[k].astype(bf16), grad, ((0,), (0,))).astype(bf16)
    return query_grad * scale


def attend_both(
    order, flags, rows_in, packed, queries, pairs, positions, key_positions, tables, scale
):
    heads, rows, head_dim = queries.shape
    width = rows_in.shape[1]
    spans = len(packed)
    across, depth = heads * head_dim, width // spans
    half = spans // 2

    def kernel(flag_ref, rows_ref, *refs):
        packed_refs, refs = refs[:spans], refs[spans:]
        query_ref, refs = refs[0], refs[1:]
        views, refs = spread(refs[: len(pairs)]), refs[len(pairs) :]
        row_ref, key_ref, table_ref, attended, turned_back, keep, send, held, sems = refs
        started = copies(
            [w.at[:across, 3 * across : 3 * across + depth] for w in packed_refs],
            [held.at[:, k * depth : (k + 1) * depth] for k in range(spans)],
            [sems.at[k] for k in range(spans)],
        )
        all_parts = []
        for h in range(heads):
            parts = attention(query_ref[h], views, h, row_ref, key_ref, scale)
            summed = None
            for k in range(spans):
                term = plain(parts[k].astype(bf16), views[k][1, h])
                summed = term if summed is None else summed + term
            attended[:, h * head_dim : (h + 1) * head_dim] = summed.astype(bf16)
            all_parts.append(parts)
        for copy in started:
            copy.wait()
        grads = turned(rows_ref[...], held[...]).astype(bf16)
        for h in range(heads):
            made = attention_grads(
                grads[:, h * head_dim : (h + 1) * head_dim],
                query_ref[h],
                all_parts[h],
                views,
                h,
                keep,
                send,
                scale,
            )
            turned_back[h] = turn(made, table_ref, -1).astype(bf16)

    ins = [(rows_in, whole(rows_in))] + [(w, kept_out) for w in packed]
    ins += [
        (array, whole(array)) for array in (queries, *pairs, positions, key_positions, tables)
    ]
    outs = [full_out((rows, across)), full_out((heads, rows, head_dim))]
    outs += [full_out((half, 2, heads, rows, head_dim))] * 2
    scratch = [pltpu.VMEM((across, width), bf16), pltpu.SemaphoreType.DMA((spans,))]
    return run(order, flags, kernel, ins, outs, scratch, "attend_both")


def hidden_both(order, flags, second, pieces, at_piece, expand, contract, normal, gains):
    rows, width = second.shape
    hidden, depth = contract[0].shape
    spans = len(contract)
    tile = min(512, hidden)
    tiles = hidden // tile

    def kernel(flag_ref, second_ref, *refs):
        piece_refs, refs = refs[: len(pieces)], refs[len(pieces) :]
        expand_refs, refs = refs[:spans], refs[spans:]
        contract_refs, refs = refs[:spans], refs[spans:]
        normal_ref, gain_ref, rows_out, active, grads, part, side, *refs = refs
        held_up, held_down, sems_up, sems_down = refs
        started = []
        for t in range(tiles):
            block = slice(t * tile, (t + 1) * tile)
            places = [slice(k * depth, (k + 1) * depth) for k in range(spans)]
            up = copies(
                [w.at[:, block] for w in expand_refs],
                [held_up.at[place, block] for place in places],
                [sems_up.at[t, k] for k in range(spans)],
            )
            down = copies(
                [w.at[block, :] for w in contract_refs],
                [held_down.at[block, place] for place in places],
                [sems_down.at[t, k] for k in range(spans)],
            )
            started.append((up, down))
        start = 0
        for piece_ref in piece_refs:
            size = piece_ref.shape[1]
            rows_out[start : start + size, :] = piece_ref[0]
            start += size
        for t in range(tiles):
            block = slice(t * tile, (t + 1) * tile)
            for copy in started[t][0] + started[t][1]:
                copy.wait()
            pre = plain(second_ref[...], held_up[:, block])
            risen = 0.5 * (1.0 + lax.erf(pre * half_root))
            active[:, block] = (pre * risen).astype(bf16)
            slope = risen + pre * jnp.exp(-0.5 * pre * pre) * bell
            grads[:, block] = (turned(rows_out[...], held_down[block, :]) * slope).astype(bf16)
        for k in range(spans):
            place = slice(k * depth, (k + 1) * depth)
            made = turned(grads[...], held_up[place, :])
            side[0:1, place] = jnp.sum(
                made * normal_ref[:, place].astype(f32), axis=0, keepdims=True
            )
            side[1:2, place] = jnp.sum(made, axis=0, keepdims=True)
            part[:, place] = made * gain_ref[1:2, place]

    ins = [(second, whole(second))]
    ins += [(piece, at((1,) + piece.shape[1:], (at_piece, 0, 0))) for piece in pieces]
    ins += [(w, kept_out) for w in expand] + [(w, kept_out) for w in contract]
    ins += [(normal, whole(normal)), (gains, whole(gains))]
    outs = [
        full_out((rows, width)),
        full_out((rows, hidden)),
        full_out((rows, hidden)),
        full_out((rows, width), f32),
        full_out((2, width), f32),
    ]
    scratch = [
        pltpu.VMEM((width, hidden), bf16),
        pltpu.VMEM((hidden, width), bf16),
        pltpu.SemaphoreType.DMA((tiles, spans)),
        pltpu.SemaphoreType.DMA((tiles, spans)),
    ]
    return run(order, flags, kernel, ins, outs, scratch, "hidden_both")


def branch_out(order, flags, groups, contract, packed, lanes):
    hidden, depth = contract[0].shape
    spans = len(contract)
    across = depth
    width = depth * spans
    span_rows = groups[0][0].shape[0]
    block = span_rows // lanes
    count = len(groups)

    def kernel(flag_ref, *refs):
        group_refs, refs = refs[: 2 * count], refs[2 * count :]
        contract_refs, packed_refs = refs[:spans], refs[spans : 2 * spans]
        blocks, refs = refs[2 * spans : 2 * spans + count * lanes], refs[2 * spans + count * lanes :]
        held, held_out, sems = refs
        outputs = [w.at[:across, 3 * across : 3 * across + depth] for w in packed_refs]
        started = copies(
            [ref for k in range(spans) for ref in (outputs[k], contract_refs[k])],
            [ref for k in range(spans) for ref in (held_out.at[k], held.at[k])],
            [sems.at[j] for j in range(2 * spans)],
        )
        for k in range(spans):
            started[2 * k].wait()
            started[2 * k + 1].wait()
            columns = slice(k * depth, (k + 1) * depth)
            for c in range(count):
                made = plain(group_refs[2 * c + 1][...], held_out[k])
                made = made + plain(group_refs[2 * c][...], held[k])
                for j in range(lanes):
                    rows = made[j * block : (j + 1) * block]
                    blocks[c * lanes + j][:, columns] = rows.astype(bf16)

    ins = []
    for active, attended in groups:
        place = attended.shape[1] // across - 1
        ins += [
            (active, at((span_rows, hidden), (0, 0))),
            (attended, at((span_rows, across), (0, place))),
        ]
    ins += [(w, kept_out) for w in contract] + [(w, kept_out) for w in packed]
    outs = [full_out((block, width))] * (count * lanes)
    scratch = [
        pltpu.VMEM((spans, hidden, depth), bf16),
        pltpu.VMEM((spans, across, depth), bf16),
        pltpu.SemaphoreType.DMA((2 * spans,)),
    ]
    return run(order, flags, kernel, ins, outs, scratch, "branch")


def attend_back(order, flags, pieces, packed, queries, pairs, probs, tables, scale):
    rows = sum(piece.shape[1] for piece in pieces)
    width = pieces[0].shape[2]
    heads, _, head_dim = queries.shape
    spans = len(packed)
    across, depth = heads * head_dim, width // spans
    half = spans // 2

    def kernel(flag_ref, *refs):
        piece_refs, refs = refs[: len(pieces)], refs[len(pieces) :]
        packed_refs, refs = refs[:spans], refs[spans:]
        query_ref, refs = refs[0], refs[1:]
        views, refs = spread(refs[: len(pairs)]), refs[len(pairs) :]
        prob_ref, table_ref, rows_out, turned_back, keep, send, *refs = refs
        columns_out, (held, sems) = refs[:spans], refs[spans:]
        started = copies(
            [w.at[:across, 3 * across : 3 * across + depth] for w in packed_refs],
            [held.at[:, k * depth : (k + 1) * depth] for k in range(spans)],
            [sems.at[k] for k in range(spans)],
        )
        start = 0
        for piece_ref in piece_refs:
            size = piece_ref.shape[1]
            rows_out[start : start + size, :] = piece_ref[0]
            start += size
        for k in range(spans):
            columns_out[k][...] = rows_out[:, k * depth : (k + 1) * depth]
        for copy in started:
            copy.wait()
        grads = turned(rows_out[...], held[...]).astype(bf16)
        for h in range(heads):
            made = attention_grads(
                grads[:, h * head_dim : (h + 1) * head_dim],
                query_ref[h],
                [prob_ref[k, h] for k in range(spans)],
                views,
                h,
                keep,
                send,
                scale,
            )
            turned_back[h] = turn(made, table_ref, -1).astype(bf16)

    ins = [(piece, whole(piece)) for piece in pieces] + [(w, kept_out) for w in packed]
    ins += [(array, whole(array)) for array in (queries, *pairs, probs, tables)]
    outs = [full_out((rows, width)), full_out((heads, rows, head_dim))]
    outs += [full_out((half, 2, heads, rows, head_dim))] * 2
    outs += [full_out((rows, depth))] * spans
    scratch = [pltpu.VMEM((across, width), bf16), pltpu.SemaphoreType.DMA((spans,))]
    return run(order, flags, kernel, ins, outs, scratch, "attend_back")


def hidden_back(order, flags, upstream, contract, expand, slope, normal, gains):
    span_rows, width = upstream.shape
    hidden, depth = contract[0].shape
    spans = len(contract)
    tile = min(512, hidden)
    tiles = hidden // tile

    def kernel(flag_ref, *refs):
        upstream_ref, refs = refs[0], refs[1:]
        contract_refs, refs = refs[:spans], refs[spans:]
        expand_refs, refs = refs[:spans], refs[spans:]
        slope_ref, normal_ref, gain_ref, grads, part, side, held, held_up, sems, sems_up = refs
        started = [
            copies(
                [w.at[t * tile : (t + 1) * tile, :] for w in contract_refs],
                [held.at[t, :, k * depth : (k + 1) * depth] for k in range(spans)],
                [sems.at[t, k] for k in range(spans)],
            )
            for t in range(tiles)
        ]
        started_up = copies(
            expand_refs, [held_up.at[k] for k in range(spans)], [sems_up.at[k] for k in range(spans)]
        )
        for t in range(tiles):
            for copy in started[t]:
                copy.wait()
            columns = slice(t * tile, (t + 1) * tile)
            grads[:, columns] = (
                turned(upstream_ref[...], held[t]) * slope_ref[:, columns].astype(f32)
            ).astype(bf16)
        for k in range(spans):
            started_up[k].wait()
            made = turned(grads[...], held_up[k])
            columns = slice(k * depth, (k + 1) * depth)
            side[0:1, columns] = jnp.sum(
                made * normal_ref[:, columns].astype(f32), axis=0, keepdims=True
            )
            side[1:2, columns] = jnp.sum(made, axis=0, keepdims=True)
            part[:, columns] = made * gain_ref[1:2, columns]

    ins = [(upstream, whole(upstream))]
    ins += [(w, kept_out) for w in contract] + [(w, kept_out) for w in expand]
    ins += [
        (slope, whole(slope)),
        (normal, whole(normal)),
        (gains, whole(gains)),
    ]
    outs = [
        full_out((span_rows, hidden)),
        full_out((span_rows, width), f32),
        full_out((2, width), f32),
    ]
    scratch = [
        pltpu.VMEM((tiles, tile, width), bf16),
        pltpu.VMEM((spans, depth, hidden), bf16),
        pltpu.SemaphoreType.DMA((tiles, spans)),
        pltpu.SemaphoreType.DMA((spans,)),
    ]
    return run(order, flags, kernel, ins, outs, scratch, "hidden_back")


def project_back(
    order, flags, turned_back, own, came, weights, part, normal, gains, tables, lanes
):
    heads, span_rows, head_dim = turned_back.shape
    spans = len(weights)
    width = part.shape[1]
    depth, columns = width // spans, 3 * heads * head_dim
    block = span_rows // lanes

    def kernel(flag_ref, *refs):
        query_ref, own_ref, came_ref, refs = refs[0], refs[1], refs[2], refs[3:]
        weight_refs, refs = refs[:spans], refs[spans:]
        part_ref, normal_ref, gain_ref, table_ref, grads, side, *refs = refs
        blocks, (held, sems) = refs[:lanes], refs[lanes:]
        started = copies(
            [w.at[:depth, :columns] for w in weight_refs],
            [held.at[k] for k in range(spans)],
            [sems.at[k] for k in range(spans)],
        )
        for h in range(heads):
            at_column = h * 3 * head_dim
            keys = own_ref[0, h].astype(f32) + came_ref[0, h].astype(f32)
            values = own_ref[1, h].astype(f32) + came_ref[1, h].astype(f32)
            grads[:, at_column : at_column + head_dim] = query_ref[h]
            grads[:, at_column + head_dim : at_column + 2 * head_dim] = turn(
                keys, table_ref, -1
            ).astype(bf16)
            grads[:, at_column + 2 * head_dim : at_column + 3 * head_dim] = values.astype(bf16)
        for k in range(spans):
            started[k].wait()
            made = turned(grads[...], held[k])
            span_columns = slice(k * depth, (k + 1) * depth)
            side[0:1, span_columns] = jnp.sum(
                made * normal_ref[:, span_columns].astype(f32), axis=0, keepdims=True
            )
            side[1:2, span_columns] = jnp.sum(made, axis=0, keepdims=True)
            both = (made * gain_ref[0:1, span_columns] + part_ref[:, span_columns]).astype(bf16)
            for j in range(lanes):
                blocks[j][:, span_columns] = both[j * block : (j + 1) * block]

    ins = [(array, whole(array)) for array in (turned_back, own, came)]
    ins += [(w, kept_out) for w in weights]
    ins += [(part, whole(part)), (normal, whole(normal))]
    ins += [(gains, whole(gains)), (tables, whole(tables))]
    outs = [full_out((span_rows, columns)), full_out((2, width), f32)]
    outs += [full_out((block, width))] * lanes
    scratch = [pltpu.VMEM((spans, depth, columns), bf16), pltpu.SemaphoreType.DMA((spans,))]
    return run(order, flags, kernel, ins, outs, scratch, "project_back")


def weight_sums(order, flags, lefts, rights, by_rows, spans):
    rows = sum(piece.shape[0] for piece in lefts[1][0])
    left_width = sum(group[0].shape[1] for group in lefts[1])
    right_width = sum(group[0].shape[1] for group in rights[1])
    if by_rows:
        tile = left_width // spans
        steps, block = spans // 2, (tile, right_width)
    else:
        tile = min(512, left_width)
        while left_width % tile:
            tile //= 2
        steps, block = left_width // tile, (tile, right_width // 2)
    chunk = min(1024, block[1])
    while right_width % chunk:
        chunk //= 2
    pieces = [
        [piece for groups in (lefts[s], rights[s]) for group in groups for piece in group]
        for s in (0, 1)
    ]
    most = max(len(p) for p in pieces)

    def kernel(flag_ref, *refs):
        piece_refs = (refs[: len(pieces[0])], refs[len(pieces[0]) : len(pieces[0]) + len(pieces[1])])
        keep, send, left, right, flipped, sems = refs[len(pieces[0]) + len(pieces[1]) :]
        g = pl.program_id(0)
        for s in (0, 1):

            @pl.when((g == 0) & (flag_ref[2] == s))
            def _(s=s):
                targets = []
                for held, groups in ((left, lefts[s]), (right, rights[s])):
                    column = 0
                    for group in groups:
                        row, wide = 0, group[0].shape[1]
                        for piece in group:
                            targets.append(
                                held.at[row : row + piece.shape[0], column : column + wide]
                            )
                            row += piece.shape[0]
                        column += wide
                started = copies(
                    piece_refs[s], targets, [sems.at[j] for j in range(len(targets))]
                )
                for copy in started:
                    copy.wait()

        def product(column, store):
            flipped[...] = left[:, pl.ds(pl.multiple_of(column, LANES), tile)].T

            def one(c, _):
                columns = pl.ds(pl.multiple_of(c * chunk, chunk), chunk)
                store(c, plain(flipped[...], right[:, columns]).astype(bf16))
                return 0

            lax.fori_loop(0, right_width // chunk, one, 0)

        if by_rows:

            def to(target):
                def store(c, made):
                    target[:, pl.ds(pl.multiple_of(c * chunk, chunk), chunk)] = made

                return store

            product(g * tile, to(keep))
            product((g + steps) * tile, to(send))
        else:
            half = right_width // 2 // chunk

            def store(c, made):
                @pl.when(c < half)
                def _():
                    keep[:, pl.ds(pl.multiple_of(c * chunk, chunk), chunk)] = made

                @pl.when(c >= half)
                def _():
                    send[:, pl.ds(pl.multiple_of((c - half) * chunk, chunk), chunk)] = made

            product(g * tile, store)

    ins = [(piece, kept_out) for s in (0, 1) for piece in pieces[s]]
    dims = (steps * tile, block[1])
    outs = [(shape(dims), pl.BlockSpec(block, lambda g: (g, 0)))] * 2
    scratch = [
        pltpu.VMEM((rows, left_width), bf16),
        pltpu.VMEM((rows, right_width), bf16),
        pltpu.VMEM((tile, rows), bf16),
        pltpu.SemaphoreType.DMA((most,)),
    ]
    return run(
        order, flags, kernel, ins, outs, scratch, "weight_sums", grid=(steps,)
    )


def owner_sums(order, flags, lefts, rights):
    left_width, right_width = lefts[0][0].shape[1], rights[0][0].shape[1]
    rows = sum(piece.shape[0] for piece in lefts[0])
    count = len(lefts)
    tile = min(512, left_width)
    while left_width % tile:
        tile //= 2
    pieces = [lefts[m] + rights[m] for m in range(count)]
    most = max(len(p) for p in pieces)

    def kernel(flag_ref, *refs):
        piece_refs, refs = refs[: sum(map(len, pieces))], refs[sum(map(len, pieces)) :]
        out, left, right, flipped, sems = refs
        started, used = [], 0
        for m in range(count):
            targets = []
            for held, group in ((left, lefts[m]), (right, rights[m])):
                row = 0
                for piece in group:
                    targets.append(held.at[m, row : row + piece.shape[0]])
                    row += piece.shape[0]
            started.append(
                copies(
                    piece_refs[used : used + len(targets)],
                    targets,
                    [sems.at[m, j] for j in range(len(targets))],
                )
            )
            used += len(targets)
        for m in range(count):
            for copy in started[m]:
                copy.wait()

            def one(t, _, m=m):
                block = pl.ds(pl.multiple_of(t * tile, tile), tile)
                flipped[...] = left[m, :, block].T
                made = plain(flipped[...], right[m])
                out[block, :] = made if m == 0 else out[block, :] + made
                return 0

            lax.fori_loop(0, left_width // tile, one, 0)

    ins = [(piece, kept_out) for group in pieces for piece in group]
    outs = [full_out((left_width, right_width), f32)]
    scratch = [
        pltpu.VMEM((count, rows, left_width), bf16),
        pltpu.VMEM((count, rows, right_width), bf16),
        pltpu.VMEM((tile, rows), bf16),
        pltpu.SemaphoreType.DMA((count, most)),
    ]
    return run(order, flags, kernel, ins, outs, scratch, "owner_sums")[0]


def fold(order, flags, keep, came, dim):
    rows, columns = keep.shape
    if dim == 0:
        tile = rows // 4
        steps, block = rows // 2 // tile, (tile, columns)
        places = [lambda g: (g, 0), lambda g: (g + steps, 0)]
        half = (rows // 2, columns)
    else:
        tile = rows // 4
        steps, block = rows // tile, (tile, columns // 2)
        places = [lambda g: (g, 0), lambda g: (g, 1)]
        half = (rows, columns // 2)

    def kernel(flag_ref, keep_low, keep_high, came_low, came_high, low, high):
        low[...] = (keep_low[...].astype(f32) + came_low[...].astype(f32)).astype(bf16)
        high[...] = (keep_high[...].astype(f32) + came_high[...].astype(f32)).astype(bf16)

    ins = [(array, pl.BlockSpec(block, place)) for array in (keep, came) for place in places]
    outs = [(shape(half), pl.BlockSpec(block, lambda g: (g, 0)))] * 2
    return run(order, flags, kernel, ins, outs, [], "fold", grid=(steps,))


def shards(
    block_input,
    out_grad,
    triple_weight,
    output_weight,
    expand_weight,
    contract_weight,
    norm_gains,
    norm_biases,
):
    section = lax.axis_index("pipe")
    span = lax.axis_index("ctx")
    lane = lax.axis_index("tp")
    spans = lax.axis_size("ctx")
    lanes = lax.axis_size("tp")
    micros, rows, width = block_input.shape
    span_rows = rows * lanes
    heads = triple_weight.shape[2]
    head_dim = triple_weight.shape[4]
    across_units = heads * head_dim
    scale = head_dim ** (-0.5)
    first_section = section == 0
    both = (0, 1)

    def hop(array, axis, step, sections):
        size = lax.axis_size(axis)
        pairs = [(s * size + a, s * size + (a ^ step)) for s in sections for a in range(size)]
        return lax.ppermute(array, ("pipe", axis), pairs)

    order = Order()

    def flags_for(wanted):
        return jnp.stack([jnp.asarray(wanted), span, section]).astype(jnp.int32)

    flags = [flags_for(section == s) for s in both]
    always = flags_for(1)

    kept = [[SimpleNamespace() for _ in range(micros)] for _ in both]
    due = {}
    slot_index = [0]

    def slot(hops, kernels=()):
        now = slot_index[0]
        slot_index[0] += 1
        ready = due.pop(now, [])
        hops = [h if len(h) == 3 else h + (1,) for h in hops]
        if hops:
            gated = fence([operand for operand, _, _ in hops], order.last + ready)
            order.last = [min(gated, key=lambda array: array.size)]
            for passed, (_, go, slots) in zip(gated, hops):
                results = go(passed)
                results = results if isinstance(results, list) else [results]
                due.setdefault(now + slots, []).extend(results)
        else:
            order.last = order.last + ready
        for kernel in kernels:
            kernel()

    def halved(keep, came, dim):
        middle = keep.shape[dim] // 2
        total = keep.astype(f32) + came.astype(f32)
        return (
            lax.slice_in_dim(total, 0, middle, axis=dim).astype(bf16),
            lax.slice_in_dim(total, middle, 2 * middle, axis=dim).astype(bf16),
        )

    def spread_hops(pieces, axis, axis_name, sections, first):
        step = lax.axis_size(axis_name) // 4
        going = first
        while step:
            pieces.append(hop(going, axis_name, step, sections))
            going = jnp.concatenate(pieces, axis=axis)
            step //= 2
        return pieces[-1]

    def fold_hops(k, first, axis_name, dim, sections):
        step, size = 1, lax.axis_size(axis_name)
        while 2 * step < size:
            came = hop(first, axis_name, step, sections)
            k.keep, k.send = halved(k.keep, came, dim)
            first = k.send
            step *= 2
        return came

    depth = width // spans
    far = spans // 2
    assert depth == across_units
    small = jnp.concatenate([norm_gains[0], norm_biases[0]], axis=0)
    packed = jnp.concatenate(
        [triple_weight[0].reshape(depth, -1), output_weight[0].reshape(-1, depth)],
        axis=1,
    )
    packed = jnp.pad(packed, ((0, 16), (0, 0)))
    packed = lax.dynamic_update_slice(packed, small, (depth, 0))
    own_expand, own_contract = expand_weight[0], contract_weight[0]
    hidden = own_expand.shape[1]
    inputs = xor_blocks(block_input, span, spans)
    cotangent = xor_blocks(out_grad, span, spans)
    early = jnp.where(first_section, inputs, cotangent)

    in_row = jnp.arange(rows, dtype=jnp.int32)
    in_span = jnp.concatenate([(lane ^ j) * rows + in_row for j in doubling(lanes)])
    positions = span * span_rows + in_span
    key_positions = jnp.stack([(span ^ k) * span_rows + in_span for k in doubling(spans)])
    tables = rope_tables(positions)
    position_column = positions[:, None]
    key_positions = key_positions[:, None, :]

    def blocks_of(own, came):
        held, step = {0: own, far: came}, far // 2
        while step:
            for k in list(held):
                held[k ^ step] = hop(held[k], "ctx", step, both)
            step //= 2
        return [held[k] for k in doubling(spans)]

    lane_offsets = doubling(lanes)

    def across(array, j, source):
        pairs = [(source * lanes + a, (1 - source) * lanes + (a ^ j)) for a in range(lanes)]
        return lax.ppermute(array, ("pipe", "tp"), pairs)

    def rows_far(s, m):
        k = kept[s][m]

        def go(passed):
            k.rows = passed
            k.pieces = [passed, hop(passed, "tp", lanes // 2, (s,))]
            return k.pieces[1]

        return k.rows, go

    def rows_near(s, m):
        k = kept[s][m]

        def go(passed):
            last_piece = spread_hops(k.pieces, 0, "tp", (s,), passed)
            k.row_pieces = [piece[None] for piece in k.pieces]
            return last_piece

        return jnp.concatenate(k.pieces, axis=0), go

    def pair_far(s, m):
        k = kept[s][m]

        def go(passed):
            k.pairs = [passed, hop(passed, "ctx", far, (s,))]
            return k.pairs[1]

        return k.pair, go

    def pair_near(s, m):
        k = kept[s][m]

        def go(passed):
            return spread_hops(k.pairs, 0, "ctx", (s,), passed)

        return jnp.concatenate(k.pairs, axis=0), go

    def pair_grad_near(s, m):
        k = kept[s][m].pair_grad
        return k.send, lambda passed: fold_hops(k, passed, "ctx", 0, (s,))

    def pair_grad_far(s, m):
        k = kept[s][m].pair_grad

        def go(passed):
            k.came = hop(passed, "ctx", far, (s,))
            return k.came

        return k.send, go

    def sum_hops(s, m):
        blocks = kept[s][m].blocks
        arrived = kept[s][m].arrived = []

        def one(j):
            def go(passed):
                arrived.append(hop(passed, "tp", lane_offsets[j], (s,)))
                return arrived[-1]

            return blocks[j], go

        return [one(j) for j in range(1, lanes)]

    def sum_near(s, k):
        k.keep = jnp.concatenate(k.blocks[: lanes // 2], axis=0)
        going = jnp.concatenate(k.blocks[lanes // 2 :], axis=0)
        return going, lambda passed: fold_hops(k, passed, "tp", 0, (s,))

    def sum_far(s, k):
        def go(passed):
            k.blocks, k.arrived = [k.keep], [hop(passed, "tp", lanes // 2, (s,))]
            return k.arrived[0]

        return k.send, go

    def units_far(m):
        k = kept[0][m]

        def go(passed):
            k.all_units = [passed, hop(passed, "ctx", far, (0,))]
            return k.all_units[1]

        return k.units, go

    def units_near(m):
        k = kept[0][m]

        def go(passed):
            return spread_hops(k.all_units, 0, "ctx", (0,), passed)

        return jnp.concatenate(k.all_units, axis=0), go

    def column_hops(m):
        k = kept[0][m]
        k.own_columns = [k.columns[0]]

        def one(j):
            def go(passed):
                k.own_columns.append(hop(passed, "ctx", doubling(spans)[j], (0,)))
                return k.own_columns[-1]

            return k.columns[j], go

        return [one(j) for j in range(1, spans)]

    def total_of(k):
        return sum(array.astype(f32) for array in [k.blocks[0], *k.arrived])

    def norm_back(upstream, combined, entering):
        normalized, inverse = normalize(entering.astype(f32))
        return (
            upstream.astype(f32)
            + inverse
            * (
                combined
                - jnp.mean(combined, axis=-1, keepdims=True)
                - normalized * jnp.mean(combined * normalized, axis=-1, keepdims=True)
            )
        ).astype(bf16)

    def middle_of(m):
        return (inputs[m].astype(f32) + total_of(kept[0][m])).astype(bf16)

    def entry_of(m):
        k = kept[1][m]
        return norm_back(cotangent[m], total_of(k), k.rows)

    def hand(s, m):
        k, other = kept[s][m], kept[1 - s][m]
        k.given = middle_of(m) if s == 0 else entry_of(m)

        def go(passed):
            k.given = passed
            pieces = [across(passed, j, s) for j in lane_offsets]
            other.rows = pieces[0]
            other.row_pieces = [piece[None] for piece in pieces]
            return pieces

        return k.given, go

    def hand_one(s, m):
        k, other = kept[s][m], kept[1 - s][m]
        k.given = middle_of(m) if s == 0 else entry_of(m)

        def go(passed):
            k.given = passed
            other.rows = across(passed, 0, s)
            return other.rows

        return k.given, go

    def run_project(s, m):
        k = kept[s][m]
        pieces, place = (early_pieces, m) if s == 0 else (k.row_pieces, 0)
        k.first, k.second, k.normal, k.queries, pair = project(
            order, flags[s], pieces, place, gains, biases, tables, packed, heads, head_dim
        )
        k.pair = pair[None]

    def run_expand(m):
        k = kept[0][m]
        k.units, k.slope = expand_up(
            order, flags[0], k.second, expand, span_rows, across_units
        )

    def run_attend(m):
        k = kept[0][m]
        k.units, k.probs = attend(
            order,
            flags[0],
            k.units,
            k.queries,
            k.pairs,
            position_column,
            key_positions,
            scale,
        )

    def run_branch(m):
        k = kept[0][m]
        k.blocks = branch_out(
            order, flags[0], [(k.units, k.units)], contract, packed, lanes
        )

    def run_hidden_both(m):
        k = kept[1][m]
        k.upstream, k.active, k.hidden, k.part, k.side_second = hidden_both(
            order, flags[1], k.second, early_pieces, m, expand, contract, k.normal, gains
        )

    def run_attend_both(m):
        k = kept[1][m]
        k.attended, k.turned_back, keep, send = attend_both(
            order,
            flags[1],
            k.upstream,
            packed,
            k.queries,
            k.pairs,
            position_column,
            key_positions,
            tables,
            scale,
        )
        k.pair_grad = SimpleNamespace(keep=keep, send=send)

    def run_attend_back(m):
        k = kept[0][m]
        k.upstream, k.turned_back, keep, send, *k.columns = attend_back(
            order,
            flags[0],
            k.row_pieces,
            packed,
            k.queries,
            k.pairs,
            k.probs,
            tables,
            scale,
        )
        k.pair_grad = SimpleNamespace(keep=keep, send=send)

    def run_hidden_back(m):
        k = kept[0][m]
        k.hidden, k.part, k.side_second = hidden_back(
            order,
            flags[0],
            k.upstream,
            contract,
            expand,
            k.slope,
            k.normal,
            gains,
        )

    def run_project_back(s, m):
        k = kept[s][m]
        own, arrived = k.pair_grad.keep, k.pair_grad.came
        k.stacked, k.side_first, *k.blocks = project_back(
            order,
            flags[s],
            k.turned_back,
            own.reshape(own.shape[1:]),
            arrived.reshape(arrived.shape[1:]),
            packed,
            k.part,
            k.normal,
            gains,
            tables,
            lanes,
        )

    def of(name, s, count=micros):
        return [getattr(kept[s][m], name) for m in range(count)]

    branch_sums, expand_sums, triple_sums = (
        SimpleNamespace(parts=[], flags=f, sections=secs)
        for f, secs in ((flags[1], (1,)), (always, both), (always, both))
    )

    def run_sums(w, lefts, rights, by_rows):
        w.dim = 0 if by_rows else 1
        w.keep, w.send = weight_sums(order, w.flags, lefts, rights, by_rows, spans)

    def wide_near(w):
        def go(passed):
            w.came = hop(passed, "ctx", 1, w.sections)
            return w.came

        return w.send, go

    def run_fold(w):
        step = 2
        w.keep, w.send = fold(order, w.flags, w.keep, w.came, w.dim)
        while 2 * step < spans:
            w.came = hop(w.send, "ctx", step, w.sections)
            w.keep, w.send = fold(order, w.flags, w.keep, w.came, w.dim)
            step *= 2

    def wide_far(w, start, stop):
        def go(passed):
            w.parts.append(hop(passed, "ctx", far, w.sections))
            return w.parts[-1]

        return w.send[start:stop], go

    weights = SimpleNamespace(expand_came=[], contract_came=[])
    half_depth = depth // 2

    def expand_far(start, stop):
        def go(passed):
            weights.expand_came.append(hop(passed, "ctx", far, both))
            return weights.expand_came[-1]

        return own_expand[start:stop], go

    def packed_far(passed):
        weights.packed_came = hop(passed, "ctx", far, both)
        return weights.packed_came

    def packed_near(passed):
        weights.packed = blocks_of(packed, passed)
        return weights.packed[1:]

    def expand_near(passed):
        weights.expand = blocks_of(own_expand, passed)
        return weights.expand[1:]

    def contract_far(start, stop):
        def go(passed):
            weights.contract_came.append(hop(passed, "ctx", far, both))
            return weights.contract_came[-1]

        return own_contract[start:stop], go

    def contract_near(passed):
        weights.contract = blocks_of(own_contract, passed)
        return weights.contract[1:]

    def early_hops(passed):
        weights.early = [passed] + [hop(passed, "tp", j, both) for j in lane_offsets[1:]]
        return weights.early[1:]

    due[0] = [expand_far(0, half_depth)[1](own_expand[:half_depth])]
    slot([(packed, packed_far), expand_far(half_depth, depth), (early, early_hops)])
    early_pieces = weights.early
    slot(
        [
            (weights.packed_came, packed_near),
            (jnp.concatenate(weights.expand_came, axis=0), expand_near, 2),
        ]
    )
    packed, expand = weights.packed, weights.expand
    small_full = jnp.concatenate(
        [piece[depth : depth + 4, :depth] for piece in packed], axis=1
    ).astype(f32)
    gains, biases = small_full[:2], small_full[2:]
    slot(
        [contract_far(0, hidden // 2)],
        [lambda m=m: run_project(0, m) for m in range(micros)],
    )
    slot(
        [pair_far(0, 0), contract_far(hidden // 2, hidden)],
        [lambda m=m: run_expand(m) for m in range(micros)],
    )
    contract_came = jnp.concatenate(weights.contract_came, axis=0)
    slot([(contract_came, contract_near), pair_near(0, 0), pair_far(0, 1)])
    contract = weights.contract
    a, b = kept
    slot([pair_near(0, 1)], [lambda: run_attend(0), lambda: run_branch(0)])
    slot(sum_hops(0, 0) + [pair_far(0, 2)], [lambda: run_attend(1), lambda: run_branch(1)])
    slot([hand(0, 0)] + sum_hops(0, 1))
    slot([hand(0, 1), pair_near(0, 2)], [lambda: run_project(1, 0)])
    slot(
        [pair_far(1, 0)],
        [
            lambda: run_hidden_both(0),
            lambda: run_project(1, 1),
            lambda: run_attend(2),
            lambda: run_branch(2),
        ],
    )
    slot([pair_near(1, 0), pair_far(1, 1), sum_near(0, a[2])])
    slot(
        [pair_near(1, 1), sum_far(0, a[2]), units_far(0)],
        [lambda: run_attend_both(0), lambda: run_hidden_both(1)],
    )
    slot([pair_grad_near(1, 0), hand_one(0, 2)], [lambda: run_attend_both(1)])
    slot([pair_grad_far(1, 0), rows_far(1, 2), pair_grad_near(1, 1), units_near(0)])
    slot(
        [rows_near(1, 2), pair_grad_far(1, 1), units_far(1)], [lambda: run_project_back(1, 0)]
    )
    slot(
        [sum_near(1, b[0]), units_near(1)],
        [lambda: run_project(1, 2), lambda: run_project_back(1, 1)],
    )
    slot(
        [pair_far(1, 2), sum_far(1, b[0]), sum_near(1, b[1]), units_far(2)],
        [lambda: run_hidden_both(2)],
    )
    slot([pair_near(1, 2), hand_one(1, 0), sum_far(1, b[1]), units_near(2)])
    slot([hand_one(1, 1), rows_far(0, 0)], [lambda: run_attend_both(2)])
    slot([pair_grad_near(1, 2), rows_near(0, 0), rows_far(0, 1)])
    slot([pair_grad_far(1, 2), rows_near(0, 1)], [lambda: run_attend_back(0)])
    slot(
        [pair_grad_near(0, 0)] + column_hops(0),
        [lambda: run_project_back(1, 2), lambda: run_hidden_back(0)],
    )

    def run_branch_sums():
        run_sums(
            branch_sums,
            [[], [of("active", 1), of("attended", 1)]],
            [[], [of("upstream", 1)]],
            False,
        )

    slot(
        sum_hops(1, 2) + [pair_grad_far(0, 0)],
        [lambda: run_attend_back(1), run_branch_sums],
    )
    slot(
        [hand(1, 2), pair_grad_near(0, 1)],
        [lambda: run_hidden_back(1), lambda: run_project_back(0, 0)],
    )
    finals = [SimpleNamespace() for _ in range(micros)]

    def run_final_branch():
        blocks = branch_out(
            order,
            flags[1],
            [(k.active, k.attended) for k in kept[1]],
            contract,
            packed,
            lanes,
        )
        for m in range(micros):
            finals[m].blocks = blocks[m * lanes : (m + 1) * lanes]

    def run_expand_sums():
        run_sums(
            expand_sums,
            [[of("second", s)] for s in both],
            [[of("hidden", s)] for s in both],
            True,
        )

    def run_triple_sums():
        run_sums(
            triple_sums,
            [[of("first", s)] for s in both],
            [[of("stacked", s)] for s in both],
            True,
        )

    def run_owner_sums():
        branch_sums.whole = owner_sums(
            order, flags[0], of("all_units", 0), of("own_columns", 0)
        )

    half_hidden = hidden // 2
    slot(
        [pair_grad_far(0, 1), wide_near(branch_sums)] + column_hops(1),
        [lambda: run_attend_back(2)],
    )
    slot(
        [pair_grad_near(0, 2), sum_near(0, a[0])] + column_hops(2),
        [
            lambda: run_hidden_back(2),
            lambda: run_project_back(0, 1),
            lambda: run_fold(branch_sums),
        ],
    )
    slot(
        [pair_grad_far(0, 2), sum_far(0, a[0]), wide_far(branch_sums, 0, half_hidden)],
        [run_expand_sums],
    )
    slot(
        [wide_near(expand_sums), wide_far(branch_sums, half_hidden, hidden)],
        [lambda: run_project_back(0, 2), run_final_branch],
    )
    slot(
        [
            sum_near(0, a[1]),
            sum_near(0, a[2]),
            wide_far(branch_sums, hidden, hidden + across_units),
            sum_near(1, finals[0]),
            sum_near(1, finals[1]),
        ],
        [lambda: run_fold(expand_sums), run_triple_sums],
    )

    def side_of(mades):
        return sum(
            jnp.concatenate([k.side_first, k.side_second], axis=0) for k in mades
        )

    side = SimpleNamespace(
        all=jnp.where(first_section, side_of(kept[0]), side_of(kept[1]))
    )

    def side_hops(passed):
        step = 1
        while step < spans:
            middle = passed.shape[1] // 2
            came = hop(passed[:, middle:], "ctx", step, both)
            passed = passed[:, :middle] + came
            step *= 2
        step = 1
        while step < lanes:
            came = hop(passed, "tp", step, both)
            passed = passed + came
            step *= 2
        side.all = passed
        return came

    slot(
        [
            wide_far(expand_sums, 0, half_depth),
            wide_near(triple_sums),
            sum_far(0, a[1]),
            sum_far(0, a[2]),
            sum_near(1, finals[2]),
        ],
        [run_owner_sums],
    )
    slot(
        [wide_far(expand_sums, half_depth, depth)]
        + [sum_far(1, finals[m]) for m in range(micros)],
        [lambda: run_fold(triple_sums)],
    )
    slot([wide_far(triple_sums, 0, depth), (side.all, side_hops)])

    def wide_total(keep, parts):
        came = jnp.concatenate(parts, axis=0) if len(parts) > 1 else parts[0]
        return keep.astype(f32) + came.astype(f32)

    contract_grads = jnp.where(
        first_section,
        branch_sums.whole[:hidden],
        wide_total(branch_sums.keep[:hidden], branch_sums.parts[:2]),
    )
    output_grads = jnp.where(
        first_section,
        branch_sums.whole[hidden:],
        wide_total(branch_sums.keep[hidden:], branch_sums.parts[2:]),
    )
    expand_grads = wide_total(expand_sums.keep, expand_sums.parts)
    triple_grads = wide_total(triple_sums.keep, triple_sums.parts)
    layer_outputs = jnp.stack(
        [
            jnp.where(
                first_section,
                kept[0][m].given,
                (kept[1][m].rows.astype(f32) + total_of(finals[m])).astype(bf16),
            )
            for m in range(micros)
        ]
    )
    entry_grads = jnp.stack(
        [
            jnp.where(
                first_section,
                norm_back(kept[0][m].rows, total_of(kept[0][m]), inputs[m]),
                kept[1][m].given,
            )
            for m in range(micros)
        ]
    )
    gain_grads = jnp.stack([side.all[0], side.all[2]])
    bias_grads = jnp.stack([side.all[1], side.all[3]])
    return (
        xor_blocks(layer_outputs, span, spans, inverse=True)[None],
        xor_blocks(entry_grads, span, spans, inverse=True)[None],
        triple_grads.reshape(triple_weight.shape),
        output_grads.reshape(output_weight.shape),
        expand_grads[None],
        contract_grads[None],
        gain_grads[None],
        bias_grads[None],
    )


def solution(mesh):
    return jax.shard_map(
        shards,
        mesh=mesh,
        in_specs=(
            P(None, ("ctx", "tp"), None),
            P(None, ("ctx", "tp"), None),
            P("pipe", "ctx", "tp", None, None),
            P("pipe", "tp", None, "ctx"),
            P("pipe", "ctx", "tp"),
            P("pipe", "tp", "ctx"),
            P("pipe", None, "ctx"),
            P("pipe", None, "ctx"),
        ),
        out_specs=(
            P("pipe", None, ("ctx", "tp"), None),
            P("pipe", None, ("ctx", "tp"), None),
            P("pipe", "ctx", "tp", None, None),
            P("pipe", "tp", None, "ctx"),
            P("pipe", "ctx", "tp"),
            P("pipe", "tp", "ctx"),
            P("pipe", None, "ctx"),
            P("pipe", None, "ctx"),
        ),
        check_vma=False,
    )
```

```python
import functools
from types import SimpleNamespace

import jax
import jax.numpy as jnp
from jax import lax
from jax.experimental import pallas as pl
from jax.experimental.pallas import tpu as pltpu
from jax.sharding import PartitionSpec as P

ROT = 64
LANES = 128
epsilon = 1e-05
masked_score = -1e30
f32 = jnp.float32
bf16 = jnp.bfloat16
vmem_bytes = 56 * 1024 * 1024
half_root = 0.7071067811865476
bell = 0.3989422804014327


def dot(a, b, dims):
    return lax.dot_general(a, b, (dims, ((), ())), preferred_element_type=f32)


def plain(a, b):
    return dot(a, b, ((1,), (0,)))


def turned(a, b):
    return dot(a, b, ((1,), (1,)))


def doubling(count):
    order, step = [0], count // 2
    while step:
        order += [k ^ step for k in order]
        step //= 2
    return order


def xor_blocks(values, index, count, inverse=False):
    width = values.shape[-1] // count
    order = doubling(count)

    def taken(places):
        return jnp.concatenate(
            [values[..., k * width : (k + 1) * width] for k in places], axis=-1
        )

    if inverse:
        values = taken([order.index(k) for k in range(count)])
    step = 1
    while step < count:
        swapped = taken([k ^ step for k in range(count)])
        values = jnp.where((index & step) != 0, swapped, values)
        step *= 2
    return values if inverse else taken(order)


def rope_tables(positions):
    half = ROT // 2
    frequency = 10000.0 ** (-jnp.arange(0, ROT, 2, dtype=f32) / ROT)
    angles = positions.astype(f32)[:, None] * frequency[None, :]
    cosine, sine = jnp.cos(angles), jnp.sin(angles)
    count = positions.shape[0]
    rest = jnp.zeros((count, LANES - ROT), f32)
    none = jnp.zeros((count, half), f32)
    return jnp.stack(
        [
            jnp.concatenate([cosine, cosine, rest + 1.0], axis=1),
            jnp.concatenate([-sine, none, rest], axis=1),
            jnp.concatenate([none, sine, rest], axis=1),
        ]
    )


def turn(values, tables, sign):
    half = ROT // 2
    part = values[:, :LANES]
    moved = (
        pltpu.roll(part, LANES - half, 1) * tables[1] + pltpu.roll(part, half, 1) * tables[2]
    )
    part = part * tables[0] + (moved if sign > 0 else -moved)
    return jnp.concatenate([part, values[:, LANES:]], axis=1)


def normalize(values):
    center = values - jnp.mean(values, axis=-1, keepdims=True)
    inverse = lax.rsqrt(jnp.mean(center * center, axis=-1, keepdims=True) + epsilon)
    return (center * inverse, inverse)


def whole(array):
    zeros = (0,) * array.ndim
    return pl.BlockSpec(array.shape, lambda *_: zeros)


def at(block, place):
    return pl.BlockSpec(block, lambda *_: place)


kept_out = pl.BlockSpec(memory_space=pl.ANY)


def shape(dims, dtype=bf16):
    return jax.ShapeDtypeStruct(dims, dtype)


class Order:
    def __init__(self):
        self.last = []

    def follow(self, results):
        self.last = [min(results, key=lambda array: array.size * array.dtype.itemsize)]

    def also(self, array):
        self.last = self.last + [array]


took = dict(
    project=7,
    expand=8,
    attend=5,
    branch=8,
    hidden_both=14,
    attend_both=11,
    attend_back=8,
    hidden_back=13,
    project_back=8,
    weight_sums=16,
    fold=7,
)
peak = 1.15e9


def run(order, flags, kernel, ins, outs, scratch, name, grid=(1,)):
    taken = len(ins)
    ins = [(flags, pl.BlockSpec(memory_space=pltpu.SMEM))] + list(ins)
    ins += [(array, kept_out) for array in order.last]
    arrays = [array for array, _ in ins]

    def body(flag_ref, *refs):
        @pl.when(flag_ref[0] == 1)
        def _():
            kernel(flag_ref, *refs[:taken], *refs[len(ins) - 1 :])

    results = pl.pallas_call(
        body,
        grid=grid,
        in_specs=[spec for _, spec in ins],
        out_specs=[spec for _, spec in outs],
        out_shape=[struct for struct, _ in outs],
        scratch_shapes=scratch,
        compiler_params=pltpu.CompilerParams(vmem_limit_bytes=vmem_bytes),
        cost_estimate=pl.CostEstimate(
            flops=int(took[name] * peak), bytes_accessed=0, transcendentals=0
        ),
        name=name,
    )(*arrays)
    order.follow(results)
    return results


def fence(through, waits):
    count = len(through)

    def kernel(*refs):
        pass

    return pl.pallas_call(
        kernel,
        in_specs=[kept_out] * (count + len(waits)),
        out_specs=[kept_out] * count,
        out_shape=[shape(array.shape, array.dtype) for array in through],
        input_output_aliases={j: j for j in range(count)},
        compiler_params=pltpu.CompilerParams(vmem_limit_bytes=vmem_bytes),
        cost_estimate=pl.CostEstimate(flops=1, bytes_accessed=1, transcendentals=0),
        name="fence",
    )(*through, *waits)


def full_out(dims, dtype=bf16):
    zeros = (0,) * len(dims)
    return (shape(dims, dtype), pl.BlockSpec(dims, lambda *_: zeros))


def copies(sources, targets, sems):
    started = []
    for source, target, sem in zip(sources, targets, sems):
        copy = pltpu.make_async_copy(source, target, sem)
        copy.start()
        started.append(copy)
    return started


def project(order, flags, pieces, at_piece, gains, biases, tables, weights, heads, head_dim):
    count, width = 1, pieces[0].shape[2]
    span_rows = sum(piece.shape[1] for piece in pieces)
    rows = count * span_rows
    chunk = pieces[0].shape[1]
    spans = len(weights)
    depth = width // spans
    wide = 3 * head_dim
    columns = heads * wide

    def kernel(flag_ref, *refs):
        piece_refs = refs[: len(pieces)]
        gain_ref, bias_ref, table_ref = refs[len(pieces) : len(pieces) + 3]
        weight_refs = refs[len(pieces) + 3 : len(pieces) + 3 + spans]
        first, second, normal, queries, pair, held, sems = refs[len(pieces) + 3 + spans :]
        started = []
        for h in range(heads):
            started.append(
                copies(
                    [w.at[:depth, h * wide : (h + 1) * wide] for w in weight_refs],
                    [held.at[h, k * depth : (k + 1) * depth] for k in range(spans)],
                    [sems.at[h, k] for k in range(spans)],
                )
            )
        start = 0
        for piece_ref in piece_refs:
            chunks = piece_ref.shape[1] // chunk

            def one(i, _, piece_ref=piece_ref, start=start, chunks=chunks):
                m, c = i // chunks, i % chunks
                values = piece_ref[m, pl.ds(pl.multiple_of(c * chunk, chunk), chunk), :]
                normed, _ = normalize(values.astype(f32))
                to = pl.ds(
                    pl.multiple_of(m * span_rows + start + c * chunk, chunk), chunk
                )
                normal[to, :] = normed.astype(bf16)
                first[to, :] = (normed * gain_ref[0:1] + bias_ref[0:1]).astype(bf16)
                second[to, :] = (normed * gain_ref[1:2] + bias_ref[1:2]).astype(bf16)
                return 0

            lax.fori_loop(0, count * chunks, one, 0)
            start += piece_ref.shape[1]
        for h in range(heads):
            for copy in started[h]:
                copy.wait()

            def two(m, _, h=h):
                to = pl.ds(pl.multiple_of(m * span_rows, span_rows), span_rows)
                made = plain(first[to, :], held[h])
                queries[h, to, :] = turn(made[:, :head_dim], table_ref, 1).astype(bf16)
                pair[0, h, to, :] = turn(
                    made[:, head_dim : 2 * head_dim], table_ref, 1
                ).astype(bf16)
                pair[1, h, to, :] = made[:, 2 * head_dim :].astype(bf16)
                return 0

            lax.fori_loop(0, count, two, 0)

    ins = [(piece, at((1,) + piece.shape[1:], (at_piece, 0, 0))) for piece in pieces]
    ins += [(array, whole(array)) for array in (gains, biases, tables)]
    ins += [(w, kept_out) for w in weights]
    outs = [full_out((rows, width))] * 3 + [
        full_out((heads, rows, head_dim)),
        full_out((2, heads, rows, head_dim)),
    ]
    scratch = [
        pltpu.VMEM((heads, width, wide), bf16),
        pltpu.SemaphoreType.DMA((heads, spans)),
    ]
    return run(order, flags, kernel, ins, outs, scratch, "project")


def expand_up(order, flags, second, weights, span_rows):
    rows, width = second.shape
    depth, hidden = weights[0].shape
    spans = len(weights)
    tile = min(512, hidden)
    tiles = hidden // tile

    def kernel(flag_ref, *refs):
        second_ref, weight_refs = refs[0], refs[1 : 1 + spans]
        active, slope, held, sems = refs[1 + spans :]
        started = []
        for t in range(tiles):
            started.append(
                copies(
                    [w.at[:, t * tile : (t + 1) * tile] for w in weight_refs],
                    [held.at[t, k * depth : (k + 1) * depth] for k in range(spans)],
                    [sems.at[t, k] for k in range(spans)],
                )
            )
        for t in range(tiles):
            for copy in started[t]:
                copy.wait()

            def one(m, _, t=t):
                to = pl.ds(pl.multiple_of(m * span_rows, span_rows), span_rows)
                pre = plain(second_ref[to, :], held[t])
                risen = 0.5 * (1.0 + lax.erf(pre * half_root))
                columns = slice(t * tile, (t + 1) * tile)
                active[to, columns] = (pre * risen).astype(bf16)
                slope[to, columns] = (
                    risen + pre * jnp.exp(-0.5 * pre * pre) * bell
                ).astype(bf16)
                return 0

            lax.fori_loop(0, rows // span_rows, one, 0)

    ins = [(second, whole(second))] + [(w, kept_out) for w in weights]
    outs = [full_out((rows, hidden))] * 2
    scratch = [
        pltpu.VMEM((tiles, width, tile), bf16),
        pltpu.SemaphoreType.DMA((tiles, spans)),
    ]
    return run(order, flags, kernel, ins, outs, scratch, "expand")


def spread(refs):
    return [ref.at[j] for ref in refs for j in range(ref.shape[0])]


def attention(here, pairs, head, row_ref, key_ref, scale):
    scores = []
    for k, pair in enumerate(pairs):
        raw = turned(here, pair[0, head]) * scale
        scores.append(jnp.where(key_ref[k] <= row_ref[...], raw, masked_score))
    top = functools.reduce(
        jnp.maximum, [jnp.max(part, axis=1, keepdims=True) for part in scores]
    )
    scores = [jnp.exp(part - top) for part in scores]
    inverse = 1.0 / sum(jnp.sum(part, axis=1, keepdims=True) for part in scores)
    return [part * inverse for part in scores]


def attend(order, flags, queries, pairs, positions, key_positions, scale):
    heads, rows, head_dim = queries.shape
    spans = sum(pair.shape[0] for pair in pairs)

    def kernel(flag_ref, query_ref, *refs):
        views, refs = spread(refs[: len(pairs)]), refs[len(pairs) :]
        row_ref, key_ref, attended, probs = refs
        for h in range(heads):
            parts = attention(query_ref[h], views, h, row_ref, key_ref, scale)
            summed = None
            for k in range(spans):
                part = parts[k].astype(bf16)
                probs[k, h] = part
                term = plain(part, views[k][1, h])
                summed = term if summed is None else summed + term
            attended[:, h * head_dim : (h + 1) * head_dim] = summed.astype(bf16)

    ins = [
        (array, whole(array)) for array in (queries, *pairs, positions, key_positions)
    ]
    outs = [full_out((rows, heads * head_dim)), full_out((spans, heads, rows, rows))]
    return run(order, flags, kernel, ins, outs, [], "attend")


def attention_grads(grad, here, parts, views, head, keep, send, scale):
    half = keep.shape[0]
    grad_probs = [turned(grad, view[1, head]) for view in views]
    delta = sum(
        jnp.sum(part.astype(f32) * slope, axis=1, keepdims=True)
        for part, slope in zip(parts, grad_probs)
    )
    query_grad = None
    for k, view in enumerate(views):
        slopes = (parts[k].astype(f32) * (grad_probs[k] - delta)).astype(bf16)
        term = plain(slopes, view[0, head])
        query_grad = term if query_grad is None else query_grad + term
        side = keep if k < half else send
        side[k % half, 0, head] = (dot(slopes, here, ((0,), (0,))) * scale).astype(bf16)
        side[k % half, 1, head] = dot(parts[k].astype(bf16), grad, ((0,), (0,))).astype(bf16)
    return query_grad * scale


def attend_both(
    order, flags, rows_in, packed, queries, pairs, positions, key_positions, tables, scale
):
    heads, rows, head_dim = queries.shape
    width = rows_in.shape[1]
    spans = len(packed)
    across, depth = heads * head_dim, width // spans
    half = spans // 2

    def kernel(flag_ref, rows_ref, *refs):
        packed_refs, refs = refs[:spans], refs[spans:]
        query_ref, refs = refs[0], refs[1:]
        views, refs = spread(refs[: len(pairs)]), refs[len(pairs) :]
        row_ref, key_ref, table_ref, attended, turned_back, keep, send, held, sems = refs
        started = copies(
            [w.at[:across, 3 * across : 3 * across + depth] for w in packed_refs],
            [held.at[:, k * depth : (k + 1) * depth] for k in range(spans)],
            [sems.at[k] for k in range(spans)],
        )
        all_parts = []
        for h in range(heads):
            parts = attention(query_ref[h], views, h, row_ref, key_ref, scale)
            summed = None
            for k in range(spans):
                term = plain(parts[k].astype(bf16), views[k][1, h])
                summed = term if summed is None else summed + term
            attended[:, h * head_dim : (h + 1) * head_dim] = summed.astype(bf16)
            all_parts.append(parts)
        for copy in started:
            copy.wait()
        grads = turned(rows_ref[...], held[...]).astype(bf16)
        for h in range(heads):
            made = attention_grads(
                grads[:, h * head_dim : (h + 1) * head_dim],
                query_ref[h],
                all_parts[h],
                views,
                h,
                keep,
                send,
                scale,
            )
            turned_back[h] = turn(made, table_ref, -1).astype(bf16)

    ins = [(rows_in, whole(rows_in))] + [(w, kept_out) for w in packed]
    ins += [
        (array, whole(array)) for array in (queries, *pairs, positions, key_positions, tables)
    ]
    outs = [full_out((rows, across)), full_out((heads, rows, head_dim))]
    outs += [full_out((half, 2, heads, rows, head_dim))] * 2
    scratch = [pltpu.VMEM((across, width), bf16), pltpu.SemaphoreType.DMA((spans,))]
    return run(order, flags, kernel, ins, outs, scratch, "attend_both")


def hidden_both(order, flags, second, pieces, at_piece, expand, contract, normal, gains):
    rows, width = second.shape
    hidden, depth = contract[0].shape
    spans = len(contract)
    tile = min(512, hidden)
    tiles = hidden // tile

    def kernel(flag_ref, second_ref, *refs):
        piece_refs, refs = refs[: len(pieces)], refs[len(pieces) :]
        expand_refs, refs = refs[:spans], refs[spans:]
        contract_refs, refs = refs[:spans], refs[spans:]
        normal_ref, gain_ref, rows_out, active, grads, part, side, *refs = refs
        held_up, held_down, sems_up, sems_down = refs
        started = []
        for t in range(tiles):
            block = slice(t * tile, (t + 1) * tile)
            places = [slice(k * depth, (k + 1) * depth) for k in range(spans)]
            up = copies(
                [w.at[:, block] for w in expand_refs],
                [held_up.at[place, block] for place in places],
                [sems_up.at[t, k] for k in range(spans)],
            )
            down = copies(
                [w.at[block, :] for w in contract_refs],
                [held_down.at[block, place] for place in places],
                [sems_down.at[t, k] for k in range(spans)],
            )
            started.append((up, down))
        start = 0
        for piece_ref in piece_refs:
            size = piece_ref.shape[1]
            rows_out[start : start + size, :] = piece_ref[0]
            start += size
        for t in range(tiles):
            block = slice(t * tile, (t + 1) * tile)
            for copy in started[t][0] + started[t][1]:
                copy.wait()
            pre = plain(second_ref[...], held_up[:, block])
            risen = 0.5 * (1.0 + lax.erf(pre * half_root))
            active[:, block] = (pre * risen).astype(bf16)
            slope = risen + pre * jnp.exp(-0.5 * pre * pre) * bell
            grads[:, block] = (turned(rows_out[...], held_down[block, :]) * slope).astype(bf16)
        for k in range(spans):
            place = slice(k * depth, (k + 1) * depth)
            made = turned(grads[...], held_up[place, :])
            side[0:1, place] = jnp.sum(
                made * normal_ref[:, place].astype(f32), axis=0, keepdims=True
            )
            side[1:2, place] = jnp.sum(made, axis=0, keepdims=True)
            part[:, place] = made * gain_ref[1:2, place]

    ins = [(second, whole(second))]
    ins += [(piece, at((1,) + piece.shape[1:], (at_piece, 0, 0))) for piece in pieces]
    ins += [(w, kept_out) for w in expand] + [(w, kept_out) for w in contract]
    ins += [(normal, whole(normal)), (gains, whole(gains))]
    outs = [
        full_out((rows, width)),
        full_out((rows, hidden)),
        full_out((rows, hidden)),
        full_out((rows, width), f32),
        full_out((2, width), f32),
    ]
    scratch = [
        pltpu.VMEM((width, hidden), bf16),
        pltpu.VMEM((hidden, width), bf16),
        pltpu.SemaphoreType.DMA((tiles, spans)),
        pltpu.SemaphoreType.DMA((tiles, spans)),
    ]
    return run(order, flags, kernel, ins, outs, scratch, "hidden_both")


def branch_out(order, flags, groups, contract, packed, lanes):
    hidden, depth = contract[0].shape
    across = groups[0][1].shape[1]
    spans = len(contract)
    width = depth * spans
    span_rows = groups[0][0].shape[0]
    block = span_rows // lanes
    count = len(groups)

    def kernel(flag_ref, *refs):
        group_refs, refs = refs[: 2 * count], refs[2 * count :]
        contract_refs, packed_refs = refs[:spans], refs[spans : 2 * spans]
        blocks, refs = refs[2 * spans : 2 * spans + count * lanes], refs[2 * spans + count * lanes :]
        held, held_out, sems = refs
        outputs = [w.at[:across, 3 * across : 3 * across + depth] for w in packed_refs]
        started = copies(
            [ref for k in range(spans) for ref in (outputs[k], contract_refs[k])],
            [ref for k in range(spans) for ref in (held_out.at[k], held.at[k])],
            [sems.at[j] for j in range(2 * spans)],
        )
        for k in range(spans):
            started[2 * k].wait()
            started[2 * k + 1].wait()
            columns = slice(k * depth, (k + 1) * depth)
            for c in range(count):
                made = plain(group_refs[2 * c + 1][...], held_out[k])
                made = made + plain(group_refs[2 * c][...], held[k])
                for j in range(lanes):
                    rows = made[j * block : (j + 1) * block]
                    blocks[c * lanes + j][:, columns] = rows.astype(bf16)

    ins = []
    for active, attended in groups:
        ins += [(active, whole(active)), (attended, whole(attended))]
    ins += [(w, kept_out) for w in contract] + [(w, kept_out) for w in packed]
    outs = [full_out((block, width))] * (count * lanes)
    scratch = [
        pltpu.VMEM((spans, hidden, depth), bf16),
        pltpu.VMEM((spans, across, depth), bf16),
        pltpu.SemaphoreType.DMA((2 * spans,)),
    ]
    return run(order, flags, kernel, ins, outs, scratch, "branch")


def attend_back(order, flags, pieces, packed, queries, pairs, probs, tables, scale):
    rows = sum(piece.shape[1] for piece in pieces)
    width = pieces[0].shape[2]
    heads, _, head_dim = queries.shape
    spans = len(packed)
    across, depth = heads * head_dim, width // spans
    half = spans // 2

    def kernel(flag_ref, *refs):
        piece_refs, refs = refs[: len(pieces)], refs[len(pieces) :]
        packed_refs, refs = refs[:spans], refs[spans:]
        query_ref, refs = refs[0], refs[1:]
        views, refs = spread(refs[: len(pairs)]), refs[len(pairs) :]
        prob_ref, table_ref, rows_out, turned_back, keep, send, held, sems = refs
        started = copies(
            [w.at[:across, 3 * across : 3 * across + depth] for w in packed_refs],
            [held.at[:, k * depth : (k + 1) * depth] for k in range(spans)],
            [sems.at[k] for k in range(spans)],
        )
        start = 0
        for piece_ref in piece_refs:
            size = piece_ref.shape[1]
            rows_out[start : start + size, :] = piece_ref[0]
            start += size
        for copy in started:
            copy.wait()
        grads = turned(rows_out[...], held[...]).astype(bf16)
        for h in range(heads):
            made = attention_grads(
                grads[:, h * head_dim : (h + 1) * head_dim],
                query_ref[h],
                [prob_ref[k, h] for k in range(spans)],
                views,
                h,
                keep,
                send,
                scale,
            )
            turned_back[h] = turn(made, table_ref, -1).astype(bf16)

    ins = [(piece, whole(piece)) for piece in pieces] + [(w, kept_out) for w in packed]
    ins += [(array, whole(array)) for array in (queries, *pairs, probs, tables)]
    outs = [full_out((rows, width)), full_out((heads, rows, head_dim))]
    outs += [full_out((half, 2, heads, rows, head_dim))] * 2
    scratch = [pltpu.VMEM((across, width), bf16), pltpu.SemaphoreType.DMA((spans,))]
    return run(order, flags, kernel, ins, outs, scratch, "attend_back")


def hidden_back(order, flags, upstream, contract, expand, slope, normal, gains):
    span_rows, width = upstream.shape
    hidden, depth = contract[0].shape
    spans = len(contract)
    tile = min(512, hidden)
    tiles = hidden // tile

    def kernel(flag_ref, *refs):
        upstream_ref, refs = refs[0], refs[1:]
        contract_refs, refs = refs[:spans], refs[spans:]
        expand_refs, refs = refs[:spans], refs[spans:]
        slope_ref, normal_ref, gain_ref, grads, part, side, held, held_up, sems, sems_up = refs
        started = [
            copies(
                [w.at[t * tile : (t + 1) * tile, :] for w in contract_refs],
                [held.at[t, :, k * depth : (k + 1) * depth] for k in range(spans)],
                [sems.at[t, k] for k in range(spans)],
            )
            for t in range(tiles)
        ]
        started_up = copies(
            expand_refs, [held_up.at[k] for k in range(spans)], [sems_up.at[k] for k in range(spans)]
        )
        for t in range(tiles):
            for copy in started[t]:
                copy.wait()
            columns = slice(t * tile, (t + 1) * tile)
            grads[:, columns] = (
                turned(upstream_ref[...], held[t]) * slope_ref[:, columns].astype(f32)
            ).astype(bf16)
        for k in range(spans):
            started_up[k].wait()
            made = turned(grads[...], held_up[k])
            columns = slice(k * depth, (k + 1) * depth)
            side[0:1, columns] = jnp.sum(
                made * normal_ref[:, columns].astype(f32), axis=0, keepdims=True
            )
            side[1:2, columns] = jnp.sum(made, axis=0, keepdims=True)
            part[:, columns] = made * gain_ref[1:2, columns]

    ins = [(upstream, whole(upstream))]
    ins += [(w, kept_out) for w in contract] + [(w, kept_out) for w in expand]
    ins += [
        (slope, whole(slope)),
        (normal, whole(normal)),
        (gains, whole(gains)),
    ]
    outs = [
        full_out((span_rows, hidden)),
        full_out((span_rows, width), f32),
        full_out((2, width), f32),
    ]
    scratch = [
        pltpu.VMEM((tiles, tile, width), bf16),
        pltpu.VMEM((spans, depth, hidden), bf16),
        pltpu.SemaphoreType.DMA((tiles, spans)),
        pltpu.SemaphoreType.DMA((spans,)),
    ]
    return run(order, flags, kernel, ins, outs, scratch, "hidden_back")


def project_back(
    order, flags, turned_back, own, came, weights, part, normal, gains, tables, lanes
):
    heads, span_rows, head_dim = turned_back.shape
    spans = len(weights)
    width = part.shape[1]
    depth, columns = width // spans, 3 * heads * head_dim
    block = span_rows // lanes

    def kernel(flag_ref, *refs):
        query_ref, own_ref, came_ref, refs = refs[0], refs[1], refs[2], refs[3:]
        weight_refs, refs = refs[:spans], refs[spans:]
        part_ref, normal_ref, gain_ref, table_ref, grads, side, *refs = refs
        blocks, (held, sems) = refs[:lanes], refs[lanes:]
        started = copies(
            [w.at[:depth, :columns] for w in weight_refs],
            [held.at[k] for k in range(spans)],
            [sems.at[k] for k in range(spans)],
        )
        for h in range(heads):
            at_column = h * 3 * head_dim
            keys = own_ref[0, h].astype(f32) + came_ref[0, h].astype(f32)
            values = own_ref[1, h].astype(f32) + came_ref[1, h].astype(f32)
            grads[:, at_column : at_column + head_dim] = query_ref[h]
            grads[:, at_column + head_dim : at_column + 2 * head_dim] = turn(
                keys, table_ref, -1
            ).astype(bf16)
            grads[:, at_column + 2 * head_dim : at_column + 3 * head_dim] = values.astype(bf16)
        for k in range(spans):
            started[k].wait()
            made = turned(grads[...], held[k])
            span_columns = slice(k * depth, (k + 1) * depth)
            side[0:1, span_columns] = jnp.sum(
                made * normal_ref[:, span_columns].astype(f32), axis=0, keepdims=True
            )
            side[1:2, span_columns] = jnp.sum(made, axis=0, keepdims=True)
            both = (made * gain_ref[0:1, span_columns] + part_ref[:, span_columns]).astype(bf16)
            for j in range(lanes):
                blocks[j][:, span_columns] = both[j * block : (j + 1) * block]

    ins = [(array, whole(array)) for array in (turned_back, own, came)]
    ins += [(w, kept_out) for w in weights]
    ins += [(part, whole(part)), (normal, whole(normal))]
    ins += [(gains, whole(gains)), (tables, whole(tables))]
    outs = [full_out((span_rows, columns)), full_out((2, width), f32)]
    outs += [full_out((block, width))] * lanes
    scratch = [pltpu.VMEM((spans, depth, columns), bf16), pltpu.SemaphoreType.DMA((spans,))]
    return run(order, flags, kernel, ins, outs, scratch, "project_back")


def weight_sums(order, flags, lefts, rights, by_rows, spans):
    rows = sum(piece.shape[0] for piece in lefts[0][0])
    left_width = sum(group[0].shape[1] for group in lefts[0])
    right_width = sum(group[0].shape[1] for group in rights[0])
    if by_rows:
        tile = left_width // spans
        steps, block = spans // 2, (tile, right_width)
    else:
        tile = min(512, left_width)
        while left_width % tile:
            tile //= 2
        steps, block = left_width // tile, (tile, right_width // 2)
    chunk = min(1024, block[1])
    while right_width % chunk:
        chunk //= 2
    pieces = [
        [piece for groups in (lefts[s], rights[s]) for group in groups for piece in group]
        for s in (0, 1)
    ]
    most = max(len(p) for p in pieces)

    def kernel(flag_ref, *refs):
        piece_refs = (refs[: len(pieces[0])], refs[len(pieces[0]) : len(pieces[0]) + len(pieces[1])])
        keep, send, left, right, flipped, sems = refs[len(pieces[0]) + len(pieces[1]) :]
        g = pl.program_id(0)
        for s in (0, 1):

            @pl.when((g == 0) & (flag_ref[2] == s))
            def _(s=s):
                targets = []
                for held, groups in ((left, lefts[s]), (right, rights[s])):
                    column = 0
                    for group in groups:
                        row, wide = 0, group[0].shape[1]
                        for piece in group:
                            targets.append(
                                held.at[row : row + piece.shape[0], column : column + wide]
                            )
                            row += piece.shape[0]
                        column += wide
                started = copies(
                    piece_refs[s], targets, [sems.at[j] for j in range(len(targets))]
                )
                for copy in started:
                    copy.wait()

        def product(column, store):
            flipped[...] = left[:, pl.ds(pl.multiple_of(column, LANES), tile)].T

            def one(c, _):
                columns = pl.ds(pl.multiple_of(c * chunk, chunk), chunk)
                store(c, plain(flipped[...], right[:, columns]).astype(bf16))
                return 0

            lax.fori_loop(0, right_width // chunk, one, 0)

        if by_rows:

            def to(target):
                def store(c, made):
                    target[:, pl.ds(pl.multiple_of(c * chunk, chunk), chunk)] = made

                return store

            product(g * tile, to(keep))
            product((g + steps) * tile, to(send))
        else:
            half = right_width // 2 // chunk

            def store(c, made):
                @pl.when(c < half)
                def _():
                    keep[:, pl.ds(pl.multiple_of(c * chunk, chunk), chunk)] = made

                @pl.when(c >= half)
                def _():
                    send[:, pl.ds(pl.multiple_of((c - half) * chunk, chunk), chunk)] = made

            product(g * tile, store)

    ins = [(piece, kept_out) for s in (0, 1) for piece in pieces[s]]
    dims = (steps * tile, block[1])
    outs = [(shape(dims), pl.BlockSpec(block, lambda g: (g, 0)))] * 2
    scratch = [
        pltpu.VMEM((rows, left_width), bf16),
        pltpu.VMEM((rows, right_width), bf16),
        pltpu.VMEM((tile, rows), bf16),
        pltpu.SemaphoreType.DMA((most,)),
    ]
    return run(
        order, flags, kernel, ins, outs, scratch, "weight_sums", grid=(steps,)
    )


def fold(order, flags, keep, came, dim):
    rows, columns = keep.shape
    if dim == 0:
        tile = rows // 4
        steps, block = rows // 2 // tile, (tile, columns)
        places = [lambda g: (g, 0), lambda g: (g + steps, 0)]
        half = (rows // 2, columns)
    else:
        tile = rows // 4
        steps, block = rows // tile, (tile, columns // 2)
        places = [lambda g: (g, 0), lambda g: (g, 1)]
        half = (rows, columns // 2)

    def kernel(flag_ref, keep_low, keep_high, came_low, came_high, low, high):
        low[...] = (keep_low[...].astype(f32) + came_low[...].astype(f32)).astype(bf16)
        high[...] = (keep_high[...].astype(f32) + came_high[...].astype(f32)).astype(bf16)

    ins = [(array, pl.BlockSpec(block, place)) for array in (keep, came) for place in places]
    outs = [(shape(half), pl.BlockSpec(block, lambda g: (g, 0)))] * 2
    return run(order, flags, kernel, ins, outs, [], "fold", grid=(steps,))


def shards(
    block_input,
    out_grad,
    triple_weight,
    output_weight,
    expand_weight,
    contract_weight,
    norm_gains,
    norm_biases,
):
    section = lax.axis_index("pipe")
    span = lax.axis_index("ctx")
    lane = lax.axis_index("tp")
    spans = lax.axis_size("ctx")
    lanes = lax.axis_size("tp")
    micros, rows, width = block_input.shape
    span_rows = rows * lanes
    heads = triple_weight.shape[2]
    head_dim = triple_weight.shape[4]
    across_units = heads * head_dim
    scale = head_dim ** (-0.5)
    first_section = section == 0
    both = (0, 1)

    def hop(array, axis, step, sections):
        size = lax.axis_size(axis)
        pairs = [(s * size + a, s * size + (a ^ step)) for s in sections for a in range(size)]
        return lax.ppermute(array, ("pipe", axis), pairs)

    order = Order()

    def flags_for(wanted):
        return jnp.stack([jnp.asarray(wanted), span, section]).astype(jnp.int32)

    flags = [flags_for(section == s) for s in both]
    always = flags_for(1)

    kept = [[SimpleNamespace() for _ in range(micros)] for _ in both]
    due = {}
    slot_index = [0]

    def slot(hops, kernels=()):
        now = slot_index[0]
        slot_index[0] += 1
        ready = due.pop(now, [])
        hops = [h if len(h) == 3 else h + (1,) for h in hops]
        if hops:
            gated = fence([operand for operand, _, _ in hops], order.last + ready)
            order.last = [min(gated, key=lambda array: array.size)]
            for passed, (_, go, slots) in zip(gated, hops):
                results = go(passed)
                results = results if isinstance(results, list) else [results]
                due.setdefault(now + slots, []).extend(results)
        else:
            order.last = order.last + ready
        for kernel in kernels:
            kernel()

    def halved(keep, came, dim):
        middle = keep.shape[dim] // 2
        total = keep.astype(f32) + came.astype(f32)
        return (
            lax.slice_in_dim(total, 0, middle, axis=dim).astype(bf16),
            lax.slice_in_dim(total, middle, 2 * middle, axis=dim).astype(bf16),
        )

    def spread_hops(pieces, axis, axis_name, sections, first):
        step = lax.axis_size(axis_name) // 4
        going = first
        while step:
            pieces.append(hop(going, axis_name, step, sections))
            going = jnp.concatenate(pieces, axis=axis)
            step //= 2
        return pieces[-1]

    def fold_hops(k, first, axis_name, dim, sections):
        step, size = 1, lax.axis_size(axis_name)
        while 2 * step < size:
            came = hop(first, axis_name, step, sections)
            k.keep, k.send = halved(k.keep, came, dim)
            first = k.send
            step *= 2
        return came

    depth = width // spans
    far = spans // 2
    assert depth == across_units
    small = jnp.concatenate([norm_gains[0], norm_biases[0]], axis=0)
    packed = jnp.concatenate(
        [triple_weight[0].reshape(depth, -1), output_weight[0].reshape(-1, depth)],
        axis=1,
    )
    packed = jnp.pad(packed, ((0, 16), (0, 0)))
    packed = lax.dynamic_update_slice(packed, small, (depth, 0))
    own_expand, own_contract = expand_weight[0], contract_weight[0]
    hidden = own_expand.shape[1]
    inputs = xor_blocks(block_input, span, spans)
    cotangent = xor_blocks(out_grad, span, spans)
    early = jnp.where(first_section, inputs, cotangent)

    in_row = jnp.arange(rows, dtype=jnp.int32)
    in_span = jnp.concatenate([(lane ^ j) * rows + in_row for j in doubling(lanes)])
    positions = span * span_rows + in_span
    key_positions = jnp.stack([(span ^ k) * span_rows + in_span for k in doubling(spans)])
    tables = rope_tables(positions)
    position_column = positions[:, None]
    key_positions = key_positions[:, None, :]

    def blocks_of(own, came):
        held, step = {0: own, far: came}, far // 2
        while step:
            for k in list(held):
                held[k ^ step] = hop(held[k], "ctx", step, both)
            step //= 2
        return [held[k] for k in doubling(spans)]

    lane_offsets = doubling(lanes)

    def across(array, j, source):
        pairs = [(source * lanes + a, (1 - source) * lanes + (a ^ j)) for a in range(lanes)]
        return lax.ppermute(array, ("pipe", "tp"), pairs)

    def rows_far(s, m):
        k = kept[s][m]

        def go(passed):
            k.rows = passed
            k.pieces = [passed, hop(passed, "tp", lanes // 2, (s,))]
            return k.pieces[1]

        return k.rows, go

    def rows_near(s, m):
        k = kept[s][m]

        def go(passed):
            last_piece = spread_hops(k.pieces, 0, "tp", (s,), passed)
            k.row_pieces = [piece[None] for piece in k.pieces]
            return last_piece

        return jnp.concatenate(k.pieces, axis=0), go

    def pair_far(s, m):
        k = kept[s][m]

        def go(passed):
            k.pairs = [passed, hop(passed, "ctx", far, (s,))]
            return k.pairs[1]

        return k.pair, go

    def pair_near(s, m):
        k = kept[s][m]

        def go(passed):
            return spread_hops(k.pairs, 0, "ctx", (s,), passed)

        return jnp.concatenate(k.pairs, axis=0), go

    def pair_grad_near(s, m):
        k = kept[s][m].pair_grad
        return k.send, lambda passed: fold_hops(k, passed, "ctx", 0, (s,))

    def pair_grad_far(s, m):
        k = kept[s][m].pair_grad

        def go(passed):
            k.came = hop(passed, "ctx", far, (s,))
            return k.came

        return k.send, go

    def sum_hops(s, m):
        blocks = kept[s][m].blocks
        arrived = kept[s][m].arrived = []

        def one(j):
            def go(passed):
                arrived.append(hop(passed, "tp", lane_offsets[j], (s,)))
                return arrived[-1]

            return blocks[j], go

        return [one(j) for j in range(1, lanes)]

    def sum_near(s, k):
        k.keep = jnp.concatenate(k.blocks[: lanes // 2], axis=0)
        going = jnp.concatenate(k.blocks[lanes // 2 :], axis=0)
        return going, lambda passed: fold_hops(k, passed, "tp", 0, (s,))

    def sum_far(s, k):
        def go(passed):
            k.blocks, k.arrived = [k.keep], [hop(passed, "tp", lanes // 2, (s,))]
            return k.arrived[0]

        return k.send, go

    def total_of(k):
        return sum(array.astype(f32) for array in [k.blocks[0], *k.arrived])

    def norm_back(upstream, combined, entering):
        normalized, inverse = normalize(entering.astype(f32))
        return (
            upstream.astype(f32)
            + inverse
            * (
                combined
                - jnp.mean(combined, axis=-1, keepdims=True)
                - normalized * jnp.mean(combined * normalized, axis=-1, keepdims=True)
            )
        ).astype(bf16)

    def middle_of(m):
        return (inputs[m].astype(f32) + total_of(kept[0][m])).astype(bf16)

    def entry_of(m):
        k = kept[1][m]
        return norm_back(cotangent[m], total_of(k), k.rows)

    def hand(s, m):
        k, other = kept[s][m], kept[1 - s][m]
        k.given = middle_of(m) if s == 0 else entry_of(m)

        def go(passed):
            k.given = passed
            pieces = [across(passed, j, s) for j in lane_offsets]
            other.rows = pieces[0]
            other.row_pieces = [piece[None] for piece in pieces]
            return pieces

        return k.given, go

    def hand_one(s, m):
        k, other = kept[s][m], kept[1 - s][m]
        k.given = middle_of(m) if s == 0 else entry_of(m)

        def go(passed):
            k.given = passed
            other.rows = across(passed, 0, s)
            return other.rows

        return k.given, go

    def run_project(s, m):
        k = kept[s][m]
        pieces, place = (early_pieces, m) if s == 0 else (k.row_pieces, 0)
        k.first, k.second, k.normal, k.queries, pair = project(
            order, flags[s], pieces, place, gains, biases, tables, packed, heads, head_dim
        )
        k.pair = pair[None]

    def run_expand(m):
        k = kept[0][m]
        k.active, k.slope = expand_up(order, flags[0], k.second, weights.expand, span_rows)

    def run_attend(m):
        k = kept[0][m]
        k.attended, k.probs = attend(
            order, flags[0], k.queries, k.pairs, position_column, key_positions, scale
        )

    def run_branch(m):
        k = kept[0][m]
        k.blocks = branch_out(
            order, flags[0], [(k.active, k.attended)], contract, packed, lanes
        )

    def run_hidden_both(m):
        k = kept[1][m]
        k.upstream, k.active, k.hidden, k.part, k.side_second = hidden_both(
            order,
            flags[1],
            k.second,
            early_pieces,
            m,
            weights.expand,
            contract,
            k.normal,
            gains,
        )

    def run_attend_both(m):
        k = kept[1][m]
        k.attended, k.turned_back, keep, send = attend_both(
            order,
            flags[1],
            k.upstream,
            packed,
            k.queries,
            k.pairs,
            position_column,
            key_positions,
            tables,
            scale,
        )
        k.pair_grad = SimpleNamespace(keep=keep, send=send)

    def run_attend_back(m):
        k = kept[0][m]
        k.upstream, k.turned_back, keep, send = attend_back(
            order,
            flags[0],
            k.row_pieces,
            packed,
            k.queries,
            k.pairs,
            k.probs,
            tables,
            scale,
        )
        k.pair_grad = SimpleNamespace(keep=keep, send=send)

    def run_hidden_back(m):
        k = kept[0][m]
        k.hidden, k.part, k.side_second = hidden_back(
            order,
            flags[0],
            k.upstream,
            contract,
            weights.expand,
            k.slope,
            k.normal,
            gains,
        )

    def run_project_back(s, m):
        k = kept[s][m]
        own, arrived = k.pair_grad.keep, k.pair_grad.came
        k.stacked, k.side_first, *k.blocks = project_back(
            order,
            flags[s],
            k.turned_back,
            own.reshape(own.shape[1:]),
            arrived.reshape(arrived.shape[1:]),
            packed,
            k.part,
            k.normal,
            gains,
            tables,
            lanes,
        )

    def of(name, s, count=micros):
        return [getattr(kept[s][m], name) for m in range(count)]

    branch_sums, expand_sums, triple_sums = (SimpleNamespace(parts=[]) for _ in range(3))

    def run_sums(w, lefts, rights, by_rows):
        w.dim = 0 if by_rows else 1
        w.keep, w.send = weight_sums(order, always, lefts, rights, by_rows, spans)

    def wide_near(w):
        def go(passed):
            w.came = hop(passed, "ctx", 1, both)
            return w.came

        return w.send, go

    def run_fold(w):
        step = 2
        w.keep, w.send = fold(order, always, w.keep, w.came, w.dim)
        while 2 * step < spans:
            w.came = hop(w.send, "ctx", step, both)
            w.keep, w.send = fold(order, always, w.keep, w.came, w.dim)
            step *= 2

    def wide_far(w, start, stop):
        def go(passed):
            w.parts.append(hop(passed, "ctx", far, both))
            return w.parts[-1]

        return w.send[start:stop], go

    weights = SimpleNamespace(expand_came=[], contract_came=[])
    half_depth = depth // 2

    def expand_far(start, stop):
        def go(passed):
            weights.expand_came.append(hop(passed, "ctx", far, both))
            return weights.expand_came[-1]

        return own_expand[start:stop], go

    def packed_far(passed):
        weights.packed_came = hop(passed, "ctx", far, both)
        return weights.packed_came

    def packed_near(passed):
        weights.packed = blocks_of(packed, passed)
        return weights.packed[1:]

    def expand_near(passed):
        weights.expand = blocks_of(own_expand, passed)
        return weights.expand[1:]

    def contract_far(start, stop):
        def go(passed):
            weights.contract_came.append(hop(passed, "ctx", far, both))
            return weights.contract_came[-1]

        return own_contract[start:stop], go

    def contract_near(passed):
        weights.contract = blocks_of(own_contract, passed)
        return weights.contract[1:]

    def early_hops(passed):
        weights.early = [passed] + [hop(passed, "tp", j, both) for j in lane_offsets[1:]]
        return weights.early[1:]

    due[1] = [expand_far(0, half_depth)[1](own_expand[:half_depth])]
    slot([(packed, packed_far), (early, early_hops)])
    early_pieces = weights.early
    slot([(weights.packed_came, packed_near), expand_far(half_depth, depth)])
    packed = weights.packed
    small_full = jnp.concatenate(
        [piece[depth : depth + 4, :depth] for piece in packed], axis=1
    ).astype(f32)
    gains, biases = small_full[:2], small_full[2:]
    slot(
        [
            (jnp.concatenate(weights.expand_came, axis=0), expand_near),
            contract_far(0, hidden // 2),
        ],
        [lambda m=m: run_project(0, m) for m in range(micros)],
    )
    a, b = kept
    slot(
        [pair_far(0, 0), contract_far(hidden // 2, hidden)],
        [lambda m=m: run_expand(m) for m in range(micros)],
    )
    contract_came = jnp.concatenate(weights.contract_came, axis=0)
    slot([(contract_came, contract_near), pair_near(0, 0)])
    contract = weights.contract
    slot([pair_far(0, 1)], [lambda: run_attend(0), lambda: run_branch(0)])
    slot([sum_near(0, a[0]), pair_near(0, 1), pair_far(0, 2)])
    slot(
        [sum_far(0, a[0]), pair_near(0, 2)], [lambda: run_attend(1), lambda: run_branch(1)]
    )
    slot(
        [hand_one(0, 0), sum_near(0, a[1])], [lambda: run_attend(2), lambda: run_branch(2)]
    )
    slot([rows_far(1, 0), sum_far(0, a[1])])
    slot([rows_near(1, 0), hand_one(0, 1), sum_near(0, a[2])])
    slot([rows_far(1, 1), sum_far(0, a[2])], [lambda: run_project(1, 0)])
    slot(
        [pair_far(1, 0), rows_near(1, 1), hand_one(0, 2)], [lambda: run_hidden_both(0)]
    )
    slot([pair_near(1, 0), rows_far(1, 2)], [lambda: run_project(1, 1)])
    slot(
        [pair_far(1, 1), rows_near(1, 2)],
        [lambda: run_attend_both(0), lambda: run_hidden_both(1)],
    )
    slot([pair_grad_near(1, 0), pair_near(1, 1)], [lambda: run_project(1, 2)])
    slot(
        [pair_grad_far(1, 0), pair_far(1, 2)],
        [lambda: run_attend_both(1), lambda: run_hidden_both(2)],
    )
    slot([pair_grad_near(1, 1), pair_near(1, 2)], [lambda: run_project_back(1, 0)])
    slot([sum_near(1, b[0]), pair_grad_far(1, 1)], [lambda: run_attend_both(2)])
    slot([sum_far(1, b[0]), pair_grad_near(1, 2)], [lambda: run_project_back(1, 1)])
    slot([hand_one(1, 0), sum_near(1, b[1]), pair_grad_far(1, 2)])
    slot([sum_far(1, b[1]), rows_far(0, 0)], [lambda: run_project_back(1, 2)])
    slot([sum_near(1, b[2]), hand_one(1, 1), rows_near(0, 0)])
    slot([sum_far(1, b[2]), rows_far(0, 1)], [lambda: run_attend_back(0)])
    slot(
        [hand_one(1, 2), rows_near(0, 1), pair_grad_near(0, 0)],
        [lambda: run_hidden_back(0)],
    )
    slot([rows_far(0, 2), pair_grad_far(0, 0)], [lambda: run_attend_back(1)])
    slot([rows_near(0, 2), pair_grad_near(0, 1)], [lambda: run_hidden_back(1)])
    last = micros - 1

    def run_branch_sums():
        run_sums(
            branch_sums,
            [[of("active", s), of("attended", s)] for s in both],
            [
                [of("upstream", 0, last) + [piece[0] for piece in a[last].row_pieces]],
                [of("upstream", 1)],
            ],
            False,
        )

    def run_expand_sums():
        run_sums(
            expand_sums,
            [[of("second", s)] for s in both],
            [[of("hidden", s)] for s in both],
            True,
        )

    def run_triple_sums():
        run_sums(
            triple_sums,
            [[of("first", s)] for s in both],
            [[of("stacked", s)] for s in both],
            True,
        )

    finals = SimpleNamespace()

    def run_final_branch():
        blocks = branch_out(
            order,
            flags[1],
            [(k.active, k.attended) for k in b],
            contract,
            packed,
            lanes,
        )
        halves = [
            [jnp.concatenate(blocks[m * lanes + at : m * lanes + at + lanes // 2]) for at in places]
            for m in range(micros)
            for places in [(0, lanes // 2)]
        ]
        finals.keep = jnp.stack([low for low, _ in halves])
        finals.send = jnp.stack([high for _, high in halves])

    def finals_near():
        return finals.send, lambda passed: fold_hops(finals, passed, "tp", 1, (1,))

    def finals_far():
        def go(passed):
            finals.came = hop(passed, "tp", lanes // 2, (1,))
            return finals.came

        return finals.send, go

    slot([pair_grad_far(0, 1)], [run_branch_sums])
    slot(
        [wide_near(branch_sums)], [lambda: run_attend_back(2), lambda: run_project_back(0, 0)]
    )
    slot([pair_grad_near(0, 2), sum_near(0, a[0])], [lambda: run_fold(branch_sums)])
    half_hidden = hidden // 2
    slot(
        [wide_far(branch_sums, 0, half_hidden), pair_grad_far(0, 2), sum_far(0, a[0])],
        [lambda: run_hidden_back(2), lambda: run_project_back(0, 1)],
    )
    slot(
        [wide_far(branch_sums, half_hidden, hidden), sum_near(0, a[1])],
        [lambda: run_project_back(0, 2), run_triple_sums],
    )
    slot(
        [
            wide_far(branch_sums, hidden, hidden + across_units),
            wide_near(triple_sums),
            sum_far(0, a[1]),
            sum_near(0, a[2]),
        ],
        [run_expand_sums],
    )

    def side_of(mades):
        return sum(
            jnp.concatenate([k.side_first, k.side_second], axis=0) for k in mades
        )

    side = SimpleNamespace(all=jnp.where(first_section, side_of(a), side_of(b)))

    def side_hops(passed):
        step = 1
        while step < spans:
            middle = passed.shape[1] // 2
            came = hop(passed[:, middle:], "ctx", step, both)
            passed = passed[:, :middle] + came
            step *= 2
        step = 1
        while step < lanes:
            came = hop(passed, "tp", step, both)
            passed = passed + came
            step *= 2
        side.all = passed
        return came

    slot([wide_near(expand_sums)], [lambda: run_fold(triple_sums)])
    slot(
        [wide_far(triple_sums, 0, depth), sum_far(0, a[2])],
        [lambda: run_fold(expand_sums), run_final_branch],
    )
    slot([wide_far(expand_sums, 0, half_depth), finals_near(), (side.all, side_hops)])
    slot([wide_far(expand_sums, half_depth, depth), finals_far()])

    def wide_total(keep, parts):
        came = jnp.concatenate(parts, axis=0) if len(parts) > 1 else parts[0]
        return keep.astype(f32) + came.astype(f32)

    contract_grads = wide_total(branch_sums.keep[:hidden], branch_sums.parts[:2])
    output_grads = wide_total(branch_sums.keep[hidden:], branch_sums.parts[2:])
    expand_grads = wide_total(expand_sums.keep, expand_sums.parts)
    triple_grads = wide_total(triple_sums.keep, triple_sums.parts)
    layer_outputs = jnp.stack(
        [
            jnp.where(
                first_section,
                kept[0][m].given,
                (
                    b[m].rows.astype(f32)
                    + finals.keep[m].astype(f32)
                    + finals.came[m].astype(f32)
                ).astype(bf16),
            )
            for m in range(micros)
        ]
    )
    entry_grads = jnp.stack(
        [
            jnp.where(
                first_section,
                norm_back(kept[0][m].rows, total_of(kept[0][m]), inputs[m]),
                kept[1][m].given,
            )
            for m in range(micros)
        ]
    )
    gain_grads = jnp.stack([side.all[0], side.all[2]])
    bias_grads = jnp.stack([side.all[1], side.all[3]])
    return (
        xor_blocks(layer_outputs, span, spans, inverse=True)[None],
        xor_blocks(entry_grads, span, spans, inverse=True)[None],
        triple_grads.reshape(triple_weight.shape),
        output_grads.reshape(output_weight.shape),
        expand_grads[None],
        contract_grads[None],
        gain_grads[None],
        bias_grads[None],
    )


def solution(mesh):
    return jax.shard_map(
        shards,
        mesh=mesh,
        in_specs=(
            P(None, ("ctx", "tp"), None),
            P(None, ("ctx", "tp"), None),
            P("pipe", "ctx", "tp", None, None),
            P("pipe", "tp", None, "ctx"),
            P("pipe", "ctx", "tp"),
            P("pipe", "tp", "ctx"),
            P("pipe", None, "ctx"),
            P("pipe", None, "ctx"),
        ),
        out_specs=(
            P("pipe", None, ("ctx", "tp"), None),
            P("pipe", None, ("ctx", "tp"), None),
            P("pipe", "ctx", "tp", None, None),
            P("pipe", "tp", None, "ctx"),
            P("pipe", "ctx", "tp"),
            P("pipe", "tp", "ctx"),
            P("pipe", None, "ctx"),
            P("pipe", None, "ctx"),
        ),
        check_vma=False,
    )
```

```python
import functools
from types import SimpleNamespace

import jax
import jax.numpy as jnp
from jax import lax
from jax.experimental import pallas as pl
from jax.experimental.pallas import tpu as pltpu
from jax.sharding import PartitionSpec as P

ROT = 64
LANES = 128
epsilon = 1e-05
masked_score = -1e30
f32 = jnp.float32
bf16 = jnp.bfloat16
vmem_bytes = 64 * 1024 * 1024
half_root = 0.7071067811865476
bell = 0.3989422804014327


def dot(a, b, dims):
    return lax.dot_general(a, b, (dims, ((), ())), preferred_element_type=f32)


def plain(a, b):
    return dot(a, b, ((1,), (0,)))


def turned(a, b):
    return dot(a, b, ((1,), (1,)))


def doubling(count):
    order, step = [0], count // 2
    while step:
        order += [k ^ step for k in order]
        step //= 2
    return order


def xor_blocks(values, index, count, inverse=False):
    width = values.shape[-1] // count
    order = doubling(count)

    def taken(places):
        return jnp.concatenate(
            [values[..., k * width : (k + 1) * width] for k in places], axis=-1
        )

    if inverse:
        values = taken([order.index(k) for k in range(count)])
    step = 1
    while step < count:
        swapped = taken([k ^ step for k in range(count)])
        values = jnp.where((index & step) != 0, swapped, values)
        step *= 2
    return values if inverse else taken(order)


def rope_tables(positions):
    half = ROT // 2
    frequency = 10000.0 ** (-jnp.arange(0, ROT, 2, dtype=f32) / ROT)
    angles = positions.astype(f32)[:, None] * frequency[None, :]
    cosine, sine = jnp.cos(angles), jnp.sin(angles)
    count = positions.shape[0]
    rest = jnp.zeros((count, LANES - ROT), f32)
    none = jnp.zeros((count, half), f32)
    return jnp.stack(
        [
            jnp.concatenate([cosine, cosine, rest + 1.0], axis=1),
            jnp.concatenate([-sine, none, rest], axis=1),
            jnp.concatenate([none, sine, rest], axis=1),
        ]
    )


def turn(values, tables, sign):
    half = ROT // 2
    part = values[:, :LANES]
    moved = (
        pltpu.roll(part, LANES - half, 1) * tables[1] + pltpu.roll(part, half, 1) * tables[2]
    )
    part = part * tables[0] + (moved if sign > 0 else -moved)
    return jnp.concatenate([part, values[:, LANES:]], axis=1)


def normalize(values):
    center = values - jnp.mean(values, axis=-1, keepdims=True)
    inverse = lax.rsqrt(jnp.mean(center * center, axis=-1, keepdims=True) + epsilon)
    return (center * inverse, inverse)


def whole(array):
    zeros = (0,) * array.ndim
    return pl.BlockSpec(array.shape, lambda *_: zeros)


def at(block, place):
    return pl.BlockSpec(block, lambda *_: place)


kept_out = pl.BlockSpec(memory_space=pl.ANY)


def shape(dims, dtype=bf16):
    return jax.ShapeDtypeStruct(dims, dtype)


class Order:
    def __init__(self):
        self.last = []

    def follow(self, results):
        self.last = [min(results, key=lambda array: array.size * array.dtype.itemsize)]

    def also(self, array):
        self.last = self.last + [array]


took = dict(
    project=7,
    expand=8,
    attend=5,
    branch=8,
    hidden_both=14,
    attend_both=11,
    attend_back=8,
    hidden_back=13,
    project_back=8,
    weight_sums=16,
    fold=7,
)
peak = 1.15e9


def run(order, flags, kernel, ins, outs, scratch, name, grid=(1,)):
    taken = len(ins)
    ins = [(flags, pl.BlockSpec(memory_space=pltpu.SMEM))] + list(ins)
    ins += [(array, kept_out) for array in order.last]
    arrays = [array for array, _ in ins]

    def body(flag_ref, *refs):
        @pl.when(flag_ref[0] == 1)
        def _():
            kernel(flag_ref, *refs[:taken], *refs[len(ins) - 1 :])

    results = pl.pallas_call(
        body,
        grid=grid,
        in_specs=[spec for _, spec in ins],
        out_specs=[spec for _, spec in outs],
        out_shape=[struct for struct, _ in outs],
        scratch_shapes=scratch,
        compiler_params=pltpu.CompilerParams(vmem_limit_bytes=vmem_bytes),
        cost_estimate=pl.CostEstimate(
            flops=int(took[name] * peak), bytes_accessed=0, transcendentals=0
        ),
        name=name,
    )(*arrays)
    order.follow(results)
    return results


def fence(through, waits):
    count = len(through)

    def kernel(*refs):
        pass

    return pl.pallas_call(
        kernel,
        in_specs=[kept_out] * (count + len(waits)),
        out_specs=[kept_out] * count,
        out_shape=[shape(array.shape, array.dtype) for array in through],
        input_output_aliases={j: j for j in range(count)},
        compiler_params=pltpu.CompilerParams(vmem_limit_bytes=vmem_bytes),
        cost_estimate=pl.CostEstimate(flops=1, bytes_accessed=1, transcendentals=0),
        name="fence",
    )(*through, *waits)


def full_out(dims, dtype=bf16):
    zeros = (0,) * len(dims)
    return (shape(dims, dtype), pl.BlockSpec(dims, lambda *_: zeros))


def copies(sources, targets, sems):
    started = []
    for source, target, sem in zip(sources, targets, sems):
        copy = pltpu.make_async_copy(source, target, sem)
        copy.start()
        started.append(copy)
    return started


def project(order, flags, pieces, at_piece, gains, biases, tables, weights, heads, head_dim):
    count, width = 1, pieces[0].shape[2]
    span_rows = sum(piece.shape[1] for piece in pieces)
    rows = count * span_rows
    chunk = pieces[0].shape[1]
    spans = len(weights)
    depth = width // spans
    wide = 3 * head_dim
    columns = heads * wide

    def kernel(flag_ref, *refs):
        piece_refs = refs[: len(pieces)]
        gain_ref, bias_ref, table_ref = refs[len(pieces) : len(pieces) + 3]
        weight_refs = refs[len(pieces) + 3 : len(pieces) + 3 + spans]
        first, second, normal, queries, pair, held, sems = refs[len(pieces) + 3 + spans :]
        started = []
        for h in range(heads):
            started.append(
                copies(
                    [w.at[:depth, h * wide : (h + 1) * wide] for w in weight_refs],
                    [held.at[h, k * depth : (k + 1) * depth] for k in range(spans)],
                    [sems.at[h, k] for k in range(spans)],
                )
            )
        start = 0
        for piece_ref in piece_refs:
            chunks = piece_ref.shape[1] // chunk

            def one(i, _, piece_ref=piece_ref, start=start, chunks=chunks):
                m, c = i // chunks, i % chunks
                values = piece_ref[m, pl.ds(pl.multiple_of(c * chunk, chunk), chunk), :]
                normed, _ = normalize(values.astype(f32))
                to = pl.ds(
                    pl.multiple_of(m * span_rows + start + c * chunk, chunk), chunk
                )
                normal[to, :] = normed.astype(bf16)
                first[to, :] = (normed * gain_ref[0:1] + bias_ref[0:1]).astype(bf16)
                second[to, :] = (normed * gain_ref[1:2] + bias_ref[1:2]).astype(bf16)
                return 0

            lax.fori_loop(0, count * chunks, one, 0)
            start += piece_ref.shape[1]
        for h in range(heads):
            for copy in started[h]:
                copy.wait()

            def two(m, _, h=h):
                to = pl.ds(pl.multiple_of(m * span_rows, span_rows), span_rows)
                made = plain(first[to, :], held[h])
                queries[h, to, :] = turn(made[:, :head_dim], table_ref, 1).astype(bf16)
                pair[0, h, to, :] = turn(
                    made[:, head_dim : 2 * head_dim], table_ref, 1
                ).astype(bf16)
                pair[1, h, to, :] = made[:, 2 * head_dim :].astype(bf16)
                return 0

            lax.fori_loop(0, count, two, 0)

    ins = [(piece, at((1,) + piece.shape[1:], (at_piece, 0, 0))) for piece in pieces]
    ins += [(array, whole(array)) for array in (gains, biases, tables)]
    ins += [(w, kept_out) for w in weights]
    outs = [full_out((rows, width))] * 3 + [
        full_out((heads, rows, head_dim)),
        full_out((2, heads, rows, head_dim)),
    ]
    scratch = [
        pltpu.VMEM((heads, width, wide), bf16),
        pltpu.SemaphoreType.DMA((heads, spans)),
    ]
    return run(order, flags, kernel, ins, outs, scratch, "project")


def expand_up(order, flags, second, weights, span_rows):
    rows, width = second.shape
    depth, hidden = weights[0].shape
    spans = len(weights)
    tile = min(512, hidden)
    tiles = hidden // tile

    def kernel(flag_ref, *refs):
        second_ref, weight_refs = refs[0], refs[1 : 1 + spans]
        active, slope, held, sems = refs[1 + spans :]
        started = []
        for t in range(tiles):
            started.append(
                copies(
                    [w.at[:, t * tile : (t + 1) * tile] for w in weight_refs],
                    [held.at[t, k * depth : (k + 1) * depth] for k in range(spans)],
                    [sems.at[t, k] for k in range(spans)],
                )
            )
        for t in range(tiles):
            for copy in started[t]:
                copy.wait()

            def one(m, _, t=t):
                to = pl.ds(pl.multiple_of(m * span_rows, span_rows), span_rows)
                pre = plain(second_ref[to, :], held[t])
                risen = 0.5 * (1.0 + lax.erf(pre * half_root))
                columns = slice(t * tile, (t + 1) * tile)
                active[to, columns] = (pre * risen).astype(bf16)
                slope[to, columns] = (
                    risen + pre * jnp.exp(-0.5 * pre * pre) * bell
                ).astype(bf16)
                return 0

            lax.fori_loop(0, rows // span_rows, one, 0)

    ins = [(second, whole(second))] + [(w, kept_out) for w in weights]
    outs = [full_out((rows, hidden))] * 2
    scratch = [
        pltpu.VMEM((tiles, width, tile), bf16),
        pltpu.SemaphoreType.DMA((tiles, spans)),
    ]
    return run(order, flags, kernel, ins, outs, scratch, "expand")


def spread(refs):
    return [ref.at[j] for ref in refs for j in range(ref.shape[0])]


def attention(here, pairs, head, row_ref, key_ref, scale):
    scores = []
    for k, pair in enumerate(pairs):
        raw = turned(here, pair[0, head]) * scale
        scores.append(jnp.where(key_ref[k] <= row_ref[...], raw, masked_score))
    top = functools.reduce(
        jnp.maximum, [jnp.max(part, axis=1, keepdims=True) for part in scores]
    )
    scores = [jnp.exp(part - top) for part in scores]
    inverse = 1.0 / sum(jnp.sum(part, axis=1, keepdims=True) for part in scores)
    return [part * inverse for part in scores]


def attend(order, flags, queries, pairs, positions, key_positions, scale):
    heads, rows, head_dim = queries.shape
    spans = sum(pair.shape[0] for pair in pairs)

    def kernel(flag_ref, query_ref, *refs):
        views, refs = spread(refs[: len(pairs)]), refs[len(pairs) :]
        row_ref, key_ref, attended, probs = refs
        for h in range(heads):
            parts = attention(query_ref[h], views, h, row_ref, key_ref, scale)
            summed = None
            for k in range(spans):
                part = parts[k].astype(bf16)
                probs[k, h] = part
                term = plain(part, views[k][1, h])
                summed = term if summed is None else summed + term
            attended[:, h * head_dim : (h + 1) * head_dim] = summed.astype(bf16)

    ins = [
        (array, whole(array)) for array in (queries, *pairs, positions, key_positions)
    ]
    outs = [full_out((rows, heads * head_dim)), full_out((spans, heads, rows, rows))]
    return run(order, flags, kernel, ins, outs, [], "attend")


def attention_grads(grad, here, parts, views, head, keep, send, scale):
    half = keep.shape[0]
    grad_probs = [turned(grad, view[1, head]) for view in views]
    delta = sum(
        jnp.sum(part.astype(f32) * slope, axis=1, keepdims=True)
        for part, slope in zip(parts, grad_probs)
    )
    query_grad = None
    for k, view in enumerate(views):
        slopes = (parts[k].astype(f32) * (grad_probs[k] - delta)).astype(bf16)
        term = plain(slopes, view[0, head])
        query_grad = term if query_grad is None else query_grad + term
        side = keep if k < half else send
        side[k % half, 0, head] = (dot(slopes, here, ((0,), (0,))) * scale).astype(bf16)
        side[k % half, 1, head] = dot(parts[k].astype(bf16), grad, ((0,), (0,))).astype(bf16)
    return query_grad * scale


def attend_both(
    order, flags, rows_in, packed, queries, pairs, positions, key_positions, tables, scale
):
    heads, rows, head_dim = queries.shape
    width = rows_in.shape[1]
    spans = len(packed)
    across, depth = heads * head_dim, width // spans
    half = spans // 2

    def kernel(flag_ref, rows_ref, *refs):
        packed_refs, refs = refs[:spans], refs[spans:]
        query_ref, refs = refs[0], refs[1:]
        views, refs = spread(refs[: len(pairs)]), refs[len(pairs) :]
        row_ref, key_ref, table_ref, attended, turned_back, keep, send, held, sems = refs
        started = copies(
            [w.at[:across, 3 * across : 3 * across + depth] for w in packed_refs],
            [held.at[:, k * depth : (k + 1) * depth] for k in range(spans)],
            [sems.at[k] for k in range(spans)],
        )
        all_parts = []
        for h in range(heads):
            parts = attention(query_ref[h], views, h, row_ref, key_ref, scale)
            summed = None
            for k in range(spans):
                term = plain(parts[k].astype(bf16), views[k][1, h])
                summed = term if summed is None else summed + term
            attended[:, h * head_dim : (h + 1) * head_dim] = summed.astype(bf16)
            all_parts.append(parts)
        for copy in started:
            copy.wait()
        grads = turned(rows_ref[...], held[...]).astype(bf16)
        for h in range(heads):
            made = attention_grads(
                grads[:, h * head_dim : (h + 1) * head_dim],
                query_ref[h],
                all_parts[h],
                views,
                h,
                keep,
                send,
                scale,
            )
            turned_back[h] = turn(made, table_ref, -1).astype(bf16)

    ins = [(rows_in, whole(rows_in))] + [(w, kept_out) for w in packed]
    ins += [
        (array, whole(array)) for array in (queries, *pairs, positions, key_positions, tables)
    ]
    outs = [full_out((rows, across)), full_out((heads, rows, head_dim))]
    outs += [full_out((half, 2, heads, rows, head_dim))] * 2
    scratch = [pltpu.VMEM((across, width), bf16), pltpu.SemaphoreType.DMA((spans,))]
    return run(order, flags, kernel, ins, outs, scratch, "attend_both")


def hidden_both(order, flags, second, pieces, at_piece, expand, contract, normal, gains):
    rows, width = second.shape
    hidden, depth = contract[0].shape
    spans = len(contract)
    tile = min(512, hidden)
    tiles = hidden // tile

    def kernel(flag_ref, second_ref, *refs):
        piece_refs, refs = refs[: len(pieces)], refs[len(pieces) :]
        expand_refs, refs = refs[:spans], refs[spans:]
        contract_refs, refs = refs[:spans], refs[spans:]
        normal_ref, gain_ref, rows_out, active, grads, part, side, *refs = refs
        held_up, held_down, sems_up, sems_down = refs
        started = []
        for t in range(tiles):
            block = slice(t * tile, (t + 1) * tile)
            places = [slice(k * depth, (k + 1) * depth) for k in range(spans)]
            up = copies(
                [w.at[:, block] for w in expand_refs],
                [held_up.at[place, block] for place in places],
                [sems_up.at[t, k] for k in range(spans)],
            )
            down = copies(
                [w.at[block, :] for w in contract_refs],
                [held_down.at[block, place] for place in places],
                [sems_down.at[t, k] for k in range(spans)],
            )
            started.append((up, down))
        start = 0
        for piece_ref in piece_refs:
            size = piece_ref.shape[1]
            rows_out[start : start + size, :] = piece_ref[0]
            start += size
        for t in range(tiles):
            block = slice(t * tile, (t + 1) * tile)
            for copy in started[t][0] + started[t][1]:
                copy.wait()
            pre = plain(second_ref[...], held_up[:, block])
            risen = 0.5 * (1.0 + lax.erf(pre * half_root))
            active[:, block] = (pre * risen).astype(bf16)
            slope = risen + pre * jnp.exp(-0.5 * pre * pre) * bell
            grads[:, block] = (turned(rows_out[...], held_down[block, :]) * slope).astype(bf16)
        for k in range(spans):
            place = slice(k * depth, (k + 1) * depth)
            made = turned(grads[...], held_up[place, :])
            side[0:1, place] = jnp.sum(
                made * normal_ref[:, place].astype(f32), axis=0, keepdims=True
            )
            side[1:2, place] = jnp.sum(made, axis=0, keepdims=True)
            part[:, place] = made * gain_ref[1:2, place]

    ins = [(second, whole(second))]
    ins += [(piece, at((1,) + piece.shape[1:], (at_piece, 0, 0))) for piece in pieces]
    ins += [(w, kept_out) for w in expand] + [(w, kept_out) for w in contract]
    ins += [(normal, whole(normal)), (gains, whole(gains))]
    outs = [
        full_out((rows, width)),
        full_out((rows, hidden)),
        full_out((rows, hidden)),
        full_out((rows, width), f32),
        full_out((2, width), f32),
    ]
    scratch = [
        pltpu.VMEM((width, hidden), bf16),
        pltpu.VMEM((hidden, width), bf16),
        pltpu.SemaphoreType.DMA((tiles, spans)),
        pltpu.SemaphoreType.DMA((tiles, spans)),
    ]
    return run(order, flags, kernel, ins, outs, scratch, "hidden_both")


def branch_out(order, flags, groups, contract, packed):
    hidden, depth = contract[0].shape
    across = groups[0][1].shape[1]
    spans = len(contract)
    width = depth * spans
    span_rows = groups[0][0].shape[0]
    block = span_rows // 2
    count = len(groups)

    def kernel(flag_ref, *refs):
        group_refs, refs = refs[: 2 * count], refs[2 * count :]
        contract_refs, packed_refs = refs[:spans], refs[spans : 2 * spans]
        blocks, refs = refs[2 * spans : 2 * (spans + count)], refs[2 * (spans + count) :]
        held, held_out, sems = refs
        outputs = [w.at[:across, 3 * across : 3 * across + depth] for w in packed_refs]
        started = copies(
            [ref for k in range(spans) for ref in (outputs[k], contract_refs[k])],
            [ref for k in range(spans) for ref in (held_out.at[k], held.at[k])],
            [sems.at[j] for j in range(2 * spans)],
        )
        for k in range(spans):
            started[2 * k].wait()
            started[2 * k + 1].wait()
            columns = slice(k * depth, (k + 1) * depth)
            for c in range(count):
                made = plain(group_refs[2 * c + 1][...], held_out[k])
                made = made + plain(group_refs[2 * c][...], held[k])
                blocks[2 * c][:, columns] = made[:block].astype(bf16)
                blocks[2 * c + 1][:, columns] = made[block:].astype(bf16)

    ins = []
    for active, attended in groups:
        ins += [(active, whole(active)), (attended, whole(attended))]
    ins += [(w, kept_out) for w in contract] + [(w, kept_out) for w in packed]
    outs = [full_out((block, width))] * (2 * count)
    scratch = [
        pltpu.VMEM((spans, hidden, depth), bf16),
        pltpu.VMEM((spans, across, depth), bf16),
        pltpu.SemaphoreType.DMA((2 * spans,)),
    ]
    return run(order, flags, kernel, ins, outs, scratch, "branch")


def attend_back(order, flags, pieces, packed, queries, pairs, probs, tables, scale):
    rows = sum(piece.shape[1] for piece in pieces)
    width = pieces[0].shape[2]
    heads, _, head_dim = queries.shape
    spans = len(packed)
    across, depth = heads * head_dim, width // spans
    half = spans // 2

    def kernel(flag_ref, *refs):
        piece_refs, refs = refs[: len(pieces)], refs[len(pieces) :]
        packed_refs, refs = refs[:spans], refs[spans:]
        query_ref, refs = refs[0], refs[1:]
        views, refs = spread(refs[: len(pairs)]), refs[len(pairs) :]
        prob_ref, table_ref, rows_out, turned_back, keep, send, held, sems = refs
        started = copies(
            [w.at[:across, 3 * across : 3 * across + depth] for w in packed_refs],
            [held.at[:, k * depth : (k + 1) * depth] for k in range(spans)],
            [sems.at[k] for k in range(spans)],
        )
        start = 0
        for piece_ref in piece_refs:
            size = piece_ref.shape[1]
            rows_out[start : start + size, :] = piece_ref[0]
            start += size
        for copy in started:
            copy.wait()
        grads = turned(rows_out[...], held[...]).astype(bf16)
        for h in range(heads):
            made = attention_grads(
                grads[:, h * head_dim : (h + 1) * head_dim],
                query_ref[h],
                [prob_ref[k, h] for k in range(spans)],
                views,
                h,
                keep,
                send,
                scale,
            )
            turned_back[h] = turn(made, table_ref, -1).astype(bf16)

    ins = [(piece, whole(piece)) for piece in pieces] + [(w, kept_out) for w in packed]
    ins += [(array, whole(array)) for array in (queries, *pairs, probs, tables)]
    outs = [full_out((rows, width)), full_out((heads, rows, head_dim))]
    outs += [full_out((half, 2, heads, rows, head_dim))] * 2
    scratch = [pltpu.VMEM((across, width), bf16), pltpu.SemaphoreType.DMA((spans,))]
    return run(order, flags, kernel, ins, outs, scratch, "attend_back")


def hidden_back(order, flags, upstream, contract, expand, slope, normal, gains):
    span_rows, width = upstream.shape
    hidden, depth = contract[0].shape
    spans = len(contract)
    tile = min(512, hidden)
    tiles = hidden // tile

    def kernel(flag_ref, *refs):
        upstream_ref, refs = refs[0], refs[1:]
        contract_refs, refs = refs[:spans], refs[spans:]
        expand_refs, refs = refs[:spans], refs[spans:]
        slope_ref, normal_ref, gain_ref, grads, part, side, held, held_up, sems, sems_up = refs
        started = [
            copies(
                [w.at[t * tile : (t + 1) * tile, :] for w in contract_refs],
                [held.at[t, :, k * depth : (k + 1) * depth] for k in range(spans)],
                [sems.at[t, k] for k in range(spans)],
            )
            for t in range(tiles)
        ]
        started_up = copies(
            expand_refs, [held_up.at[k] for k in range(spans)], [sems_up.at[k] for k in range(spans)]
        )
        for t in range(tiles):
            for copy in started[t]:
                copy.wait()
            columns = slice(t * tile, (t + 1) * tile)
            grads[:, columns] = (
                turned(upstream_ref[...], held[t]) * slope_ref[:, columns].astype(f32)
            ).astype(bf16)
        for k in range(spans):
            started_up[k].wait()
            made = turned(grads[...], held_up[k])
            columns = slice(k * depth, (k + 1) * depth)
            side[0:1, columns] = jnp.sum(
                made * normal_ref[:, columns].astype(f32), axis=0, keepdims=True
            )
            side[1:2, columns] = jnp.sum(made, axis=0, keepdims=True)
            part[:, columns] = made * gain_ref[1:2, columns]

    ins = [(upstream, whole(upstream))]
    ins += [(w, kept_out) for w in contract] + [(w, kept_out) for w in expand]
    ins += [
        (slope, whole(slope)),
        (normal, whole(normal)),
        (gains, whole(gains)),
    ]
    outs = [
        full_out((span_rows, hidden)),
        full_out((span_rows, width), f32),
        full_out((2, width), f32),
    ]
    scratch = [
        pltpu.VMEM((tiles, tile, width), bf16),
        pltpu.VMEM((spans, depth, hidden), bf16),
        pltpu.SemaphoreType.DMA((tiles, spans)),
        pltpu.SemaphoreType.DMA((spans,)),
    ]
    return run(order, flags, kernel, ins, outs, scratch, "hidden_back")


def project_back(
    order, flags, turned_back, own, came, weights, part, normal, gains, tables
):
    heads, span_rows, head_dim = turned_back.shape
    spans = len(weights)
    width = part.shape[1]
    depth, columns = width // spans, 3 * heads * head_dim
    block = span_rows // 2

    def kernel(flag_ref, *refs):
        query_ref, own_ref, came_ref, refs = refs[0], refs[1], refs[2], refs[3:]
        weight_refs, refs = refs[:spans], refs[spans:]
        part_ref, normal_ref, gain_ref, table_ref, grads, side, *refs = refs
        low, high, held, sems = refs
        started = copies(
            [w.at[:depth, :columns] for w in weight_refs],
            [held.at[k] for k in range(spans)],
            [sems.at[k] for k in range(spans)],
        )
        for h in range(heads):
            at_column = h * 3 * head_dim
            keys = own_ref[0, h].astype(f32) + came_ref[0, h].astype(f32)
            values = own_ref[1, h].astype(f32) + came_ref[1, h].astype(f32)
            grads[:, at_column : at_column + head_dim] = query_ref[h]
            grads[:, at_column + head_dim : at_column + 2 * head_dim] = turn(
                keys, table_ref, -1
            ).astype(bf16)
            grads[:, at_column + 2 * head_dim : at_column + 3 * head_dim] = values.astype(bf16)
        for k in range(spans):
            started[k].wait()
            made = turned(grads[...], held[k])
            span_columns = slice(k * depth, (k + 1) * depth)
            side[0:1, span_columns] = jnp.sum(
                made * normal_ref[:, span_columns].astype(f32), axis=0, keepdims=True
            )
            side[1:2, span_columns] = jnp.sum(made, axis=0, keepdims=True)
            both = (made * gain_ref[0:1, span_columns] + part_ref[:, span_columns]).astype(bf16)
            low[:, span_columns] = both[:block]
            high[:, span_columns] = both[block:]

    ins = [(array, whole(array)) for array in (turned_back, own, came)]
    ins += [(w, kept_out) for w in weights]
    ins += [(part, whole(part)), (normal, whole(normal))]
    ins += [(gains, whole(gains)), (tables, whole(tables))]
    outs = [full_out((span_rows, columns)), full_out((2, width), f32)]
    outs += [full_out((block, width))] * 2
    scratch = [pltpu.VMEM((spans, depth, columns), bf16), pltpu.SemaphoreType.DMA((spans,))]
    return run(order, flags, kernel, ins, outs, scratch, "project_back")


def weight_sums(order, flags, lefts, rights, by_rows, spans):
    rows = sum(piece.shape[0] for piece in lefts[0][0])
    left_width = sum(group[0].shape[1] for group in lefts[0])
    right_width = sum(group[0].shape[1] for group in rights[0])
    if by_rows:
        tile = left_width // spans
        steps, block = spans // 2, (tile, right_width)
    else:
        tile = min(512, left_width)
        while left_width % tile:
            tile //= 2
        steps, block = left_width // tile, (tile, right_width // 2)
    chunk = min(1024, block[1])
    while right_width % chunk:
        chunk //= 2
    pieces = [
        [piece for groups in (lefts[s], rights[s]) for group in groups for piece in group]
        for s in (0, 1)
    ]
    most = max(len(p) for p in pieces)

    def kernel(flag_ref, *refs):
        piece_refs = (refs[: len(pieces[0])], refs[len(pieces[0]) : len(pieces[0]) + len(pieces[1])])
        keep, send, left, right, flipped, sems = refs[len(pieces[0]) + len(pieces[1]) :]
        g = pl.program_id(0)
        for s in (0, 1):

            @pl.when((g == 0) & (flag_ref[2] == s))
            def _(s=s):
                targets = []
                for held, groups in ((left, lefts[s]), (right, rights[s])):
                    column = 0
                    for group in groups:
                        row, wide = 0, group[0].shape[1]
                        for piece in group:
                            targets.append(
                                held.at[row : row + piece.shape[0], column : column + wide]
                            )
                            row += piece.shape[0]
                        column += wide
                started = copies(
                    piece_refs[s], targets, [sems.at[j] for j in range(len(targets))]
                )
                for copy in started:
                    copy.wait()

        def product(column, store):
            flipped[...] = left[:, pl.ds(pl.multiple_of(column, LANES), tile)].T

            def one(c, _):
                columns = pl.ds(pl.multiple_of(c * chunk, chunk), chunk)
                store(c, plain(flipped[...], right[:, columns]).astype(bf16))
                return 0

            lax.fori_loop(0, right_width // chunk, one, 0)

        if by_rows:

            def to(target):
                def store(c, made):
                    target[:, pl.ds(pl.multiple_of(c * chunk, chunk), chunk)] = made

                return store

            product(g * tile, to(keep))
            product((g + steps) * tile, to(send))
        else:
            half = right_width // 2 // chunk

            def store(c, made):
                @pl.when(c < half)
                def _():
                    keep[:, pl.ds(pl.multiple_of(c * chunk, chunk), chunk)] = made

                @pl.when(c >= half)
                def _():
                    send[:, pl.ds(pl.multiple_of((c - half) * chunk, chunk), chunk)] = made

            product(g * tile, store)

    ins = [(piece, kept_out) for s in (0, 1) for piece in pieces[s]]
    dims = (steps * tile, block[1])
    outs = [(shape(dims), pl.BlockSpec(block, lambda g: (g, 0)))] * 2
    scratch = [
        pltpu.VMEM((rows, left_width), bf16),
        pltpu.VMEM((rows, right_width), bf16),
        pltpu.VMEM((tile, rows), bf16),
        pltpu.SemaphoreType.DMA((most,)),
    ]
    return run(
        order, flags, kernel, ins, outs, scratch, "weight_sums", grid=(steps,)
    )


def fold(order, flags, keep, came, dim):
    rows, columns = keep.shape
    if dim == 0:
        tile = rows // 4
        steps, block = rows // 2 // tile, (tile, columns)
        places = [lambda g: (g, 0), lambda g: (g + steps, 0)]
        half = (rows // 2, columns)
    else:
        tile = rows // 4
        steps, block = rows // tile, (tile, columns // 2)
        places = [lambda g: (g, 0), lambda g: (g, 1)]
        half = (rows, columns // 2)

    def kernel(flag_ref, keep_low, keep_high, came_low, came_high, low, high):
        low[...] = (keep_low[...].astype(f32) + came_low[...].astype(f32)).astype(bf16)
        high[...] = (keep_high[...].astype(f32) + came_high[...].astype(f32)).astype(bf16)

    ins = [(array, pl.BlockSpec(block, place)) for array in (keep, came) for place in places]
    outs = [(shape(half), pl.BlockSpec(block, lambda g: (g, 0)))] * 2
    return run(order, flags, kernel, ins, outs, [], "fold", grid=(steps,))


def shards(
    block_input,
    out_grad,
    triple_weight,
    output_weight,
    expand_weight,
    contract_weight,
    norm_gains,
    norm_biases,
):
    section = lax.axis_index("pipe")
    span = lax.axis_index("ctx")
    lane = lax.axis_index("tp")
    spans = lax.axis_size("ctx")
    lanes = lax.axis_size("tp")
    micros, rows, width = block_input.shape
    span_rows = rows * lanes
    heads = triple_weight.shape[2]
    head_dim = triple_weight.shape[4]
    across_units = heads * head_dim
    scale = head_dim ** (-0.5)
    first_section = section == 0
    both = (0, 1)

    def hop(array, axis, step, sections):
        size = lax.axis_size(axis)
        pairs = [(s * size + a, s * size + (a ^ step)) for s in sections for a in range(size)]
        return lax.ppermute(array, ("pipe", axis), pairs)

    order = Order()

    def flags_for(wanted):
        return jnp.stack([jnp.asarray(wanted), span, section]).astype(jnp.int32)

    flags = [flags_for(section == s) for s in both]
    always = flags_for(1)

    kept = [[SimpleNamespace() for _ in range(micros)] for _ in both]
    due = {}
    slot_index = [0]

    def slot(hops, kernels=()):
        now = slot_index[0]
        slot_index[0] += 1
        ready = due.pop(now, [])
        hops = [h if len(h) == 3 else h + (1,) for h in hops]
        if hops:
            gated = fence([operand for operand, _, _ in hops], order.last + ready)
            order.last = [min(gated, key=lambda array: array.size)]
            for passed, (_, go, slots) in zip(gated, hops):
                results = go(passed)
                results = results if isinstance(results, list) else [results]
                due.setdefault(now + slots, []).extend(results)
        else:
            order.last = order.last + ready
        for kernel in kernels:
            kernel()

    def halved(keep, came, dim):
        middle = keep.shape[dim] // 2
        total = keep.astype(f32) + came.astype(f32)
        return (
            lax.slice_in_dim(total, 0, middle, axis=dim).astype(bf16),
            lax.slice_in_dim(total, middle, 2 * middle, axis=dim).astype(bf16),
        )

    def spread_hops(pieces, axis, axis_name, sections, first):
        step = lax.axis_size(axis_name) // 4
        going = first
        while step:
            pieces.append(hop(going, axis_name, step, sections))
            going = jnp.concatenate(pieces, axis=axis)
            step //= 2
        return pieces[-1]

    def fold_hops(k, first, axis_name, dim, sections):
        step, size = 1, lax.axis_size(axis_name)
        while 2 * step < size:
            came = hop(first, axis_name, step, sections)
            k.keep, k.send = halved(k.keep, came, dim)
            first = k.send
            step *= 2
        return came

    depth = width // spans
    far = spans // 2
    assert depth == across_units
    small = jnp.concatenate([norm_gains[0], norm_biases[0]], axis=0)
    packed = jnp.concatenate(
        [triple_weight[0].reshape(depth, -1), output_weight[0].reshape(-1, depth)],
        axis=1,
    )
    packed = jnp.pad(packed, ((0, 16), (0, 0)))
    packed = lax.dynamic_update_slice(packed, small, (depth, 0))
    own_expand, own_contract = expand_weight[0], contract_weight[0]
    hidden = own_expand.shape[1]
    inputs = xor_blocks(block_input, span, spans)
    cotangent = xor_blocks(out_grad, span, spans)
    early = jnp.where(first_section, inputs, cotangent)

    in_row = jnp.arange(rows, dtype=jnp.int32)
    in_span = jnp.concatenate([(lane ^ j) * rows + in_row for j in doubling(lanes)])
    positions = span * span_rows + in_span
    key_positions = jnp.stack([(span ^ k) * span_rows + in_span for k in doubling(spans)])
    tables = rope_tables(positions)
    position_column = positions[:, None]
    key_positions = key_positions[:, None, :]

    def blocks_of(own, came):
        held, step = {0: own, far: came}, far // 2
        while step:
            for k in list(held):
                held[k ^ step] = hop(held[k], "ctx", step, both)
            step //= 2
        return [held[k] for k in doubling(spans)]

    lane_offsets = doubling(lanes)

    def across(array, j, source):
        pairs = [(source * lanes + a, (1 - source) * lanes + (a ^ j)) for a in range(lanes)]
        return lax.ppermute(array, ("pipe", "tp"), pairs)

    def rows_far(s, m):
        k = kept[s][m]

        def go(passed):
            k.rows = passed
            k.pieces = [passed, hop(passed, "tp", lanes // 2, (s,))]
            return k.pieces[1]

        return k.rows, go

    def rows_near(s, m):
        k = kept[s][m]

        def go(passed):
            last_piece = spread_hops(k.pieces, 0, "tp", (s,), passed)
            k.row_pieces = [piece[None] for piece in k.pieces]
            return last_piece

        return jnp.concatenate(k.pieces, axis=0), go

    def pair_far(s, m):
        k = kept[s][m]

        def go(passed):
            k.pairs = [passed, hop(passed, "ctx", far, (s,))]
            return k.pairs[1]

        return k.pair, go

    def pair_near(s, m):
        k = kept[s][m]

        def go(passed):
            return spread_hops(k.pairs, 0, "ctx", (s,), passed)

        return jnp.concatenate(k.pairs, axis=0), go

    def pair_grad_near(s, m):
        k = kept[s][m].pair_grad
        return k.send, lambda passed: fold_hops(k, passed, "ctx", 0, (s,))

    def pair_grad_far(s, m):
        k = kept[s][m].pair_grad

        def go(passed):
            k.came = hop(passed, "ctx", far, (s,))
            return k.came

        return k.send, go

    def sum_near(s, k):
        k.keep, going = k.blocks
        return going, lambda passed: fold_hops(k, passed, "tp", 0, (s,))

    def sum_far(s, k):
        def go(passed):
            k.blocks, k.arrived = [k.keep], [hop(passed, "tp", lanes // 2, (s,))]
            return k.arrived[0]

        return k.send, go

    def total_of(k):
        return sum(array.astype(f32) for array in [k.blocks[0], *k.arrived])

    def norm_back(upstream, combined, entering):
        normalized, inverse = normalize(entering.astype(f32))
        return (
            upstream.astype(f32)
            + inverse
            * (
                combined
                - jnp.mean(combined, axis=-1, keepdims=True)
                - normalized * jnp.mean(combined * normalized, axis=-1, keepdims=True)
            )
        ).astype(bf16)

    def middle_of(m):
        return (inputs[m].astype(f32) + total_of(kept[0][m])).astype(bf16)

    def entry_of(m):
        k = kept[1][m]
        return norm_back(cotangent[m], total_of(k), k.rows)

    def hand_one(s, m):
        k, other = kept[s][m], kept[1 - s][m]
        k.given = middle_of(m) if s == 0 else entry_of(m)

        def go(passed):
            k.given = passed
            other.rows = across(passed, 0, s)
            return other.rows

        return k.given, go

    def run_project(s, m):
        k = kept[s][m]
        pieces, place = (early_pieces, m) if s == 0 else (k.row_pieces, 0)
        k.first, k.second, k.normal, k.queries, pair = project(
            order, flags[s], pieces, place, gains, biases, tables, packed, heads, head_dim
        )
        k.pair = pair[None]

    def run_expand(m):
        k = kept[0][m]
        k.active, k.slope = expand_up(order, flags[0], k.second, weights.expand, span_rows)

    def run_attend(m):
        k = kept[0][m]
        k.attended, k.probs = attend(
            order, flags[0], k.queries, k.pairs, position_column, key_positions, scale
        )

    def run_branch(m):
        k = kept[0][m]
        k.blocks = branch_out(
            order, flags[0], [(k.active, k.attended)], contract, packed
        )

    def run_hidden_both(m):
        k = kept[1][m]
        k.upstream, k.active, k.hidden, k.part, k.side_second = hidden_both(
            order,
            flags[1],
            k.second,
            early_pieces,
            m,
            weights.expand,
            contract,
            k.normal,
            gains,
        )

    def run_attend_both(m):
        k = kept[1][m]
        k.attended, k.turned_back, keep, send = attend_both(
            order,
            flags[1],
            k.upstream,
            packed,
            k.queries,
            k.pairs,
            position_column,
            key_positions,
            tables,
            scale,
        )
        k.pair_grad = SimpleNamespace(keep=keep, send=send)

    def run_attend_back(m):
        k = kept[0][m]
        k.upstream, k.turned_back, keep, send = attend_back(
            order,
            flags[0],
            k.row_pieces,
            packed,
            k.queries,
            k.pairs,
            k.probs,
            tables,
            scale,
        )
        k.pair_grad = SimpleNamespace(keep=keep, send=send)

    def run_hidden_back(m):
        k = kept[0][m]
        k.hidden, k.part, k.side_second = hidden_back(
            order,
            flags[0],
            k.upstream,
            contract,
            weights.expand,
            k.slope,
            k.normal,
            gains,
        )

    def run_project_back(s, m):
        k = kept[s][m]
        own, arrived = k.pair_grad.keep, k.pair_grad.came
        k.stacked, k.side_first, *k.blocks = project_back(
            order,
            flags[s],
            k.turned_back,
            own.reshape(own.shape[1:]),
            arrived.reshape(arrived.shape[1:]),
            packed,
            k.part,
            k.normal,
            gains,
            tables,
        )

    def of(name, s, count=micros):
        return [getattr(kept[s][m], name) for m in range(count)]

    branch_sums, expand_sums, triple_sums = (SimpleNamespace(parts=[]) for _ in range(3))

    def run_sums(w, lefts, rights, by_rows):
        w.dim = 0 if by_rows else 1
        w.keep, w.send = weight_sums(order, always, lefts, rights, by_rows, spans)

    def wide_near(w):
        def go(passed):
            w.came = hop(passed, "ctx", 1, both)
            return w.came

        return w.send, go

    def run_fold(w):
        step = 2
        w.keep, w.send = fold(order, always, w.keep, w.came, w.dim)
        while 2 * step < spans:
            w.came = hop(w.send, "ctx", step, both)
            w.keep, w.send = fold(order, always, w.keep, w.came, w.dim)
            step *= 2

    def wide_far(w, start, stop):
        def go(passed):
            w.parts.append(hop(passed, "ctx", far, both))
            return w.parts[-1]

        return w.send[start:stop], go

    weights = SimpleNamespace(contract_came=[])
    half_depth = depth // 2
    contract_cut = 9 * hidden // 16

    def expand_far(passed):
        weights.expand_came = hop(passed, "ctx", far, both)
        return weights.expand_came

    def packed_far(passed):
        weights.packed_came = hop(passed, "ctx", far, both)
        return weights.packed_came

    def packed_near(passed):
        weights.packed = blocks_of(packed, passed)
        return weights.packed[1:]

    def expand_near(passed):
        weights.expand = blocks_of(own_expand, passed)
        return weights.expand[1:]

    def contract_far(start, stop):
        def go(passed):
            weights.contract_came.append(hop(passed, "ctx", far, both))
            return weights.contract_came[-1]

        return own_contract[start:stop], go

    def contract_near(passed):
        weights.contract = blocks_of(own_contract, passed)
        return weights.contract[1:]

    def early_hops(passed):
        weights.early = [passed] + [hop(passed, "tp", j, both) for j in lane_offsets[1:]]
        return weights.early[1:]

    slot([(packed, packed_far), (own_expand, expand_far), (early, early_hops)])
    early_pieces = weights.early
    slot([(weights.packed_came, packed_near), (weights.expand_came, expand_near)])
    packed = weights.packed
    small_full = jnp.concatenate(
        [piece[depth : depth + 4, :depth] for piece in packed], axis=1
    ).astype(f32)
    gains, biases = small_full[:2], small_full[2:]
    slot(
        [contract_far(0, contract_cut)],
        [lambda m=m: run_project(0, m) for m in range(micros)],
    )
    a, b = kept
    slot(
        [pair_far(0, 0), contract_far(contract_cut, hidden)],
        [lambda m=m: run_expand(m) for m in range(micros)],
    )
    contract_came = jnp.concatenate(weights.contract_came, axis=0)
    slot([(contract_came, contract_near), pair_near(0, 0)])
    contract = weights.contract
    slot([pair_far(0, 1)], [lambda: run_attend(0), lambda: run_branch(0)])
    slot([sum_near(0, a[0]), pair_near(0, 1), pair_far(0, 2)])
    slot(
        [sum_far(0, a[0]), pair_near(0, 2)], [lambda: run_attend(1), lambda: run_branch(1)]
    )
    slot(
        [hand_one(0, 0), sum_near(0, a[1])], [lambda: run_attend(2), lambda: run_branch(2)]
    )
    slot([rows_far(1, 0), sum_far(0, a[1])])
    slot([rows_near(1, 0), hand_one(0, 1), sum_near(0, a[2])])
    slot([rows_far(1, 1), sum_far(0, a[2])], [lambda: run_project(1, 0)])
    slot(
        [pair_far(1, 0), rows_near(1, 1), hand_one(0, 2)], [lambda: run_hidden_both(0)]
    )
    slot([pair_near(1, 0), rows_far(1, 2)], [lambda: run_project(1, 1)])
    slot(
        [pair_far(1, 1), rows_near(1, 2)],
        [lambda: run_attend_both(0), lambda: run_hidden_both(1)],
    )
    slot([pair_grad_near(1, 0), pair_near(1, 1)], [lambda: run_project(1, 2)])
    slot(
        [pair_grad_far(1, 0), pair_far(1, 2)],
        [lambda: run_attend_both(1), lambda: run_hidden_both(2)],
    )
    slot([pair_grad_near(1, 1), pair_near(1, 2)], [lambda: run_project_back(1, 0)])
    slot([sum_near(1, b[0]), pair_grad_far(1, 1)], [lambda: run_attend_both(2)])
    slot([sum_far(1, b[0]), pair_grad_near(1, 2)], [lambda: run_project_back(1, 1)])
    slot([hand_one(1, 0), sum_near(1, b[1]), pair_grad_far(1, 2)])
    slot([sum_far(1, b[1]), rows_far(0, 0)], [lambda: run_project_back(1, 2)])
    slot([sum_near(1, b[2]), hand_one(1, 1), rows_near(0, 0)])
    slot([sum_far(1, b[2]), rows_far(0, 1)], [lambda: run_attend_back(0)])
    slot(
        [hand_one(1, 2), rows_near(0, 1), pair_grad_near(0, 0)],
        [lambda: run_hidden_back(0)],
    )
    slot([rows_far(0, 2), pair_grad_far(0, 0)], [lambda: run_attend_back(1)])
    slot([rows_near(0, 2), pair_grad_near(0, 1)], [lambda: run_hidden_back(1)])
    last = micros - 1

    def run_branch_sums():
        run_sums(
            branch_sums,
            [[of("active", s), of("attended", s)] for s in both],
            [
                [of("upstream", 0, last) + [piece[0] for piece in a[last].row_pieces]],
                [of("upstream", 1)],
            ],
            False,
        )

    def run_expand_sums():
        run_sums(
            expand_sums,
            [[of("second", s)] for s in both],
            [[of("hidden", s)] for s in both],
            True,
        )

    def run_triple_sums():
        run_sums(
            triple_sums,
            [[of("first", s)] for s in both],
            [[of("stacked", s)] for s in both],
            True,
        )

    finals = SimpleNamespace()

    def run_final_branch():
        blocks = branch_out(
            order, flags[1], [(k.active, k.attended) for k in b], contract, packed
        )
        finals.keep = jnp.stack(blocks[0::2])
        finals.send = jnp.stack(blocks[1::2])

    def finals_near():
        return finals.send, lambda passed: fold_hops(finals, passed, "tp", 1, (1,))

    def finals_far():
        def go(passed):
            finals.came = hop(passed, "tp", lanes // 2, (1,))
            return finals.came

        return finals.send, go

    slot([pair_grad_far(0, 1)], [run_branch_sums])
    slot(
        [wide_near(branch_sums)], [lambda: run_attend_back(2), lambda: run_project_back(0, 0)]
    )
    slot([pair_grad_near(0, 2), sum_near(0, a[0])], [lambda: run_fold(branch_sums)])
    cut = [0, hidden // 4, 3 * hidden // 4, hidden + across_units]
    slot(
        [pair_grad_far(0, 2), wide_far(branch_sums, cut[0], cut[1]), sum_far(0, a[0])],
        [lambda: run_hidden_back(2), lambda: run_project_back(0, 1)],
    )
    slot(
        [wide_far(branch_sums, cut[1], cut[2]), sum_near(0, a[1])],
        [lambda: run_project_back(0, 2), run_triple_sums],
    )

    def side_of(mades):
        return sum(
            jnp.concatenate([k.side_first, k.side_second], axis=0) for k in mades
        )

    side = SimpleNamespace(all=jnp.where(first_section, side_of(a), side_of(b)))

    def side_ctx(passed):
        step = 1
        while step < spans:
            middle = passed.shape[1] // 2
            came = hop(passed[:, middle:], "ctx", step, both)
            passed = passed[:, :middle] + came
            step *= 2
        side.all = passed
        return came

    def side_tp(passed):
        step = 1
        while step < lanes:
            came = hop(passed, "tp", step, both)
            passed = passed + came
            step *= 2
        side.all = passed
        return came

    slot([wide_near(triple_sums), (side.all, side_ctx), sum_near(0, a[2])])
    slot([], [lambda: run_fold(triple_sums)])
    slot([wide_far(triple_sums, 0, half_depth), sum_far(0, a[1])], [run_expand_sums])
    slot([wide_near(expand_sums), wide_far(triple_sums, half_depth, depth), sum_far(0, a[2])])
    slot([wide_far(branch_sums, cut[2], cut[3])], [lambda: run_fold(expand_sums)])
    slot([wide_far(expand_sums, 0, half_depth), (side.all, side_tp)], [run_final_branch])
    slot([wide_far(expand_sums, half_depth, depth), finals_near()])
    slot([finals_far()])

    def wide_total(keep, parts):
        came = jnp.concatenate(parts, axis=0) if len(parts) > 1 else parts[0]
        return keep.astype(f32) + came.astype(f32)

    branch_grads = wide_total(branch_sums.keep, branch_sums.parts)
    contract_grads, output_grads = branch_grads[:hidden], branch_grads[hidden:]
    expand_grads = wide_total(expand_sums.keep, expand_sums.parts)
    triple_grads = wide_total(triple_sums.keep, triple_sums.parts)
    layer_outputs = jnp.stack(
        [
            jnp.where(
                first_section,
                kept[0][m].given,
                (
                    b[m].rows.astype(f32)
                    + finals.keep[m].astype(f32)
                    + finals.came[m].astype(f32)
                ).astype(bf16),
            )
            for m in range(micros)
        ]
    )
    entry_grads = jnp.stack(
        [
            jnp.where(
                first_section,
                norm_back(kept[0][m].rows, total_of(kept[0][m]), inputs[m]),
                kept[1][m].given,
            )
            for m in range(micros)
        ]
    )
    gain_grads = jnp.stack([side.all[0], side.all[2]])
    bias_grads = jnp.stack([side.all[1], side.all[3]])
    return (
        xor_blocks(layer_outputs, span, spans, inverse=True)[None],
        xor_blocks(entry_grads, span, spans, inverse=True)[None],
        triple_grads.reshape(triple_weight.shape),
        output_grads.reshape(output_weight.shape),
        expand_grads[None],
        contract_grads[None],
        gain_grads[None],
        bias_grads[None],
    )


def solution(mesh):
    return jax.shard_map(
        shards,
        mesh=mesh,
        in_specs=(
            P(None, ("ctx", "tp"), None),
            P(None, ("ctx", "tp"), None),
            P("pipe", "ctx", "tp", None, None),
            P("pipe", "tp", None, "ctx"),
            P("pipe", "ctx", "tp"),
            P("pipe", "tp", "ctx"),
            P("pipe", None, "ctx"),
            P("pipe", None, "ctx"),
        ),
        out_specs=(
            P("pipe", None, ("ctx", "tp"), None),
            P("pipe", None, ("ctx", "tp"), None),
            P("pipe", "ctx", "tp", None, None),
            P("pipe", "tp", None, "ctx"),
            P("pipe", "ctx", "tp"),
            P("pipe", "tp", "ctx"),
            P("pipe", None, "ctx"),
            P("pipe", None, "ctx"),
        ),
        check_vma=False,
    )
```

```python
import functools
import math
from types import SimpleNamespace

import jax
import jax.numpy as jnp
from jax import lax
from jax.experimental import pallas as pl
from jax.experimental.pallas import tpu as pltpu
from jax.sharding import PartitionSpec as P

ROT = 64
LANES = 128
epsilon = 1e-05
masked_score = -1e30
f32 = jnp.float32
bf16 = jnp.bfloat16
mebibyte = 1024 * 1024
half_root = 0.7071067811865476
bell = 0.3989422804014327


def dot(a, b, dims):
    return lax.dot_general(a, b, (dims, ((), ())), preferred_element_type=f32)


def plain(a, b):
    return dot(a, b, ((1,), (0,)))


def turned(a, b):
    return dot(a, b, ((1,), (1,)))


def doubling(count):
    order, step = [0], count // 2
    while step:
        order += [k ^ step for k in order]
        step //= 2
    return order


def xor_blocks(values, index, count, inverse=False):
    width = values.shape[-1] // count
    order = doubling(count)

    def taken(places):
        return jnp.concatenate(
            [values[..., k * width : (k + 1) * width] for k in places], axis=-1
        )

    if inverse:
        values = taken([order.index(k) for k in range(count)])
    step = 1
    while step < count:
        swapped = taken([k ^ step for k in range(count)])
        values = jnp.where((index & step) != 0, swapped, values)
        step *= 2
    return values if inverse else taken(order)


def rope_tables(positions):
    half = ROT // 2
    frequency = 10000.0 ** (-jnp.arange(0, ROT, 2, dtype=f32) / ROT)
    angles = positions.astype(f32)[:, None] * frequency[None, :]
    cosine, sine = jnp.cos(angles), jnp.sin(angles)
    count = positions.shape[0]
    rest = jnp.zeros((count, LANES - ROT), f32)
    none = jnp.zeros((count, half), f32)
    return jnp.stack(
        [
            jnp.concatenate([cosine, cosine, rest + 1.0], axis=1),
            jnp.concatenate([-sine, none, rest], axis=1),
            jnp.concatenate([none, sine, rest], axis=1),
        ]
    )


def turn(values, tables, sign):
    half = ROT // 2
    part = values[:, :LANES]
    moved = (
        pltpu.roll(part, LANES - half, 1) * tables[1] + pltpu.roll(part, half, 1) * tables[2]
    )
    part = part * tables[0] + (moved if sign > 0 else -moved)
    return jnp.concatenate([part, values[:, LANES:]], axis=1)


def normalize(values):
    center = values - jnp.mean(values, axis=-1, keepdims=True)
    inverse = lax.rsqrt(jnp.mean(center * center, axis=-1, keepdims=True) + epsilon)
    return (center * inverse, inverse)


def whole(array):
    zeros = (0,) * array.ndim
    return pl.BlockSpec(array.shape, lambda *_: zeros)


def at(block, place):
    return pl.BlockSpec(block, lambda *_: place)


kept_out = pl.BlockSpec(memory_space=pl.ANY)


def shape(dims, dtype=bf16):
    return jax.ShapeDtypeStruct(dims, dtype)


class Order:
    def __init__(self):
        self.last = []

    def follow(self, results):
        self.last = [min(results, key=lambda array: array.size * array.dtype.itemsize)]

    def also(self, array):
        self.last = self.last + [array]


took = dict(
    project=7,
    expand=8,
    attend=5,
    branch=8,
    hidden_both=14,
    attend_both=11,
    attend_back=8,
    hidden_back=13,
    project_back=8,
    weight_sums=16,
    fold=7,
)
peak = 1.15e9


def run(order, flags, kernel, ins, outs, scratch, name, grid=(1,), work=0):
    taken = len(ins)
    ins = [(flags, pl.BlockSpec(memory_space=pltpu.SMEM))] + list(ins)
    ins += [(array, kept_out) for array in order.last]
    arrays = [array for array, _ in ins]
    once = grid == (1,)

    def sized(spec, dtype):
        if spec.block_shape is None:
            return spec, 0
        size = math.prod(spec.block_shape) * jnp.dtype(dtype).itemsize
        if not once:
            return spec, 2 * size
        single = pl.BlockSpec(
            spec.block_shape, spec.index_map, pipeline_mode=pl.Buffered(1)
        )
        return single, size

    in_specs = [sized(spec, array.dtype) for array, spec in ins]
    out_specs = [sized(spec, struct.dtype) for struct, spec in outs]
    held = sum(size for _, size in in_specs + out_specs)
    for buffer in scratch:
        if buffer.memory_space == pltpu.VMEM:
            held += math.prod(buffer.shape) * jnp.dtype(buffer.dtype).itemsize

    def body(flag_ref, *refs):
        @pl.when(flag_ref[0] == 1)
        def _():
            kernel(flag_ref, *refs[:taken], *refs[len(ins) - 1 :])

    results = pl.pallas_call(
        body,
        grid=grid,
        in_specs=[spec for spec, _ in in_specs],
        out_specs=[spec for spec, _ in out_specs],
        out_shape=[struct for struct, _ in outs],
        scratch_shapes=scratch,
        compiler_params=pltpu.CompilerParams(
            vmem_limit_bytes=int(held + (work + 4) * mebibyte)
        ),
        cost_estimate=pl.CostEstimate(
            flops=int(took[name] * peak), bytes_accessed=0, transcendentals=0
        ),
        name=name,
    )(*arrays)
    order.follow(results)
    return results


def fence(through, waits):
    count = len(through)

    def kernel(*refs):
        pass

    return pl.pallas_call(
        kernel,
        in_specs=[kept_out] * (count + len(waits)),
        out_specs=[kept_out] * count,
        out_shape=[shape(array.shape, array.dtype) for array in through],
        input_output_aliases={j: j for j in range(count)},
        compiler_params=pltpu.CompilerParams(vmem_limit_bytes=mebibyte),
        cost_estimate=pl.CostEstimate(flops=1, bytes_accessed=1, transcendentals=0),
        name="fence",
    )(*through, *waits)


def full_out(dims, dtype=bf16):
    zeros = (0,) * len(dims)
    return (shape(dims, dtype), pl.BlockSpec(dims, lambda *_: zeros))


def copies(sources, targets, sems):
    started = []
    for source, target, sem in zip(sources, targets, sems):
        copy = pltpu.make_async_copy(source, target, sem)
        copy.start()
        started.append(copy)
    return started


def project(order, flags, pieces, at_piece, gains, biases, tables, weights, heads, head_dim):
    count, width = 1, pieces[0].shape[2]
    span_rows = sum(piece.shape[1] for piece in pieces)
    rows = count * span_rows
    chunk = pieces[0].shape[1]
    spans = len(weights)
    depth = width // spans
    wide = 3 * head_dim
    columns = heads * wide

    def kernel(flag_ref, *refs):
        piece_refs = refs[: len(pieces)]
        gain_ref, bias_ref, table_ref = refs[len(pieces) : len(pieces) + 3]
        weight_refs = refs[len(pieces) + 3 : len(pieces) + 3 + spans]
        first, second, normal, queries, pair, held, sems = refs[len(pieces) + 3 + spans :]
        started = []
        for h in range(heads):
            started.append(
                copies(
                    [w.at[:depth, h * wide : (h + 1) * wide] for w in weight_refs],
                    [held.at[h, k * depth : (k + 1) * depth] for k in range(spans)],
                    [sems.at[h, k] for k in range(spans)],
                )
            )
        start = 0
        for piece_ref in piece_refs:
            chunks = piece_ref.shape[1] // chunk

            def one(i, _, piece_ref=piece_ref, start=start, chunks=chunks):
                m, c = i // chunks, i % chunks
                values = piece_ref[m, pl.ds(pl.multiple_of(c * chunk, chunk), chunk), :]
                normed, _ = normalize(values.astype(f32))
                to = pl.ds(
                    pl.multiple_of(m * span_rows + start + c * chunk, chunk), chunk
                )
                normal[to, :] = normed.astype(bf16)
                first[to, :] = (normed * gain_ref[0:1] + bias_ref[0:1]).astype(bf16)
                second[to, :] = (normed * gain_ref[1:2] + bias_ref[1:2]).astype(bf16)
                return 0

            lax.fori_loop(0, count * chunks, one, 0)
            start += piece_ref.shape[1]
        for h in range(heads):
            for copy in started[h]:
                copy.wait()

            def two(m, _, h=h):
                to = pl.ds(pl.multiple_of(m * span_rows, span_rows), span_rows)
                made = plain(first[to, :], held[h])
                queries[h, to, :] = turn(made[:, :head_dim], table_ref, 1).astype(bf16)
                pair[0, h, to, :] = turn(
                    made[:, head_dim : 2 * head_dim], table_ref, 1
                ).astype(bf16)
                pair[1, h, to, :] = made[:, 2 * head_dim :].astype(bf16)
                return 0

            lax.fori_loop(0, count, two, 0)

    ins = [(piece, at((1,) + piece.shape[1:], (at_piece, 0, 0))) for piece in pieces]
    ins += [(array, whole(array)) for array in (gains, biases, tables)]
    ins += [(w, kept_out) for w in weights]
    outs = [full_out((rows, width))] * 3 + [
        full_out((heads, rows, head_dim)),
        full_out((2, heads, rows, head_dim)),
    ]
    scratch = [
        pltpu.VMEM((heads, width, wide), bf16),
        pltpu.SemaphoreType.DMA((heads, spans)),
    ]
    return run(order, flags, kernel, ins, outs, scratch, "project")


def expand_up(order, flags, second, weights, span_rows):
    rows, width = second.shape
    depth, hidden = weights[0].shape
    spans = len(weights)
    tile = min(512, hidden)
    tiles = hidden // tile

    def kernel(flag_ref, *refs):
        second_ref, weight_refs = refs[0], refs[1 : 1 + spans]
        active, slope, held, sems = refs[1 + spans :]
        started = []
        for t in range(tiles):
            started.append(
                copies(
                    [w.at[:, t * tile : (t + 1) * tile] for w in weight_refs],
                    [held.at[t, k * depth : (k + 1) * depth] for k in range(spans)],
                    [sems.at[t, k] for k in range(spans)],
                )
            )
        for t in range(tiles):
            for copy in started[t]:
                copy.wait()

            def one(m, _, t=t):
                to = pl.ds(pl.multiple_of(m * span_rows, span_rows), span_rows)
                pre = plain(second_ref[to, :], held[t])
                risen = 0.5 * (1.0 + lax.erf(pre * half_root))
                columns = slice(t * tile, (t + 1) * tile)
                active[to, columns] = (pre * risen).astype(bf16)
                slope[to, columns] = (
                    risen + pre * jnp.exp(-0.5 * pre * pre) * bell
                ).astype(bf16)
                return 0

            lax.fori_loop(0, rows // span_rows, one, 0)

    ins = [(second, whole(second))] + [(w, kept_out) for w in weights]
    outs = [full_out((rows, hidden))] * 2
    scratch = [
        pltpu.VMEM((tiles, width, tile), bf16),
        pltpu.SemaphoreType.DMA((tiles, spans)),
    ]
    return run(order, flags, kernel, ins, outs, scratch, "expand")


def spread(refs):
    return [ref.at[j] for ref in refs for j in range(ref.shape[0])]


def attention(here, pairs, head, row_ref, key_ref, scale):
    scores = []
    for k, pair in enumerate(pairs):
        raw = turned(here, pair[0, head]) * scale
        scores.append(jnp.where(key_ref[k] <= row_ref[...], raw, masked_score))
    top = functools.reduce(
        jnp.maximum, [jnp.max(part, axis=1, keepdims=True) for part in scores]
    )
    scores = [jnp.exp(part - top) for part in scores]
    inverse = 1.0 / sum(jnp.sum(part, axis=1, keepdims=True) for part in scores)
    return [part * inverse for part in scores]


def attend(order, flags, queries, pairs, positions, key_positions, scale):
    heads, rows, head_dim = queries.shape
    spans = sum(pair.shape[0] for pair in pairs)

    def kernel(flag_ref, query_ref, *refs):
        views, refs = spread(refs[: len(pairs)]), refs[len(pairs) :]
        row_ref, key_ref, attended, probs = refs
        for h in range(heads):
            parts = attention(query_ref[h], views, h, row_ref, key_ref, scale)
            summed = None
            for k in range(spans):
                part = parts[k].astype(bf16)
                probs[k, h] = part
                term = plain(part, views[k][1, h])
                summed = term if summed is None else summed + term
            attended[:, h * head_dim : (h + 1) * head_dim] = summed.astype(bf16)

    ins = [
        (array, whole(array)) for array in (queries, *pairs, positions, key_positions)
    ]
    outs = [full_out((rows, heads * head_dim)), full_out((spans, heads, rows, rows))]
    work = spans * rows * rows * 4 * heads * 4 / mebibyte
    return run(order, flags, kernel, ins, outs, [], "attend", work=work)


def attention_grads(grad, here, parts, views, head, keep, send, scale):
    half = keep.shape[0]
    grad_probs = [turned(grad, view[1, head]) for view in views]
    delta = sum(
        jnp.sum(part.astype(f32) * slope, axis=1, keepdims=True)
        for part, slope in zip(parts, grad_probs)
    )
    query_grad = None
    for k, view in enumerate(views):
        slopes = (parts[k].astype(f32) * (grad_probs[k] - delta)).astype(bf16)
        term = plain(slopes, view[0, head])
        query_grad = term if query_grad is None else query_grad + term
        side = keep if k < half else send
        side[k % half, 0, head] = (dot(slopes, here, ((0,), (0,))) * scale).astype(bf16)
        side[k % half, 1, head] = dot(parts[k].astype(bf16), grad, ((0,), (0,))).astype(bf16)
    return query_grad * scale


def attend_both(
    order, flags, rows_in, packed, queries, pairs, positions, key_positions, tables, scale
):
    heads, rows, head_dim = queries.shape
    width = rows_in.shape[1]
    spans = len(packed)
    across, depth = heads * head_dim, width // spans
    half = spans // 2

    def kernel(flag_ref, rows_ref, *refs):
        packed_refs, refs = refs[:spans], refs[spans:]
        query_ref, refs = refs[0], refs[1:]
        views, refs = spread(refs[: len(pairs)]), refs[len(pairs) :]
        row_ref, key_ref, table_ref, attended, turned_back, keep, send, held, sems = refs
        started = copies(
            [w.at[:across, 3 * across : 3 * across + depth] for w in packed_refs],
            [held.at[:, k * depth : (k + 1) * depth] for k in range(spans)],
            [sems.at[k] for k in range(spans)],
        )
        all_parts = []
        for h in range(heads):
            parts = attention(query_ref[h], views, h, row_ref, key_ref, scale)
            summed = None
            for k in range(spans):
                term = plain(parts[k].astype(bf16), views[k][1, h])
                summed = term if summed is None else summed + term
            attended[:, h * head_dim : (h + 1) * head_dim] = summed.astype(bf16)
            all_parts.append(parts)
        for copy in started:
            copy.wait()
        grads = turned(rows_ref[...], held[...]).astype(bf16)
        for h in range(heads):
            made = attention_grads(
                grads[:, h * head_dim : (h + 1) * head_dim],
                query_ref[h],
                all_parts[h],
                views,
                h,
                keep,
                send,
                scale,
            )
            turned_back[h] = turn(made, table_ref, -1).astype(bf16)

    ins = [(rows_in, whole(rows_in))] + [(w, kept_out) for w in packed]
    ins += [
        (array, whole(array)) for array in (queries, *pairs, positions, key_positions, tables)
    ]
    outs = [full_out((rows, across)), full_out((heads, rows, head_dim))]
    outs += [full_out((half, 2, heads, rows, head_dim))] * 2
    scratch = [pltpu.VMEM((across, width), bf16), pltpu.SemaphoreType.DMA((spans,))]
    work = spans * rows * rows * 4 * (heads + 4) / mebibyte
    return run(order, flags, kernel, ins, outs, scratch, "attend_both", work=work)


def hidden_both(order, flags, second, pieces, at_piece, expand, contract, normal, gains):
    rows, width = second.shape
    hidden, depth = contract[0].shape
    spans = len(contract)
    tile = min(512, hidden)
    tiles = hidden // tile

    def kernel(flag_ref, second_ref, *refs):
        piece_refs, refs = refs[: len(pieces)], refs[len(pieces) :]
        expand_refs, refs = refs[:spans], refs[spans:]
        contract_refs, refs = refs[:spans], refs[spans:]
        normal_ref, gain_ref, rows_out, active, grads, part, side, *refs = refs
        held_up, held_down, sems_up, sems_down = refs
        started = []
        for t in range(tiles):
            block = slice(t * tile, (t + 1) * tile)
            places = [slice(k * depth, (k + 1) * depth) for k in range(spans)]
            up = copies(
                [w.at[:, block] for w in expand_refs],
                [held_up.at[place, block] for place in places],
                [sems_up.at[t, k] for k in range(spans)],
            )
            down = copies(
                [w.at[block, :] for w in contract_refs],
                [held_down.at[block, place] for place in places],
                [sems_down.at[t, k] for k in range(spans)],
            )
            started.append((up, down))
        start = 0
        for piece_ref in piece_refs:
            size = piece_ref.shape[1]
            rows_out[start : start + size, :] = piece_ref[0]
            start += size
        for t in range(tiles):
            block = slice(t * tile, (t + 1) * tile)
            for copy in started[t][0] + started[t][1]:
                copy.wait()
            pre = plain(second_ref[...], held_up[:, block])
            risen = 0.5 * (1.0 + lax.erf(pre * half_root))
            active[:, block] = (pre * risen).astype(bf16)
            slope = risen + pre * jnp.exp(-0.5 * pre * pre) * bell
            grads[:, block] = (turned(rows_out[...], held_down[block, :]) * slope).astype(bf16)
        for k in range(spans):
            place = slice(k * depth, (k + 1) * depth)
            made = turned(grads[...], held_up[place, :])
            side[0:1, place] = jnp.sum(
                made * normal_ref[:, place].astype(f32), axis=0, keepdims=True
            )
            side[1:2, place] = jnp.sum(made, axis=0, keepdims=True)
            part[:, place] = made * gain_ref[1:2, place]

    ins = [(second, whole(second))]
    ins += [(piece, at((1,) + piece.shape[1:], (at_piece, 0, 0))) for piece in pieces]
    ins += [(w, kept_out) for w in expand] + [(w, kept_out) for w in contract]
    ins += [(normal, whole(normal)), (gains, whole(gains))]
    outs = [
        full_out((rows, width)),
        full_out((rows, hidden)),
        full_out((rows, hidden)),
        full_out((rows, width), f32),
        full_out((2, width), f32),
    ]
    scratch = [
        pltpu.VMEM((width, hidden), bf16),
        pltpu.VMEM((hidden, width), bf16),
        pltpu.SemaphoreType.DMA((tiles, spans)),
        pltpu.SemaphoreType.DMA((tiles, spans)),
    ]
    return run(order, flags, kernel, ins, outs, scratch, "hidden_both")


def branch_out(order, flags, groups, contract, packed):
    hidden, depth = contract[0].shape
    across = groups[0][1].shape[1]
    spans = len(contract)
    width = depth * spans
    span_rows = groups[0][0].shape[0]
    block = span_rows // 2
    count = len(groups)

    def kernel(flag_ref, *refs):
        group_refs, refs = refs[: 2 * count], refs[2 * count :]
        contract_refs, packed_refs = refs[:spans], refs[spans : 2 * spans]
        blocks, refs = refs[2 * spans : 2 * (spans + count)], refs[2 * (spans + count) :]
        held, held_out, sems = refs
        outputs = [w.at[:across, 3 * across : 3 * across + depth] for w in packed_refs]
        started = copies(
            [ref for k in range(spans) for ref in (outputs[k], contract_refs[k])],
            [ref for k in range(spans) for ref in (held_out.at[k], held.at[k])],
            [sems.at[j] for j in range(2 * spans)],
        )
        for k in range(spans):
            started[2 * k].wait()
            started[2 * k + 1].wait()
            columns = slice(k * depth, (k + 1) * depth)
            for c in range(count):
                made = plain(group_refs[2 * c + 1][...], held_out[k])
                made = made + plain(group_refs[2 * c][...], held[k])
                blocks[2 * c][:, columns] = made[:block].astype(bf16)
                blocks[2 * c + 1][:, columns] = made[block:].astype(bf16)

    ins = []
    for active, attended in groups:
        ins += [(active, whole(active)), (attended, whole(attended))]
    ins += [(w, kept_out) for w in contract] + [(w, kept_out) for w in packed]
    outs = [full_out((block, width))] * (2 * count)
    scratch = [
        pltpu.VMEM((spans, hidden, depth), bf16),
        pltpu.VMEM((spans, across, depth), bf16),
        pltpu.SemaphoreType.DMA((2 * spans,)),
    ]
    return run(order, flags, kernel, ins, outs, scratch, "branch")


def attend_back(order, flags, pieces, packed, queries, pairs, probs, tables, scale):
    rows = sum(piece.shape[1] for piece in pieces)
    width = pieces[0].shape[2]
    heads, _, head_dim = queries.shape
    spans = len(packed)
    across, depth = heads * head_dim, width // spans
    half = spans // 2

    def kernel(flag_ref, *refs):
        piece_refs, refs = refs[: len(pieces)], refs[len(pieces) :]
        packed_refs, refs = refs[:spans], refs[spans:]
        query_ref, refs = refs[0], refs[1:]
        views, refs = spread(refs[: len(pairs)]), refs[len(pairs) :]
        prob_ref, table_ref, rows_out, turned_back, keep, send, held, sems = refs
        started = copies(
            [w.at[:across, 3 * across : 3 * across + depth] for w in packed_refs],
            [held.at[:, k * depth : (k + 1) * depth] for k in range(spans)],
            [sems.at[k] for k in range(spans)],
        )
        start = 0
        for piece_ref in piece_refs:
            size = piece_ref.shape[1]
            rows_out[start : start + size, :] = piece_ref[0]
            start += size
        for copy in started:
            copy.wait()
        grads = turned(rows_out[...], held[...]).astype(bf16)
        for h in range(heads):
            made = attention_grads(
                grads[:, h * head_dim : (h + 1) * head_dim],
                query_ref[h],
                [prob_ref[k, h] for k in range(spans)],
                views,
                h,
                keep,
                send,
                scale,
            )
            turned_back[h] = turn(made, table_ref, -1).astype(bf16)

    ins = [(piece, whole(piece)) for piece in pieces] + [(w, kept_out) for w in packed]
    ins += [(array, whole(array)) for array in (queries, *pairs, probs, tables)]
    outs = [full_out((rows, width)), full_out((heads, rows, head_dim))]
    outs += [full_out((half, 2, heads, rows, head_dim))] * 2
    scratch = [pltpu.VMEM((across, width), bf16), pltpu.SemaphoreType.DMA((spans,))]
    work = spans * rows * rows * 4 * 4 / mebibyte
    return run(order, flags, kernel, ins, outs, scratch, "attend_back", work=work)


def hidden_back(order, flags, upstream, contract, expand, slope, normal, gains):
    span_rows, width = upstream.shape
    hidden, depth = contract[0].shape
    spans = len(contract)
    tile = min(512, hidden)
    tiles = hidden // tile

    def kernel(flag_ref, *refs):
        upstream_ref, refs = refs[0], refs[1:]
        contract_refs, refs = refs[:spans], refs[spans:]
        expand_refs, refs = refs[:spans], refs[spans:]
        slope_ref, normal_ref, gain_ref, grads, part, side, held, held_up, sems, sems_up = refs
        started = [
            copies(
                [w.at[t * tile : (t + 1) * tile, :] for w in contract_refs],
                [held.at[t, :, k * depth : (k + 1) * depth] for k in range(spans)],
                [sems.at[t, k] for k in range(spans)],
            )
            for t in range(tiles)
        ]
        started_up = copies(
            expand_refs, [held_up.at[k] for k in range(spans)], [sems_up.at[k] for k in range(spans)]
        )
        for t in range(tiles):
            for copy in started[t]:
                copy.wait()
            columns = slice(t * tile, (t + 1) * tile)
            grads[:, columns] = (
                turned(upstream_ref[...], held[t]) * slope_ref[:, columns].astype(f32)
            ).astype(bf16)
        for k in range(spans):
            started_up[k].wait()
            made = turned(grads[...], held_up[k])
            columns = slice(k * depth, (k + 1) * depth)
            side[0:1, columns] = jnp.sum(
                made * normal_ref[:, columns].astype(f32), axis=0, keepdims=True
            )
            side[1:2, columns] = jnp.sum(made, axis=0, keepdims=True)
            part[:, columns] = made * gain_ref[1:2, columns]

    ins = [(upstream, whole(upstream))]
    ins += [(w, kept_out) for w in contract] + [(w, kept_out) for w in expand]
    ins += [
        (slope, whole(slope)),
        (normal, whole(normal)),
        (gains, whole(gains)),
    ]
    outs = [
        full_out((span_rows, hidden)),
        full_out((span_rows, width), f32),
        full_out((2, width), f32),
    ]
    scratch = [
        pltpu.VMEM((tiles, tile, width), bf16),
        pltpu.VMEM((spans, depth, hidden), bf16),
        pltpu.SemaphoreType.DMA((tiles, spans)),
        pltpu.SemaphoreType.DMA((spans,)),
    ]
    return run(order, flags, kernel, ins, outs, scratch, "hidden_back")


def project_back(
    order, flags, turned_back, own, came, weights, part, normal, gains, tables
):
    heads, span_rows, head_dim = turned_back.shape
    spans = len(weights)
    width = part.shape[1]
    depth, columns = width // spans, 3 * heads * head_dim
    block = span_rows // 2

    def kernel(flag_ref, *refs):
        query_ref, own_ref, came_ref, refs = refs[0], refs[1], refs[2], refs[3:]
        weight_refs, refs = refs[:spans], refs[spans:]
        part_ref, normal_ref, gain_ref, table_ref, grads, side, *refs = refs
        low, high, held, sems = refs
        started = copies(
            [w.at[:depth, :columns] for w in weight_refs],
            [held.at[k] for k in range(spans)],
            [sems.at[k] for k in range(spans)],
        )
        for h in range(heads):
            at_column = h * 3 * head_dim
            keys = own_ref[0, h].astype(f32) + came_ref[0, h].astype(f32)
            values = own_ref[1, h].astype(f32) + came_ref[1, h].astype(f32)
            grads[:, at_column : at_column + head_dim] = query_ref[h]
            grads[:, at_column + head_dim : at_column + 2 * head_dim] = turn(
                keys, table_ref, -1
            ).astype(bf16)
            grads[:, at_column + 2 * head_dim : at_column + 3 * head_dim] = values.astype(bf16)
        for k in range(spans):
            started[k].wait()
            made = turned(grads[...], held[k])
            span_columns = slice(k * depth, (k + 1) * depth)
            side[0:1, span_columns] = jnp.sum(
                made * normal_ref[:, span_columns].astype(f32), axis=0, keepdims=True
            )
            side[1:2, span_columns] = jnp.sum(made, axis=0, keepdims=True)
            both = (made * gain_ref[0:1, span_columns] + part_ref[:, span_columns]).astype(bf16)
            low[:, span_columns] = both[:block]
            high[:, span_columns] = both[block:]

    ins = [(array, whole(array)) for array in (turned_back, own, came)]
    ins += [(w, kept_out) for w in weights]
    ins += [(part, whole(part)), (normal, whole(normal))]
    ins += [(gains, whole(gains)), (tables, whole(tables))]
    outs = [full_out((span_rows, columns)), full_out((2, width), f32)]
    outs += [full_out((block, width))] * 2
    scratch = [pltpu.VMEM((spans, depth, columns), bf16), pltpu.SemaphoreType.DMA((spans,))]
    return run(order, flags, kernel, ins, outs, scratch, "project_back")


def weight_sums(order, flags, lefts, rights, by_rows, spans):
    rows = sum(piece.shape[0] for piece in lefts[0][0])
    left_width = sum(group[0].shape[1] for group in lefts[0])
    right_width = sum(group[0].shape[1] for group in rights[0])
    if by_rows:
        tile = left_width // spans
        steps, block = spans // 2, (tile, right_width)
    else:
        tile = min(512, left_width)
        while left_width % tile:
            tile //= 2
        steps, block = left_width // tile, (tile, right_width // 2)
    chunk = min(1024, block[1])
    while right_width % chunk:
        chunk //= 2
    pieces = [
        [piece for groups in (lefts[s], rights[s]) for group in groups for piece in group]
        for s in (0, 1)
    ]
    most = max(len(p) for p in pieces)

    def kernel(flag_ref, *refs):
        piece_refs = (refs[: len(pieces[0])], refs[len(pieces[0]) : len(pieces[0]) + len(pieces[1])])
        keep, send, left, right, flipped, sems = refs[len(pieces[0]) + len(pieces[1]) :]
        g = pl.program_id(0)
        for s in (0, 1):

            @pl.when((g == 0) & (flag_ref[2] == s))
            def _(s=s):
                targets = []
                for held, groups in ((left, lefts[s]), (right, rights[s])):
                    column = 0
                    for group in groups:
                        row, wide = 0, group[0].shape[1]
                        for piece in group:
                            targets.append(
                                held.at[row : row + piece.shape[0], column : column + wide]
                            )
                            row += piece.shape[0]
                        column += wide
                started = copies(
                    piece_refs[s], targets, [sems.at[j] for j in range(len(targets))]
                )
                for copy in started:
                    copy.wait()

        def product(column, store):
            flipped[...] = left[:, pl.ds(pl.multiple_of(column, LANES), tile)].T

            def one(c, _):
                columns = pl.ds(pl.multiple_of(c * chunk, chunk), chunk)
                store(c, plain(flipped[...], right[:, columns]).astype(bf16))
                return 0

            lax.fori_loop(0, right_width // chunk, one, 0)

        if by_rows:

            def to(target):
                def store(c, made):
                    target[:, pl.ds(pl.multiple_of(c * chunk, chunk), chunk)] = made

                return store

            product(g * tile, to(keep))
            product((g + steps) * tile, to(send))
        else:
            half = right_width // 2 // chunk

            def store(c, made):
                @pl.when(c < half)
                def _():
                    keep[:, pl.ds(pl.multiple_of(c * chunk, chunk), chunk)] = made

                @pl.when(c >= half)
                def _():
                    send[:, pl.ds(pl.multiple_of((c - half) * chunk, chunk), chunk)] = made

            product(g * tile, store)

    ins = [(piece, kept_out) for s in (0, 1) for piece in pieces[s]]
    dims = (steps * tile, block[1])
    outs = [(shape(dims), pl.BlockSpec(block, lambda g: (g, 0)))] * 2
    scratch = [
        pltpu.VMEM((rows, left_width), bf16),
        pltpu.VMEM((rows, right_width), bf16),
        pltpu.VMEM((tile, rows), bf16),
        pltpu.SemaphoreType.DMA((most,)),
    ]
    return run(
        order, flags, kernel, ins, outs, scratch, "weight_sums", grid=(steps,)
    )


def fold(order, flags, keep, came, dim):
    rows, columns = keep.shape
    if dim == 0:
        tile = rows // 4
        steps, block = rows // 2 // tile, (tile, columns)
        places = [lambda g: (g, 0), lambda g: (g + steps, 0)]
        half = (rows // 2, columns)
    else:
        tile = rows // 4
        steps, block = rows // tile, (tile, columns // 2)
        places = [lambda g: (g, 0), lambda g: (g, 1)]
        half = (rows, columns // 2)

    def kernel(flag_ref, keep_low, keep_high, came_low, came_high, low, high):
        low[...] = (keep_low[...].astype(f32) + came_low[...].astype(f32)).astype(bf16)
        high[...] = (keep_high[...].astype(f32) + came_high[...].astype(f32)).astype(bf16)

    ins = [(array, pl.BlockSpec(block, place)) for array in (keep, came) for place in places]
    outs = [(shape(half), pl.BlockSpec(block, lambda g: (g, 0)))] * 2
    return run(order, flags, kernel, ins, outs, [], "fold", grid=(steps,))


def shards(
    block_input,
    out_grad,
    triple_weight,
    output_weight,
    expand_weight,
    contract_weight,
    norm_gains,
    norm_biases,
):
    section = lax.axis_index("pipe")
    span = lax.axis_index("ctx")
    lane = lax.axis_index("tp")
    spans = lax.axis_size("ctx")
    lanes = lax.axis_size("tp")
    micros, rows, width = block_input.shape
    span_rows = rows * lanes
    heads = triple_weight.shape[2]
    head_dim = triple_weight.shape[4]
    across_units = heads * head_dim
    scale = head_dim ** (-0.5)
    first_section = section == 0
    both = (0, 1)

    def hop(array, axis, step, sections):
        size = lax.axis_size(axis)
        pairs = [(s * size + a, s * size + (a ^ step)) for s in sections for a in range(size)]
        return lax.ppermute(array, ("pipe", axis), pairs)

    order = Order()

    def flags_for(wanted):
        return jnp.stack([jnp.asarray(wanted), span, section]).astype(jnp.int32)

    flags = [flags_for(section == s) for s in both]
    always = flags_for(1)

    kept = [[SimpleNamespace() for _ in range(micros)] for _ in both]
    due = {}
    slot_index = [0]

    def slot(hops, kernels=()):
        now = slot_index[0]
        slot_index[0] += 1
        ready = due.pop(now, [])
        hops = [h if len(h) == 3 else h + (1,) for h in hops]
        if hops:
            gated = fence([operand for operand, _, _ in hops], order.last + ready)
            order.last = [min(gated, key=lambda array: array.size)]
            for passed, (_, go, slots) in zip(gated, hops):
                results = go(passed)
                results = results if isinstance(results, list) else [results]
                due.setdefault(now + slots, []).extend(results)
        else:
            order.last = order.last + ready
        for kernel in kernels:
            kernel()

    def halved(keep, came, dim):
        middle = keep.shape[dim] // 2
        total = keep.astype(f32) + came.astype(f32)
        return (
            lax.slice_in_dim(total, 0, middle, axis=dim).astype(bf16),
            lax.slice_in_dim(total, middle, 2 * middle, axis=dim).astype(bf16),
        )

    def spread_hops(pieces, axis, axis_name, sections, first):
        step = lax.axis_size(axis_name) // 4
        going = first
        while step:
            pieces.append(hop(going, axis_name, step, sections))
            going = jnp.concatenate(pieces, axis=axis)
            step //= 2
        return pieces[-1]

    def fold_hops(k, first, axis_name, dim, sections):
        step, size = 1, lax.axis_size(axis_name)
        while 2 * step < size:
            came = hop(first, axis_name, step, sections)
            k.keep, k.send = halved(k.keep, came, dim)
            first = k.send
            step *= 2
        return came

    depth = width // spans
    far = spans // 2
    assert depth == across_units
    small = jnp.concatenate([norm_gains[0], norm_biases[0]], axis=0)
    packed = jnp.concatenate(
        [triple_weight[0].reshape(depth, -1), output_weight[0].reshape(-1, depth)],
        axis=1,
    )
    packed = jnp.pad(packed, ((0, 16), (0, 0)))
    packed = lax.dynamic_update_slice(packed, small, (depth, 0))
    own_expand, own_contract = expand_weight[0], contract_weight[0]
    hidden = own_expand.shape[1]
    inputs = xor_blocks(block_input, span, spans)
    cotangent = xor_blocks(out_grad, span, spans)
    early = jnp.where(first_section, inputs, cotangent)

    in_row = jnp.arange(rows, dtype=jnp.int32)
    in_span = jnp.concatenate([(lane ^ j) * rows + in_row for j in doubling(lanes)])
    positions = span * span_rows + in_span
    key_positions = jnp.stack([(span ^ k) * span_rows + in_span for k in doubling(spans)])
    tables = rope_tables(positions)
    position_column = positions[:, None]
    key_positions = key_positions[:, None, :]

    def blocks_of(own, came):
        held, step = {0: own, far: came}, far // 2
        while step:
            for k in list(held):
                held[k ^ step] = hop(held[k], "ctx", step, both)
            step //= 2
        return [held[k] for k in doubling(spans)]

    lane_offsets = doubling(lanes)

    def across(array, j, source):
        pairs = [(source * lanes + a, (1 - source) * lanes + (a ^ j)) for a in range(lanes)]
        return lax.ppermute(array, ("pipe", "tp"), pairs)

    def rows_far(s, m):
        k = kept[s][m]

        def go(passed):
            k.rows = passed
            k.pieces = [passed, hop(passed, "tp", lanes // 2, (s,))]
            return k.pieces[1]

        return k.rows, go

    def rows_near(s, m):
        k = kept[s][m]

        def go(passed):
            last_piece = spread_hops(k.pieces, 0, "tp", (s,), passed)
            k.row_pieces = [piece[None] for piece in k.pieces]
            return last_piece

        return jnp.concatenate(k.pieces, axis=0), go

    def pair_far(s, m):
        k = kept[s][m]

        def go(passed):
            k.pairs = [passed, hop(passed, "ctx", far, (s,))]
            return k.pairs[1]

        return k.pair, go

    def pair_near(s, m):
        k = kept[s][m]

        def go(passed):
            return spread_hops(k.pairs, 0, "ctx", (s,), passed)

        return jnp.concatenate(k.pairs, axis=0), go

    def pair_grad_near(s, m):
        k = kept[s][m].pair_grad
        return k.send, lambda passed: fold_hops(k, passed, "ctx", 0, (s,))

    def pair_grad_far(s, m):
        k = kept[s][m].pair_grad

        def go(passed):
            k.came = hop(passed, "ctx", far, (s,))
            return k.came

        return k.send, go

    def sum_near(s, k):
        k.keep, going = k.blocks
        return going, lambda passed: fold_hops(k, passed, "tp", 0, (s,))

    def sum_far(s, k):
        def go(passed):
            k.blocks, k.arrived = [k.keep], [hop(passed, "tp", lanes // 2, (s,))]
            return k.arrived[0]

        return k.send, go

    def total_of(k):
        return sum(array.astype(f32) for array in [k.blocks[0], *k.arrived])

    def norm_back(upstream, combined, entering):
        normalized, inverse = normalize(entering.astype(f32))
        return (
            upstream.astype(f32)
            + inverse
            * (
                combined
                - jnp.mean(combined, axis=-1, keepdims=True)
                - normalized * jnp.mean(combined * normalized, axis=-1, keepdims=True)
            )
        ).astype(bf16)

    def middle_of(m):
        return (inputs[m].astype(f32) + total_of(kept[0][m])).astype(bf16)

    def entry_of(m):
        k = kept[1][m]
        return norm_back(cotangent[m], total_of(k), k.rows)

    def hand_one(s, m):
        k, other = kept[s][m], kept[1 - s][m]
        k.given = middle_of(m) if s == 0 else entry_of(m)

        def go(passed):
            k.given = passed
            other.rows = across(passed, 0, s)
            return other.rows

        return k.given, go

    def run_project(s, m):
        k = kept[s][m]
        pieces, place = (early_pieces, m) if s == 0 else (k.row_pieces, 0)
        k.first, k.second, k.normal, k.queries, pair = project(
            order, flags[s], pieces, place, gains, biases, tables, packed, heads, head_dim
        )
        k.pair = pair[None]

    def run_expand(m):
        k = kept[0][m]
        k.active, k.slope = expand_up(order, flags[0], k.second, weights.expand, span_rows)

    def run_attend(m):
        k = kept[0][m]
        k.attended, k.probs = attend(
            order, flags[0], k.queries, k.pairs, position_column, key_positions, scale
        )

    def run_branch(m):
        k = kept[0][m]
        k.blocks = branch_out(
            order, flags[0], [(k.active, k.attended)], contract, packed
        )

    def run_hidden_both(m):
        k = kept[1][m]
        k.upstream, k.active, k.hidden, k.part, k.side_second = hidden_both(
            order,
            flags[1],
            k.second,
            early_pieces,
            m,
            weights.expand,
            contract,
            k.normal,
            gains,
        )

    def run_attend_both(m):
        k = kept[1][m]
        k.attended, k.turned_back, keep, send = attend_both(
            order,
            flags[1],
            k.upstream,
            packed,
            k.queries,
            k.pairs,
            position_column,
            key_positions,
            tables,
            scale,
        )
        k.pair_grad = SimpleNamespace(keep=keep, send=send)

    def run_attend_back(m):
        k = kept[0][m]
        k.upstream, k.turned_back, keep, send = attend_back(
            order,
            flags[0],
            k.row_pieces,
            packed,
            k.queries,
            k.pairs,
            k.probs,
            tables,
            scale,
        )
        k.pair_grad = SimpleNamespace(keep=keep, send=send)

    def run_hidden_back(m):
        k = kept[0][m]
        k.hidden, k.part, k.side_second = hidden_back(
            order,
            flags[0],
            k.upstream,
            contract,
            weights.expand,
            k.slope,
            k.normal,
            gains,
        )

    def run_project_back(s, m):
        k = kept[s][m]
        own, arrived = k.pair_grad.keep, k.pair_grad.came
        k.stacked, k.side_first, *k.blocks = project_back(
            order,
            flags[s],
            k.turned_back,
            own.reshape(own.shape[1:]),
            arrived.reshape(arrived.shape[1:]),
            packed,
            k.part,
            k.normal,
            gains,
            tables,
        )

    def of(name, s, count=micros):
        return [getattr(kept[s][m], name) for m in range(count)]

    branch_sums, expand_sums, triple_sums = (SimpleNamespace(parts=[]) for _ in range(3))

    def run_sums(w, lefts, rights, by_rows):
        w.dim = 0 if by_rows else 1
        w.keep, w.send = weight_sums(order, always, lefts, rights, by_rows, spans)

    def wide_near(w):
        def go(passed):
            w.came = hop(passed, "ctx", 1, both)
            return w.came

        return w.send, go

    def run_fold(w):
        step = 2
        w.keep, w.send = fold(order, always, w.keep, w.came, w.dim)
        while 2 * step < spans:
            w.came = hop(w.send, "ctx", step, both)
            w.keep, w.send = fold(order, always, w.keep, w.came, w.dim)
            step *= 2

    def wide_far(w, start, stop):
        def go(passed):
            w.parts.append(hop(passed, "ctx", far, both))
            return w.parts[-1]

        return w.send[start:stop], go

    weights = SimpleNamespace(contract_came=[])
    half_depth = depth // 2
    contract_cut = 9 * hidden // 16

    def expand_far(passed):
        weights.expand_came = hop(passed, "ctx", far, both)
        return weights.expand_came

    def packed_far(passed):
        weights.packed_came = hop(passed, "ctx", far, both)
        return weights.packed_came

    def packed_near(passed):
        weights.packed = blocks_of(packed, passed)
        return weights.packed[1:]

    def expand_near(passed):
        weights.expand = blocks_of(own_expand, passed)
        return weights.expand[1:]

    def contract_far(start, stop):
        def go(passed):
            weights.contract_came.append(hop(passed, "ctx", far, both))
            return weights.contract_came[-1]

        return own_contract[start:stop], go

    def contract_near(passed):
        weights.contract = blocks_of(own_contract, passed)
        return weights.contract[1:]

    def early_hops(passed):
        weights.early = [passed] + [hop(passed, "tp", j, both) for j in lane_offsets[1:]]
        return weights.early[1:]

    slot([(packed, packed_far), (own_expand, expand_far), (early, early_hops)])
    early_pieces = weights.early
    slot([(weights.packed_came, packed_near), (weights.expand_came, expand_near)])
    packed = weights.packed
    small_full = jnp.concatenate(
        [piece[depth : depth + 4, :depth] for piece in packed], axis=1
    ).astype(f32)
    gains, biases = small_full[:2], small_full[2:]
    slot(
        [contract_far(0, contract_cut)],
        [lambda m=m: run_project(0, m) for m in range(micros)],
    )
    a, b = kept
    slot(
        [pair_far(0, 0), contract_far(contract_cut, hidden)],
        [lambda m=m: run_expand(m) for m in range(micros)],
    )
    contract_came = jnp.concatenate(weights.contract_came, axis=0)
    slot([(contract_came, contract_near), pair_near(0, 0)])
    contract = weights.contract
    slot([pair_far(0, 1)], [lambda: run_attend(0), lambda: run_branch(0)])
    slot([sum_near(0, a[0]), pair_near(0, 1), pair_far(0, 2)])
    slot(
        [sum_far(0, a[0]), pair_near(0, 2)], [lambda: run_attend(1), lambda: run_branch(1)]
    )
    slot(
        [hand_one(0, 0), sum_near(0, a[1])], [lambda: run_attend(2), lambda: run_branch(2)]
    )
    slot([rows_far(1, 0), sum_far(0, a[1])])
    slot([rows_near(1, 0), hand_one(0, 1), sum_near(0, a[2])])
    slot([rows_far(1, 1), sum_far(0, a[2])], [lambda: run_project(1, 0)])
    slot(
        [pair_far(1, 0), rows_near(1, 1), hand_one(0, 2)], [lambda: run_hidden_both(0)]
    )
    slot([pair_near(1, 0), rows_far(1, 2)], [lambda: run_project(1, 1)])
    slot(
        [pair_far(1, 1), rows_near(1, 2)],
        [lambda: run_attend_both(0), lambda: run_hidden_both(1)],
    )
    slot([pair_grad_near(1, 0), pair_near(1, 1)], [lambda: run_project(1, 2)])
    slot(
        [pair_grad_far(1, 0), pair_far(1, 2)],
        [lambda: run_attend_both(1), lambda: run_hidden_both(2)],
    )
    slot([pair_grad_near(1, 1), pair_near(1, 2)], [lambda: run_project_back(1, 0)])
    slot([sum_near(1, b[0]), pair_grad_far(1, 1)], [lambda: run_attend_both(2)])
    slot([sum_far(1, b[0]), pair_grad_near(1, 2)], [lambda: run_project_back(1, 1)])
    slot([hand_one(1, 0), sum_near(1, b[1]), pair_grad_far(1, 2)])
    slot([sum_far(1, b[1]), rows_far(0, 0)], [lambda: run_project_back(1, 2)])
    slot([sum_near(1, b[2]), hand_one(1, 1), rows_near(0, 0)])
    slot([sum_far(1, b[2]), rows_far(0, 1)], [lambda: run_attend_back(0)])
    slot(
        [hand_one(1, 2), rows_near(0, 1), pair_grad_near(0, 0)],
        [lambda: run_hidden_back(0)],
    )
    slot([rows_far(0, 2), pair_grad_far(0, 0)], [lambda: run_attend_back(1)])
    slot([rows_near(0, 2), pair_grad_near(0, 1)], [lambda: run_hidden_back(1)])
    last = micros - 1

    def run_branch_sums():
        run_sums(
            branch_sums,
            [[of("active", s), of("attended", s)] for s in both],
            [
                [of("upstream", 0, last) + [piece[0] for piece in a[last].row_pieces]],
                [of("upstream", 1)],
            ],
            False,
        )

    def run_expand_sums():
        run_sums(
            expand_sums,
            [[of("second", s)] for s in both],
            [[of("hidden", s)] for s in both],
            True,
        )

    def run_triple_sums():
        run_sums(
            triple_sums,
            [[of("first", s)] for s in both],
            [[of("stacked", s)] for s in both],
            True,
        )

    finals = SimpleNamespace()

    def run_final_branch():
        blocks = branch_out(
            order, flags[1], [(k.active, k.attended) for k in b], contract, packed
        )
        finals.keep = jnp.stack(blocks[0::2])
        finals.send = jnp.stack(blocks[1::2])

    def finals_near():
        return finals.send, lambda passed: fold_hops(finals, passed, "tp", 1, (1,))

    def finals_far():
        def go(passed):
            finals.came = hop(passed, "tp", lanes // 2, (1,))
            return finals.came

        return finals.send, go

    slot([pair_grad_far(0, 1)], [run_branch_sums])
    slot(
        [wide_near(branch_sums)], [lambda: run_attend_back(2), lambda: run_project_back(0, 0)]
    )
    slot([pair_grad_near(0, 2), sum_near(0, a[0])], [lambda: run_fold(branch_sums)])
    cut = [0, hidden // 4, 3 * hidden // 4, hidden + across_units]
    slot(
        [pair_grad_far(0, 2), wide_far(branch_sums, cut[0], cut[1]), sum_far(0, a[0])],
        [lambda: run_hidden_back(2), lambda: run_project_back(0, 1)],
    )
    slot(
        [wide_far(branch_sums, cut[1], cut[2]), sum_near(0, a[1])],
        [lambda: run_project_back(0, 2), run_triple_sums],
    )

    def side_of(mades):
        return sum(
            jnp.concatenate([k.side_first, k.side_second], axis=0) for k in mades
        )

    side = SimpleNamespace(all=jnp.where(first_section, side_of(a), side_of(b)))

    def side_ctx(passed):
        step = 1
        while step < spans:
            middle = passed.shape[1] // 2
            came = hop(passed[:, middle:], "ctx", step, both)
            passed = passed[:, :middle] + came
            step *= 2
        side.all = passed
        return came

    def side_tp(passed):
        step = 1
        while step < lanes:
            came = hop(passed, "tp", step, both)
            passed = passed + came
            step *= 2
        side.all = passed
        return came

    slot([wide_near(triple_sums), (side.all, side_ctx), sum_near(0, a[2])])
    slot([], [lambda: run_fold(triple_sums)])
    slot([wide_far(triple_sums, 0, half_depth), sum_far(0, a[1])], [run_expand_sums])
    slot([wide_near(expand_sums), wide_far(triple_sums, half_depth, depth), sum_far(0, a[2])])
    slot([wide_far(branch_sums, cut[2], cut[3])], [lambda: run_fold(expand_sums)])
    slot([wide_far(expand_sums, 0, half_depth), (side.all, side_tp)], [run_final_branch])
    slot([wide_far(expand_sums, half_depth, depth), finals_near()])
    slot([finals_far()])

    def wide_total(keep, parts):
        came = jnp.concatenate(parts, axis=0) if len(parts) > 1 else parts[0]
        return keep.astype(f32) + came.astype(f32)

    branch_grads = wide_total(branch_sums.keep, branch_sums.parts)
    contract_grads, output_grads = branch_grads[:hidden], branch_grads[hidden:]
    expand_grads = wide_total(expand_sums.keep, expand_sums.parts)
    triple_grads = wide_total(triple_sums.keep, triple_sums.parts)
    layer_outputs = jnp.stack(
        [
            jnp.where(
                first_section,
                kept[0][m].given,
                (
                    b[m].rows.astype(f32)
                    + finals.keep[m].astype(f32)
                    + finals.came[m].astype(f32)
                ).astype(bf16),
            )
            for m in range(micros)
        ]
    )
    entry_grads = jnp.stack(
        [
            jnp.where(
                first_section,
                norm_back(kept[0][m].rows, total_of(kept[0][m]), inputs[m]),
                kept[1][m].given,
            )
            for m in range(micros)
        ]
    )
    gain_grads = jnp.stack([side.all[0], side.all[2]])
    bias_grads = jnp.stack([side.all[1], side.all[3]])
    return (
        xor_blocks(layer_outputs, span, spans, inverse=True)[None],
        xor_blocks(entry_grads, span, spans, inverse=True)[None],
        triple_grads.reshape(triple_weight.shape),
        output_grads.reshape(output_weight.shape),
        expand_grads[None],
        contract_grads[None],
        gain_grads[None],
        bias_grads[None],
    )


def solution(mesh):
    return jax.shard_map(
        shards,
        mesh=mesh,
        in_specs=(
            P(None, ("ctx", "tp"), None),
            P(None, ("ctx", "tp"), None),
            P("pipe", "ctx", "tp", None, None),
            P("pipe", "tp", None, "ctx"),
            P("pipe", "ctx", "tp"),
            P("pipe", "tp", "ctx"),
            P("pipe", None, "ctx"),
            P("pipe", None, "ctx"),
        ),
        out_specs=(
            P("pipe", None, ("ctx", "tp"), None),
            P("pipe", None, ("ctx", "tp"), None),
            P("pipe", "ctx", "tp", None, None),
            P("pipe", "tp", None, "ctx"),
            P("pipe", "ctx", "tp"),
            P("pipe", "tp", "ctx"),
            P("pipe", None, "ctx"),
            P("pipe", None, "ctx"),
        ),
        check_vma=False,
    )
```

```python
import functools
import math
from types import SimpleNamespace

import jax
import jax.numpy as jnp
from jax import lax
from jax.experimental import pallas as pl
from jax.experimental.pallas import tpu as pltpu
from jax.sharding import PartitionSpec as P

ROT = 64
LANES = 128
epsilon = 1e-05
masked_score = -1e30
f32 = jnp.float32
bf16 = jnp.bfloat16
mebibyte = 1024 * 1024
half_root = 0.7071067811865476
bell = 0.3989422804014327


def dot(a, b, dims):
    return lax.dot_general(a, b, (dims, ((), ())), preferred_element_type=f32)


def plain(a, b):
    return dot(a, b, ((1,), (0,)))


def turned(a, b):
    return dot(a, b, ((1,), (1,)))


def doubling(count):
    order, step = [0], count // 2
    while step:
        order += [k ^ step for k in order]
        step //= 2
    return order


def xor_blocks(values, index, count, inverse=False):
    width = values.shape[-1] // count
    order = doubling(count)

    def taken(places):
        return jnp.concatenate(
            [values[..., k * width : (k + 1) * width] for k in places], axis=-1
        )

    if inverse:
        values = taken([order.index(k) for k in range(count)])
    step = 1
    while step < count:
        swapped = taken([k ^ step for k in range(count)])
        values = jnp.where((index & step) != 0, swapped, values)
        step *= 2
    return values if inverse else taken(order)


def rope_tables(positions):
    half = ROT // 2
    frequency = 10000.0 ** (-jnp.arange(0, ROT, 2, dtype=f32) / ROT)
    angles = positions.astype(f32)[:, None] * frequency[None, :]
    cosine, sine = jnp.cos(angles), jnp.sin(angles)
    count = positions.shape[0]
    rest = jnp.zeros((count, LANES - ROT), f32)
    none = jnp.zeros((count, half), f32)
    return jnp.stack(
        [
            jnp.concatenate([cosine, cosine, rest + 1.0], axis=1),
            jnp.concatenate([-sine, none, rest], axis=1),
            jnp.concatenate([none, sine, rest], axis=1),
        ]
    )


def turn(values, tables, sign):
    half = ROT // 2
    part = values[:, :LANES]
    moved = (
        pltpu.roll(part, LANES - half, 1) * tables[1] + pltpu.roll(part, half, 1) * tables[2]
    )
    part = part * tables[0] + (moved if sign > 0 else -moved)
    return jnp.concatenate([part, values[:, LANES:]], axis=1)


def normalize(values):
    center = values - jnp.mean(values, axis=-1, keepdims=True)
    inverse = lax.rsqrt(jnp.mean(center * center, axis=-1, keepdims=True) + epsilon)
    return (center * inverse, inverse)


def whole(array):
    zeros = (0,) * array.ndim
    return pl.BlockSpec(array.shape, lambda *_: zeros)


def at(block, place):
    return pl.BlockSpec(block, lambda *_: place)


kept_out = pl.BlockSpec(memory_space=pl.ANY)


def shape(dims, dtype=bf16):
    return jax.ShapeDtypeStruct(dims, dtype)


class Order:
    def __init__(self):
        self.last = []

    def follow(self, results):
        self.last = [min(results, key=lambda array: array.size * array.dtype.itemsize)]

    def also(self, array):
        self.last = self.last + [array]


took = dict(
    project=5,
    expand=6,
    attend=3,
    branch=6,
    hidden_both=11,
    attend_both=5,
    attend_back=5,
    hidden_back=9,
    project_back=5,
    weight_sums=11,
    fold=3,
    owner_sums=13,
)
peak = 1.15e9


def run(order, flags, kernel, ins, outs, scratch, name, grid=(1,), work=0, in_place={}):
    taken = len(ins)
    ins = [(flags, pl.BlockSpec(memory_space=pltpu.SMEM))] + list(ins)
    ins += [(array, kept_out) for array in order.last]
    arrays = [array for array, _ in ins]
    once = grid == (1,)

    def sized(spec, dtype):
        if spec.block_shape is None:
            return spec, 0
        size = math.prod(spec.block_shape) * jnp.dtype(dtype).itemsize
        if not once:
            return spec, 2 * size
        single = pl.BlockSpec(
            spec.block_shape, spec.index_map, pipeline_mode=pl.Buffered(1)
        )
        return single, size

    in_specs = [sized(spec, array.dtype) for array, spec in ins]
    out_specs = [sized(spec, struct.dtype) for struct, spec in outs]
    held = sum(size for _, size in in_specs + out_specs)
    for buffer in scratch:
        if buffer.memory_space == pltpu.VMEM:
            held += math.prod(buffer.shape) * jnp.dtype(buffer.dtype).itemsize

    def body(flag_ref, *refs):
        @pl.when(flag_ref[0] == 1)
        def _():
            kernel(flag_ref, *refs[:taken], *refs[len(ins) - 1 :])

    results = pl.pallas_call(
        body,
        grid=grid,
        in_specs=[spec for spec, _ in in_specs],
        out_specs=[spec for spec, _ in out_specs],
        out_shape=[struct for struct, _ in outs],
        scratch_shapes=scratch,
        input_output_aliases=in_place,
        compiler_params=pltpu.CompilerParams(
            vmem_limit_bytes=int(held + (work + 4) * mebibyte)
        ),
        cost_estimate=pl.CostEstimate(
            flops=int(took[name] * peak), bytes_accessed=0, transcendentals=0
        ),
        name=name,
    )(*arrays)
    order.follow(results)
    return results


def fence(through, waits):
    count = len(through)

    def kernel(*refs):
        pass

    return pl.pallas_call(
        kernel,
        in_specs=[kept_out] * (count + len(waits)),
        out_specs=[kept_out] * count,
        out_shape=[shape(array.shape, array.dtype) for array in through],
        input_output_aliases={j: j for j in range(count)},
        compiler_params=pltpu.CompilerParams(vmem_limit_bytes=mebibyte),
        cost_estimate=pl.CostEstimate(flops=1, bytes_accessed=1, transcendentals=0),
        name="fence",
    )(*through, *waits)


def full_out(dims, dtype=bf16):
    zeros = (0,) * len(dims)
    return (shape(dims, dtype), pl.BlockSpec(dims, lambda *_: zeros))


def copies(sources, targets, sems):
    started = []
    for source, target, sem in zip(sources, targets, sems):
        copy = pltpu.make_async_copy(source, target, sem)
        copy.start()
        started.append(copy)
    return started


def project(order, flags, pieces, at_piece, gains, biases, tables, weights, heads, head_dim):
    count, width = 1, pieces[0].shape[2]
    span_rows = sum(piece.shape[1] for piece in pieces)
    rows = count * span_rows
    chunk = pieces[0].shape[1]
    spans = len(weights)
    depth = width // spans
    wide = 3 * head_dim
    columns = heads * wide

    def kernel(flag_ref, *refs):
        piece_refs = refs[: len(pieces)]
        gain_ref, bias_ref, table_ref = refs[len(pieces) : len(pieces) + 3]
        weight_refs = refs[len(pieces) + 3 : len(pieces) + 3 + spans]
        first, second, normal, queries, pair, held, sems = refs[len(pieces) + 3 + spans :]
        started = []
        for h in range(heads):
            started.append(
                copies(
                    [w.at[:depth, h * wide : (h + 1) * wide] for w in weight_refs],
                    [held.at[h, k * depth : (k + 1) * depth] for k in range(spans)],
                    [sems.at[h, k] for k in range(spans)],
                )
            )
        start = 0
        for piece_ref in piece_refs:
            chunks = piece_ref.shape[1] // chunk

            def one(i, _, piece_ref=piece_ref, start=start, chunks=chunks):
                m, c = i // chunks, i % chunks
                values = piece_ref[m, pl.ds(pl.multiple_of(c * chunk, chunk), chunk), :]
                normed, _ = normalize(values.astype(f32))
                to = pl.ds(
                    pl.multiple_of(m * span_rows + start + c * chunk, chunk), chunk
                )
                normal[to, :] = normed.astype(bf16)
                first[to, :] = (normed * gain_ref[0:1] + bias_ref[0:1]).astype(bf16)
                second[to, :] = (normed * gain_ref[1:2] + bias_ref[1:2]).astype(bf16)
                return 0

            lax.fori_loop(0, count * chunks, one, 0)
            start += piece_ref.shape[1]
        for h in range(heads):
            for copy in started[h]:
                copy.wait()

            def two(m, _, h=h):
                to = pl.ds(pl.multiple_of(m * span_rows, span_rows), span_rows)
                made = plain(first[to, :], held[h])
                queries[h, to, :] = turn(made[:, :head_dim], table_ref, 1).astype(bf16)
                pair[0, h, to, :] = turn(
                    made[:, head_dim : 2 * head_dim], table_ref, 1
                ).astype(bf16)
                pair[1, h, to, :] = made[:, 2 * head_dim :].astype(bf16)
                return 0

            lax.fori_loop(0, count, two, 0)

    ins = [(piece, at((1,) + piece.shape[1:], (at_piece, 0, 0))) for piece in pieces]
    ins += [(array, whole(array)) for array in (gains, biases, tables)]
    ins += [(w, kept_out) for w in weights]
    outs = [full_out((rows, width))] * 3 + [
        full_out((heads, rows, head_dim)),
        full_out((2, heads, rows, head_dim)),
    ]
    scratch = [
        pltpu.VMEM((heads, width, wide), bf16),
        pltpu.SemaphoreType.DMA((heads, spans)),
    ]
    return run(order, flags, kernel, ins, outs, scratch, "project")


def expand_up(order, flags, second, weights, span_rows, room):
    rows, width = second.shape
    depth, hidden = weights[0].shape
    spans = len(weights)
    tile = min(512, hidden)
    tiles = hidden // tile

    def kernel(flag_ref, *refs):
        second_ref, weight_refs = refs[0], refs[1 : 1 + spans]
        active, slope, held, sems = refs[1 + spans :]
        started = []
        for t in range(tiles):
            started.append(
                copies(
                    [w.at[:, t * tile : (t + 1) * tile] for w in weight_refs],
                    [held.at[t, k * depth : (k + 1) * depth] for k in range(spans)],
                    [sems.at[t, k] for k in range(spans)],
                )
            )
        for t in range(tiles):
            for copy in started[t]:
                copy.wait()

            def one(m, _, t=t):
                to = pl.ds(pl.multiple_of(m * span_rows, span_rows), span_rows)
                pre = plain(second_ref[to, :], held[t])
                risen = 0.5 * (1.0 + lax.erf(pre * half_root))
                columns = slice(t * tile, (t + 1) * tile)
                active[to, columns] = (pre * risen).astype(bf16)
                slope[to, columns] = (
                    risen + pre * jnp.exp(-0.5 * pre * pre) * bell
                ).astype(bf16)
                return 0

            lax.fori_loop(0, rows // span_rows, one, 0)

    ins = [(second, whole(second))] + [(w, kept_out) for w in weights]
    outs = [
        (shape((rows, hidden + room)), at((rows, hidden), (0, 0))),
        full_out((rows, hidden)),
    ]
    scratch = [
        pltpu.VMEM((tiles, width, tile), bf16),
        pltpu.SemaphoreType.DMA((tiles, spans)),
    ]
    return run(order, flags, kernel, ins, outs, scratch, "expand")


def spread(refs):
    return [ref.at[j] for ref in refs for j in range(ref.shape[0])]


def attention(here, pairs, head, row_ref, key_ref, scale):
    scores = []
    for k, pair in enumerate(pairs):
        raw = turned(here, pair[0, head]) * scale
        scores.append(jnp.where(key_ref[k] <= row_ref[...], raw, masked_score))
    top = functools.reduce(
        jnp.maximum, [jnp.max(part, axis=1, keepdims=True) for part in scores]
    )
    scores = [jnp.exp(part - top) for part in scores]
    inverse = 1.0 / sum(jnp.sum(part, axis=1, keepdims=True) for part in scores)
    return [part * inverse for part in scores]


def attend(order, flags, units, queries, pairs, positions, key_positions, scale):
    heads, rows, head_dim = queries.shape
    spans = sum(pair.shape[0] for pair in pairs)
    across = heads * head_dim

    def kernel(flag_ref, units_ref, query_ref, *refs):
        views, refs = spread(refs[: len(pairs)]), refs[len(pairs) :]
        row_ref, key_ref, attended, probs = refs
        for h in range(heads):
            parts = attention(query_ref[h], views, h, row_ref, key_ref, scale)
            summed = None
            for k in range(spans):
                part = parts[k].astype(bf16)
                probs[k, h] = part
                term = plain(part, views[k][1, h])
                summed = term if summed is None else summed + term
            attended[:, h * head_dim : (h + 1) * head_dim] = summed.astype(bf16)

    ins = [(units, kept_out)]
    ins += [(array, whole(array)) for array in (queries, *pairs, positions, key_positions)]
    outs = [
        (shape(units.shape), at((rows, across), (0, units.shape[1] // across - 1))),
        full_out((spans, heads, rows, rows)),
    ]
    work = spans * rows * rows * 4 * heads * 4 / mebibyte
    return run(
        order, flags, kernel, ins, outs, [], "attend", work=work, in_place={1: 0}
    )


def attention_grads(grad, here, parts, views, head, keep, send, scale):
    half = keep.shape[0]
    grad_probs = [turned(grad, view[1, head]) for view in views]
    delta = sum(
        jnp.sum(part.astype(f32) * slope, axis=1, keepdims=True)
        for part, slope in zip(parts, grad_probs)
    )
    query_grad = None
    for k, view in enumerate(views):
        slopes = (parts[k].astype(f32) * (grad_probs[k] - delta)).astype(bf16)
        term = plain(slopes, view[0, head])
        query_grad = term if query_grad is None else query_grad + term
        side = keep if k < half else send
        side[k % half, 0, head] = (dot(slopes, here, ((0,), (0,))) * scale).astype(bf16)
        side[k % half, 1, head] = dot(parts[k].astype(bf16), grad, ((0,), (0,))).astype(bf16)
    return query_grad * scale


def attend_both(
    order, flags, rows_in, packed, queries, pairs, positions, key_positions, tables, scale
):
    heads, rows, head_dim = queries.shape
    width = rows_in.shape[1]
    spans = len(packed)
    across, depth = heads * head_dim, width // spans
    half = spans // 2

    def kernel(flag_ref, rows_ref, *refs):
        packed_refs, refs = refs[:spans], refs[spans:]
        query_ref, refs = refs[0], refs[1:]
        views, refs = spread(refs[: len(pairs)]), refs[len(pairs) :]
        row_ref, key_ref, table_ref, attended, turned_back, keep, send, held, sems = refs
        started = copies(
            [w.at[:across, 3 * across : 3 * across + depth] for w in packed_refs],
            [held.at[:, k * depth : (k + 1) * depth] for k in range(spans)],
            [sems.at[k] for k in range(spans)],
        )
        all_parts = []
        for h in range(heads):
            parts = attention(query_ref[h], views, h, row_ref, key_ref, scale)
            summed = None
            for k in range(spans):
                term = plain(parts[k].astype(bf16), views[k][1, h])
                summed = term if summed is None else summed + term
            attended[:, h * head_dim : (h + 1) * head_dim] = summed.astype(bf16)
            all_parts.append(parts)
        for copy in started:
            copy.wait()
        grads = turned(rows_ref[...], held[...]).astype(bf16)
        for h in range(heads):
            made = attention_grads(
                grads[:, h * head_dim : (h + 1) * head_dim],
                query_ref[h],
                all_parts[h],
                views,
                h,
                keep,
                send,
                scale,
            )
            turned_back[h] = turn(made, table_ref, -1).astype(bf16)

    ins = [(rows_in, whole(rows_in))] + [(w, kept_out) for w in packed]
    ins += [
        (array, whole(array)) for array in (queries, *pairs, positions, key_positions, tables)
    ]
    outs = [full_out((rows, across)), full_out((heads, rows, head_dim))]
    outs += [full_out((half, 2, heads, rows, head_dim))] * 2
    scratch = [pltpu.VMEM((across, width), bf16), pltpu.SemaphoreType.DMA((spans,))]
    work = spans * rows * rows * 4 * (heads + 4) / mebibyte
    return run(order, flags, kernel, ins, outs, scratch, "attend_both", work=work)


def hidden_both(order, flags, second, pieces, at_piece, expand, contract, normal, gains):
    rows, width = second.shape
    hidden, depth = contract[0].shape
    spans = len(contract)
    tile = min(512, hidden)
    tiles = hidden // tile

    def kernel(flag_ref, second_ref, *refs):
        piece_refs, refs = refs[: len(pieces)], refs[len(pieces) :]
        expand_refs, refs = refs[:spans], refs[spans:]
        contract_refs, refs = refs[:spans], refs[spans:]
        normal_ref, gain_ref, rows_out, active, grads, part, side, *refs = refs
        held_up, held_down, sems_up, sems_down = refs
        started = []
        for t in range(tiles):
            block = slice(t * tile, (t + 1) * tile)
            places = [slice(k * depth, (k + 1) * depth) for k in range(spans)]
            up = copies(
                [w.at[:, block] for w in expand_refs],
                [held_up.at[place, block] for place in places],
                [sems_up.at[t, k] for k in range(spans)],
            )
            down = copies(
                [w.at[block, :] for w in contract_refs],
                [held_down.at[block, place] for place in places],
                [sems_down.at[t, k] for k in range(spans)],
            )
            started.append((up, down))
        start = 0
        for piece_ref in piece_refs:
            size = piece_ref.shape[1]
            rows_out[start : start + size, :] = piece_ref[0]
            start += size
        for t in range(tiles):
            block = slice(t * tile, (t + 1) * tile)
            for copy in started[t][0] + started[t][1]:
                copy.wait()
            pre = plain(second_ref[...], held_up[:, block])
            risen = 0.5 * (1.0 + lax.erf(pre * half_root))
            active[:, block] = (pre * risen).astype(bf16)
            slope = risen + pre * jnp.exp(-0.5 * pre * pre) * bell
            grads[:, block] = (turned(rows_out[...], held_down[block, :]) * slope).astype(bf16)
        for k in range(spans):
            place = slice(k * depth, (k + 1) * depth)
            made = turned(grads[...], held_up[place, :])
            side[0:1, place] = jnp.sum(
                made * normal_ref[:, place].astype(f32), axis=0, keepdims=True
            )
            side[1:2, place] = jnp.sum(made, axis=0, keepdims=True)
            part[:, place] = made * gain_ref[1:2, place]

    ins = [(second, whole(second))]
    ins += [(piece, at((1,) + piece.shape[1:], (at_piece, 0, 0))) for piece in pieces]
    ins += [(w, kept_out) for w in expand] + [(w, kept_out) for w in contract]
    ins += [(normal, whole(normal)), (gains, whole(gains))]
    outs = [
        full_out((rows, width)),
        full_out((rows, hidden)),
        full_out((rows, hidden)),
        full_out((rows, width), f32),
        full_out((2, width), f32),
    ]
    scratch = [
        pltpu.VMEM((width, hidden), bf16),
        pltpu.VMEM((hidden, width), bf16),
        pltpu.SemaphoreType.DMA((tiles, spans)),
        pltpu.SemaphoreType.DMA((tiles, spans)),
    ]
    return run(order, flags, kernel, ins, outs, scratch, "hidden_both")


def branch_out(order, flags, groups, contract, packed):
    hidden, depth = contract[0].shape
    spans = len(contract)
    across = depth
    width = depth * spans
    span_rows = groups[0][0].shape[0]
    block = span_rows // 2
    count = len(groups)

    def kernel(flag_ref, *refs):
        group_refs, refs = refs[: 2 * count], refs[2 * count :]
        contract_refs, packed_refs = refs[:spans], refs[spans : 2 * spans]
        blocks, refs = refs[2 * spans : 2 * (spans + count)], refs[2 * (spans + count) :]
        held, held_out, sems = refs
        outputs = [w.at[:across, 3 * across : 3 * across + depth] for w in packed_refs]
        started = copies(
            [ref for k in range(spans) for ref in (outputs[k], contract_refs[k])],
            [ref for k in range(spans) for ref in (held_out.at[k], held.at[k])],
            [sems.at[j] for j in range(2 * spans)],
        )
        for k in range(spans):
            started[2 * k].wait()
            started[2 * k + 1].wait()
            columns = slice(k * depth, (k + 1) * depth)
            for c in range(count):
                made = plain(group_refs[2 * c + 1][...], held_out[k])
                made = made + plain(group_refs[2 * c][...], held[k])
                blocks[2 * c][:, columns] = made[:block].astype(bf16)
                blocks[2 * c + 1][:, columns] = made[block:].astype(bf16)

    ins = []
    for active, attended in groups:
        place = attended.shape[1] // across - 1
        ins += [
            (active, at((span_rows, hidden), (0, 0))),
            (attended, at((span_rows, across), (0, place))),
        ]
    ins += [(w, kept_out) for w in contract] + [(w, kept_out) for w in packed]
    outs = [full_out((block, width))] * (2 * count)
    scratch = [
        pltpu.VMEM((spans, hidden, depth), bf16),
        pltpu.VMEM((spans, across, depth), bf16),
        pltpu.SemaphoreType.DMA((2 * spans,)),
    ]
    return run(order, flags, kernel, ins, outs, scratch, "branch")


def attend_back(order, flags, pieces, packed, queries, pairs, probs, tables, scale):
    rows = sum(piece.shape[1] for piece in pieces)
    width = pieces[0].shape[2]
    heads, _, head_dim = queries.shape
    spans = len(packed)
    across, depth = heads * head_dim, width // spans
    half = spans // 2

    def kernel(flag_ref, *refs):
        piece_refs, refs = refs[: len(pieces)], refs[len(pieces) :]
        packed_refs, refs = refs[:spans], refs[spans:]
        query_ref, refs = refs[0], refs[1:]
        views, refs = spread(refs[: len(pairs)]), refs[len(pairs) :]
        prob_ref, table_ref, rows_out, turned_back, keep, send, *refs = refs
        columns_out, (held, sems) = refs[:spans], refs[spans:]
        started = copies(
            [w.at[:across, 3 * across : 3 * across + depth] for w in packed_refs],
            [held.at[:, k * depth : (k + 1) * depth] for k in range(spans)],
            [sems.at[k] for k in range(spans)],
        )
        start = 0
        for piece_ref in piece_refs:
            size = piece_ref.shape[1]
            rows_out[start : start + size, :] = piece_ref[0]
            start += size
        for k in range(spans):
            columns_out[k][...] = rows_out[:, k * depth : (k + 1) * depth]
        for copy in started:
            copy.wait()
        grads = turned(rows_out[...], held[...]).astype(bf16)
        for h in range(heads):
            made = attention_grads(
                grads[:, h * head_dim : (h + 1) * head_dim],
                query_ref[h],
                [prob_ref[k, h] for k in range(spans)],
                views,
                h,
                keep,
                send,
                scale,
            )
            turned_back[h] = turn(made, table_ref, -1).astype(bf16)

    ins = [(piece, whole(piece)) for piece in pieces] + [(w, kept_out) for w in packed]
    ins += [(array, whole(array)) for array in (queries, *pairs, probs, tables)]
    outs = [full_out((rows, width)), full_out((heads, rows, head_dim))]
    outs += [full_out((half, 2, heads, rows, head_dim))] * 2
    outs += [full_out((rows, depth))] * spans
    scratch = [pltpu.VMEM((across, width), bf16), pltpu.SemaphoreType.DMA((spans,))]
    work = spans * rows * rows * 4 * 4 / mebibyte
    return run(order, flags, kernel, ins, outs, scratch, "attend_back", work=work)


def hidden_back(order, flags, upstream, contract, expand, slope, normal, gains):
    span_rows, width = upstream.shape
    hidden, depth = contract[0].shape
    spans = len(contract)
    tile = min(512, hidden)
    tiles = hidden // tile

    def kernel(flag_ref, *refs):
        upstream_ref, refs = refs[0], refs[1:]
        contract_refs, refs = refs[:spans], refs[spans:]
        expand_refs, refs = refs[:spans], refs[spans:]
        slope_ref, normal_ref, gain_ref, grads, part, side, held, held_up, sems, sems_up = refs
        started = [
            copies(
                [w.at[t * tile : (t + 1) * tile, :] for w in contract_refs],
                [held.at[t, :, k * depth : (k + 1) * depth] for k in range(spans)],
                [sems.at[t, k] for k in range(spans)],
            )
            for t in range(tiles)
        ]
        started_up = copies(
            expand_refs, [held_up.at[k] for k in range(spans)], [sems_up.at[k] for k in range(spans)]
        )
        for t in range(tiles):
            for copy in started[t]:
                copy.wait()
            columns = slice(t * tile, (t + 1) * tile)
            grads[:, columns] = (
                turned(upstream_ref[...], held[t]) * slope_ref[:, columns].astype(f32)
            ).astype(bf16)
        for k in range(spans):
            started_up[k].wait()
            made = turned(grads[...], held_up[k])
            columns = slice(k * depth, (k + 1) * depth)
            side[0:1, columns] = jnp.sum(
                made * normal_ref[:, columns].astype(f32), axis=0, keepdims=True
            )
            side[1:2, columns] = jnp.sum(made, axis=0, keepdims=True)
            part[:, columns] = made * gain_ref[1:2, columns]

    ins = [(upstream, whole(upstream))]
    ins += [(w, kept_out) for w in contract] + [(w, kept_out) for w in expand]
    ins += [
        (slope, whole(slope)),
        (normal, whole(normal)),
        (gains, whole(gains)),
    ]
    outs = [
        full_out((span_rows, hidden)),
        full_out((span_rows, width), f32),
        full_out((2, width), f32),
    ]
    scratch = [
        pltpu.VMEM((tiles, tile, width), bf16),
        pltpu.VMEM((spans, depth, hidden), bf16),
        pltpu.SemaphoreType.DMA((tiles, spans)),
        pltpu.SemaphoreType.DMA((spans,)),
    ]
    return run(order, flags, kernel, ins, outs, scratch, "hidden_back")


def project_back(
    order, flags, turned_back, own, came, weights, part, normal, gains, tables
):
    heads, span_rows, head_dim = turned_back.shape
    spans = len(weights)
    width = part.shape[1]
    depth, columns = width // spans, 3 * heads * head_dim
    block = span_rows // 2

    def kernel(flag_ref, *refs):
        query_ref, own_ref, came_ref, refs = refs[0], refs[1], refs[2], refs[3:]
        weight_refs, refs = refs[:spans], refs[spans:]
        part_ref, normal_ref, gain_ref, table_ref, grads, side, *refs = refs
        low, high, held, sems = refs
        started = copies(
            [w.at[:depth, :columns] for w in weight_refs],
            [held.at[k] for k in range(spans)],
            [sems.at[k] for k in range(spans)],
        )
        for h in range(heads):
            at_column = h * 3 * head_dim
            keys = own_ref[0, h].astype(f32) + came_ref[0, h].astype(f32)
            values = own_ref[1, h].astype(f32) + came_ref[1, h].astype(f32)
            grads[:, at_column : at_column + head_dim] = query_ref[h]
            grads[:, at_column + head_dim : at_column + 2 * head_dim] = turn(
                keys, table_ref, -1
            ).astype(bf16)
            grads[:, at_column + 2 * head_dim : at_column + 3 * head_dim] = values.astype(bf16)
        for k in range(spans):
            started[k].wait()
            made = turned(grads[...], held[k])
            span_columns = slice(k * depth, (k + 1) * depth)
            side[0:1, span_columns] = jnp.sum(
                made * normal_ref[:, span_columns].astype(f32), axis=0, keepdims=True
            )
            side[1:2, span_columns] = jnp.sum(made, axis=0, keepdims=True)
            both = (made * gain_ref[0:1, span_columns] + part_ref[:, span_columns]).astype(bf16)
            low[:, span_columns] = both[:block]
            high[:, span_columns] = both[block:]

    ins = [(array, whole(array)) for array in (turned_back, own, came)]
    ins += [(w, kept_out) for w in weights]
    ins += [(part, whole(part)), (normal, whole(normal))]
    ins += [(gains, whole(gains)), (tables, whole(tables))]
    outs = [full_out((span_rows, columns)), full_out((2, width), f32)]
    outs += [full_out((block, width))] * 2
    scratch = [pltpu.VMEM((spans, depth, columns), bf16), pltpu.SemaphoreType.DMA((spans,))]
    return run(order, flags, kernel, ins, outs, scratch, "project_back")


def weight_sums(order, flags, lefts, rights, by_rows, spans):
    rows = sum(piece.shape[0] for piece in lefts[1][0])
    left_width = sum(group[0].shape[1] for group in lefts[1])
    right_width = sum(group[0].shape[1] for group in rights[1])
    if by_rows:
        tile = left_width // spans
        steps, block = spans // 2, (tile, right_width)
    else:
        tile = min(512, left_width)
        while left_width % tile:
            tile //= 2
        steps, block = left_width // tile, (tile, right_width // 2)
    chunk = min(1024, block[1])
    while right_width % chunk:
        chunk //= 2
    pieces = [
        [piece for groups in (lefts[s], rights[s]) for group in groups for piece in group]
        for s in (0, 1)
    ]
    most = max(len(p) for p in pieces)

    def kernel(flag_ref, *refs):
        piece_refs = (refs[: len(pieces[0])], refs[len(pieces[0]) : len(pieces[0]) + len(pieces[1])])
        keep, send, left, right, flipped, sems = refs[len(pieces[0]) + len(pieces[1]) :]
        g = pl.program_id(0)
        for s in (0, 1):

            @pl.when((g == 0) & (flag_ref[2] == s))
            def _(s=s):
                targets = []
                for held, groups in ((left, lefts[s]), (right, rights[s])):
                    column = 0
                    for group in groups:
                        row, wide = 0, group[0].shape[1]
                        for piece in group:
                            targets.append(
                                held.at[row : row + piece.shape[0], column : column + wide]
                            )
                            row += piece.shape[0]
                        column += wide
                started = copies(
                    piece_refs[s], targets, [sems.at[j] for j in range(len(targets))]
                )
                for copy in started:
                    copy.wait()

        def product(column, store):
            flipped[...] = left[:, pl.ds(pl.multiple_of(column, LANES), tile)].T

            def one(c, _):
                columns = pl.ds(pl.multiple_of(c * chunk, chunk), chunk)
                store(c, plain(flipped[...], right[:, columns]).astype(bf16))
                return 0

            lax.fori_loop(0, right_width // chunk, one, 0)

        if by_rows:

            def to(target):
                def store(c, made):
                    target[:, pl.ds(pl.multiple_of(c * chunk, chunk), chunk)] = made

                return store

            product(g * tile, to(keep))
            product((g + steps) * tile, to(send))
        else:
            half = right_width // 2 // chunk

            def store(c, made):
                @pl.when(c < half)
                def _():
                    keep[:, pl.ds(pl.multiple_of(c * chunk, chunk), chunk)] = made

                @pl.when(c >= half)
                def _():
                    send[:, pl.ds(pl.multiple_of((c - half) * chunk, chunk), chunk)] = made

            product(g * tile, store)

    ins = [(piece, kept_out) for s in (0, 1) for piece in pieces[s]]
    dims = (steps * tile, block[1])
    outs = [(shape(dims), pl.BlockSpec(block, lambda g: (g, 0)))] * 2
    scratch = [
        pltpu.VMEM((rows, left_width), bf16),
        pltpu.VMEM((rows, right_width), bf16),
        pltpu.VMEM((tile, rows), bf16),
        pltpu.SemaphoreType.DMA((most,)),
    ]
    return run(
        order, flags, kernel, ins, outs, scratch, "weight_sums", grid=(steps,)
    )


def owner_sums(order, flags, lefts, rights):
    left_width, right_width = lefts[0][0].shape[1], rights[0][0].shape[1]
    rows = sum(piece.shape[0] for piece in lefts[0])
    count = len(lefts)
    tile = min(512, left_width)
    while left_width % tile:
        tile //= 2
    pieces = [lefts[m] + rights[m] for m in range(count)]
    most = max(len(p) for p in pieces)

    def kernel(flag_ref, *refs):
        piece_refs, refs = refs[: sum(map(len, pieces))], refs[sum(map(len, pieces)) :]
        out, left, right, flipped, sems = refs
        started, used = [], 0
        for m in range(count):
            targets = []
            for held, group in ((left, lefts[m]), (right, rights[m])):
                row = 0
                for piece in group:
                    targets.append(held.at[m, row : row + piece.shape[0]])
                    row += piece.shape[0]
            started.append(
                copies(
                    piece_refs[used : used + len(targets)],
                    targets,
                    [sems.at[m, j] for j in range(len(targets))],
                )
            )
            used += len(targets)
        for m in range(count):
            for copy in started[m]:
                copy.wait()

            def one(t, _, m=m):
                block = pl.ds(pl.multiple_of(t * tile, tile), tile)
                flipped[...] = left[m, :, block].T
                made = plain(flipped[...], right[m])
                out[block, :] = made if m == 0 else out[block, :] + made
                return 0

            lax.fori_loop(0, left_width // tile, one, 0)

    ins = [(piece, kept_out) for group in pieces for piece in group]
    outs = [full_out((left_width, right_width), f32)]
    scratch = [
        pltpu.VMEM((count, rows, left_width), bf16),
        pltpu.VMEM((count, rows, right_width), bf16),
        pltpu.VMEM((tile, rows), bf16),
        pltpu.SemaphoreType.DMA((count, most)),
    ]
    return run(order, flags, kernel, ins, outs, scratch, "owner_sums")[0]


def fold(order, flags, keep, came, dim):
    rows, columns = keep.shape
    if dim == 0:
        tile = rows // 4
        steps, block = rows // 2 // tile, (tile, columns)
        places = [lambda g: (g, 0), lambda g: (g + steps, 0)]
        half = (rows // 2, columns)
    else:
        tile = rows // 4
        steps, block = rows // tile, (tile, columns // 2)
        places = [lambda g: (g, 0), lambda g: (g, 1)]
        half = (rows, columns // 2)

    def kernel(flag_ref, keep_low, keep_high, came_low, came_high, low, high):
        low[...] = (keep_low[...].astype(f32) + came_low[...].astype(f32)).astype(bf16)
        high[...] = (keep_high[...].astype(f32) + came_high[...].astype(f32)).astype(bf16)

    ins = [(array, pl.BlockSpec(block, place)) for array in (keep, came) for place in places]
    outs = [(shape(half), pl.BlockSpec(block, lambda g: (g, 0)))] * 2
    return run(order, flags, kernel, ins, outs, [], "fold", grid=(steps,))


def shards(
    block_input,
    out_grad,
    triple_weight,
    output_weight,
    expand_weight,
    contract_weight,
    norm_gains,
    norm_biases,
):
    section = lax.axis_index("pipe")
    span = lax.axis_index("ctx")
    lane = lax.axis_index("tp")
    spans = lax.axis_size("ctx")
    lanes = lax.axis_size("tp")
    micros, rows, width = block_input.shape
    span_rows = rows * lanes
    heads = triple_weight.shape[2]
    head_dim = triple_weight.shape[4]
    across_units = heads * head_dim
    scale = head_dim ** (-0.5)
    first_section = section == 0
    both = (0, 1)

    def hop(array, axis, step, sections):
        size = lax.axis_size(axis)
        pairs = [(s * size + a, s * size + (a ^ step)) for s in sections for a in range(size)]
        return lax.ppermute(array, ("pipe", axis), pairs)

    order = Order()

    def flags_for(wanted):
        return jnp.stack([jnp.asarray(wanted), span, section]).astype(jnp.int32)

    flags = [flags_for(section == s) for s in both]
    always = flags_for(1)

    kept = [[SimpleNamespace() for _ in range(micros)] for _ in both]
    due = {}
    slot_index = [0]

    def slot(hops, kernels=()):
        now = slot_index[0]
        slot_index[0] += 1
        ready = due.pop(now, [])
        hops = [h if len(h) == 3 else h + (1,) for h in hops]
        if hops:
            gated = fence([operand for operand, _, _ in hops], order.last + ready)
            order.last = [min(gated, key=lambda array: array.size)]
            for passed, (_, go, slots) in zip(gated, hops):
                results = go(passed)
                results = results if isinstance(results, list) else [results]
                due.setdefault(now + slots, []).extend(results)
        else:
            order.last = order.last + ready
        for kernel in kernels:
            kernel()

    def halved(keep, came, dim):
        middle = keep.shape[dim] // 2
        total = keep.astype(f32) + came.astype(f32)
        return (
            lax.slice_in_dim(total, 0, middle, axis=dim).astype(bf16),
            lax.slice_in_dim(total, middle, 2 * middle, axis=dim).astype(bf16),
        )

    def spread_hops(pieces, axis, axis_name, sections, first):
        step = lax.axis_size(axis_name) // 4
        going = first
        while step:
            pieces.append(hop(going, axis_name, step, sections))
            going = jnp.concatenate(pieces, axis=axis)
            step //= 2
        return pieces[-1]

    def fold_hops(k, first, axis_name, dim, sections):
        step, size = 1, lax.axis_size(axis_name)
        while 2 * step < size:
            came = hop(first, axis_name, step, sections)
            k.keep, k.send = halved(k.keep, came, dim)
            first = k.send
            step *= 2
        return came

    depth = width // spans
    far = spans // 2
    assert depth == across_units
    small = jnp.concatenate([norm_gains[0], norm_biases[0]], axis=0)
    packed = jnp.concatenate(
        [triple_weight[0].reshape(depth, -1), output_weight[0].reshape(-1, depth)],
        axis=1,
    )
    packed = jnp.pad(packed, ((0, 16), (0, 0)))
    packed = lax.dynamic_update_slice(packed, small, (depth, 0))
    own_expand, own_contract = expand_weight[0], contract_weight[0]
    hidden = own_expand.shape[1]
    inputs = xor_blocks(block_input, span, spans)
    cotangent = xor_blocks(out_grad, span, spans)
    early = jnp.where(first_section, inputs, cotangent)

    in_row = jnp.arange(rows, dtype=jnp.int32)
    in_span = jnp.concatenate([(lane ^ j) * rows + in_row for j in doubling(lanes)])
    positions = span * span_rows + in_span
    key_positions = jnp.stack([(span ^ k) * span_rows + in_span for k in doubling(spans)])
    tables = rope_tables(positions)
    position_column = positions[:, None]
    key_positions = key_positions[:, None, :]

    def blocks_of(own, came):
        held, step = {0: own, far: came}, far // 2
        while step:
            for k in list(held):
                held[k ^ step] = hop(held[k], "ctx", step, both)
            step //= 2
        return [held[k] for k in doubling(spans)]

    lane_offsets = doubling(lanes)

    def across(array, j, source):
        pairs = [(source * lanes + a, (1 - source) * lanes + (a ^ j)) for a in range(lanes)]
        return lax.ppermute(array, ("pipe", "tp"), pairs)

    def rows_far(s, m):
        k = kept[s][m]

        def go(passed):
            k.rows = passed
            k.pieces = [passed, hop(passed, "tp", lanes // 2, (s,))]
            return k.pieces[1]

        return k.rows, go

    def rows_near(s, m):
        k = kept[s][m]

        def go(passed):
            last_piece = spread_hops(k.pieces, 0, "tp", (s,), passed)
            k.row_pieces = [piece[None] for piece in k.pieces]
            return last_piece

        return jnp.concatenate(k.pieces, axis=0), go

    def pair_far(s, m):
        k = kept[s][m]

        def go(passed):
            k.pairs = [passed, hop(passed, "ctx", far, (s,))]
            return k.pairs[1]

        return k.pair, go

    def pair_near(s, m):
        k = kept[s][m]

        def go(passed):
            return spread_hops(k.pairs, 0, "ctx", (s,), passed)

        return jnp.concatenate(k.pairs, axis=0), go

    def pair_grad_near(s, m):
        k = kept[s][m].pair_grad
        return k.send, lambda passed: fold_hops(k, passed, "ctx", 0, (s,))

    def pair_grad_far(s, m):
        k = kept[s][m].pair_grad

        def go(passed):
            k.came = hop(passed, "ctx", far, (s,))
            return k.came

        return k.send, go

    def sum_near(s, k):
        k.keep, going = k.blocks
        return going, lambda passed: fold_hops(k, passed, "tp", 0, (s,))

    def sum_far(s, k):
        def go(passed):
            k.blocks, k.arrived = [k.keep], [hop(passed, "tp", lanes // 2, (s,))]
            return k.arrived[0]

        return k.send, go

    def sum_hops(s, k):
        low, high = k.blocks
        blocks = [part[at : at + rows] for part in (low, high) for at in range(0, low.shape[0], rows)]
        k.blocks, k.arrived = blocks[:1], []

        def one(j):
            def go(passed):
                k.arrived.append(hop(passed, "tp", lane_offsets[j], (s,)))
                return k.arrived[-1]

            return blocks[j], go

        return [one(j) for j in range(1, lanes)]

    def pair_grad_hops(s, m):
        k = kept[s][m].pair_grad
        half = spans // 2
        pieces = [part[j : j + 1] for part in (k.keep, k.send) for j in range(half)]
        k.keep, arrived = pieces[0], []

        def one(j):
            def go(passed):
                arrived.append(hop(passed, "ctx", doubling(spans)[j], (s,)))
                k.came = sum(array.astype(f32) for array in arrived)
                return arrived[-1]

            return pieces[j], go

        return [one(j) for j in range(1, spans)]

    def units_far(m):
        k = kept[0][m]

        def go(passed):
            k.all_units = [passed, hop(passed, "ctx", far, (0,))]
            return k.all_units[1]

        return k.units, go

    def units_near(m):
        k = kept[0][m]

        def go(passed):
            return spread_hops(k.all_units, 0, "ctx", (0,), passed)

        return jnp.concatenate(k.all_units, axis=0), go

    def column_hops(m):
        k = kept[0][m]
        k.own_columns = [k.columns[0]]

        def one(j):
            def go(passed):
                k.own_columns.append(hop(passed, "ctx", doubling(spans)[j], (0,)))
                return k.own_columns[-1]

            return k.columns[j], go

        return [one(j) for j in range(1, spans)]

    def total_of(k):
        return sum(array.astype(f32) for array in [k.blocks[0], *k.arrived])

    def norm_back(upstream, combined, entering):
        normalized, inverse = normalize(entering.astype(f32))
        return (
            upstream.astype(f32)
            + inverse
            * (
                combined
                - jnp.mean(combined, axis=-1, keepdims=True)
                - normalized * jnp.mean(combined * normalized, axis=-1, keepdims=True)
            )
        ).astype(bf16)

    def middle_of(m):
        return (inputs[m].astype(f32) + total_of(kept[0][m])).astype(bf16)

    def entry_of(m):
        k = kept[1][m]
        return norm_back(cotangent[m], total_of(k), k.rows)

    def hand(s, m):
        k, other = kept[s][m], kept[1 - s][m]
        k.given = middle_of(m) if s == 0 else entry_of(m)

        def go(passed):
            k.given = passed
            pieces = [across(passed, j, s) for j in lane_offsets]
            other.rows = pieces[0]
            other.row_pieces = [piece[None] for piece in pieces]
            return pieces

        return k.given, go

    def hand_one(s, m):
        k, other = kept[s][m], kept[1 - s][m]
        k.given = middle_of(m) if s == 0 else entry_of(m)

        def go(passed):
            k.given = passed
            other.rows = across(passed, 0, s)
            return other.rows

        return k.given, go

    def run_project(s, m):
        k = kept[s][m]
        pieces, place = (early_pieces, m) if s == 0 else (k.row_pieces, 0)
        k.first, k.second, k.normal, k.queries, pair = project(
            order, flags[s], pieces, place, gains, biases, tables, packed, heads, head_dim
        )
        k.pair = pair[None]

    def run_expand(m):
        k = kept[0][m]
        k.units, k.slope = expand_up(
            order, flags[0], k.second, weights.expand, span_rows, across_units
        )

    def run_attend(m):
        k = kept[0][m]
        k.units, k.probs = attend(
            order,
            flags[0],
            k.units,
            k.queries,
            k.pairs,
            position_column,
            key_positions,
            scale,
        )

    def run_branch(m):
        k = kept[0][m]
        k.blocks = branch_out(
            order, flags[0], [(k.units, k.units)], contract, packed
        )

    def run_hidden_both(m):
        k = kept[1][m]
        k.upstream, k.active, k.hidden, k.part, k.side_second = hidden_both(
            order,
            flags[1],
            k.second,
            early_pieces,
            m,
            weights.expand,
            contract,
            k.normal,
            gains,
        )

    def run_attend_both(m):
        k = kept[1][m]
        k.attended, k.turned_back, keep, send = attend_both(
            order,
            flags[1],
            k.upstream,
            packed,
            k.queries,
            k.pairs,
            position_column,
            key_positions,
            tables,
            scale,
        )
        k.pair_grad = SimpleNamespace(keep=keep, send=send)

    def run_attend_back(m):
        k = kept[0][m]
        k.upstream, k.turned_back, keep, send, *k.columns = attend_back(
            order,
            flags[0],
            k.row_pieces,
            packed,
            k.queries,
            k.pairs,
            k.probs,
            tables,
            scale,
        )
        k.pair_grad = SimpleNamespace(keep=keep, send=send)

    def run_hidden_back(m):
        k = kept[0][m]
        k.hidden, k.part, k.side_second = hidden_back(
            order,
            flags[0],
            k.upstream,
            contract,
            weights.expand,
            k.slope,
            k.normal,
            gains,
        )

    def run_project_back(s, m):
        k = kept[s][m]
        own, arrived = k.pair_grad.keep, k.pair_grad.came
        k.stacked, k.side_first, *k.blocks = project_back(
            order,
            flags[s],
            k.turned_back,
            own.reshape(own.shape[1:]),
            arrived.reshape(arrived.shape[1:]),
            packed,
            k.part,
            k.normal,
            gains,
            tables,
        )

    def of(name, s, count=micros):
        return [getattr(kept[s][m], name) for m in range(count)]

    branch_sums, expand_sums, triple_sums = (
        SimpleNamespace(parts=[], flags=f, sections=secs)
        for f, secs in ((flags[1], (1,)), (always, both), (always, both))
    )

    def run_sums(w, lefts, rights, by_rows):
        w.dim = 0 if by_rows else 1
        w.keep, w.send = weight_sums(order, w.flags, lefts, rights, by_rows, spans)

    def wide_near(w):
        def go(passed):
            w.came = hop(passed, "ctx", 1, w.sections)
            return w.came

        return w.send, go

    def run_fold(w):
        step = 2
        w.keep, w.send = fold(order, w.flags, w.keep, w.came, w.dim)
        while 2 * step < spans:
            w.came = hop(w.send, "ctx", step, w.sections)
            w.keep, w.send = fold(order, w.flags, w.keep, w.came, w.dim)
            step *= 2

    def wide_far(w, start, stop):
        def go(passed):
            w.parts.append(hop(passed, "ctx", far, w.sections))
            return w.parts[-1]

        return w.send[start:stop], go

    weights = SimpleNamespace(expand_came=[], contract_came=[])
    half_depth = depth // 2

    def expand_far(start, stop):
        def go(passed):
            weights.expand_came.append(hop(passed, "ctx", far, both))
            return weights.expand_came[-1]

        return own_expand[start:stop], go

    def packed_far(passed):
        weights.packed_came = hop(passed, "ctx", far, both)
        return weights.packed_came

    def packed_near(passed):
        weights.packed = blocks_of(packed, passed)
        return weights.packed[1:]

    def expand_near(passed):
        weights.expand = blocks_of(own_expand, passed)
        return weights.expand[1:]

    def contract_far(start, stop):
        def go(passed):
            weights.contract_came.append(hop(passed, "ctx", far, both))
            return weights.contract_came[-1]

        return own_contract[start:stop], go

    def contract_near(passed):
        weights.contract = blocks_of(own_contract, passed)
        return weights.contract[1:]

    def early_hops(passed):
        weights.early = [passed] + [hop(passed, "tp", j, both) for j in lane_offsets[1:]]
        return weights.early[1:]

    quarter = depth // 4
    due[0] = [expand_far(0, quarter)[1](own_expand[:quarter])]
    slot([(packed, packed_far), expand_far(quarter, depth), (early, early_hops)])
    early_pieces = weights.early
    cuts = [0, hidden // 4, 11 * hidden // 16, hidden]
    expand_came = jnp.concatenate(weights.expand_came, axis=0)
    slot(
        [
            (weights.packed_came, packed_near),
            (expand_came, expand_near),
            contract_far(cuts[0], cuts[1]),
        ]
    )
    packed = weights.packed
    small_full = jnp.concatenate(
        [piece[depth : depth + 4, :depth] for piece in packed], axis=1
    ).astype(f32)
    gains, biases = small_full[:2], small_full[2:]
    slot(
        [contract_far(cuts[1], cuts[2])],
        [lambda m=m: run_project(0, m) for m in range(micros)],
    )
    a, b = kept
    slot(
        [pair_far(0, 0), contract_far(cuts[2], cuts[3])],
        [lambda m=m: run_expand(m) for m in range(micros)],
    )
    contract_came = jnp.concatenate(weights.contract_came, axis=0)
    slot([(contract_came, contract_near), pair_near(0, 0), pair_far(0, 1)])
    contract = weights.contract
    slot([pair_near(0, 1)], [lambda: run_attend(0), lambda: run_branch(0)])
    slot(
        sum_hops(0, a[0]) + [pair_far(0, 2)], [lambda: run_attend(1), lambda: run_branch(1)]
    )
    slot([hand(0, 0), pair_near(0, 2)])
    slot(
        sum_hops(0, a[1]),
        [lambda: run_project(1, 0), lambda: run_attend(2), lambda: run_branch(2)],
    )
    slot([pair_far(1, 0)], [lambda: run_hidden_both(0)])
    slot([pair_near(1, 0)])
    slot([hand(0, 1)], [lambda: run_attend_both(0)])
    slot([pair_grad_near(1, 0)] + sum_hops(0, a[2]), [lambda: run_project(1, 1)])
    slot(
        [pair_far(1, 1), pair_grad_far(1, 0), units_far(0)], [lambda: run_hidden_both(1)]
    )
    slot([pair_near(1, 1)], [lambda: run_project_back(1, 0)])
    slot([hand(0, 2)], [lambda: run_attend_both(1)])
    slot(
        [pair_grad_near(1, 1), sum_near(1, b[0]), units_near(0)], [lambda: run_project(1, 2)]
    )
    slot(
        [pair_far(1, 2), pair_grad_far(1, 1), sum_far(1, b[0]), units_far(1)],
        [lambda: run_hidden_both(2)],
    )
    slot(
        [pair_near(1, 2), hand_one(1, 0), units_near(1)], [lambda: run_project_back(1, 1)]
    )
    slot(
        [sum_near(1, b[1]), rows_far(0, 0), units_far(2)], [lambda: run_attend_both(2)]
    )
    slot(pair_grad_hops(1, 2) + [sum_far(1, b[1]), rows_near(0, 0)])
    slot(
        [hand_one(1, 1), units_near(2)],
        [lambda: run_project_back(1, 2), lambda: run_attend_back(0)],
    )

    def run_branch_sums():
        run_sums(
            branch_sums,
            [[], [of("active", 1), of("attended", 1)]],
            [[], [of("upstream", 1)]],
            False,
        )

    slot(
        sum_hops(1, b[2]) + [rows_far(0, 1), pair_grad_near(0, 0)],
        [lambda: run_hidden_back(0), run_branch_sums],
    )
    slot([hand(1, 2), rows_near(0, 1)])
    finals = SimpleNamespace()

    def run_final_branch():
        blocks = branch_out(
            order, flags[1], [(k.active, k.attended) for k in b], contract, packed
        )
        finals.keep = jnp.stack(blocks[0::2])
        finals.send = jnp.stack(blocks[1::2])

    def finals_near():
        return finals.send, lambda passed: fold_hops(finals, passed, "tp", 1, (1,))

    def finals_far():
        def go(passed):
            finals.came = hop(passed, "tp", lanes // 2, (1,))
            return finals.came

        return finals.send, go

    def run_expand_sums():
        run_sums(
            expand_sums,
            [[of("second", s)] for s in both],
            [[of("hidden", s)] for s in both],
            True,
        )

    def run_triple_sums():
        run_sums(
            triple_sums,
            [[of("first", s)] for s in both],
            [[of("stacked", s)] for s in both],
            True,
        )

    def run_owner_sums():
        branch_sums.whole = owner_sums(
            order, flags[0], of("all_units", 0), of("own_columns", 0)
        )

    slot(
        [pair_grad_far(0, 0), wide_near(branch_sums)] + column_hops(0),
        [lambda: run_attend_back(2), lambda: run_attend_back(1), lambda: run_hidden_back(2)],
    )
    slot(
        [pair_grad_near(0, 2), pair_grad_near(0, 1)] + column_hops(2),
        [lambda: run_hidden_back(1), run_expand_sums, lambda: run_fold(branch_sums)],
    )
    part = hidden // 2
    slot(
        [
            wide_near(expand_sums),
            pair_grad_far(0, 2),
            pair_grad_far(0, 1),
            wide_far(branch_sums, 0, part),
        ],
        [lambda: run_project_back(0, 0)],
    )
    slot([], [lambda: run_fold(expand_sums)])
    slot(
        [wide_far(expand_sums, 0, half_depth)] + column_hops(1),
        [
            lambda: run_project_back(0, 1),
            lambda: run_project_back(0, 2),
            run_triple_sums,
        ],
    )

    def side_of(mades):
        return sum(
            jnp.concatenate([k.side_first, k.side_second], axis=0) for k in mades
        )

    side = SimpleNamespace(all=jnp.where(first_section, side_of(a), side_of(b)))

    def side_hops(passed):
        step = 1
        while step < spans:
            middle = passed.shape[1] // 2
            came = hop(passed[:, middle:], "ctx", step, both)
            passed = passed[:, :middle] + came
            step *= 2
        step = 1
        while step < lanes:
            came = hop(passed, "tp", step, both)
            passed = passed + came
            step *= 2
        side.all = passed
        return came

    slot(
        [
            wide_near(triple_sums),
            wide_far(expand_sums, half_depth, depth),
            wide_far(branch_sums, part, hidden),
            sum_near(0, a[0]),
            sum_near(0, a[1]),
        ],
        [run_owner_sums],
    )
    slot([], [lambda: run_fold(triple_sums)])
    slot(
        [
            wide_far(triple_sums, 0, half_depth),
            sum_far(0, a[0]),
            sum_far(0, a[1]),
            sum_near(0, a[2]),
        ],
        [run_final_branch],
    )
    slot(
        [
            wide_far(triple_sums, half_depth, depth),
            sum_far(0, a[2]),
            wide_far(branch_sums, hidden, hidden + across_units),
            finals_near(),
            (side.all, side_hops),
        ]
    )
    slot([finals_far()])

    def wide_total(keep, parts):
        came = jnp.concatenate(parts, axis=0) if len(parts) > 1 else parts[0]
        return keep.astype(f32) + came.astype(f32)

    contract_grads = jnp.where(
        first_section,
        branch_sums.whole[:hidden],
        wide_total(branch_sums.keep[:hidden], branch_sums.parts[:2]),
    )
    output_grads = jnp.where(
        first_section,
        branch_sums.whole[hidden:],
        wide_total(branch_sums.keep[hidden:], branch_sums.parts[2:]),
    )
    expand_grads = wide_total(expand_sums.keep, expand_sums.parts)
    triple_grads = wide_total(triple_sums.keep, triple_sums.parts)
    layer_outputs = jnp.stack(
        [
            jnp.where(
                first_section,
                kept[0][m].given,
                (
                    b[m].rows.astype(f32)
                    + finals.keep[m].astype(f32)
                    + finals.came[m].astype(f32)
                ).astype(bf16),
            )
            for m in range(micros)
        ]
    )
    entry_grads = jnp.stack(
        [
            jnp.where(
                first_section,
                norm_back(kept[0][m].rows, total_of(kept[0][m]), inputs[m]),
                kept[1][m].given,
            )
            for m in range(micros)
        ]
    )
    gain_grads = jnp.stack([side.all[0], side.all[2]])
    bias_grads = jnp.stack([side.all[1], side.all[3]])
    return (
        xor_blocks(layer_outputs, span, spans, inverse=True)[None],
        xor_blocks(entry_grads, span, spans, inverse=True)[None],
        triple_grads.reshape(triple_weight.shape),
        output_grads.reshape(output_weight.shape),
        expand_grads[None],
        contract_grads[None],
        gain_grads[None],
        bias_grads[None],
    )


def solution(mesh):
    return jax.shard_map(
        shards,
        mesh=mesh,
        in_specs=(
            P(None, ("ctx", "tp"), None),
            P(None, ("ctx", "tp"), None),
            P("pipe", "ctx", "tp", None, None),
            P("pipe", "tp", None, "ctx"),
            P("pipe", "ctx", "tp"),
            P("pipe", "tp", "ctx"),
            P("pipe", None, "ctx"),
            P("pipe", None, "ctx"),
        ),
        out_specs=(
            P("pipe", None, ("ctx", "tp"), None),
            P("pipe", None, ("ctx", "tp"), None),
            P("pipe", "ctx", "tp", None, None),
            P("pipe", "tp", None, "ctx"),
            P("pipe", "ctx", "tp"),
            P("pipe", "tp", "ctx"),
            P("pipe", None, "ctx"),
            P("pipe", None, "ctx"),
        ),
        check_vma=False,
    )
```

```python
import functools
import math
from types import SimpleNamespace

import jax
import jax.numpy as jnp
from jax import lax
from jax.experimental import pallas as pl
from jax.experimental.pallas import tpu as pltpu
from jax.sharding import PartitionSpec as P

ROT = 64
LANES = 128
epsilon = 1e-05
masked_score = -1e30
f32 = jnp.float32
bf16 = jnp.bfloat16
mebibyte = 1024 * 1024
half_root = 0.7071067811865476
bell = 0.3989422804014327


def dot(a, b, dims):
    return lax.dot_general(a, b, (dims, ((), ())), preferred_element_type=f32)


def plain(a, b):
    return dot(a, b, ((1,), (0,)))


def turned(a, b):
    return dot(a, b, ((1,), (1,)))


def doubling(count):
    order, step = [0], count // 2
    while step:
        order += [k ^ step for k in order]
        step //= 2
    return order


def xor_blocks(values, index, count, inverse=False):
    width = values.shape[-1] // count
    order = doubling(count)

    def taken(places):
        return jnp.concatenate(
            [values[..., k * width : (k + 1) * width] for k in places], axis=-1
        )

    if inverse:
        values = taken([order.index(k) for k in range(count)])
    step = 1
    while step < count:
        swapped = taken([k ^ step for k in range(count)])
        values = jnp.where((index & step) != 0, swapped, values)
        step *= 2
    return values if inverse else taken(order)


def rope_tables(positions):
    half = ROT // 2
    frequency = 10000.0 ** (-jnp.arange(0, ROT, 2, dtype=f32) / ROT)
    angles = positions.astype(f32)[:, None] * frequency[None, :]
    cosine, sine = jnp.cos(angles), jnp.sin(angles)
    count = positions.shape[0]
    rest = jnp.zeros((count, LANES - ROT), f32)
    none = jnp.zeros((count, half), f32)
    return jnp.stack(
        [
            jnp.concatenate([cosine, cosine, rest + 1.0], axis=1),
            jnp.concatenate([-sine, none, rest], axis=1),
            jnp.concatenate([none, sine, rest], axis=1),
        ]
    )


def turn(values, tables, sign):
    half = ROT // 2
    part = values[:, :LANES]
    moved = (
        pltpu.roll(part, LANES - half, 1) * tables[1] + pltpu.roll(part, half, 1) * tables[2]
    )
    part = part * tables[0] + (moved if sign > 0 else -moved)
    return jnp.concatenate([part, values[:, LANES:]], axis=1)


def normalize(values):
    center = values - jnp.mean(values, axis=-1, keepdims=True)
    inverse = lax.rsqrt(jnp.mean(center * center, axis=-1, keepdims=True) + epsilon)
    return (center * inverse, inverse)


def whole(array):
    zeros = (0,) * array.ndim
    return pl.BlockSpec(array.shape, lambda *_: zeros)


def at(block, place):
    return pl.BlockSpec(block, lambda *_: place)


kept_out = pl.BlockSpec(memory_space=pl.ANY)


def shape(dims, dtype=bf16):
    return jax.ShapeDtypeStruct(dims, dtype)


class Order:
    def __init__(self):
        self.last = []

    def follow(self, results):
        self.last = [min(results, key=lambda array: array.size * array.dtype.itemsize)]

    def also(self, array):
        self.last = self.last + [array]


took = dict(
    project=7,
    expand=8,
    attend=5,
    branch=8,
    hidden_both=14,
    attend_both=11,
    attend_back=8,
    hidden_back=13,
    project_back=8,
    weight_sums=16,
    fold=7,
)
peak = 1.15e9


def run(order, flags, kernel, ins, outs, scratch, name, grid=(1,), work=0):
    taken = len(ins)
    ins = [(flags, pl.BlockSpec(memory_space=pltpu.SMEM))] + list(ins)
    ins += [(array, kept_out) for array in order.last]
    arrays = [array for array, _ in ins]
    once = grid == (1,)

    def sized(spec, dtype):
        if spec.block_shape is None:
            return spec, 0
        size = math.prod(spec.block_shape) * jnp.dtype(dtype).itemsize
        if not once:
            return spec, 2 * size
        single = pl.BlockSpec(
            spec.block_shape, spec.index_map, pipeline_mode=pl.Buffered(1)
        )
        return single, size

    in_specs = [sized(spec, array.dtype) for array, spec in ins]
    out_specs = [sized(spec, struct.dtype) for struct, spec in outs]
    held = sum(size for _, size in in_specs + out_specs)
    for buffer in scratch:
        if buffer.memory_space == pltpu.VMEM:
            held += math.prod(buffer.shape) * jnp.dtype(buffer.dtype).itemsize

    def body(flag_ref, *refs):
        @pl.when(flag_ref[0] == 1)
        def _():
            kernel(flag_ref, *refs[:taken], *refs[len(ins) - 1 :])

    results = pl.pallas_call(
        body,
        grid=grid,
        in_specs=[spec for spec, _ in in_specs],
        out_specs=[spec for spec, _ in out_specs],
        out_shape=[struct for struct, _ in outs],
        scratch_shapes=scratch,
        compiler_params=pltpu.CompilerParams(
            vmem_limit_bytes=int(held + (work + 4) * mebibyte)
        ),
        cost_estimate=pl.CostEstimate(
            flops=int(took[name] * peak), bytes_accessed=0, transcendentals=0
        ),
        name=name,
    )(*arrays)
    order.follow(results)
    return results


def fence(through, waits):
    count = len(through)

    def kernel(*refs):
        pass

    return pl.pallas_call(
        kernel,
        in_specs=[kept_out] * (count + len(waits)),
        out_specs=[kept_out] * count,
        out_shape=[shape(array.shape, array.dtype) for array in through],
        input_output_aliases={j: j for j in range(count)},
        compiler_params=pltpu.CompilerParams(vmem_limit_bytes=mebibyte),
        cost_estimate=pl.CostEstimate(flops=1, bytes_accessed=1, transcendentals=0),
        name="fence",
    )(*through, *waits)


def full_out(dims, dtype=bf16):
    zeros = (0,) * len(dims)
    return (shape(dims, dtype), pl.BlockSpec(dims, lambda *_: zeros))


def copies(sources, targets, sems):
    started = []
    for source, target, sem in zip(sources, targets, sems):
        copy = pltpu.make_async_copy(source, target, sem)
        copy.start()
        started.append(copy)
    return started


def project(order, flags, pieces, at_piece, gains, biases, tables, weights, heads, head_dim):
    count, width = 1, pieces[0].shape[2]
    span_rows = sum(piece.shape[1] for piece in pieces)
    rows = count * span_rows
    chunk = pieces[0].shape[1]
    spans = len(weights)
    depth = width // spans
    wide = 3 * head_dim
    columns = heads * wide

    def kernel(flag_ref, *refs):
        piece_refs = refs[: len(pieces)]
        gain_ref, bias_ref, table_ref = refs[len(pieces) : len(pieces) + 3]
        weight_refs = refs[len(pieces) + 3 : len(pieces) + 3 + spans]
        first, second, normal, queries, pair, held, sems = refs[len(pieces) + 3 + spans :]
        started = []
        for h in range(heads):
            started.append(
                copies(
                    [w.at[:depth, h * wide : (h + 1) * wide] for w in weight_refs],
                    [held.at[h, k * depth : (k + 1) * depth] for k in range(spans)],
                    [sems.at[h, k] for k in range(spans)],
                )
            )
        start = 0
        for piece_ref in piece_refs:
            chunks = piece_ref.shape[1] // chunk

            def one(i, _, piece_ref=piece_ref, start=start, chunks=chunks):
                m, c = i // chunks, i % chunks
                values = piece_ref[m, pl.ds(pl.multiple_of(c * chunk, chunk), chunk), :]
                normed, _ = normalize(values.astype(f32))
                to = pl.ds(
                    pl.multiple_of(m * span_rows + start + c * chunk, chunk), chunk
                )
                normal[to, :] = normed.astype(bf16)
                first[to, :] = (normed * gain_ref[0:1] + bias_ref[0:1]).astype(bf16)
                second[to, :] = (normed * gain_ref[1:2] + bias_ref[1:2]).astype(bf16)
                return 0

            lax.fori_loop(0, count * chunks, one, 0)
            start += piece_ref.shape[1]
        for h in range(heads):
            for copy in started[h]:
                copy.wait()

            def two(m, _, h=h):
                to = pl.ds(pl.multiple_of(m * span_rows, span_rows), span_rows)
                made = plain(first[to, :], held[h])
                queries[h, to, :] = turn(made[:, :head_dim], table_ref, 1).astype(bf16)
                pair[0, h, to, :] = turn(
                    made[:, head_dim : 2 * head_dim], table_ref, 1
                ).astype(bf16)
                pair[1, h, to, :] = made[:, 2 * head_dim :].astype(bf16)
                return 0

            lax.fori_loop(0, count, two, 0)

    ins = [(piece, at((1,) + piece.shape[1:], (at_piece, 0, 0))) for piece in pieces]
    ins += [(array, whole(array)) for array in (gains, biases, tables)]
    ins += [(w, kept_out) for w in weights]
    outs = [full_out((rows, width))] * 3 + [
        full_out((heads, rows, head_dim)),
        full_out((2, heads, rows, head_dim)),
    ]
    scratch = [
        pltpu.VMEM((heads, width, wide), bf16),
        pltpu.SemaphoreType.DMA((heads, spans)),
    ]
    return run(order, flags, kernel, ins, outs, scratch, "project")


def expand_up(order, flags, second, weights, span_rows):
    rows, width = second.shape
    depth, hidden = weights[0].shape
    spans = len(weights)
    tile = min(512, hidden)
    tiles = hidden // tile

    def kernel(flag_ref, *refs):
        second_ref, weight_refs = refs[0], refs[1 : 1 + spans]
        active, slope, held, sems = refs[1 + spans :]
        started = []
        for t in range(tiles):
            started.append(
                copies(
                    [w.at[:, t * tile : (t + 1) * tile] for w in weight_refs],
                    [held.at[t, k * depth : (k + 1) * depth] for k in range(spans)],
                    [sems.at[t, k] for k in range(spans)],
                )
            )
        for t in range(tiles):
            for copy in started[t]:
                copy.wait()

            def one(m, _, t=t):
                to = pl.ds(pl.multiple_of(m * span_rows, span_rows), span_rows)
                pre = plain(second_ref[to, :], held[t])
                risen = 0.5 * (1.0 + lax.erf(pre * half_root))
                columns = slice(t * tile, (t + 1) * tile)
                active[to, columns] = (pre * risen).astype(bf16)
                slope[to, columns] = (
                    risen + pre * jnp.exp(-0.5 * pre * pre) * bell
                ).astype(bf16)
                return 0

            lax.fori_loop(0, rows // span_rows, one, 0)

    ins = [(second, whole(second))] + [(w, kept_out) for w in weights]
    outs = [full_out((rows, hidden))] * 2
    scratch = [
        pltpu.VMEM((tiles, width, tile), bf16),
        pltpu.SemaphoreType.DMA((tiles, spans)),
    ]
    return run(order, flags, kernel, ins, outs, scratch, "expand")


def spread(refs):
    return [ref.at[j] for ref in refs for j in range(ref.shape[0])]


def attention(here, pairs, head, row_ref, key_ref, scale):
    scores = []
    for k, pair in enumerate(pairs):
        raw = turned(here, pair[0, head]) * scale
        scores.append(jnp.where(key_ref[k] <= row_ref[...], raw, masked_score))
    top = functools.reduce(
        jnp.maximum, [jnp.max(part, axis=1, keepdims=True) for part in scores]
    )
    scores = [jnp.exp(part - top) for part in scores]
    inverse = 1.0 / sum(jnp.sum(part, axis=1, keepdims=True) for part in scores)
    return [part * inverse for part in scores]


def attend(order, flags, queries, pairs, positions, key_positions, scale):
    heads, rows, head_dim = queries.shape
    spans = sum(pair.shape[0] for pair in pairs)

    def kernel(flag_ref, query_ref, *refs):
        views, refs = spread(refs[: len(pairs)]), refs[len(pairs) :]
        row_ref, key_ref, attended, probs = refs
        for h in range(heads):
            parts = attention(query_ref[h], views, h, row_ref, key_ref, scale)
            summed = None
            for k in range(spans):
                part = parts[k].astype(bf16)
                probs[k, h] = part
                term = plain(part, views[k][1, h])
                summed = term if summed is None else summed + term
            attended[:, h * head_dim : (h + 1) * head_dim] = summed.astype(bf16)

    ins = [
        (array, whole(array)) for array in (queries, *pairs, positions, key_positions)
    ]
    outs = [full_out((rows, heads * head_dim)), full_out((spans, heads, rows, rows))]
    work = spans * rows * rows * 4 * heads * 4 / mebibyte
    return run(order, flags, kernel, ins, outs, [], "attend", work=work)


def attention_grads(grad, here, parts, views, head, keep, send, scale):
    half = keep.shape[0]
    grad_probs = [turned(grad, view[1, head]) for view in views]
    delta = sum(
        jnp.sum(part.astype(f32) * slope, axis=1, keepdims=True)
        for part, slope in zip(parts, grad_probs)
    )
    query_grad = None
    for k, view in enumerate(views):
        slopes = (parts[k].astype(f32) * (grad_probs[k] - delta)).astype(bf16)
        term = plain(slopes, view[0, head])
        query_grad = term if query_grad is None else query_grad + term
        side = keep if k < half else send
        side[k % half, 0, head] = (dot(slopes, here, ((0,), (0,))) * scale).astype(bf16)
        side[k % half, 1, head] = dot(parts[k].astype(bf16), grad, ((0,), (0,))).astype(bf16)
    return query_grad * scale


def attend_both(
    order, flags, rows_in, packed, queries, pairs, positions, key_positions, tables, scale
):
    heads, rows, head_dim = queries.shape
    width = rows_in.shape[1]
    spans = len(packed)
    across, depth = heads * head_dim, width // spans
    half = spans // 2

    def kernel(flag_ref, rows_ref, *refs):
        packed_refs, refs = refs[:spans], refs[spans:]
        query_ref, refs = refs[0], refs[1:]
        views, refs = spread(refs[: len(pairs)]), refs[len(pairs) :]
        row_ref, key_ref, table_ref, attended, turned_back, keep, send, held, sems = refs
        started = copies(
            [w.at[:across, 3 * across : 3 * across + depth] for w in packed_refs],
            [held.at[:, k * depth : (k + 1) * depth] for k in range(spans)],
            [sems.at[k] for k in range(spans)],
        )
        all_parts = []
        for h in range(heads):
            parts = attention(query_ref[h], views, h, row_ref, key_ref, scale)
            summed = None
            for k in range(spans):
                term = plain(parts[k].astype(bf16), views[k][1, h])
                summed = term if summed is None else summed + term
            attended[:, h * head_dim : (h + 1) * head_dim] = summed.astype(bf16)
            all_parts.append(parts)
        for copy in started:
            copy.wait()
        grads = turned(rows_ref[...], held[...]).astype(bf16)
        for h in range(heads):
            made = attention_grads(
                grads[:, h * head_dim : (h + 1) * head_dim],
                query_ref[h],
                all_parts[h],
                views,
                h,
                keep,
                send,
                scale,
            )
            turned_back[h] = turn(made, table_ref, -1).astype(bf16)

    ins = [(rows_in, whole(rows_in))] + [(w, kept_out) for w in packed]
    ins += [
        (array, whole(array)) for array in (queries, *pairs, positions, key_positions, tables)
    ]
    outs = [full_out((rows, across)), full_out((heads, rows, head_dim))]
    outs += [full_out((half, 2, heads, rows, head_dim))] * 2
    scratch = [pltpu.VMEM((across, width), bf16), pltpu.SemaphoreType.DMA((spans,))]
    work = spans * rows * rows * 4 * (heads + 4) / mebibyte
    return run(order, flags, kernel, ins, outs, scratch, "attend_both", work=work)


def hidden_both(order, flags, second, pieces, at_piece, expand, contract, normal, gains):
    rows, width = second.shape
    hidden, depth = contract[0].shape
    spans = len(contract)
    tile = min(512, hidden)
    tiles = hidden // tile

    def kernel(flag_ref, second_ref, *refs):
        piece_refs, refs = refs[: len(pieces)], refs[len(pieces) :]
        expand_refs, refs = refs[:spans], refs[spans:]
        contract_refs, refs = refs[:spans], refs[spans:]
        normal_ref, gain_ref, rows_out, active, grads, part, side, *refs = refs
        held_up, held_down, sems_up, sems_down = refs
        started = []
        for t in range(tiles):
            block = slice(t * tile, (t + 1) * tile)
            places = [slice(k * depth, (k + 1) * depth) for k in range(spans)]
            up = copies(
                [w.at[:, block] for w in expand_refs],
                [held_up.at[place, block] for place in places],
                [sems_up.at[t, k] for k in range(spans)],
            )
            down = copies(
                [w.at[block, :] for w in contract_refs],
                [held_down.at[block, place] for place in places],
                [sems_down.at[t, k] for k in range(spans)],
            )
            started.append((up, down))
        start = 0
        for piece_ref in piece_refs:
            size = piece_ref.shape[1]
            rows_out[start : start + size, :] = piece_ref[0]
            start += size
        for t in range(tiles):
            block = slice(t * tile, (t + 1) * tile)
            for copy in started[t][0] + started[t][1]:
                copy.wait()
            pre = plain(second_ref[...], held_up[:, block])
            risen = 0.5 * (1.0 + lax.erf(pre * half_root))
            active[:, block] = (pre * risen).astype(bf16)
            slope = risen + pre * jnp.exp(-0.5 * pre * pre) * bell
            grads[:, block] = (turned(rows_out[...], held_down[block, :]) * slope).astype(bf16)
        for k in range(spans):
            place = slice(k * depth, (k + 1) * depth)
            made = turned(grads[...], held_up[place, :])
            side[0:1, place] = jnp.sum(
                made * normal_ref[:, place].astype(f32), axis=0, keepdims=True
            )
            side[1:2, place] = jnp.sum(made, axis=0, keepdims=True)
            part[:, place] = made * gain_ref[1:2, place]

    ins = [(second, whole(second))]
    ins += [(piece, at((1,) + piece.shape[1:], (at_piece, 0, 0))) for piece in pieces]
    ins += [(w, kept_out) for w in expand] + [(w, kept_out) for w in contract]
    ins += [(normal, whole(normal)), (gains, whole(gains))]
    outs = [
        full_out((rows, width)),
        full_out((rows, hidden)),
        full_out((rows, hidden)),
        full_out((rows, width), f32),
        full_out((2, width), f32),
    ]
    scratch = [
        pltpu.VMEM((width, hidden), bf16),
        pltpu.VMEM((hidden, width), bf16),
        pltpu.SemaphoreType.DMA((tiles, spans)),
        pltpu.SemaphoreType.DMA((tiles, spans)),
    ]
    return run(order, flags, kernel, ins, outs, scratch, "hidden_both")


def branch_out(order, flags, groups, contract, packed):
    hidden, depth = contract[0].shape
    across = groups[0][1].shape[1]
    spans = len(contract)
    width = depth * spans
    span_rows = groups[0][0].shape[0]
    block = span_rows // 2
    count = len(groups)

    def kernel(flag_ref, *refs):
        group_refs, refs = refs[: 2 * count], refs[2 * count :]
        contract_refs, packed_refs = refs[:spans], refs[spans : 2 * spans]
        blocks, refs = refs[2 * spans : 2 * (spans + count)], refs[2 * (spans + count) :]
        held, held_out, sems = refs
        outputs = [w.at[:across, 3 * across : 3 * across + depth] for w in packed_refs]
        started = copies(
            [ref for k in range(spans) for ref in (outputs[k], contract_refs[k])],
            [ref for k in range(spans) for ref in (held_out.at[k], held.at[k])],
            [sems.at[j] for j in range(2 * spans)],
        )
        for k in range(spans):
            started[2 * k].wait()
            started[2 * k + 1].wait()
            columns = slice(k * depth, (k + 1) * depth)
            for c in range(count):
                made = plain(group_refs[2 * c + 1][...], held_out[k])
                made = made + plain(group_refs[2 * c][...], held[k])
                blocks[2 * c][:, columns] = made[:block].astype(bf16)
                blocks[2 * c + 1][:, columns] = made[block:].astype(bf16)

    ins = []
    for active, attended in groups:
        ins += [(active, whole(active)), (attended, whole(attended))]
    ins += [(w, kept_out) for w in contract] + [(w, kept_out) for w in packed]
    outs = [full_out((block, width))] * (2 * count)
    scratch = [
        pltpu.VMEM((spans, hidden, depth), bf16),
        pltpu.VMEM((spans, across, depth), bf16),
        pltpu.SemaphoreType.DMA((2 * spans,)),
    ]
    return run(order, flags, kernel, ins, outs, scratch, "branch")


def attend_back(order, flags, pieces, packed, queries, pairs, probs, tables, scale):
    rows = sum(piece.shape[1] for piece in pieces)
    width = pieces[0].shape[2]
    heads, _, head_dim = queries.shape
    spans = len(packed)
    across, depth = heads * head_dim, width // spans
    half = spans // 2

    def kernel(flag_ref, *refs):
        piece_refs, refs = refs[: len(pieces)], refs[len(pieces) :]
        packed_refs, refs = refs[:spans], refs[spans:]
        query_ref, refs = refs[0], refs[1:]
        views, refs = spread(refs[: len(pairs)]), refs[len(pairs) :]
        prob_ref, table_ref, rows_out, turned_back, keep, send, held, sems = refs
        started = copies(
            [w.at[:across, 3 * across : 3 * across + depth] for w in packed_refs],
            [held.at[:, k * depth : (k + 1) * depth] for k in range(spans)],
            [sems.at[k] for k in range(spans)],
        )
        start = 0
        for piece_ref in piece_refs:
            size = piece_ref.shape[1]
            rows_out[start : start + size, :] = piece_ref[0]
            start += size
        for copy in started:
            copy.wait()
        grads = turned(rows_out[...], held[...]).astype(bf16)
        for h in range(heads):
            made = attention_grads(
                grads[:, h * head_dim : (h + 1) * head_dim],
                query_ref[h],
                [prob_ref[k, h] for k in range(spans)],
                views,
                h,
                keep,
                send,
                scale,
            )
            turned_back[h] = turn(made, table_ref, -1).astype(bf16)

    ins = [(piece, whole(piece)) for piece in pieces] + [(w, kept_out) for w in packed]
    ins += [(array, whole(array)) for array in (queries, *pairs, probs, tables)]
    outs = [full_out((rows, width)), full_out((heads, rows, head_dim))]
    outs += [full_out((half, 2, heads, rows, head_dim))] * 2
    scratch = [pltpu.VMEM((across, width), bf16), pltpu.SemaphoreType.DMA((spans,))]
    work = spans * rows * rows * 4 * 4 / mebibyte
    return run(order, flags, kernel, ins, outs, scratch, "attend_back", work=work)


def hidden_back(order, flags, upstream, contract, expand, slope, normal, gains):
    span_rows, width = upstream.shape
    hidden, depth = contract[0].shape
    spans = len(contract)
    tile = min(512, hidden)
    tiles = hidden // tile

    def kernel(flag_ref, *refs):
        upstream_ref, refs = refs[0], refs[1:]
        contract_refs, refs = refs[:spans], refs[spans:]
        expand_refs, refs = refs[:spans], refs[spans:]
        slope_ref, normal_ref, gain_ref, grads, part, side, held, held_up, sems, sems_up = refs
        started = [
            copies(
                [w.at[t * tile : (t + 1) * tile, :] for w in contract_refs],
                [held.at[t, :, k * depth : (k + 1) * depth] for k in range(spans)],
                [sems.at[t, k] for k in range(spans)],
            )
            for t in range(tiles)
        ]
        started_up = copies(
            expand_refs, [held_up.at[k] for k in range(spans)], [sems_up.at[k] for k in range(spans)]
        )
        for t in range(tiles):
            for copy in started[t]:
                copy.wait()
            columns = slice(t * tile, (t + 1) * tile)
            grads[:, columns] = (
                turned(upstream_ref[...], held[t]) * slope_ref[:, columns].astype(f32)
            ).astype(bf16)
        for k in range(spans):
            started_up[k].wait()
            made = turned(grads[...], held_up[k])
            columns = slice(k * depth, (k + 1) * depth)
            side[0:1, columns] = jnp.sum(
                made * normal_ref[:, columns].astype(f32), axis=0, keepdims=True
            )
            side[1:2, columns] = jnp.sum(made, axis=0, keepdims=True)
            part[:, columns] = made * gain_ref[1:2, columns]

    ins = [(upstream, whole(upstream))]
    ins += [(w, kept_out) for w in contract] + [(w, kept_out) for w in expand]
    ins += [
        (slope, whole(slope)),
        (normal, whole(normal)),
        (gains, whole(gains)),
    ]
    outs = [
        full_out((span_rows, hidden)),
        full_out((span_rows, width), f32),
        full_out((2, width), f32),
    ]
    scratch = [
        pltpu.VMEM((tiles, tile, width), bf16),
        pltpu.VMEM((spans, depth, hidden), bf16),
        pltpu.SemaphoreType.DMA((tiles, spans)),
        pltpu.SemaphoreType.DMA((spans,)),
    ]
    return run(order, flags, kernel, ins, outs, scratch, "hidden_back")


def project_back(
    order, flags, turned_back, own, came, weights, part, normal, gains, tables
):
    heads, span_rows, head_dim = turned_back.shape
    spans = len(weights)
    width = part.shape[1]
    depth, columns = width // spans, 3 * heads * head_dim
    block = span_rows // 2

    def kernel(flag_ref, *refs):
        query_ref, own_ref, came_ref, refs = refs[0], refs[1], refs[2], refs[3:]
        weight_refs, refs = refs[:spans], refs[spans:]
        part_ref, normal_ref, gain_ref, table_ref, grads, side, *refs = refs
        low, high, held, sems = refs
        started = copies(
            [w.at[:depth, :columns] for w in weight_refs],
            [held.at[k] for k in range(spans)],
            [sems.at[k] for k in range(spans)],
        )
        for h in range(heads):
            at_column = h * 3 * head_dim
            keys = own_ref[0, h].astype(f32) + came_ref[0, h].astype(f32)
            values = own_ref[1, h].astype(f32) + came_ref[1, h].astype(f32)
            grads[:, at_column : at_column + head_dim] = query_ref[h]
            grads[:, at_column + head_dim : at_column + 2 * head_dim] = turn(
                keys, table_ref, -1
            ).astype(bf16)
            grads[:, at_column + 2 * head_dim : at_column + 3 * head_dim] = values.astype(bf16)
        for k in range(spans):
            started[k].wait()
            made = turned(grads[...], held[k])
            span_columns = slice(k * depth, (k + 1) * depth)
            side[0:1, span_columns] = jnp.sum(
                made * normal_ref[:, span_columns].astype(f32), axis=0, keepdims=True
            )
            side[1:2, span_columns] = jnp.sum(made, axis=0, keepdims=True)
            both = (made * gain_ref[0:1, span_columns] + part_ref[:, span_columns]).astype(bf16)
            low[:, span_columns] = both[:block]
            high[:, span_columns] = both[block:]

    ins = [(array, whole(array)) for array in (turned_back, own, came)]
    ins += [(w, kept_out) for w in weights]
    ins += [(part, whole(part)), (normal, whole(normal))]
    ins += [(gains, whole(gains)), (tables, whole(tables))]
    outs = [full_out((span_rows, columns)), full_out((2, width), f32)]
    outs += [full_out((block, width))] * 2
    scratch = [pltpu.VMEM((spans, depth, columns), bf16), pltpu.SemaphoreType.DMA((spans,))]
    return run(order, flags, kernel, ins, outs, scratch, "project_back")


def weight_sums(order, flags, lefts, rights, by_rows, spans):
    rows = sum(piece.shape[0] for piece in lefts[0][0])
    left_width = sum(group[0].shape[1] for group in lefts[0])
    right_width = sum(group[0].shape[1] for group in rights[0])
    if by_rows:
        tile = left_width // spans
        steps, block = spans // 2, (tile, right_width)
    else:
        tile = min(512, left_width)
        while left_width % tile:
            tile //= 2
        steps, block = left_width // tile, (tile, right_width // 2)
    chunk = min(1024, block[1])
    while right_width % chunk:
        chunk //= 2
    pieces = [
        [piece for groups in (lefts[s], rights[s]) for group in groups for piece in group]
        for s in (0, 1)
    ]
    most = max(len(p) for p in pieces)

    def kernel(flag_ref, *refs):
        piece_refs = (refs[: len(pieces[0])], refs[len(pieces[0]) : len(pieces[0]) + len(pieces[1])])
        keep, send, left, right, flipped, sems = refs[len(pieces[0]) + len(pieces[1]) :]
        g = pl.program_id(0)
        for s in (0, 1):

            @pl.when((g == 0) & (flag_ref[2] == s))
            def _(s=s):
                targets = []
                for held, groups in ((left, lefts[s]), (right, rights[s])):
                    column = 0
                    for group in groups:
                        row, wide = 0, group[0].shape[1]
                        for piece in group:
                            targets.append(
                                held.at[row : row + piece.shape[0], column : column + wide]
                            )
                            row += piece.shape[0]
                        column += wide
                started = copies(
                    piece_refs[s], targets, [sems.at[j] for j in range(len(targets))]
                )
                for copy in started:
                    copy.wait()

        def product(column, store):
            flipped[...] = left[:, pl.ds(pl.multiple_of(column, LANES), tile)].T

            def one(c, _):
                columns = pl.ds(pl.multiple_of(c * chunk, chunk), chunk)
                store(c, plain(flipped[...], right[:, columns]).astype(bf16))
                return 0

            lax.fori_loop(0, right_width // chunk, one, 0)

        if by_rows:

            def to(target):
                def store(c, made):
                    target[:, pl.ds(pl.multiple_of(c * chunk, chunk), chunk)] = made

                return store

            product(g * tile, to(keep))
            product((g + steps) * tile, to(send))
        else:
            half = right_width // 2 // chunk

            def store(c, made):
                @pl.when(c < half)
                def _():
                    keep[:, pl.ds(pl.multiple_of(c * chunk, chunk), chunk)] = made

                @pl.when(c >= half)
                def _():
                    send[:, pl.ds(pl.multiple_of((c - half) * chunk, chunk), chunk)] = made

            product(g * tile, store)

    ins = [(piece, kept_out) for s in (0, 1) for piece in pieces[s]]
    dims = (steps * tile, block[1])
    outs = [(shape(dims), pl.BlockSpec(block, lambda g: (g, 0)))] * 2
    scratch = [
        pltpu.VMEM((rows, left_width), bf16),
        pltpu.VMEM((rows, right_width), bf16),
        pltpu.VMEM((tile, rows), bf16),
        pltpu.SemaphoreType.DMA((most,)),
    ]
    return run(
        order, flags, kernel, ins, outs, scratch, "weight_sums", grid=(steps,)
    )


def fold(order, flags, keep, came, dim):
    rows, columns = keep.shape
    if dim == 0:
        tile = rows // 4
        steps, block = rows // 2 // tile, (tile, columns)
        places = [lambda g: (g, 0), lambda g: (g + steps, 0)]
        half = (rows // 2, columns)
    else:
        tile = rows // 4
        steps, block = rows // tile, (tile, columns // 2)
        places = [lambda g: (g, 0), lambda g: (g, 1)]
        half = (rows, columns // 2)

    def kernel(flag_ref, keep_low, keep_high, came_low, came_high, low, high):
        low[...] = (keep_low[...].astype(f32) + came_low[...].astype(f32)).astype(bf16)
        high[...] = (keep_high[...].astype(f32) + came_high[...].astype(f32)).astype(bf16)

    ins = [(array, pl.BlockSpec(block, place)) for array in (keep, came) for place in places]
    outs = [(shape(half), pl.BlockSpec(block, lambda g: (g, 0)))] * 2
    return run(order, flags, kernel, ins, outs, [], "fold", grid=(steps,))


def shards(
    block_input,
    out_grad,
    triple_weight,
    output_weight,
    expand_weight,
    contract_weight,
    norm_gains,
    norm_biases,
):
    section = lax.axis_index("pipe")
    span = lax.axis_index("ctx")
    lane = lax.axis_index("tp")
    spans = lax.axis_size("ctx")
    lanes = lax.axis_size("tp")
    micros, rows, width = block_input.shape
    span_rows = rows * lanes
    heads = triple_weight.shape[2]
    head_dim = triple_weight.shape[4]
    across_units = heads * head_dim
    scale = head_dim ** (-0.5)
    first_section = section == 0
    both = (0, 1)

    def hop(array, axis, step, sections):
        size = lax.axis_size(axis)
        pairs = [(s * size + a, s * size + (a ^ step)) for s in sections for a in range(size)]
        return lax.ppermute(array, ("pipe", axis), pairs)

    order = Order()

    def flags_for(wanted):
        return jnp.stack([jnp.asarray(wanted), span, section]).astype(jnp.int32)

    flags = [flags_for(section == s) for s in both]
    always = flags_for(1)

    kept = [[SimpleNamespace() for _ in range(micros)] for _ in both]
    due = {}
    slot_index = [0]

    def slot(hops, kernels=()):
        now = slot_index[0]
        slot_index[0] += 1
        ready = due.pop(now, [])
        hops = [h if len(h) == 3 else h + (1,) for h in hops]
        if hops:
            gated = fence([operand for operand, _, _ in hops], order.last + ready)
            order.last = [min(gated, key=lambda array: array.size)]
            for passed, (_, go, slots) in zip(gated, hops):
                results = go(passed)
                results = results if isinstance(results, list) else [results]
                due.setdefault(now + slots, []).extend(results)
        else:
            order.last = order.last + ready
        for kernel in kernels:
            kernel()

    def halved(keep, came, dim):
        middle = keep.shape[dim] // 2
        total = keep.astype(f32) + came.astype(f32)
        return (
            lax.slice_in_dim(total, 0, middle, axis=dim).astype(bf16),
            lax.slice_in_dim(total, middle, 2 * middle, axis=dim).astype(bf16),
        )

    def spread_hops(pieces, axis, axis_name, sections, first):
        step = lax.axis_size(axis_name) // 4
        going = first
        while step:
            pieces.append(hop(going, axis_name, step, sections))
            going = jnp.concatenate(pieces, axis=axis)
            step //= 2
        return pieces[-1]

    def fold_hops(k, first, axis_name, dim, sections):
        step, size = 1, lax.axis_size(axis_name)
        while 2 * step < size:
            came = hop(first, axis_name, step, sections)
            k.keep, k.send = halved(k.keep, came, dim)
            first = k.send
            step *= 2
        return came

    depth = width // spans
    far = spans // 2
    assert depth == across_units
    small = jnp.concatenate([norm_gains[0], norm_biases[0]], axis=0)
    packed = jnp.concatenate(
        [triple_weight[0].reshape(depth, -1), output_weight[0].reshape(-1, depth)],
        axis=1,
    )
    packed = jnp.pad(packed, ((0, 16), (0, 0)))
    packed = lax.dynamic_update_slice(packed, small, (depth, 0))
    own_expand, own_contract = expand_weight[0], contract_weight[0]
    hidden = own_expand.shape[1]
    inputs = xor_blocks(block_input, span, spans)
    cotangent = xor_blocks(out_grad, span, spans)
    early = jnp.where(first_section, inputs, cotangent)

    in_row = jnp.arange(rows, dtype=jnp.int32)
    in_span = jnp.concatenate([(lane ^ j) * rows + in_row for j in doubling(lanes)])
    positions = span * span_rows + in_span
    key_positions = jnp.stack([(span ^ k) * span_rows + in_span for k in doubling(spans)])
    tables = rope_tables(positions)
    position_column = positions[:, None]
    key_positions = key_positions[:, None, :]

    def blocks_of(own, came):
        held, step = {0: own, far: came}, far // 2
        while step:
            for k in list(held):
                held[k ^ step] = hop(held[k], "ctx", step, both)
            step //= 2
        return [held[k] for k in doubling(spans)]

    lane_offsets = doubling(lanes)

    def across(array, j, source):
        pairs = [(source * lanes + a, (1 - source) * lanes + (a ^ j)) for a in range(lanes)]
        return lax.ppermute(array, ("pipe", "tp"), pairs)

    def rows_far(s, m):
        k = kept[s][m]

        def go(passed):
            k.rows = passed
            k.pieces = [passed, hop(passed, "tp", lanes // 2, (s,))]
            return k.pieces[1]

        return k.rows, go

    def rows_near(s, m):
        k = kept[s][m]

        def go(passed):
            last_piece = spread_hops(k.pieces, 0, "tp", (s,), passed)
            k.row_pieces = [piece[None] for piece in k.pieces]
            return last_piece

        return jnp.concatenate(k.pieces, axis=0), go

    def one_way(array, direction, s):
        pairs = [
            (s * spans + a, s * spans + (a ^ far))
            for a in range(spans)
            if direction * ((a ^ far) - a) > 0
        ]
        return lax.ppermute(array, ("pipe", "ctx"), pairs)

    def pair_far(s, m):
        k = kept[s][m]

        def go(passed):
            k.pairs = [passed, one_way(passed, 1, s)]
            return k.pairs[1]

        return k.pair, go

    def pair_near(s, m):
        k = kept[s][m]

        def go(passed):
            return spread_hops(k.pairs, 0, "ctx", (s,), passed)

        return jnp.concatenate(k.pairs, axis=0), go

    def pair_grad_near(s, m):
        k = kept[s][m].pair_grad
        return k.send, lambda passed: fold_hops(k, passed, "ctx", 0, (s,))

    def pair_grad_far(s, m):
        k = kept[s][m].pair_grad

        def go(passed):
            k.came = one_way(passed, -1, s)
            return k.came

        return k.send, go

    def sum_near(s, k):
        k.keep, going = k.blocks
        return going, lambda passed: fold_hops(k, passed, "tp", 0, (s,))

    def sum_far(s, k):
        def go(passed):
            k.blocks, k.arrived = [k.keep], [hop(passed, "tp", lanes // 2, (s,))]
            return k.arrived[0]

        return k.send, go

    def total_of(k):
        return sum(array.astype(f32) for array in [k.blocks[0], *k.arrived])

    def norm_back(upstream, combined, entering):
        normalized, inverse = normalize(entering.astype(f32))
        return (
            upstream.astype(f32)
            + inverse
            * (
                combined
                - jnp.mean(combined, axis=-1, keepdims=True)
                - normalized * jnp.mean(combined * normalized, axis=-1, keepdims=True)
            )
        ).astype(bf16)

    def middle_of(m):
        return (inputs[m].astype(f32) + total_of(kept[0][m])).astype(bf16)

    def entry_of(m):
        k = kept[1][m]
        return norm_back(cotangent[m], total_of(k), k.rows)

    def hand_one(s, m):
        k, other = kept[s][m], kept[1 - s][m]
        k.given = middle_of(m) if s == 0 else entry_of(m)

        def go(passed):
            k.given = passed
            other.rows = across(passed, 0, s)
            return other.rows

        return k.given, go

    def run_project(s, m):
        k = kept[s][m]
        pieces, place = (early_pieces, m) if s == 0 else (k.row_pieces, 0)
        k.first, k.second, k.normal, k.queries, pair = project(
            order, flags[s], pieces, place, gains, biases, tables, packed, heads, head_dim
        )
        k.pair = pair[None]

    def run_expand(m):
        k = kept[0][m]
        k.active, k.slope = expand_up(order, flags[0], k.second, weights.expand, span_rows)

    def run_attend(m):
        k = kept[0][m]
        k.attended, k.probs = attend(
            order, flags[0], k.queries, k.pairs, position_column, key_positions, scale
        )

    def run_branch(m):
        k = kept[0][m]
        k.blocks = branch_out(
            order, flags[0], [(k.active, k.attended)], contract, packed
        )

    def run_hidden_both(m):
        k = kept[1][m]
        k.upstream, k.active, k.hidden, k.part, k.side_second = hidden_both(
            order,
            flags[1],
            k.second,
            early_pieces,
            m,
            weights.expand,
            contract,
            k.normal,
            gains,
        )

    def run_attend_both(m):
        k = kept[1][m]
        k.attended, k.turned_back, keep, send = attend_both(
            order,
            flags[1],
            k.upstream,
            packed,
            k.queries,
            k.pairs,
            position_column,
            key_positions,
            tables,
            scale,
        )
        k.pair_grad = SimpleNamespace(keep=keep, send=send)

    def run_attend_back(m):
        k = kept[0][m]
        k.upstream, k.turned_back, keep, send = attend_back(
            order,
            flags[0],
            k.row_pieces,
            packed,
            k.queries,
            k.pairs,
            k.probs,
            tables,
            scale,
        )
        k.pair_grad = SimpleNamespace(keep=keep, send=send)

    def run_hidden_back(m):
        k = kept[0][m]
        k.hidden, k.part, k.side_second = hidden_back(
            order,
            flags[0],
            k.upstream,
            contract,
            weights.expand,
            k.slope,
            k.normal,
            gains,
        )

    def run_project_back(s, m):
        k = kept[s][m]
        own, arrived = k.pair_grad.keep, k.pair_grad.came
        k.stacked, k.side_first, *k.blocks = project_back(
            order,
            flags[s],
            k.turned_back,
            own.reshape(own.shape[1:]),
            arrived.reshape(arrived.shape[1:]),
            packed,
            k.part,
            k.normal,
            gains,
            tables,
        )

    def of(name, s, count=micros):
        return [getattr(kept[s][m], name) for m in range(count)]

    branch_sums, expand_sums, triple_sums = (SimpleNamespace(parts=[]) for _ in range(3))

    def run_sums(w, lefts, rights, by_rows):
        w.dim = 0 if by_rows else 1
        w.keep, w.send = weight_sums(order, always, lefts, rights, by_rows, spans)

    def wide_near(w):
        def go(passed):
            w.came = hop(passed, "ctx", 1, both)
            return w.came

        return w.send, go

    def run_fold(w):
        step = 2
        w.keep, w.send = fold(order, always, w.keep, w.came, w.dim)
        while 2 * step < spans:
            w.came = hop(w.send, "ctx", step, both)
            w.keep, w.send = fold(order, always, w.keep, w.came, w.dim)
            step *= 2

    def wide_far(w, start, stop):
        def go(passed):
            w.parts.append(hop(passed, "ctx", far, both))
            return w.parts[-1]

        return w.send[start:stop], go

    weights = SimpleNamespace(expand_came=[], contract_came=[])
    half_depth = depth // 2

    def expand_far(start, stop):
        def go(passed):
            weights.expand_came.append(hop(passed, "ctx", far, both))
            return weights.expand_came[-1]

        return own_expand[start:stop], go

    def packed_far(passed):
        weights.packed_came = hop(passed, "ctx", far, both)
        return weights.packed_came

    def packed_near(passed):
        weights.packed = blocks_of(packed, passed)
        return weights.packed[1:]

    def expand_near(passed):
        weights.expand = blocks_of(own_expand, passed)
        return weights.expand[1:]

    def contract_far(start, stop):
        def go(passed):
            weights.contract_came.append(hop(passed, "ctx", far, both))
            return weights.contract_came[-1]

        return own_contract[start:stop], go

    def contract_near(passed):
        weights.contract = blocks_of(own_contract, passed)
        return weights.contract[1:]

    def early_hops(passed):
        weights.early = [passed] + [hop(passed, "tp", j, both) for j in lane_offsets[1:]]
        return weights.early[1:]

    quarter = depth // 4
    due[0] = [expand_far(0, quarter)[1](own_expand[:quarter])]
    slot([(packed, packed_far), expand_far(quarter, depth), (early, early_hops)])
    early_pieces = weights.early
    cuts = [0, hidden // 4, 11 * hidden // 16, hidden]
    expand_came = jnp.concatenate(weights.expand_came, axis=0)
    slot(
        [
            (weights.packed_came, packed_near),
            (expand_came, expand_near),
            contract_far(cuts[0], cuts[1]),
        ]
    )
    packed = weights.packed
    small_full = jnp.concatenate(
        [piece[depth : depth + 4, :depth] for piece in packed], axis=1
    ).astype(f32)
    gains, biases = small_full[:2], small_full[2:]
    slot(
        [contract_far(cuts[1], cuts[2])],
        [lambda m=m: run_project(0, m) for m in range(micros)],
    )
    a, b = kept
    slot(
        [pair_far(0, 0), contract_far(cuts[2], cuts[3])],
        [lambda m=m: run_expand(m) for m in range(micros)],
    )
    contract_came = jnp.concatenate(weights.contract_came, axis=0)
    slot([(contract_came, contract_near), pair_near(0, 0)])
    contract = weights.contract
    slot([pair_far(0, 1)], [lambda: run_attend(0), lambda: run_branch(0)])
    slot([sum_near(0, a[0]), pair_near(0, 1), pair_far(0, 2)])
    slot(
        [sum_far(0, a[0]), pair_near(0, 2)], [lambda: run_attend(1), lambda: run_branch(1)]
    )
    slot(
        [hand_one(0, 0), sum_near(0, a[1])], [lambda: run_attend(2), lambda: run_branch(2)]
    )
    slot([rows_far(1, 0), sum_far(0, a[1])])
    slot([rows_near(1, 0), hand_one(0, 1), sum_near(0, a[2])])
    slot([rows_far(1, 1), sum_far(0, a[2])], [lambda: run_project(1, 0)])
    slot(
        [pair_far(1, 0), rows_near(1, 1), hand_one(0, 2)], [lambda: run_hidden_both(0)]
    )
    slot([pair_near(1, 0), rows_far(1, 2)], [lambda: run_project(1, 1)])
    slot(
        [pair_far(1, 1), rows_near(1, 2)],
        [lambda: run_attend_both(0), lambda: run_hidden_both(1)],
    )
    slot([pair_grad_near(1, 0), pair_near(1, 1)], [lambda: run_project(1, 2)])
    slot(
        [pair_grad_far(1, 0), pair_far(1, 2)],
        [lambda: run_attend_both(1), lambda: run_hidden_both(2)],
    )
    slot([pair_grad_near(1, 1), pair_near(1, 2)], [lambda: run_project_back(1, 0)])
    slot([sum_near(1, b[0]), pair_grad_far(1, 1)], [lambda: run_attend_both(2)])
    slot([sum_far(1, b[0]), pair_grad_near(1, 2)], [lambda: run_project_back(1, 1)])
    slot([hand_one(1, 0), sum_near(1, b[1]), pair_grad_far(1, 2)])
    slot([sum_far(1, b[1]), rows_far(0, 0)], [lambda: run_project_back(1, 2)])
    slot([sum_near(1, b[2]), hand_one(1, 1), rows_near(0, 0)])
    slot([sum_far(1, b[2]), rows_far(0, 1)], [lambda: run_attend_back(0)])
    slot(
        [hand_one(1, 2), rows_near(0, 1), pair_grad_near(0, 0)],
        [lambda: run_hidden_back(0)],
    )
    slot([rows_far(0, 2), pair_grad_far(0, 0)], [lambda: run_attend_back(1)])
    slot([rows_near(0, 2), pair_grad_near(0, 1)], [lambda: run_hidden_back(1)])
    last = micros - 1

    def run_branch_sums():
        run_sums(
            branch_sums,
            [[of("active", s), of("attended", s)] for s in both],
            [
                [of("upstream", 0, last) + [piece[0] for piece in a[last].row_pieces]],
                [of("upstream", 1)],
            ],
            False,
        )

    def run_expand_sums():
        run_sums(
            expand_sums,
            [[of("second", s)] for s in both],
            [[of("hidden", s)] for s in both],
            True,
        )

    def run_triple_sums():
        run_sums(
            triple_sums,
            [[of("first", s)] for s in both],
            [[of("stacked", s)] for s in both],
            True,
        )

    finals = SimpleNamespace()

    def run_final_branch():
        blocks = branch_out(
            order, flags[1], [(k.active, k.attended) for k in b], contract, packed
        )
        finals.keep = jnp.stack(blocks[0::2])
        finals.send = jnp.stack(blocks[1::2])

    def finals_near():
        return finals.send, lambda passed: fold_hops(finals, passed, "tp", 1, (1,))

    def finals_far():
        def go(passed):
            finals.came = hop(passed, "tp", lanes // 2, (1,))
            return finals.came

        return finals.send, go

    slot([pair_grad_far(0, 1)], [run_branch_sums])
    slot(
        [wide_near(branch_sums)], [lambda: run_attend_back(2), lambda: run_project_back(0, 0)]
    )
    slot([pair_grad_near(0, 2)], [lambda: run_fold(branch_sums)])
    cut = [0, 3 * hidden // 8, 7 * hidden // 8, hidden + across_units]
    slot(
        [pair_grad_far(0, 2), wide_far(branch_sums, cut[0], cut[1])],
        [lambda: run_hidden_back(2), lambda: run_project_back(0, 1)],
    )
    slot(
        [wide_far(branch_sums, cut[1], cut[2])],
        [lambda: run_project_back(0, 2), run_triple_sums],
    )

    def side_of(mades):
        return sum(
            jnp.concatenate([k.side_first, k.side_second], axis=0) for k in mades
        )

    side = SimpleNamespace(all=jnp.where(first_section, side_of(a), side_of(b)))

    def side_ctx(passed):
        step = 1
        while step < spans:
            middle = passed.shape[1] // 2
            came = hop(passed[:, middle:], "ctx", step, both)
            passed = passed[:, :middle] + came
            step *= 2
        side.all = passed
        return came

    def side_tp(passed):
        step = 1
        while step < lanes:
            came = hop(passed, "tp", step, both)
            passed = passed + came
            step *= 2
        side.all = passed
        return came

    def held_back(w, j):
        def go(passed):
            w.parts[j] = passed
            return []

        return w.parts[j], go

    slot([wide_near(triple_sums), (side.all, side_ctx)])
    slot([], [lambda: run_fold(triple_sums)])
    slot([wide_far(triple_sums, 0, half_depth), sum_near(0, a[0])], [run_expand_sums])
    slot(
        [
            wide_near(expand_sums),
            wide_far(triple_sums, half_depth, depth),
            sum_far(0, a[0]),
        ],
        [run_final_branch],
    )
    slot(
        [wide_far(branch_sums, cut[2], cut[3]), sum_near(0, a[1]), finals_near()],
        [lambda: run_fold(expand_sums)],
    )
    slot(
        [
            wide_far(expand_sums, 0, half_depth),
            sum_far(0, a[1]),
            sum_near(0, a[2]),
            (side.all, side_tp),
            held_back(triple_sums, 1),
            held_back(branch_sums, 2),
        ]
    )
    slot([wide_far(expand_sums, half_depth, depth), sum_far(0, a[2]), finals_far()])

    def wide_total(keep, parts):
        came = jnp.concatenate(parts, axis=0) if len(parts) > 1 else parts[0]
        return keep.astype(f32) + came.astype(f32)

    branch_grads = wide_total(branch_sums.keep, branch_sums.parts)
    contract_grads, output_grads = branch_grads[:hidden], branch_grads[hidden:]
    expand_grads = wide_total(expand_sums.keep, expand_sums.parts)
    triple_grads = wide_total(triple_sums.keep, triple_sums.parts)
    layer_outputs = jnp.stack(
        [
            jnp.where(
                first_section,
                kept[0][m].given,
                (
                    b[m].rows.astype(f32)
                    + finals.keep[m].astype(f32)
                    + finals.came[m].astype(f32)
                ).astype(bf16),
            )
            for m in range(micros)
        ]
    )
    entry_grads = jnp.stack(
        [
            jnp.where(
                first_section,
                norm_back(kept[0][m].rows, total_of(kept[0][m]), inputs[m]),
                kept[1][m].given,
            )
            for m in range(micros)
        ]
    )
    gain_grads = jnp.stack([side.all[0], side.all[2]])
    bias_grads = jnp.stack([side.all[1], side.all[3]])
    return (
        xor_blocks(layer_outputs, span, spans, inverse=True)[None],
        xor_blocks(entry_grads, span, spans, inverse=True)[None],
        triple_grads.reshape(triple_weight.shape),
        output_grads.reshape(output_weight.shape),
        expand_grads[None],
        contract_grads[None],
        gain_grads[None],
        bias_grads[None],
    )


def solution(mesh):
    return jax.shard_map(
        shards,
        mesh=mesh,
        in_specs=(
            P(None, ("ctx", "tp"), None),
            P(None, ("ctx", "tp"), None),
            P("pipe", "ctx", "tp", None, None),
            P("pipe", "tp", None, "ctx"),
            P("pipe", "ctx", "tp"),
            P("pipe", "tp", "ctx"),
            P("pipe", None, "ctx"),
            P("pipe", None, "ctx"),
        ),
        out_specs=(
            P("pipe", None, ("ctx", "tp"), None),
            P("pipe", None, ("ctx", "tp"), None),
            P("pipe", "ctx", "tp", None, None),
            P("pipe", "tp", None, "ctx"),
            P("pipe", "ctx", "tp"),
            P("pipe", "tp", "ctx"),
            P("pipe", None, "ctx"),
            P("pipe", None, "ctx"),
        ),
        check_vma=False,
    )
```

```python
import functools
import math
from types import SimpleNamespace

import jax
import jax.numpy as jnp
from jax import lax
from jax.experimental import pallas as pl
from jax.experimental.pallas import tpu as pltpu
from jax.sharding import PartitionSpec as P

ROT = 64
LANES = 128
epsilon = 1e-05
masked_score = -1e30
f32 = jnp.float32
bf16 = jnp.bfloat16
mebibyte = 1024 * 1024
half_root = 0.7071067811865476
bell = 0.3989422804014327


def dot(a, b, dims):
    return lax.dot_general(a, b, (dims, ((), ())), preferred_element_type=f32)


def plain(a, b):
    return dot(a, b, ((1,), (0,)))


def turned(a, b):
    return dot(a, b, ((1,), (1,)))


def doubling(count):
    order, step = [0], count // 2
    while step:
        order += [k ^ step for k in order]
        step //= 2
    return order


def xor_blocks(values, index, count, inverse=False):
    width = values.shape[-1] // count
    order = doubling(count)

    def taken(places):
        return jnp.concatenate(
            [values[..., k * width : (k + 1) * width] for k in places], axis=-1
        )

    if inverse:
        values = taken([order.index(k) for k in range(count)])
    step = 1
    while step < count:
        swapped = taken([k ^ step for k in range(count)])
        values = jnp.where((index & step) != 0, swapped, values)
        step *= 2
    return values if inverse else taken(order)


def rope_tables(positions):
    half = ROT // 2
    frequency = 10000.0 ** (-jnp.arange(0, ROT, 2, dtype=f32) / ROT)
    angles = positions.astype(f32)[:, None] * frequency[None, :]
    cosine, sine = jnp.cos(angles), jnp.sin(angles)
    count = positions.shape[0]
    rest = jnp.zeros((count, LANES - ROT), f32)
    none = jnp.zeros((count, half), f32)
    return jnp.stack(
        [
            jnp.concatenate([cosine, cosine, rest + 1.0], axis=1),
            jnp.concatenate([-sine, none, rest], axis=1),
            jnp.concatenate([none, sine, rest], axis=1),
        ]
    )


def turn(values, tables, sign):
    half = ROT // 2
    part = values[:, :LANES]
    moved = (
        pltpu.roll(part, LANES - half, 1) * tables[1] + pltpu.roll(part, half, 1) * tables[2]
    )
    part = part * tables[0] + (moved if sign > 0 else -moved)
    return jnp.concatenate([part, values[:, LANES:]], axis=1)


def normalize(values):
    center = values - jnp.mean(values, axis=-1, keepdims=True)
    inverse = lax.rsqrt(jnp.mean(center * center, axis=-1, keepdims=True) + epsilon)
    return (center * inverse, inverse)


def whole(array):
    zeros = (0,) * array.ndim
    return pl.BlockSpec(array.shape, lambda *_: zeros)


def at(block, place):
    return pl.BlockSpec(block, lambda *_: place)


kept_out = pl.BlockSpec(memory_space=pl.ANY)


def shape(dims, dtype=bf16):
    return jax.ShapeDtypeStruct(dims, dtype)


class Order:
    def __init__(self):
        self.last = []

    def follow(self, results):
        self.last = [min(results, key=lambda array: array.size * array.dtype.itemsize)]

    def also(self, array):
        self.last = self.last + [array]


took = dict(
    project=7,
    expand=8,
    attend=5,
    branch=8,
    hidden_both=14,
    attend_both=11,
    attend_back=8,
    hidden_back=13,
    project_back=8,
    weight_sums=16,
    fold=7,
)
peak = 1.15e9


def run(order, flags, kernel, ins, outs, scratch, name, grid=(1,), work=0):
    taken = len(ins)
    ins = [(flags, pl.BlockSpec(memory_space=pltpu.SMEM))] + list(ins)
    ins += [(array, kept_out) for array in order.last]
    arrays = [array for array, _ in ins]
    once = grid == (1,)

    def sized(spec, dtype):
        if spec.block_shape is None:
            return spec, 0
        size = math.prod(spec.block_shape) * jnp.dtype(dtype).itemsize
        if not once:
            return spec, 2 * size
        single = pl.BlockSpec(
            spec.block_shape, spec.index_map, pipeline_mode=pl.Buffered(1)
        )
        return single, size

    in_specs = [sized(spec, array.dtype) for array, spec in ins]
    out_specs = [sized(spec, struct.dtype) for struct, spec in outs]
    held = sum(size for _, size in in_specs + out_specs)
    for buffer in scratch:
        if buffer.memory_space == pltpu.VMEM:
            held += math.prod(buffer.shape) * jnp.dtype(buffer.dtype).itemsize

    def body(flag_ref, *refs):
        @pl.when(flag_ref[0] == 1)
        def _():
            kernel(flag_ref, *refs[:taken], *refs[len(ins) - 1 :])

    results = pl.pallas_call(
        body,
        grid=grid,
        in_specs=[spec for spec, _ in in_specs],
        out_specs=[spec for spec, _ in out_specs],
        out_shape=[struct for struct, _ in outs],
        scratch_shapes=scratch,
        compiler_params=pltpu.CompilerParams(
            vmem_limit_bytes=int(held + (work + 4) * mebibyte)
        ),
        cost_estimate=pl.CostEstimate(
            flops=int(took[name] * peak), bytes_accessed=0, transcendentals=0
        ),
        name=name,
    )(*arrays)
    order.follow(results)
    return results


def fence(through, waits):
    count = len(through)

    def kernel(*refs):
        pass

    return pl.pallas_call(
        kernel,
        in_specs=[kept_out] * (count + len(waits)),
        out_specs=[kept_out] * count,
        out_shape=[shape(array.shape, array.dtype) for array in through],
        input_output_aliases={j: j for j in range(count)},
        compiler_params=pltpu.CompilerParams(vmem_limit_bytes=mebibyte),
        cost_estimate=pl.CostEstimate(flops=1, bytes_accessed=1, transcendentals=0),
        name="fence",
    )(*through, *waits)


def full_out(dims, dtype=bf16):
    zeros = (0,) * len(dims)
    return (shape(dims, dtype), pl.BlockSpec(dims, lambda *_: zeros))


def copies(sources, targets, sems):
    started = []
    for source, target, sem in zip(sources, targets, sems):
        copy = pltpu.make_async_copy(source, target, sem)
        copy.start()
        started.append(copy)
    return started


def project(order, flags, pieces, at_piece, gains, biases, tables, weights, heads, head_dim):
    count, width = 1, pieces[0].shape[2]
    span_rows = sum(piece.shape[1] for piece in pieces)
    rows = count * span_rows
    chunk = pieces[0].shape[1]
    spans = len(weights)
    depth = width // spans
    wide = 3 * head_dim
    columns = heads * wide

    def kernel(flag_ref, *refs):
        piece_refs = refs[: len(pieces)]
        gain_ref, bias_ref, table_ref = refs[len(pieces) : len(pieces) + 3]
        weight_refs = refs[len(pieces) + 3 : len(pieces) + 3 + spans]
        first, second, normal, queries, pair, held, sems = refs[len(pieces) + 3 + spans :]
        started = []
        for h in range(heads):
            started.append(
                copies(
                    [w.at[:depth, h * wide : (h + 1) * wide] for w in weight_refs],
                    [held.at[h, k * depth : (k + 1) * depth] for k in range(spans)],
                    [sems.at[h, k] for k in range(spans)],
                )
            )
        start = 0
        for piece_ref in piece_refs:
            chunks = piece_ref.shape[1] // chunk

            def one(i, _, piece_ref=piece_ref, start=start, chunks=chunks):
                m, c = i // chunks, i % chunks
                values = piece_ref[m, pl.ds(pl.multiple_of(c * chunk, chunk), chunk), :]
                normed, _ = normalize(values.astype(f32))
                to = pl.ds(
                    pl.multiple_of(m * span_rows + start + c * chunk, chunk), chunk
                )
                normal[to, :] = normed.astype(bf16)
                first[to, :] = (normed * gain_ref[0:1] + bias_ref[0:1]).astype(bf16)
                second[to, :] = (normed * gain_ref[1:2] + bias_ref[1:2]).astype(bf16)
                return 0

            lax.fori_loop(0, count * chunks, one, 0)
            start += piece_ref.shape[1]
        for h in range(heads):
            for copy in started[h]:
                copy.wait()

            def two(m, _, h=h):
                to = pl.ds(pl.multiple_of(m * span_rows, span_rows), span_rows)
                made = plain(first[to, :], held[h])
                queries[h, to, :] = turn(made[:, :head_dim], table_ref, 1).astype(bf16)
                pair[0, h, to, :] = turn(
                    made[:, head_dim : 2 * head_dim], table_ref, 1
                ).astype(bf16)
                pair[1, h, to, :] = made[:, 2 * head_dim :].astype(bf16)
                return 0

            lax.fori_loop(0, count, two, 0)

    ins = [(piece, at((1,) + piece.shape[1:], (at_piece, 0, 0))) for piece in pieces]
    ins += [(array, whole(array)) for array in (gains, biases, tables)]
    ins += [(w, kept_out) for w in weights]
    outs = [full_out((rows, width))] * 3 + [
        full_out((heads, rows, head_dim)),
        full_out((2, heads, rows, head_dim)),
    ]
    scratch = [
        pltpu.VMEM((heads, width, wide), bf16),
        pltpu.SemaphoreType.DMA((heads, spans)),
    ]
    return run(order, flags, kernel, ins, outs, scratch, "project")


def expand_up(order, flags, second, weights, span_rows):
    rows, width = second.shape
    depth, hidden = weights[0].shape
    spans = len(weights)
    tile = min(512, hidden)
    tiles = hidden // tile

    def kernel(flag_ref, *refs):
        second_ref, weight_refs = refs[0], refs[1 : 1 + spans]
        active, slope, held, sems = refs[1 + spans :]
        started = []
        for t in range(tiles):
            started.append(
                copies(
                    [w.at[:, t * tile : (t + 1) * tile] for w in weight_refs],
                    [held.at[t, k * depth : (k + 1) * depth] for k in range(spans)],
                    [sems.at[t, k] for k in range(spans)],
                )
            )
        for t in range(tiles):
            for copy in started[t]:
                copy.wait()

            def one(m, _, t=t):
                to = pl.ds(pl.multiple_of(m * span_rows, span_rows), span_rows)
                pre = plain(second_ref[to, :], held[t])
                risen = 0.5 * (1.0 + lax.erf(pre * half_root))
                columns = slice(t * tile, (t + 1) * tile)
                active[to, columns] = (pre * risen).astype(bf16)
                slope[to, columns] = (
                    risen + pre * jnp.exp(-0.5 * pre * pre) * bell
                ).astype(bf16)
                return 0

            lax.fori_loop(0, rows // span_rows, one, 0)

    ins = [(second, whole(second))] + [(w, kept_out) for w in weights]
    outs = [full_out((rows, hidden))] * 2
    scratch = [
        pltpu.VMEM((tiles, width, tile), bf16),
        pltpu.SemaphoreType.DMA((tiles, spans)),
    ]
    return run(order, flags, kernel, ins, outs, scratch, "expand")


def spread(refs):
    return [ref.at[j] for ref in refs for j in range(ref.shape[0])]


def attention(here, pairs, head, row_ref, key_ref, scale):
    scores = []
    for k, pair in enumerate(pairs):
        raw = turned(here, pair[0, head]) * scale
        scores.append(jnp.where(key_ref[k] <= row_ref[...], raw, masked_score))
    top = functools.reduce(
        jnp.maximum, [jnp.max(part, axis=1, keepdims=True) for part in scores]
    )
    scores = [jnp.exp(part - top) for part in scores]
    inverse = 1.0 / sum(jnp.sum(part, axis=1, keepdims=True) for part in scores)
    return [part * inverse for part in scores]


def attend(order, flags, queries, pairs, positions, key_positions, scale):
    heads, rows, head_dim = queries.shape
    spans = sum(pair.shape[0] for pair in pairs)

    def kernel(flag_ref, query_ref, *refs):
        views, refs = spread(refs[: len(pairs)]), refs[len(pairs) :]
        row_ref, key_ref, attended, probs = refs
        for h in range(heads):
            parts = attention(query_ref[h], views, h, row_ref, key_ref, scale)
            summed = None
            for k in range(spans):
                part = parts[k].astype(bf16)
                probs[k, h] = part
                term = plain(part, views[k][1, h])
                summed = term if summed is None else summed + term
            attended[:, h * head_dim : (h + 1) * head_dim] = summed.astype(bf16)

    ins = [
        (array, whole(array)) for array in (queries, *pairs, positions, key_positions)
    ]
    outs = [full_out((rows, heads * head_dim)), full_out((spans, heads, rows, rows))]
    work = spans * rows * rows * 4 * heads * 4 / mebibyte
    return run(order, flags, kernel, ins, outs, [], "attend", work=work)


def attention_grads(grad, here, parts, views, head, keep, send, scale):
    half = keep.shape[0]
    grad_probs = [turned(grad, view[1, head]) for view in views]
    delta = sum(
        jnp.sum(part.astype(f32) * slope, axis=1, keepdims=True)
        for part, slope in zip(parts, grad_probs)
    )
    query_grad = None
    for k, view in enumerate(views):
        slopes = (parts[k].astype(f32) * (grad_probs[k] - delta)).astype(bf16)
        term = plain(slopes, view[0, head])
        query_grad = term if query_grad is None else query_grad + term
        side = keep if k < half else send
        side[k % half, 0, head] = (dot(slopes, here, ((0,), (0,))) * scale).astype(bf16)
        side[k % half, 1, head] = dot(parts[k].astype(bf16), grad, ((0,), (0,))).astype(bf16)
    return query_grad * scale


def attend_both(
    order, flags, rows_in, packed, queries, pairs, positions, key_positions, tables, scale
):
    heads, rows, head_dim = queries.shape
    width = rows_in.shape[1]
    spans = len(packed)
    across, depth = heads * head_dim, width // spans
    half = spans // 2

    def kernel(flag_ref, rows_ref, *refs):
        packed_refs, refs = refs[:spans], refs[spans:]
        query_ref, refs = refs[0], refs[1:]
        views, refs = spread(refs[: len(pairs)]), refs[len(pairs) :]
        row_ref, key_ref, table_ref, attended, turned_back, keep, send, held, sems = refs
        started = copies(
            [w.at[:across, 3 * across : 3 * across + depth] for w in packed_refs],
            [held.at[:, k * depth : (k + 1) * depth] for k in range(spans)],
            [sems.at[k] for k in range(spans)],
        )
        all_parts = []
        for h in range(heads):
            parts = attention(query_ref[h], views, h, row_ref, key_ref, scale)
            summed = None
            for k in range(spans):
                term = plain(parts[k].astype(bf16), views[k][1, h])
                summed = term if summed is None else summed + term
            attended[:, h * head_dim : (h + 1) * head_dim] = summed.astype(bf16)
            all_parts.append(parts)
        for copy in started:
            copy.wait()
        grads = turned(rows_ref[...], held[...]).astype(bf16)
        for h in range(heads):
            made = attention_grads(
                grads[:, h * head_dim : (h + 1) * head_dim],
                query_ref[h],
                all_parts[h],
                views,
                h,
                keep,
                send,
                scale,
            )
            turned_back[h] = turn(made, table_ref, -1).astype(bf16)

    ins = [(rows_in, whole(rows_in))] + [(w, kept_out) for w in packed]
    ins += [
        (array, whole(array)) for array in (queries, *pairs, positions, key_positions, tables)
    ]
    outs = [full_out((rows, across)), full_out((heads, rows, head_dim))]
    outs += [full_out((half, 2, heads, rows, head_dim))] * 2
    scratch = [pltpu.VMEM((across, width), bf16), pltpu.SemaphoreType.DMA((spans,))]
    work = spans * rows * rows * 4 * (heads + 4) / mebibyte
    return run(order, flags, kernel, ins, outs, scratch, "attend_both", work=work)


def hidden_both(order, flags, second, pieces, at_piece, expand, contract, normal, gains):
    rows, width = second.shape
    hidden, depth = contract[0].shape
    spans = len(contract)
    tile = min(512, hidden)
    tiles = hidden // tile

    def kernel(flag_ref, second_ref, *refs):
        piece_refs, refs = refs[: len(pieces)], refs[len(pieces) :]
        expand_refs, refs = refs[:spans], refs[spans:]
        contract_refs, refs = refs[:spans], refs[spans:]
        normal_ref, gain_ref, rows_out, active, grads, part, side, *refs = refs
        held_up, held_down, sems_up, sems_down = refs
        started = []
        for t in range(tiles):
            block = slice(t * tile, (t + 1) * tile)
            places = [slice(k * depth, (k + 1) * depth) for k in range(spans)]
            up = copies(
                [w.at[:, block] for w in expand_refs],
                [held_up.at[place, block] for place in places],
                [sems_up.at[t, k] for k in range(spans)],
            )
            down = copies(
                [w.at[block, :] for w in contract_refs],
                [held_down.at[block, place] for place in places],
                [sems_down.at[t, k] for k in range(spans)],
            )
            started.append((up, down))
        start = 0
        for piece_ref in piece_refs:
            size = piece_ref.shape[1]
            rows_out[start : start + size, :] = piece_ref[0]
            start += size
        for t in range(tiles):
            block = slice(t * tile, (t + 1) * tile)
            for copy in started[t][0] + started[t][1]:
                copy.wait()
            pre = plain(second_ref[...], held_up[:, block])
            risen = 0.5 * (1.0 + lax.erf(pre * half_root))
            active[:, block] = (pre * risen).astype(bf16)
            slope = risen + pre * jnp.exp(-0.5 * pre * pre) * bell
            grads[:, block] = (turned(rows_out[...], held_down[block, :]) * slope).astype(bf16)
        for k in range(spans):
            place = slice(k * depth, (k + 1) * depth)
            made = turned(grads[...], held_up[place, :])
            side[0:1, place] = jnp.sum(
                made * normal_ref[:, place].astype(f32), axis=0, keepdims=True
            )
            side[1:2, place] = jnp.sum(made, axis=0, keepdims=True)
            part[:, place] = made * gain_ref[1:2, place]

    ins = [(second, whole(second))]
    ins += [(piece, at((1,) + piece.shape[1:], (at_piece, 0, 0))) for piece in pieces]
    ins += [(w, kept_out) for w in expand] + [(w, kept_out) for w in contract]
    ins += [(normal, whole(normal)), (gains, whole(gains))]
    outs = [
        full_out((rows, width)),
        full_out((rows, hidden)),
        full_out((rows, hidden)),
        full_out((rows, width), f32),
        full_out((2, width), f32),
    ]
    scratch = [
        pltpu.VMEM((width, hidden), bf16),
        pltpu.VMEM((hidden, width), bf16),
        pltpu.SemaphoreType.DMA((tiles, spans)),
        pltpu.SemaphoreType.DMA((tiles, spans)),
    ]
    return run(order, flags, kernel, ins, outs, scratch, "hidden_both")


def branch_out(order, flags, groups, contract, packed):
    hidden, depth = contract[0].shape
    across = groups[0][1].shape[1]
    spans = len(contract)
    width = depth * spans
    span_rows = groups[0][0].shape[0]
    block = span_rows // 2
    count = len(groups)

    def kernel(flag_ref, *refs):
        group_refs, refs = refs[: 2 * count], refs[2 * count :]
        contract_refs, packed_refs = refs[:spans], refs[spans : 2 * spans]
        blocks, refs = refs[2 * spans : 2 * (spans + count)], refs[2 * (spans + count) :]
        held, held_out, sems = refs
        outputs = [w.at[:across, 3 * across : 3 * across + depth] for w in packed_refs]
        started = copies(
            [ref for k in range(spans) for ref in (outputs[k], contract_refs[k])],
            [ref for k in range(spans) for ref in (held_out.at[k], held.at[k])],
            [sems.at[j] for j in range(2 * spans)],
        )
        for k in range(spans):
            started[2 * k].wait()
            started[2 * k + 1].wait()
            columns = slice(k * depth, (k + 1) * depth)
            for c in range(count):
                made = plain(group_refs[2 * c + 1][...], held_out[k])
                made = made + plain(group_refs[2 * c][...], held[k])
                blocks[2 * c][:, columns] = made[:block].astype(bf16)
                blocks[2 * c + 1][:, columns] = made[block:].astype(bf16)

    ins = []
    for active, attended in groups:
        ins += [(active, whole(active)), (attended, whole(attended))]
    ins += [(w, kept_out) for w in contract] + [(w, kept_out) for w in packed]
    outs = [full_out((block, width))] * (2 * count)
    scratch = [
        pltpu.VMEM((spans, hidden, depth), bf16),
        pltpu.VMEM((spans, across, depth), bf16),
        pltpu.SemaphoreType.DMA((2 * spans,)),
    ]
    return run(order, flags, kernel, ins, outs, scratch, "branch")


def attend_back(order, flags, pieces, packed, queries, pairs, probs, tables, scale):
    rows = sum(piece.shape[1] for piece in pieces)
    width = pieces[0].shape[2]
    heads, _, head_dim = queries.shape
    spans = len(packed)
    across, depth = heads * head_dim, width // spans
    half = spans // 2

    def kernel(flag_ref, *refs):
        piece_refs, refs = refs[: len(pieces)], refs[len(pieces) :]
        packed_refs, refs = refs[:spans], refs[spans:]
        query_ref, refs = refs[0], refs[1:]
        views, refs = spread(refs[: len(pairs)]), refs[len(pairs) :]
        prob_ref, table_ref, rows_out, turned_back, keep, send, held, sems = refs
        started = copies(
            [w.at[:across, 3 * across : 3 * across + depth] for w in packed_refs],
            [held.at[:, k * depth : (k + 1) * depth] for k in range(spans)],
            [sems.at[k] for k in range(spans)],
        )
        start = 0
        for piece_ref in piece_refs:
            size = piece_ref.shape[1]
            rows_out[start : start + size, :] = piece_ref[0]
            start += size
        for copy in started:
            copy.wait()
        grads = turned(rows_out[...], held[...]).astype(bf16)
        for h in range(heads):
            made = attention_grads(
                grads[:, h * head_dim : (h + 1) * head_dim],
                query_ref[h],
                [prob_ref[k, h] for k in range(spans)],
                views,
                h,
                keep,
                send,
                scale,
            )
            turned_back[h] = turn(made, table_ref, -1).astype(bf16)

    ins = [(piece, whole(piece)) for piece in pieces] + [(w, kept_out) for w in packed]
    ins += [(array, whole(array)) for array in (queries, *pairs, probs, tables)]
    outs = [full_out((rows, width)), full_out((heads, rows, head_dim))]
    outs += [full_out((half, 2, heads, rows, head_dim))] * 2
    scratch = [pltpu.VMEM((across, width), bf16), pltpu.SemaphoreType.DMA((spans,))]
    work = spans * rows * rows * 4 * 4 / mebibyte
    return run(order, flags, kernel, ins, outs, scratch, "attend_back", work=work)


def hidden_back(order, flags, upstream, contract, expand, slope, normal, gains):
    span_rows, width = upstream.shape
    hidden, depth = contract[0].shape
    spans = len(contract)
    tile = min(512, hidden)
    tiles = hidden // tile

    def kernel(flag_ref, *refs):
        upstream_ref, refs = refs[0], refs[1:]
        contract_refs, refs = refs[:spans], refs[spans:]
        expand_refs, refs = refs[:spans], refs[spans:]
        slope_ref, normal_ref, gain_ref, grads, part, side, held, held_up, sems, sems_up = refs
        started = [
            copies(
                [w.at[t * tile : (t + 1) * tile, :] for w in contract_refs],
                [held.at[t, :, k * depth : (k + 1) * depth] for k in range(spans)],
                [sems.at[t, k] for k in range(spans)],
            )
            for t in range(tiles)
        ]
        started_up = copies(
            expand_refs, [held_up.at[k] for k in range(spans)], [sems_up.at[k] for k in range(spans)]
        )
        for t in range(tiles):
            for copy in started[t]:
                copy.wait()
            columns = slice(t * tile, (t + 1) * tile)
            grads[:, columns] = (
                turned(upstream_ref[...], held[t]) * slope_ref[:, columns].astype(f32)
            ).astype(bf16)
        for k in range(spans):
            started_up[k].wait()
            made = turned(grads[...], held_up[k])
            columns = slice(k * depth, (k + 1) * depth)
            side[0:1, columns] = jnp.sum(
                made * normal_ref[:, columns].astype(f32), axis=0, keepdims=True
            )
            side[1:2, columns] = jnp.sum(made, axis=0, keepdims=True)
            part[:, columns] = made * gain_ref[1:2, columns]

    ins = [(upstream, whole(upstream))]
    ins += [(w, kept_out) for w in contract] + [(w, kept_out) for w in expand]
    ins += [
        (slope, whole(slope)),
        (normal, whole(normal)),
        (gains, whole(gains)),
    ]
    outs = [
        full_out((span_rows, hidden)),
        full_out((span_rows, width), f32),
        full_out((2, width), f32),
    ]
    scratch = [
        pltpu.VMEM((tiles, tile, width), bf16),
        pltpu.VMEM((spans, depth, hidden), bf16),
        pltpu.SemaphoreType.DMA((tiles, spans)),
        pltpu.SemaphoreType.DMA((spans,)),
    ]
    return run(order, flags, kernel, ins, outs, scratch, "hidden_back")


def project_back(
    order, flags, turned_back, own, came, weights, part, normal, gains, tables
):
    heads, span_rows, head_dim = turned_back.shape
    spans = len(weights)
    width = part.shape[1]
    depth, columns = width // spans, 3 * heads * head_dim
    block = span_rows // 2

    def kernel(flag_ref, *refs):
        query_ref, own_ref, came_ref, refs = refs[0], refs[1], refs[2], refs[3:]
        weight_refs, refs = refs[:spans], refs[spans:]
        part_ref, normal_ref, gain_ref, table_ref, grads, side, *refs = refs
        low, high, held, sems = refs
        started = copies(
            [w.at[:depth, :columns] for w in weight_refs],
            [held.at[k] for k in range(spans)],
            [sems.at[k] for k in range(spans)],
        )
        for h in range(heads):
            at_column = h * 3 * head_dim
            keys = own_ref[0, h].astype(f32) + came_ref[0, h].astype(f32)
            values = own_ref[1, h].astype(f32) + came_ref[1, h].astype(f32)
            grads[:, at_column : at_column + head_dim] = query_ref[h]
            grads[:, at_column + head_dim : at_column + 2 * head_dim] = turn(
                keys, table_ref, -1
            ).astype(bf16)
            grads[:, at_column + 2 * head_dim : at_column + 3 * head_dim] = values.astype(bf16)
        for k in range(spans):
            started[k].wait()
            made = turned(grads[...], held[k])
            span_columns = slice(k * depth, (k + 1) * depth)
            side[0:1, span_columns] = jnp.sum(
                made * normal_ref[:, span_columns].astype(f32), axis=0, keepdims=True
            )
            side[1:2, span_columns] = jnp.sum(made, axis=0, keepdims=True)
            both = (made * gain_ref[0:1, span_columns] + part_ref[:, span_columns]).astype(bf16)
            low[:, span_columns] = both[:block]
            high[:, span_columns] = both[block:]

    ins = [(array, whole(array)) for array in (turned_back, own, came)]
    ins += [(w, kept_out) for w in weights]
    ins += [(part, whole(part)), (normal, whole(normal))]
    ins += [(gains, whole(gains)), (tables, whole(tables))]
    outs = [full_out((span_rows, columns)), full_out((2, width), f32)]
    outs += [full_out((block, width))] * 2
    scratch = [pltpu.VMEM((spans, depth, columns), bf16), pltpu.SemaphoreType.DMA((spans,))]
    return run(order, flags, kernel, ins, outs, scratch, "project_back")


def weight_sums(order, flags, lefts, rights, by_rows, spans):
    rows = sum(piece.shape[0] for piece in lefts[0][0])
    left_width = sum(group[0].shape[1] for group in lefts[0])
    right_width = sum(group[0].shape[1] for group in rights[0])
    if by_rows:
        tile = left_width // spans
        steps, block = spans // 2, (tile, right_width)
    else:
        tile = min(512, left_width)
        while left_width % tile:
            tile //= 2
        steps, block = left_width // tile, (tile, right_width // 2)
    chunk = min(1024, block[1])
    while right_width % chunk:
        chunk //= 2
    pieces = [
        [piece for groups in (lefts[s], rights[s]) for group in groups for piece in group]
        for s in (0, 1)
    ]
    most = max(len(p) for p in pieces)

    def kernel(flag_ref, *refs):
        piece_refs = (refs[: len(pieces[0])], refs[len(pieces[0]) : len(pieces[0]) + len(pieces[1])])
        keep, send, left, right, flipped, sems = refs[len(pieces[0]) + len(pieces[1]) :]
        g = pl.program_id(0)
        for s in (0, 1):

            @pl.when((g == 0) & (flag_ref[2] == s))
            def _(s=s):
                targets = []
                for held, groups in ((left, lefts[s]), (right, rights[s])):
                    column = 0
                    for group in groups:
                        row, wide = 0, group[0].shape[1]
                        for piece in group:
                            targets.append(
                                held.at[row : row + piece.shape[0], column : column + wide]
                            )
                            row += piece.shape[0]
                        column += wide
                started = copies(
                    piece_refs[s], targets, [sems.at[j] for j in range(len(targets))]
                )
                for copy in started:
                    copy.wait()

        def product(column, store):
            flipped[...] = left[:, pl.ds(pl.multiple_of(column, LANES), tile)].T

            def one(c, _):
                columns = pl.ds(pl.multiple_of(c * chunk, chunk), chunk)
                store(c, plain(flipped[...], right[:, columns]).astype(bf16))
                return 0

            lax.fori_loop(0, right_width // chunk, one, 0)

        if by_rows:

            def to(target):
                def store(c, made):
                    target[:, pl.ds(pl.multiple_of(c * chunk, chunk), chunk)] = made

                return store

            product(g * tile, to(keep))
            product((g + steps) * tile, to(send))
        else:
            half = right_width // 2 // chunk

            def store(c, made):
                @pl.when(c < half)
                def _():
                    keep[:, pl.ds(pl.multiple_of(c * chunk, chunk), chunk)] = made

                @pl.when(c >= half)
                def _():
                    send[:, pl.ds(pl.multiple_of((c - half) * chunk, chunk), chunk)] = made

            product(g * tile, store)

    ins = [(piece, kept_out) for s in (0, 1) for piece in pieces[s]]
    dims = (steps * tile, block[1])
    outs = [(shape(dims), pl.BlockSpec(block, lambda g: (g, 0)))] * 2
    scratch = [
        pltpu.VMEM((rows, left_width), bf16),
        pltpu.VMEM((rows, right_width), bf16),
        pltpu.VMEM((tile, rows), bf16),
        pltpu.SemaphoreType.DMA((most,)),
    ]
    return run(
        order, flags, kernel, ins, outs, scratch, "weight_sums", grid=(steps,)
    )


def fold(order, flags, keep, came, dim):
    rows, columns = keep.shape
    if dim == 0:
        tile = rows // 4
        steps, block = rows // 2 // tile, (tile, columns)
        places = [lambda g: (g, 0), lambda g: (g + steps, 0)]
        half = (rows // 2, columns)
    else:
        tile = rows // 4
        steps, block = rows // tile, (tile, columns // 2)
        places = [lambda g: (g, 0), lambda g: (g, 1)]
        half = (rows, columns // 2)

    def kernel(flag_ref, keep_low, keep_high, came_low, came_high, low, high):
        low[...] = (keep_low[...].astype(f32) + came_low[...].astype(f32)).astype(bf16)
        high[...] = (keep_high[...].astype(f32) + came_high[...].astype(f32)).astype(bf16)

    ins = [(array, pl.BlockSpec(block, place)) for array in (keep, came) for place in places]
    outs = [(shape(half), pl.BlockSpec(block, lambda g: (g, 0)))] * 2
    return run(order, flags, kernel, ins, outs, [], "fold", grid=(steps,))


def shards(
    block_input,
    out_grad,
    triple_weight,
    output_weight,
    expand_weight,
    contract_weight,
    norm_gains,
    norm_biases,
):
    section = lax.axis_index("pipe")
    span = lax.axis_index("ctx")
    lane = lax.axis_index("tp")
    spans = lax.axis_size("ctx")
    lanes = lax.axis_size("tp")
    micros, rows, width = block_input.shape
    span_rows = rows * lanes
    heads = triple_weight.shape[2]
    head_dim = triple_weight.shape[4]
    across_units = heads * head_dim
    scale = head_dim ** (-0.5)
    first_section = section == 0
    both = (0, 1)

    def hop(array, axis, step, sections):
        size = lax.axis_size(axis)
        pairs = [(s * size + a, s * size + (a ^ step)) for s in sections for a in range(size)]
        return lax.ppermute(array, ("pipe", axis), pairs)

    order = Order()

    def flags_for(wanted):
        return jnp.stack([jnp.asarray(wanted), span, section]).astype(jnp.int32)

    flags = [flags_for(section == s) for s in both]
    always = flags_for(1)

    kept = [[SimpleNamespace() for _ in range(micros)] for _ in both]
    due = {}
    slot_index = [0]

    def slot(hops, kernels=()):
        now = slot_index[0]
        slot_index[0] += 1
        ready = due.pop(now, [])
        hops = [h if len(h) == 3 else h + (1,) for h in hops]
        if hops:
            gated = fence([operand for operand, _, _ in hops], order.last + ready)
            order.last = [min(gated, key=lambda array: array.size)]
            for passed, (_, go, slots) in zip(gated, hops):
                results = go(passed)
                results = results if isinstance(results, list) else [results]
                due.setdefault(now + slots, []).extend(results)
        else:
            order.last = order.last + ready
        for kernel in kernels:
            kernel()

    def halved(keep, came, dim):
        middle = keep.shape[dim] // 2
        total = keep.astype(f32) + came.astype(f32)
        return (
            lax.slice_in_dim(total, 0, middle, axis=dim).astype(bf16),
            lax.slice_in_dim(total, middle, 2 * middle, axis=dim).astype(bf16),
        )

    def spread_hops(pieces, axis, axis_name, sections, first):
        step = lax.axis_size(axis_name) // 4
        going = first
        while step:
            pieces.append(hop(going, axis_name, step, sections))
            going = jnp.concatenate(pieces, axis=axis)
            step //= 2
        return pieces[-1]

    def fold_hops(k, first, axis_name, dim, sections):
        step, size = 1, lax.axis_size(axis_name)
        while 2 * step < size:
            came = hop(first, axis_name, step, sections)
            k.keep, k.send = halved(k.keep, came, dim)
            first = k.send
            step *= 2
        return came

    depth = width // spans
    far = spans // 2
    assert depth == across_units
    small = jnp.concatenate([norm_gains[0], norm_biases[0]], axis=0)
    packed = jnp.concatenate(
        [triple_weight[0].reshape(depth, -1), output_weight[0].reshape(-1, depth)],
        axis=1,
    )
    packed = jnp.pad(packed, ((0, 16), (0, 0)))
    packed = lax.dynamic_update_slice(packed, small, (depth, 0))
    own_expand, own_contract = expand_weight[0], contract_weight[0]
    hidden = own_expand.shape[1]
    inputs = xor_blocks(block_input, span, spans)
    cotangent = xor_blocks(out_grad, span, spans)
    early = jnp.where(first_section, inputs, cotangent)

    in_row = jnp.arange(rows, dtype=jnp.int32)
    in_span = jnp.concatenate([(lane ^ j) * rows + in_row for j in doubling(lanes)])
    positions = span * span_rows + in_span
    key_positions = jnp.stack([(span ^ k) * span_rows + in_span for k in doubling(spans)])
    tables = rope_tables(positions)
    position_column = positions[:, None]
    key_positions = key_positions[:, None, :]

    def blocks_of(own, came):
        held, step = {0: own, far: came}, far // 2
        while step:
            for k in list(held):
                held[k ^ step] = hop(held[k], "ctx", step, both)
            step //= 2
        return [held[k] for k in doubling(spans)]

    lane_offsets = doubling(lanes)

    def across(array, j, source):
        pairs = [(source * lanes + a, (1 - source) * lanes + (a ^ j)) for a in range(lanes)]
        return lax.ppermute(array, ("pipe", "tp"), pairs)

    def rows_far(s, m):
        k = kept[s][m]

        def go(passed):
            k.rows = passed
            k.pieces = [passed, hop(passed, "tp", lanes // 2, (s,))]
            return k.pieces[1]

        return k.rows, go

    def rows_near(s, m):
        k = kept[s][m]

        def go(passed):
            last_piece = spread_hops(k.pieces, 0, "tp", (s,), passed)
            k.row_pieces = [piece[None] for piece in k.pieces]
            return last_piece

        return jnp.concatenate(k.pieces, axis=0), go

    def one_way(array, direction, s):
        pairs = [
            (s * spans + a, s * spans + (a ^ far))
            for a in range(spans)
            if direction * ((a ^ far) - a) > 0
        ]
        return lax.ppermute(array, ("pipe", "ctx"), pairs)

    def pair_far(s, m):
        k = kept[s][m]

        def go(passed):
            k.pairs = [passed, one_way(passed, 1, s)]
            return k.pairs[1]

        return k.pair, go

    def pair_near(s, m):
        k = kept[s][m]

        def go(passed):
            return spread_hops(k.pairs, 0, "ctx", (s,), passed)

        return jnp.concatenate(k.pairs, axis=0), go

    def pair_grad_near(s, m):
        k = kept[s][m].pair_grad
        return k.send, lambda passed: fold_hops(k, passed, "ctx", 0, (s,))

    def pair_grad_far(s, m):
        k = kept[s][m].pair_grad

        def go(passed):
            k.came = one_way(passed, -1, s)
            return k.came

        return k.send, go

    def sum_near(s, k):
        k.keep, going = k.blocks
        return going, lambda passed: fold_hops(k, passed, "tp", 0, (s,))

    def sum_far(s, k):
        def go(passed):
            k.blocks, k.arrived = [k.keep], [hop(passed, "tp", lanes // 2, (s,))]
            return k.arrived[0]

        return k.send, go

    def total_of(k):
        return sum(array.astype(f32) for array in [k.blocks[0], *k.arrived])

    def norm_back(upstream, combined, entering):
        normalized, inverse = normalize(entering.astype(f32))
        return (
            upstream.astype(f32)
            + inverse
            * (
                combined
                - jnp.mean(combined, axis=-1, keepdims=True)
                - normalized * jnp.mean(combined * normalized, axis=-1, keepdims=True)
            )
        ).astype(bf16)

    def middle_of(m):
        return (inputs[m].astype(f32) + total_of(kept[0][m])).astype(bf16)

    def entry_of(m):
        k = kept[1][m]
        return norm_back(cotangent[m], total_of(k), k.rows)

    def hand_one(s, m):
        k, other = kept[s][m], kept[1 - s][m]
        k.given = middle_of(m) if s == 0 else entry_of(m)

        def go(passed):
            k.given = passed
            other.rows = across(passed, 0, s)
            return other.rows

        return k.given, go

    def run_project(s, m):
        k = kept[s][m]
        pieces, place = (early_pieces, m) if s == 0 else (k.row_pieces, 0)
        k.first, k.second, k.normal, k.queries, pair = project(
            order, flags[s], pieces, place, gains, biases, tables, packed, heads, head_dim
        )
        k.pair = pair[None]

    def run_expand(m):
        k = kept[0][m]
        k.active, k.slope = expand_up(order, flags[0], k.second, weights.expand, span_rows)

    def run_attend(m):
        k = kept[0][m]
        k.attended, k.probs = attend(
            order, flags[0], k.queries, k.pairs, position_column, key_positions, scale
        )

    def run_branch(m):
        k = kept[0][m]
        k.blocks = branch_out(
            order, flags[0], [(k.active, k.attended)], contract, packed
        )

    def run_hidden_both(m):
        k = kept[1][m]
        k.upstream, k.active, k.hidden, k.part, k.side_second = hidden_both(
            order,
            flags[1],
            k.second,
            early_pieces,
            m,
            weights.expand,
            contract,
            k.normal,
            gains,
        )

    def run_attend_both(m):
        k = kept[1][m]
        k.attended, k.turned_back, keep, send = attend_both(
            order,
            flags[1],
            k.upstream,
            packed,
            k.queries,
            k.pairs,
            position_column,
            key_positions,
            tables,
            scale,
        )
        k.pair_grad = SimpleNamespace(keep=keep, send=send)

    def run_attend_back(m):
        k = kept[0][m]
        k.upstream, k.turned_back, keep, send = attend_back(
            order,
            flags[0],
            k.row_pieces,
            packed,
            k.queries,
            k.pairs,
            k.probs,
            tables,
            scale,
        )
        k.pair_grad = SimpleNamespace(keep=keep, send=send)

    def run_hidden_back(m):
        k = kept[0][m]
        k.hidden, k.part, k.side_second = hidden_back(
            order,
            flags[0],
            k.upstream,
            contract,
            weights.expand,
            k.slope,
            k.normal,
            gains,
        )

    def run_project_back(s, m):
        k = kept[s][m]
        own, arrived = k.pair_grad.keep, k.pair_grad.came
        k.stacked, k.side_first, *k.blocks = project_back(
            order,
            flags[s],
            k.turned_back,
            own.reshape(own.shape[1:]),
            arrived.reshape(arrived.shape[1:]),
            packed,
            k.part,
            k.normal,
            gains,
            tables,
        )

    def of(name, s, count=micros):
        return [getattr(kept[s][m], name) for m in range(count)]

    branch_sums, expand_sums, triple_sums = (SimpleNamespace(parts=[]) for _ in range(3))

    def run_sums(w, lefts, rights, by_rows):
        w.dim = 0 if by_rows else 1
        w.keep, w.send = weight_sums(order, always, lefts, rights, by_rows, spans)

    def wide_near(w):
        def go(passed):
            w.came = hop(passed, "ctx", 1, both)
            return w.came

        return w.send, go

    def run_fold(w):
        step = 2
        w.keep, w.send = fold(order, always, w.keep, w.came, w.dim)
        while 2 * step < spans:
            w.came = hop(w.send, "ctx", step, both)
            w.keep, w.send = fold(order, always, w.keep, w.came, w.dim)
            step *= 2

    def wide_far(w, start, stop):
        def go(passed):
            w.parts.append(hop(passed, "ctx", far, both))
            return w.parts[-1]

        return w.send[start:stop], go

    weights = SimpleNamespace(expand_came=[], contract_came=[])
    half_depth = depth // 2

    def expand_far(start, stop):
        def go(passed):
            weights.expand_came.append(hop(passed, "ctx", far, both))
            return weights.expand_came[-1]

        return own_expand[start:stop], go

    def packed_far(passed):
        weights.packed_came = hop(passed, "ctx", far, both)
        return weights.packed_came

    def packed_near(passed):
        weights.packed = blocks_of(packed, passed)
        return weights.packed[1:]

    def expand_near(passed):
        weights.expand = blocks_of(own_expand, passed)
        return weights.expand[1:]

    def contract_far(start, stop):
        def go(passed):
            weights.contract_came.append(hop(passed, "ctx", far, both))
            return weights.contract_came[-1]

        return own_contract[start:stop], go

    def contract_near(passed):
        weights.contract = blocks_of(own_contract, passed)
        return weights.contract[1:]

    def early_hops(passed):
        weights.early = [passed] + [hop(passed, "tp", j, both) for j in lane_offsets[1:]]
        return weights.early[1:]

    due[0] = [expand_far(0, half_depth)[1](own_expand[:half_depth])]
    slot([(packed, packed_far), expand_far(half_depth, depth), (early, early_hops)])
    early_pieces = weights.early
    cuts = [0, hidden // 4, 11 * hidden // 16, hidden]
    expand_came = jnp.concatenate(weights.expand_came, axis=0)
    slot(
        [
            (weights.packed_came, packed_near),
            (expand_came, expand_near),
            contract_far(cuts[0], cuts[1]),
        ]
    )
    packed = weights.packed
    small_full = jnp.concatenate(
        [piece[depth : depth + 4, :depth] for piece in packed], axis=1
    ).astype(f32)
    gains, biases = small_full[:2], small_full[2:]
    slot(
        [contract_far(cuts[1], cuts[2])],
        [lambda m=m: run_project(0, m) for m in range(micros)],
    )
    a, b = kept
    slot(
        [pair_far(0, 0), contract_far(cuts[2], cuts[3])],
        [lambda m=m: run_expand(m) for m in range(micros)],
    )
    contract_came = jnp.concatenate(weights.contract_came, axis=0)
    slot([(contract_came, contract_near), pair_near(0, 0)])
    contract = weights.contract
    slot([pair_far(0, 1)], [lambda: run_attend(0), lambda: run_branch(0)])
    slot([sum_near(0, a[0]), pair_near(0, 1)])
    slot([sum_far(0, a[0]), pair_far(0, 2)], [lambda: run_attend(1), lambda: run_branch(1)])
    slot([hand_one(0, 0), sum_near(0, a[1]), pair_near(0, 2)])
    slot(
        [rows_far(1, 0), sum_far(0, a[1])], [lambda: run_attend(2), lambda: run_branch(2)]
    )
    slot([rows_near(1, 0), hand_one(0, 1), sum_near(0, a[2])])
    slot([rows_far(1, 1), sum_far(0, a[2])], [lambda: run_project(1, 0)])
    slot(
        [pair_far(1, 0), rows_near(1, 1), hand_one(0, 2)], [lambda: run_hidden_both(0)]
    )
    slot([pair_near(1, 0), rows_far(1, 2)], [lambda: run_project(1, 1)])
    slot(
        [pair_far(1, 1), rows_near(1, 2)],
        [lambda: run_attend_both(0), lambda: run_hidden_both(1)],
    )
    slot([pair_grad_near(1, 0), pair_near(1, 1)], [lambda: run_project(1, 2)])
    slot(
        [pair_grad_far(1, 0), pair_far(1, 2)],
        [lambda: run_attend_both(1), lambda: run_hidden_both(2)],
    )
    slot([pair_grad_near(1, 1), pair_near(1, 2)], [lambda: run_project_back(1, 0)])
    slot([sum_near(1, b[0]), pair_grad_far(1, 1)], [lambda: run_attend_both(2)])
    slot([sum_far(1, b[0]), pair_grad_near(1, 2)], [lambda: run_project_back(1, 1)])
    slot([hand_one(1, 0), sum_near(1, b[1]), pair_grad_far(1, 2)])
    slot([sum_far(1, b[1]), rows_far(0, 0)], [lambda: run_project_back(1, 2)])
    slot([sum_near(1, b[2]), hand_one(1, 1), rows_near(0, 0)])
    slot([sum_far(1, b[2]), rows_far(0, 1)], [lambda: run_attend_back(0)])
    slot(
        [hand_one(1, 2), rows_near(0, 1), pair_grad_near(0, 0)],
        [lambda: run_hidden_back(0)],
    )
    slot([rows_far(0, 2), pair_grad_far(0, 0)], [lambda: run_attend_back(1)])
    slot(
        [rows_near(0, 2), pair_grad_near(0, 1)],
        [lambda: run_hidden_back(1), lambda: run_project_back(0, 0)],
    )
    last = micros - 1

    def run_branch_sums():
        run_sums(
            branch_sums,
            [[of("active", s), of("attended", s)] for s in both],
            [
                [of("upstream", 0, last) + [piece[0] for piece in a[last].row_pieces]],
                [of("upstream", 1)],
            ],
            False,
        )

    def run_expand_sums():
        run_sums(
            expand_sums,
            [[of("second", s)] for s in both],
            [[of("hidden", s)] for s in both],
            True,
        )

    def run_triple_sums():
        run_sums(
            triple_sums,
            [[of("first", s)] for s in both],
            [[of("stacked", s)] for s in both],
            True,
        )

    finals = SimpleNamespace()

    def run_final_branch():
        blocks = branch_out(
            order, flags[1], [(k.active, k.attended) for k in b], contract, packed
        )
        finals.keep = jnp.stack(blocks[0::2])
        finals.send = jnp.stack(blocks[1::2])

    def finals_near():
        return finals.send, lambda passed: fold_hops(finals, passed, "tp", 1, (1,))

    def finals_far():
        def go(passed):
            finals.came = hop(passed, "tp", lanes // 2, (1,))
            return finals.came

        return finals.send, go

    slot([pair_grad_far(0, 1), sum_near(0, a[0])], [run_branch_sums])
    slot(
        [wide_near(branch_sums)], [lambda: run_attend_back(2), lambda: run_project_back(0, 1)]
    )
    slot([pair_grad_near(0, 2)], [lambda: run_fold(branch_sums)])
    cut = [0, 3 * hidden // 8, 7 * hidden // 8, hidden + across_units]
    slot(
        [
            pair_grad_far(0, 2),
            wide_far(branch_sums, cut[0], cut[1]),
            sum_far(0, a[0]),
            sum_near(0, a[1]),
        ],
        [lambda: run_hidden_back(2)],
    )
    slot(
        [wide_far(branch_sums, cut[1], cut[2]), sum_far(0, a[1])],
        [lambda: run_project_back(0, 2), run_triple_sums],
    )

    def side_of(mades):
        return sum(
            jnp.concatenate([k.side_first, k.side_second], axis=0) for k in mades
        )

    side = SimpleNamespace(all=jnp.where(first_section, side_of(a), side_of(b)))

    def side_ctx(passed):
        step = 1
        while step < spans:
            middle = passed.shape[1] // 2
            came = hop(passed[:, middle:], "ctx", step, both)
            passed = passed[:, :middle] + came
            step *= 2
        side.all = passed
        return came

    def side_near(passed):
        step = 1
        while 2 * step < lanes:
            came = hop(passed, "tp", step, both)
            passed = passed + came
            step *= 2
        side.all = passed
        return came

    def side_far(passed):
        came = hop(passed, "tp", lanes // 2, both)
        side.all = passed + came
        return came

    def held_back(w, j):
        def go(passed):
            w.parts[j] = passed
            return []

        return w.parts[j], go

    def wide_total(keep, parts):
        came = jnp.concatenate(parts, axis=0) if len(parts) > 1 else parts[0]
        return keep.astype(f32) + came.astype(f32)

    slot(
        [
            wide_near(triple_sums),
            (side.all, side_ctx),
            wide_far(branch_sums, cut[2], cut[3]),
        ]
    )
    slot([], [lambda: run_fold(triple_sums)])
    slot([wide_far(triple_sums, 0, half_depth), sum_near(0, a[2])], [run_expand_sums])
    slot(
        [
            wide_near(expand_sums),
            wide_far(triple_sums, half_depth, depth),
            (side.all, side_near),
        ],
        [run_final_branch],
    )
    slot([], [lambda: run_fold(expand_sums)])
    slot(
        [
            wide_far(expand_sums, 0, half_depth),
            sum_far(0, a[2]),
            finals_near(),
            (side.all, side_far),
            held_back(triple_sums, 1),
            held_back(branch_sums, 2),
        ]
    )
    triple_grads = wide_total(triple_sums.keep, triple_sums.parts)
    triple_grads = triple_grads.reshape(triple_weight.shape)
    branch_grads = wide_total(branch_sums.keep, branch_sums.parts)
    contract_grads, output_grads = branch_grads[:hidden], branch_grads[hidden:]
    due.setdefault(slot_index[0], []).extend([triple_grads, contract_grads])
    slot([wide_far(expand_sums, half_depth, depth), finals_far()])
    expand_grads = wide_total(expand_sums.keep, expand_sums.parts)
    layer_outputs = jnp.stack(
        [
            jnp.where(
                first_section,
                kept[0][m].given,
                (
                    b[m].rows.astype(f32)
                    + finals.keep[m].astype(f32)
                    + finals.came[m].astype(f32)
                ).astype(bf16),
            )
            for m in range(micros)
        ]
    )
    entry_grads = jnp.stack(
        [
            jnp.where(
                first_section,
                norm_back(kept[0][m].rows, total_of(kept[0][m]), inputs[m]),
                kept[1][m].given,
            )
            for m in range(micros)
        ]
    )
    gain_grads = jnp.stack([side.all[0], side.all[2]])
    bias_grads = jnp.stack([side.all[1], side.all[3]])
    return (
        xor_blocks(layer_outputs, span, spans, inverse=True)[None],
        xor_blocks(entry_grads, span, spans, inverse=True)[None],
        triple_grads,
        output_grads.reshape(output_weight.shape),
        expand_grads[None],
        contract_grads[None],
        gain_grads[None],
        bias_grads[None],
    )


def solution(mesh):
    return jax.shard_map(
        shards,
        mesh=mesh,
        in_specs=(
            P(None, ("ctx", "tp"), None),
            P(None, ("ctx", "tp"), None),
            P("pipe", "ctx", "tp", None, None),
            P("pipe", "tp", None, "ctx"),
            P("pipe", "ctx", "tp"),
            P("pipe", "tp", "ctx"),
            P("pipe", None, "ctx"),
            P("pipe", None, "ctx"),
        ),
        out_specs=(
            P("pipe", None, ("ctx", "tp"), None),
            P("pipe", None, ("ctx", "tp"), None),
            P("pipe", "ctx", "tp", None, None),
            P("pipe", "tp", None, "ctx"),
            P("pipe", "ctx", "tp"),
            P("pipe", "tp", "ctx"),
            P("pipe", None, "ctx"),
            P("pipe", None, "ctx"),
        ),
        check_vma=False,
    )
```

```python
import functools
import math
from types import SimpleNamespace

import jax
import jax.numpy as jnp
from jax import lax
from jax.experimental import pallas as pl
from jax.experimental.pallas import tpu as pltpu
from jax.sharding import PartitionSpec as P

ROT = 64
LANES = 128
epsilon = 1e-05
masked_score = -1e30
f32 = jnp.float32
bf16 = jnp.bfloat16
mebibyte = 1024 * 1024
half_root = 0.7071067811865476
bell = 0.3989422804014327


def dot(a, b, dims):
    return lax.dot_general(a, b, (dims, ((), ())), preferred_element_type=f32)


def plain(a, b):
    return dot(a, b, ((1,), (0,)))


def turned(a, b):
    return dot(a, b, ((1,), (1,)))


def doubling(count):
    order, step = [0], count // 2
    while step:
        order += [k ^ step for k in order]
        step //= 2
    return order


def xor_blocks(values, index, count, inverse=False):
    width = values.shape[-1] // count
    order = doubling(count)

    def taken(places):
        return jnp.concatenate(
            [values[..., k * width : (k + 1) * width] for k in places], axis=-1
        )

    if inverse:
        values = taken([order.index(k) for k in range(count)])
    step = 1
    while step < count:
        swapped = taken([k ^ step for k in range(count)])
        values = jnp.where((index & step) != 0, swapped, values)
        step *= 2
    return values if inverse else taken(order)


def rope_tables(positions):
    half = ROT // 2
    frequency = 10000.0 ** (-jnp.arange(0, ROT, 2, dtype=f32) / ROT)
    angles = positions.astype(f32)[:, None] * frequency[None, :]
    cosine, sine = jnp.cos(angles), jnp.sin(angles)
    count = positions.shape[0]
    rest = jnp.zeros((count, LANES - ROT), f32)
    none = jnp.zeros((count, half), f32)
    return jnp.stack(
        [
            jnp.concatenate([cosine, cosine, rest + 1.0], axis=1),
            jnp.concatenate([-sine, none, rest], axis=1),
            jnp.concatenate([none, sine, rest], axis=1),
        ]
    )


def turn(values, tables, sign):
    half = ROT // 2
    part = values[:, :LANES]
    moved = (
        pltpu.roll(part, LANES - half, 1) * tables[1] + pltpu.roll(part, half, 1) * tables[2]
    )
    part = part * tables[0] + (moved if sign > 0 else -moved)
    return jnp.concatenate([part, values[:, LANES:]], axis=1)


def normalize(values):
    center = values - jnp.mean(values, axis=-1, keepdims=True)
    inverse = lax.rsqrt(jnp.mean(center * center, axis=-1, keepdims=True) + epsilon)
    return (center * inverse, inverse)


def whole(array):
    zeros = (0,) * array.ndim
    return pl.BlockSpec(array.shape, lambda *_: zeros)


def at(block, place):
    return pl.BlockSpec(block, lambda *_: place)


kept_out = pl.BlockSpec(memory_space=pl.ANY)


def shape(dims, dtype=bf16):
    return jax.ShapeDtypeStruct(dims, dtype)


class Order:
    def __init__(self):
        self.last = []

    def follow(self, results):
        self.last = [min(results, key=lambda array: array.size * array.dtype.itemsize)]

    def also(self, array):
        self.last = self.last + [array]


took = dict(
    project=5,
    expand=6,
    attend=3,
    branch=6,
    hidden_both=11,
    attend_both=5,
    attend_back=5,
    hidden_back=9,
    project_back=5,
    weight_sums=11,
    fold=3,
    owner_sums=13,
)
peak = 1.15e9


def run(order, flags, kernel, ins, outs, scratch, name, grid=(1,), work=0, in_place={}):
    taken = len(ins)
    ins = [(flags, pl.BlockSpec(memory_space=pltpu.SMEM))] + list(ins)
    ins += [(array, kept_out) for array in order.last]
    arrays = [array for array, _ in ins]
    once = grid == (1,)

    def sized(spec, dtype):
        if spec.block_shape is None:
            return spec, 0
        size = math.prod(spec.block_shape) * jnp.dtype(dtype).itemsize
        if not once:
            return spec, 2 * size
        single = pl.BlockSpec(
            spec.block_shape, spec.index_map, pipeline_mode=pl.Buffered(1)
        )
        return single, size

    in_specs = [sized(spec, array.dtype) for array, spec in ins]
    out_specs = [sized(spec, struct.dtype) for struct, spec in outs]
    held = sum(size for _, size in in_specs + out_specs)
    for buffer in scratch:
        if buffer.memory_space == pltpu.VMEM:
            held += math.prod(buffer.shape) * jnp.dtype(buffer.dtype).itemsize

    def body(flag_ref, *refs):
        @pl.when(flag_ref[0] == 1)
        def _():
            kernel(flag_ref, *refs[:taken], *refs[len(ins) - 1 :])

    results = pl.pallas_call(
        body,
        grid=grid,
        in_specs=[spec for spec, _ in in_specs],
        out_specs=[spec for spec, _ in out_specs],
        out_shape=[struct for struct, _ in outs],
        scratch_shapes=scratch,
        input_output_aliases=in_place,
        compiler_params=pltpu.CompilerParams(
            vmem_limit_bytes=int(held + (work + 4) * mebibyte)
        ),
        cost_estimate=pl.CostEstimate(
            flops=int(took[name] * peak), bytes_accessed=0, transcendentals=0
        ),
        name=name,
    )(*arrays)
    order.follow(results)
    return results


def fence(through, waits):
    count = len(through)

    def kernel(*refs):
        pass

    return pl.pallas_call(
        kernel,
        in_specs=[kept_out] * (count + len(waits)),
        out_specs=[kept_out] * count,
        out_shape=[shape(array.shape, array.dtype) for array in through],
        input_output_aliases={j: j for j in range(count)},
        compiler_params=pltpu.CompilerParams(vmem_limit_bytes=mebibyte),
        cost_estimate=pl.CostEstimate(flops=1, bytes_accessed=1, transcendentals=0),
        name="fence",
    )(*through, *waits)


def full_out(dims, dtype=bf16):
    zeros = (0,) * len(dims)
    return (shape(dims, dtype), pl.BlockSpec(dims, lambda *_: zeros))


def copies(sources, targets, sems):
    started = []
    for source, target, sem in zip(sources, targets, sems):
        copy = pltpu.make_async_copy(source, target, sem)
        copy.start()
        started.append(copy)
    return started


def project(order, flags, pieces, at_piece, gains, biases, tables, weights, heads, head_dim):
    count, width = 1, pieces[0].shape[2]
    span_rows = sum(piece.shape[1] for piece in pieces)
    rows = count * span_rows
    chunk = pieces[0].shape[1]
    spans = len(weights)
    depth = width // spans
    wide = 3 * head_dim
    columns = heads * wide

    def kernel(flag_ref, *refs):
        piece_refs = refs[: len(pieces)]
        gain_ref, bias_ref, table_ref = refs[len(pieces) : len(pieces) + 3]
        weight_refs = refs[len(pieces) + 3 : len(pieces) + 3 + spans]
        first, second, normal, queries, pair, held, sems = refs[len(pieces) + 3 + spans :]
        started = []
        for h in range(heads):
            started.append(
                copies(
                    [w.at[:depth, h * wide : (h + 1) * wide] for w in weight_refs],
                    [held.at[h, k * depth : (k + 1) * depth] for k in range(spans)],
                    [sems.at[h, k] for k in range(spans)],
                )
            )
        start = 0
        for piece_ref in piece_refs:
            chunks = piece_ref.shape[1] // chunk

            def one(i, _, piece_ref=piece_ref, start=start, chunks=chunks):
                m, c = i // chunks, i % chunks
                values = piece_ref[m, pl.ds(pl.multiple_of(c * chunk, chunk), chunk), :]
                normed, _ = normalize(values.astype(f32))
                to = pl.ds(
                    pl.multiple_of(m * span_rows + start + c * chunk, chunk), chunk
                )
                normal[to, :] = normed.astype(bf16)
                first[to, :] = (normed * gain_ref[0:1] + bias_ref[0:1]).astype(bf16)
                second[to, :] = (normed * gain_ref[1:2] + bias_ref[1:2]).astype(bf16)
                return 0

            lax.fori_loop(0, count * chunks, one, 0)
            start += piece_ref.shape[1]
        for h in range(heads):
            for copy in started[h]:
                copy.wait()

            def two(m, _, h=h):
                to = pl.ds(pl.multiple_of(m * span_rows, span_rows), span_rows)
                made = plain(first[to, :], held[h])
                queries[h, to, :] = turn(made[:, :head_dim], table_ref, 1).astype(bf16)
                pair[0, h, to, :] = turn(
                    made[:, head_dim : 2 * head_dim], table_ref, 1
                ).astype(bf16)
                pair[1, h, to, :] = made[:, 2 * head_dim :].astype(bf16)
                return 0

            lax.fori_loop(0, count, two, 0)

    ins = [(piece, at((1,) + piece.shape[1:], (at_piece, 0, 0))) for piece in pieces]
    ins += [(array, whole(array)) for array in (gains, biases, tables)]
    ins += [(w, kept_out) for w in weights]
    outs = [full_out((rows, width))] * 3 + [
        full_out((heads, rows, head_dim)),
        full_out((2, heads, rows, head_dim)),
    ]
    scratch = [
        pltpu.VMEM((heads, width, wide), bf16),
        pltpu.SemaphoreType.DMA((heads, spans)),
    ]
    return run(order, flags, kernel, ins, outs, scratch, "project")


def expand_up(order, flags, second, weights, span_rows, room):
    rows, width = second.shape
    depth, hidden = weights[0].shape
    spans = len(weights)
    tile = min(512, hidden)
    tiles = hidden // tile

    def kernel(flag_ref, *refs):
        second_ref, weight_refs = refs[0], refs[1 : 1 + spans]
        active, slope, held, sems = refs[1 + spans :]
        started = []
        for t in range(tiles):
            started.append(
                copies(
                    [w.at[:, t * tile : (t + 1) * tile] for w in weight_refs],
                    [held.at[t, k * depth : (k + 1) * depth] for k in range(spans)],
                    [sems.at[t, k] for k in range(spans)],
                )
            )
        for t in range(tiles):
            for copy in started[t]:
                copy.wait()

            def one(m, _, t=t):
                to = pl.ds(pl.multiple_of(m * span_rows, span_rows), span_rows)
                pre = plain(second_ref[to, :], held[t])
                risen = 0.5 * (1.0 + lax.erf(pre * half_root))
                columns = slice(t * tile, (t + 1) * tile)
                active[to, columns] = (pre * risen).astype(bf16)
                slope[to, columns] = (
                    risen + pre * jnp.exp(-0.5 * pre * pre) * bell
                ).astype(bf16)
                return 0

            lax.fori_loop(0, rows // span_rows, one, 0)

    ins = [(second, whole(second))] + [(w, kept_out) for w in weights]
    outs = [
        (shape((rows, hidden + room)), at((rows, hidden), (0, 0))),
        full_out((rows, hidden)),
    ]
    scratch = [
        pltpu.VMEM((tiles, width, tile), bf16),
        pltpu.SemaphoreType.DMA((tiles, spans)),
    ]
    return run(order, flags, kernel, ins, outs, scratch, "expand")


def spread(refs):
    return [ref.at[j] for ref in refs for j in range(ref.shape[0])]


def attention(here, pairs, head, row_ref, key_ref, scale):
    scores = []
    for k, pair in enumerate(pairs):
        raw = turned(here, pair[0, head]) * scale
        scores.append(jnp.where(key_ref[k] <= row_ref[...], raw, masked_score))
    top = functools.reduce(
        jnp.maximum, [jnp.max(part, axis=1, keepdims=True) for part in scores]
    )
    scores = [jnp.exp(part - top) for part in scores]
    inverse = 1.0 / sum(jnp.sum(part, axis=1, keepdims=True) for part in scores)
    return [part * inverse for part in scores]


def attend(order, flags, units, queries, pairs, positions, key_positions, scale):
    heads, rows, head_dim = queries.shape
    spans = sum(pair.shape[0] for pair in pairs)
    across = heads * head_dim

    def kernel(flag_ref, units_ref, query_ref, *refs):
        views, refs = spread(refs[: len(pairs)]), refs[len(pairs) :]
        row_ref, key_ref, attended, probs = refs
        for h in range(heads):
            parts = attention(query_ref[h], views, h, row_ref, key_ref, scale)
            summed = None
            for k in range(spans):
                part = parts[k].astype(bf16)
                probs[k, h] = part
                term = plain(part, views[k][1, h])
                summed = term if summed is None else summed + term
            attended[:, h * head_dim : (h + 1) * head_dim] = summed.astype(bf16)

    ins = [(units, kept_out)]
    ins += [(array, whole(array)) for array in (queries, *pairs, positions, key_positions)]
    outs = [
        (shape(units.shape), at((rows, across), (0, units.shape[1] // across - 1))),
        full_out((spans, heads, rows, rows)),
    ]
    work = spans * rows * rows * 4 * heads * 4 / mebibyte
    return run(
        order, flags, kernel, ins, outs, [], "attend", work=work, in_place={1: 0}
    )


def attention_grads(grad, here, parts, views, head, keep, send, scale):
    half = keep.shape[0]
    grad_probs = [turned(grad, view[1, head]) for view in views]
    delta = sum(
        jnp.sum(part.astype(f32) * slope, axis=1, keepdims=True)
        for part, slope in zip(parts, grad_probs)
    )
    query_grad = None
    for k, view in enumerate(views):
        slopes = (parts[k].astype(f32) * (grad_probs[k] - delta)).astype(bf16)
        term = plain(slopes, view[0, head])
        query_grad = term if query_grad is None else query_grad + term
        side = keep if k < half else send
        side[k % half, 0, head] = (dot(slopes, here, ((0,), (0,))) * scale).astype(bf16)
        side[k % half, 1, head] = dot(parts[k].astype(bf16), grad, ((0,), (0,))).astype(bf16)
    return query_grad * scale


def attend_both(
    order, flags, rows_in, packed, queries, pairs, positions, key_positions, tables, scale
):
    heads, rows, head_dim = queries.shape
    width = rows_in.shape[1]
    spans = len(packed)
    across, depth = heads * head_dim, width // spans
    half = spans // 2

    def kernel(flag_ref, rows_ref, *refs):
        packed_refs, refs = refs[:spans], refs[spans:]
        query_ref, refs = refs[0], refs[1:]
        views, refs = spread(refs[: len(pairs)]), refs[len(pairs) :]
        row_ref, key_ref, table_ref, attended, turned_back, keep, send, held, sems = refs
        started = copies(
            [w.at[:across, 3 * across : 3 * across + depth] for w in packed_refs],
            [held.at[:, k * depth : (k + 1) * depth] for k in range(spans)],
            [sems.at[k] for k in range(spans)],
        )
        all_parts = []
        for h in range(heads):
            parts = attention(query_ref[h], views, h, row_ref, key_ref, scale)
            summed = None
            for k in range(spans):
                term = plain(parts[k].astype(bf16), views[k][1, h])
                summed = term if summed is None else summed + term
            attended[:, h * head_dim : (h + 1) * head_dim] = summed.astype(bf16)
            all_parts.append(parts)
        for copy in started:
            copy.wait()
        grads = turned(rows_ref[...], held[...]).astype(bf16)
        for h in range(heads):
            made = attention_grads(
                grads[:, h * head_dim : (h + 1) * head_dim],
                query_ref[h],
                all_parts[h],
                views,
                h,
                keep,
                send,
                scale,
            )
            turned_back[h] = turn(made, table_ref, -1).astype(bf16)

    ins = [(rows_in, whole(rows_in))] + [(w, kept_out) for w in packed]
    ins += [
        (array, whole(array)) for array in (queries, *pairs, positions, key_positions, tables)
    ]
    outs = [full_out((rows, across)), full_out((heads, rows, head_dim))]
    outs += [full_out((half, 2, heads, rows, head_dim))] * 2
    scratch = [pltpu.VMEM((across, width), bf16), pltpu.SemaphoreType.DMA((spans,))]
    work = spans * rows * rows * 4 * (heads + 4) / mebibyte
    return run(order, flags, kernel, ins, outs, scratch, "attend_both", work=work)


def hidden_both(order, flags, second, pieces, at_piece, expand, contract, normal, gains):
    rows, width = second.shape
    hidden, depth = contract[0].shape
    spans = len(contract)
    tile = min(512, hidden)
    tiles = hidden // tile

    def kernel(flag_ref, second_ref, *refs):
        piece_refs, refs = refs[: len(pieces)], refs[len(pieces) :]
        expand_refs, refs = refs[:spans], refs[spans:]
        contract_refs, refs = refs[:spans], refs[spans:]
        normal_ref, gain_ref, rows_out, active, grads, part, side, *refs = refs
        held_up, held_down, sems_up, sems_down = refs
        started = []
        for t in range(tiles):
            block = slice(t * tile, (t + 1) * tile)
            places = [slice(k * depth, (k + 1) * depth) for k in range(spans)]
            up = copies(
                [w.at[:, block] for w in expand_refs],
                [held_up.at[place, block] for place in places],
                [sems_up.at[t, k] for k in range(spans)],
            )
            down = copies(
                [w.at[block, :] for w in contract_refs],
                [held_down.at[block, place] for place in places],
                [sems_down.at[t, k] for k in range(spans)],
            )
            started.append((up, down))
        start = 0
        for piece_ref in piece_refs:
            size = piece_ref.shape[1]
            rows_out[start : start + size, :] = piece_ref[0]
            start += size
        for t in range(tiles):
            block = slice(t * tile, (t + 1) * tile)
            for copy in started[t][0] + started[t][1]:
                copy.wait()
            pre = plain(second_ref[...], held_up[:, block])
            risen = 0.5 * (1.0 + lax.erf(pre * half_root))
            active[:, block] = (pre * risen).astype(bf16)
            slope = risen + pre * jnp.exp(-0.5 * pre * pre) * bell
            grads[:, block] = (turned(rows_out[...], held_down[block, :]) * slope).astype(bf16)
        for k in range(spans):
            place = slice(k * depth, (k + 1) * depth)
            made = turned(grads[...], held_up[place, :])
            side[0:1, place] = jnp.sum(
                made * normal_ref[:, place].astype(f32), axis=0, keepdims=True
            )
            side[1:2, place] = jnp.sum(made, axis=0, keepdims=True)
            part[:, place] = made * gain_ref[1:2, place]

    ins = [(second, whole(second))]
    ins += [(piece, at((1,) + piece.shape[1:], (at_piece, 0, 0))) for piece in pieces]
    ins += [(w, kept_out) for w in expand] + [(w, kept_out) for w in contract]
    ins += [(normal, whole(normal)), (gains, whole(gains))]
    outs = [
        full_out((rows, width)),
        full_out((rows, hidden)),
        full_out((rows, hidden)),
        full_out((rows, width), f32),
        full_out((2, width), f32),
    ]
    scratch = [
        pltpu.VMEM((width, hidden), bf16),
        pltpu.VMEM((hidden, width), bf16),
        pltpu.SemaphoreType.DMA((tiles, spans)),
        pltpu.SemaphoreType.DMA((tiles, spans)),
    ]
    return run(order, flags, kernel, ins, outs, scratch, "hidden_both")


def branch_out(order, flags, groups, contract, packed):
    hidden, depth = contract[0].shape
    spans = len(contract)
    across = depth
    width = depth * spans
    span_rows = groups[0][0].shape[0]
    block = span_rows // 2
    count = len(groups)

    def kernel(flag_ref, *refs):
        group_refs, refs = refs[: 2 * count], refs[2 * count :]
        contract_refs, packed_refs = refs[:spans], refs[spans : 2 * spans]
        blocks, refs = refs[2 * spans : 2 * (spans + count)], refs[2 * (spans + count) :]
        held, held_out, sems = refs
        outputs = [w.at[:across, 3 * across : 3 * across + depth] for w in packed_refs]
        started = copies(
            [ref for k in range(spans) for ref in (outputs[k], contract_refs[k])],
            [ref for k in range(spans) for ref in (held_out.at[k], held.at[k])],
            [sems.at[j] for j in range(2 * spans)],
        )
        for k in range(spans):
            started[2 * k].wait()
            started[2 * k + 1].wait()
            columns = slice(k * depth, (k + 1) * depth)
            for c in range(count):
                made = plain(group_refs[2 * c + 1][...], held_out[k])
                made = made + plain(group_refs[2 * c][...], held[k])
                blocks[2 * c][:, columns] = made[:block].astype(bf16)
                blocks[2 * c + 1][:, columns] = made[block:].astype(bf16)

    ins = []
    for active, attended in groups:
        place = attended.shape[1] // across - 1
        ins += [
            (active, at((span_rows, hidden), (0, 0))),
            (attended, at((span_rows, across), (0, place))),
        ]
    ins += [(w, kept_out) for w in contract] + [(w, kept_out) for w in packed]
    outs = [full_out((block, width))] * (2 * count)
    scratch = [
        pltpu.VMEM((spans, hidden, depth), bf16),
        pltpu.VMEM((spans, across, depth), bf16),
        pltpu.SemaphoreType.DMA((2 * spans,)),
    ]
    return run(order, flags, kernel, ins, outs, scratch, "branch")


def attend_back(order, flags, pieces, packed, queries, pairs, probs, tables, scale):
    rows = sum(piece.shape[1] for piece in pieces)
    width = pieces[0].shape[2]
    heads, _, head_dim = queries.shape
    spans = len(packed)
    across, depth = heads * head_dim, width // spans
    half = spans // 2

    def kernel(flag_ref, *refs):
        piece_refs, refs = refs[: len(pieces)], refs[len(pieces) :]
        packed_refs, refs = refs[:spans], refs[spans:]
        query_ref, refs = refs[0], refs[1:]
        views, refs = spread(refs[: len(pairs)]), refs[len(pairs) :]
        prob_ref, table_ref, rows_out, turned_back, keep, send, *refs = refs
        columns_out, (held, sems) = refs[:spans], refs[spans:]
        started = copies(
            [w.at[:across, 3 * across : 3 * across + depth] for w in packed_refs],
            [held.at[:, k * depth : (k + 1) * depth] for k in range(spans)],
            [sems.at[k] for k in range(spans)],
        )
        start = 0
        for piece_ref in piece_refs:
            size = piece_ref.shape[1]
            rows_out[start : start + size, :] = piece_ref[0]
            start += size
        for k in range(spans):
            columns_out[k][...] = rows_out[:, k * depth : (k + 1) * depth]
        for copy in started:
            copy.wait()
        grads = turned(rows_out[...], held[...]).astype(bf16)
        for h in range(heads):
            made = attention_grads(
                grads[:, h * head_dim : (h + 1) * head_dim],
                query_ref[h],
                [prob_ref[k, h] for k in range(spans)],
                views,
                h,
                keep,
                send,
                scale,
            )
            turned_back[h] = turn(made, table_ref, -1).astype(bf16)

    ins = [(piece, whole(piece)) for piece in pieces] + [(w, kept_out) for w in packed]
    ins += [(array, whole(array)) for array in (queries, *pairs, probs, tables)]
    outs = [full_out((rows, width)), full_out((heads, rows, head_dim))]
    outs += [full_out((half, 2, heads, rows, head_dim))] * 2
    outs += [full_out((rows, depth))] * spans
    scratch = [pltpu.VMEM((across, width), bf16), pltpu.SemaphoreType.DMA((spans,))]
    work = spans * rows * rows * 4 * 4 / mebibyte
    return run(order, flags, kernel, ins, outs, scratch, "attend_back", work=work)


def hidden_back(order, flags, upstream, contract, expand, slope, normal, gains):
    span_rows, width = upstream.shape
    hidden, depth = contract[0].shape
    spans = len(contract)
    tile = min(512, hidden)
    tiles = hidden // tile

    def kernel(flag_ref, *refs):
        upstream_ref, refs = refs[0], refs[1:]
        contract_refs, refs = refs[:spans], refs[spans:]
        expand_refs, refs = refs[:spans], refs[spans:]
        slope_ref, normal_ref, gain_ref, grads, part, side, held, held_up, sems, sems_up = refs
        started = [
            copies(
                [w.at[t * tile : (t + 1) * tile, :] for w in contract_refs],
                [held.at[t, :, k * depth : (k + 1) * depth] for k in range(spans)],
                [sems.at[t, k] for k in range(spans)],
            )
            for t in range(tiles)
        ]
        started_up = copies(
            expand_refs, [held_up.at[k] for k in range(spans)], [sems_up.at[k] for k in range(spans)]
        )
        for t in range(tiles):
            for copy in started[t]:
                copy.wait()
            columns = slice(t * tile, (t + 1) * tile)
            grads[:, columns] = (
                turned(upstream_ref[...], held[t]) * slope_ref[:, columns].astype(f32)
            ).astype(bf16)
        for k in range(spans):
            started_up[k].wait()
            made = turned(grads[...], held_up[k])
            columns = slice(k * depth, (k + 1) * depth)
            side[0:1, columns] = jnp.sum(
                made * normal_ref[:, columns].astype(f32), axis=0, keepdims=True
            )
            side[1:2, columns] = jnp.sum(made, axis=0, keepdims=True)
            part[:, columns] = made * gain_ref[1:2, columns]

    ins = [(upstream, whole(upstream))]
    ins += [(w, kept_out) for w in contract] + [(w, kept_out) for w in expand]
    ins += [
        (slope, whole(slope)),
        (normal, whole(normal)),
        (gains, whole(gains)),
    ]
    outs = [
        full_out((span_rows, hidden)),
        full_out((span_rows, width), f32),
        full_out((2, width), f32),
    ]
    scratch = [
        pltpu.VMEM((tiles, tile, width), bf16),
        pltpu.VMEM((spans, depth, hidden), bf16),
        pltpu.SemaphoreType.DMA((tiles, spans)),
        pltpu.SemaphoreType.DMA((spans,)),
    ]
    return run(order, flags, kernel, ins, outs, scratch, "hidden_back")


def project_back(
    order, flags, turned_back, own, came, weights, part, normal, gains, tables
):
    heads, span_rows, head_dim = turned_back.shape
    spans = len(weights)
    width = part.shape[1]
    depth, columns = width // spans, 3 * heads * head_dim
    block = span_rows // 2

    def kernel(flag_ref, *refs):
        query_ref, own_ref, came_ref, refs = refs[0], refs[1], refs[2], refs[3:]
        weight_refs, refs = refs[:spans], refs[spans:]
        part_ref, normal_ref, gain_ref, table_ref, grads, side, *refs = refs
        low, high, held, sems = refs
        started = copies(
            [w.at[:depth, :columns] for w in weight_refs],
            [held.at[k] for k in range(spans)],
            [sems.at[k] for k in range(spans)],
        )
        for h in range(heads):
            at_column = h * 3 * head_dim
            keys = own_ref[0, h].astype(f32) + came_ref[0, h].astype(f32)
            values = own_ref[1, h].astype(f32) + came_ref[1, h].astype(f32)
            grads[:, at_column : at_column + head_dim] = query_ref[h]
            grads[:, at_column + head_dim : at_column + 2 * head_dim] = turn(
                keys, table_ref, -1
            ).astype(bf16)
            grads[:, at_column + 2 * head_dim : at_column + 3 * head_dim] = values.astype(bf16)
        for k in range(spans):
            started[k].wait()
            made = turned(grads[...], held[k])
            span_columns = slice(k * depth, (k + 1) * depth)
            side[0:1, span_columns] = jnp.sum(
                made * normal_ref[:, span_columns].astype(f32), axis=0, keepdims=True
            )
            side[1:2, span_columns] = jnp.sum(made, axis=0, keepdims=True)
            both = (made * gain_ref[0:1, span_columns] + part_ref[:, span_columns]).astype(bf16)
            low[:, span_columns] = both[:block]
            high[:, span_columns] = both[block:]

    ins = [(array, whole(array)) for array in (turned_back, own, came)]
    ins += [(w, kept_out) for w in weights]
    ins += [(part, whole(part)), (normal, whole(normal))]
    ins += [(gains, whole(gains)), (tables, whole(tables))]
    outs = [full_out((span_rows, columns)), full_out((2, width), f32)]
    outs += [full_out((block, width))] * 2
    scratch = [pltpu.VMEM((spans, depth, columns), bf16), pltpu.SemaphoreType.DMA((spans,))]
    return run(order, flags, kernel, ins, outs, scratch, "project_back")


def weight_sums(order, flags, lefts, rights, by_rows, spans):
    counts = [sum(piece.shape[0] for piece in lefts[s][0]) for s in (0, 1)]
    rows = max(counts)
    left_width = sum(group[0].shape[1] for group in lefts[0])
    right_width = sum(group[0].shape[1] for group in rights[0])
    if by_rows:
        tile = left_width // spans
        steps, block = spans // 2, (tile, right_width)
    else:
        tile = min(512, left_width)
        while left_width % tile:
            tile //= 2
        steps, block = left_width // tile, (tile, right_width // 2)
    chunk = min(1024, block[1])
    while right_width % chunk:
        chunk //= 2
    pieces = [
        [piece for groups in (lefts[s], rights[s]) for group in groups for piece in group]
        for s in (0, 1)
    ]
    most = max(len(p) for p in pieces)

    def kernel(flag_ref, *refs):
        piece_refs = (refs[: len(pieces[0])], refs[len(pieces[0]) : len(pieces[0]) + len(pieces[1])])
        keep, send, left, right, flipped, sems = refs[len(pieces[0]) + len(pieces[1]) :]
        g = pl.program_id(0)
        for s in (0, 1):

            @pl.when((g == 0) & (flag_ref[2] == s))
            def _(s=s):
                targets = []
                for held, groups in ((left, lefts[s]), (right, rights[s])):
                    column = 0
                    for group in groups:
                        row, wide = 0, group[0].shape[1]
                        for piece in group:
                            targets.append(
                                held.at[row : row + piece.shape[0], column : column + wide]
                            )
                            row += piece.shape[0]
                        column += wide
                started = copies(
                    piece_refs[s], targets, [sems.at[j] for j in range(len(targets))]
                )
                if counts[s] < rows:
                    left[counts[s] :, :] = jnp.zeros((rows - counts[s], left_width), bf16)
                    right[counts[s] :, :] = jnp.zeros((rows - counts[s], right_width), bf16)
                for copy in started:
                    copy.wait()

        def product(column, store):
            flipped[...] = left[:, pl.ds(pl.multiple_of(column, LANES), tile)].T

            def one(c, _):
                columns = pl.ds(pl.multiple_of(c * chunk, chunk), chunk)
                store(c, plain(flipped[...], right[:, columns]).astype(bf16))
                return 0

            lax.fori_loop(0, right_width // chunk, one, 0)

        if by_rows:

            def to(target):
                def store(c, made):
                    target[:, pl.ds(pl.multiple_of(c * chunk, chunk), chunk)] = made

                return store

            product(g * tile, to(keep))
            product((g + steps) * tile, to(send))
        else:
            half = right_width // 2 // chunk

            def store(c, made):
                @pl.when(c < half)
                def _():
                    keep[:, pl.ds(pl.multiple_of(c * chunk, chunk), chunk)] = made

                @pl.when(c >= half)
                def _():
                    send[:, pl.ds(pl.multiple_of((c - half) * chunk, chunk), chunk)] = made

            product(g * tile, store)

    ins = [(piece, kept_out) for s in (0, 1) for piece in pieces[s]]
    dims = (steps * tile, block[1])
    outs = [(shape(dims), pl.BlockSpec(block, lambda g: (g, 0)))] * 2
    scratch = [
        pltpu.VMEM((rows, left_width), bf16),
        pltpu.VMEM((rows, right_width), bf16),
        pltpu.VMEM((tile, rows), bf16),
        pltpu.SemaphoreType.DMA((most,)),
    ]
    return run(
        order, flags, kernel, ins, outs, scratch, "weight_sums", grid=(steps,)
    )


def owner_sums(order, flags, lefts, rights):
    left_width, right_width = lefts[0][0].shape[1], rights[0][0].shape[1]
    rows = sum(piece.shape[0] for piece in lefts[0])
    count = len(lefts)
    tile = min(512, left_width)
    while left_width % tile:
        tile //= 2
    pieces = [lefts[m] + rights[m] for m in range(count)]
    most = max(len(p) for p in pieces)

    def kernel(flag_ref, *refs):
        piece_refs, refs = refs[: sum(map(len, pieces))], refs[sum(map(len, pieces)) :]
        out, left, right, flipped, sems = refs
        started, used = [], 0
        for m in range(count):
            targets = []
            for held, group in ((left, lefts[m]), (right, rights[m])):
                row = 0
                for piece in group:
                    targets.append(held.at[m, row : row + piece.shape[0]])
                    row += piece.shape[0]
            started.append(
                copies(
                    piece_refs[used : used + len(targets)],
                    targets,
                    [sems.at[m, j] for j in range(len(targets))],
                )
            )
            used += len(targets)
        for m in range(count):
            for copy in started[m]:
                copy.wait()

            def one(t, _, m=m):
                block = pl.ds(pl.multiple_of(t * tile, tile), tile)
                flipped[...] = left[m, :, block].T
                made = plain(flipped[...], right[m])
                out[block, :] = made if m == 0 else out[block, :] + made
                return 0

            lax.fori_loop(0, left_width // tile, one, 0)

    ins = [(piece, kept_out) for group in pieces for piece in group]
    outs = [full_out((left_width, right_width), f32)]
    scratch = [
        pltpu.VMEM((count, rows, left_width), bf16),
        pltpu.VMEM((count, rows, right_width), bf16),
        pltpu.VMEM((tile, rows), bf16),
        pltpu.SemaphoreType.DMA((count, most)),
    ]
    return run(order, flags, kernel, ins, outs, scratch, "owner_sums")[0]


def fold(order, flags, keep, came, dim):
    rows, columns = keep.shape
    if dim == 0:
        tile = rows // 4
        steps, block = rows // 2 // tile, (tile, columns)
        places = [lambda g: (g, 0), lambda g: (g + steps, 0)]
        half = (rows // 2, columns)
    else:
        tile = rows // 4
        steps, block = rows // tile, (tile, columns // 2)
        places = [lambda g: (g, 0), lambda g: (g, 1)]
        half = (rows, columns // 2)

    def kernel(flag_ref, keep_low, keep_high, came_low, came_high, low, high):
        low[...] = (keep_low[...].astype(f32) + came_low[...].astype(f32)).astype(bf16)
        high[...] = (keep_high[...].astype(f32) + came_high[...].astype(f32)).astype(bf16)

    ins = [(array, pl.BlockSpec(block, place)) for array in (keep, came) for place in places]
    outs = [(shape(half), pl.BlockSpec(block, lambda g: (g, 0)))] * 2
    return run(order, flags, kernel, ins, outs, [], "fold", grid=(steps,))


def shards(
    block_input,
    out_grad,
    triple_weight,
    output_weight,
    expand_weight,
    contract_weight,
    norm_gains,
    norm_biases,
):
    section = lax.axis_index("pipe")
    span = lax.axis_index("ctx")
    lane = lax.axis_index("tp")
    spans = lax.axis_size("ctx")
    lanes = lax.axis_size("tp")
    micros, rows, width = block_input.shape
    span_rows = rows * lanes
    heads = triple_weight.shape[2]
    head_dim = triple_weight.shape[4]
    across_units = heads * head_dim
    scale = head_dim ** (-0.5)
    first_section = section == 0
    both = (0, 1)

    def hop(array, axis, step, sections):
        size = lax.axis_size(axis)
        pairs = [(s * size + a, s * size + (a ^ step)) for s in sections for a in range(size)]
        return lax.ppermute(array, ("pipe", axis), pairs)

    order = Order()

    def flags_for(wanted):
        return jnp.stack([jnp.asarray(wanted), span, section]).astype(jnp.int32)

    flags = [flags_for(section == s) for s in both]
    always = flags_for(1)

    kept = [[SimpleNamespace() for _ in range(micros)] for _ in both]
    due = {}
    slot_index = [0]

    def slot(hops, kernels=()):
        now = slot_index[0]
        slot_index[0] += 1
        ready = due.pop(now, [])
        hops = [h if len(h) == 3 else h + (1,) for h in hops]
        if hops:
            gated = fence([operand for operand, _, _ in hops], order.last + ready)
            order.last = [min(gated, key=lambda array: array.size)]
            for passed, (_, go, slots) in zip(gated, hops):
                results = go(passed)
                results = results if isinstance(results, list) else [results]
                due.setdefault(now + slots, []).extend(results)
        else:
            order.last = order.last + ready
        for kernel in kernels:
            kernel()

    def halved(keep, came, dim):
        middle = keep.shape[dim] // 2
        total = keep.astype(f32) + came.astype(f32)
        return (
            lax.slice_in_dim(total, 0, middle, axis=dim).astype(bf16),
            lax.slice_in_dim(total, middle, 2 * middle, axis=dim).astype(bf16),
        )

    def spread_hops(pieces, axis, axis_name, sections, first):
        step = lax.axis_size(axis_name) // 4
        going = first
        while step:
            pieces.append(hop(going, axis_name, step, sections))
            going = jnp.concatenate(pieces, axis=axis)
            step //= 2
        return pieces[-1]

    def fold_hops(k, first, axis_name, dim, sections):
        step, size = 1, lax.axis_size(axis_name)
        while 2 * step < size:
            came = hop(first, axis_name, step, sections)
            k.keep, k.send = halved(k.keep, came, dim)
            first = k.send
            step *= 2
        return came

    depth = width // spans
    far = spans // 2
    assert depth == across_units
    small = jnp.concatenate([norm_gains[0], norm_biases[0]], axis=0)
    packed = jnp.concatenate(
        [triple_weight[0].reshape(depth, -1), output_weight[0].reshape(-1, depth)],
        axis=1,
    )
    packed = jnp.pad(packed, ((0, 16), (0, 0)))
    packed = lax.dynamic_update_slice(packed, small, (depth, 0))
    own_expand, own_contract = expand_weight[0], contract_weight[0]
    hidden = own_expand.shape[1]
    inputs = xor_blocks(block_input, span, spans)
    cotangent = xor_blocks(out_grad, span, spans)
    early = jnp.where(first_section, inputs, cotangent)

    in_row = jnp.arange(rows, dtype=jnp.int32)
    in_span = jnp.concatenate([(lane ^ j) * rows + in_row for j in doubling(lanes)])
    positions = span * span_rows + in_span
    key_positions = jnp.stack([(span ^ k) * span_rows + in_span for k in doubling(spans)])
    tables = rope_tables(positions)
    position_column = positions[:, None]
    key_positions = key_positions[:, None, :]

    def blocks_of(own, came):
        held, step = {0: own, far: came}, far // 2
        while step:
            for k in list(held):
                held[k ^ step] = hop(held[k], "ctx", step, both)
            step //= 2
        return [held[k] for k in doubling(spans)]

    lane_offsets = doubling(lanes)

    def across(array, j, source):
        pairs = [(source * lanes + a, (1 - source) * lanes + (a ^ j)) for a in range(lanes)]
        return lax.ppermute(array, ("pipe", "tp"), pairs)

    def rows_far(s, m):
        k = kept[s][m]

        def go(passed):
            k.rows = passed
            k.pieces = [passed, hop(passed, "tp", lanes // 2, (s,))]
            return k.pieces[1]

        return k.rows, go

    def rows_near(s, m):
        k = kept[s][m]

        def go(passed):
            last_piece = spread_hops(k.pieces, 0, "tp", (s,), passed)
            k.row_pieces = [piece[None] for piece in k.pieces]
            return last_piece

        return jnp.concatenate(k.pieces, axis=0), go

    def one_way(array, direction, s):
        pairs = [
            (s * spans + a, s * spans + (a ^ far))
            for a in range(spans)
            if direction * ((a ^ far) - a) > 0
        ]
        return lax.ppermute(array, ("pipe", "ctx"), pairs)

    def pair_far(s, m):
        k = kept[s][m]

        def go(passed):
            k.pairs = [passed, one_way(passed, 1, s)]
            return k.pairs[1]

        return k.pair, go

    def pair_near(s, m):
        k = kept[s][m]

        def go(passed):
            return spread_hops(k.pairs, 0, "ctx", (s,), passed)

        return jnp.concatenate(k.pairs, axis=0), go

    def pair_grad_near(s, m):
        k = kept[s][m].pair_grad
        return k.send, lambda passed: fold_hops(k, passed, "ctx", 0, (s,))

    def pair_grad_far(s, m):
        k = kept[s][m].pair_grad

        def go(passed):
            k.came = one_way(passed, -1, s)
            return k.came

        return k.send, go

    def sum_near(s, k):
        k.keep, going = k.blocks
        return going, lambda passed: fold_hops(k, passed, "tp", 0, (s,))

    def sum_far(s, k):
        def go(passed):
            k.blocks, k.arrived = [k.keep], [hop(passed, "tp", lanes // 2, (s,))]
            return k.arrived[0]

        return k.send, go

    def units_far(m):
        k = kept[0][m]

        def go(passed):
            k.all_units = [passed, hop(passed, "ctx", far, (0,))]
            return k.all_units[1]

        return k.units, go

    def units_near(m):
        k = kept[0][m]

        def go(passed):
            return spread_hops(k.all_units, 0, "ctx", (0,), passed)

        return jnp.concatenate(k.all_units, axis=0), go

    def column_hops(m):
        k = kept[0][m]
        k.own_columns = [k.columns[0]]

        def one(j):
            def go(passed):
                k.own_columns.append(hop(passed, "ctx", doubling(spans)[j], (0,)))
                return k.own_columns[-1]

            return k.columns[j], go

        return [one(j) for j in range(1, spans)]

    def total_of(k):
        return sum(array.astype(f32) for array in [k.blocks[0], *k.arrived])

    def norm_back(upstream, combined, entering):
        normalized, inverse = normalize(entering.astype(f32))
        return (
            upstream.astype(f32)
            + inverse
            * (
                combined
                - jnp.mean(combined, axis=-1, keepdims=True)
                - normalized * jnp.mean(combined * normalized, axis=-1, keepdims=True)
            )
        ).astype(bf16)

    def middle_of(m):
        return (inputs[m].astype(f32) + total_of(kept[0][m])).astype(bf16)

    def entry_of(m):
        k = kept[1][m]
        return norm_back(cotangent[m], total_of(k), k.rows)

    def hand_one(s, m):
        k, other = kept[s][m], kept[1 - s][m]
        k.given = middle_of(m) if s == 0 else entry_of(m)

        def go(passed):
            k.given = passed
            other.rows = across(passed, 0, s)
            return other.rows

        return k.given, go

    def run_project(s, m):
        k = kept[s][m]
        pieces, place = (early_pieces, m) if s == 0 else (k.row_pieces, 0)
        k.first, k.second, k.normal, k.queries, pair = project(
            order, flags[s], pieces, place, gains, biases, tables, packed, heads, head_dim
        )
        k.pair = pair[None]

    def run_expand(m):
        k = kept[0][m]
        k.units, k.slope = expand_up(
            order, flags[0], k.second, weights.expand, span_rows, across_units
        )

    def run_attend(m):
        k = kept[0][m]
        k.units, k.probs = attend(
            order,
            flags[0],
            k.units,
            k.queries,
            k.pairs,
            position_column,
            key_positions,
            scale,
        )

    def run_branch(m):
        k = kept[0][m]
        k.blocks = branch_out(
            order, flags[0], [(k.units, k.units)], contract, packed
        )

    def run_hidden_both(m):
        k = kept[1][m]
        k.upstream, k.active, k.hidden, k.part, k.side_second = hidden_both(
            order,
            flags[1],
            k.second,
            early_pieces,
            m,
            weights.expand,
            contract,
            k.normal,
            gains,
        )

    def run_attend_both(m):
        k = kept[1][m]
        k.attended, k.turned_back, keep, send = attend_both(
            order,
            flags[1],
            k.upstream,
            packed,
            k.queries,
            k.pairs,
            position_column,
            key_positions,
            tables,
            scale,
        )
        k.pair_grad = SimpleNamespace(keep=keep, send=send)

    def run_attend_back(m):
        k = kept[0][m]
        k.upstream, k.turned_back, keep, send, *k.columns = attend_back(
            order,
            flags[0],
            k.row_pieces,
            packed,
            k.queries,
            k.pairs,
            k.probs,
            tables,
            scale,
        )
        k.pair_grad = SimpleNamespace(keep=keep, send=send)

    def run_hidden_back(m):
        k = kept[0][m]
        k.hidden, k.part, k.side_second = hidden_back(
            order,
            flags[0],
            k.upstream,
            contract,
            weights.expand,
            k.slope,
            k.normal,
            gains,
        )

    def run_project_back(s, m):
        k = kept[s][m]
        own, arrived = k.pair_grad.keep, k.pair_grad.came
        k.stacked, k.side_first, *k.blocks = project_back(
            order,
            flags[s],
            k.turned_back,
            own.reshape(own.shape[1:]),
            arrived.reshape(arrived.shape[1:]),
            packed,
            k.part,
            k.normal,
            gains,
            tables,
        )

    def of(name, s, count=micros):
        return [getattr(kept[s][m], name) for m in range(count)]

    branch_sums, expand_sums, triple_sums = (SimpleNamespace(parts=[]) for _ in range(3))

    def run_sums(w, lefts, rights, by_rows):
        w.dim = 0 if by_rows else 1
        w.keep, w.send = weight_sums(order, always, lefts, rights, by_rows, spans)

    def wide_near(w):
        def go(passed):
            w.came = hop(passed, "ctx", 1, both)
            return w.came

        return w.send, go

    def run_fold(w):
        step = 2
        w.keep, w.send = fold(order, always, w.keep, w.came, w.dim)
        while 2 * step < spans:
            w.came = hop(w.send, "ctx", step, both)
            w.keep, w.send = fold(order, always, w.keep, w.came, w.dim)
            step *= 2

    def wide_far(w, start, stop):
        def go(passed):
            w.parts.append(hop(passed, "ctx", far, both))
            return w.parts[-1]

        return w.send[start:stop], go

    weights = SimpleNamespace(expand_came=[], contract_came=[])
    half_depth = depth // 2

    def expand_far(start, stop):
        def go(passed):
            weights.expand_came.append(hop(passed, "ctx", far, both))
            return weights.expand_came[-1]

        return own_expand[start:stop], go

    def packed_far(passed):
        weights.packed_came = hop(passed, "ctx", far, both)
        return weights.packed_came

    def packed_near(passed):
        weights.packed = blocks_of(packed, passed)
        return weights.packed[1:]

    def expand_near(passed):
        weights.expand = blocks_of(own_expand, passed)
        return weights.expand[1:]

    def contract_far(start, stop):
        def go(passed):
            weights.contract_came.append(hop(passed, "ctx", far, both))
            return weights.contract_came[-1]

        return own_contract[start:stop], go

    def contract_near(passed):
        weights.contract = blocks_of(own_contract, passed)
        return weights.contract[1:]

    def early_hops(passed):
        weights.early = [passed] + [hop(passed, "tp", j, both) for j in lane_offsets[1:]]
        return weights.early[1:]

    due[0] = [expand_far(0, half_depth)[1](own_expand[:half_depth])]
    slot([(packed, packed_far), expand_far(half_depth, depth), (early, early_hops)])
    early_pieces = weights.early
    cuts = [0, hidden // 4, 11 * hidden // 16, hidden]
    expand_came = jnp.concatenate(weights.expand_came, axis=0)
    slot(
        [
            (weights.packed_came, packed_near),
            (expand_came, expand_near),
            contract_far(cuts[0], cuts[1]),
        ]
    )
    packed = weights.packed
    small_full = jnp.concatenate(
        [piece[depth : depth + 4, :depth] for piece in packed], axis=1
    ).astype(f32)
    gains, biases = small_full[:2], small_full[2:]
    slot(
        [contract_far(cuts[1], cuts[2])],
        [lambda m=m: run_project(0, m) for m in range(micros)],
    )
    a, b = kept
    slot(
        [pair_far(0, 0), contract_far(cuts[2], cuts[3])],
        [lambda m=m: run_expand(m) for m in range(micros)],
    )
    contract_came = jnp.concatenate(weights.contract_came, axis=0)
    slot([(contract_came, contract_near), pair_near(0, 0)])
    contract = weights.contract
    slot([pair_far(0, 1)], [lambda: run_attend(0), lambda: run_branch(0)])
    slot([sum_near(0, a[0]), pair_near(0, 1)])
    slot([sum_far(0, a[0]), pair_far(0, 2)], [lambda: run_attend(1), lambda: run_branch(1)])
    slot([hand_one(0, 0), sum_near(0, a[1]), pair_near(0, 2)])
    slot(
        [rows_far(1, 0), sum_far(0, a[1])], [lambda: run_attend(2), lambda: run_branch(2)]
    )
    slot([rows_near(1, 0), hand_one(0, 1), sum_near(0, a[2])])
    slot([rows_far(1, 1), sum_far(0, a[2])], [lambda: run_project(1, 0)])
    slot(
        [pair_far(1, 0), rows_near(1, 1), hand_one(0, 2)], [lambda: run_hidden_both(0)]
    )
    slot([pair_near(1, 0), rows_far(1, 2)], [lambda: run_project(1, 1)])
    slot(
        [pair_far(1, 1), rows_near(1, 2)],
        [lambda: run_attend_both(0), lambda: run_hidden_both(1)],
    )
    slot([pair_grad_near(1, 0), pair_near(1, 1)], [lambda: run_project(1, 2)])
    last = micros - 1
    slot(
        [pair_grad_far(1, 0), pair_far(1, 2), units_far(last)],
        [lambda: run_attend_both(1), lambda: run_hidden_both(2)],
    )
    slot(
        [pair_grad_near(1, 1), pair_near(1, 2), units_near(last)],
        [lambda: run_project_back(1, 0)],
    )
    slot([sum_near(1, b[0]), pair_grad_far(1, 1)], [lambda: run_attend_both(2)])
    slot([sum_far(1, b[0]), pair_grad_near(1, 2)], [lambda: run_project_back(1, 1)])
    slot([hand_one(1, 0), sum_near(1, b[1]), pair_grad_far(1, 2)])
    slot([sum_far(1, b[1]), rows_far(0, 0)], [lambda: run_project_back(1, 2)])
    slot([sum_near(1, b[2]), hand_one(1, 1), rows_near(0, 0)])
    slot([sum_far(1, b[2]), rows_far(0, 1)], [lambda: run_attend_back(0)])
    slot(
        [hand_one(1, 2), rows_near(0, 1), pair_grad_near(0, 0)],
        [lambda: run_hidden_back(0)],
    )

    def run_branch_sums():
        run_sums(
            branch_sums,
            [[of("units", 0, last)], [of("active", 1), of("attended", 1)]],
            [[of("upstream", 0, last)], [of("upstream", 1)]],
            False,
        )

    slot(
        [rows_far(0, 2), pair_grad_far(0, 0)], [lambda: run_attend_back(1), run_branch_sums]
    )
    slot(
        [rows_near(0, 2), pair_grad_near(0, 1), wide_near(branch_sums)],
        [lambda: run_hidden_back(1), lambda: run_project_back(0, 0)],
    )
    slot([], [lambda: run_fold(branch_sums)])

    def run_expand_sums():
        run_sums(
            expand_sums,
            [[of("second", s)] for s in both],
            [[of("hidden", s)] for s in both],
            True,
        )

    def run_triple_sums():
        run_sums(
            triple_sums,
            [[of("first", s)] for s in both],
            [[of("stacked", s)] for s in both],
            True,
        )

    finals = SimpleNamespace()

    def run_final_branch():
        blocks = branch_out(
            order, flags[1], [(k.active, k.attended) for k in b], contract, packed
        )
        finals.keep = jnp.stack(blocks[0::2])
        finals.send = jnp.stack(blocks[1::2])

    def finals_near():
        return finals.send, lambda passed: fold_hops(finals, passed, "tp", 1, (1,))

    def finals_far():
        def go(passed):
            finals.came = hop(passed, "tp", lanes // 2, (1,))
            return finals.came

        return finals.send, go

    def run_owner_sums():
        k = a[last]
        branch_sums.whole = owner_sums(order, flags[0], [k.all_units], [k.own_columns])

    cut = [0, hidden // 2, hidden, hidden + across_units]
    slot(
        [wide_far(branch_sums, cut[0], cut[1]), pair_grad_far(0, 1)],
        [lambda: run_attend_back(2), lambda: run_hidden_back(2)],
    )
    slot(
        [wide_far(branch_sums, cut[1], cut[2]), pair_grad_near(0, 2)] + column_hops(last),
        [run_expand_sums, lambda: run_project_back(0, 1)],
    )
    slot(
        [
            wide_near(expand_sums),
            pair_grad_far(0, 2),
            wide_far(branch_sums, cut[2], cut[3]),
            sum_near(0, a[0]),
        ],
        [run_owner_sums],
    )
    slot([], [lambda: run_fold(expand_sums)])
    slot(
        [wide_far(expand_sums, 0, half_depth), sum_far(0, a[0]), sum_near(0, a[1])],
        [lambda: run_project_back(0, 2), run_triple_sums],
    )

    def side_of(mades):
        return sum(
            jnp.concatenate([k.side_first, k.side_second], axis=0) for k in mades
        )

    side = SimpleNamespace(all=jnp.where(first_section, side_of(a), side_of(b)))

    def side_ctx(passed):
        step = 1
        while step < spans:
            middle = passed.shape[1] // 2
            came = hop(passed[:, middle:], "ctx", step, both)
            passed = passed[:, :middle] + came
            step *= 2
        side.all = passed
        return came

    def side_near(passed):
        step = 1
        while 2 * step < lanes:
            came = hop(passed, "tp", step, both)
            passed = passed + came
            step *= 2
        side.all = passed
        return came

    def side_far(passed):
        came = hop(passed, "tp", lanes // 2, both)
        side.all = passed + came
        return came

    def wide_total(keep, parts):
        came = jnp.concatenate(parts, axis=0) if len(parts) > 1 else parts[0]
        return keep.astype(f32) + came.astype(f32)

    slot(
        [
            wide_near(triple_sums),
            wide_far(expand_sums, half_depth, depth),
            (side.all, side_ctx),
            sum_far(0, a[1]),
        ],
        [run_final_branch],
    )
    slot([], [lambda: run_fold(triple_sums)])
    slot(
        [
            wide_far(triple_sums, 0, half_depth),
            sum_near(0, a[2]),
            (side.all, side_near),
            finals_near(),
        ]
    )
    slot(
        [
            wide_far(triple_sums, half_depth, depth),
            sum_far(0, a[2]),
            (side.all, side_far),
            finals_far(),
        ]
    )
    triple_grads = wide_total(triple_sums.keep, triple_sums.parts)
    triple_grads = triple_grads.reshape(triple_weight.shape)
    branch_grads = wide_total(branch_sums.keep, branch_sums.parts)
    branch_grads = branch_grads + jnp.where(first_section, branch_sums.whole, 0.0)
    contract_grads, output_grads = branch_grads[:hidden], branch_grads[hidden:]
    expand_grads = wide_total(expand_sums.keep, expand_sums.parts)
    layer_outputs = jnp.stack(
        [
            jnp.where(
                first_section,
                kept[0][m].given,
                (
                    b[m].rows.astype(f32)
                    + finals.keep[m].astype(f32)
                    + finals.came[m].astype(f32)
                ).astype(bf16),
            )
            for m in range(micros)
        ]
    )
    entry_grads = jnp.stack(
        [
            jnp.where(
                first_section,
                norm_back(kept[0][m].rows, total_of(kept[0][m]), inputs[m]),
                kept[1][m].given,
            )
            for m in range(micros)
        ]
    )
    gain_grads = jnp.stack([side.all[0], side.all[2]])
    bias_grads = jnp.stack([side.all[1], side.all[3]])
    return (
        xor_blocks(layer_outputs, span, spans, inverse=True)[None],
        xor_blocks(entry_grads, span, spans, inverse=True)[None],
        triple_grads,
        output_grads.reshape(output_weight.shape),
        expand_grads[None],
        contract_grads[None],
        gain_grads[None],
        bias_grads[None],
    )


def solution(mesh):
    return jax.shard_map(
        shards,
        mesh=mesh,
        in_specs=(
            P(None, ("ctx", "tp"), None),
            P(None, ("ctx", "tp"), None),
            P("pipe", "ctx", "tp", None, None),
            P("pipe", "tp", None, "ctx"),
            P("pipe", "ctx", "tp"),
            P("pipe", "tp", "ctx"),
            P("pipe", None, "ctx"),
            P("pipe", None, "ctx"),
        ),
        out_specs=(
            P("pipe", None, ("ctx", "tp"), None),
            P("pipe", None, ("ctx", "tp"), None),
            P("pipe", "ctx", "tp", None, None),
            P("pipe", "tp", None, "ctx"),
            P("pipe", "ctx", "tp"),
            P("pipe", "tp", "ctx"),
            P("pipe", None, "ctx"),
            P("pipe", None, "ctx"),
        ),
        check_vma=False,
    )
```

```python
import functools
import math
from types import SimpleNamespace

import jax
import jax.numpy as jnp
from jax import lax
from jax.experimental import pallas as pl
from jax.experimental.pallas import tpu as pltpu
from jax.sharding import PartitionSpec as P

ROT = 64
LANES = 128
epsilon = 1e-05
masked_score = -1e30
f32 = jnp.float32
bf16 = jnp.bfloat16
mebibyte = 1024 * 1024
half_root = 0.7071067811865476
bell = 0.3989422804014327


def dot(a, b, dims):
    return lax.dot_general(a, b, (dims, ((), ())), preferred_element_type=f32)


def plain(a, b):
    return dot(a, b, ((1,), (0,)))


def turned(a, b):
    return dot(a, b, ((1,), (1,)))


def doubling(count):
    order, step = [0], count // 2
    while step:
        order += [k ^ step for k in order]
        step //= 2
    return order


def xor_blocks(values, index, count, inverse=False):
    width = values.shape[-1] // count
    order = doubling(count)

    def taken(places):
        return jnp.concatenate(
            [values[..., k * width : (k + 1) * width] for k in places], axis=-1
        )

    if inverse:
        values = taken([order.index(k) for k in range(count)])
    step = 1
    while step < count:
        swapped = taken([k ^ step for k in range(count)])
        values = jnp.where((index & step) != 0, swapped, values)
        step *= 2
    return values if inverse else taken(order)


def rope_tables(positions):
    half = ROT // 2
    frequency = 10000.0 ** (-jnp.arange(0, ROT, 2, dtype=f32) / ROT)
    angles = positions.astype(f32)[:, None] * frequency[None, :]
    cosine, sine = jnp.cos(angles), jnp.sin(angles)
    count = positions.shape[0]
    rest = jnp.zeros((count, LANES - ROT), f32)
    none = jnp.zeros((count, half), f32)
    return jnp.stack(
        [
            jnp.concatenate([cosine, cosine, rest + 1.0], axis=1),
            jnp.concatenate([-sine, none, rest], axis=1),
            jnp.concatenate([none, sine, rest], axis=1),
        ]
    )


def turn(values, tables, sign):
    half = ROT // 2
    part = values[:, :LANES]
    moved = (
        pltpu.roll(part, LANES - half, 1) * tables[1] + pltpu.roll(part, half, 1) * tables[2]
    )
    part = part * tables[0] + (moved if sign > 0 else -moved)
    return jnp.concatenate([part, values[:, LANES:]], axis=1)


def normalize(values):
    center = values - jnp.mean(values, axis=-1, keepdims=True)
    inverse = lax.rsqrt(jnp.mean(center * center, axis=-1, keepdims=True) + epsilon)
    return (center * inverse, inverse)


def whole(array):
    zeros = (0,) * array.ndim
    return pl.BlockSpec(array.shape, lambda *_: zeros)


def at(block, place):
    return pl.BlockSpec(block, lambda *_: place)


kept_out = pl.BlockSpec(memory_space=pl.ANY)


def shape(dims, dtype=bf16):
    return jax.ShapeDtypeStruct(dims, dtype)


class Order:
    def __init__(self):
        self.last = []

    def follow(self, results):
        self.last = [min(results, key=lambda array: array.size * array.dtype.itemsize)]

    def also(self, array):
        self.last = self.last + [array]


took = dict(
    project=7,
    expand=8,
    attend=5,
    branch=8,
    hidden_both=14,
    attend_both=11,
    attend_back=8,
    hidden_back=13,
    project_back=8,
    weight_sums=16,
    fold=7,
)
peak = 1.15e9


def run(order, flags, kernel, ins, outs, scratch, name, grid=(1,), work=0):
    taken = len(ins)
    ins = [(flags, pl.BlockSpec(memory_space=pltpu.SMEM))] + list(ins)
    ins += [(array, kept_out) for array in order.last]
    arrays = [array for array, _ in ins]
    once = grid == (1,)

    def sized(spec, dtype):
        if spec.block_shape is None:
            return spec, 0
        size = math.prod(spec.block_shape) * jnp.dtype(dtype).itemsize
        if not once:
            return spec, 2 * size
        single = pl.BlockSpec(
            spec.block_shape, spec.index_map, pipeline_mode=pl.Buffered(1)
        )
        return single, size

    in_specs = [sized(spec, array.dtype) for array, spec in ins]
    out_specs = [sized(spec, struct.dtype) for struct, spec in outs]
    held = sum(size for _, size in in_specs + out_specs)
    for buffer in scratch:
        if buffer.memory_space == pltpu.VMEM:
            held += math.prod(buffer.shape) * jnp.dtype(buffer.dtype).itemsize

    def body(flag_ref, *refs):
        @pl.when(flag_ref[0] == 1)
        def _():
            kernel(flag_ref, *refs[:taken], *refs[len(ins) - 1 :])

    results = pl.pallas_call(
        body,
        grid=grid,
        in_specs=[spec for spec, _ in in_specs],
        out_specs=[spec for spec, _ in out_specs],
        out_shape=[struct for struct, _ in outs],
        scratch_shapes=scratch,
        compiler_params=pltpu.CompilerParams(
            vmem_limit_bytes=int(held + (work + 4) * mebibyte)
        ),
        cost_estimate=pl.CostEstimate(
            flops=int(took[name] * peak), bytes_accessed=0, transcendentals=0
        ),
        name=name,
    )(*arrays)
    order.follow(results)
    return results


def fence(through, waits):
    count = len(through)

    def kernel(*refs):
        pass

    return pl.pallas_call(
        kernel,
        in_specs=[kept_out] * (count + len(waits)),
        out_specs=[kept_out] * count,
        out_shape=[shape(array.shape, array.dtype) for array in through],
        input_output_aliases={j: j for j in range(count)},
        compiler_params=pltpu.CompilerParams(vmem_limit_bytes=mebibyte),
        cost_estimate=pl.CostEstimate(flops=1, bytes_accessed=1, transcendentals=0),
        name="fence",
    )(*through, *waits)


def full_out(dims, dtype=bf16):
    zeros = (0,) * len(dims)
    return (shape(dims, dtype), pl.BlockSpec(dims, lambda *_: zeros))


def copies(sources, targets, sems):
    started = []
    for source, target, sem in zip(sources, targets, sems):
        copy = pltpu.make_async_copy(source, target, sem)
        copy.start()
        started.append(copy)
    return started


def project(order, flags, pieces, at_piece, gains, biases, tables, weights, heads, head_dim):
    count, width = 1, pieces[0].shape[2]
    span_rows = sum(piece.shape[1] for piece in pieces)
    rows = count * span_rows
    chunk = pieces[0].shape[1]
    spans = len(weights)
    depth = width // spans
    wide = 3 * head_dim
    columns = heads * wide

    def kernel(flag_ref, *refs):
        piece_refs = refs[: len(pieces)]
        gain_ref, bias_ref, table_ref = refs[len(pieces) : len(pieces) + 3]
        weight_refs = refs[len(pieces) + 3 : len(pieces) + 3 + spans]
        first, second, normal, queries, pair, held, sems = refs[len(pieces) + 3 + spans :]
        started = []
        for h in range(heads):
            started.append(
                copies(
                    [w.at[:depth, h * wide : (h + 1) * wide] for w in weight_refs],
                    [held.at[h, k * depth : (k + 1) * depth] for k in range(spans)],
                    [sems.at[h, k] for k in range(spans)],
                )
            )
        start = 0
        for piece_ref in piece_refs:
            chunks = piece_ref.shape[1] // chunk

            def one(i, _, piece_ref=piece_ref, start=start, chunks=chunks):
                m, c = i // chunks, i % chunks
                values = piece_ref[m, pl.ds(pl.multiple_of(c * chunk, chunk), chunk), :]
                normed, _ = normalize(values.astype(f32))
                to = pl.ds(
                    pl.multiple_of(m * span_rows + start + c * chunk, chunk), chunk
                )
                normal[to, :] = normed.astype(bf16)
                first[to, :] = (normed * gain_ref[0:1] + bias_ref[0:1]).astype(bf16)
                second[to, :] = (normed * gain_ref[1:2] + bias_ref[1:2]).astype(bf16)
                return 0

            lax.fori_loop(0, count * chunks, one, 0)
            start += piece_ref.shape[1]
        for h in range(heads):
            for copy in started[h]:
                copy.wait()

            def two(m, _, h=h):
                to = pl.ds(pl.multiple_of(m * span_rows, span_rows), span_rows)
                made = plain(first[to, :], held[h])
                queries[h, to, :] = turn(made[:, :head_dim], table_ref, 1).astype(bf16)
                pair[0, h, to, :] = turn(
                    made[:, head_dim : 2 * head_dim], table_ref, 1
                ).astype(bf16)
                pair[1, h, to, :] = made[:, 2 * head_dim :].astype(bf16)
                return 0

            lax.fori_loop(0, count, two, 0)

    ins = [(piece, at((1,) + piece.shape[1:], (at_piece, 0, 0))) for piece in pieces]
    ins += [(array, whole(array)) for array in (gains, biases, tables)]
    ins += [(w, kept_out) for w in weights]
    outs = [full_out((rows, width))] * 3 + [
        full_out((heads, rows, head_dim)),
        full_out((2, heads, rows, head_dim)),
    ]
    scratch = [
        pltpu.VMEM((heads, width, wide), bf16),
        pltpu.SemaphoreType.DMA((heads, spans)),
    ]
    return run(order, flags, kernel, ins, outs, scratch, "project")


def expand_up(order, flags, second, weights, span_rows):
    rows, width = second.shape
    depth, hidden = weights[0].shape
    spans = len(weights)
    tile = min(512, hidden)
    tiles = hidden // tile

    def kernel(flag_ref, *refs):
        second_ref, weight_refs = refs[0], refs[1 : 1 + spans]
        active, slope, held, sems = refs[1 + spans :]
        started = []
        for t in range(tiles):
            started.append(
                copies(
                    [w.at[:, t * tile : (t + 1) * tile] for w in weight_refs],
                    [held.at[t, k * depth : (k + 1) * depth] for k in range(spans)],
                    [sems.at[t, k] for k in range(spans)],
                )
            )
        for t in range(tiles):
            for copy in started[t]:
                copy.wait()

            def one(m, _, t=t):
                to = pl.ds(pl.multiple_of(m * span_rows, span_rows), span_rows)
                pre = plain(second_ref[to, :], held[t])
                risen = 0.5 * (1.0 + lax.erf(pre * half_root))
                columns = slice(t * tile, (t + 1) * tile)
                active[to, columns] = (pre * risen).astype(bf16)
                slope[to, columns] = (
                    risen + pre * jnp.exp(-0.5 * pre * pre) * bell
                ).astype(bf16)
                return 0

            lax.fori_loop(0, rows // span_rows, one, 0)

    ins = [(second, whole(second))] + [(w, kept_out) for w in weights]
    outs = [full_out((rows, hidden))] * 2
    scratch = [
        pltpu.VMEM((tiles, width, tile), bf16),
        pltpu.SemaphoreType.DMA((tiles, spans)),
    ]
    return run(order, flags, kernel, ins, outs, scratch, "expand")


def spread(refs):
    return [ref.at[j] for ref in refs for j in range(ref.shape[0])]


def attention(here, pairs, head, row_ref, key_ref, scale):
    scores = []
    for k, pair in enumerate(pairs):
        raw = turned(here, pair[0, head]) * scale
        scores.append(jnp.where(key_ref[k] <= row_ref[...], raw, masked_score))
    top = functools.reduce(
        jnp.maximum, [jnp.max(part, axis=1, keepdims=True) for part in scores]
    )
    scores = [jnp.exp(part - top) for part in scores]
    inverse = 1.0 / sum(jnp.sum(part, axis=1, keepdims=True) for part in scores)
    return [part * inverse for part in scores]


def attend(order, flags, queries, pairs, positions, key_positions, scale):
    heads, rows, head_dim = queries.shape
    spans = sum(pair.shape[0] for pair in pairs)

    def kernel(flag_ref, query_ref, *refs):
        views, refs = spread(refs[: len(pairs)]), refs[len(pairs) :]
        row_ref, key_ref, attended, probs = refs
        for h in range(heads):
            parts = attention(query_ref[h], views, h, row_ref, key_ref, scale)
            summed = None
            for k in range(spans):
                part = parts[k].astype(bf16)
                probs[k, h] = part
                term = plain(part, views[k][1, h])
                summed = term if summed is None else summed + term
            attended[:, h * head_dim : (h + 1) * head_dim] = summed.astype(bf16)

    ins = [
        (array, whole(array)) for array in (queries, *pairs, positions, key_positions)
    ]
    outs = [full_out((rows, heads * head_dim)), full_out((spans, heads, rows, rows))]
    work = spans * rows * rows * 4 * heads * 4 / mebibyte
    return run(order, flags, kernel, ins, outs, [], "attend", work=work)


def attention_grads(grad, here, parts, views, head, keep, send, scale):
    half = keep.shape[0]
    grad_probs = [turned(grad, view[1, head]) for view in views]
    delta = sum(
        jnp.sum(part.astype(f32) * slope, axis=1, keepdims=True)
        for part, slope in zip(parts, grad_probs)
    )
    query_grad = None
    for k, view in enumerate(views):
        slopes = (parts[k].astype(f32) * (grad_probs[k] - delta)).astype(bf16)
        term = plain(slopes, view[0, head])
        query_grad = term if query_grad is None else query_grad + term
        side = keep if k < half else send
        side[k % half, 0, head] = (dot(slopes, here, ((0,), (0,))) * scale).astype(bf16)
        side[k % half, 1, head] = dot(parts[k].astype(bf16), grad, ((0,), (0,))).astype(bf16)
    return query_grad * scale


def attend_both(
    order, flags, rows_in, packed, queries, pairs, positions, key_positions, tables, scale
):
    heads, rows, head_dim = queries.shape
    width = rows_in.shape[1]
    spans = len(packed)
    across, depth = heads * head_dim, width // spans
    half = spans // 2

    def kernel(flag_ref, rows_ref, *refs):
        packed_refs, refs = refs[:spans], refs[spans:]
        query_ref, refs = refs[0], refs[1:]
        views, refs = spread(refs[: len(pairs)]), refs[len(pairs) :]
        row_ref, key_ref, table_ref, attended, turned_back, keep, send, held, sems = refs
        started = copies(
            [w.at[:across, 3 * across : 3 * across + depth] for w in packed_refs],
            [held.at[:, k * depth : (k + 1) * depth] for k in range(spans)],
            [sems.at[k] for k in range(spans)],
        )
        all_parts = []
        for h in range(heads):
            parts = attention(query_ref[h], views, h, row_ref, key_ref, scale)
            summed = None
            for k in range(spans):
                term = plain(parts[k].astype(bf16), views[k][1, h])
                summed = term if summed is None else summed + term
            attended[:, h * head_dim : (h + 1) * head_dim] = summed.astype(bf16)
            all_parts.append(parts)
        for copy in started:
            copy.wait()
        grads = turned(rows_ref[...], held[...]).astype(bf16)
        for h in range(heads):
            made = attention_grads(
                grads[:, h * head_dim : (h + 1) * head_dim],
                query_ref[h],
                all_parts[h],
                views,
                h,
                keep,
                send,
                scale,
            )
            turned_back[h] = turn(made, table_ref, -1).astype(bf16)

    ins = [(rows_in, whole(rows_in))] + [(w, kept_out) for w in packed]
    ins += [
        (array, whole(array)) for array in (queries, *pairs, positions, key_positions, tables)
    ]
    outs = [full_out((rows, across)), full_out((heads, rows, head_dim))]
    outs += [full_out((half, 2, heads, rows, head_dim))] * 2
    scratch = [pltpu.VMEM((across, width), bf16), pltpu.SemaphoreType.DMA((spans,))]
    work = spans * rows * rows * 4 * (heads + 4) / mebibyte
    return run(order, flags, kernel, ins, outs, scratch, "attend_both", work=work)


def hidden_both(order, flags, second, pieces, at_piece, expand, contract, normal, gains):
    rows, width = second.shape
    hidden, depth = contract[0].shape
    spans = len(contract)
    tile = min(512, hidden)
    tiles = hidden // tile

    def kernel(flag_ref, second_ref, *refs):
        piece_refs, refs = refs[: len(pieces)], refs[len(pieces) :]
        expand_refs, refs = refs[:spans], refs[spans:]
        contract_refs, refs = refs[:spans], refs[spans:]
        normal_ref, gain_ref, rows_out, active, grads, part, side, *refs = refs
        held_up, held_down, sems_up, sems_down = refs
        started = []
        for t in range(tiles):
            block = slice(t * tile, (t + 1) * tile)
            places = [slice(k * depth, (k + 1) * depth) for k in range(spans)]
            up = copies(
                [w.at[:, block] for w in expand_refs],
                [held_up.at[place, block] for place in places],
                [sems_up.at[t, k] for k in range(spans)],
            )
            down = copies(
                [w.at[block, :] for w in contract_refs],
                [held_down.at[block, place] for place in places],
                [sems_down.at[t, k] for k in range(spans)],
            )
            started.append((up, down))
        start = 0
        for piece_ref in piece_refs:
            size = piece_ref.shape[1]
            rows_out[start : start + size, :] = piece_ref[0]
            start += size
        for t in range(tiles):
            block = slice(t * tile, (t + 1) * tile)
            for copy in started[t][0] + started[t][1]:
                copy.wait()
            pre = plain(second_ref[...], held_up[:, block])
            risen = 0.5 * (1.0 + lax.erf(pre * half_root))
            active[:, block] = (pre * risen).astype(bf16)
            slope = risen + pre * jnp.exp(-0.5 * pre * pre) * bell
            grads[:, block] = (turned(rows_out[...], held_down[block, :]) * slope).astype(bf16)
        for k in range(spans):
            place = slice(k * depth, (k + 1) * depth)
            made = turned(grads[...], held_up[place, :])
            side[0:1, place] = jnp.sum(
                made * normal_ref[:, place].astype(f32), axis=0, keepdims=True
            )
            side[1:2, place] = jnp.sum(made, axis=0, keepdims=True)
            part[:, place] = made * gain_ref[1:2, place]

    ins = [(second, whole(second))]
    ins += [(piece, at((1,) + piece.shape[1:], (at_piece, 0, 0))) for piece in pieces]
    ins += [(w, kept_out) for w in expand] + [(w, kept_out) for w in contract]
    ins += [(normal, whole(normal)), (gains, whole(gains))]
    outs = [
        full_out((rows, width)),
        full_out((rows, hidden)),
        full_out((rows, hidden)),
        full_out((rows, width), f32),
        full_out((2, width), f32),
    ]
    scratch = [
        pltpu.VMEM((width, hidden), bf16),
        pltpu.VMEM((hidden, width), bf16),
        pltpu.SemaphoreType.DMA((tiles, spans)),
        pltpu.SemaphoreType.DMA((tiles, spans)),
    ]
    return run(order, flags, kernel, ins, outs, scratch, "hidden_both")


def branch_out(order, flags, groups, contract, packed):
    hidden, depth = contract[0].shape
    across = groups[0][1].shape[1]
    spans = len(contract)
    width = depth * spans
    span_rows = groups[0][0].shape[0]
    block = span_rows // 2
    count = len(groups)

    def kernel(flag_ref, *refs):
        group_refs, refs = refs[: 2 * count], refs[2 * count :]
        contract_refs, packed_refs = refs[:spans], refs[spans : 2 * spans]
        blocks, refs = refs[2 * spans : 2 * (spans + count)], refs[2 * (spans + count) :]
        held, held_out, sems = refs
        outputs = [w.at[:across, 3 * across : 3 * across + depth] for w in packed_refs]
        started = copies(
            [ref for k in range(spans) for ref in (outputs[k], contract_refs[k])],
            [ref for k in range(spans) for ref in (held_out.at[k], held.at[k])],
            [sems.at[j] for j in range(2 * spans)],
        )
        for k in range(spans):
            started[2 * k].wait()
            started[2 * k + 1].wait()
            columns = slice(k * depth, (k + 1) * depth)
            for c in range(count):
                made = plain(group_refs[2 * c + 1][...], held_out[k])
                made = made + plain(group_refs[2 * c][...], held[k])
                blocks[2 * c][:, columns] = made[:block].astype(bf16)
                blocks[2 * c + 1][:, columns] = made[block:].astype(bf16)

    ins = []
    for active, attended in groups:
        ins += [(active, whole(active)), (attended, whole(attended))]
    ins += [(w, kept_out) for w in contract] + [(w, kept_out) for w in packed]
    outs = [full_out((block, width))] * (2 * count)
    scratch = [
        pltpu.VMEM((spans, hidden, depth), bf16),
        pltpu.VMEM((spans, across, depth), bf16),
        pltpu.SemaphoreType.DMA((2 * spans,)),
    ]
    return run(order, flags, kernel, ins, outs, scratch, "branch")


def attend_back(order, flags, pieces, packed, queries, pairs, probs, tables, scale):
    rows = sum(piece.shape[1] for piece in pieces)
    width = pieces[0].shape[2]
    heads, _, head_dim = queries.shape
    spans = len(packed)
    across, depth = heads * head_dim, width // spans
    half = spans // 2

    def kernel(flag_ref, *refs):
        piece_refs, refs = refs[: len(pieces)], refs[len(pieces) :]
        packed_refs, refs = refs[:spans], refs[spans:]
        query_ref, refs = refs[0], refs[1:]
        views, refs = spread(refs[: len(pairs)]), refs[len(pairs) :]
        prob_ref, table_ref, rows_out, turned_back, keep, send, held, sems = refs
        started = copies(
            [w.at[:across, 3 * across : 3 * across + depth] for w in packed_refs],
            [held.at[:, k * depth : (k + 1) * depth] for k in range(spans)],
            [sems.at[k] for k in range(spans)],
        )
        start = 0
        for piece_ref in piece_refs:
            size = piece_ref.shape[1]
            rows_out[start : start + size, :] = piece_ref[0]
            start += size
        for copy in started:
            copy.wait()
        grads = turned(rows_out[...], held[...]).astype(bf16)
        for h in range(heads):
            made = attention_grads(
                grads[:, h * head_dim : (h + 1) * head_dim],
                query_ref[h],
                [prob_ref[k, h] for k in range(spans)],
                views,
                h,
                keep,
                send,
                scale,
            )
            turned_back[h] = turn(made, table_ref, -1).astype(bf16)

    ins = [(piece, whole(piece)) for piece in pieces] + [(w, kept_out) for w in packed]
    ins += [(array, whole(array)) for array in (queries, *pairs, probs, tables)]
    outs = [full_out((rows, width)), full_out((heads, rows, head_dim))]
    outs += [full_out((half, 2, heads, rows, head_dim))] * 2
    scratch = [pltpu.VMEM((across, width), bf16), pltpu.SemaphoreType.DMA((spans,))]
    work = spans * rows * rows * 4 * 4 / mebibyte
    return run(order, flags, kernel, ins, outs, scratch, "attend_back", work=work)


def hidden_back(order, flags, upstream, contract, expand, slope, normal, gains):
    span_rows, width = upstream.shape
    hidden, depth = contract[0].shape
    spans = len(contract)
    tile = min(512, hidden)
    tiles = hidden // tile

    def kernel(flag_ref, *refs):
        upstream_ref, refs = refs[0], refs[1:]
        contract_refs, refs = refs[:spans], refs[spans:]
        expand_refs, refs = refs[:spans], refs[spans:]
        slope_ref, normal_ref, gain_ref, grads, part, side, held, held_up, sems, sems_up = refs
        started = [
            copies(
                [w.at[t * tile : (t + 1) * tile, :] for w in contract_refs],
                [held.at[t, :, k * depth : (k + 1) * depth] for k in range(spans)],
                [sems.at[t, k] for k in range(spans)],
            )
            for t in range(tiles)
        ]
        started_up = copies(
            expand_refs, [held_up.at[k] for k in range(spans)], [sems_up.at[k] for k in range(spans)]
        )
        for t in range(tiles):
            for copy in started[t]:
                copy.wait()
            columns = slice(t * tile, (t + 1) * tile)
            grads[:, columns] = (
                turned(upstream_ref[...], held[t]) * slope_ref[:, columns].astype(f32)
            ).astype(bf16)
        for k in range(spans):
            started_up[k].wait()
            made = turned(grads[...], held_up[k])
            columns = slice(k * depth, (k + 1) * depth)
            side[0:1, columns] = jnp.sum(
                made * normal_ref[:, columns].astype(f32), axis=0, keepdims=True
            )
            side[1:2, columns] = jnp.sum(made, axis=0, keepdims=True)
            part[:, columns] = made * gain_ref[1:2, columns]

    ins = [(upstream, whole(upstream))]
    ins += [(w, kept_out) for w in contract] + [(w, kept_out) for w in expand]
    ins += [
        (slope, whole(slope)),
        (normal, whole(normal)),
        (gains, whole(gains)),
    ]
    outs = [
        full_out((span_rows, hidden)),
        full_out((span_rows, width), f32),
        full_out((2, width), f32),
    ]
    scratch = [
        pltpu.VMEM((tiles, tile, width), bf16),
        pltpu.VMEM((spans, depth, hidden), bf16),
        pltpu.SemaphoreType.DMA((tiles, spans)),
        pltpu.SemaphoreType.DMA((spans,)),
    ]
    return run(order, flags, kernel, ins, outs, scratch, "hidden_back")


def project_back(
    order, flags, turned_back, own, came, weights, part, normal, gains, tables
):
    heads, span_rows, head_dim = turned_back.shape
    spans = len(weights)
    width = part.shape[1]
    depth, columns = width // spans, 3 * heads * head_dim
    block = span_rows // 2

    def kernel(flag_ref, *refs):
        query_ref, own_ref, came_ref, refs = refs[0], refs[1], refs[2], refs[3:]
        weight_refs, refs = refs[:spans], refs[spans:]
        part_ref, normal_ref, gain_ref, table_ref, grads, side, *refs = refs
        low, high, held, sems = refs
        started = copies(
            [w.at[:depth, :columns] for w in weight_refs],
            [held.at[k] for k in range(spans)],
            [sems.at[k] for k in range(spans)],
        )
        for h in range(heads):
            at_column = h * 3 * head_dim
            keys = own_ref[0, h].astype(f32) + came_ref[0, h].astype(f32)
            values = own_ref[1, h].astype(f32) + came_ref[1, h].astype(f32)
            grads[:, at_column : at_column + head_dim] = query_ref[h]
            grads[:, at_column + head_dim : at_column + 2 * head_dim] = turn(
                keys, table_ref, -1
            ).astype(bf16)
            grads[:, at_column + 2 * head_dim : at_column + 3 * head_dim] = values.astype(bf16)
        for k in range(spans):
            started[k].wait()
            made = turned(grads[...], held[k])
            span_columns = slice(k * depth, (k + 1) * depth)
            side[0:1, span_columns] = jnp.sum(
                made * normal_ref[:, span_columns].astype(f32), axis=0, keepdims=True
            )
            side[1:2, span_columns] = jnp.sum(made, axis=0, keepdims=True)
            both = (made * gain_ref[0:1, span_columns] + part_ref[:, span_columns]).astype(bf16)
            low[:, span_columns] = both[:block]
            high[:, span_columns] = both[block:]

    ins = [(array, whole(array)) for array in (turned_back, own, came)]
    ins += [(w, kept_out) for w in weights]
    ins += [(part, whole(part)), (normal, whole(normal))]
    ins += [(gains, whole(gains)), (tables, whole(tables))]
    outs = [full_out((span_rows, columns)), full_out((2, width), f32)]
    outs += [full_out((block, width))] * 2
    scratch = [pltpu.VMEM((spans, depth, columns), bf16), pltpu.SemaphoreType.DMA((spans,))]
    return run(order, flags, kernel, ins, outs, scratch, "project_back")


def weight_sums(order, flags, lefts, rights, by_rows, spans):
    rows = sum(piece.shape[0] for piece in lefts[0][0])
    left_width = sum(group[0].shape[1] for group in lefts[0])
    right_width = sum(group[0].shape[1] for group in rights[0])
    if by_rows:
        tile = left_width // spans
        steps, block = spans // 2, (tile, right_width)
    else:
        tile = min(512, left_width)
        while left_width % tile:
            tile //= 2
        steps, block = left_width // tile, (tile, right_width // 2)
    chunk = min(1024, block[1])
    while right_width % chunk:
        chunk //= 2
    pieces = [
        [piece for groups in (lefts[s], rights[s]) for group in groups for piece in group]
        for s in (0, 1)
    ]
    most = max(len(p) for p in pieces)

    def kernel(flag_ref, *refs):
        piece_refs = (refs[: len(pieces[0])], refs[len(pieces[0]) : len(pieces[0]) + len(pieces[1])])
        keep, send, left, right, flipped, sems = refs[len(pieces[0]) + len(pieces[1]) :]
        g = pl.program_id(0)
        for s in (0, 1):

            @pl.when((g == 0) & (flag_ref[2] == s))
            def _(s=s):
                targets = []
                for held, groups in ((left, lefts[s]), (right, rights[s])):
                    column = 0
                    for group in groups:
                        row, wide = 0, group[0].shape[1]
                        for piece in group:
                            targets.append(
                                held.at[row : row + piece.shape[0], column : column + wide]
                            )
                            row += piece.shape[0]
                        column += wide
                started = copies(
                    piece_refs[s], targets, [sems.at[j] for j in range(len(targets))]
                )
                for copy in started:
                    copy.wait()

        def product(column, store):
            flipped[...] = left[:, pl.ds(pl.multiple_of(column, LANES), tile)].T

            def one(c, _):
                columns = pl.ds(pl.multiple_of(c * chunk, chunk), chunk)
                store(c, plain(flipped[...], right[:, columns]).astype(bf16))
                return 0

            lax.fori_loop(0, right_width // chunk, one, 0)

        if by_rows:

            def to(target):
                def store(c, made):
                    target[:, pl.ds(pl.multiple_of(c * chunk, chunk), chunk)] = made

                return store

            product(g * tile, to(keep))
            product((g + steps) * tile, to(send))
        else:
            half = right_width // 2 // chunk

            def store(c, made):
                @pl.when(c < half)
                def _():
                    keep[:, pl.ds(pl.multiple_of(c * chunk, chunk), chunk)] = made

                @pl.when(c >= half)
                def _():
                    send[:, pl.ds(pl.multiple_of((c - half) * chunk, chunk), chunk)] = made

            product(g * tile, store)

    ins = [(piece, kept_out) for s in (0, 1) for piece in pieces[s]]
    dims = (steps * tile, block[1])
    outs = [(shape(dims), pl.BlockSpec(block, lambda g: (g, 0)))] * 2
    scratch = [
        pltpu.VMEM((rows, left_width), bf16),
        pltpu.VMEM((rows, right_width), bf16),
        pltpu.VMEM((tile, rows), bf16),
        pltpu.SemaphoreType.DMA((most,)),
    ]
    return run(
        order, flags, kernel, ins, outs, scratch, "weight_sums", grid=(steps,)
    )


def fold(order, flags, keep, came, dim):
    rows, columns = keep.shape
    if dim == 0:
        tile = rows // 4
        steps, block = rows // 2 // tile, (tile, columns)
        places = [lambda g: (g, 0), lambda g: (g + steps, 0)]
        half = (rows // 2, columns)
    else:
        tile = rows // 4
        steps, block = rows // tile, (tile, columns // 2)
        places = [lambda g: (g, 0), lambda g: (g, 1)]
        half = (rows, columns // 2)

    def kernel(flag_ref, keep_low, keep_high, came_low, came_high, low, high):
        low[...] = (keep_low[...].astype(f32) + came_low[...].astype(f32)).astype(bf16)
        high[...] = (keep_high[...].astype(f32) + came_high[...].astype(f32)).astype(bf16)

    ins = [(array, pl.BlockSpec(block, place)) for array in (keep, came) for place in places]
    outs = [(shape(half), pl.BlockSpec(block, lambda g: (g, 0)))] * 2
    return run(order, flags, kernel, ins, outs, [], "fold", grid=(steps,))


def shards(
    block_input,
    out_grad,
    triple_weight,
    output_weight,
    expand_weight,
    contract_weight,
    norm_gains,
    norm_biases,
):
    section = lax.axis_index("pipe")
    span = lax.axis_index("ctx")
    lane = lax.axis_index("tp")
    spans = lax.axis_size("ctx")
    lanes = lax.axis_size("tp")
    micros, rows, width = block_input.shape
    span_rows = rows * lanes
    heads = triple_weight.shape[2]
    head_dim = triple_weight.shape[4]
    across_units = heads * head_dim
    scale = head_dim ** (-0.5)
    first_section = section == 0
    both = (0, 1)

    def hop(array, axis, step, sections):
        size = lax.axis_size(axis)
        pairs = [(s * size + a, s * size + (a ^ step)) for s in sections for a in range(size)]
        return lax.ppermute(array, ("pipe", axis), pairs)

    order = Order()

    def flags_for(wanted):
        return jnp.stack([jnp.asarray(wanted), span, section]).astype(jnp.int32)

    flags = [flags_for(section == s) for s in both]
    always = flags_for(1)

    kept = [[SimpleNamespace() for _ in range(micros)] for _ in both]
    due = {}
    slot_index = [0]

    def slot(hops, kernels=()):
        now = slot_index[0]
        slot_index[0] += 1
        ready = due.pop(now, [])
        hops = [h if len(h) == 3 else h + (1,) for h in hops]
        if hops:
            gated = fence([operand for operand, _, _ in hops], order.last + ready)
            order.last = [min(gated, key=lambda array: array.size)]
            for passed, (_, go, slots) in zip(gated, hops):
                results = go(passed)
                results = results if isinstance(results, list) else [results]
                due.setdefault(now + slots, []).extend(results)
        else:
            order.last = order.last + ready
        for kernel in kernels:
            kernel()

    def halved(keep, came, dim):
        middle = keep.shape[dim] // 2
        total = keep.astype(f32) + came.astype(f32)
        return (
            lax.slice_in_dim(total, 0, middle, axis=dim).astype(bf16),
            lax.slice_in_dim(total, middle, 2 * middle, axis=dim).astype(bf16),
        )

    def spread_hops(pieces, axis, axis_name, sections, first):
        step = lax.axis_size(axis_name) // 4
        going = first
        while step:
            pieces.append(hop(going, axis_name, step, sections))
            going = jnp.concatenate(pieces, axis=axis)
            step //= 2
        return pieces[-1]

    def fold_hops(k, first, axis_name, dim, sections):
        step, size = 1, lax.axis_size(axis_name)
        while 2 * step < size:
            came = hop(first, axis_name, step, sections)
            k.keep, k.send = halved(k.keep, came, dim)
            first = k.send
            step *= 2
        return came

    depth = width // spans
    far = spans // 2
    assert depth == across_units
    small = jnp.concatenate([norm_gains[0], norm_biases[0]], axis=0)
    packed = jnp.concatenate(
        [triple_weight[0].reshape(depth, -1), output_weight[0].reshape(-1, depth)],
        axis=1,
    )
    packed = jnp.pad(packed, ((0, 16), (0, 0)))
    packed = lax.dynamic_update_slice(packed, small, (depth, 0))
    own_expand, own_contract = expand_weight[0], contract_weight[0]
    hidden = own_expand.shape[1]
    inputs = xor_blocks(block_input, span, spans)
    cotangent = xor_blocks(out_grad, span, spans)
    early = jnp.where(first_section, inputs, cotangent)

    in_row = jnp.arange(rows, dtype=jnp.int32)
    in_span = jnp.concatenate([(lane ^ j) * rows + in_row for j in doubling(lanes)])
    positions = span * span_rows + in_span
    key_positions = jnp.stack([(span ^ k) * span_rows + in_span for k in doubling(spans)])
    tables = rope_tables(positions)
    position_column = positions[:, None]
    key_positions = key_positions[:, None, :]

    def blocks_of(own, came):
        held, step = {0: own, far: came}, far // 2
        while step:
            for k in list(held):
                held[k ^ step] = hop(held[k], "ctx", step, both)
            step //= 2
        return [held[k] for k in doubling(spans)]

    lane_offsets = doubling(lanes)

    def across(array, j, source):
        pairs = [(source * lanes + a, (1 - source) * lanes + (a ^ j)) for a in range(lanes)]
        return lax.ppermute(array, ("pipe", "tp"), pairs)

    def rows_far(s, m):
        k = kept[s][m]

        def go(passed):
            k.rows = passed
            k.pieces = [passed, hop(passed, "tp", lanes // 2, (s,))]
            return k.pieces[1]

        return k.rows, go

    def rows_near(s, m):
        k = kept[s][m]

        def go(passed):
            last_piece = spread_hops(k.pieces, 0, "tp", (s,), passed)
            k.row_pieces = [piece[None] for piece in k.pieces]
            return last_piece

        return jnp.concatenate(k.pieces, axis=0), go

    def one_way(array, direction, s):
        pairs = [
            (s * spans + a, s * spans + (a ^ far))
            for a in range(spans)
            if direction * ((a ^ far) - a) > 0
        ]
        return lax.ppermute(array, ("pipe", "ctx"), pairs)

    def pair_far(s, m):
        k = kept[s][m]

        def go(passed):
            k.pairs = [passed, one_way(passed, 1, s)]
            return k.pairs[1]

        return k.pair, go

    def pair_near(s, m):
        k = kept[s][m]

        def go(passed):
            return spread_hops(k.pairs, 0, "ctx", (s,), passed)

        return jnp.concatenate(k.pairs, axis=0), go

    def pair_grad_near(s, m):
        k = kept[s][m].pair_grad
        return k.send, lambda passed: fold_hops(k, passed, "ctx", 0, (s,))

    def pair_grad_both(s, m):
        k = kept[s][m].pair_grad

        def go(passed):
            fold_hops(k, passed, "ctx", 0, (s,))
            k.came = one_way(k.send, -1, s)
            return k.came

        return k.send, go

    def pair_grad_far(s, m):
        k = kept[s][m].pair_grad

        def go(passed):
            k.came = one_way(passed, -1, s)
            return k.came

        return k.send, go

    def sum_near(s, k):
        k.keep, going = k.blocks
        return going, lambda passed: fold_hops(k, passed, "tp", 0, (s,))

    def sum_far(s, k):
        def go(passed):
            k.blocks, k.arrived = [k.keep], [hop(passed, "tp", lanes // 2, (s,))]
            return k.arrived[0]

        return k.send, go

    def total_of(k):
        return sum(array.astype(f32) for array in [k.blocks[0], *k.arrived])

    def norm_back(upstream, combined, entering):
        normalized, inverse = normalize(entering.astype(f32))
        return (
            upstream.astype(f32)
            + inverse
            * (
                combined
                - jnp.mean(combined, axis=-1, keepdims=True)
                - normalized * jnp.mean(combined * normalized, axis=-1, keepdims=True)
            )
        ).astype(bf16)

    def middle_of(m):
        return (inputs[m].astype(f32) + total_of(kept[0][m])).astype(bf16)

    def entry_of(m):
        k = kept[1][m]
        return norm_back(cotangent[m], total_of(k), k.rows)

    def hand_one(s, m):
        k, other = kept[s][m], kept[1 - s][m]
        k.given = middle_of(m) if s == 0 else entry_of(m)

        def go(passed):
            k.given = passed
            other.rows = across(passed, 0, s)
            return other.rows

        return k.given, go

    def run_project(s, m):
        k = kept[s][m]
        pieces, place = (early_pieces, m) if s == 0 else (k.row_pieces, 0)
        k.first, k.second, k.normal, k.queries, pair = project(
            order, flags[s], pieces, place, gains, biases, tables, packed, heads, head_dim
        )
        k.pair = pair[None]

    def run_expand(m):
        k = kept[0][m]
        k.active, k.slope = expand_up(order, flags[0], k.second, weights.expand, span_rows)

    def run_attend(m):
        k = kept[0][m]
        k.attended, k.probs = attend(
            order, flags[0], k.queries, k.pairs, position_column, key_positions, scale
        )

    def run_branch(m):
        k = kept[0][m]
        k.blocks = branch_out(
            order, flags[0], [(k.active, k.attended)], contract, packed
        )

    def run_hidden_both(m):
        k = kept[1][m]
        k.upstream, k.active, k.hidden, k.part, k.side_second = hidden_both(
            order,
            flags[1],
            k.second,
            early_pieces,
            m,
            weights.expand,
            contract,
            k.normal,
            gains,
        )

    def run_attend_both(m):
        k = kept[1][m]
        k.attended, k.turned_back, keep, send = attend_both(
            order,
            flags[1],
            k.upstream,
            packed,
            k.queries,
            k.pairs,
            position_column,
            key_positions,
            tables,
            scale,
        )
        k.pair_grad = SimpleNamespace(keep=keep, send=send)

    def run_attend_back(m):
        k = kept[0][m]
        k.upstream, k.turned_back, keep, send = attend_back(
            order,
            flags[0],
            k.row_pieces,
            packed,
            k.queries,
            k.pairs,
            k.probs,
            tables,
            scale,
        )
        k.pair_grad = SimpleNamespace(keep=keep, send=send)

    def run_hidden_back(m):
        k = kept[0][m]
        k.hidden, k.part, k.side_second = hidden_back(
            order,
            flags[0],
            k.upstream,
            contract,
            weights.expand,
            k.slope,
            k.normal,
            gains,
        )

    def run_project_back(s, m):
        k = kept[s][m]
        own, arrived = k.pair_grad.keep, k.pair_grad.came
        k.stacked, k.side_first, *k.blocks = project_back(
            order,
            flags[s],
            k.turned_back,
            own.reshape(own.shape[1:]),
            arrived.reshape(arrived.shape[1:]),
            packed,
            k.part,
            k.normal,
            gains,
            tables,
        )

    def of(name, s, count=micros):
        return [getattr(kept[s][m], name) for m in range(count)]

    branch_sums, expand_sums, triple_sums = (SimpleNamespace(parts=[]) for _ in range(3))

    def run_sums(w, lefts, rights, by_rows):
        w.dim = 0 if by_rows else 1
        w.keep, w.send = weight_sums(order, always, lefts, rights, by_rows, spans)

    def wide_near(w):
        def go(passed):
            w.came = hop(passed, "ctx", 1, both)
            return w.came

        return w.send, go

    def run_fold(w):
        step = 2
        w.keep, w.send = fold(order, always, w.keep, w.came, w.dim)
        while 2 * step < spans:
            w.came = hop(w.send, "ctx", step, both)
            w.keep, w.send = fold(order, always, w.keep, w.came, w.dim)
            step *= 2

    def wide_far(w, start, stop):
        def go(passed):
            w.parts.append(hop(passed, "ctx", far, both))
            return w.parts[-1]

        return w.send[start:stop], go

    weights = SimpleNamespace(expand_came=[], contract_came=[])
    half_depth = depth // 2

    def expand_far(start, stop):
        def go(passed):
            weights.expand_came.append(hop(passed, "ctx", far, both))
            return weights.expand_came[-1]

        return own_expand[start:stop], go

    def packed_far(passed):
        weights.packed_came = hop(passed, "ctx", far, both)
        return weights.packed_came

    def packed_near(passed):
        weights.packed = blocks_of(packed, passed)
        return weights.packed[1:]

    def expand_near(passed):
        weights.expand = blocks_of(own_expand, passed)
        return weights.expand[1:]

    def contract_far(start, stop):
        def go(passed):
            weights.contract_came.append(hop(passed, "ctx", far, both))
            return weights.contract_came[-1]

        return own_contract[start:stop], go

    def contract_near(passed):
        weights.contract = blocks_of(own_contract, passed)
        return weights.contract[1:]

    def early_hops(passed):
        weights.early = [passed] + [hop(passed, "tp", j, both) for j in lane_offsets[1:]]
        return weights.early[1:]

    due[0] = [expand_far(0, half_depth)[1](own_expand[:half_depth])]
    slot([(packed, packed_far), expand_far(half_depth, depth), (early, early_hops)])
    early_pieces = weights.early
    cuts = [0, hidden // 4, 11 * hidden // 16, hidden]
    expand_came = jnp.concatenate(weights.expand_came, axis=0)
    slot(
        [
            (weights.packed_came, packed_near),
            (expand_came, expand_near),
            contract_far(cuts[0], cuts[1]),
        ]
    )
    packed = weights.packed
    small_full = jnp.concatenate(
        [piece[depth : depth + 4, :depth] for piece in packed], axis=1
    ).astype(f32)
    gains, biases = small_full[:2], small_full[2:]
    slot(
        [contract_far(cuts[1], cuts[2])],
        [lambda m=m: run_project(0, m) for m in range(micros)],
    )
    a, b = kept
    slot(
        [pair_far(0, 0), contract_far(cuts[2], cuts[3])],
        [lambda m=m: run_expand(m) for m in range(micros)],
    )
    contract_came = jnp.concatenate(weights.contract_came, axis=0)
    slot([(contract_came, contract_near), pair_near(0, 0)])
    contract = weights.contract
    slot([pair_far(0, 1)], [lambda: run_attend(0), lambda: run_branch(0)])
    slot([sum_near(0, a[0]), pair_near(0, 1)])
    slot([sum_far(0, a[0]), pair_far(0, 2)], [lambda: run_attend(1), lambda: run_branch(1)])
    slot([hand_one(0, 0), sum_near(0, a[1]), pair_near(0, 2)])
    slot(
        [rows_far(1, 0), sum_far(0, a[1])], [lambda: run_attend(2), lambda: run_branch(2)]
    )
    slot([rows_near(1, 0), hand_one(0, 1), sum_near(0, a[2])])
    slot([rows_far(1, 1), sum_far(0, a[2])], [lambda: run_project(1, 0)])
    slot(
        [pair_far(1, 0), rows_near(1, 1), hand_one(0, 2)], [lambda: run_hidden_both(0)]
    )
    slot([pair_near(1, 0), rows_far(1, 2)], [lambda: run_project(1, 1)])
    slot(
        [pair_far(1, 1), rows_near(1, 2)],
        [lambda: run_attend_both(0), lambda: run_hidden_both(1)],
    )
    slot([pair_grad_near(1, 0), pair_near(1, 1)], [lambda: run_project(1, 2)])
    slot(
        [pair_grad_far(1, 0), pair_far(1, 2)],
        [lambda: run_attend_both(1), lambda: run_hidden_both(2)],
    )
    slot([pair_grad_near(1, 1), pair_near(1, 2)], [lambda: run_project_back(1, 0)])
    slot([sum_near(1, b[0]), pair_grad_far(1, 1)], [lambda: run_attend_both(2)])
    slot([sum_far(1, b[0]), pair_grad_near(1, 2)], [lambda: run_project_back(1, 1)])
    slot([hand_one(1, 0), sum_near(1, b[1]), pair_grad_far(1, 2)])
    slot([sum_far(1, b[1]), rows_far(0, 0)], [lambda: run_project_back(1, 2)])
    slot([sum_near(1, b[2]), hand_one(1, 1), rows_near(0, 0)])
    slot([sum_far(1, b[2]), rows_far(0, 1)], [lambda: run_attend_back(0)])
    slot(
        [hand_one(1, 2), rows_near(0, 1), pair_grad_near(0, 0)],
        [lambda: run_hidden_back(0)],
    )
    slot([rows_far(0, 2), pair_grad_far(0, 0)], [lambda: run_attend_back(1)])
    slot(
        [rows_near(0, 2), pair_grad_near(0, 1)],
        [lambda: run_hidden_back(1), lambda: run_project_back(0, 0)],
    )
    last = micros - 1

    def run_branch_sums():
        run_sums(
            branch_sums,
            [[of("active", s), of("attended", s)] for s in both],
            [
                [of("upstream", 0, last) + [piece[0] for piece in a[last].row_pieces]],
                [of("upstream", 1)],
            ],
            False,
        )

    def run_expand_sums():
        run_sums(
            expand_sums,
            [[of("second", s)] for s in both],
            [[of("hidden", s)] for s in both],
            True,
        )

    def run_triple_sums():
        run_sums(
            triple_sums,
            [[of("first", s)] for s in both],
            [[of("stacked", s)] for s in both],
            True,
        )

    finals = SimpleNamespace()

    def run_final_branch():
        blocks = branch_out(
            order, flags[1], [(k.active, k.attended) for k in b], contract, packed
        )
        finals.keep = jnp.stack(blocks[0::2])
        finals.send = jnp.stack(blocks[1::2])

    def finals_near():
        return finals.send, lambda passed: fold_hops(finals, passed, "tp", 1, (1,))

    def finals_far():
        def go(passed):
            finals.came = hop(passed, "tp", lanes // 2, (1,))
            return finals.came

        return finals.send, go

    slot([pair_grad_far(0, 1), sum_near(0, a[0])], [run_branch_sums])
    slot(
        [wide_near(branch_sums)], [lambda: run_attend_back(2), lambda: run_project_back(0, 1)]
    )
    slot(
        [pair_grad_both(0, 2)], [lambda: run_fold(branch_sums), lambda: run_hidden_back(2)]
    )
    cut = [0, hidden // 2, hidden, hidden + across_units]
    slot(
        [wide_far(branch_sums, cut[0], cut[1]), sum_far(0, a[0]), sum_near(0, a[1])],
        [lambda: run_project_back(0, 2), run_triple_sums],
    )

    def side_of(mades):
        return sum(
            jnp.concatenate([k.side_first, k.side_second], axis=0) for k in mades
        )

    side = SimpleNamespace(all=jnp.where(first_section, side_of(a), side_of(b)))

    def side_ctx(passed):
        step = 1
        while step < spans:
            middle = passed.shape[1] // 2
            came = hop(passed[:, middle:], "ctx", step, both)
            passed = passed[:, :middle] + came
            step *= 2
        side.all = passed
        return came

    def side_near(passed):
        step = 1
        while 2 * step < lanes:
            came = hop(passed, "tp", step, both)
            passed = passed + came
            step *= 2
        side.all = passed
        return came

    def side_far(passed):
        came = hop(passed, "tp", lanes // 2, both)
        side.all = passed + came
        return came

    def held_back(w, j):
        def go(passed):
            w.parts[j] = passed
            return []

        return w.parts[j], go

    def wide_total(keep, parts):
        came = jnp.concatenate(parts, axis=0) if len(parts) > 1 else parts[0]
        return keep.astype(f32) + came.astype(f32)

    slot(
        [
            wide_near(triple_sums),
            wide_far(branch_sums, cut[1], cut[2]),
            (side.all, side_ctx),
            sum_far(0, a[1]),
        ],
        [run_expand_sums, run_final_branch],
    )
    slot([], [lambda: run_fold(triple_sums)])
    slot(
        [
            wide_near(expand_sums),
            wide_far(triple_sums, 0, half_depth),
            wide_far(branch_sums, cut[2], cut[3]),
            sum_near(0, a[2]),
            finals_near(),
        ]
    )
    slot([], [lambda: run_fold(expand_sums)])
    slot(
        [
            wide_far(triple_sums, half_depth, depth),
            wide_far(expand_sums, 0, depth // 4),
            sum_far(0, a[2]),
            (side.all, side_near),
            finals_far(),
        ]
    )
    slot(
        [
            wide_far(expand_sums, depth // 4, depth),
            (side.all, side_far),
            held_back(triple_sums, 1),
            held_back(branch_sums, 2),
        ]
    )
    triple_grads = wide_total(triple_sums.keep, triple_sums.parts)
    triple_grads = triple_grads.reshape(triple_weight.shape)
    branch_grads = wide_total(branch_sums.keep, branch_sums.parts)
    contract_grads, output_grads = branch_grads[:hidden], branch_grads[hidden:]
    expand_grads = wide_total(expand_sums.keep, expand_sums.parts)
    layer_outputs = jnp.stack(
        [
            jnp.where(
                first_section,
                kept[0][m].given,
                (
                    b[m].rows.astype(f32)
                    + finals.keep[m].astype(f32)
                    + finals.came[m].astype(f32)
                ).astype(bf16),
            )
            for m in range(micros)
        ]
    )
    entry_grads = jnp.stack(
        [
            jnp.where(
                first_section,
                norm_back(kept[0][m].rows, total_of(kept[0][m]), inputs[m]),
                kept[1][m].given,
            )
            for m in range(micros)
        ]
    )
    gain_grads = jnp.stack([side.all[0], side.all[2]])
    bias_grads = jnp.stack([side.all[1], side.all[3]])
    return (
        xor_blocks(layer_outputs, span, spans, inverse=True)[None],
        xor_blocks(entry_grads, span, spans, inverse=True)[None],
        triple_grads,
        output_grads.reshape(output_weight.shape),
        expand_grads[None],
        contract_grads[None],
        gain_grads[None],
        bias_grads[None],
    )


def solution(mesh):
    return jax.shard_map(
        shards,
        mesh=mesh,
        in_specs=(
            P(None, ("ctx", "tp"), None),
            P(None, ("ctx", "tp"), None),
            P("pipe", "ctx", "tp", None, None),
            P("pipe", "tp", None, "ctx"),
            P("pipe", "ctx", "tp"),
            P("pipe", "tp", "ctx"),
            P("pipe", None, "ctx"),
            P("pipe", None, "ctx"),
        ),
        out_specs=(
            P("pipe", None, ("ctx", "tp"), None),
            P("pipe", None, ("ctx", "tp"), None),
            P("pipe", "ctx", "tp", None, None),
            P("pipe", "tp", None, "ctx"),
            P("pipe", "ctx", "tp"),
            P("pipe", "tp", "ctx"),
            P("pipe", None, "ctx"),
            P("pipe", None, "ctx"),
        ),
        check_vma=False,
    )
```

```python
import functools
import math
from types import SimpleNamespace

import jax
import jax.numpy as jnp
from jax import lax
from jax.experimental import pallas as pl
from jax.experimental.pallas import tpu as pltpu
from jax.sharding import PartitionSpec as P

ROT = 64
LANES = 128
epsilon = 1e-05
masked_score = -1e30
f32 = jnp.float32
bf16 = jnp.bfloat16
mebibyte = 1024 * 1024
half_root = 0.7071067811865476
bell = 0.3989422804014327


def dot(a, b, dims):
    return lax.dot_general(a, b, (dims, ((), ())), preferred_element_type=f32)


def plain(a, b):
    return dot(a, b, ((1,), (0,)))


def turned(a, b):
    return dot(a, b, ((1,), (1,)))


def doubling(count):
    order, step = [0], count // 2
    while step:
        order += [k ^ step for k in order]
        step //= 2
    return order


def xor_blocks(values, index, count, inverse=False):
    width = values.shape[-1] // count
    order = doubling(count)

    def taken(places):
        return jnp.concatenate(
            [values[..., k * width : (k + 1) * width] for k in places], axis=-1
        )

    if inverse:
        values = taken([order.index(k) for k in range(count)])
    step = 1
    while step < count:
        swapped = taken([k ^ step for k in range(count)])
        values = jnp.where((index & step) != 0, swapped, values)
        step *= 2
    return values if inverse else taken(order)


def rope_tables(positions):
    half = ROT // 2
    frequency = 10000.0 ** (-jnp.arange(0, ROT, 2, dtype=f32) / ROT)
    angles = positions.astype(f32)[:, None] * frequency[None, :]
    cosine, sine = jnp.cos(angles), jnp.sin(angles)
    count = positions.shape[0]
    rest = jnp.zeros((count, LANES - ROT), f32)
    none = jnp.zeros((count, half), f32)
    return jnp.stack(
        [
            jnp.concatenate([cosine, cosine, rest + 1.0], axis=1),
            jnp.concatenate([-sine, none, rest], axis=1),
            jnp.concatenate([none, sine, rest], axis=1),
        ]
    )


def turn(values, tables, sign):
    half = ROT // 2
    part = values[:, :LANES]
    moved = (
        pltpu.roll(part, LANES - half, 1) * tables[1] + pltpu.roll(part, half, 1) * tables[2]
    )
    part = part * tables[0] + (moved if sign > 0 else -moved)
    return jnp.concatenate([part, values[:, LANES:]], axis=1)


def normalize(values):
    center = values - jnp.mean(values, axis=-1, keepdims=True)
    inverse = lax.rsqrt(jnp.mean(center * center, axis=-1, keepdims=True) + epsilon)
    return (center * inverse, inverse)


def whole(array):
    zeros = (0,) * array.ndim
    return pl.BlockSpec(array.shape, lambda *_: zeros)


def at(block, place):
    return pl.BlockSpec(block, lambda *_: place)


kept_out = pl.BlockSpec(memory_space=pl.ANY)


def shape(dims, dtype=bf16):
    return jax.ShapeDtypeStruct(dims, dtype)


class Order:
    def __init__(self):
        self.last = []

    def follow(self, results):
        self.last = [min(results, key=lambda array: array.size * array.dtype.itemsize)]

    def also(self, array):
        self.last = self.last + [array]


took = dict(
    project=5,
    expand=6,
    attend=3,
    branch=6,
    hidden_both=11,
    attend_both=5,
    attend_back=5,
    hidden_back=9,
    project_back=5,
    weight_sums=11,
    fold=3,
    owner_sums=13,
)
peak = 1.15e9


def run(order, flags, kernel, ins, outs, scratch, name, grid=(1,), work=0, in_place={}):
    taken = len(ins)
    ins = [(flags, pl.BlockSpec(memory_space=pltpu.SMEM))] + list(ins)
    ins += [(array, kept_out) for array in order.last]
    arrays = [array for array, _ in ins]
    once = grid == (1,)

    def sized(spec, dtype):
        if spec.block_shape is None:
            return spec, 0
        size = math.prod(spec.block_shape) * jnp.dtype(dtype).itemsize
        if not once:
            return spec, 2 * size
        single = pl.BlockSpec(
            spec.block_shape, spec.index_map, pipeline_mode=pl.Buffered(1)
        )
        return single, size

    in_specs = [sized(spec, array.dtype) for array, spec in ins]
    out_specs = [sized(spec, struct.dtype) for struct, spec in outs]
    held = sum(size for _, size in in_specs + out_specs)
    for buffer in scratch:
        if buffer.memory_space == pltpu.VMEM:
            held += math.prod(buffer.shape) * jnp.dtype(buffer.dtype).itemsize

    def body(flag_ref, *refs):
        @pl.when(flag_ref[0] == 1)
        def _():
            kernel(flag_ref, *refs[:taken], *refs[len(ins) - 1 :])

    results = pl.pallas_call(
        body,
        grid=grid,
        in_specs=[spec for spec, _ in in_specs],
        out_specs=[spec for spec, _ in out_specs],
        out_shape=[struct for struct, _ in outs],
        scratch_shapes=scratch,
        input_output_aliases=in_place,
        compiler_params=pltpu.CompilerParams(
            vmem_limit_bytes=int(held + (work + 4) * mebibyte)
        ),
        cost_estimate=pl.CostEstimate(
            flops=int(took[name] * peak), bytes_accessed=0, transcendentals=0
        ),
        name=name,
    )(*arrays)
    order.follow(results)
    return results


def fence(through, waits):
    count = len(through)

    def kernel(*refs):
        pass

    return pl.pallas_call(
        kernel,
        in_specs=[kept_out] * (count + len(waits)),
        out_specs=[kept_out] * count,
        out_shape=[shape(array.shape, array.dtype) for array in through],
        input_output_aliases={j: j for j in range(count)},
        compiler_params=pltpu.CompilerParams(vmem_limit_bytes=mebibyte),
        cost_estimate=pl.CostEstimate(flops=1, bytes_accessed=1, transcendentals=0),
        name="fence",
    )(*through, *waits)


def full_out(dims, dtype=bf16):
    zeros = (0,) * len(dims)
    return (shape(dims, dtype), pl.BlockSpec(dims, lambda *_: zeros))


def copies(sources, targets, sems):
    started = []
    for source, target, sem in zip(sources, targets, sems):
        copy = pltpu.make_async_copy(source, target, sem)
        copy.start()
        started.append(copy)
    return started


def project(order, flags, pieces, at_piece, gains, biases, tables, weights, heads, head_dim):
    count, width = 1, pieces[0].shape[2]
    span_rows = sum(piece.shape[1] for piece in pieces)
    rows = count * span_rows
    chunk = pieces[0].shape[1]
    spans = len(weights)
    depth = width // spans
    wide = 3 * head_dim
    columns = heads * wide

    def kernel(flag_ref, *refs):
        piece_refs = refs[: len(pieces)]
        gain_ref, bias_ref, table_ref = refs[len(pieces) : len(pieces) + 3]
        weight_refs = refs[len(pieces) + 3 : len(pieces) + 3 + spans]
        first, second, normal, queries, pair, held, sems = refs[len(pieces) + 3 + spans :]
        started = []
        for h in range(heads):
            started.append(
                copies(
                    [w.at[:depth, h * wide : (h + 1) * wide] for w in weight_refs],
                    [held.at[h, k * depth : (k + 1) * depth] for k in range(spans)],
                    [sems.at[h, k] for k in range(spans)],
                )
            )
        start = 0
        for piece_ref in piece_refs:
            chunks = piece_ref.shape[1] // chunk

            def one(i, _, piece_ref=piece_ref, start=start, chunks=chunks):
                m, c = i // chunks, i % chunks
                values = piece_ref[m, pl.ds(pl.multiple_of(c * chunk, chunk), chunk), :]
                normed, _ = normalize(values.astype(f32))
                to = pl.ds(
                    pl.multiple_of(m * span_rows + start + c * chunk, chunk), chunk
                )
                normal[to, :] = normed.astype(bf16)
                first[to, :] = (normed * gain_ref[0:1] + bias_ref[0:1]).astype(bf16)
                second[to, :] = (normed * gain_ref[1:2] + bias_ref[1:2]).astype(bf16)
                return 0

            lax.fori_loop(0, count * chunks, one, 0)
            start += piece_ref.shape[1]
        for h in range(heads):
            for copy in started[h]:
                copy.wait()

            def two(m, _, h=h):
                to = pl.ds(pl.multiple_of(m * span_rows, span_rows), span_rows)
                made = plain(first[to, :], held[h])
                queries[h, to, :] = turn(made[:, :head_dim], table_ref, 1).astype(bf16)
                pair[0, h, to, :] = turn(
                    made[:, head_dim : 2 * head_dim], table_ref, 1
                ).astype(bf16)
                pair[1, h, to, :] = made[:, 2 * head_dim :].astype(bf16)
                return 0

            lax.fori_loop(0, count, two, 0)

    ins = [(piece, at((1,) + piece.shape[1:], (at_piece, 0, 0))) for piece in pieces]
    ins += [(array, whole(array)) for array in (gains, biases, tables)]
    ins += [(w, kept_out) for w in weights]
    outs = [full_out((rows, width))] * 3 + [
        full_out((heads, rows, head_dim)),
        full_out((2, heads, rows, head_dim)),
    ]
    scratch = [
        pltpu.VMEM((heads, width, wide), bf16),
        pltpu.SemaphoreType.DMA((heads, spans)),
    ]
    return run(order, flags, kernel, ins, outs, scratch, "project")


def expand_up(order, flags, second, weights, span_rows, room):
    rows, width = second.shape
    depth, hidden = weights[0].shape
    spans = len(weights)
    tile = min(512, hidden)
    tiles = hidden // tile

    def kernel(flag_ref, *refs):
        second_ref, weight_refs = refs[0], refs[1 : 1 + spans]
        active, slope, held, sems = refs[1 + spans :]
        started = []
        for t in range(tiles):
            started.append(
                copies(
                    [w.at[:, t * tile : (t + 1) * tile] for w in weight_refs],
                    [held.at[t, k * depth : (k + 1) * depth] for k in range(spans)],
                    [sems.at[t, k] for k in range(spans)],
                )
            )
        for t in range(tiles):
            for copy in started[t]:
                copy.wait()

            def one(m, _, t=t):
                to = pl.ds(pl.multiple_of(m * span_rows, span_rows), span_rows)
                pre = plain(second_ref[to, :], held[t])
                risen = 0.5 * (1.0 + lax.erf(pre * half_root))
                columns = slice(t * tile, (t + 1) * tile)
                active[to, columns] = (pre * risen).astype(bf16)
                slope[to, columns] = (
                    risen + pre * jnp.exp(-0.5 * pre * pre) * bell
                ).astype(bf16)
                return 0

            lax.fori_loop(0, rows // span_rows, one, 0)

    ins = [(second, whole(second))] + [(w, kept_out) for w in weights]
    outs = [
        (shape((rows, hidden + room)), at((rows, hidden), (0, 0))),
        full_out((rows, hidden)),
    ]
    scratch = [
        pltpu.VMEM((tiles, width, tile), bf16),
        pltpu.SemaphoreType.DMA((tiles, spans)),
    ]
    return run(order, flags, kernel, ins, outs, scratch, "expand")


def spread(refs):
    return [ref.at[j] for ref in refs for j in range(ref.shape[0])]


def attention(here, pairs, head, row_ref, key_ref, scale):
    scores = []
    for k, pair in enumerate(pairs):
        raw = turned(here, pair[0, head]) * scale
        scores.append(jnp.where(key_ref[k] <= row_ref[...], raw, masked_score))
    top = functools.reduce(
        jnp.maximum, [jnp.max(part, axis=1, keepdims=True) for part in scores]
    )
    scores = [jnp.exp(part - top) for part in scores]
    inverse = 1.0 / sum(jnp.sum(part, axis=1, keepdims=True) for part in scores)
    return [part * inverse for part in scores]


def attend(order, flags, units, queries, pairs, positions, key_positions, scale):
    heads, rows, head_dim = queries.shape
    spans = sum(pair.shape[0] for pair in pairs)
    across = heads * head_dim

    def kernel(flag_ref, units_ref, query_ref, *refs):
        views, refs = spread(refs[: len(pairs)]), refs[len(pairs) :]
        row_ref, key_ref, attended, probs = refs
        for h in range(heads):
            parts = attention(query_ref[h], views, h, row_ref, key_ref, scale)
            summed = None
            for k in range(spans):
                part = parts[k].astype(bf16)
                probs[k, h] = part
                term = plain(part, views[k][1, h])
                summed = term if summed is None else summed + term
            attended[:, h * head_dim : (h + 1) * head_dim] = summed.astype(bf16)

    ins = [(units, kept_out)]
    ins += [(array, whole(array)) for array in (queries, *pairs, positions, key_positions)]
    outs = [
        (shape(units.shape), at((rows, across), (0, units.shape[1] // across - 1))),
        full_out((spans, heads, rows, rows)),
    ]
    work = spans * rows * rows * 4 * heads * 4 / mebibyte
    return run(
        order, flags, kernel, ins, outs, [], "attend", work=work, in_place={1: 0}
    )


def attention_grads(grad, here, parts, views, head, keep, send, scale):
    half = keep.shape[0]
    grad_probs = [turned(grad, view[1, head]) for view in views]
    delta = sum(
        jnp.sum(part.astype(f32) * slope, axis=1, keepdims=True)
        for part, slope in zip(parts, grad_probs)
    )
    query_grad = None
    for k, view in enumerate(views):
        slopes = (parts[k].astype(f32) * (grad_probs[k] - delta)).astype(bf16)
        term = plain(slopes, view[0, head])
        query_grad = term if query_grad is None else query_grad + term
        side = keep if k < half else send
        side[k % half, 0, head] = (dot(slopes, here, ((0,), (0,))) * scale).astype(bf16)
        side[k % half, 1, head] = dot(parts[k].astype(bf16), grad, ((0,), (0,))).astype(bf16)
    return query_grad * scale


def attend_both(
    order, flags, rows_in, packed, queries, pairs, positions, key_positions, tables, scale
):
    heads, rows, head_dim = queries.shape
    width = rows_in.shape[1]
    spans = len(packed)
    across, depth = heads * head_dim, width // spans
    half = spans // 2

    def kernel(flag_ref, rows_ref, *refs):
        packed_refs, refs = refs[:spans], refs[spans:]
        query_ref, refs = refs[0], refs[1:]
        views, refs = spread(refs[: len(pairs)]), refs[len(pairs) :]
        row_ref, key_ref, table_ref, attended, turned_back, keep, send, held, sems = refs
        started = copies(
            [w.at[:across, 3 * across : 3 * across + depth] for w in packed_refs],
            [held.at[:, k * depth : (k + 1) * depth] for k in range(spans)],
            [sems.at[k] for k in range(spans)],
        )
        all_parts = []
        for h in range(heads):
            parts = attention(query_ref[h], views, h, row_ref, key_ref, scale)
            summed = None
            for k in range(spans):
                term = plain(parts[k].astype(bf16), views[k][1, h])
                summed = term if summed is None else summed + term
            attended[:, h * head_dim : (h + 1) * head_dim] = summed.astype(bf16)
            all_parts.append(parts)
        for copy in started:
            copy.wait()
        grads = turned(rows_ref[...], held[...]).astype(bf16)
        for h in range(heads):
            made = attention_grads(
                grads[:, h * head_dim : (h + 1) * head_dim],
                query_ref[h],
                all_parts[h],
                views,
                h,
                keep,
                send,
                scale,
            )
            turned_back[h] = turn(made, table_ref, -1).astype(bf16)

    ins = [(rows_in, whole(rows_in))] + [(w, kept_out) for w in packed]
    ins += [
        (array, whole(array)) for array in (queries, *pairs, positions, key_positions, tables)
    ]
    outs = [full_out((rows, across)), full_out((heads, rows, head_dim))]
    outs += [full_out((half, 2, heads, rows, head_dim))] * 2
    scratch = [pltpu.VMEM((across, width), bf16), pltpu.SemaphoreType.DMA((spans,))]
    work = spans * rows * rows * 4 * (heads + 4) / mebibyte
    return run(order, flags, kernel, ins, outs, scratch, "attend_both", work=work)


def hidden_both(order, flags, second, pieces, at_piece, expand, contract, normal, gains):
    rows, width = second.shape
    hidden, depth = contract[0].shape
    spans = len(contract)
    tile = min(512, hidden)
    tiles = hidden // tile

    def kernel(flag_ref, second_ref, *refs):
        piece_refs, refs = refs[: len(pieces)], refs[len(pieces) :]
        expand_refs, refs = refs[:spans], refs[spans:]
        contract_refs, refs = refs[:spans], refs[spans:]
        normal_ref, gain_ref, rows_out, active, grads, part, side, *refs = refs
        held_up, held_down, sems_up, sems_down = refs
        started = []
        for t in range(tiles):
            block = slice(t * tile, (t + 1) * tile)
            places = [slice(k * depth, (k + 1) * depth) for k in range(spans)]
            up = copies(
                [w.at[:, block] for w in expand_refs],
                [held_up.at[place, block] for place in places],
                [sems_up.at[t, k] for k in range(spans)],
            )
            down = copies(
                [w.at[block, :] for w in contract_refs],
                [held_down.at[block, place] for place in places],
                [sems_down.at[t, k] for k in range(spans)],
            )
            started.append((up, down))
        start = 0
        for piece_ref in piece_refs:
            size = piece_ref.shape[1]
            rows_out[start : start + size, :] = piece_ref[0]
            start += size
        for t in range(tiles):
            block = slice(t * tile, (t + 1) * tile)
            for copy in started[t][0] + started[t][1]:
                copy.wait()
            pre = plain(second_ref[...], held_up[:, block])
            risen = 0.5 * (1.0 + lax.erf(pre * half_root))
            active[:, block] = (pre * risen).astype(bf16)
            slope = risen + pre * jnp.exp(-0.5 * pre * pre) * bell
            grads[:, block] = (turned(rows_out[...], held_down[block, :]) * slope).astype(bf16)
        for k in range(spans):
            place = slice(k * depth, (k + 1) * depth)
            made = turned(grads[...], held_up[place, :])
            side[0:1, place] = jnp.sum(
                made * normal_ref[:, place].astype(f32), axis=0, keepdims=True
            )
            side[1:2, place] = jnp.sum(made, axis=0, keepdims=True)
            part[:, place] = made * gain_ref[1:2, place]

    ins = [(second, whole(second))]
    ins += [(piece, at((1,) + piece.shape[1:], (at_piece, 0, 0))) for piece in pieces]
    ins += [(w, kept_out) for w in expand] + [(w, kept_out) for w in contract]
    ins += [(normal, whole(normal)), (gains, whole(gains))]
    outs = [
        full_out((rows, width)),
        full_out((rows, hidden)),
        full_out((rows, hidden)),
        full_out((rows, width), f32),
        full_out((2, width), f32),
    ]
    scratch = [
        pltpu.VMEM((width, hidden), bf16),
        pltpu.VMEM((hidden, width), bf16),
        pltpu.SemaphoreType.DMA((tiles, spans)),
        pltpu.SemaphoreType.DMA((tiles, spans)),
    ]
    return run(order, flags, kernel, ins, outs, scratch, "hidden_both")


def branch_out(order, flags, groups, contract, packed):
    hidden, depth = contract[0].shape
    spans = len(contract)
    across = depth
    width = depth * spans
    span_rows = groups[0][0].shape[0]
    block = span_rows // 2
    count = len(groups)

    def kernel(flag_ref, *refs):
        group_refs, refs = refs[: 2 * count], refs[2 * count :]
        contract_refs, packed_refs = refs[:spans], refs[spans : 2 * spans]
        blocks, refs = refs[2 * spans : 2 * (spans + count)], refs[2 * (spans + count) :]
        held, held_out, sems = refs
        outputs = [w.at[:across, 3 * across : 3 * across + depth] for w in packed_refs]
        started = copies(
            [ref for k in range(spans) for ref in (outputs[k], contract_refs[k])],
            [ref for k in range(spans) for ref in (held_out.at[k], held.at[k])],
            [sems.at[j] for j in range(2 * spans)],
        )
        for k in range(spans):
            started[2 * k].wait()
            started[2 * k + 1].wait()
            columns = slice(k * depth, (k + 1) * depth)
            for c in range(count):
                made = plain(group_refs[2 * c + 1][...], held_out[k])
                made = made + plain(group_refs[2 * c][...], held[k])
                blocks[2 * c][:, columns] = made[:block].astype(bf16)
                blocks[2 * c + 1][:, columns] = made[block:].astype(bf16)

    ins = []
    for active, attended in groups:
        place = attended.shape[1] // across - 1
        ins += [
            (active, at((span_rows, hidden), (0, 0))),
            (attended, at((span_rows, across), (0, place))),
        ]
    ins += [(w, kept_out) for w in contract] + [(w, kept_out) for w in packed]
    outs = [full_out((block, width))] * (2 * count)
    scratch = [
        pltpu.VMEM((spans, hidden, depth), bf16),
        pltpu.VMEM((spans, across, depth), bf16),
        pltpu.SemaphoreType.DMA((2 * spans,)),
    ]
    return run(order, flags, kernel, ins, outs, scratch, "branch")


def attend_back(order, flags, pieces, packed, queries, pairs, probs, tables, scale):
    rows = sum(piece.shape[1] for piece in pieces)
    width = pieces[0].shape[2]
    heads, _, head_dim = queries.shape
    spans = len(packed)
    across, depth = heads * head_dim, width // spans
    half = spans // 2

    def kernel(flag_ref, *refs):
        piece_refs, refs = refs[: len(pieces)], refs[len(pieces) :]
        packed_refs, refs = refs[:spans], refs[spans:]
        query_ref, refs = refs[0], refs[1:]
        views, refs = spread(refs[: len(pairs)]), refs[len(pairs) :]
        prob_ref, table_ref, rows_out, turned_back, keep, send, *refs = refs
        columns_out, (held, sems) = refs[:spans], refs[spans:]
        started = copies(
            [w.at[:across, 3 * across : 3 * across + depth] for w in packed_refs],
            [held.at[:, k * depth : (k + 1) * depth] for k in range(spans)],
            [sems.at[k] for k in range(spans)],
        )
        start = 0
        for piece_ref in piece_refs:
            size = piece_ref.shape[1]
            rows_out[start : start + size, :] = piece_ref[0]
            start += size
        for k in range(spans):
            columns_out[k][...] = rows_out[:, k * depth : (k + 1) * depth]
        for copy in started:
            copy.wait()
        grads = turned(rows_out[...], held[...]).astype(bf16)
        for h in range(heads):
            made = attention_grads(
                grads[:, h * head_dim : (h + 1) * head_dim],
                query_ref[h],
                [prob_ref[k, h] for k in range(spans)],
                views,
                h,
                keep,
                send,
                scale,
            )
            turned_back[h] = turn(made, table_ref, -1).astype(bf16)

    ins = [(piece, whole(piece)) for piece in pieces] + [(w, kept_out) for w in packed]
    ins += [(array, whole(array)) for array in (queries, *pairs, probs, tables)]
    outs = [full_out((rows, width)), full_out((heads, rows, head_dim))]
    outs += [full_out((half, 2, heads, rows, head_dim))] * 2
    outs += [full_out((rows, depth))] * spans
    scratch = [pltpu.VMEM((across, width), bf16), pltpu.SemaphoreType.DMA((spans,))]
    work = spans * rows * rows * 4 * 4 / mebibyte
    return run(order, flags, kernel, ins, outs, scratch, "attend_back", work=work)


def hidden_back(order, flags, upstream, contract, expand, slope, normal, gains):
    span_rows, width = upstream.shape
    hidden, depth = contract[0].shape
    spans = len(contract)
    tile = min(512, hidden)
    tiles = hidden // tile

    def kernel(flag_ref, *refs):
        upstream_ref, refs = refs[0], refs[1:]
        contract_refs, refs = refs[:spans], refs[spans:]
        expand_refs, refs = refs[:spans], refs[spans:]
        slope_ref, normal_ref, gain_ref, grads, part, side, held, held_up, sems, sems_up = refs
        started = [
            copies(
                [w.at[t * tile : (t + 1) * tile, :] for w in contract_refs],
                [held.at[t, :, k * depth : (k + 1) * depth] for k in range(spans)],
                [sems.at[t, k] for k in range(spans)],
            )
            for t in range(tiles)
        ]
        started_up = copies(
            expand_refs, [held_up.at[k] for k in range(spans)], [sems_up.at[k] for k in range(spans)]
        )
        for t in range(tiles):
            for copy in started[t]:
                copy.wait()
            columns = slice(t * tile, (t + 1) * tile)
            grads[:, columns] = (
                turned(upstream_ref[...], held[t]) * slope_ref[:, columns].astype(f32)
            ).astype(bf16)
        for k in range(spans):
            started_up[k].wait()
            made = turned(grads[...], held_up[k])
            columns = slice(k * depth, (k + 1) * depth)
            side[0:1, columns] = jnp.sum(
                made * normal_ref[:, columns].astype(f32), axis=0, keepdims=True
            )
            side[1:2, columns] = jnp.sum(made, axis=0, keepdims=True)
            part[:, columns] = made * gain_ref[1:2, columns]

    ins = [(upstream, whole(upstream))]
    ins += [(w, kept_out) for w in contract] + [(w, kept_out) for w in expand]
    ins += [
        (slope, whole(slope)),
        (normal, whole(normal)),
        (gains, whole(gains)),
    ]
    outs = [
        full_out((span_rows, hidden)),
        full_out((span_rows, width), f32),
        full_out((2, width), f32),
    ]
    scratch = [
        pltpu.VMEM((tiles, tile, width), bf16),
        pltpu.VMEM((spans, depth, hidden), bf16),
        pltpu.SemaphoreType.DMA((tiles, spans)),
        pltpu.SemaphoreType.DMA((spans,)),
    ]
    return run(order, flags, kernel, ins, outs, scratch, "hidden_back")


def project_back(
    order, flags, turned_back, own, came, weights, part, normal, gains, tables
):
    heads, span_rows, head_dim = turned_back.shape
    spans = len(weights)
    width = part.shape[1]
    depth, columns = width // spans, 3 * heads * head_dim
    block = span_rows // 2

    def kernel(flag_ref, *refs):
        query_ref, own_ref, came_ref, refs = refs[0], refs[1], refs[2], refs[3:]
        weight_refs, refs = refs[:spans], refs[spans:]
        part_ref, normal_ref, gain_ref, table_ref, grads, side, *refs = refs
        low, high, held, sems = refs
        started = copies(
            [w.at[:depth, :columns] for w in weight_refs],
            [held.at[k] for k in range(spans)],
            [sems.at[k] for k in range(spans)],
        )
        for h in range(heads):
            at_column = h * 3 * head_dim
            keys = own_ref[0, h].astype(f32) + came_ref[0, h].astype(f32)
            values = own_ref[1, h].astype(f32) + came_ref[1, h].astype(f32)
            grads[:, at_column : at_column + head_dim] = query_ref[h]
            grads[:, at_column + head_dim : at_column + 2 * head_dim] = turn(
                keys, table_ref, -1
            ).astype(bf16)
            grads[:, at_column + 2 * head_dim : at_column + 3 * head_dim] = values.astype(bf16)
        for k in range(spans):
            started[k].wait()
            made = turned(grads[...], held[k])
            span_columns = slice(k * depth, (k + 1) * depth)
            side[0:1, span_columns] = jnp.sum(
                made * normal_ref[:, span_columns].astype(f32), axis=0, keepdims=True
            )
            side[1:2, span_columns] = jnp.sum(made, axis=0, keepdims=True)
            both = (made * gain_ref[0:1, span_columns] + part_ref[:, span_columns]).astype(bf16)
            low[:, span_columns] = both[:block]
            high[:, span_columns] = both[block:]

    ins = [(array, whole(array)) for array in (turned_back, own, came)]
    ins += [(w, kept_out) for w in weights]
    ins += [(part, whole(part)), (normal, whole(normal))]
    ins += [(gains, whole(gains)), (tables, whole(tables))]
    outs = [full_out((span_rows, columns)), full_out((2, width), f32)]
    outs += [full_out((block, width))] * 2
    scratch = [pltpu.VMEM((spans, depth, columns), bf16), pltpu.SemaphoreType.DMA((spans,))]
    return run(order, flags, kernel, ins, outs, scratch, "project_back")


def weight_sums(order, flags, lefts, rights, by_rows, spans):
    rows = sum(piece.shape[0] for piece in lefts[1][0])
    left_width = sum(group[0].shape[1] for group in lefts[1])
    right_width = sum(group[0].shape[1] for group in rights[1])
    if by_rows:
        tile = left_width // spans
        steps, block = spans // 2, (tile, right_width)
    else:
        tile = min(512, left_width)
        while left_width % tile:
            tile //= 2
        steps, block = left_width // tile, (tile, right_width // 2)
    chunk = min(1024, block[1])
    while right_width % chunk:
        chunk //= 2
    pieces = [
        [piece for groups in (lefts[s], rights[s]) for group in groups for piece in group]
        for s in (0, 1)
    ]
    most = max(len(p) for p in pieces)

    def kernel(flag_ref, *refs):
        piece_refs = (refs[: len(pieces[0])], refs[len(pieces[0]) : len(pieces[0]) + len(pieces[1])])
        keep, send, left, right, flipped, sems = refs[len(pieces[0]) + len(pieces[1]) :]
        g = pl.program_id(0)
        for s in (0, 1):

            @pl.when((g == 0) & (flag_ref[2] == s))
            def _(s=s):
                targets = []
                for held, groups in ((left, lefts[s]), (right, rights[s])):
                    column = 0
                    for group in groups:
                        row, wide = 0, group[0].shape[1]
                        for piece in group:
                            targets.append(
                                held.at[row : row + piece.shape[0], column : column + wide]
                            )
                            row += piece.shape[0]
                        column += wide
                started = copies(
                    piece_refs[s], targets, [sems.at[j] for j in range(len(targets))]
                )
                for copy in started:
                    copy.wait()

        def product(column, store):
            flipped[...] = left[:, pl.ds(pl.multiple_of(column, LANES), tile)].T

            def one(c, _):
                columns = pl.ds(pl.multiple_of(c * chunk, chunk), chunk)
                store(c, plain(flipped[...], right[:, columns]).astype(bf16))
                return 0

            lax.fori_loop(0, right_width // chunk, one, 0)

        if by_rows:

            def to(target):
                def store(c, made):
                    target[:, pl.ds(pl.multiple_of(c * chunk, chunk), chunk)] = made

                return store

            product(g * tile, to(keep))
            product((g + steps) * tile, to(send))
        else:
            half = right_width // 2 // chunk

            def store(c, made):
                @pl.when(c < half)
                def _():
                    keep[:, pl.ds(pl.multiple_of(c * chunk, chunk), chunk)] = made

                @pl.when(c >= half)
                def _():
                    send[:, pl.ds(pl.multiple_of((c - half) * chunk, chunk), chunk)] = made

            product(g * tile, store)

    ins = [(piece, kept_out) for s in (0, 1) for piece in pieces[s]]
    dims = (steps * tile, block[1])
    outs = [(shape(dims), pl.BlockSpec(block, lambda g: (g, 0)))] * 2
    scratch = [
        pltpu.VMEM((rows, left_width), bf16),
        pltpu.VMEM((rows, right_width), bf16),
        pltpu.VMEM((tile, rows), bf16),
        pltpu.SemaphoreType.DMA((most,)),
    ]
    return run(
        order, flags, kernel, ins, outs, scratch, "weight_sums", grid=(steps,)
    )


def owner_sums(order, flags, lefts, rights):
    left_width, right_width = lefts[0][0].shape[1], rights[0][0].shape[1]
    rows = sum(piece.shape[0] for piece in lefts[0])
    count = len(lefts)
    tile = min(512, left_width)
    while left_width % tile:
        tile //= 2
    pieces = [lefts[m] + rights[m] for m in range(count)]
    most = max(len(p) for p in pieces)

    def kernel(flag_ref, *refs):
        piece_refs, refs = refs[: sum(map(len, pieces))], refs[sum(map(len, pieces)) :]
        out, left, right, flipped, sems = refs
        started, used = [], 0
        for m in range(count):
            targets = []
            for held, group in ((left, lefts[m]), (right, rights[m])):
                row = 0
                for piece in group:
                    targets.append(held.at[m, row : row + piece.shape[0]])
                    row += piece.shape[0]
            started.append(
                copies(
                    piece_refs[used : used + len(targets)],
                    targets,
                    [sems.at[m, j] for j in range(len(targets))],
                )
            )
            used += len(targets)
        for m in range(count):
            for copy in started[m]:
                copy.wait()

            def one(t, _, m=m):
                block = pl.ds(pl.multiple_of(t * tile, tile), tile)
                flipped[...] = left[m, :, block].T
                made = plain(flipped[...], right[m])
                out[block, :] = made if m == 0 else out[block, :] + made
                return 0

            lax.fori_loop(0, left_width // tile, one, 0)

    ins = [(piece, kept_out) for group in pieces for piece in group]
    outs = [full_out((left_width, right_width), f32)]
    scratch = [
        pltpu.VMEM((count, rows, left_width), bf16),
        pltpu.VMEM((count, rows, right_width), bf16),
        pltpu.VMEM((tile, rows), bf16),
        pltpu.SemaphoreType.DMA((count, most)),
    ]
    return run(order, flags, kernel, ins, outs, scratch, "owner_sums")[0]


def fold(order, flags, keep, came, dim):
    rows, columns = keep.shape
    if dim == 0:
        tile = rows // 4
        steps, block = rows // 2 // tile, (tile, columns)
        places = [lambda g: (g, 0), lambda g: (g + steps, 0)]
        half = (rows // 2, columns)
    else:
        tile = rows // 4
        steps, block = rows // tile, (tile, columns // 2)
        places = [lambda g: (g, 0), lambda g: (g, 1)]
        half = (rows, columns // 2)

    def kernel(flag_ref, keep_low, keep_high, came_low, came_high, low, high):
        low[...] = (keep_low[...].astype(f32) + came_low[...].astype(f32)).astype(bf16)
        high[...] = (keep_high[...].astype(f32) + came_high[...].astype(f32)).astype(bf16)

    ins = [(array, pl.BlockSpec(block, place)) for array in (keep, came) for place in places]
    outs = [(shape(half), pl.BlockSpec(block, lambda g: (g, 0)))] * 2
    return run(order, flags, kernel, ins, outs, [], "fold", grid=(steps,))


def shards(
    block_input,
    out_grad,
    triple_weight,
    output_weight,
    expand_weight,
    contract_weight,
    norm_gains,
    norm_biases,
):
    section = lax.axis_index("pipe")
    span = lax.axis_index("ctx")
    lane = lax.axis_index("tp")
    spans = lax.axis_size("ctx")
    lanes = lax.axis_size("tp")
    micros, rows, width = block_input.shape
    span_rows = rows * lanes
    heads = triple_weight.shape[2]
    head_dim = triple_weight.shape[4]
    across_units = heads * head_dim
    scale = head_dim ** (-0.5)
    first_section = section == 0
    both = (0, 1)

    def hop(array, axis, step, sections):
        size = lax.axis_size(axis)
        pairs = [(s * size + a, s * size + (a ^ step)) for s in sections for a in range(size)]
        return lax.ppermute(array, ("pipe", axis), pairs)

    order = Order()

    def flags_for(wanted):
        return jnp.stack([jnp.asarray(wanted), span, section]).astype(jnp.int32)

    flags = [flags_for(section == s) for s in both]
    always = flags_for(1)

    kept = [[SimpleNamespace() for _ in range(micros)] for _ in both]
    due = {}
    slot_index = [0]

    def slot(hops, kernels=()):
        now = slot_index[0]
        slot_index[0] += 1
        ready = due.pop(now, [])
        hops = [h if len(h) == 3 else h + (1,) for h in hops]
        if hops:
            gated = fence([operand for operand, _, _ in hops], order.last + ready)
            order.last = [min(gated, key=lambda array: array.size)]
            for passed, (_, go, slots) in zip(gated, hops):
                results = go(passed)
                results = results if isinstance(results, list) else [results]
                due.setdefault(now + slots, []).extend(results)
        else:
            order.last = order.last + ready
        for kernel in kernels:
            kernel()

    def halved(keep, came, dim):
        middle = keep.shape[dim] // 2
        total = keep.astype(f32) + came.astype(f32)
        return (
            lax.slice_in_dim(total, 0, middle, axis=dim).astype(bf16),
            lax.slice_in_dim(total, middle, 2 * middle, axis=dim).astype(bf16),
        )

    def spread_hops(pieces, axis, axis_name, sections, first):
        step = lax.axis_size(axis_name) // 4
        going = first
        while step:
            pieces.append(hop(going, axis_name, step, sections))
            going = jnp.concatenate(pieces, axis=axis)
            step //= 2
        return pieces[-1]

    def fold_hops(k, first, axis_name, dim, sections):
        step, size = 1, lax.axis_size(axis_name)
        while 2 * step < size:
            came = hop(first, axis_name, step, sections)
            k.keep, k.send = halved(k.keep, came, dim)
            first = k.send
            step *= 2
        return came

    depth = width // spans
    far = spans // 2
    assert depth == across_units
    small = jnp.concatenate([norm_gains[0], norm_biases[0]], axis=0)
    packed = jnp.concatenate(
        [triple_weight[0].reshape(depth, -1), output_weight[0].reshape(-1, depth)],
        axis=1,
    )
    packed = jnp.pad(packed, ((0, 16), (0, 0)))
    packed = lax.dynamic_update_slice(packed, small, (depth, 0))
    own_expand, own_contract = expand_weight[0], contract_weight[0]
    hidden = own_expand.shape[1]
    inputs = xor_blocks(block_input, span, spans)
    cotangent = xor_blocks(out_grad, span, spans)
    early = jnp.where(first_section, inputs, cotangent)

    in_row = jnp.arange(rows, dtype=jnp.int32)
    in_span = jnp.concatenate([(lane ^ j) * rows + in_row for j in doubling(lanes)])
    positions = span * span_rows + in_span
    key_positions = jnp.stack([(span ^ k) * span_rows + in_span for k in doubling(spans)])
    tables = rope_tables(positions)
    position_column = positions[:, None]
    key_positions = key_positions[:, None, :]

    def blocks_of(own, came):
        held, step = {0: own, far: came}, far // 2
        while step:
            for k in list(held):
                held[k ^ step] = hop(held[k], "ctx", step, both)
            step //= 2
        return [held[k] for k in doubling(spans)]

    lane_offsets = doubling(lanes)

    def across(array, j, source):
        pairs = [(source * lanes + a, (1 - source) * lanes + (a ^ j)) for a in range(lanes)]
        return lax.ppermute(array, ("pipe", "tp"), pairs)

    def rows_far(s, m):
        k = kept[s][m]

        def go(passed):
            k.rows = passed
            k.pieces = [passed, hop(passed, "tp", lanes // 2, (s,))]
            return k.pieces[1]

        return k.rows, go

    def rows_near(s, m):
        k = kept[s][m]

        def go(passed):
            last_piece = spread_hops(k.pieces, 0, "tp", (s,), passed)
            k.row_pieces = [piece[None] for piece in k.pieces]
            return last_piece

        return jnp.concatenate(k.pieces, axis=0), go

    def one_way(array, direction, s):
        pairs = [
            (s * spans + a, s * spans + (a ^ far))
            for a in range(spans)
            if direction * ((a ^ far) - a) > 0
        ]
        return lax.ppermute(array, ("pipe", "ctx"), pairs)

    def pair_far(s, m):
        k = kept[s][m]

        def go(passed):
            k.pairs = [passed, one_way(passed, 1, s)]
            return k.pairs[1]

        return k.pair, go

    def pair_near(s, m):
        k = kept[s][m]

        def go(passed):
            return spread_hops(k.pairs, 0, "ctx", (s,), passed)

        return jnp.concatenate(k.pairs, axis=0), go

    def pair_grad_near(s, m):
        k = kept[s][m].pair_grad
        return k.send, lambda passed: fold_hops(k, passed, "ctx", 0, (s,))

    def pair_grad_both(s, m):
        k = kept[s][m].pair_grad

        def go(passed):
            fold_hops(k, passed, "ctx", 0, (s,))
            k.came = one_way(k.send, -1, s)
            return k.came

        return k.send, go

    def pair_grad_far(s, m):
        k = kept[s][m].pair_grad

        def go(passed):
            k.came = one_way(passed, -1, s)
            return k.came

        return k.send, go

    def sum_near(s, k):
        k.keep, going = k.blocks
        return going, lambda passed: fold_hops(k, passed, "tp", 0, (s,))

    def sum_far(s, k):
        def go(passed):
            k.blocks, k.arrived = [k.keep], [hop(passed, "tp", lanes // 2, (s,))]
            return k.arrived[0]

        return k.send, go

    def units_far(m):
        k = kept[0][m]

        def go(passed):
            k.units, k.units_came = passed, hop(passed, "ctx", far, (0,))
            return k.units_came

        return k.units, go

    def units_near(m):
        k = kept[0][m]

        def go(passed):
            held, step = {0: k.units, far: passed}, far // 2
            while step:
                for j in list(held):
                    held[j ^ step] = hop(held[j], "ctx", step, (0,))
                step //= 2
            k.all_units = [held[j] for j in doubling(spans)]
            return [array for j, array in held.items() if j not in (0, far)]

        return k.units_came, go

    def column_hops(m):
        k = kept[0][m]
        k.own_columns = [k.columns[0]]

        def one(j):
            def go(passed):
                k.own_columns.append(hop(passed, "ctx", doubling(spans)[j], (0,)))
                return k.own_columns[-1]

            return k.columns[j], go

        return [one(j) for j in range(1, spans)]

    def total_of(k):
        return sum(array.astype(f32) for array in [k.blocks[0], *k.arrived])

    def norm_back(upstream, combined, entering):
        normalized, inverse = normalize(entering.astype(f32))
        return (
            upstream.astype(f32)
            + inverse
            * (
                combined
                - jnp.mean(combined, axis=-1, keepdims=True)
                - normalized * jnp.mean(combined * normalized, axis=-1, keepdims=True)
            )
        ).astype(bf16)

    def middle_of(m):
        return (inputs[m].astype(f32) + total_of(kept[0][m])).astype(bf16)

    def entry_of(m):
        k = kept[1][m]
        return norm_back(cotangent[m], total_of(k), k.rows)

    def hand_one(s, m):
        k, other = kept[s][m], kept[1 - s][m]
        k.given = middle_of(m) if s == 0 else entry_of(m)

        def go(passed):
            k.given = passed
            other.rows = across(passed, 0, s)
            return other.rows

        return k.given, go

    def run_project(s, m):
        k = kept[s][m]
        pieces, place = (early_pieces, m) if s == 0 else (k.row_pieces, 0)
        k.first, k.second, k.normal, k.queries, pair = project(
            order, flags[s], pieces, place, gains, biases, tables, packed, heads, head_dim
        )
        k.pair = pair[None]

    def run_expand(m):
        k = kept[0][m]
        k.units, k.slope = expand_up(
            order, flags[0], k.second, weights.expand, span_rows, across_units
        )

    def run_attend(m):
        k = kept[0][m]
        k.units, k.probs = attend(
            order,
            flags[0],
            k.units,
            k.queries,
            k.pairs,
            position_column,
            key_positions,
            scale,
        )

    def run_branch(m):
        k = kept[0][m]
        k.blocks = branch_out(
            order, flags[0], [(k.units, k.units)], contract, packed
        )

    def run_hidden_both(m):
        k = kept[1][m]
        k.upstream, k.active, k.hidden, k.part, k.side_second = hidden_both(
            order,
            flags[1],
            k.second,
            early_pieces,
            m,
            weights.expand,
            contract,
            k.normal,
            gains,
        )

    def run_attend_both(m):
        k = kept[1][m]
        k.attended, k.turned_back, keep, send = attend_both(
            order,
            flags[1],
            k.upstream,
            packed,
            k.queries,
            k.pairs,
            position_column,
            key_positions,
            tables,
            scale,
        )
        k.pair_grad = SimpleNamespace(keep=keep, send=send)

    def run_attend_back(m):
        k = kept[0][m]
        k.upstream, k.turned_back, keep, send, *k.columns = attend_back(
            order,
            flags[0],
            k.row_pieces,
            packed,
            k.queries,
            k.pairs,
            k.probs,
            tables,
            scale,
        )
        k.pair_grad = SimpleNamespace(keep=keep, send=send)

    def run_hidden_back(m):
        k = kept[0][m]
        k.hidden, k.part, k.side_second = hidden_back(
            order,
            flags[0],
            k.upstream,
            contract,
            weights.expand,
            k.slope,
            k.normal,
            gains,
        )

    def run_project_back(s, m):
        k = kept[s][m]
        own, arrived = k.pair_grad.keep, k.pair_grad.came
        k.stacked, k.side_first, *k.blocks = project_back(
            order,
            flags[s],
            k.turned_back,
            own.reshape(own.shape[1:]),
            arrived.reshape(arrived.shape[1:]),
            packed,
            k.part,
            k.normal,
            gains,
            tables,
        )

    def of(name, s, count=micros):
        return [getattr(kept[s][m], name) for m in range(count)]

    branch_sums, expand_sums, triple_sums = (
        SimpleNamespace(parts=[], flags=f, sections=secs)
        for f, secs in ((flags[1], (1,)), (always, both), (always, both))
    )

    def run_sums(w, lefts, rights, by_rows):
        w.dim = 0 if by_rows else 1
        w.keep, w.send = weight_sums(order, w.flags, lefts, rights, by_rows, spans)

    def wide_near(w):
        def go(passed):
            w.came = hop(passed, "ctx", 1, w.sections)
            return w.came

        return w.send, go

    def run_fold(w):
        step = 2
        w.keep, w.send = fold(order, w.flags, w.keep, w.came, w.dim)
        while 2 * step < spans:
            w.came = hop(w.send, "ctx", step, w.sections)
            w.keep, w.send = fold(order, w.flags, w.keep, w.came, w.dim)
            step *= 2

    def wide_far(w, start, stop):
        def go(passed):
            w.parts.append(hop(passed, "ctx", far, w.sections))
            return w.parts[-1]

        return w.send[start:stop], go

    weights = SimpleNamespace(expand_came=[], contract_came=[])
    half_depth = depth // 2

    def expand_far(start, stop):
        def go(passed):
            weights.expand_came.append(hop(passed, "ctx", far, both))
            return weights.expand_came[-1]

        return own_expand[start:stop], go

    def packed_far(passed):
        weights.packed_came = hop(passed, "ctx", far, both)
        return weights.packed_came

    def packed_near(passed):
        weights.packed = blocks_of(packed, passed)
        return weights.packed[1:]

    def expand_near(passed):
        weights.expand = blocks_of(own_expand, passed)
        return weights.expand[1:]

    def contract_far(start, stop):
        def go(passed):
            weights.contract_came.append(hop(passed, "ctx", far, both))
            return weights.contract_came[-1]

        return own_contract[start:stop], go

    def contract_near(passed):
        weights.contract = blocks_of(own_contract, passed)
        return weights.contract[1:]

    def early_hops(passed):
        weights.early = [passed] + [hop(passed, "tp", j, both) for j in lane_offsets[1:]]
        return weights.early[1:]

    due[0] = [expand_far(0, half_depth)[1](own_expand[:half_depth])]
    slot([(packed, packed_far), expand_far(half_depth, depth), (early, early_hops)])
    early_pieces = weights.early
    cuts = [0, hidden // 4, 11 * hidden // 16, hidden]
    expand_came = jnp.concatenate(weights.expand_came, axis=0)
    slot(
        [
            (weights.packed_came, packed_near),
            (expand_came, expand_near),
            contract_far(cuts[0], cuts[1]),
        ]
    )
    packed = weights.packed
    small_full = jnp.concatenate(
        [piece[depth : depth + 4, :depth] for piece in packed], axis=1
    ).astype(f32)
    gains, biases = small_full[:2], small_full[2:]
    slot(
        [contract_far(cuts[1], cuts[2])],
        [lambda m=m: run_project(0, m) for m in range(micros)],
    )
    a, b = kept
    slot(
        [pair_far(0, 0), contract_far(cuts[2], cuts[3])],
        [lambda m=m: run_expand(m) for m in range(micros)],
    )
    contract_came = jnp.concatenate(weights.contract_came, axis=0)
    slot([(contract_came, contract_near), pair_near(0, 0)])
    contract = weights.contract
    slot([pair_far(0, 1)], [lambda: run_attend(0), lambda: run_branch(0)])
    slot([sum_near(0, a[0]), pair_near(0, 1)])
    slot([sum_far(0, a[0]), pair_far(0, 2)], [lambda: run_attend(1), lambda: run_branch(1)])
    slot([hand_one(0, 0), sum_near(0, a[1]), pair_near(0, 2)])
    slot(
        [rows_far(1, 0), sum_far(0, a[1])], [lambda: run_attend(2), lambda: run_branch(2)]
    )
    slot([rows_near(1, 0), hand_one(0, 1), sum_near(0, a[2])])
    slot([rows_far(1, 1), sum_far(0, a[2])], [lambda: run_project(1, 0)])
    slot(
        [pair_far(1, 0), rows_near(1, 1), hand_one(0, 2)], [lambda: run_hidden_both(0)]
    )
    slot([pair_near(1, 0), rows_far(1, 2), units_far(0)], [lambda: run_project(1, 1)])
    slot(
        [pair_far(1, 1), rows_near(1, 2), units_near(0), units_far(1)],
        [lambda: run_attend_both(0), lambda: run_hidden_both(1)],
    )
    slot(
        [pair_grad_near(1, 0), pair_near(1, 1), units_near(1), units_far(2)],
        [lambda: run_project(1, 2)],
    )
    slot(
        [pair_grad_far(1, 0), pair_far(1, 2), units_near(2)],
        [lambda: run_attend_both(1), lambda: run_hidden_both(2)],
    )
    slot([pair_grad_near(1, 1), pair_near(1, 2)], [lambda: run_project_back(1, 0)])
    slot([sum_near(1, b[0]), pair_grad_far(1, 1)], [lambda: run_attend_both(2)])
    slot([sum_far(1, b[0]), pair_grad_near(1, 2)], [lambda: run_project_back(1, 1)])
    slot([hand_one(1, 0), sum_near(1, b[1]), pair_grad_far(1, 2)])
    slot([sum_far(1, b[1]), rows_far(0, 0)], [lambda: run_project_back(1, 2)])
    slot([sum_near(1, b[2]), hand_one(1, 1), rows_near(0, 0)])
    slot([sum_far(1, b[2]), rows_far(0, 1)], [lambda: run_attend_back(0)])

    def run_branch_sums():
        run_sums(
            branch_sums,
            [[], [of("active", 1), of("attended", 1)]],
            [[], [of("upstream", 1)]],
            False,
        )

    cut = [0, hidden // 2, hidden, hidden + across_units]
    slot(
        [hand_one(1, 2), rows_near(0, 1), pair_grad_near(0, 0)],
        [lambda: run_hidden_back(0), run_branch_sums],
    )
    slot(
        [rows_far(0, 2), pair_grad_far(0, 0), wide_near(branch_sums)],
        [lambda: run_attend_back(1)],
    )
    slot([], [lambda: run_fold(branch_sums)])
    slot(
        [
            rows_near(0, 2),
            pair_grad_near(0, 1),
            wide_far(branch_sums, cut[0], cut[1]),
        ],
        [lambda: run_hidden_back(1), lambda: run_project_back(0, 0)],
    )
    last = micros - 1

    def run_expand_sums():
        run_sums(
            expand_sums,
            [[of("second", s)] for s in both],
            [[of("hidden", s)] for s in both],
            True,
        )

    def run_triple_sums():
        run_sums(
            triple_sums,
            [[of("first", s)] for s in both],
            [[of("stacked", s)] for s in both],
            True,
        )

    finals = SimpleNamespace()

    def run_final_branch():
        blocks = branch_out(
            order, flags[1], [(k.active, k.attended) for k in b], contract, packed
        )
        finals.keep = jnp.stack(blocks[0::2])
        finals.send = jnp.stack(blocks[1::2])

    def finals_near():
        return finals.send, lambda passed: fold_hops(finals, passed, "tp", 1, (1,))

    def finals_far():
        def go(passed):
            finals.came = hop(passed, "tp", lanes // 2, (1,))
            return finals.came

        return finals.send, go

    def run_owner_sums():
        branch_sums.whole = owner_sums(
            order, flags[0], of("all_units", 0), of("own_columns", 0)
        )

    slot(
        [pair_grad_far(0, 1), sum_near(0, a[0])] + column_hops(0),
        [lambda: run_attend_back(2), lambda: run_hidden_back(2)],
    )
    slot(
        [pair_grad_near(0, 2), wide_far(branch_sums, cut[1], cut[2])] + column_hops(1),
        [run_expand_sums],
    )
    slot(
        [wide_near(expand_sums), pair_grad_far(0, 2)] + column_hops(2),
        [lambda: run_project_back(0, 1)],
    )
    slot([], [lambda: run_fold(expand_sums)])
    slot(
        [
            wide_far(expand_sums, 0, half_depth),
            sum_far(0, a[0]),
            sum_near(0, a[1]),
            wide_far(branch_sums, cut[2], cut[3]),
        ],
        [lambda: run_project_back(0, 2), run_triple_sums],
    )

    def side_of(mades):
        return sum(
            jnp.concatenate([k.side_first, k.side_second], axis=0) for k in mades
        )

    side = SimpleNamespace(all=jnp.where(first_section, side_of(a), side_of(b)))

    def side_ctx(passed):
        step = 1
        while step < spans:
            middle = passed.shape[1] // 2
            came = hop(passed[:, middle:], "ctx", step, both)
            passed = passed[:, :middle] + came
            step *= 2
        side.all = passed
        return came

    def side_near(passed):
        step = 1
        while 2 * step < lanes:
            came = hop(passed, "tp", step, both)
            passed = passed + came
            step *= 2
        side.all = passed
        return came

    def side_far(passed):
        came = hop(passed, "tp", lanes // 2, both)
        side.all = passed + came
        return came

    def held_back(w, j):
        def go(passed):
            w.parts[j] = passed
            return []

        return w.parts[j], go

    def wide_total(keep, parts):
        came = jnp.concatenate(parts, axis=0) if len(parts) > 1 else parts[0]
        return keep.astype(f32) + came.astype(f32)

    slot(
        [
            wide_near(triple_sums),
            wide_far(expand_sums, half_depth, depth),
            (side.all, side_ctx),
            sum_far(0, a[1]),
        ],
        [run_owner_sums, run_final_branch],
    )
    slot([], [lambda: run_fold(triple_sums)])
    slot(
        [
            wide_far(triple_sums, 0, half_depth),
            sum_near(0, a[2]),
            (side.all, side_near),
            finals_near(),
        ]
    )
    slot(
        [
            wide_far(triple_sums, half_depth, depth),
            sum_far(0, a[2]),
            (side.all, side_far),
            finals_far(),
            held_back(expand_sums, 1),
        ]
    )
    triple_grads = wide_total(triple_sums.keep, triple_sums.parts)
    triple_grads = triple_grads.reshape(triple_weight.shape)
    contract_grads = jnp.where(
        first_section,
        branch_sums.whole[:hidden],
        wide_total(branch_sums.keep[:hidden], branch_sums.parts[:2]),
    )
    output_grads = jnp.where(
        first_section,
        branch_sums.whole[hidden:],
        wide_total(branch_sums.keep[hidden:], branch_sums.parts[2:]),
    )
    expand_grads = wide_total(expand_sums.keep, expand_sums.parts)
    layer_outputs = jnp.stack(
        [
            jnp.where(
                first_section,
                kept[0][m].given,
                (
                    b[m].rows.astype(f32)
                    + finals.keep[m].astype(f32)
                    + finals.came[m].astype(f32)
                ).astype(bf16),
            )
            for m in range(micros)
        ]
    )
    entry_grads = jnp.stack(
        [
            jnp.where(
                first_section,
                norm_back(kept[0][m].rows, total_of(kept[0][m]), inputs[m]),
                kept[1][m].given,
            )
            for m in range(micros)
        ]
    )
    gain_grads = jnp.stack([side.all[0], side.all[2]])
    bias_grads = jnp.stack([side.all[1], side.all[3]])
    return (
        xor_blocks(layer_outputs, span, spans, inverse=True)[None],
        xor_blocks(entry_grads, span, spans, inverse=True)[None],
        triple_grads,
        output_grads.reshape(output_weight.shape),
        expand_grads[None],
        contract_grads[None],
        gain_grads[None],
        bias_grads[None],
    )


def solution(mesh):
    return jax.shard_map(
        shards,
        mesh=mesh,
        in_specs=(
            P(None, ("ctx", "tp"), None),
            P(None, ("ctx", "tp"), None),
            P("pipe", "ctx", "tp", None, None),
            P("pipe", "tp", None, "ctx"),
            P("pipe", "ctx", "tp"),
            P("pipe", "tp", "ctx"),
            P("pipe", None, "ctx"),
            P("pipe", None, "ctx"),
        ),
        out_specs=(
            P("pipe", None, ("ctx", "tp"), None),
            P("pipe", None, ("ctx", "tp"), None),
            P("pipe", "ctx", "tp", None, None),
            P("pipe", "tp", None, "ctx"),
            P("pipe", "ctx", "tp"),
            P("pipe", "tp", "ctx"),
            P("pipe", None, "ctx"),
            P("pipe", None, "ctx"),
        ),
        check_vma=False,
    )
```

```python
import functools
import math
from types import SimpleNamespace

import jax
import jax.numpy as jnp
from jax import lax
from jax.experimental import pallas as pl
from jax.experimental.pallas import tpu as pltpu
from jax.sharding import PartitionSpec as P

ROT = 64
LANES = 128
epsilon = 1e-05
masked_score = -1e30
f32 = jnp.float32
bf16 = jnp.bfloat16
mebibyte = 1024 * 1024
half_root = 0.7071067811865476
bell = 0.3989422804014327


def dot(a, b, dims):
    return lax.dot_general(a, b, (dims, ((), ())), preferred_element_type=f32)


def plain(a, b):
    return dot(a, b, ((1,), (0,)))


def turned(a, b):
    return dot(a, b, ((1,), (1,)))


def doubling(count):
    order, step = [0], count // 2
    while step:
        order += [k ^ step for k in order]
        step //= 2
    return order


def xor_blocks(values, index, count, inverse=False):
    width = values.shape[-1] // count
    order = doubling(count)

    def taken(places):
        return jnp.concatenate(
            [values[..., k * width : (k + 1) * width] for k in places], axis=-1
        )

    if inverse:
        values = taken([order.index(k) for k in range(count)])
    step = 1
    while step < count:
        swapped = taken([k ^ step for k in range(count)])
        values = jnp.where((index & step) != 0, swapped, values)
        step *= 2
    return values if inverse else taken(order)


def rope_tables(positions):
    half = ROT // 2
    frequency = 10000.0 ** (-jnp.arange(0, ROT, 2, dtype=f32) / ROT)
    angles = positions.astype(f32)[:, None] * frequency[None, :]
    cosine, sine = jnp.cos(angles), jnp.sin(angles)
    count = positions.shape[0]
    rest = jnp.zeros((count, LANES - ROT), f32)
    none = jnp.zeros((count, half), f32)
    return jnp.stack(
        [
            jnp.concatenate([cosine, cosine, rest + 1.0], axis=1),
            jnp.concatenate([-sine, none, rest], axis=1),
            jnp.concatenate([none, sine, rest], axis=1),
        ]
    )


def turn(values, tables, sign):
    half = ROT // 2
    part = values[:, :LANES]
    moved = (
        pltpu.roll(part, LANES - half, 1) * tables[1] + pltpu.roll(part, half, 1) * tables[2]
    )
    part = part * tables[0] + (moved if sign > 0 else -moved)
    return jnp.concatenate([part, values[:, LANES:]], axis=1)


def normalize(values):
    center = values - jnp.mean(values, axis=-1, keepdims=True)
    inverse = lax.rsqrt(jnp.mean(center * center, axis=-1, keepdims=True) + epsilon)
    return (center * inverse, inverse)


def whole(array):
    zeros = (0,) * array.ndim
    return pl.BlockSpec(array.shape, lambda *_: zeros)


def at(block, place):
    return pl.BlockSpec(block, lambda *_: place)


kept_out = pl.BlockSpec(memory_space=pl.ANY)


def shape(dims, dtype=bf16):
    return jax.ShapeDtypeStruct(dims, dtype)


class Order:
    def __init__(self):
        self.last = []

    def follow(self, results):
        self.last = [min(results, key=lambda array: array.size * array.dtype.itemsize)]

    def also(self, array):
        self.last = self.last + [array]


took = dict(
    project=7,
    expand=8,
    attend=5,
    branch=8,
    hidden_both=14,
    attend_both=11,
    attend_back=8,
    hidden_back=13,
    project_back=8,
    weight_sums=16,
    fold=7,
)
peak = 1.15e9


def run(order, flags, kernel, ins, outs, scratch, name, grid=(1,), work=0):
    taken = len(ins)
    ins = [(flags, pl.BlockSpec(memory_space=pltpu.SMEM))] + list(ins)
    ins += [(array, kept_out) for array in order.last]
    arrays = [array for array, _ in ins]
    once = grid == (1,)

    def sized(spec, dtype):
        if spec.block_shape is None:
            return spec, 0
        size = math.prod(spec.block_shape) * jnp.dtype(dtype).itemsize
        if not once:
            return spec, 2 * size
        single = pl.BlockSpec(
            spec.block_shape, spec.index_map, pipeline_mode=pl.Buffered(1)
        )
        return single, size

    in_specs = [sized(spec, array.dtype) for array, spec in ins]
    out_specs = [sized(spec, struct.dtype) for struct, spec in outs]
    held = sum(size for _, size in in_specs + out_specs)
    for buffer in scratch:
        if buffer.memory_space == pltpu.VMEM:
            held += math.prod(buffer.shape) * jnp.dtype(buffer.dtype).itemsize

    def body(flag_ref, *refs):
        @pl.when(flag_ref[0] == 1)
        def _():
            kernel(flag_ref, *refs[:taken], *refs[len(ins) - 1 :])

    results = pl.pallas_call(
        body,
        grid=grid,
        in_specs=[spec for spec, _ in in_specs],
        out_specs=[spec for spec, _ in out_specs],
        out_shape=[struct for struct, _ in outs],
        scratch_shapes=scratch,
        compiler_params=pltpu.CompilerParams(
            vmem_limit_bytes=int(held + (work + 4) * mebibyte)
        ),
        cost_estimate=pl.CostEstimate(
            flops=int(took[name] * peak), bytes_accessed=0, transcendentals=0
        ),
        name=name,
    )(*arrays)
    order.follow(results)
    return results


def fence(through, waits):
    count = len(through)

    def kernel(*refs):
        pass

    return pl.pallas_call(
        kernel,
        in_specs=[kept_out] * (count + len(waits)),
        out_specs=[kept_out] * count,
        out_shape=[shape(array.shape, array.dtype) for array in through],
        input_output_aliases={j: j for j in range(count)},
        compiler_params=pltpu.CompilerParams(vmem_limit_bytes=mebibyte),
        cost_estimate=pl.CostEstimate(flops=1, bytes_accessed=1, transcendentals=0),
        name="fence",
    )(*through, *waits)


def full_out(dims, dtype=bf16):
    zeros = (0,) * len(dims)
    return (shape(dims, dtype), pl.BlockSpec(dims, lambda *_: zeros))


def copies(sources, targets, sems):
    started = []
    for source, target, sem in zip(sources, targets, sems):
        copy = pltpu.make_async_copy(source, target, sem)
        copy.start()
        started.append(copy)
    return started


def project(order, flags, pieces, at_piece, gains, biases, tables, weights, heads, head_dim):
    count, width = 1, pieces[0].shape[2]
    span_rows = sum(piece.shape[1] for piece in pieces)
    rows = count * span_rows
    chunk = pieces[0].shape[1]
    spans = len(weights)
    depth = width // spans
    wide = 3 * head_dim
    columns = heads * wide

    def kernel(flag_ref, *refs):
        piece_refs = refs[: len(pieces)]
        gain_ref, bias_ref, table_ref = refs[len(pieces) : len(pieces) + 3]
        weight_refs = refs[len(pieces) + 3 : len(pieces) + 3 + spans]
        first, second, normal, queries, pair, held, sems = refs[len(pieces) + 3 + spans :]
        started = []
        for h in range(heads):
            started.append(
                copies(
                    [w.at[:depth, h * wide : (h + 1) * wide] for w in weight_refs],
                    [held.at[h, k * depth : (k + 1) * depth] for k in range(spans)],
                    [sems.at[h, k] for k in range(spans)],
                )
            )
        start = 0
        for piece_ref in piece_refs:
            chunks = piece_ref.shape[1] // chunk

            def one(i, _, piece_ref=piece_ref, start=start, chunks=chunks):
                m, c = i // chunks, i % chunks
                values = piece_ref[m, pl.ds(pl.multiple_of(c * chunk, chunk), chunk), :]
                normed, _ = normalize(values.astype(f32))
                to = pl.ds(
                    pl.multiple_of(m * span_rows + start + c * chunk, chunk), chunk
                )
                normal[to, :] = normed.astype(bf16)
                first[to, :] = (normed * gain_ref[0:1] + bias_ref[0:1]).astype(bf16)
                second[to, :] = (normed * gain_ref[1:2] + bias_ref[1:2]).astype(bf16)
                return 0

            lax.fori_loop(0, count * chunks, one, 0)
            start += piece_ref.shape[1]
        for h in range(heads):
            for copy in started[h]:
                copy.wait()

            def two(m, _, h=h):
                to = pl.ds(pl.multiple_of(m * span_rows, span_rows), span_rows)
                made = plain(first[to, :], held[h])
                queries[h, to, :] = turn(made[:, :head_dim], table_ref, 1).astype(bf16)
                pair[0, h, to, :] = turn(
                    made[:, head_dim : 2 * head_dim], table_ref, 1
                ).astype(bf16)
                pair[1, h, to, :] = made[:, 2 * head_dim :].astype(bf16)
                return 0

            lax.fori_loop(0, count, two, 0)

    ins = [(piece, at((1,) + piece.shape[1:], (at_piece, 0, 0))) for piece in pieces]
    ins += [(array, whole(array)) for array in (gains, biases, tables)]
    ins += [(w, kept_out) for w in weights]
    outs = [full_out((rows, width))] * 3 + [
        full_out((heads, rows, head_dim)),
        full_out((2, heads, rows, head_dim)),
    ]
    scratch = [
        pltpu.VMEM((heads, width, wide), bf16),
        pltpu.SemaphoreType.DMA((heads, spans)),
    ]
    return run(order, flags, kernel, ins, outs, scratch, "project")


def expand_up(order, flags, second, weights, span_rows):
    rows, width = second.shape
    depth, hidden = weights[0].shape
    spans = len(weights)
    tile = min(512, hidden)
    tiles = hidden // tile

    def kernel(flag_ref, *refs):
        second_ref, weight_refs = refs[0], refs[1 : 1 + spans]
        active, slope, held, sems = refs[1 + spans :]
        started = []
        for t in range(tiles):
            started.append(
                copies(
                    [w.at[:, t * tile : (t + 1) * tile] for w in weight_refs],
                    [held.at[t, k * depth : (k + 1) * depth] for k in range(spans)],
                    [sems.at[t, k] for k in range(spans)],
                )
            )
        for t in range(tiles):
            for copy in started[t]:
                copy.wait()

            def one(m, _, t=t):
                to = pl.ds(pl.multiple_of(m * span_rows, span_rows), span_rows)
                pre = plain(second_ref[to, :], held[t])
                risen = 0.5 * (1.0 + lax.erf(pre * half_root))
                columns = slice(t * tile, (t + 1) * tile)
                active[to, columns] = (pre * risen).astype(bf16)
                slope[to, columns] = (
                    risen + pre * jnp.exp(-0.5 * pre * pre) * bell
                ).astype(bf16)
                return 0

            lax.fori_loop(0, rows // span_rows, one, 0)

    ins = [(second, whole(second))] + [(w, kept_out) for w in weights]
    outs = [full_out((rows, hidden))] * 2
    scratch = [
        pltpu.VMEM((tiles, width, tile), bf16),
        pltpu.SemaphoreType.DMA((tiles, spans)),
    ]
    return run(order, flags, kernel, ins, outs, scratch, "expand")


def spread(refs):
    return [ref.at[j] for ref in refs for j in range(ref.shape[0])]


def attention(here, pairs, head, row_ref, key_ref, scale):
    scores = []
    for k, pair in enumerate(pairs):
        raw = turned(here, pair[0, head]) * scale
        scores.append(jnp.where(key_ref[k] <= row_ref[...], raw, masked_score))
    top = functools.reduce(
        jnp.maximum, [jnp.max(part, axis=1, keepdims=True) for part in scores]
    )
    scores = [jnp.exp(part - top) for part in scores]
    inverse = 1.0 / sum(jnp.sum(part, axis=1, keepdims=True) for part in scores)
    return [part * inverse for part in scores]


def attend(order, flags, queries, pairs, positions, key_positions, scale):
    heads, rows, head_dim = queries.shape
    spans = sum(pair.shape[0] for pair in pairs)

    def kernel(flag_ref, query_ref, *refs):
        views, refs = spread(refs[: len(pairs)]), refs[len(pairs) :]
        row_ref, key_ref, attended, probs = refs
        for h in range(heads):
            parts = attention(query_ref[h], views, h, row_ref, key_ref, scale)
            summed = None
            for k in range(spans):
                part = parts[k].astype(bf16)
                probs[k, h] = part
                term = plain(part, views[k][1, h])
                summed = term if summed is None else summed + term
            attended[:, h * head_dim : (h + 1) * head_dim] = summed.astype(bf16)

    ins = [
        (array, whole(array)) for array in (queries, *pairs, positions, key_positions)
    ]
    outs = [full_out((rows, heads * head_dim)), full_out((spans, heads, rows, rows))]
    work = spans * rows * rows * 4 * heads * 4 / mebibyte
    return run(order, flags, kernel, ins, outs, [], "attend", work=work)


def attention_grads(grad, here, parts, views, head, keep, send, scale):
    half = keep.shape[0]
    grad_probs = [turned(grad, view[1, head]) for view in views]
    delta = sum(
        jnp.sum(part.astype(f32) * slope, axis=1, keepdims=True)
        for part, slope in zip(parts, grad_probs)
    )
    query_grad = None
    for k, view in enumerate(views):
        slopes = (parts[k].astype(f32) * (grad_probs[k] - delta)).astype(bf16)
        term = plain(slopes, view[0, head])
        query_grad = term if query_grad is None else query_grad + term
        side = keep if k < half else send
        side[k % half, 0, head] = (dot(slopes, here, ((0,), (0,))) * scale).astype(bf16)
        side[k % half, 1, head] = dot(parts[k].astype(bf16), grad, ((0,), (0,))).astype(bf16)
    return query_grad * scale


def attend_both(
    order, flags, rows_in, packed, queries, pairs, positions, key_positions, tables, scale
):
    heads, rows, head_dim = queries.shape
    width = rows_in.shape[1]
    spans = len(packed)
    across, depth = heads * head_dim, width // spans
    half = spans // 2

    def kernel(flag_ref, rows_ref, *refs):
        packed_refs, refs = refs[:spans], refs[spans:]
        query_ref, refs = refs[0], refs[1:]
        views, refs = spread(refs[: len(pairs)]), refs[len(pairs) :]
        row_ref, key_ref, table_ref, attended, turned_back, keep, send, held, sems = refs
        started = copies(
            [w.at[:across, 3 * across : 3 * across + depth] for w in packed_refs],
            [held.at[:, k * depth : (k + 1) * depth] for k in range(spans)],
            [sems.at[k] for k in range(spans)],
        )
        all_parts = []
        for h in range(heads):
            parts = attention(query_ref[h], views, h, row_ref, key_ref, scale)
            summed = None
            for k in range(spans):
                term = plain(parts[k].astype(bf16), views[k][1, h])
                summed = term if summed is None else summed + term
            attended[:, h * head_dim : (h + 1) * head_dim] = summed.astype(bf16)
            all_parts.append(parts)
        for copy in started:
            copy.wait()
        grads = turned(rows_ref[...], held[...]).astype(bf16)
        for h in range(heads):
            made = attention_grads(
                grads[:, h * head_dim : (h + 1) * head_dim],
                query_ref[h],
                all_parts[h],
                views,
                h,
                keep,
                send,
                scale,
            )
            turned_back[h] = turn(made, table_ref, -1).astype(bf16)

    ins = [(rows_in, whole(rows_in))] + [(w, kept_out) for w in packed]
    ins += [
        (array, whole(array)) for array in (queries, *pairs, positions, key_positions, tables)
    ]
    outs = [full_out((rows, across)), full_out((heads, rows, head_dim))]
    outs += [full_out((half, 2, heads, rows, head_dim))] * 2
    scratch = [pltpu.VMEM((across, width), bf16), pltpu.SemaphoreType.DMA((spans,))]
    work = spans * rows * rows * 4 * (heads + 4) / mebibyte
    return run(order, flags, kernel, ins, outs, scratch, "attend_both", work=work)


def hidden_both(order, flags, second, pieces, at_piece, expand, contract, normal, gains):
    rows, width = second.shape
    hidden, depth = contract[0].shape
    spans = len(contract)
    tile = min(512, hidden)
    tiles = hidden // tile

    def kernel(flag_ref, second_ref, *refs):
        piece_refs, refs = refs[: len(pieces)], refs[len(pieces) :]
        expand_refs, refs = refs[:spans], refs[spans:]
        contract_refs, refs = refs[:spans], refs[spans:]
        normal_ref, gain_ref, rows_out, active, grads, part, side, *refs = refs
        held_up, held_down, sems_up, sems_down = refs
        started = []
        for t in range(tiles):
            block = slice(t * tile, (t + 1) * tile)
            places = [slice(k * depth, (k + 1) * depth) for k in range(spans)]
            up = copies(
                [w.at[:, block] for w in expand_refs],
                [held_up.at[place, block] for place in places],
                [sems_up.at[t, k] for k in range(spans)],
            )
            down = copies(
                [w.at[block, :] for w in contract_refs],
                [held_down.at[block, place] for place in places],
                [sems_down.at[t, k] for k in range(spans)],
            )
            started.append((up, down))
        start = 0
        for piece_ref in piece_refs:
            size = piece_ref.shape[1]
            rows_out[start : start + size, :] = piece_ref[0]
            start += size
        for t in range(tiles):
            block = slice(t * tile, (t + 1) * tile)
            for copy in started[t][0] + started[t][1]:
                copy.wait()
            pre = plain(second_ref[...], held_up[:, block])
            risen = 0.5 * (1.0 + lax.erf(pre * half_root))
            active[:, block] = (pre * risen).astype(bf16)
            slope = risen + pre * jnp.exp(-0.5 * pre * pre) * bell
            grads[:, block] = (turned(rows_out[...], held_down[block, :]) * slope).astype(bf16)
        for k in range(spans):
            place = slice(k * depth, (k + 1) * depth)
            made = turned(grads[...], held_up[place, :])
            side[0:1, place] = jnp.sum(
                made * normal_ref[:, place].astype(f32), axis=0, keepdims=True
            )
            side[1:2, place] = jnp.sum(made, axis=0, keepdims=True)
            part[:, place] = made * gain_ref[1:2, place]

    ins = [(second, whole(second))]
    ins += [(piece, at((1,) + piece.shape[1:], (at_piece, 0, 0))) for piece in pieces]
    ins += [(w, kept_out) for w in expand] + [(w, kept_out) for w in contract]
    ins += [(normal, whole(normal)), (gains, whole(gains))]
    outs = [
        full_out((rows, width)),
        full_out((rows, hidden)),
        full_out((rows, hidden)),
        full_out((rows, width), f32),
        full_out((2, width), f32),
    ]
    scratch = [
        pltpu.VMEM((width, hidden), bf16),
        pltpu.VMEM((hidden, width), bf16),
        pltpu.SemaphoreType.DMA((tiles, spans)),
        pltpu.SemaphoreType.DMA((tiles, spans)),
    ]
    return run(order, flags, kernel, ins, outs, scratch, "hidden_both")


def branch_out(order, flags, groups, contract, packed):
    hidden, depth = contract[0].shape
    across = groups[0][1].shape[1]
    spans = len(contract)
    width = depth * spans
    span_rows = groups[0][0].shape[0]
    block = span_rows // 2
    count = len(groups)

    def kernel(flag_ref, *refs):
        group_refs, refs = refs[: 2 * count], refs[2 * count :]
        contract_refs, packed_refs = refs[:spans], refs[spans : 2 * spans]
        blocks, refs = refs[2 * spans : 2 * (spans + count)], refs[2 * (spans + count) :]
        held, held_out, sems = refs
        outputs = [w.at[:across, 3 * across : 3 * across + depth] for w in packed_refs]
        started = copies(
            [ref for k in range(spans) for ref in (outputs[k], contract_refs[k])],
            [ref for k in range(spans) for ref in (held_out.at[k], held.at[k])],
            [sems.at[j] for j in range(2 * spans)],
        )
        for k in range(spans):
            started[2 * k].wait()
            started[2 * k + 1].wait()
            columns = slice(k * depth, (k + 1) * depth)
            for c in range(count):
                made = plain(group_refs[2 * c + 1][...], held_out[k])
                made = made + plain(group_refs[2 * c][...], held[k])
                blocks[2 * c][:, columns] = made[:block].astype(bf16)
                blocks[2 * c + 1][:, columns] = made[block:].astype(bf16)

    ins = []
    for active, attended in groups:
        ins += [(active, whole(active)), (attended, whole(attended))]
    ins += [(w, kept_out) for w in contract] + [(w, kept_out) for w in packed]
    outs = [full_out((block, width))] * (2 * count)
    scratch = [
        pltpu.VMEM((spans, hidden, depth), bf16),
        pltpu.VMEM((spans, across, depth), bf16),
        pltpu.SemaphoreType.DMA((2 * spans,)),
    ]
    return run(order, flags, kernel, ins, outs, scratch, "branch")


def attend_back(order, flags, pieces, packed, queries, pairs, probs, tables, scale):
    rows = sum(piece.shape[1] for piece in pieces)
    width = pieces[0].shape[2]
    heads, _, head_dim = queries.shape
    spans = len(packed)
    across, depth = heads * head_dim, width // spans
    half = spans // 2

    def kernel(flag_ref, *refs):
        piece_refs, refs = refs[: len(pieces)], refs[len(pieces) :]
        packed_refs, refs = refs[:spans], refs[spans:]
        query_ref, refs = refs[0], refs[1:]
        views, refs = spread(refs[: len(pairs)]), refs[len(pairs) :]
        prob_ref, table_ref, rows_out, turned_back, keep, send, held, sems = refs
        started = copies(
            [w.at[:across, 3 * across : 3 * across + depth] for w in packed_refs],
            [held.at[:, k * depth : (k + 1) * depth] for k in range(spans)],
            [sems.at[k] for k in range(spans)],
        )
        start = 0
        for piece_ref in piece_refs:
            size = piece_ref.shape[1]
            rows_out[start : start + size, :] = piece_ref[0]
            start += size
        for copy in started:
            copy.wait()
        grads = turned(rows_out[...], held[...]).astype(bf16)
        for h in range(heads):
            made = attention_grads(
                grads[:, h * head_dim : (h + 1) * head_dim],
                query_ref[h],
                [prob_ref[k, h] for k in range(spans)],
                views,
                h,
                keep,
                send,
                scale,
            )
            turned_back[h] = turn(made, table_ref, -1).astype(bf16)

    ins = [(piece, whole(piece)) for piece in pieces] + [(w, kept_out) for w in packed]
    ins += [(array, whole(array)) for array in (queries, *pairs, probs, tables)]
    outs = [full_out((rows, width)), full_out((heads, rows, head_dim))]
    outs += [full_out((half, 2, heads, rows, head_dim))] * 2
    scratch = [pltpu.VMEM((across, width), bf16), pltpu.SemaphoreType.DMA((spans,))]
    work = spans * rows * rows * 4 * 4 / mebibyte
    return run(order, flags, kernel, ins, outs, scratch, "attend_back", work=work)


def hidden_back(order, flags, upstream, contract, expand, slope, normal, gains):
    span_rows, width = upstream.shape
    hidden, depth = contract[0].shape
    spans = len(contract)
    tile = min(512, hidden)
    tiles = hidden // tile

    def kernel(flag_ref, *refs):
        upstream_ref, refs = refs[0], refs[1:]
        contract_refs, refs = refs[:spans], refs[spans:]
        expand_refs, refs = refs[:spans], refs[spans:]
        slope_ref, normal_ref, gain_ref, grads, part, side, held, held_up, sems, sems_up = refs
        started = [
            copies(
                [w.at[t * tile : (t + 1) * tile, :] for w in contract_refs],
                [held.at[t, :, k * depth : (k + 1) * depth] for k in range(spans)],
                [sems.at[t, k] for k in range(spans)],
            )
            for t in range(tiles)
        ]
        started_up = copies(
            expand_refs, [held_up.at[k] for k in range(spans)], [sems_up.at[k] for k in range(spans)]
        )
        for t in range(tiles):
            for copy in started[t]:
                copy.wait()
            columns = slice(t * tile, (t + 1) * tile)
            grads[:, columns] = (
                turned(upstream_ref[...], held[t]) * slope_ref[:, columns].astype(f32)
            ).astype(bf16)
        for k in range(spans):
            started_up[k].wait()
            made = turned(grads[...], held_up[k])
            columns = slice(k * depth, (k + 1) * depth)
            side[0:1, columns] = jnp.sum(
                made * normal_ref[:, columns].astype(f32), axis=0, keepdims=True
            )
            side[1:2, columns] = jnp.sum(made, axis=0, keepdims=True)
            part[:, columns] = made * gain_ref[1:2, columns]

    ins = [(upstream, whole(upstream))]
    ins += [(w, kept_out) for w in contract] + [(w, kept_out) for w in expand]
    ins += [
        (slope, whole(slope)),
        (normal, whole(normal)),
        (gains, whole(gains)),
    ]
    outs = [
        full_out((span_rows, hidden)),
        full_out((span_rows, width), f32),
        full_out((2, width), f32),
    ]
    scratch = [
        pltpu.VMEM((tiles, tile, width), bf16),
        pltpu.VMEM((spans, depth, hidden), bf16),
        pltpu.SemaphoreType.DMA((tiles, spans)),
        pltpu.SemaphoreType.DMA((spans,)),
    ]
    return run(order, flags, kernel, ins, outs, scratch, "hidden_back")


def project_back(
    order, flags, turned_back, own, came, weights, part, normal, gains, tables
):
    heads, span_rows, head_dim = turned_back.shape
    spans = len(weights)
    width = part.shape[1]
    depth, columns = width // spans, 3 * heads * head_dim
    block = span_rows // 2

    def kernel(flag_ref, *refs):
        query_ref, own_ref, came_ref, refs = refs[0], refs[1], refs[2], refs[3:]
        weight_refs, refs = refs[:spans], refs[spans:]
        part_ref, normal_ref, gain_ref, table_ref, grads, side, *refs = refs
        low, high, held, sems = refs
        started = copies(
            [w.at[:depth, :columns] for w in weight_refs],
            [held.at[k] for k in range(spans)],
            [sems.at[k] for k in range(spans)],
        )
        for h in range(heads):
            at_column = h * 3 * head_dim
            keys = own_ref[0, h].astype(f32) + came_ref[0, h].astype(f32)
            values = own_ref[1, h].astype(f32) + came_ref[1, h].astype(f32)
            grads[:, at_column : at_column + head_dim] = query_ref[h]
            grads[:, at_column + head_dim : at_column + 2 * head_dim] = turn(
                keys, table_ref, -1
            ).astype(bf16)
            grads[:, at_column + 2 * head_dim : at_column + 3 * head_dim] = values.astype(bf16)
        for k in range(spans):
            started[k].wait()
            made = turned(grads[...], held[k])
            span_columns = slice(k * depth, (k + 1) * depth)
            side[0:1, span_columns] = jnp.sum(
                made * normal_ref[:, span_columns].astype(f32), axis=0, keepdims=True
            )
            side[1:2, span_columns] = jnp.sum(made, axis=0, keepdims=True)
            both = (made * gain_ref[0:1, span_columns] + part_ref[:, span_columns]).astype(bf16)
            low[:, span_columns] = both[:block]
            high[:, span_columns] = both[block:]

    ins = [(array, whole(array)) for array in (turned_back, own, came)]
    ins += [(w, kept_out) for w in weights]
    ins += [(part, whole(part)), (normal, whole(normal))]
    ins += [(gains, whole(gains)), (tables, whole(tables))]
    outs = [full_out((span_rows, columns)), full_out((2, width), f32)]
    outs += [full_out((block, width))] * 2
    scratch = [pltpu.VMEM((spans, depth, columns), bf16), pltpu.SemaphoreType.DMA((spans,))]
    return run(order, flags, kernel, ins, outs, scratch, "project_back")


def weight_sums(order, flags, lefts, rights, by_rows, spans):
    rows = sum(piece.shape[0] for piece in lefts[0][0])
    left_width = sum(group[0].shape[1] for group in lefts[0])
    right_width = sum(group[0].shape[1] for group in rights[0])
    if by_rows:
        tile = left_width // spans
        steps, block = spans // 2, (tile, right_width)
    else:
        tile = min(512, left_width)
        while left_width % tile:
            tile //= 2
        steps, block = left_width // tile, (tile, right_width // 2)
    chunk = min(1024, block[1])
    while right_width % chunk:
        chunk //= 2
    pieces = [
        [piece for groups in (lefts[s], rights[s]) for group in groups for piece in group]
        for s in (0, 1)
    ]
    most = max(len(p) for p in pieces)

    def kernel(flag_ref, *refs):
        piece_refs = (refs[: len(pieces[0])], refs[len(pieces[0]) : len(pieces[0]) + len(pieces[1])])
        keep, send, left, right, flipped, sems = refs[len(pieces[0]) + len(pieces[1]) :]
        g = pl.program_id(0)
        for s in (0, 1):

            @pl.when((g == 0) & (flag_ref[2] == s))
            def _(s=s):
                targets = []
                for held, groups in ((left, lefts[s]), (right, rights[s])):
                    column = 0
                    for group in groups:
                        row, wide = 0, group[0].shape[1]
                        for piece in group:
                            targets.append(
                                held.at[row : row + piece.shape[0], column : column + wide]
                            )
                            row += piece.shape[0]
                        column += wide
                started = copies(
                    piece_refs[s], targets, [sems.at[j] for j in range(len(targets))]
                )
                for copy in started:
                    copy.wait()

        def product(column, store):
            flipped[...] = left[:, pl.ds(pl.multiple_of(column, LANES), tile)].T

            def one(c, _):
                columns = pl.ds(pl.multiple_of(c * chunk, chunk), chunk)
                store(c, plain(flipped[...], right[:, columns]).astype(bf16))
                return 0

            lax.fori_loop(0, right_width // chunk, one, 0)

        if by_rows:

            def to(target):
                def store(c, made):
                    target[:, pl.ds(pl.multiple_of(c * chunk, chunk), chunk)] = made

                return store

            product(g * tile, to(keep))
            product((g + steps) * tile, to(send))
        else:
            half = right_width // 2 // chunk

            def store(c, made):
                @pl.when(c < half)
                def _():
                    keep[:, pl.ds(pl.multiple_of(c * chunk, chunk), chunk)] = made

                @pl.when(c >= half)
                def _():
                    send[:, pl.ds(pl.multiple_of((c - half) * chunk, chunk), chunk)] = made

            product(g * tile, store)

    ins = [(piece, kept_out) for s in (0, 1) for piece in pieces[s]]
    dims = (steps * tile, block[1])
    outs = [(shape(dims), pl.BlockSpec(block, lambda g: (g, 0)))] * 2
    scratch = [
        pltpu.VMEM((rows, left_width), bf16),
        pltpu.VMEM((rows, right_width), bf16),
        pltpu.VMEM((tile, rows), bf16),
        pltpu.SemaphoreType.DMA((most,)),
    ]
    return run(
        order, flags, kernel, ins, outs, scratch, "weight_sums", grid=(steps,)
    )


def fold(order, flags, keep, came, dim):
    rows, columns = keep.shape
    if dim == 0:
        tile = rows // 4
        steps, block = rows // 2 // tile, (tile, columns)
        places = [lambda g: (g, 0), lambda g: (g + steps, 0)]
        half = (rows // 2, columns)
    else:
        tile = rows // 4
        steps, block = rows // tile, (tile, columns // 2)
        places = [lambda g: (g, 0), lambda g: (g, 1)]
        half = (rows, columns // 2)

    def kernel(flag_ref, keep_low, keep_high, came_low, came_high, low, high):
        low[...] = (keep_low[...].astype(f32) + came_low[...].astype(f32)).astype(bf16)
        high[...] = (keep_high[...].astype(f32) + came_high[...].astype(f32)).astype(bf16)

    ins = [(array, pl.BlockSpec(block, place)) for array in (keep, came) for place in places]
    outs = [(shape(half), pl.BlockSpec(block, lambda g: (g, 0)))] * 2
    return run(order, flags, kernel, ins, outs, [], "fold", grid=(steps,))


def shards(
    block_input,
    out_grad,
    triple_weight,
    output_weight,
    expand_weight,
    contract_weight,
    norm_gains,
    norm_biases,
):
    section = lax.axis_index("pipe")
    span = lax.axis_index("ctx")
    lane = lax.axis_index("tp")
    spans = lax.axis_size("ctx")
    lanes = lax.axis_size("tp")
    micros, rows, width = block_input.shape
    span_rows = rows * lanes
    heads = triple_weight.shape[2]
    head_dim = triple_weight.shape[4]
    across_units = heads * head_dim
    scale = head_dim ** (-0.5)
    first_section = section == 0
    both = (0, 1)

    def hop(array, axis, step, sections):
        size = lax.axis_size(axis)
        pairs = [(s * size + a, s * size + (a ^ step)) for s in sections for a in range(size)]
        return lax.ppermute(array, ("pipe", axis), pairs)

    order = Order()

    def flags_for(wanted):
        return jnp.stack([jnp.asarray(wanted), span, section]).astype(jnp.int32)

    flags = [flags_for(section == s) for s in both]
    always = flags_for(1)

    kept = [[SimpleNamespace() for _ in range(micros)] for _ in both]
    due = {}
    slot_index = [0]

    def slot(hops, kernels=()):
        now = slot_index[0]
        slot_index[0] += 1
        ready = due.pop(now, [])
        hops = [h if len(h) == 3 else h + (1,) for h in hops]
        if hops:
            gated = fence([operand for operand, _, _ in hops], order.last + ready)
            order.last = [min(gated, key=lambda array: array.size)]
            for passed, (_, go, slots) in zip(gated, hops):
                results = go(passed)
                results = results if isinstance(results, list) else [results]
                due.setdefault(now + slots, []).extend(results)
        else:
            order.last = order.last + ready
        for kernel in kernels:
            kernel()

    def halved(keep, came, dim):
        middle = keep.shape[dim] // 2
        total = keep.astype(f32) + came.astype(f32)
        return (
            lax.slice_in_dim(total, 0, middle, axis=dim).astype(bf16),
            lax.slice_in_dim(total, middle, 2 * middle, axis=dim).astype(bf16),
        )

    def spread_hops(pieces, axis, axis_name, sections, first):
        step = lax.axis_size(axis_name) // 4
        going = first
        while step:
            pieces.append(hop(going, axis_name, step, sections))
            going = jnp.concatenate(pieces, axis=axis)
            step //= 2
        return pieces[-1]

    def fold_hops(k, first, axis_name, dim, sections):
        step, size = 1, lax.axis_size(axis_name)
        while 2 * step < size:
            came = hop(first, axis_name, step, sections)
            k.keep, k.send = halved(k.keep, came, dim)
            first = k.send
            step *= 2
        return came

    depth = width // spans
    far = spans // 2
    assert depth == across_units
    small = jnp.concatenate([norm_gains[0], norm_biases[0]], axis=0)
    packed = jnp.concatenate(
        [triple_weight[0].reshape(depth, -1), output_weight[0].reshape(-1, depth)],
        axis=1,
    )
    packed = jnp.pad(packed, ((0, 16), (0, 0)))
    packed = lax.dynamic_update_slice(packed, small, (depth, 0))
    own_expand, own_contract = expand_weight[0], contract_weight[0]
    hidden = own_expand.shape[1]
    inputs = xor_blocks(block_input, span, spans)
    cotangent = xor_blocks(out_grad, span, spans)
    early = jnp.where(first_section, inputs, cotangent)

    in_row = jnp.arange(rows, dtype=jnp.int32)
    in_span = jnp.concatenate([(lane ^ j) * rows + in_row for j in doubling(lanes)])
    positions = span * span_rows + in_span
    key_positions = jnp.stack([(span ^ k) * span_rows + in_span for k in doubling(spans)])
    tables = rope_tables(positions)
    position_column = positions[:, None]
    key_positions = key_positions[:, None, :]

    def blocks_of(own, came):
        held, step = {0: own, far: came}, far // 2
        while step:
            for k in list(held):
                held[k ^ step] = hop(held[k], "ctx", step, both)
            step //= 2
        return [held[k] for k in doubling(spans)]

    lane_offsets = doubling(lanes)

    def across(array, j, source):
        pairs = [(source * lanes + a, (1 - source) * lanes + (a ^ j)) for a in range(lanes)]
        return lax.ppermute(array, ("pipe", "tp"), pairs)

    def rows_far(s, m):
        k = kept[s][m]

        def go(passed):
            k.rows = passed
            k.pieces = [passed, hop(passed, "tp", lanes // 2, (s,))]
            return k.pieces[1]

        return k.rows, go

    def rows_near(s, m):
        k = kept[s][m]

        def go(passed):
            last_piece = spread_hops(k.pieces, 0, "tp", (s,), passed)
            k.row_pieces = [piece[None] for piece in k.pieces]
            return last_piece

        return jnp.concatenate(k.pieces, axis=0), go

    def one_way(array, direction, s):
        pairs = [
            (s * spans + a, s * spans + (a ^ far))
            for a in range(spans)
            if direction * ((a ^ far) - a) > 0
        ]
        return lax.ppermute(array, ("pipe", "ctx"), pairs)

    def pair_far(s, m):
        k = kept[s][m]

        def go(passed):
            k.pairs = [passed, one_way(passed, 1, s)]
            return k.pairs[1]

        return k.pair, go

    def pair_near(s, m):
        k = kept[s][m]

        def go(passed):
            return spread_hops(k.pairs, 0, "ctx", (s,), passed)

        return jnp.concatenate(k.pairs, axis=0), go

    def pair_grad_near(s, m):
        k = kept[s][m].pair_grad
        return k.send, lambda passed: fold_hops(k, passed, "ctx", 0, (s,))

    def pair_grad_both(s, m):
        k = kept[s][m].pair_grad

        def go(passed):
            fold_hops(k, passed, "ctx", 0, (s,))
            k.came = one_way(k.send, -1, s)
            return k.came

        return k.send, go

    def pair_grad_far(s, m):
        k = kept[s][m].pair_grad

        def go(passed):
            k.came = one_way(passed, -1, s)
            return k.came

        return k.send, go

    def sum_near(s, k):
        k.keep, going = k.blocks
        return going, lambda passed: fold_hops(k, passed, "tp", 0, (s,))

    def sum_far(s, k):
        def go(passed):
            k.blocks, k.arrived = [k.keep], [hop(passed, "tp", lanes // 2, (s,))]
            return k.arrived[0]

        return k.send, go

    def total_of(k):
        return sum(array.astype(f32) for array in [k.blocks[0], *k.arrived])

    def norm_back(upstream, combined, entering):
        normalized, inverse = normalize(entering.astype(f32))
        return (
            upstream.astype(f32)
            + inverse
            * (
                combined
                - jnp.mean(combined, axis=-1, keepdims=True)
                - normalized * jnp.mean(combined * normalized, axis=-1, keepdims=True)
            )
        ).astype(bf16)

    def middle_of(m):
        return (inputs[m].astype(f32) + total_of(kept[0][m])).astype(bf16)

    def entry_of(m):
        k = kept[1][m]
        return norm_back(cotangent[m], total_of(k), k.rows)

    def hand_one(s, m):
        k, other = kept[s][m], kept[1 - s][m]
        k.given = middle_of(m) if s == 0 else entry_of(m)

        def go(passed):
            k.given = passed
            other.rows = across(passed, 0, s)
            return other.rows

        return k.given, go

    def run_project(s, m):
        k = kept[s][m]
        pieces, place = (early_pieces, m) if s == 0 else (k.row_pieces, 0)
        k.first, k.second, k.normal, k.queries, pair = project(
            order, flags[s], pieces, place, gains, biases, tables, packed, heads, head_dim
        )
        k.pair = pair[None]

    def run_expand(m):
        k = kept[0][m]
        k.active, k.slope = expand_up(order, flags[0], k.second, weights.expand, span_rows)

    def run_attend(m):
        k = kept[0][m]
        k.attended, k.probs = attend(
            order, flags[0], k.queries, k.pairs, position_column, key_positions, scale
        )

    def run_branch(m):
        k = kept[0][m]
        k.blocks = branch_out(
            order, flags[0], [(k.active, k.attended)], contract, packed
        )

    def run_hidden_both(m):
        k = kept[1][m]
        k.upstream, k.active, k.hidden, k.part, k.side_second = hidden_both(
            order,
            flags[1],
            k.second,
            early_pieces,
            m,
            weights.expand,
            contract,
            k.normal,
            gains,
        )

    def run_attend_both(m):
        k = kept[1][m]
        k.attended, k.turned_back, keep, send = attend_both(
            order,
            flags[1],
            k.upstream,
            packed,
            k.queries,
            k.pairs,
            position_column,
            key_positions,
            tables,
            scale,
        )
        k.pair_grad = SimpleNamespace(keep=keep, send=send)

    def run_attend_back(m):
        k = kept[0][m]
        k.upstream, k.turned_back, keep, send = attend_back(
            order,
            flags[0],
            k.row_pieces,
            packed,
            k.queries,
            k.pairs,
            k.probs,
            tables,
            scale,
        )
        k.pair_grad = SimpleNamespace(keep=keep, send=send)

    def run_hidden_back(m):
        k = kept[0][m]
        k.hidden, k.part, k.side_second = hidden_back(
            order,
            flags[0],
            k.upstream,
            contract,
            weights.expand,
            k.slope,
            k.normal,
            gains,
        )

    def run_project_back(s, m):
        k = kept[s][m]
        own, arrived = k.pair_grad.keep, k.pair_grad.came
        k.stacked, k.side_first, *k.blocks = project_back(
            order,
            flags[s],
            k.turned_back,
            own.reshape(own.shape[1:]),
            arrived.reshape(arrived.shape[1:]),
            packed,
            k.part,
            k.normal,
            gains,
            tables,
        )

    def of(name, s, count=micros):
        return [getattr(kept[s][m], name) for m in range(count)]

    branch_sums, expand_sums, triple_sums = (SimpleNamespace(parts=[]) for _ in range(3))

    def run_sums(w, lefts, rights, by_rows):
        w.dim = 0 if by_rows else 1
        w.keep, w.send = weight_sums(order, always, lefts, rights, by_rows, spans)

    def wide_near(w):
        def go(passed):
            w.came = hop(passed, "ctx", 1, both)
            return w.came

        return w.send, go

    def run_fold(w):
        step = 2
        w.keep, w.send = fold(order, always, w.keep, w.came, w.dim)
        while 2 * step < spans:
            w.came = hop(w.send, "ctx", step, both)
            w.keep, w.send = fold(order, always, w.keep, w.came, w.dim)
            step *= 2

    def wide_far(w, start, stop):
        def go(passed):
            w.parts.append(hop(passed, "ctx", far, both))
            return w.parts[-1]

        return w.send[start:stop], go

    weights = SimpleNamespace(expand_came=[], contract_came=[])
    half_depth = depth // 2

    def expand_far(start, stop):
        def go(passed):
            weights.expand_came.append(hop(passed, "ctx", far, both))
            return weights.expand_came[-1]

        return own_expand[start:stop], go

    def packed_far(passed):
        weights.packed_came = hop(passed, "ctx", far, both)
        return weights.packed_came

    def packed_near(passed):
        weights.packed = blocks_of(packed, passed)
        return weights.packed[1:]

    def expand_near(passed):
        weights.expand = blocks_of(own_expand, passed)
        return weights.expand[1:]

    def contract_far(start, stop):
        def go(passed):
            weights.contract_came.append(hop(passed, "ctx", far, both))
            return weights.contract_came[-1]

        return own_contract[start:stop], go

    def contract_near(passed):
        weights.contract = blocks_of(own_contract, passed)
        return weights.contract[1:]

    def early_hops(passed):
        weights.early = [passed] + [hop(passed, "tp", j, both) for j in lane_offsets[1:]]
        return weights.early[1:]

    due[0] = [expand_far(0, half_depth)[1](own_expand[:half_depth])]
    slot([(packed, packed_far), expand_far(half_depth, depth), (early, early_hops)])
    early_pieces = weights.early
    cuts = [0, hidden // 4, 11 * hidden // 16, hidden]
    expand_came = jnp.concatenate(weights.expand_came, axis=0)
    slot(
        [
            (weights.packed_came, packed_near),
            (expand_came, expand_near),
            contract_far(cuts[0], cuts[1]),
        ]
    )
    packed = weights.packed
    small_full = jnp.concatenate(
        [piece[depth : depth + 4, :depth] for piece in packed], axis=1
    ).astype(f32)
    gains, biases = small_full[:2], small_full[2:]
    slot(
        [contract_far(cuts[1], cuts[2])],
        [lambda m=m: run_project(0, m) for m in range(micros)],
    )
    a, b = kept
    slot(
        [pair_far(0, 0), contract_far(cuts[2], cuts[3])],
        [lambda m=m: run_expand(m) for m in range(micros)],
    )
    contract_came = jnp.concatenate(weights.contract_came, axis=0)
    slot([(contract_came, contract_near), pair_near(0, 0)])
    contract = weights.contract
    slot([pair_far(0, 1)], [lambda: run_attend(0), lambda: run_branch(0)])
    slot([sum_near(0, a[0]), pair_near(0, 1)])
    slot([sum_far(0, a[0]), pair_far(0, 2)], [lambda: run_attend(1), lambda: run_branch(1)])
    slot([hand_one(0, 0), sum_near(0, a[1]), pair_near(0, 2)])
    slot(
        [rows_far(1, 0), sum_far(0, a[1])], [lambda: run_attend(2), lambda: run_branch(2)]
    )
    slot([rows_near(1, 0), hand_one(0, 1), sum_near(0, a[2])])
    slot([rows_far(1, 1), sum_far(0, a[2])], [lambda: run_project(1, 0)])
    slot(
        [pair_far(1, 0), rows_near(1, 1), hand_one(0, 2)], [lambda: run_hidden_both(0)]
    )
    slot([pair_near(1, 0), rows_far(1, 2)], [lambda: run_project(1, 1)])
    slot(
        [pair_far(1, 1), rows_near(1, 2)],
        [lambda: run_attend_both(0), lambda: run_hidden_both(1)],
    )
    slot([pair_grad_near(1, 0), pair_near(1, 1)], [lambda: run_project(1, 2)])
    slot(
        [pair_grad_far(1, 0), pair_far(1, 2)],
        [lambda: run_attend_both(1), lambda: run_hidden_both(2)],
    )
    slot([pair_grad_near(1, 1), pair_near(1, 2)], [lambda: run_project_back(1, 0)])
    slot([sum_near(1, b[0]), pair_grad_far(1, 1)], [lambda: run_attend_both(2)])
    slot([sum_far(1, b[0]), pair_grad_near(1, 2)], [lambda: run_project_back(1, 1)])
    slot([hand_one(1, 0), sum_near(1, b[1]), pair_grad_far(1, 2)])
    slot([sum_far(1, b[1]), rows_far(0, 0)], [lambda: run_project_back(1, 2)])
    slot([sum_near(1, b[2]), hand_one(1, 1), rows_near(0, 0)])
    slot([sum_far(1, b[2]), rows_far(0, 1)], [lambda: run_attend_back(0)])
    slot(
        [hand_one(1, 2), rows_near(0, 1), pair_grad_near(0, 0)],
        [lambda: run_hidden_back(0)],
    )
    slot([rows_far(0, 2), pair_grad_far(0, 0)], [lambda: run_attend_back(1)])
    slot(
        [rows_near(0, 2), pair_grad_near(0, 1)],
        [lambda: run_hidden_back(1), lambda: run_project_back(0, 0)],
    )
    last = micros - 1

    def run_branch_sums():
        run_sums(
            branch_sums,
            [[of("active", s), of("attended", s)] for s in both],
            [
                [of("upstream", 0, last) + [piece[0] for piece in a[last].row_pieces]],
                [of("upstream", 1)],
            ],
            False,
        )

    def run_expand_sums():
        run_sums(
            expand_sums,
            [[of("second", s)] for s in both],
            [[of("hidden", s)] for s in both],
            True,
        )

    def run_triple_sums():
        run_sums(
            triple_sums,
            [[of("first", s)] for s in both],
            [[of("stacked", s)] for s in both],
            True,
        )

    finals = SimpleNamespace()

    def run_final_branch():
        blocks = branch_out(
            order, flags[1], [(k.active, k.attended) for k in b], contract, packed
        )
        finals.keep = jnp.stack(blocks[0::2])
        finals.send = jnp.stack(blocks[1::2])

    def last_near(w, s):
        return w.send, lambda passed: fold_hops(w, passed, "tp", 1, (s,))

    def last_far(w, s):
        def go(passed):
            w.came = hop(passed, "tp", lanes // 2, (s,))
            return w.came

        return w.send, go

    slot([pair_grad_far(0, 1)], [run_branch_sums])
    slot(
        [wide_near(branch_sums)], [lambda: run_attend_back(2), lambda: run_project_back(0, 1)]
    )
    slot([], [lambda: run_fold(branch_sums)])
    cut = [0, hidden // 2, hidden, hidden + across_units]
    slot(
        [wide_far(branch_sums, cut[0], cut[1]), pair_grad_both(0, 2)],
        [lambda: run_hidden_back(2)],
    )
    slot(
        [wide_far(branch_sums, cut[1], cut[2])],
        [lambda: run_project_back(0, 2), run_triple_sums],
    )
    outs = SimpleNamespace(
        keep=jnp.stack([k.blocks[0] for k in a]), send=jnp.stack([k.blocks[1] for k in a])
    )

    def side_of(mades):
        return sum(
            jnp.concatenate([k.side_first, k.side_second], axis=0) for k in mades
        )

    side = SimpleNamespace(all=jnp.where(first_section, side_of(a), side_of(b)))

    def side_ctx(passed):
        step = 1
        while step < spans:
            middle = passed.shape[1] // 2
            came = hop(passed[:, middle:], "ctx", step, both)
            passed = passed[:, :middle] + came
            step *= 2
        side.all = passed
        return came

    def side_near(passed):
        step = 1
        while 2 * step < lanes:
            came = hop(passed, "tp", step, both)
            passed = passed + came
            step *= 2
        side.all = passed
        return came

    def side_far(passed):
        came = hop(passed, "tp", lanes // 2, both)
        side.all = passed + came
        return came

    def held_back(w, j):
        def go(passed):
            w.parts[j] = passed
            return []

        return w.parts[j], go

    def wide_total(keep, parts):
        came = jnp.concatenate(parts, axis=0) if len(parts) > 1 else parts[0]
        return keep.astype(f32) + came.astype(f32)

    slot(
        [
            wide_near(triple_sums),
            wide_far(branch_sums, cut[2], cut[3]),
            (side.all, side_ctx),
        ],
        [run_expand_sums, run_final_branch],
    )
    slot([], [lambda: run_fold(triple_sums)])
    slot(
        [
            wide_far(triple_sums, 0, depth),
            wide_near(expand_sums),
            last_near(outs, 0),
            last_near(finals, 1),
            (side.all, side_near),
        ]
    )
    slot([], [lambda: run_fold(expand_sums)])
    slot(
        [
            wide_far(expand_sums, 0, depth),
            last_far(outs, 0),
            last_far(finals, 1),
            (side.all, side_far),
            held_back(triple_sums, 0),
            held_back(branch_sums, 2),
        ]
    )
    triple_grads = wide_total(triple_sums.keep, triple_sums.parts)
    triple_grads = triple_grads.reshape(triple_weight.shape)
    branch_grads = wide_total(branch_sums.keep, branch_sums.parts)
    contract_grads, output_grads = branch_grads[:hidden], branch_grads[hidden:]
    expand_grads = wide_total(expand_sums.keep, expand_sums.parts)
    layer_outputs = jnp.stack(
        [
            jnp.where(
                first_section,
                kept[0][m].given,
                (
                    b[m].rows.astype(f32)
                    + finals.keep[m].astype(f32)
                    + finals.came[m].astype(f32)
                ).astype(bf16),
            )
            for m in range(micros)
        ]
    )
    own_rows = jnp.stack(of("rows", 0))
    entry_grads = jnp.where(
        first_section,
        norm_back(own_rows, outs.keep.astype(f32) + outs.came.astype(f32), inputs),
        jnp.stack(of("given", 1)),
    )
    gain_grads = jnp.stack([side.all[0], side.all[2]])
    bias_grads = jnp.stack([side.all[1], side.all[3]])
    return (
        xor_blocks(layer_outputs, span, spans, inverse=True)[None],
        xor_blocks(entry_grads, span, spans, inverse=True)[None],
        triple_grads,
        output_grads.reshape(output_weight.shape),
        expand_grads[None],
        contract_grads[None],
        gain_grads[None],
        bias_grads[None],
    )


def solution(mesh):
    return jax.shard_map(
        shards,
        mesh=mesh,
        in_specs=(
            P(None, ("ctx", "tp"), None),
            P(None, ("ctx", "tp"), None),
            P("pipe", "ctx", "tp", None, None),
            P("pipe", "tp", None, "ctx"),
            P("pipe", "ctx", "tp"),
            P("pipe", "tp", "ctx"),
            P("pipe", None, "ctx"),
            P("pipe", None, "ctx"),
        ),
        out_specs=(
            P("pipe", None, ("ctx", "tp"), None),
            P("pipe", None, ("ctx", "tp"), None),
            P("pipe", "ctx", "tp", None, None),
            P("pipe", "tp", None, "ctx"),
            P("pipe", "ctx", "tp"),
            P("pipe", "tp", "ctx"),
            P("pipe", None, "ctx"),
            P("pipe", None, "ctx"),
        ),
        check_vma=False,
    )
```

```python
import functools
import math
from types import SimpleNamespace

import jax
import jax.numpy as jnp
from jax import lax
from jax.experimental import pallas as pl
from jax.experimental.pallas import tpu as pltpu
from jax.sharding import PartitionSpec as P

ROT = 64
LANES = 128
epsilon = 1e-05
masked_score = -1e30
f32 = jnp.float32
bf16 = jnp.bfloat16
mebibyte = 1024 * 1024
half_root = 0.7071067811865476
bell = 0.3989422804014327


def dot(a, b, dims):
    return lax.dot_general(a, b, (dims, ((), ())), preferred_element_type=f32)


def plain(a, b):
    return dot(a, b, ((1,), (0,)))


def turned(a, b):
    return dot(a, b, ((1,), (1,)))


def doubling(count):
    order, step = [0], count // 2
    while step:
        order += [k ^ step for k in order]
        step //= 2
    return order


def xor_blocks(values, index, count, inverse=False):
    width = values.shape[-1] // count
    order = doubling(count)

    def taken(places):
        return jnp.concatenate(
            [values[..., k * width : (k + 1) * width] for k in places], axis=-1
        )

    if inverse:
        values = taken([order.index(k) for k in range(count)])
    step = 1
    while step < count:
        swapped = taken([k ^ step for k in range(count)])
        values = jnp.where((index & step) != 0, swapped, values)
        step *= 2
    return values if inverse else taken(order)


def rope_tables(positions):
    half = ROT // 2
    frequency = 10000.0 ** (-jnp.arange(0, ROT, 2, dtype=f32) / ROT)
    angles = positions.astype(f32)[:, None] * frequency[None, :]
    cosine, sine = jnp.cos(angles), jnp.sin(angles)
    count = positions.shape[0]
    rest = jnp.zeros((count, LANES - ROT), f32)
    none = jnp.zeros((count, half), f32)
    return jnp.stack(
        [
            jnp.concatenate([cosine, cosine, rest + 1.0], axis=1),
            jnp.concatenate([-sine, none, rest], axis=1),
            jnp.concatenate([none, sine, rest], axis=1),
        ]
    )


def turn(values, tables, sign):
    half = ROT // 2
    part = values[:, :LANES]
    moved = (
        pltpu.roll(part, LANES - half, 1) * tables[1] + pltpu.roll(part, half, 1) * tables[2]
    )
    part = part * tables[0] + (moved if sign > 0 else -moved)
    return jnp.concatenate([part, values[:, LANES:]], axis=1)


def normalize(values):
    center = values - jnp.mean(values, axis=-1, keepdims=True)
    inverse = lax.rsqrt(jnp.mean(center * center, axis=-1, keepdims=True) + epsilon)
    return (center * inverse, inverse)


def whole(array):
    zeros = (0,) * array.ndim
    return pl.BlockSpec(array.shape, lambda *_: zeros)


def at(block, place):
    return pl.BlockSpec(block, lambda *_: place)


kept_out = pl.BlockSpec(memory_space=pl.ANY)


def shape(dims, dtype=bf16):
    return jax.ShapeDtypeStruct(dims, dtype)


class Order:
    def __init__(self):
        self.last = []

    def follow(self, results):
        self.last = [min(results, key=lambda array: array.size * array.dtype.itemsize)]

    def also(self, array):
        self.last = self.last + [array]


took = dict(
    project=7,
    expand=8,
    attend=5,
    branch=8,
    hidden_both=14,
    attend_both=11,
    attend_back=8,
    hidden_back=13,
    project_back=8,
    weight_sums=16,
    fold=7,
)
peak = 1.15e9


def run(order, flags, kernel, ins, outs, scratch, name, grid=(1,), work=0):
    taken = len(ins)
    ins = [(flags, pl.BlockSpec(memory_space=pltpu.SMEM))] + list(ins)
    ins += [(array, kept_out) for array in order.last]
    arrays = [array for array, _ in ins]
    once = grid == (1,)

    def sized(spec, dtype):
        if spec.block_shape is None:
            return spec, 0
        size = math.prod(spec.block_shape) * jnp.dtype(dtype).itemsize
        if not once:
            return spec, 2 * size
        single = pl.BlockSpec(
            spec.block_shape, spec.index_map, pipeline_mode=pl.Buffered(1)
        )
        return single, size

    in_specs = [sized(spec, array.dtype) for array, spec in ins]
    out_specs = [sized(spec, struct.dtype) for struct, spec in outs]
    held = sum(size for _, size in in_specs + out_specs)
    for buffer in scratch:
        if buffer.memory_space == pltpu.VMEM:
            held += math.prod(buffer.shape) * jnp.dtype(buffer.dtype).itemsize

    def body(flag_ref, *refs):
        @pl.when(flag_ref[0] == 1)
        def _():
            kernel(flag_ref, *refs[:taken], *refs[len(ins) - 1 :])

    results = pl.pallas_call(
        body,
        grid=grid,
        in_specs=[spec for spec, _ in in_specs],
        out_specs=[spec for spec, _ in out_specs],
        out_shape=[struct for struct, _ in outs],
        scratch_shapes=scratch,
        compiler_params=pltpu.CompilerParams(
            vmem_limit_bytes=int(held + (work + 4) * mebibyte)
        ),
        cost_estimate=pl.CostEstimate(
            flops=int(took[name] * peak), bytes_accessed=0, transcendentals=0
        ),
        name=name,
    )(*arrays)
    order.follow(results)
    return results


def fence(through, waits):
    count = len(through)

    def kernel(*refs):
        pass

    return pl.pallas_call(
        kernel,
        in_specs=[kept_out] * (count + len(waits)),
        out_specs=[kept_out] * count,
        out_shape=[shape(array.shape, array.dtype) for array in through],
        input_output_aliases={j: j for j in range(count)},
        compiler_params=pltpu.CompilerParams(vmem_limit_bytes=mebibyte),
        cost_estimate=pl.CostEstimate(flops=1, bytes_accessed=1, transcendentals=0),
        name="fence",
    )(*through, *waits)


def full_out(dims, dtype=bf16):
    zeros = (0,) * len(dims)
    return (shape(dims, dtype), pl.BlockSpec(dims, lambda *_: zeros))


def copies(sources, targets, sems):
    started = []
    for source, target, sem in zip(sources, targets, sems):
        copy = pltpu.make_async_copy(source, target, sem)
        copy.start()
        started.append(copy)
    return started


def project(order, flags, pieces, at_piece, gains, biases, tables, weights, heads, head_dim):
    count, width = 1, pieces[0].shape[2]
    span_rows = sum(piece.shape[1] for piece in pieces)
    rows = count * span_rows
    chunk = pieces[0].shape[1]
    spans = len(weights)
    depth = width // spans
    wide = 3 * head_dim
    columns = heads * wide

    def kernel(flag_ref, *refs):
        piece_refs = refs[: len(pieces)]
        gain_ref, bias_ref, table_ref = refs[len(pieces) : len(pieces) + 3]
        weight_refs = refs[len(pieces) + 3 : len(pieces) + 3 + spans]
        first, second, normal, queries, pair, held, sems = refs[len(pieces) + 3 + spans :]
        started = []
        for h in range(heads):
            started.append(
                copies(
                    [w.at[:depth, h * wide : (h + 1) * wide] for w in weight_refs],
                    [held.at[h, k * depth : (k + 1) * depth] for k in range(spans)],
                    [sems.at[h, k] for k in range(spans)],
                )
            )
        start = 0
        for piece_ref in piece_refs:
            chunks = piece_ref.shape[1] // chunk

            def one(i, _, piece_ref=piece_ref, start=start, chunks=chunks):
                m, c = i // chunks, i % chunks
                values = piece_ref[m, pl.ds(pl.multiple_of(c * chunk, chunk), chunk), :]
                normed, _ = normalize(values.astype(f32))
                to = pl.ds(
                    pl.multiple_of(m * span_rows + start + c * chunk, chunk), chunk
                )
                normal[to, :] = normed.astype(bf16)
                first[to, :] = (normed * gain_ref[0:1] + bias_ref[0:1]).astype(bf16)
                second[to, :] = (normed * gain_ref[1:2] + bias_ref[1:2]).astype(bf16)
                return 0

            lax.fori_loop(0, count * chunks, one, 0)
            start += piece_ref.shape[1]
        for h in range(heads):
            for copy in started[h]:
                copy.wait()

            def two(m, _, h=h):
                to = pl.ds(pl.multiple_of(m * span_rows, span_rows), span_rows)
                made = plain(first[to, :], held[h])
                queries[h, to, :] = turn(made[:, :head_dim], table_ref, 1).astype(bf16)
                pair[0, h, to, :] = turn(
                    made[:, head_dim : 2 * head_dim], table_ref, 1
                ).astype(bf16)
                pair[1, h, to, :] = made[:, 2 * head_dim :].astype(bf16)
                return 0

            lax.fori_loop(0, count, two, 0)

    ins = [(piece, at((1,) + piece.shape[1:], (at_piece, 0, 0))) for piece in pieces]
    ins += [(array, whole(array)) for array in (gains, biases, tables)]
    ins += [(w, kept_out) for w in weights]
    outs = [full_out((rows, width))] * 3 + [
        full_out((heads, rows, head_dim)),
        full_out((2, heads, rows, head_dim)),
    ]
    scratch = [
        pltpu.VMEM((heads, width, wide), bf16),
        pltpu.SemaphoreType.DMA((heads, spans)),
    ]
    return run(order, flags, kernel, ins, outs, scratch, "project")


def expand_up(order, flags, second, weights, span_rows):
    rows, width = second.shape
    depth, hidden = weights[0].shape
    spans = len(weights)
    tile = min(512, hidden)
    tiles = hidden // tile

    def kernel(flag_ref, *refs):
        second_ref, weight_refs = refs[0], refs[1 : 1 + spans]
        active, slope, held, sems = refs[1 + spans :]
        started = []
        for t in range(tiles):
            started.append(
                copies(
                    [w.at[:, t * tile : (t + 1) * tile] for w in weight_refs],
                    [held.at[t, k * depth : (k + 1) * depth] for k in range(spans)],
                    [sems.at[t, k] for k in range(spans)],
                )
            )
        for t in range(tiles):
            for copy in started[t]:
                copy.wait()

            def one(m, _, t=t):
                to = pl.ds(pl.multiple_of(m * span_rows, span_rows), span_rows)
                pre = plain(second_ref[to, :], held[t])
                risen = 0.5 * (1.0 + lax.erf(pre * half_root))
                columns = slice(t * tile, (t + 1) * tile)
                active[to, columns] = (pre * risen).astype(bf16)
                slope[to, columns] = (
                    risen + pre * jnp.exp(-0.5 * pre * pre) * bell
                ).astype(bf16)
                return 0

            lax.fori_loop(0, rows // span_rows, one, 0)

    ins = [(second, whole(second))] + [(w, kept_out) for w in weights]
    outs = [full_out((rows, hidden))] * 2
    scratch = [
        pltpu.VMEM((tiles, width, tile), bf16),
        pltpu.SemaphoreType.DMA((tiles, spans)),
    ]
    return run(order, flags, kernel, ins, outs, scratch, "expand")


def spread(refs):
    return [ref.at[j] for ref in refs for j in range(ref.shape[0])]


def attention(here, pairs, head, row_ref, key_ref, scale):
    scores = []
    for k, pair in enumerate(pairs):
        raw = turned(here, pair[0, head]) * scale
        scores.append(jnp.where(key_ref[k] <= row_ref[...], raw, masked_score))
    top = functools.reduce(
        jnp.maximum, [jnp.max(part, axis=1, keepdims=True) for part in scores]
    )
    scores = [jnp.exp(part - top) for part in scores]
    inverse = 1.0 / sum(jnp.sum(part, axis=1, keepdims=True) for part in scores)
    return [part * inverse for part in scores]


def attend(order, flags, queries, pairs, positions, key_positions, scale):
    heads, rows, head_dim = queries.shape
    spans = sum(pair.shape[0] for pair in pairs)

    def kernel(flag_ref, query_ref, *refs):
        views, refs = spread(refs[: len(pairs)]), refs[len(pairs) :]
        row_ref, key_ref, attended, probs = refs
        for h in range(heads):
            parts = attention(query_ref[h], views, h, row_ref, key_ref, scale)
            summed = None
            for k in range(spans):
                part = parts[k].astype(bf16)
                probs[k, h] = part
                term = plain(part, views[k][1, h])
                summed = term if summed is None else summed + term
            attended[:, h * head_dim : (h + 1) * head_dim] = summed.astype(bf16)

    ins = [
        (array, whole(array)) for array in (queries, *pairs, positions, key_positions)
    ]
    outs = [full_out((rows, heads * head_dim)), full_out((spans, heads, rows, rows))]
    work = spans * rows * rows * 4 * heads * 4 / mebibyte
    return run(order, flags, kernel, ins, outs, [], "attend", work=work)


def attention_grads(grad, here, parts, views, head, keep, send, scale):
    half = keep.shape[0]
    grad_probs = [turned(grad, view[1, head]) for view in views]
    delta = sum(
        jnp.sum(part.astype(f32) * slope, axis=1, keepdims=True)
        for part, slope in zip(parts, grad_probs)
    )
    query_grad = None
    for k, view in enumerate(views):
        slopes = (parts[k].astype(f32) * (grad_probs[k] - delta)).astype(bf16)
        term = plain(slopes, view[0, head])
        query_grad = term if query_grad is None else query_grad + term
        side = keep if k < half else send
        side[k % half, 0, head] = (dot(slopes, here, ((0,), (0,))) * scale).astype(bf16)
        side[k % half, 1, head] = dot(parts[k].astype(bf16), grad, ((0,), (0,))).astype(bf16)
    return query_grad * scale


def attend_both(
    order, flags, rows_in, packed, queries, pairs, positions, key_positions, tables, scale
):
    heads, rows, head_dim = queries.shape
    width = rows_in.shape[1]
    spans = len(packed)
    across, depth = heads * head_dim, width // spans
    half = spans // 2

    def kernel(flag_ref, rows_ref, *refs):
        packed_refs, refs = refs[:spans], refs[spans:]
        query_ref, refs = refs[0], refs[1:]
        views, refs = spread(refs[: len(pairs)]), refs[len(pairs) :]
        row_ref, key_ref, table_ref, attended, turned_back, keep, send, held, sems = refs
        started = copies(
            [w.at[:across, 3 * across : 3 * across + depth] for w in packed_refs],
            [held.at[:, k * depth : (k + 1) * depth] for k in range(spans)],
            [sems.at[k] for k in range(spans)],
        )
        all_parts = []
        for h in range(heads):
            parts = attention(query_ref[h], views, h, row_ref, key_ref, scale)
            summed = None
            for k in range(spans):
                term = plain(parts[k].astype(bf16), views[k][1, h])
                summed = term if summed is None else summed + term
            attended[:, h * head_dim : (h + 1) * head_dim] = summed.astype(bf16)
            all_parts.append(parts)
        for copy in started:
            copy.wait()
        grads = turned(rows_ref[...], held[...]).astype(bf16)
        for h in range(heads):
            made = attention_grads(
                grads[:, h * head_dim : (h + 1) * head_dim],
                query_ref[h],
                all_parts[h],
                views,
                h,
                keep,
                send,
                scale,
            )
            turned_back[h] = turn(made, table_ref, -1).astype(bf16)

    ins = [(rows_in, whole(rows_in))] + [(w, kept_out) for w in packed]
    ins += [
        (array, whole(array)) for array in (queries, *pairs, positions, key_positions, tables)
    ]
    outs = [full_out((rows, across)), full_out((heads, rows, head_dim))]
    outs += [full_out((half, 2, heads, rows, head_dim))] * 2
    scratch = [pltpu.VMEM((across, width), bf16), pltpu.SemaphoreType.DMA((spans,))]
    work = spans * rows * rows * 4 * (heads + 4) / mebibyte
    return run(order, flags, kernel, ins, outs, scratch, "attend_both", work=work)


def hidden_both(order, flags, second, pieces, at_piece, expand, contract, normal, gains):
    rows, width = second.shape
    hidden, depth = contract[0].shape
    spans = len(contract)
    tile = min(512, hidden)
    tiles = hidden // tile

    def kernel(flag_ref, second_ref, *refs):
        piece_refs, refs = refs[: len(pieces)], refs[len(pieces) :]
        expand_refs, refs = refs[:spans], refs[spans:]
        contract_refs, refs = refs[:spans], refs[spans:]
        normal_ref, gain_ref, rows_out, active, grads, part, side, *refs = refs
        held_up, held_down, sems_up, sems_down = refs
        started = []
        for t in range(tiles):
            block = slice(t * tile, (t + 1) * tile)
            places = [slice(k * depth, (k + 1) * depth) for k in range(spans)]
            up = copies(
                [w.at[:, block] for w in expand_refs],
                [held_up.at[place, block] for place in places],
                [sems_up.at[t, k] for k in range(spans)],
            )
            down = copies(
                [w.at[block, :] for w in contract_refs],
                [held_down.at[block, place] for place in places],
                [sems_down.at[t, k] for k in range(spans)],
            )
            started.append((up, down))
        start = 0
        for piece_ref in piece_refs:
            size = piece_ref.shape[1]
            rows_out[start : start + size, :] = piece_ref[0]
            start += size
        for t in range(tiles):
            block = slice(t * tile, (t + 1) * tile)
            for copy in started[t][0] + started[t][1]:
                copy.wait()
            pre = plain(second_ref[...], held_up[:, block])
            risen = 0.5 * (1.0 + lax.erf(pre * half_root))
            active[:, block] = (pre * risen).astype(bf16)
            slope = risen + pre * jnp.exp(-0.5 * pre * pre) * bell
            grads[:, block] = (turned(rows_out[...], held_down[block, :]) * slope).astype(bf16)
        for k in range(spans):
            place = slice(k * depth, (k + 1) * depth)
            made = turned(grads[...], held_up[place, :])
            side[0:1, place] = jnp.sum(
                made * normal_ref[:, place].astype(f32), axis=0, keepdims=True
            )
            side[1:2, place] = jnp.sum(made, axis=0, keepdims=True)
            part[:, place] = made * gain_ref[1:2, place]

    ins = [(second, whole(second))]
    ins += [(piece, at((1,) + piece.shape[1:], (at_piece, 0, 0))) for piece in pieces]
    ins += [(w, kept_out) for w in expand] + [(w, kept_out) for w in contract]
    ins += [(normal, whole(normal)), (gains, whole(gains))]
    outs = [
        full_out((rows, width)),
        full_out((rows, hidden)),
        full_out((rows, hidden)),
        full_out((rows, width), f32),
        full_out((2, width), f32),
    ]
    scratch = [
        pltpu.VMEM((width, hidden), bf16),
        pltpu.VMEM((hidden, width), bf16),
        pltpu.SemaphoreType.DMA((tiles, spans)),
        pltpu.SemaphoreType.DMA((tiles, spans)),
    ]
    return run(order, flags, kernel, ins, outs, scratch, "hidden_both")


def branch_out(order, flags, groups, contract, packed):
    hidden, depth = contract[0].shape
    across = groups[0][1].shape[1]
    spans = len(contract)
    width = depth * spans
    span_rows = groups[0][0].shape[0]
    block = span_rows // 2
    count = len(groups)

    def kernel(flag_ref, *refs):
        group_refs, refs = refs[: 2 * count], refs[2 * count :]
        contract_refs, packed_refs = refs[:spans], refs[spans : 2 * spans]
        blocks, refs = refs[2 * spans : 2 * (spans + count)], refs[2 * (spans + count) :]
        held, held_out, sems = refs
        outputs = [w.at[:across, 3 * across : 3 * across + depth] for w in packed_refs]
        started = copies(
            [ref for k in range(spans) for ref in (outputs[k], contract_refs[k])],
            [ref for k in range(spans) for ref in (held_out.at[k], held.at[k])],
            [sems.at[j] for j in range(2 * spans)],
        )
        for k in range(spans):
            started[2 * k].wait()
            started[2 * k + 1].wait()
            columns = slice(k * depth, (k + 1) * depth)
            for c in range(count):
                made = plain(group_refs[2 * c + 1][...], held_out[k])
                made = made + plain(group_refs[2 * c][...], held[k])
                blocks[2 * c][:, columns] = made[:block].astype(bf16)
                blocks[2 * c + 1][:, columns] = made[block:].astype(bf16)

    ins = []
    for active, attended in groups:
        ins += [(active, whole(active)), (attended, whole(attended))]
    ins += [(w, kept_out) for w in contract] + [(w, kept_out) for w in packed]
    outs = [full_out((block, width))] * (2 * count)
    scratch = [
        pltpu.VMEM((spans, hidden, depth), bf16),
        pltpu.VMEM((spans, across, depth), bf16),
        pltpu.SemaphoreType.DMA((2 * spans,)),
    ]
    return run(order, flags, kernel, ins, outs, scratch, "branch")


def attend_back(order, flags, pieces, packed, queries, pairs, probs, tables, scale):
    rows = sum(piece.shape[1] for piece in pieces)
    width = pieces[0].shape[2]
    heads, _, head_dim = queries.shape
    spans = len(packed)
    across, depth = heads * head_dim, width // spans
    half = spans // 2

    def kernel(flag_ref, *refs):
        piece_refs, refs = refs[: len(pieces)], refs[len(pieces) :]
        packed_refs, refs = refs[:spans], refs[spans:]
        query_ref, refs = refs[0], refs[1:]
        views, refs = spread(refs[: len(pairs)]), refs[len(pairs) :]
        prob_ref, table_ref, rows_out, turned_back, keep, send, held, sems = refs
        started = copies(
            [w.at[:across, 3 * across : 3 * across + depth] for w in packed_refs],
            [held.at[:, k * depth : (k + 1) * depth] for k in range(spans)],
            [sems.at[k] for k in range(spans)],
        )
        start = 0
        for piece_ref in piece_refs:
            size = piece_ref.shape[1]
            rows_out[start : start + size, :] = piece_ref[0]
            start += size
        for copy in started:
            copy.wait()
        grads = turned(rows_out[...], held[...]).astype(bf16)
        for h in range(heads):
            made = attention_grads(
                grads[:, h * head_dim : (h + 1) * head_dim],
                query_ref[h],
                [prob_ref[k, h] for k in range(spans)],
                views,
                h,
                keep,
                send,
                scale,
            )
            turned_back[h] = turn(made, table_ref, -1).astype(bf16)

    ins = [(piece, whole(piece)) for piece in pieces] + [(w, kept_out) for w in packed]
    ins += [(array, whole(array)) for array in (queries, *pairs, probs, tables)]
    outs = [full_out((rows, width)), full_out((heads, rows, head_dim))]
    outs += [full_out((half, 2, heads, rows, head_dim))] * 2
    scratch = [pltpu.VMEM((across, width), bf16), pltpu.SemaphoreType.DMA((spans,))]
    work = spans * rows * rows * 4 * 4 / mebibyte
    return run(order, flags, kernel, ins, outs, scratch, "attend_back", work=work)


def hidden_back(order, flags, upstream, contract, expand, slope, normal, gains):
    span_rows, width = upstream.shape
    hidden, depth = contract[0].shape
    spans = len(contract)
    tile = min(512, hidden)
    tiles = hidden // tile

    def kernel(flag_ref, *refs):
        upstream_ref, refs = refs[0], refs[1:]
        contract_refs, refs = refs[:spans], refs[spans:]
        expand_refs, refs = refs[:spans], refs[spans:]
        slope_ref, normal_ref, gain_ref, grads, part, side, held, held_up, sems, sems_up = refs
        started = [
            copies(
                [w.at[t * tile : (t + 1) * tile, :] for w in contract_refs],
                [held.at[t, :, k * depth : (k + 1) * depth] for k in range(spans)],
                [sems.at[t, k] for k in range(spans)],
            )
            for t in range(tiles)
        ]
        started_up = copies(
            expand_refs, [held_up.at[k] for k in range(spans)], [sems_up.at[k] for k in range(spans)]
        )
        for t in range(tiles):
            for copy in started[t]:
                copy.wait()
            columns = slice(t * tile, (t + 1) * tile)
            grads[:, columns] = (
                turned(upstream_ref[...], held[t]) * slope_ref[:, columns].astype(f32)
            ).astype(bf16)
        for k in range(spans):
            started_up[k].wait()
            made = turned(grads[...], held_up[k])
            columns = slice(k * depth, (k + 1) * depth)
            side[0:1, columns] = jnp.sum(
                made * normal_ref[:, columns].astype(f32), axis=0, keepdims=True
            )
            side[1:2, columns] = jnp.sum(made, axis=0, keepdims=True)
            part[:, columns] = made * gain_ref[1:2, columns]

    ins = [(upstream, whole(upstream))]
    ins += [(w, kept_out) for w in contract] + [(w, kept_out) for w in expand]
    ins += [
        (slope, whole(slope)),
        (normal, whole(normal)),
        (gains, whole(gains)),
    ]
    outs = [
        full_out((span_rows, hidden)),
        full_out((span_rows, width), f32),
        full_out((2, width), f32),
    ]
    scratch = [
        pltpu.VMEM((tiles, tile, width), bf16),
        pltpu.VMEM((spans, depth, hidden), bf16),
        pltpu.SemaphoreType.DMA((tiles, spans)),
        pltpu.SemaphoreType.DMA((spans,)),
    ]
    return run(order, flags, kernel, ins, outs, scratch, "hidden_back")


def project_back(
    order, flags, turned_back, own, came, weights, part, normal, gains, tables
):
    heads, span_rows, head_dim = turned_back.shape
    spans = len(weights)
    width = part.shape[1]
    depth, columns = width // spans, 3 * heads * head_dim
    block = span_rows // 2

    def kernel(flag_ref, *refs):
        query_ref, own_ref, came_ref, refs = refs[0], refs[1], refs[2], refs[3:]
        weight_refs, refs = refs[:spans], refs[spans:]
        part_ref, normal_ref, gain_ref, table_ref, grads, side, *refs = refs
        low, high, held, sems = refs
        started = copies(
            [w.at[:depth, :columns] for w in weight_refs],
            [held.at[k] for k in range(spans)],
            [sems.at[k] for k in range(spans)],
        )
        for h in range(heads):
            at_column = h * 3 * head_dim
            keys = own_ref[0, h].astype(f32) + came_ref[0, h].astype(f32)
            values = own_ref[1, h].astype(f32) + came_ref[1, h].astype(f32)
            grads[:, at_column : at_column + head_dim] = query_ref[h]
            grads[:, at_column + head_dim : at_column + 2 * head_dim] = turn(
                keys, table_ref, -1
            ).astype(bf16)
            grads[:, at_column + 2 * head_dim : at_column + 3 * head_dim] = values.astype(bf16)
        for k in range(spans):
            started[k].wait()
            made = turned(grads[...], held[k])
            span_columns = slice(k * depth, (k + 1) * depth)
            side[0:1, span_columns] = jnp.sum(
                made * normal_ref[:, span_columns].astype(f32), axis=0, keepdims=True
            )
            side[1:2, span_columns] = jnp.sum(made, axis=0, keepdims=True)
            both = (made * gain_ref[0:1, span_columns] + part_ref[:, span_columns]).astype(bf16)
            low[:, span_columns] = both[:block]
            high[:, span_columns] = both[block:]

    ins = [(array, whole(array)) for array in (turned_back, own, came)]
    ins += [(w, kept_out) for w in weights]
    ins += [(part, whole(part)), (normal, whole(normal))]
    ins += [(gains, whole(gains)), (tables, whole(tables))]
    outs = [full_out((span_rows, columns)), full_out((2, width), f32)]
    outs += [full_out((block, width))] * 2
    scratch = [pltpu.VMEM((spans, depth, columns), bf16), pltpu.SemaphoreType.DMA((spans,))]
    return run(order, flags, kernel, ins, outs, scratch, "project_back")


def weight_sums(order, flags, lefts, rights, by_rows, spans):
    rows = sum(piece.shape[0] for piece in lefts[0][0])
    left_width = sum(group[0].shape[1] for group in lefts[0])
    right_width = sum(group[0].shape[1] for group in rights[0])
    if by_rows:
        tile = left_width // spans
        steps, block = spans // 2, (tile, right_width)
    else:
        tile = min(512, left_width)
        while left_width % tile:
            tile //= 2
        steps, block = left_width // tile, (tile, right_width // 2)
    chunk = min(1024, block[1])
    while right_width % chunk:
        chunk //= 2
    pieces = [
        [piece for groups in (lefts[s], rights[s]) for group in groups for piece in group]
        for s in (0, 1)
    ]
    most = max(len(p) for p in pieces)

    def kernel(flag_ref, *refs):
        piece_refs = (refs[: len(pieces[0])], refs[len(pieces[0]) : len(pieces[0]) + len(pieces[1])])
        keep, send, left, right, flipped, sems = refs[len(pieces[0]) + len(pieces[1]) :]
        g = pl.program_id(0)
        for s in (0, 1):

            @pl.when((g == 0) & (flag_ref[2] == s))
            def _(s=s):
                targets = []
                for held, groups in ((left, lefts[s]), (right, rights[s])):
                    column = 0
                    for group in groups:
                        row, wide = 0, group[0].shape[1]
                        for piece in group:
                            targets.append(
                                held.at[row : row + piece.shape[0], column : column + wide]
                            )
                            row += piece.shape[0]
                        column += wide
                started = copies(
                    piece_refs[s], targets, [sems.at[j] for j in range(len(targets))]
                )
                for copy in started:
                    copy.wait()

        def product(column, store):
            flipped[...] = left[:, pl.ds(pl.multiple_of(column, LANES), tile)].T

            def one(c, _):
                columns = pl.ds(pl.multiple_of(c * chunk, chunk), chunk)
                store(c, plain(flipped[...], right[:, columns]).astype(bf16))
                return 0

            lax.fori_loop(0, right_width // chunk, one, 0)

        if by_rows:

            def to(target):
                def store(c, made):
                    target[:, pl.ds(pl.multiple_of(c * chunk, chunk), chunk)] = made

                return store

            product(g * tile, to(keep))
            product((g + steps) * tile, to(send))
        else:
            half = right_width // 2 // chunk

            def store(c, made):
                @pl.when(c < half)
                def _():
                    keep[:, pl.ds(pl.multiple_of(c * chunk, chunk), chunk)] = made

                @pl.when(c >= half)
                def _():
                    send[:, pl.ds(pl.multiple_of((c - half) * chunk, chunk), chunk)] = made

            product(g * tile, store)

    ins = [(piece, kept_out) for s in (0, 1) for piece in pieces[s]]
    dims = (steps * tile, block[1])
    outs = [(shape(dims), pl.BlockSpec(block, lambda g: (g, 0)))] * 2
    scratch = [
        pltpu.VMEM((rows, left_width), bf16),
        pltpu.VMEM((rows, right_width), bf16),
        pltpu.VMEM((tile, rows), bf16),
        pltpu.SemaphoreType.DMA((most,)),
    ]
    return run(
        order, flags, kernel, ins, outs, scratch, "weight_sums", grid=(steps,)
    )


def fold(order, flags, keep, came, dim):
    rows, columns = keep.shape
    if dim == 0:
        tile = rows // 4
        steps, block = rows // 2 // tile, (tile, columns)
        places = [lambda g: (g, 0), lambda g: (g + steps, 0)]
        half = (rows // 2, columns)
    else:
        tile = rows // 4
        steps, block = rows // tile, (tile, columns // 2)
        places = [lambda g: (g, 0), lambda g: (g, 1)]
        half = (rows, columns // 2)

    def kernel(flag_ref, keep_low, keep_high, came_low, came_high, low, high):
        low[...] = (keep_low[...].astype(f32) + came_low[...].astype(f32)).astype(bf16)
        high[...] = (keep_high[...].astype(f32) + came_high[...].astype(f32)).astype(bf16)

    ins = [(array, pl.BlockSpec(block, place)) for array in (keep, came) for place in places]
    outs = [(shape(half), pl.BlockSpec(block, lambda g: (g, 0)))] * 2
    return run(order, flags, kernel, ins, outs, [], "fold", grid=(steps,))


def shards(
    block_input,
    out_grad,
    triple_weight,
    output_weight,
    expand_weight,
    contract_weight,
    norm_gains,
    norm_biases,
):
    section = lax.axis_index("pipe")
    span = lax.axis_index("ctx")
    lane = lax.axis_index("tp")
    spans = lax.axis_size("ctx")
    lanes = lax.axis_size("tp")
    micros, rows, width = block_input.shape
    span_rows = rows * lanes
    heads = triple_weight.shape[2]
    head_dim = triple_weight.shape[4]
    across_units = heads * head_dim
    scale = head_dim ** (-0.5)
    first_section = section == 0
    both = (0, 1)

    def hop(array, axis, step, sections):
        size = lax.axis_size(axis)
        pairs = [(s * size + a, s * size + (a ^ step)) for s in sections for a in range(size)]
        return lax.ppermute(array, ("pipe", axis), pairs)

    order = Order()

    def flags_for(wanted):
        return jnp.stack([jnp.asarray(wanted), span, section]).astype(jnp.int32)

    flags = [flags_for(section == s) for s in both]
    always = flags_for(1)

    kept = [[SimpleNamespace() for _ in range(micros)] for _ in both]
    due = {}
    slot_index = [0]

    def slot(hops, kernels=()):
        now = slot_index[0]
        slot_index[0] += 1
        ready = due.pop(now, [])
        hops = [h if len(h) == 3 else h + (1,) for h in hops]
        if hops:
            gated = fence([operand for operand, _, _ in hops], order.last + ready)
            order.last = [min(gated, key=lambda array: array.size)]
            for passed, (_, go, slots) in zip(gated, hops):
                results = go(passed)
                results = results if isinstance(results, list) else [results]
                due.setdefault(now + slots, []).extend(results)
        else:
            order.last = order.last + ready
        for kernel in kernels:
            kernel()

    def halved(keep, came, dim):
        middle = keep.shape[dim] // 2
        total = keep.astype(f32) + came.astype(f32)
        return (
            lax.slice_in_dim(total, 0, middle, axis=dim).astype(bf16),
            lax.slice_in_dim(total, middle, 2 * middle, axis=dim).astype(bf16),
        )

    def spread_hops(pieces, axis, axis_name, sections, first):
        step = lax.axis_size(axis_name) // 4
        going = first
        while step:
            pieces.append(hop(going, axis_name, step, sections))
            going = jnp.concatenate(pieces, axis=axis)
            step //= 2
        return pieces[-1]

    def fold_hops(k, first, axis_name, dim, sections):
        step, size = 1, lax.axis_size(axis_name)
        while 2 * step < size:
            came = hop(first, axis_name, step, sections)
            k.keep, k.send = halved(k.keep, came, dim)
            first = k.send
            step *= 2
        return came

    depth = width // spans
    far = spans // 2
    assert depth == across_units
    small = jnp.concatenate([norm_gains[0], norm_biases[0]], axis=0)
    packed = jnp.concatenate(
        [triple_weight[0].reshape(depth, -1), output_weight[0].reshape(-1, depth)],
        axis=1,
    )
    packed = jnp.pad(packed, ((0, 16), (0, 0)))
    packed = lax.dynamic_update_slice(packed, small, (depth, 0))
    own_expand, own_contract = expand_weight[0], contract_weight[0]
    hidden = own_expand.shape[1]
    inputs = xor_blocks(block_input, span, spans)
    cotangent = xor_blocks(out_grad, span, spans)
    early = jnp.where(first_section, inputs, cotangent)

    in_row = jnp.arange(rows, dtype=jnp.int32)
    in_span = jnp.concatenate([(lane ^ j) * rows + in_row for j in doubling(lanes)])
    positions = span * span_rows + in_span
    key_positions = jnp.stack([(span ^ k) * span_rows + in_span for k in doubling(spans)])
    tables = rope_tables(positions)
    position_column = positions[:, None]
    key_positions = key_positions[:, None, :]

    def blocks_of(own, came):
        held, step = {0: own, far: came}, far // 2
        while step:
            for k in list(held):
                held[k ^ step] = hop(held[k], "ctx", step, both)
            step //= 2
        return [held[k] for k in doubling(spans)]

    lane_offsets = doubling(lanes)

    def across(array, j, source):
        pairs = [(source * lanes + a, (1 - source) * lanes + (a ^ j)) for a in range(lanes)]
        return lax.ppermute(array, ("pipe", "tp"), pairs)

    def rows_far(s, m):
        k = kept[s][m]

        def go(passed):
            k.rows = passed
            k.pieces = [passed, hop(passed, "tp", lanes // 2, (s,))]
            return k.pieces[1]

        return k.rows, go

    def rows_near(s, m):
        k = kept[s][m]

        def go(passed):
            last_piece = spread_hops(k.pieces, 0, "tp", (s,), passed)
            k.row_pieces = [piece[None] for piece in k.pieces]
            return last_piece

        return jnp.concatenate(k.pieces, axis=0), go

    def one_way(array, direction, s):
        pairs = [
            (s * spans + a, s * spans + (a ^ far))
            for a in range(spans)
            if direction * ((a ^ far) - a) > 0
        ]
        return lax.ppermute(array, ("pipe", "ctx"), pairs)

    def pair_far(s, m):
        k = kept[s][m]

        def go(passed):
            k.pairs = [passed, one_way(passed, 1, s)]
            return k.pairs[1]

        return k.pair, go

    def pair_near(s, m):
        k = kept[s][m]

        def go(passed):
            return spread_hops(k.pairs, 0, "ctx", (s,), passed)

        return jnp.concatenate(k.pairs, axis=0), go

    def pair_grad_near(s, m):
        k = kept[s][m].pair_grad
        return k.send, lambda passed: fold_hops(k, passed, "ctx", 0, (s,))

    def pair_grad_both(s, m):
        k = kept[s][m].pair_grad

        def go(passed):
            fold_hops(k, passed, "ctx", 0, (s,))
            k.came = one_way(k.send, -1, s)
            return k.came

        return k.send, go

    def pair_grad_far(s, m):
        k = kept[s][m].pair_grad

        def go(passed):
            k.came = one_way(passed, -1, s)
            return k.came

        return k.send, go

    def sum_near(s, k):
        k.keep, going = k.blocks
        return going, lambda passed: fold_hops(k, passed, "tp", 0, (s,))

    def sum_far(s, k):
        def go(passed):
            k.blocks, k.arrived = [k.keep], [hop(passed, "tp", lanes // 2, (s,))]
            return k.arrived[0]

        return k.send, go

    def total_of(k):
        return sum(array.astype(f32) for array in [k.blocks[0], *k.arrived])

    def norm_back(upstream, combined, entering):
        normalized, inverse = normalize(entering.astype(f32))
        return (
            upstream.astype(f32)
            + inverse
            * (
                combined
                - jnp.mean(combined, axis=-1, keepdims=True)
                - normalized * jnp.mean(combined * normalized, axis=-1, keepdims=True)
            )
        ).astype(bf16)

    def middle_of(m):
        return (inputs[m].astype(f32) + total_of(kept[0][m])).astype(bf16)

    def entry_of(m):
        k = kept[1][m]
        return norm_back(cotangent[m], total_of(k), k.rows)

    def hand_one(s, m):
        k, other = kept[s][m], kept[1 - s][m]
        k.given = middle_of(m) if s == 0 else entry_of(m)

        def go(passed):
            k.given = passed
            other.rows = across(passed, 0, s)
            return other.rows

        return k.given, go

    def run_project(s, m):
        k = kept[s][m]
        pieces, place = (early_pieces, m) if s == 0 else (k.row_pieces, 0)
        k.first, k.second, k.normal, k.queries, pair = project(
            order, flags[s], pieces, place, gains, biases, tables, packed, heads, head_dim
        )
        k.pair = pair[None]

    def run_expand(m):
        k = kept[0][m]
        k.active, k.slope = expand_up(order, flags[0], k.second, weights.expand, span_rows)

    def run_attend(m):
        k = kept[0][m]
        k.attended, k.probs = attend(
            order, flags[0], k.queries, k.pairs, position_column, key_positions, scale
        )

    def run_branch(m):
        k = kept[0][m]
        k.blocks = branch_out(
            order, flags[0], [(k.active, k.attended)], contract, packed
        )

    def run_hidden_both(m):
        k = kept[1][m]
        k.upstream, k.active, k.hidden, k.part, k.side_second = hidden_both(
            order,
            flags[1],
            k.second,
            early_pieces,
            m,
            weights.expand,
            contract,
            k.normal,
            gains,
        )

    def run_attend_both(m):
        k = kept[1][m]
        k.attended, k.turned_back, keep, send = attend_both(
            order,
            flags[1],
            k.upstream,
            packed,
            k.queries,
            k.pairs,
            position_column,
            key_positions,
            tables,
            scale,
        )
        k.pair_grad = SimpleNamespace(keep=keep, send=send)

    def run_attend_back(m):
        k = kept[0][m]
        k.upstream, k.turned_back, keep, send = attend_back(
            order,
            flags[0],
            k.row_pieces,
            packed,
            k.queries,
            k.pairs,
            k.probs,
            tables,
            scale,
        )
        k.pair_grad = SimpleNamespace(keep=keep, send=send)

    def run_hidden_back(m):
        k = kept[0][m]
        k.hidden, k.part, k.side_second = hidden_back(
            order,
            flags[0],
            k.upstream,
            contract,
            weights.expand,
            k.slope,
            k.normal,
            gains,
        )

    def run_project_back(s, m):
        k = kept[s][m]
        own, arrived = k.pair_grad.keep, k.pair_grad.came
        k.stacked, k.side_first, *k.blocks = project_back(
            order,
            flags[s],
            k.turned_back,
            own.reshape(own.shape[1:]),
            arrived.reshape(arrived.shape[1:]),
            packed,
            k.part,
            k.normal,
            gains,
            tables,
        )

    def of(name, s, count=micros):
        return [getattr(kept[s][m], name) for m in range(count)]

    branch_sums, expand_sums, triple_sums = (SimpleNamespace(parts=[]) for _ in range(3))

    def run_sums(w, lefts, rights, by_rows):
        w.dim = 0 if by_rows else 1
        w.keep, w.send = weight_sums(order, always, lefts, rights, by_rows, spans)

    def wide_near(w):
        def go(passed):
            w.came = hop(passed, "ctx", 1, both)
            return w.came

        return w.send, go

    def run_fold(w):
        step = 2
        w.keep, w.send = fold(order, always, w.keep, w.came, w.dim)
        while 2 * step < spans:
            w.came = hop(w.send, "ctx", step, both)
            w.keep, w.send = fold(order, always, w.keep, w.came, w.dim)
            step *= 2

    def wide_far(w, start, stop):
        def go(passed):
            w.parts.append(hop(passed, "ctx", far, both))
            return w.parts[-1]

        return w.send[start:stop], go

    weights = SimpleNamespace(expand_came=[], contract_came=[])
    half_depth = depth // 2

    def expand_far(start, stop):
        def go(passed):
            weights.expand_came.append(hop(passed, "ctx", far, both))
            return weights.expand_came[-1]

        return own_expand[start:stop], go

    def packed_far(passed):
        weights.packed_came = hop(passed, "ctx", far, both)
        return weights.packed_came

    def packed_near(passed):
        weights.packed = blocks_of(packed, passed)
        return weights.packed[1:]

    def expand_near(passed):
        weights.expand = blocks_of(own_expand, passed)
        return weights.expand[1:]

    def contract_far(start, stop):
        def go(passed):
            weights.contract_came.append(hop(passed, "ctx", far, both))
            return weights.contract_came[-1]

        return own_contract[start:stop], go

    def contract_near(passed):
        weights.contract = blocks_of(own_contract, passed)
        return weights.contract[1:]

    def early_hops(passed):
        weights.early = [passed] + [hop(passed, "tp", j, both) for j in lane_offsets[1:]]
        return weights.early[1:]

    due[0] = [expand_far(0, half_depth)[1](own_expand[:half_depth])]
    slot([(packed, packed_far), expand_far(half_depth, depth), (early, early_hops)])
    early_pieces = weights.early
    cuts = [0, hidden // 4, 11 * hidden // 16, hidden]
    expand_came = jnp.concatenate(weights.expand_came, axis=0)
    slot(
        [
            (weights.packed_came, packed_near),
            (expand_came, expand_near),
            contract_far(cuts[0], cuts[1]),
        ]
    )
    packed = weights.packed
    small_full = jnp.concatenate(
        [piece[depth : depth + 4, :depth] for piece in packed], axis=1
    ).astype(f32)
    gains, biases = small_full[:2], small_full[2:]
    slot(
        [contract_far(cuts[1], cuts[2])],
        [lambda m=m: run_project(0, m) for m in range(micros)],
    )
    a, b = kept
    slot(
        [pair_far(0, 0), contract_far(cuts[2], cuts[3])],
        [lambda m=m: run_expand(m) for m in range(micros)],
    )
    contract_came = jnp.concatenate(weights.contract_came, axis=0)
    slot([(contract_came, contract_near), pair_near(0, 0)])
    contract = weights.contract
    slot([pair_far(0, 1)], [lambda: run_attend(0), lambda: run_branch(0)])
    slot([sum_near(0, a[0]), pair_near(0, 1)])
    slot([sum_far(0, a[0]), pair_far(0, 2)], [lambda: run_attend(1), lambda: run_branch(1)])
    slot([hand_one(0, 0), sum_near(0, a[1]), pair_near(0, 2)])
    slot(
        [rows_far(1, 0), sum_far(0, a[1])], [lambda: run_attend(2), lambda: run_branch(2)]
    )
    slot([rows_near(1, 0), hand_one(0, 1), sum_near(0, a[2])])
    slot([rows_far(1, 1), sum_far(0, a[2])], [lambda: run_project(1, 0)])
    slot(
        [pair_far(1, 0), rows_near(1, 1), hand_one(0, 2)], [lambda: run_hidden_both(0)]
    )
    slot([pair_near(1, 0), rows_far(1, 2)], [lambda: run_project(1, 1)])
    slot(
        [pair_far(1, 1), rows_near(1, 2)],
        [lambda: run_attend_both(0), lambda: run_hidden_both(1)],
    )
    slot([pair_grad_near(1, 0), pair_near(1, 1)], [lambda: run_project(1, 2)])
    slot(
        [pair_grad_far(1, 0), pair_far(1, 2)],
        [lambda: run_attend_both(1), lambda: run_hidden_both(2)],
    )
    slot([pair_grad_near(1, 1), pair_near(1, 2)], [lambda: run_project_back(1, 0)])
    slot([sum_near(1, b[0]), pair_grad_far(1, 1)], [lambda: run_attend_both(2)])
    slot([sum_far(1, b[0]), pair_grad_near(1, 2)], [lambda: run_project_back(1, 1)])
    slot([hand_one(1, 0), sum_near(1, b[1]), pair_grad_far(1, 2)])
    slot([sum_far(1, b[1]), rows_far(0, 0)], [lambda: run_project_back(1, 2)])
    slot([sum_near(1, b[2]), hand_one(1, 1), rows_near(0, 0)])
    slot([sum_far(1, b[2]), rows_far(0, 1)], [lambda: run_attend_back(0)])
    slot(
        [hand_one(1, 2), rows_near(0, 1), pair_grad_near(0, 0)],
        [lambda: run_hidden_back(0)],
    )
    slot([rows_far(0, 2), pair_grad_far(0, 0)], [lambda: run_attend_back(1)])
    slot(
        [rows_near(0, 2), pair_grad_near(0, 1)],
        [lambda: run_hidden_back(1), lambda: run_project_back(0, 0)],
    )
    last = micros - 1

    def run_branch_sums():
        run_sums(
            branch_sums,
            [[of("active", s), of("attended", s)] for s in both],
            [
                [of("upstream", 0, last) + [piece[0] for piece in a[last].row_pieces]],
                [of("upstream", 1)],
            ],
            False,
        )

    def run_expand_sums():
        run_sums(
            expand_sums,
            [[of("second", s)] for s in both],
            [[of("hidden", s)] for s in both],
            True,
        )

    def run_triple_sums():
        run_sums(
            triple_sums,
            [[of("first", s)] for s in both],
            [[of("stacked", s)] for s in both],
            True,
        )

    finals = SimpleNamespace()

    def run_final_branch():
        blocks = branch_out(
            order, flags[1], [(k.active, k.attended) for k in b], contract, packed
        )
        finals.keep = jnp.stack(blocks[0::2])
        finals.send = jnp.stack(blocks[1::2])

    def last_near(w, s):
        return w.send, lambda passed: fold_hops(w, passed, "tp", 1, (s,))

    def last_far(w, s):
        def go(passed):
            w.came = hop(passed, "tp", lanes // 2, (s,))
            return w.came

        return w.send, go

    slot([pair_grad_far(0, 1)], [run_branch_sums])
    slot(
        [wide_near(branch_sums)], [lambda: run_attend_back(2), lambda: run_project_back(0, 1)]
    )
    slot([], [lambda: run_fold(branch_sums)])
    cut = [0, 3 * hidden // 8, 7 * hidden // 8, hidden + across_units]
    slot(
        [wide_far(branch_sums, cut[0], cut[1]), pair_grad_both(0, 2)],
        [lambda: run_hidden_back(2)],
    )

    def stacked(chosen):
        keep, send = zip(*(k.blocks for k in chosen))
        return SimpleNamespace(keep=jnp.stack(keep), send=jnp.stack(send))

    outs = [stacked(a[:last])]
    slot(
        [wide_far(branch_sums, cut[1], cut[2]), last_near(outs[0], 0)],
        [lambda: run_project_back(0, 2), run_triple_sums],
    )
    outs.append(stacked(a[last:]))

    def side_of(mades):
        return sum(
            jnp.concatenate([k.side_first, k.side_second], axis=0) for k in mades
        )

    side = SimpleNamespace(all=jnp.where(first_section, side_of(a), side_of(b)))

    def side_ctx(passed):
        step = 1
        while step < spans:
            middle = passed.shape[1] // 2
            came = hop(passed[:, middle:], "ctx", step, both)
            passed = passed[:, :middle] + came
            step *= 2
        side.all = passed
        return came

    def side_near(passed):
        step = 1
        while 2 * step < lanes:
            came = hop(passed, "tp", step, both)
            passed = passed + came
            step *= 2
        side.all = passed
        return came

    def side_far(passed):
        came = hop(passed, "tp", lanes // 2, both)
        side.all = passed + came
        return came

    def held_back(w, j):
        def go(passed):
            w.parts[j] = passed
            return []

        return w.parts[j], go

    def wide_total(keep, parts):
        came = jnp.concatenate(parts, axis=0) if len(parts) > 1 else parts[0]
        return keep.astype(f32) + came.astype(f32)

    slot(
        [
            wide_near(triple_sums),
            wide_far(branch_sums, cut[2], cut[3]),
            (side.all, side_ctx),
            last_near(outs[1], 0),
        ],
        [run_expand_sums, run_final_branch],
    )
    slot([], [lambda: run_fold(triple_sums)])
    slot(
        [
            wide_far(triple_sums, 0, depth),
            wide_near(expand_sums),
            last_far(outs[0], 0),
            last_near(finals, 1),
            (side.all, side_near),
        ]
    )
    slot([], [lambda: run_fold(expand_sums)])
    slot(
        [
            wide_far(expand_sums, 0, depth),
            last_far(outs[1], 0),
            last_far(finals, 1),
            (side.all, side_far),
            held_back(triple_sums, 0),
            held_back(branch_sums, 2),
        ]
    )
    triple_grads = wide_total(triple_sums.keep, triple_sums.parts)
    triple_grads = triple_grads.reshape(triple_weight.shape)
    branch_grads = wide_total(branch_sums.keep, branch_sums.parts)
    contract_grads, output_grads = branch_grads[:hidden], branch_grads[hidden:]
    expand_grads = wide_total(expand_sums.keep, expand_sums.parts)
    layer_outputs = jnp.stack(
        [
            jnp.where(
                first_section,
                kept[0][m].given,
                (
                    b[m].rows.astype(f32)
                    + finals.keep[m].astype(f32)
                    + finals.came[m].astype(f32)
                ).astype(bf16),
            )
            for m in range(micros)
        ]
    )
    own_sums = [out.keep.astype(f32) + out.came.astype(f32) for out in outs]
    own_entries = [
        norm_back(jnp.stack([k.rows for k in chosen]), total, entering)
        for chosen, total, entering in (
            (a[:last], own_sums[0], inputs[:last]),
            (a[last:], own_sums[1], inputs[last:]),
        )
    ]
    entry_grads = jnp.where(
        first_section, jnp.concatenate(own_entries, axis=0), jnp.stack(of("given", 1))
    )
    gain_grads = jnp.stack([side.all[0], side.all[2]])
    bias_grads = jnp.stack([side.all[1], side.all[3]])
    return (
        xor_blocks(layer_outputs, span, spans, inverse=True)[None],
        xor_blocks(entry_grads, span, spans, inverse=True)[None],
        triple_grads,
        output_grads.reshape(output_weight.shape),
        expand_grads[None],
        contract_grads[None],
        gain_grads[None],
        bias_grads[None],
    )


def solution(mesh):
    return jax.shard_map(
        shards,
        mesh=mesh,
        in_specs=(
            P(None, ("ctx", "tp"), None),
            P(None, ("ctx", "tp"), None),
            P("pipe", "ctx", "tp", None, None),
            P("pipe", "tp", None, "ctx"),
            P("pipe", "ctx", "tp"),
            P("pipe", "tp", "ctx"),
            P("pipe", None, "ctx"),
            P("pipe", None, "ctx"),
        ),
        out_specs=(
            P("pipe", None, ("ctx", "tp"), None),
            P("pipe", None, ("ctx", "tp"), None),
            P("pipe", "ctx", "tp", None, None),
            P("pipe", "tp", None, "ctx"),
            P("pipe", "ctx", "tp"),
            P("pipe", "tp", "ctx"),
            P("pipe", None, "ctx"),
            P("pipe", None, "ctx"),
        ),
        check_vma=False,
    )
```

```python
import functools
import math
from types import SimpleNamespace

import jax
import jax.numpy as jnp
from jax import lax
from jax.experimental import pallas as pl
from jax.experimental.pallas import tpu as pltpu
from jax.sharding import PartitionSpec as P

ROT = 64
LANES = 128
epsilon = 1e-05
masked_score = -1e30
f32 = jnp.float32
bf16 = jnp.bfloat16
mebibyte = 1024 * 1024
half_root = 0.7071067811865476
bell = 0.3989422804014327


def dot(a, b, dims):
    return lax.dot_general(a, b, (dims, ((), ())), preferred_element_type=f32)


def plain(a, b):
    return dot(a, b, ((1,), (0,)))


def turned(a, b):
    return dot(a, b, ((1,), (1,)))


def doubling(count):
    order, step = [0], count // 2
    while step:
        order += [k ^ step for k in order]
        step //= 2
    return order


def xor_blocks(values, index, count, inverse=False):
    width = values.shape[-1] // count
    order = doubling(count)

    def taken(places):
        return jnp.concatenate(
            [values[..., k * width : (k + 1) * width] for k in places], axis=-1
        )

    if inverse:
        values = taken([order.index(k) for k in range(count)])
    step = 1
    while step < count:
        swapped = taken([k ^ step for k in range(count)])
        values = jnp.where((index & step) != 0, swapped, values)
        step *= 2
    return values if inverse else taken(order)


def rope_tables(positions):
    half = ROT // 2
    frequency = 10000.0 ** (-jnp.arange(0, ROT, 2, dtype=f32) / ROT)
    angles = positions.astype(f32)[:, None] * frequency[None, :]
    cosine, sine = jnp.cos(angles), jnp.sin(angles)
    count = positions.shape[0]
    rest = jnp.zeros((count, LANES - ROT), f32)
    none = jnp.zeros((count, half), f32)
    return jnp.stack(
        [
            jnp.concatenate([cosine, cosine, rest + 1.0], axis=1),
            jnp.concatenate([-sine, none, rest], axis=1),
            jnp.concatenate([none, sine, rest], axis=1),
        ]
    )


def turn(values, tables, sign):
    half = ROT // 2
    part = values[:, :LANES]
    moved = (
        pltpu.roll(part, LANES - half, 1) * tables[1] + pltpu.roll(part, half, 1) * tables[2]
    )
    part = part * tables[0] + (moved if sign > 0 else -moved)
    return jnp.concatenate([part, values[:, LANES:]], axis=1)


def normalize(values):
    center = values - jnp.mean(values, axis=-1, keepdims=True)
    inverse = lax.rsqrt(jnp.mean(center * center, axis=-1, keepdims=True) + epsilon)
    return (center * inverse, inverse)


def whole(array):
    zeros = (0,) * array.ndim
    return pl.BlockSpec(array.shape, lambda *_: zeros)


def at(block, place):
    return pl.BlockSpec(block, lambda *_: place)


kept_out = pl.BlockSpec(memory_space=pl.ANY)


def shape(dims, dtype=bf16):
    return jax.ShapeDtypeStruct(dims, dtype)


class Order:
    def __init__(self):
        self.last = []

    def follow(self, results):
        self.last = [min(results, key=lambda array: array.size * array.dtype.itemsize)]

    def also(self, array):
        self.last = self.last + [array]


took = dict(
    project=7,
    expand=8,
    attend=5,
    branch=8,
    hidden_both=14,
    attend_both=11,
    attend_back=8,
    hidden_back=13,
    project_back=8,
    weight_sums=16,
    fold=7,
)
peak = 1.15e9


def run(order, flags, kernel, ins, outs, scratch, name, grid=(1,), work=0):
    taken = len(ins)
    ins = [(flags, pl.BlockSpec(memory_space=pltpu.SMEM))] + list(ins)
    ins += [(array, kept_out) for array in order.last]
    arrays = [array for array, _ in ins]
    once = grid == (1,)

    def sized(spec, dtype):
        if spec.block_shape is None:
            return spec, 0
        size = math.prod(spec.block_shape) * jnp.dtype(dtype).itemsize
        if not once:
            return spec, 2 * size
        single = pl.BlockSpec(
            spec.block_shape, spec.index_map, pipeline_mode=pl.Buffered(1)
        )
        return single, size

    in_specs = [sized(spec, array.dtype) for array, spec in ins]
    out_specs = [sized(spec, struct.dtype) for struct, spec in outs]
    held = sum(size for _, size in in_specs + out_specs)
    for buffer in scratch:
        if buffer.memory_space == pltpu.VMEM:
            held += math.prod(buffer.shape) * jnp.dtype(buffer.dtype).itemsize

    def body(flag_ref, *refs):
        @pl.when(flag_ref[0] == 1)
        def _():
            kernel(flag_ref, *refs[:taken], *refs[len(ins) - 1 :])

    results = pl.pallas_call(
        body,
        grid=grid,
        in_specs=[spec for spec, _ in in_specs],
        out_specs=[spec for spec, _ in out_specs],
        out_shape=[struct for struct, _ in outs],
        scratch_shapes=scratch,
        compiler_params=pltpu.CompilerParams(
            vmem_limit_bytes=int(held + (work + 4) * mebibyte)
        ),
        cost_estimate=pl.CostEstimate(
            flops=int(took[name] * peak), bytes_accessed=0, transcendentals=0
        ),
        name=name,
    )(*arrays)
    order.follow(results)
    return results


def fence(through, waits):
    count = len(through)

    def kernel(*refs):
        pass

    return pl.pallas_call(
        kernel,
        in_specs=[kept_out] * (count + len(waits)),
        out_specs=[kept_out] * count,
        out_shape=[shape(array.shape, array.dtype) for array in through],
        input_output_aliases={j: j for j in range(count)},
        compiler_params=pltpu.CompilerParams(vmem_limit_bytes=mebibyte),
        cost_estimate=pl.CostEstimate(flops=1, bytes_accessed=1, transcendentals=0),
        name="fence",
    )(*through, *waits)


def full_out(dims, dtype=bf16):
    zeros = (0,) * len(dims)
    return (shape(dims, dtype), pl.BlockSpec(dims, lambda *_: zeros))


def copies(sources, targets, sems):
    started = []
    for source, target, sem in zip(sources, targets, sems):
        copy = pltpu.make_async_copy(source, target, sem)
        copy.start()
        started.append(copy)
    return started


def project(order, flags, pieces, at_piece, gains, biases, tables, weights, heads, head_dim):
    count, width = 1, pieces[0].shape[2]
    span_rows = sum(piece.shape[1] for piece in pieces)
    rows = count * span_rows
    chunk = pieces[0].shape[1]
    spans = len(weights)
    depth = width // spans
    wide = 3 * head_dim
    columns = heads * wide

    def kernel(flag_ref, *refs):
        piece_refs = refs[: len(pieces)]
        gain_ref, bias_ref, table_ref = refs[len(pieces) : len(pieces) + 3]
        weight_refs = refs[len(pieces) + 3 : len(pieces) + 3 + spans]
        first, second, normal, queries, pair, held, sems = refs[len(pieces) + 3 + spans :]
        started = []
        for h in range(heads):
            started.append(
                copies(
                    [w.at[:depth, h * wide : (h + 1) * wide] for w in weight_refs],
                    [held.at[h, k * depth : (k + 1) * depth] for k in range(spans)],
                    [sems.at[h, k] for k in range(spans)],
                )
            )
        start = 0
        for piece_ref in piece_refs:
            chunks = piece_ref.shape[1] // chunk

            def one(i, _, piece_ref=piece_ref, start=start, chunks=chunks):
                m, c = i // chunks, i % chunks
                values = piece_ref[m, pl.ds(pl.multiple_of(c * chunk, chunk), chunk), :]
                normed, _ = normalize(values.astype(f32))
                to = pl.ds(
                    pl.multiple_of(m * span_rows + start + c * chunk, chunk), chunk
                )
                normal[to, :] = normed.astype(bf16)
                first[to, :] = (normed * gain_ref[0:1] + bias_ref[0:1]).astype(bf16)
                second[to, :] = (normed * gain_ref[1:2] + bias_ref[1:2]).astype(bf16)
                return 0

            lax.fori_loop(0, count * chunks, one, 0)
            start += piece_ref.shape[1]
        for h in range(heads):
            for copy in started[h]:
                copy.wait()

            def two(m, _, h=h):
                to = pl.ds(pl.multiple_of(m * span_rows, span_rows), span_rows)
                made = plain(first[to, :], held[h])
                queries[h, to, :] = turn(made[:, :head_dim], table_ref, 1).astype(bf16)
                pair[0, h, to, :] = turn(
                    made[:, head_dim : 2 * head_dim], table_ref, 1
                ).astype(bf16)
                pair[1, h, to, :] = made[:, 2 * head_dim :].astype(bf16)
                return 0

            lax.fori_loop(0, count, two, 0)

    ins = [(piece, at((1,) + piece.shape[1:], (at_piece, 0, 0))) for piece in pieces]
    ins += [(array, whole(array)) for array in (gains, biases, tables)]
    ins += [(w, kept_out) for w in weights]
    outs = [full_out((rows, width))] * 3 + [
        full_out((heads, rows, head_dim)),
        full_out((2, heads, rows, head_dim)),
    ]
    scratch = [
        pltpu.VMEM((heads, width, wide), bf16),
        pltpu.SemaphoreType.DMA((heads, spans)),
    ]
    return run(order, flags, kernel, ins, outs, scratch, "project")


def expand_up(order, flags, second, weights, span_rows):
    rows, width = second.shape
    depth, hidden = weights[0].shape
    spans = len(weights)
    tile = min(512, hidden)
    tiles = hidden // tile

    def kernel(flag_ref, *refs):
        second_ref, weight_refs = refs[0], refs[1 : 1 + spans]
        active, slope, held, sems = refs[1 + spans :]
        started = []
        for t in range(tiles):
            started.append(
                copies(
                    [w.at[:, t * tile : (t + 1) * tile] for w in weight_refs],
                    [held.at[t, k * depth : (k + 1) * depth] for k in range(spans)],
                    [sems.at[t, k] for k in range(spans)],
                )
            )
        for t in range(tiles):
            for copy in started[t]:
                copy.wait()

            def one(m, _, t=t):
                to = pl.ds(pl.multiple_of(m * span_rows, span_rows), span_rows)
                pre = plain(second_ref[to, :], held[t])
                risen = 0.5 * (1.0 + lax.erf(pre * half_root))
                columns = slice(t * tile, (t + 1) * tile)
                active[to, columns] = (pre * risen).astype(bf16)
                slope[to, columns] = (
                    risen + pre * jnp.exp(-0.5 * pre * pre) * bell
                ).astype(bf16)
                return 0

            lax.fori_loop(0, rows // span_rows, one, 0)

    ins = [(second, whole(second))] + [(w, kept_out) for w in weights]
    outs = [full_out((rows, hidden))] * 2
    scratch = [
        pltpu.VMEM((tiles, width, tile), bf16),
        pltpu.SemaphoreType.DMA((tiles, spans)),
    ]
    return run(order, flags, kernel, ins, outs, scratch, "expand")


def spread(refs):
    return [ref.at[j] for ref in refs for j in range(ref.shape[0])]


def attention(here, pairs, head, row_ref, key_ref, scale):
    scores = []
    for k, pair in enumerate(pairs):
        raw = turned(here, pair[0, head]) * scale
        scores.append(jnp.where(key_ref[k] <= row_ref[...], raw, masked_score))
    top = functools.reduce(
        jnp.maximum, [jnp.max(part, axis=1, keepdims=True) for part in scores]
    )
    scores = [jnp.exp(part - top) for part in scores]
    inverse = 1.0 / sum(jnp.sum(part, axis=1, keepdims=True) for part in scores)
    return [part * inverse for part in scores]


def attend(order, flags, queries, pairs, positions, key_positions, scale):
    heads, rows, head_dim = queries.shape
    spans = sum(pair.shape[0] for pair in pairs)

    def kernel(flag_ref, query_ref, *refs):
        views, refs = spread(refs[: len(pairs)]), refs[len(pairs) :]
        row_ref, key_ref, attended, probs = refs
        for h in range(heads):
            parts = attention(query_ref[h], views, h, row_ref, key_ref, scale)
            summed = None
            for k in range(spans):
                part = parts[k].astype(bf16)
                probs[k, h] = part
                term = plain(part, views[k][1, h])
                summed = term if summed is None else summed + term
            attended[:, h * head_dim : (h + 1) * head_dim] = summed.astype(bf16)

    ins = [
        (array, whole(array)) for array in (queries, *pairs, positions, key_positions)
    ]
    outs = [full_out((rows, heads * head_dim)), full_out((spans, heads, rows, rows))]
    work = spans * rows * rows * 4 * heads * 4 / mebibyte
    return run(order, flags, kernel, ins, outs, [], "attend", work=work)


def attention_grads(grad, here, parts, views, head, keep, send, scale):
    half = keep.shape[0]
    grad_probs = [turned(grad, view[1, head]) for view in views]
    delta = sum(
        jnp.sum(part.astype(f32) * slope, axis=1, keepdims=True)
        for part, slope in zip(parts, grad_probs)
    )
    query_grad = None
    for k, view in enumerate(views):
        slopes = (parts[k].astype(f32) * (grad_probs[k] - delta)).astype(bf16)
        term = plain(slopes, view[0, head])
        query_grad = term if query_grad is None else query_grad + term
        side = keep if k < half else send
        side[k % half, 0, head] = (dot(slopes, here, ((0,), (0,))) * scale).astype(bf16)
        side[k % half, 1, head] = dot(parts[k].astype(bf16), grad, ((0,), (0,))).astype(bf16)
    return query_grad * scale


def attend_both(
    order, flags, rows_in, packed, queries, pairs, positions, key_positions, tables, scale
):
    heads, rows, head_dim = queries.shape
    width = rows_in.shape[1]
    spans = len(packed)
    across, depth = heads * head_dim, width // spans
    half = spans // 2

    def kernel(flag_ref, rows_ref, *refs):
        packed_refs, refs = refs[:spans], refs[spans:]
        query_ref, refs = refs[0], refs[1:]
        views, refs = spread(refs[: len(pairs)]), refs[len(pairs) :]
        row_ref, key_ref, table_ref, attended, turned_back, keep, send, held, sems = refs
        started = copies(
            [w.at[:across, 3 * across : 3 * across + depth] for w in packed_refs],
            [held.at[:, k * depth : (k + 1) * depth] for k in range(spans)],
            [sems.at[k] for k in range(spans)],
        )
        all_parts = []
        for h in range(heads):
            parts = attention(query_ref[h], views, h, row_ref, key_ref, scale)
            summed = None
            for k in range(spans):
                term = plain(parts[k].astype(bf16), views[k][1, h])
                summed = term if summed is None else summed + term
            attended[:, h * head_dim : (h + 1) * head_dim] = summed.astype(bf16)
            all_parts.append(parts)
        for copy in started:
            copy.wait()
        grads = turned(rows_ref[...], held[...]).astype(bf16)
        for h in range(heads):
            made = attention_grads(
                grads[:, h * head_dim : (h + 1) * head_dim],
                query_ref[h],
                all_parts[h],
                views,
                h,
                keep,
                send,
                scale,
            )
            turned_back[h] = turn(made, table_ref, -1).astype(bf16)

    ins = [(rows_in, whole(rows_in))] + [(w, kept_out) for w in packed]
    ins += [
        (array, whole(array)) for array in (queries, *pairs, positions, key_positions, tables)
    ]
    outs = [full_out((rows, across)), full_out((heads, rows, head_dim))]
    outs += [full_out((half, 2, heads, rows, head_dim))] * 2
    scratch = [pltpu.VMEM((across, width), bf16), pltpu.SemaphoreType.DMA((spans,))]
    work = spans * rows * rows * 4 * (heads + 4) / mebibyte
    return run(order, flags, kernel, ins, outs, scratch, "attend_both", work=work)


def hidden_both(order, flags, second, pieces, at_piece, expand, contract, normal, gains):
    rows, width = second.shape
    hidden, depth = contract[0].shape
    spans = len(contract)
    tile = min(512, hidden)
    tiles = hidden // tile

    def kernel(flag_ref, second_ref, *refs):
        piece_refs, refs = refs[: len(pieces)], refs[len(pieces) :]
        expand_refs, refs = refs[:spans], refs[spans:]
        contract_refs, refs = refs[:spans], refs[spans:]
        normal_ref, gain_ref, rows_out, active, grads, part, side, *refs = refs
        held_up, held_down, sems_up, sems_down = refs
        started = []
        for t in range(tiles):
            block = slice(t * tile, (t + 1) * tile)
            places = [slice(k * depth, (k + 1) * depth) for k in range(spans)]
            up = copies(
                [w.at[:, block] for w in expand_refs],
                [held_up.at[place, block] for place in places],
                [sems_up.at[t, k] for k in range(spans)],
            )
            down = copies(
                [w.at[block, :] for w in contract_refs],
                [held_down.at[block, place] for place in places],
                [sems_down.at[t, k] for k in range(spans)],
            )
            started.append((up, down))
        start = 0
        for piece_ref in piece_refs:
            size = piece_ref.shape[1]
            rows_out[start : start + size, :] = piece_ref[0]
            start += size
        for t in range(tiles):
            block = slice(t * tile, (t + 1) * tile)
            for copy in started[t][0] + started[t][1]:
                copy.wait()
            pre = plain(second_ref[...], held_up[:, block])
            risen = 0.5 * (1.0 + lax.erf(pre * half_root))
            active[:, block] = (pre * risen).astype(bf16)
            slope = risen + pre * jnp.exp(-0.5 * pre * pre) * bell
            grads[:, block] = (turned(rows_out[...], held_down[block, :]) * slope).astype(bf16)
        for k in range(spans):
            place = slice(k * depth, (k + 1) * depth)
            made = turned(grads[...], held_up[place, :])
            side[0:1, place] = jnp.sum(
                made * normal_ref[:, place].astype(f32), axis=0, keepdims=True
            )
            side[1:2, place] = jnp.sum(made, axis=0, keepdims=True)
            part[:, place] = made * gain_ref[1:2, place]

    ins = [(second, whole(second))]
    ins += [(piece, at((1,) + piece.shape[1:], (at_piece, 0, 0))) for piece in pieces]
    ins += [(w, kept_out) for w in expand] + [(w, kept_out) for w in contract]
    ins += [(normal, whole(normal)), (gains, whole(gains))]
    outs = [
        full_out((rows, width)),
        full_out((rows, hidden)),
        full_out((rows, hidden)),
        full_out((rows, width), f32),
        full_out((2, width), f32),
    ]
    scratch = [
        pltpu.VMEM((width, hidden), bf16),
        pltpu.VMEM((hidden, width), bf16),
        pltpu.SemaphoreType.DMA((tiles, spans)),
        pltpu.SemaphoreType.DMA((tiles, spans)),
    ]
    return run(order, flags, kernel, ins, outs, scratch, "hidden_both")


def branch_out(order, flags, groups, contract, packed):
    hidden, depth = contract[0].shape
    across = groups[0][1].shape[1]
    spans = len(contract)
    width = depth * spans
    span_rows = groups[0][0].shape[0]
    block = span_rows // 2
    count = len(groups)

    def kernel(flag_ref, *refs):
        group_refs, refs = refs[: 2 * count], refs[2 * count :]
        contract_refs, packed_refs = refs[:spans], refs[spans : 2 * spans]
        blocks, refs = refs[2 * spans : 2 * (spans + count)], refs[2 * (spans + count) :]
        held, held_out, sems = refs
        outputs = [w.at[:across, 3 * across : 3 * across + depth] for w in packed_refs]
        started = copies(
            [ref for k in range(spans) for ref in (outputs[k], contract_refs[k])],
            [ref for k in range(spans) for ref in (held_out.at[k], held.at[k])],
            [sems.at[j] for j in range(2 * spans)],
        )
        for k in range(spans):
            started[2 * k].wait()
            started[2 * k + 1].wait()
            columns = slice(k * depth, (k + 1) * depth)
            for c in range(count):
                made = plain(group_refs[2 * c + 1][...], held_out[k])
                made = made + plain(group_refs[2 * c][...], held[k])
                blocks[2 * c][:, columns] = made[:block].astype(bf16)
                blocks[2 * c + 1][:, columns] = made[block:].astype(bf16)

    ins = []
    for active, attended in groups:
        ins += [(active, whole(active)), (attended, whole(attended))]
    ins += [(w, kept_out) for w in contract] + [(w, kept_out) for w in packed]
    outs = [full_out((block, width))] * (2 * count)
    scratch = [
        pltpu.VMEM((spans, hidden, depth), bf16),
        pltpu.VMEM((spans, across, depth), bf16),
        pltpu.SemaphoreType.DMA((2 * spans,)),
    ]
    return run(order, flags, kernel, ins, outs, scratch, "branch")


def attend_back(order, flags, pieces, packed, queries, pairs, probs, tables, scale):
    rows = sum(piece.shape[1] for piece in pieces)
    width = pieces[0].shape[2]
    heads, _, head_dim = queries.shape
    spans = len(packed)
    across, depth = heads * head_dim, width // spans
    half = spans // 2

    def kernel(flag_ref, *refs):
        piece_refs, refs = refs[: len(pieces)], refs[len(pieces) :]
        packed_refs, refs = refs[:spans], refs[spans:]
        query_ref, refs = refs[0], refs[1:]
        views, refs = spread(refs[: len(pairs)]), refs[len(pairs) :]
        prob_ref, table_ref, rows_out, turned_back, keep, send, held, sems = refs
        started = copies(
            [w.at[:across, 3 * across : 3 * across + depth] for w in packed_refs],
            [held.at[:, k * depth : (k + 1) * depth] for k in range(spans)],
            [sems.at[k] for k in range(spans)],
        )
        start = 0
        for piece_ref in piece_refs:
            size = piece_ref.shape[1]
            rows_out[start : start + size, :] = piece_ref[0]
            start += size
        for copy in started:
            copy.wait()
        grads = turned(rows_out[...], held[...]).astype(bf16)
        for h in range(heads):
            made = attention_grads(
                grads[:, h * head_dim : (h + 1) * head_dim],
                query_ref[h],
                [prob_ref[k, h] for k in range(spans)],
                views,
                h,
                keep,
                send,
                scale,
            )
            turned_back[h] = turn(made, table_ref, -1).astype(bf16)

    ins = [(piece, whole(piece)) for piece in pieces] + [(w, kept_out) for w in packed]
    ins += [(array, whole(array)) for array in (queries, *pairs, probs, tables)]
    outs = [full_out((rows, width)), full_out((heads, rows, head_dim))]
    outs += [full_out((half, 2, heads, rows, head_dim))] * 2
    scratch = [pltpu.VMEM((across, width), bf16), pltpu.SemaphoreType.DMA((spans,))]
    work = spans * rows * rows * 4 * 4 / mebibyte
    return run(order, flags, kernel, ins, outs, scratch, "attend_back", work=work)


def hidden_back(order, flags, upstream, contract, expand, slope, normal, gains):
    span_rows, width = upstream.shape
    hidden, depth = contract[0].shape
    spans = len(contract)
    tile = min(512, hidden)
    tiles = hidden // tile

    def kernel(flag_ref, *refs):
        upstream_ref, refs = refs[0], refs[1:]
        contract_refs, refs = refs[:spans], refs[spans:]
        expand_refs, refs = refs[:spans], refs[spans:]
        slope_ref, normal_ref, gain_ref, grads, part, side, held, held_up, sems, sems_up = refs
        started = [
            copies(
                [w.at[t * tile : (t + 1) * tile, :] for w in contract_refs],
                [held.at[t, :, k * depth : (k + 1) * depth] for k in range(spans)],
                [sems.at[t, k] for k in range(spans)],
            )
            for t in range(tiles)
        ]
        started_up = copies(
            expand_refs, [held_up.at[k] for k in range(spans)], [sems_up.at[k] for k in range(spans)]
        )
        for t in range(tiles):
            for copy in started[t]:
                copy.wait()
            columns = slice(t * tile, (t + 1) * tile)
            grads[:, columns] = (
                turned(upstream_ref[...], held[t]) * slope_ref[:, columns].astype(f32)
            ).astype(bf16)
        for k in range(spans):
            started_up[k].wait()
            made = turned(grads[...], held_up[k])
            columns = slice(k * depth, (k + 1) * depth)
            side[0:1, columns] = jnp.sum(
                made * normal_ref[:, columns].astype(f32), axis=0, keepdims=True
            )
            side[1:2, columns] = jnp.sum(made, axis=0, keepdims=True)
            part[:, columns] = made * gain_ref[1:2, columns]

    ins = [(upstream, whole(upstream))]
    ins += [(w, kept_out) for w in contract] + [(w, kept_out) for w in expand]
    ins += [
        (slope, whole(slope)),
        (normal, whole(normal)),
        (gains, whole(gains)),
    ]
    outs = [
        full_out((span_rows, hidden)),
        full_out((span_rows, width), f32),
        full_out((2, width), f32),
    ]
    scratch = [
        pltpu.VMEM((tiles, tile, width), bf16),
        pltpu.VMEM((spans, depth, hidden), bf16),
        pltpu.SemaphoreType.DMA((tiles, spans)),
        pltpu.SemaphoreType.DMA((spans,)),
    ]
    return run(order, flags, kernel, ins, outs, scratch, "hidden_back")


def project_back(
    order, flags, turned_back, own, came, weights, part, normal, gains, tables
):
    heads, span_rows, head_dim = turned_back.shape
    spans = len(weights)
    width = part.shape[1]
    depth, columns = width // spans, 3 * heads * head_dim
    block = span_rows // 2

    def kernel(flag_ref, *refs):
        query_ref, own_ref, came_ref, refs = refs[0], refs[1], refs[2], refs[3:]
        weight_refs, refs = refs[:spans], refs[spans:]
        part_ref, normal_ref, gain_ref, table_ref, grads, side, *refs = refs
        low, high, held, sems = refs
        started = copies(
            [w.at[:depth, :columns] for w in weight_refs],
            [held.at[k] for k in range(spans)],
            [sems.at[k] for k in range(spans)],
        )
        for h in range(heads):
            at_column = h * 3 * head_dim
            keys = own_ref[0, h].astype(f32) + came_ref[0, h].astype(f32)
            values = own_ref[1, h].astype(f32) + came_ref[1, h].astype(f32)
            grads[:, at_column : at_column + head_dim] = query_ref[h]
            grads[:, at_column + head_dim : at_column + 2 * head_dim] = turn(
                keys, table_ref, -1
            ).astype(bf16)
            grads[:, at_column + 2 * head_dim : at_column + 3 * head_dim] = values.astype(bf16)
        for k in range(spans):
            started[k].wait()
            made = turned(grads[...], held[k])
            span_columns = slice(k * depth, (k + 1) * depth)
            side[0:1, span_columns] = jnp.sum(
                made * normal_ref[:, span_columns].astype(f32), axis=0, keepdims=True
            )
            side[1:2, span_columns] = jnp.sum(made, axis=0, keepdims=True)
            both = (made * gain_ref[0:1, span_columns] + part_ref[:, span_columns]).astype(bf16)
            low[:, span_columns] = both[:block]
            high[:, span_columns] = both[block:]

    ins = [(array, whole(array)) for array in (turned_back, own, came)]
    ins += [(w, kept_out) for w in weights]
    ins += [(part, whole(part)), (normal, whole(normal))]
    ins += [(gains, whole(gains)), (tables, whole(tables))]
    outs = [full_out((span_rows, columns)), full_out((2, width), f32)]
    outs += [full_out((block, width))] * 2
    scratch = [pltpu.VMEM((spans, depth, columns), bf16), pltpu.SemaphoreType.DMA((spans,))]
    return run(order, flags, kernel, ins, outs, scratch, "project_back")


def weight_sums(order, flags, lefts, rights, by_rows, spans):
    rows = sum(piece.shape[0] for piece in lefts[0][0])
    left_width = sum(group[0].shape[1] for group in lefts[0])
    right_width = sum(group[0].shape[1] for group in rights[0])
    if by_rows:
        tile = left_width // spans
        steps, block = spans // 2, (tile, right_width)
    else:
        tile = min(512, left_width)
        while left_width % tile:
            tile //= 2
        steps, block = left_width // tile, (tile, right_width // 2)
    chunk = min(1024, block[1])
    while right_width % chunk:
        chunk //= 2
    pieces = [
        [piece for groups in (lefts[s], rights[s]) for group in groups for piece in group]
        for s in (0, 1)
    ]
    most = max(len(p) for p in pieces)

    def kernel(flag_ref, *refs):
        piece_refs = (refs[: len(pieces[0])], refs[len(pieces[0]) : len(pieces[0]) + len(pieces[1])])
        keep, send, left, right, flipped, sems = refs[len(pieces[0]) + len(pieces[1]) :]
        g = pl.program_id(0)
        for s in (0, 1):

            @pl.when((g == 0) & (flag_ref[2] == s))
            def _(s=s):
                targets = []
                for held, groups in ((left, lefts[s]), (right, rights[s])):
                    column = 0
                    for group in groups:
                        row, wide = 0, group[0].shape[1]
                        for piece in group:
                            targets.append(
                                held.at[row : row + piece.shape[0], column : column + wide]
                            )
                            row += piece.shape[0]
                        column += wide
                started = copies(
                    piece_refs[s], targets, [sems.at[j] for j in range(len(targets))]
                )
                for copy in started:
                    copy.wait()

        def product(column, store):
            flipped[...] = left[:, pl.ds(pl.multiple_of(column, LANES), tile)].T

            def one(c, _):
                columns = pl.ds(pl.multiple_of(c * chunk, chunk), chunk)
                store(c, plain(flipped[...], right[:, columns]).astype(bf16))
                return 0

            lax.fori_loop(0, right_width // chunk, one, 0)

        if by_rows:

            def to(target):
                def store(c, made):
                    target[:, pl.ds(pl.multiple_of(c * chunk, chunk), chunk)] = made

                return store

            product(g * tile, to(keep))
            product((g + steps) * tile, to(send))
        else:
            half = right_width // 2 // chunk

            def store(c, made):
                @pl.when(c < half)
                def _():
                    keep[:, pl.ds(pl.multiple_of(c * chunk, chunk), chunk)] = made

                @pl.when(c >= half)
                def _():
                    send[:, pl.ds(pl.multiple_of((c - half) * chunk, chunk), chunk)] = made

            product(g * tile, store)

    ins = [(piece, kept_out) for s in (0, 1) for piece in pieces[s]]
    dims = (steps * tile, block[1])
    outs = [(shape(dims), pl.BlockSpec(block, lambda g: (g, 0)))] * 2
    scratch = [
        pltpu.VMEM((rows, left_width), bf16),
        pltpu.VMEM((rows, right_width), bf16),
        pltpu.VMEM((tile, rows), bf16),
        pltpu.SemaphoreType.DMA((most,)),
    ]
    return run(
        order, flags, kernel, ins, outs, scratch, "weight_sums", grid=(steps,)
    )


def fold(order, flags, keep, came, dim):
    rows, columns = keep.shape
    if dim == 0:
        tile = rows // 4
        steps, block = rows // 2 // tile, (tile, columns)
        places = [lambda g: (g, 0), lambda g: (g + steps, 0)]
        half = (rows // 2, columns)
    else:
        tile = rows // 4
        steps, block = rows // tile, (tile, columns // 2)
        places = [lambda g: (g, 0), lambda g: (g, 1)]
        half = (rows, columns // 2)

    def kernel(flag_ref, keep_low, keep_high, came_low, came_high, low, high):
        low[...] = (keep_low[...].astype(f32) + came_low[...].astype(f32)).astype(bf16)
        high[...] = (keep_high[...].astype(f32) + came_high[...].astype(f32)).astype(bf16)

    ins = [(array, pl.BlockSpec(block, place)) for array in (keep, came) for place in places]
    outs = [(shape(half), pl.BlockSpec(block, lambda g: (g, 0)))] * 2
    return run(order, flags, kernel, ins, outs, [], "fold", grid=(steps,))


def shards(
    block_input,
    out_grad,
    triple_weight,
    output_weight,
    expand_weight,
    contract_weight,
    norm_gains,
    norm_biases,
):
    section = lax.axis_index("pipe")
    span = lax.axis_index("ctx")
    lane = lax.axis_index("tp")
    spans = lax.axis_size("ctx")
    lanes = lax.axis_size("tp")
    micros, rows, width = block_input.shape
    span_rows = rows * lanes
    heads = triple_weight.shape[2]
    head_dim = triple_weight.shape[4]
    across_units = heads * head_dim
    scale = head_dim ** (-0.5)
    first_section = section == 0
    both = (0, 1)

    def hop(array, axis, step, sections):
        size = lax.axis_size(axis)
        pairs = [(s * size + a, s * size + (a ^ step)) for s in sections for a in range(size)]
        return lax.ppermute(array, ("pipe", axis), pairs)

    order = Order()

    def flags_for(wanted):
        return jnp.stack([jnp.asarray(wanted), span, section]).astype(jnp.int32)

    flags = [flags_for(section == s) for s in both]
    always = flags_for(1)

    kept = [[SimpleNamespace() for _ in range(micros)] for _ in both]
    due = {}
    slot_index = [0]

    def slot(hops, kernels=()):
        now = slot_index[0]
        slot_index[0] += 1
        ready = due.pop(now, [])
        hops = [h if len(h) == 3 else h + (1,) for h in hops]
        if hops:
            gated = fence([operand for operand, _, _ in hops], order.last + ready)
            order.last = [min(gated, key=lambda array: array.size)]
            for passed, (_, go, slots) in zip(gated, hops):
                results = go(passed)
                results = results if isinstance(results, list) else [results]
                due.setdefault(now + slots, []).extend(results)
        else:
            order.last = order.last + ready
        for kernel in kernels:
            kernel()

    def halved(keep, came, dim):
        middle = keep.shape[dim] // 2
        total = keep.astype(f32) + came.astype(f32)
        return (
            lax.slice_in_dim(total, 0, middle, axis=dim).astype(bf16),
            lax.slice_in_dim(total, middle, 2 * middle, axis=dim).astype(bf16),
        )

    def spread_hops(pieces, axis, axis_name, sections, first):
        step = lax.axis_size(axis_name) // 4
        going = first
        while step:
            pieces.append(hop(going, axis_name, step, sections))
            going = jnp.concatenate(pieces, axis=axis)
            step //= 2
        return pieces[-1]

    def fold_hops(k, first, axis_name, dim, sections):
        step, size = 1, lax.axis_size(axis_name)
        while 2 * step < size:
            came = hop(first, axis_name, step, sections)
            k.keep, k.send = halved(k.keep, came, dim)
            first = k.send
            step *= 2
        return came

    depth = width // spans
    far = spans // 2
    assert depth == across_units
    small = jnp.concatenate([norm_gains[0], norm_biases[0]], axis=0)
    packed = jnp.concatenate(
        [triple_weight[0].reshape(depth, -1), output_weight[0].reshape(-1, depth)],
        axis=1,
    )
    packed = jnp.pad(packed, ((0, 16), (0, 0)))
    packed = lax.dynamic_update_slice(packed, small, (depth, 0))
    own_expand, own_contract = expand_weight[0], contract_weight[0]
    hidden = own_expand.shape[1]
    inputs = xor_blocks(block_input, span, spans)
    cotangent = xor_blocks(out_grad, span, spans)
    early = jnp.where(first_section, inputs, cotangent)

    in_row = jnp.arange(rows, dtype=jnp.int32)
    in_span = jnp.concatenate([(lane ^ j) * rows + in_row for j in doubling(lanes)])
    positions = span * span_rows + in_span
    key_positions = jnp.stack([(span ^ k) * span_rows + in_span for k in doubling(spans)])
    tables = rope_tables(positions)
    position_column = positions[:, None]
    key_positions = key_positions[:, None, :]

    def blocks_of(own, came):
        held, step = {0: own, far: came}, far // 2
        while step:
            for k in list(held):
                held[k ^ step] = hop(held[k], "ctx", step, both)
            step //= 2
        return [held[k] for k in doubling(spans)]

    lane_offsets = doubling(lanes)

    def across(array, j, source):
        pairs = [(source * lanes + a, (1 - source) * lanes + (a ^ j)) for a in range(lanes)]
        return lax.ppermute(array, ("pipe", "tp"), pairs)

    def rows_far(s, m):
        k = kept[s][m]

        def go(passed):
            k.rows = passed
            k.pieces = [passed, hop(passed, "tp", lanes // 2, (s,))]
            return k.pieces[1]

        return k.rows, go

    def rows_near(s, m):
        k = kept[s][m]

        def go(passed):
            last_piece = spread_hops(k.pieces, 0, "tp", (s,), passed)
            k.row_pieces = [piece[None] for piece in k.pieces]
            return last_piece

        return jnp.concatenate(k.pieces, axis=0), go

    def one_way(array, direction, s):
        pairs = [
            (s * spans + a, s * spans + (a ^ far))
            for a in range(spans)
            if direction * ((a ^ far) - a) > 0
        ]
        return lax.ppermute(array, ("pipe", "ctx"), pairs)

    def pair_far(s, m):
        k = kept[s][m]

        def go(passed):
            k.pairs = [passed, one_way(passed, 1, s)]
            return k.pairs[1]

        return k.pair, go

    def pair_near(s, m):
        k = kept[s][m]

        def go(passed):
            return spread_hops(k.pairs, 0, "ctx", (s,), passed)

        return jnp.concatenate(k.pairs, axis=0), go

    def pair_grad_near(s, m):
        k = kept[s][m].pair_grad
        return k.send, lambda passed: fold_hops(k, passed, "ctx", 0, (s,))

    def pair_grad_both(s, m):
        k = kept[s][m].pair_grad

        def go(passed):
            fold_hops(k, passed, "ctx", 0, (s,))
            k.came = one_way(k.send, -1, s)
            return k.came

        return k.send, go

    def pair_grad_far(s, m):
        k = kept[s][m].pair_grad

        def go(passed):
            k.came = one_way(passed, -1, s)
            return k.came

        return k.send, go

    def sum_near(s, k):
        k.keep, going = k.blocks
        return going, lambda passed: fold_hops(k, passed, "tp", 0, (s,))

    def sum_far(s, k):
        def go(passed):
            k.blocks, k.arrived = [k.keep], [hop(passed, "tp", lanes // 2, (s,))]
            return k.arrived[0]

        return k.send, go

    def total_of(k):
        return sum(array.astype(f32) for array in [k.blocks[0], *k.arrived])

    def norm_back(upstream, combined, entering):
        normalized, inverse = normalize(entering.astype(f32))
        return (
            upstream.astype(f32)
            + inverse
            * (
                combined
                - jnp.mean(combined, axis=-1, keepdims=True)
                - normalized * jnp.mean(combined * normalized, axis=-1, keepdims=True)
            )
        ).astype(bf16)

    def middle_of(m):
        return (inputs[m].astype(f32) + total_of(kept[0][m])).astype(bf16)

    def entry_of(m):
        k = kept[1][m]
        return norm_back(cotangent[m], total_of(k), k.rows)

    def hand_one(s, m):
        k, other = kept[s][m], kept[1 - s][m]
        k.given = middle_of(m) if s == 0 else entry_of(m)

        def go(passed):
            k.given = passed
            other.rows = across(passed, 0, s)
            return other.rows

        return k.given, go

    def run_project(s, m):
        k = kept[s][m]
        pieces, place = (early_pieces, m) if s == 0 else (k.row_pieces, 0)
        k.first, k.second, k.normal, k.queries, pair = project(
            order, flags[s], pieces, place, gains, biases, tables, packed, heads, head_dim
        )
        k.pair = pair[None]

    def run_expand(m):
        k = kept[0][m]
        k.active, k.slope = expand_up(order, flags[0], k.second, weights.expand, span_rows)

    def run_attend(m):
        k = kept[0][m]
        k.attended, k.probs = attend(
            order, flags[0], k.queries, k.pairs, position_column, key_positions, scale
        )

    def run_branch(m):
        k = kept[0][m]
        k.blocks = branch_out(
            order, flags[0], [(k.active, k.attended)], contract, packed
        )

    def run_hidden_both(m):
        k = kept[1][m]
        k.upstream, k.active, k.hidden, k.part, k.side_second = hidden_both(
            order,
            flags[1],
            k.second,
            early_pieces,
            m,
            weights.expand,
            contract,
            k.normal,
            gains,
        )

    def run_attend_both(m):
        k = kept[1][m]
        k.attended, k.turned_back, keep, send = attend_both(
            order,
            flags[1],
            k.upstream,
            packed,
            k.queries,
            k.pairs,
            position_column,
            key_positions,
            tables,
            scale,
        )
        k.pair_grad = SimpleNamespace(keep=keep, send=send)

    def run_attend_back(m):
        k = kept[0][m]
        k.upstream, k.turned_back, keep, send = attend_back(
            order,
            flags[0],
            k.row_pieces,
            packed,
            k.queries,
            k.pairs,
            k.probs,
            tables,
            scale,
        )
        k.pair_grad = SimpleNamespace(keep=keep, send=send)

    def run_hidden_back(m):
        k = kept[0][m]
        k.hidden, k.part, k.side_second = hidden_back(
            order,
            flags[0],
            k.upstream,
            contract,
            weights.expand,
            k.slope,
            k.normal,
            gains,
        )

    def run_project_back(s, m):
        k = kept[s][m]
        own, arrived = k.pair_grad.keep, k.pair_grad.came
        k.stacked, k.side_first, *k.blocks = project_back(
            order,
            flags[s],
            k.turned_back,
            own.reshape(own.shape[1:]),
            arrived.reshape(arrived.shape[1:]),
            packed,
            k.part,
            k.normal,
            gains,
            tables,
        )

    def of(name, s, count=micros):
        return [getattr(kept[s][m], name) for m in range(count)]

    branch_sums, expand_sums, triple_sums = (SimpleNamespace(parts=[]) for _ in range(3))

    def run_sums(w, lefts, rights, by_rows):
        w.dim = 0 if by_rows else 1
        w.keep, w.send = weight_sums(order, always, lefts, rights, by_rows, spans)

    def wide_near(w):
        def go(passed):
            w.came = hop(passed, "ctx", 1, both)
            return w.came

        return w.send, go

    def run_fold(w):
        step = 2
        w.keep, w.send = fold(order, always, w.keep, w.came, w.dim)
        while 2 * step < spans:
            w.came = hop(w.send, "ctx", step, both)
            w.keep, w.send = fold(order, always, w.keep, w.came, w.dim)
            step *= 2

    def wide_far(w, start, stop):
        def go(passed):
            w.parts.append(hop(passed, "ctx", far, both))
            return w.parts[-1]

        return w.send[start:stop], go

    weights = SimpleNamespace(expand_came=[], contract_came=[])
    half_depth = depth // 2

    def expand_far(start, stop):
        def go(passed):
            weights.expand_came.append(hop(passed, "ctx", far, both))
            return weights.expand_came[-1]

        return own_expand[start:stop], go

    def packed_far(passed):
        weights.packed_came = hop(passed, "ctx", far, both)
        return weights.packed_came

    def packed_near(passed):
        weights.packed = blocks_of(packed, passed)
        return weights.packed[1:]

    def expand_near(passed):
        weights.expand = blocks_of(own_expand, passed)
        return weights.expand[1:]

    def contract_far(start, stop):
        def go(passed):
            weights.contract_came.append(hop(passed, "ctx", far, both))
            return weights.contract_came[-1]

        return own_contract[start:stop], go

    def contract_near(passed):
        weights.contract = blocks_of(own_contract, passed)
        return weights.contract[1:]

    def early_hops(passed):
        weights.early = [passed] + [hop(passed, "tp", j, both) for j in lane_offsets[1:]]
        return weights.early[1:]

    due[0] = [expand_far(0, half_depth)[1](own_expand[:half_depth])]
    slot([(packed, packed_far), expand_far(half_depth, depth), (early, early_hops)])
    early_pieces = weights.early
    cuts = [0, hidden // 4, 11 * hidden // 16, hidden]
    expand_came = jnp.concatenate(weights.expand_came, axis=0)
    slot(
        [
            (weights.packed_came, packed_near),
            contract_far(cuts[0], cuts[1]),
        ]
    )
    packed = weights.packed
    small_full = jnp.concatenate(
        [piece[depth : depth + 4, :depth] for piece in packed], axis=1
    ).astype(f32)
    gains, biases = small_full[:2], small_full[2:]
    slot(
        [(expand_came, expand_near), contract_far(cuts[1], cuts[2])],
        [lambda m=m: run_project(0, m) for m in range(micros)],
    )
    a, b = kept
    slot(
        [pair_far(0, 0), contract_far(cuts[2], cuts[3])],
        [lambda m=m: run_expand(m) for m in range(micros)],
    )
    contract_came = jnp.concatenate(weights.contract_came, axis=0)
    slot([(contract_came, contract_near), pair_near(0, 0)])
    contract = weights.contract
    slot([pair_far(0, 1)], [lambda: run_attend(0), lambda: run_branch(0)])
    slot([sum_near(0, a[0]), pair_near(0, 1)])
    slot([sum_far(0, a[0]), pair_far(0, 2)], [lambda: run_attend(1), lambda: run_branch(1)])
    slot([hand_one(0, 0), sum_near(0, a[1]), pair_near(0, 2)])
    slot(
        [rows_far(1, 0), sum_far(0, a[1])], [lambda: run_attend(2), lambda: run_branch(2)]
    )
    slot([rows_near(1, 0), hand_one(0, 1), sum_near(0, a[2])])
    slot([rows_far(1, 1), sum_far(0, a[2])], [lambda: run_project(1, 0)])
    slot(
        [pair_far(1, 0), rows_near(1, 1), hand_one(0, 2)], [lambda: run_hidden_both(0)]
    )
    slot([pair_near(1, 0), rows_far(1, 2)], [lambda: run_project(1, 1)])
    slot(
        [pair_far(1, 1), rows_near(1, 2)],
        [lambda: run_attend_both(0), lambda: run_hidden_both(1)],
    )
    slot([pair_grad_near(1, 0), pair_near(1, 1)], [lambda: run_project(1, 2)])
    slot(
        [pair_grad_far(1, 0), pair_far(1, 2)],
        [lambda: run_attend_both(1), lambda: run_hidden_both(2)],
    )
    slot([pair_grad_near(1, 1), pair_near(1, 2)], [lambda: run_project_back(1, 0)])
    slot([sum_near(1, b[0]), pair_grad_far(1, 1)], [lambda: run_attend_both(2)])
    slot([sum_far(1, b[0]), pair_grad_near(1, 2)], [lambda: run_project_back(1, 1)])
    slot([hand_one(1, 0), sum_near(1, b[1]), pair_grad_far(1, 2)])
    slot([sum_far(1, b[1]), rows_far(0, 0)], [lambda: run_project_back(1, 2)])
    slot([sum_near(1, b[2]), hand_one(1, 1), rows_near(0, 0)])
    slot([sum_far(1, b[2]), rows_far(0, 1)], [lambda: run_attend_back(0)])
    slot(
        [hand_one(1, 2), rows_near(0, 1), pair_grad_near(0, 0)],
        [lambda: run_hidden_back(0)],
    )
    slot([rows_far(0, 2), pair_grad_far(0, 0)], [lambda: run_attend_back(1)])
    slot(
        [rows_near(0, 2), pair_grad_near(0, 1)],
        [lambda: run_hidden_back(1), lambda: run_project_back(0, 0)],
    )
    last = micros - 1

    def run_branch_sums():
        run_sums(
            branch_sums,
            [[of("active", s), of("attended", s)] for s in both],
            [
                [of("upstream", 0, last) + [piece[0] for piece in a[last].row_pieces]],
                [of("upstream", 1)],
            ],
            False,
        )

    def run_expand_sums():
        run_sums(
            expand_sums,
            [[of("second", s)] for s in both],
            [[of("hidden", s)] for s in both],
            True,
        )

    def run_triple_sums():
        run_sums(
            triple_sums,
            [[of("first", s)] for s in both],
            [[of("stacked", s)] for s in both],
            True,
        )

    finals = SimpleNamespace()

    def run_final_branch():
        blocks = branch_out(
            order, flags[1], [(k.active, k.attended) for k in b], contract, packed
        )
        finals.keep = jnp.stack(blocks[0::2])
        finals.send = jnp.stack(blocks[1::2])

    def last_near(w, s):
        return w.send, lambda passed: fold_hops(w, passed, "tp", 1, (s,))

    def last_far(w, s):
        def go(passed):
            w.came = hop(passed, "tp", lanes // 2, (s,))
            return w.came

        return w.send, go

    slot([pair_grad_far(0, 1)], [run_branch_sums])
    slot(
        [wide_near(branch_sums)], [lambda: run_attend_back(2), lambda: run_project_back(0, 1)]
    )
    slot([], [lambda: run_fold(branch_sums)])
    cut = [0, 3 * hidden // 8, 7 * hidden // 8, hidden + across_units]
    slot(
        [wide_far(branch_sums, cut[0], cut[1]), pair_grad_both(0, 2)],
        [lambda: run_hidden_back(2)],
    )
    slot(
        [wide_far(branch_sums, cut[1], cut[2])],
        [lambda: run_project_back(0, 2), run_triple_sums],
    )
    outs = SimpleNamespace(
        keep=jnp.stack([k.blocks[0] for k in a]), send=jnp.stack([k.blocks[1] for k in a])
    )

    def side_of(mades):
        return sum(
            jnp.concatenate([k.side_first, k.side_second], axis=0) for k in mades
        )

    side = SimpleNamespace(all=jnp.where(first_section, side_of(a), side_of(b)))

    def side_ctx(passed):
        step = 1
        while step < spans:
            middle = passed.shape[1] // 2
            came = hop(passed[:, middle:], "ctx", step, both)
            passed = passed[:, :middle] + came
            step *= 2
        side.all = passed
        return came

    def side_near(passed):
        step = 1
        while 2 * step < lanes:
            came = hop(passed, "tp", step, both)
            passed = passed + came
            step *= 2
        side.all = passed
        return came

    def side_far(passed):
        came = hop(passed, "tp", lanes // 2, both)
        side.all = passed + came
        return came

    def held_back(w, j):
        def go(passed):
            w.parts[j] = passed
            return []

        return w.parts[j], go

    def wide_total(keep, parts):
        came = jnp.concatenate(parts, axis=0) if len(parts) > 1 else parts[0]
        return keep.astype(f32) + came.astype(f32)

    slot(
        [
            wide_near(triple_sums),
            wide_far(branch_sums, cut[2], cut[3]),
            (side.all, side_ctx),
        ],
        [run_expand_sums, run_final_branch],
    )
    slot([], [lambda: run_fold(triple_sums)])
    slot(
        [
            wide_far(triple_sums, 0, depth),
            wide_near(expand_sums),
            last_near(outs, 0),
            last_near(finals, 1),
            (side.all, side_near),
        ]
    )
    slot([], [lambda: run_fold(expand_sums)])
    slot(
        [
            wide_far(expand_sums, 0, depth),
            last_far(outs, 0),
            last_far(finals, 1),
            (side.all, side_far),
            held_back(triple_sums, 0),
            held_back(branch_sums, 2),
        ]
    )
    triple_grads = wide_total(triple_sums.keep, triple_sums.parts)
    triple_grads = triple_grads.reshape(triple_weight.shape)
    branch_grads = wide_total(branch_sums.keep, branch_sums.parts)
    contract_grads, output_grads = branch_grads[:hidden], branch_grads[hidden:]
    expand_grads = wide_total(expand_sums.keep, expand_sums.parts)
    layer_outputs = jnp.stack(
        [
            jnp.where(
                first_section,
                kept[0][m].given,
                (
                    b[m].rows.astype(f32)
                    + finals.keep[m].astype(f32)
                    + finals.came[m].astype(f32)
                ).astype(bf16),
            )
            for m in range(micros)
        ]
    )
    own_rows = jnp.stack(of("rows", 0))
    entry_grads = jnp.where(
        first_section,
        norm_back(own_rows, outs.keep.astype(f32) + outs.came.astype(f32), inputs),
        jnp.stack(of("given", 1)),
    )
    gain_grads = jnp.stack([side.all[0], side.all[2]])
    bias_grads = jnp.stack([side.all[1], side.all[3]])
    return (
        xor_blocks(layer_outputs, span, spans, inverse=True)[None],
        xor_blocks(entry_grads, span, spans, inverse=True)[None],
        triple_grads,
        output_grads.reshape(output_weight.shape),
        expand_grads[None],
        contract_grads[None],
        gain_grads[None],
        bias_grads[None],
    )


def solution(mesh):
    return jax.shard_map(
        shards,
        mesh=mesh,
        in_specs=(
            P(None, ("ctx", "tp"), None),
            P(None, ("ctx", "tp"), None),
            P("pipe", "ctx", "tp", None, None),
            P("pipe", "tp", None, "ctx"),
            P("pipe", "ctx", "tp"),
            P("pipe", "tp", "ctx"),
            P("pipe", None, "ctx"),
            P("pipe", None, "ctx"),
        ),
        out_specs=(
            P("pipe", None, ("ctx", "tp"), None),
            P("pipe", None, ("ctx", "tp"), None),
            P("pipe", "ctx", "tp", None, None),
            P("pipe", "tp", None, "ctx"),
            P("pipe", "ctx", "tp"),
            P("pipe", "tp", "ctx"),
            P("pipe", None, "ctx"),
            P("pipe", None, "ctx"),
        ),
        check_vma=False,
    )
```

```python
import functools
import math
from types import SimpleNamespace

import jax
import jax.numpy as jnp
from jax import lax
from jax.experimental import pallas as pl
from jax.experimental.pallas import tpu as pltpu
from jax.sharding import PartitionSpec as P

ROT = 64
LANES = 128
epsilon = 1e-05
masked_score = -1e30
f32 = jnp.float32
bf16 = jnp.bfloat16
mebibyte = 1024 * 1024
half_root = 0.7071067811865476
bell = 0.3989422804014327


def dot(a, b, dims):
    return lax.dot_general(a, b, (dims, ((), ())), preferred_element_type=f32)


def plain(a, b):
    return dot(a, b, ((1,), (0,)))


def turned(a, b):
    return dot(a, b, ((1,), (1,)))


def doubling(count):
    order, step = [0], count // 2
    while step:
        order += [k ^ step for k in order]
        step //= 2
    return order


def xor_blocks(values, index, count, inverse=False):
    width = values.shape[-1] // count
    order = doubling(count)

    def taken(places):
        return jnp.concatenate(
            [values[..., k * width : (k + 1) * width] for k in places], axis=-1
        )

    if inverse:
        values = taken([order.index(k) for k in range(count)])
    step = 1
    while step < count:
        swapped = taken([k ^ step for k in range(count)])
        values = jnp.where((index & step) != 0, swapped, values)
        step *= 2
    return values if inverse else taken(order)


def rope_tables(positions):
    half = ROT // 2
    frequency = 10000.0 ** (-jnp.arange(0, ROT, 2, dtype=f32) / ROT)
    angles = positions.astype(f32)[:, None] * frequency[None, :]
    cosine, sine = jnp.cos(angles), jnp.sin(angles)
    count = positions.shape[0]
    rest = jnp.zeros((count, LANES - ROT), f32)
    none = jnp.zeros((count, half), f32)
    return jnp.stack(
        [
            jnp.concatenate([cosine, cosine, rest + 1.0], axis=1),
            jnp.concatenate([-sine, none, rest], axis=1),
            jnp.concatenate([none, sine, rest], axis=1),
        ]
    )


def turn(values, tables, sign):
    half = ROT // 2
    part = values[:, :LANES]
    moved = (
        pltpu.roll(part, LANES - half, 1) * tables[1] + pltpu.roll(part, half, 1) * tables[2]
    )
    part = part * tables[0] + (moved if sign > 0 else -moved)
    return jnp.concatenate([part, values[:, LANES:]], axis=1)


def normalize(values):
    center = values - jnp.mean(values, axis=-1, keepdims=True)
    inverse = lax.rsqrt(jnp.mean(center * center, axis=-1, keepdims=True) + epsilon)
    return (center * inverse, inverse)


def whole(array):
    zeros = (0,) * array.ndim
    return pl.BlockSpec(array.shape, lambda *_: zeros)


def at(block, place):
    return pl.BlockSpec(block, lambda *_: place)


kept_out = pl.BlockSpec(memory_space=pl.ANY)


def shape(dims, dtype=bf16):
    return jax.ShapeDtypeStruct(dims, dtype)


class Order:
    def __init__(self):
        self.last = []

    def follow(self, results):
        self.last = [min(results, key=lambda array: array.size * array.dtype.itemsize)]

    def also(self, array):
        self.last = self.last + [array]


took = dict(
    project=7,
    expand=8,
    attend=5,
    branch=8,
    hidden_both=14,
    attend_both=11,
    attend_back=8,
    hidden_back=13,
    project_back=8,
    weight_sums=16,
    fold=7,
)
peak = 1.15e9


def run(order, flags, kernel, ins, outs, scratch, name, grid=(1,), work=0):
    taken = len(ins)
    ins = [(flags, pl.BlockSpec(memory_space=pltpu.SMEM))] + list(ins)
    ins += [(array, kept_out) for array in order.last]
    arrays = [array for array, _ in ins]
    once = grid == (1,)

    def sized(spec, dtype):
        if spec.block_shape is None:
            return spec, 0
        size = math.prod(spec.block_shape) * jnp.dtype(dtype).itemsize
        if not once:
            return spec, 2 * size
        single = pl.BlockSpec(
            spec.block_shape, spec.index_map, pipeline_mode=pl.Buffered(1)
        )
        return single, size

    in_specs = [sized(spec, array.dtype) for array, spec in ins]
    out_specs = [sized(spec, struct.dtype) for struct, spec in outs]
    held = sum(size for _, size in in_specs + out_specs)
    for buffer in scratch:
        if buffer.memory_space == pltpu.VMEM:
            held += math.prod(buffer.shape) * jnp.dtype(buffer.dtype).itemsize

    def body(flag_ref, *refs):
        @pl.when(flag_ref[0] == 1)
        def _():
            kernel(flag_ref, *refs[:taken], *refs[len(ins) - 1 :])

    results = pl.pallas_call(
        body,
        grid=grid,
        in_specs=[spec for spec, _ in in_specs],
        out_specs=[spec for spec, _ in out_specs],
        out_shape=[struct for struct, _ in outs],
        scratch_shapes=scratch,
        compiler_params=pltpu.CompilerParams(
            vmem_limit_bytes=int(held + (work + 2) * mebibyte)
        ),
        cost_estimate=pl.CostEstimate(
            flops=int(took[name] * peak), bytes_accessed=0, transcendentals=0
        ),
        name=name,
    )(*arrays)
    order.follow(results)
    return results


def fence(through, waits):
    count = len(through)

    def kernel(*refs):
        pass

    return pl.pallas_call(
        kernel,
        in_specs=[kept_out] * (count + len(waits)),
        out_specs=[kept_out] * count,
        out_shape=[shape(array.shape, array.dtype) for array in through],
        input_output_aliases={j: j for j in range(count)},
        compiler_params=pltpu.CompilerParams(vmem_limit_bytes=mebibyte),
        cost_estimate=pl.CostEstimate(flops=1, bytes_accessed=1, transcendentals=0),
        name="fence",
    )(*through, *waits)


def full_out(dims, dtype=bf16):
    zeros = (0,) * len(dims)
    return (shape(dims, dtype), pl.BlockSpec(dims, lambda *_: zeros))


def copies(sources, targets, sems):
    started = []
    for source, target, sem in zip(sources, targets, sems):
        copy = pltpu.make_async_copy(source, target, sem)
        copy.start()
        started.append(copy)
    return started


def project(order, flags, pieces, at_piece, gains, biases, tables, weights, heads, head_dim):
    count, width = 1, pieces[0].shape[2]
    span_rows = sum(piece.shape[1] for piece in pieces)
    rows = count * span_rows
    chunk = pieces[0].shape[1]
    spans = len(weights)
    depth = width // spans
    wide = 3 * head_dim
    columns = heads * wide

    def kernel(flag_ref, *refs):
        piece_refs = refs[: len(pieces)]
        gain_ref, bias_ref, table_ref = refs[len(pieces) : len(pieces) + 3]
        weight_refs = refs[len(pieces) + 3 : len(pieces) + 3 + spans]
        first, second, normal, queries, pair, held, sems = refs[len(pieces) + 3 + spans :]
        started = []
        for h in range(heads):
            started.append(
                copies(
                    [w.at[:depth, h * wide : (h + 1) * wide] for w in weight_refs],
                    [held.at[h, k * depth : (k + 1) * depth] for k in range(spans)],
                    [sems.at[h, k] for k in range(spans)],
                )
            )
        start = 0
        for piece_ref in piece_refs:
            chunks = piece_ref.shape[1] // chunk

            def one(i, _, piece_ref=piece_ref, start=start, chunks=chunks):
                m, c = i // chunks, i % chunks
                values = piece_ref[m, pl.ds(pl.multiple_of(c * chunk, chunk), chunk), :]
                normed, _ = normalize(values.astype(f32))
                to = pl.ds(
                    pl.multiple_of(m * span_rows + start + c * chunk, chunk), chunk
                )
                normal[to, :] = normed.astype(bf16)
                first[to, :] = (normed * gain_ref[0:1] + bias_ref[0:1]).astype(bf16)
                second[to, :] = (normed * gain_ref[1:2] + bias_ref[1:2]).astype(bf16)
                return 0

            lax.fori_loop(0, count * chunks, one, 0)
            start += piece_ref.shape[1]
        for h in range(heads):
            for copy in started[h]:
                copy.wait()

            def two(m, _, h=h):
                to = pl.ds(pl.multiple_of(m * span_rows, span_rows), span_rows)
                made = plain(first[to, :], held[h])
                queries[h, to, :] = turn(made[:, :head_dim], table_ref, 1).astype(bf16)
                pair[0, h, to, :] = turn(
                    made[:, head_dim : 2 * head_dim], table_ref, 1
                ).astype(bf16)
                pair[1, h, to, :] = made[:, 2 * head_dim :].astype(bf16)
                return 0

            lax.fori_loop(0, count, two, 0)

    ins = [(piece, at((1,) + piece.shape[1:], (at_piece, 0, 0))) for piece in pieces]
    ins += [(array, whole(array)) for array in (gains, biases, tables)]
    ins += [(w, kept_out) for w in weights]
    outs = [full_out((rows, width))] * 3 + [
        full_out((heads, rows, head_dim)),
        full_out((2, heads, rows, head_dim)),
    ]
    scratch = [
        pltpu.VMEM((heads, width, wide), bf16),
        pltpu.SemaphoreType.DMA((heads, spans)),
    ]
    return run(order, flags, kernel, ins, outs, scratch, "project")


def expand_up(order, flags, second, weights, span_rows):
    rows, width = second.shape
    depth, hidden = weights[0].shape
    spans = len(weights)
    tile = min(512, hidden)
    tiles = hidden // tile

    def kernel(flag_ref, *refs):
        second_ref, weight_refs = refs[0], refs[1 : 1 + spans]
        active, slope, held, sems = refs[1 + spans :]
        started = []
        for t in range(tiles):
            started.append(
                copies(
                    [w.at[:, t * tile : (t + 1) * tile] for w in weight_refs],
                    [held.at[t, k * depth : (k + 1) * depth] for k in range(spans)],
                    [sems.at[t, k] for k in range(spans)],
                )
            )
        for t in range(tiles):
            for copy in started[t]:
                copy.wait()

            def one(m, _, t=t):
                to = pl.ds(pl.multiple_of(m * span_rows, span_rows), span_rows)
                pre = plain(second_ref[to, :], held[t])
                risen = 0.5 * (1.0 + lax.erf(pre * half_root))
                columns = slice(t * tile, (t + 1) * tile)
                active[to, columns] = (pre * risen).astype(bf16)
                slope[to, columns] = (
                    risen + pre * jnp.exp(-0.5 * pre * pre) * bell
                ).astype(bf16)
                return 0

            lax.fori_loop(0, rows // span_rows, one, 0)

    ins = [(second, whole(second))] + [(w, kept_out) for w in weights]
    outs = [full_out((rows, hidden))] * 2
    scratch = [
        pltpu.VMEM((tiles, width, tile), bf16),
        pltpu.SemaphoreType.DMA((tiles, spans)),
    ]
    return run(order, flags, kernel, ins, outs, scratch, "expand")


def spread(refs):
    return [ref.at[j] for ref in refs for j in range(ref.shape[0])]


def attention(here, pairs, head, row_ref, key_ref, scale):
    scores = []
    for k, pair in enumerate(pairs):
        raw = turned(here, pair[0, head]) * scale
        scores.append(jnp.where(key_ref[k] <= row_ref[...], raw, masked_score))
    top = functools.reduce(
        jnp.maximum, [jnp.max(part, axis=1, keepdims=True) for part in scores]
    )
    scores = [jnp.exp(part - top) for part in scores]
    inverse = 1.0 / sum(jnp.sum(part, axis=1, keepdims=True) for part in scores)
    return [part * inverse for part in scores]


def attend(order, flags, queries, pairs, positions, key_positions, scale):
    heads, rows, head_dim = queries.shape
    spans = sum(pair.shape[0] for pair in pairs)

    def kernel(flag_ref, query_ref, *refs):
        views, refs = spread(refs[: len(pairs)]), refs[len(pairs) :]
        row_ref, key_ref, attended, probs = refs
        for h in range(heads):
            parts = attention(query_ref[h], views, h, row_ref, key_ref, scale)
            summed = None
            for k in range(spans):
                part = parts[k].astype(bf16)
                probs[k, h] = part
                term = plain(part, views[k][1, h])
                summed = term if summed is None else summed + term
            attended[:, h * head_dim : (h + 1) * head_dim] = summed.astype(bf16)

    ins = [
        (array, whole(array)) for array in (queries, *pairs, positions, key_positions)
    ]
    outs = [full_out((rows, heads * head_dim)), full_out((spans, heads, rows, rows))]
    work = spans * rows * rows * 4 * heads * 4 / mebibyte
    return run(order, flags, kernel, ins, outs, [], "attend", work=work)


def attention_grads(grad, here, parts, views, head, keep, send, scale):
    half = keep.shape[0]
    grad_probs = [turned(grad, view[1, head]) for view in views]
    delta = sum(
        jnp.sum(part.astype(f32) * slope, axis=1, keepdims=True)
        for part, slope in zip(parts, grad_probs)
    )
    query_grad = None
    for k, view in enumerate(views):
        slopes = (parts[k].astype(f32) * (grad_probs[k] - delta)).astype(bf16)
        term = plain(slopes, view[0, head])
        query_grad = term if query_grad is None else query_grad + term
        side = keep if k < half else send
        side[k % half, 0, head] = (dot(slopes, here, ((0,), (0,))) * scale).astype(bf16)
        side[k % half, 1, head] = dot(parts[k].astype(bf16), grad, ((0,), (0,))).astype(bf16)
    return query_grad * scale


def attend_both(
    order, flags, rows_in, packed, queries, pairs, positions, key_positions, tables, scale
):
    heads, rows, head_dim = queries.shape
    width = rows_in.shape[1]
    spans = len(packed)
    across, depth = heads * head_dim, width // spans
    half = spans // 2

    def kernel(flag_ref, rows_ref, *refs):
        packed_refs, refs = refs[:spans], refs[spans:]
        query_ref, refs = refs[0], refs[1:]
        views, refs = spread(refs[: len(pairs)]), refs[len(pairs) :]
        row_ref, key_ref, table_ref, attended, turned_back, keep, send, held, sems = refs
        started = copies(
            [w.at[:across, 3 * across : 3 * across + depth] for w in packed_refs],
            [held.at[:, k * depth : (k + 1) * depth] for k in range(spans)],
            [sems.at[k] for k in range(spans)],
        )
        all_parts = []
        for h in range(heads):
            parts = attention(query_ref[h], views, h, row_ref, key_ref, scale)
            summed = None
            for k in range(spans):
                term = plain(parts[k].astype(bf16), views[k][1, h])
                summed = term if summed is None else summed + term
            attended[:, h * head_dim : (h + 1) * head_dim] = summed.astype(bf16)
            all_parts.append(parts)
        for copy in started:
            copy.wait()
        grads = turned(rows_ref[...], held[...]).astype(bf16)
        for h in range(heads):
            made = attention_grads(
                grads[:, h * head_dim : (h + 1) * head_dim],
                query_ref[h],
                all_parts[h],
                views,
                h,
                keep,
                send,
                scale,
            )
            turned_back[h] = turn(made, table_ref, -1).astype(bf16)

    ins = [(rows_in, whole(rows_in))] + [(w, kept_out) for w in packed]
    ins += [
        (array, whole(array)) for array in (queries, *pairs, positions, key_positions, tables)
    ]
    outs = [full_out((rows, across)), full_out((heads, rows, head_dim))]
    outs += [full_out((half, 2, heads, rows, head_dim))] * 2
    scratch = [pltpu.VMEM((across, width), bf16), pltpu.SemaphoreType.DMA((spans,))]
    work = spans * rows * rows * 4 * (heads + 4) / mebibyte
    return run(order, flags, kernel, ins, outs, scratch, "attend_both", work=work)


def hidden_both(order, flags, second, pieces, at_piece, expand, contract, normal, gains):
    rows, width = second.shape
    hidden, depth = contract[0].shape
    spans = len(contract)
    tile = min(512, hidden)
    tiles = hidden // tile

    def kernel(flag_ref, second_ref, *refs):
        piece_refs, refs = refs[: len(pieces)], refs[len(pieces) :]
        expand_refs, refs = refs[:spans], refs[spans:]
        contract_refs, refs = refs[:spans], refs[spans:]
        normal_ref, gain_ref, rows_out, active, grads, part, side, *refs = refs
        held_up, held_down, sems_up, sems_down = refs
        started = []
        for t in range(tiles):
            block = slice(t * tile, (t + 1) * tile)
            places = [slice(k * depth, (k + 1) * depth) for k in range(spans)]
            up = copies(
                [w.at[:, block] for w in expand_refs],
                [held_up.at[place, block] for place in places],
                [sems_up.at[t, k] for k in range(spans)],
            )
            down = copies(
                [w.at[block, :] for w in contract_refs],
                [held_down.at[block, place] for place in places],
                [sems_down.at[t, k] for k in range(spans)],
            )
            started.append((up, down))
        start = 0
        for piece_ref in piece_refs:
            size = piece_ref.shape[1]
            rows_out[start : start + size, :] = piece_ref[0]
            start += size
        for t in range(tiles):
            block = slice(t * tile, (t + 1) * tile)
            for copy in started[t][0] + started[t][1]:
                copy.wait()
            pre = plain(second_ref[...], held_up[:, block])
            risen = 0.5 * (1.0 + lax.erf(pre * half_root))
            active[:, block] = (pre * risen).astype(bf16)
            slope = risen + pre * jnp.exp(-0.5 * pre * pre) * bell
            grads[:, block] = (turned(rows_out[...], held_down[block, :]) * slope).astype(bf16)
        for k in range(spans):
            place = slice(k * depth, (k + 1) * depth)
            made = turned(grads[...], held_up[place, :])
            side[0:1, place] = jnp.sum(
                made * normal_ref[:, place].astype(f32), axis=0, keepdims=True
            )
            side[1:2, place] = jnp.sum(made, axis=0, keepdims=True)
            part[:, place] = made * gain_ref[1:2, place]

    ins = [(second, whole(second))]
    ins += [(piece, at((1,) + piece.shape[1:], (at_piece, 0, 0))) for piece in pieces]
    ins += [(w, kept_out) for w in expand] + [(w, kept_out) for w in contract]
    ins += [(normal, whole(normal)), (gains, whole(gains))]
    outs = [
        full_out((rows, width)),
        full_out((rows, hidden)),
        full_out((rows, hidden)),
        full_out((rows, width), f32),
        full_out((2, width), f32),
    ]
    scratch = [
        pltpu.VMEM((width, hidden), bf16),
        pltpu.VMEM((hidden, width), bf16),
        pltpu.SemaphoreType.DMA((tiles, spans)),
        pltpu.SemaphoreType.DMA((tiles, spans)),
    ]
    return run(order, flags, kernel, ins, outs, scratch, "hidden_both")


def branch_out(order, flags, groups, contract, packed):
    hidden, depth = contract[0].shape
    across = groups[0][1].shape[1]
    spans = len(contract)
    width = depth * spans
    span_rows = groups[0][0].shape[0]
    block = span_rows // 2
    count = len(groups)

    def kernel(flag_ref, *refs):
        group_refs, refs = refs[: 2 * count], refs[2 * count :]
        contract_refs, packed_refs = refs[:spans], refs[spans : 2 * spans]
        blocks, refs = refs[2 * spans : 2 * (spans + count)], refs[2 * (spans + count) :]
        held, held_out, sems = refs
        outputs = [w.at[:across, 3 * across : 3 * across + depth] for w in packed_refs]
        started = copies(
            [ref for k in range(spans) for ref in (outputs[k], contract_refs[k])],
            [ref for k in range(spans) for ref in (held_out.at[k], held.at[k])],
            [sems.at[j] for j in range(2 * spans)],
        )
        for k in range(spans):
            started[2 * k].wait()
            started[2 * k + 1].wait()
            columns = slice(k * depth, (k + 1) * depth)
            for c in range(count):
                made = plain(group_refs[2 * c + 1][...], held_out[k])
                made = made + plain(group_refs[2 * c][...], held[k])
                blocks[2 * c][:, columns] = made[:block].astype(bf16)
                blocks[2 * c + 1][:, columns] = made[block:].astype(bf16)

    ins = []
    for active, attended in groups:
        ins += [(active, whole(active)), (attended, whole(attended))]
    ins += [(w, kept_out) for w in contract] + [(w, kept_out) for w in packed]
    outs = [full_out((block, width))] * (2 * count)
    scratch = [
        pltpu.VMEM((spans, hidden, depth), bf16),
        pltpu.VMEM((spans, across, depth), bf16),
        pltpu.SemaphoreType.DMA((2 * spans,)),
    ]
    return run(order, flags, kernel, ins, outs, scratch, "branch")


def attend_back(order, flags, pieces, packed, queries, pairs, probs, tables, scale):
    rows = sum(piece.shape[1] for piece in pieces)
    width = pieces[0].shape[2]
    heads, _, head_dim = queries.shape
    spans = len(packed)
    across, depth = heads * head_dim, width // spans
    half = spans // 2

    def kernel(flag_ref, *refs):
        piece_refs, refs = refs[: len(pieces)], refs[len(pieces) :]
        packed_refs, refs = refs[:spans], refs[spans:]
        query_ref, refs = refs[0], refs[1:]
        views, refs = spread(refs[: len(pairs)]), refs[len(pairs) :]
        prob_ref, table_ref, rows_out, turned_back, keep, send, held, sems = refs
        started = copies(
            [w.at[:across, 3 * across : 3 * across + depth] for w in packed_refs],
            [held.at[:, k * depth : (k + 1) * depth] for k in range(spans)],
            [sems.at[k] for k in range(spans)],
        )
        start = 0
        for piece_ref in piece_refs:
            size = piece_ref.shape[1]
            rows_out[start : start + size, :] = piece_ref[0]
            start += size
        for copy in started:
            copy.wait()
        grads = turned(rows_out[...], held[...]).astype(bf16)
        for h in range(heads):
            made = attention_grads(
                grads[:, h * head_dim : (h + 1) * head_dim],
                query_ref[h],
                [prob_ref[k, h] for k in range(spans)],
                views,
                h,
                keep,
                send,
                scale,
            )
            turned_back[h] = turn(made, table_ref, -1).astype(bf16)

    ins = [(piece, whole(piece)) for piece in pieces] + [(w, kept_out) for w in packed]
    ins += [(array, whole(array)) for array in (queries, *pairs, probs, tables)]
    outs = [full_out((rows, width)), full_out((heads, rows, head_dim))]
    outs += [full_out((half, 2, heads, rows, head_dim))] * 2
    scratch = [pltpu.VMEM((across, width), bf16), pltpu.SemaphoreType.DMA((spans,))]
    work = spans * rows * rows * 4 * 4 / mebibyte
    return run(order, flags, kernel, ins, outs, scratch, "attend_back", work=work)


def hidden_back(order, flags, upstream, contract, expand, slope, normal, gains):
    span_rows, width = upstream.shape
    hidden, depth = contract[0].shape
    spans = len(contract)
    tile = min(512, hidden)
    tiles = hidden // tile

    def kernel(flag_ref, *refs):
        upstream_ref, refs = refs[0], refs[1:]
        contract_refs, refs = refs[:spans], refs[spans:]
        expand_refs, refs = refs[:spans], refs[spans:]
        slope_ref, normal_ref, gain_ref, grads, part, side, held, held_up, sems, sems_up = refs
        started = [
            copies(
                [w.at[t * tile : (t + 1) * tile, :] for w in contract_refs],
                [held.at[t, :, k * depth : (k + 1) * depth] for k in range(spans)],
                [sems.at[t, k] for k in range(spans)],
            )
            for t in range(tiles)
        ]
        started_up = copies(
            expand_refs, [held_up.at[k] for k in range(spans)], [sems_up.at[k] for k in range(spans)]
        )
        for t in range(tiles):
            for copy in started[t]:
                copy.wait()
            columns = slice(t * tile, (t + 1) * tile)
            grads[:, columns] = (
                turned(upstream_ref[...], held[t]) * slope_ref[:, columns].astype(f32)
            ).astype(bf16)
        for k in range(spans):
            started_up[k].wait()
            made = turned(grads[...], held_up[k])
            columns = slice(k * depth, (k + 1) * depth)
            side[0:1, columns] = jnp.sum(
                made * normal_ref[:, columns].astype(f32), axis=0, keepdims=True
            )
            side[1:2, columns] = jnp.sum(made, axis=0, keepdims=True)
            part[:, columns] = made * gain_ref[1:2, columns]

    ins = [(upstream, whole(upstream))]
    ins += [(w, kept_out) for w in contract] + [(w, kept_out) for w in expand]
    ins += [
        (slope, whole(slope)),
        (normal, whole(normal)),
        (gains, whole(gains)),
    ]
    outs = [
        full_out((span_rows, hidden)),
        full_out((span_rows, width), f32),
        full_out((2, width), f32),
    ]
    scratch = [
        pltpu.VMEM((tiles, tile, width), bf16),
        pltpu.VMEM((spans, depth, hidden), bf16),
        pltpu.SemaphoreType.DMA((tiles, spans)),
        pltpu.SemaphoreType.DMA((spans,)),
    ]
    return run(order, flags, kernel, ins, outs, scratch, "hidden_back")


def project_back(
    order, flags, turned_back, own, came, weights, part, normal, gains, tables
):
    heads, span_rows, head_dim = turned_back.shape
    spans = len(weights)
    width = part.shape[1]
    depth, columns = width // spans, 3 * heads * head_dim
    block = span_rows // 2

    def kernel(flag_ref, *refs):
        query_ref, own_ref, came_ref, refs = refs[0], refs[1], refs[2], refs[3:]
        weight_refs, refs = refs[:spans], refs[spans:]
        part_ref, normal_ref, gain_ref, table_ref, grads, side, *refs = refs
        low, high, held, sems = refs
        started = copies(
            [w.at[:depth, :columns] for w in weight_refs],
            [held.at[k] for k in range(spans)],
            [sems.at[k] for k in range(spans)],
        )
        for h in range(heads):
            at_column = h * 3 * head_dim
            keys = own_ref[0, h].astype(f32) + came_ref[0, h].astype(f32)
            values = own_ref[1, h].astype(f32) + came_ref[1, h].astype(f32)
            grads[:, at_column : at_column + head_dim] = query_ref[h]
            grads[:, at_column + head_dim : at_column + 2 * head_dim] = turn(
                keys, table_ref, -1
            ).astype(bf16)
            grads[:, at_column + 2 * head_dim : at_column + 3 * head_dim] = values.astype(bf16)
        for k in range(spans):
            started[k].wait()
            made = turned(grads[...], held[k])
            span_columns = slice(k * depth, (k + 1) * depth)
            side[0:1, span_columns] = jnp.sum(
                made * normal_ref[:, span_columns].astype(f32), axis=0, keepdims=True
            )
            side[1:2, span_columns] = jnp.sum(made, axis=0, keepdims=True)
            both = (made * gain_ref[0:1, span_columns] + part_ref[:, span_columns]).astype(bf16)
            low[:, span_columns] = both[:block]
            high[:, span_columns] = both[block:]

    ins = [(array, whole(array)) for array in (turned_back, own, came)]
    ins += [(w, kept_out) for w in weights]
    ins += [(part, whole(part)), (normal, whole(normal))]
    ins += [(gains, whole(gains)), (tables, whole(tables))]
    outs = [full_out((span_rows, columns)), full_out((2, width), f32)]
    outs += [full_out((block, width))] * 2
    scratch = [pltpu.VMEM((spans, depth, columns), bf16), pltpu.SemaphoreType.DMA((spans,))]
    return run(order, flags, kernel, ins, outs, scratch, "project_back")


def weight_sums(order, flags, lefts, rights, by_rows, spans):
    rows = sum(piece.shape[0] for piece in lefts[0][0])
    left_width = sum(group[0].shape[1] for group in lefts[0])
    right_width = sum(group[0].shape[1] for group in rights[0])
    if by_rows:
        tile = left_width // spans
        steps, block = spans // 2, (tile, right_width)
    else:
        tile = min(512, left_width)
        while left_width % tile:
            tile //= 2
        steps, block = left_width // tile, (tile, right_width // 2)
    chunk = min(1024, block[1])
    while right_width % chunk:
        chunk //= 2
    pieces = [
        [piece for groups in (lefts[s], rights[s]) for group in groups for piece in group]
        for s in (0, 1)
    ]
    most = max(len(p) for p in pieces)

    def kernel(flag_ref, *refs):
        piece_refs = (refs[: len(pieces[0])], refs[len(pieces[0]) : len(pieces[0]) + len(pieces[1])])
        keep, send, left, right, flipped, sems = refs[len(pieces[0]) + len(pieces[1]) :]
        g = pl.program_id(0)
        for s in (0, 1):

            @pl.when((g == 0) & (flag_ref[2] == s))
            def _(s=s):
                targets = []
                for held, groups in ((left, lefts[s]), (right, rights[s])):
                    column = 0
                    for group in groups:
                        row, wide = 0, group[0].shape[1]
                        for piece in group:
                            targets.append(
                                held.at[row : row + piece.shape[0], column : column + wide]
                            )
                            row += piece.shape[0]
                        column += wide
                started = copies(
                    piece_refs[s], targets, [sems.at[j] for j in range(len(targets))]
                )
                for copy in started:
                    copy.wait()

        def product(column, store):
            flipped[...] = left[:, pl.ds(pl.multiple_of(column, LANES), tile)].T

            def one(c, _):
                columns = pl.ds(pl.multiple_of(c * chunk, chunk), chunk)
                store(c, plain(flipped[...], right[:, columns]).astype(bf16))
                return 0

            lax.fori_loop(0, right_width // chunk, one, 0)

        if by_rows:

            def to(target):
                def store(c, made):
                    target[:, pl.ds(pl.multiple_of(c * chunk, chunk), chunk)] = made

                return store

            product(g * tile, to(keep))
            product((g + steps) * tile, to(send))
        else:
            half = right_width // 2 // chunk

            def store(c, made):
                @pl.when(c < half)
                def _():
                    keep[:, pl.ds(pl.multiple_of(c * chunk, chunk), chunk)] = made

                @pl.when(c >= half)
                def _():
                    send[:, pl.ds(pl.multiple_of((c - half) * chunk, chunk), chunk)] = made

            product(g * tile, store)

    ins = [(piece, kept_out) for s in (0, 1) for piece in pieces[s]]
    dims = (steps * tile, block[1])
    outs = [(shape(dims), pl.BlockSpec(block, lambda g: (g, 0)))] * 2
    scratch = [
        pltpu.VMEM((rows, left_width), bf16),
        pltpu.VMEM((rows, right_width), bf16),
        pltpu.VMEM((tile, rows), bf16),
        pltpu.SemaphoreType.DMA((most,)),
    ]
    return run(
        order, flags, kernel, ins, outs, scratch, "weight_sums", grid=(steps,)
    )


def fold(order, flags, keep, came, dim):
    rows, columns = keep.shape
    if dim == 0:
        tile = rows // 4
        steps, block = rows // 2 // tile, (tile, columns)
        places = [lambda g: (g, 0), lambda g: (g + steps, 0)]
        half = (rows // 2, columns)
    else:
        tile = rows // 4
        steps, block = rows // tile, (tile, columns // 2)
        places = [lambda g: (g, 0), lambda g: (g, 1)]
        half = (rows, columns // 2)

    def kernel(flag_ref, keep_low, keep_high, came_low, came_high, low, high):
        low[...] = (keep_low[...].astype(f32) + came_low[...].astype(f32)).astype(bf16)
        high[...] = (keep_high[...].astype(f32) + came_high[...].astype(f32)).astype(bf16)

    ins = [(array, pl.BlockSpec(block, place)) for array in (keep, came) for place in places]
    outs = [(shape(half), pl.BlockSpec(block, lambda g: (g, 0)))] * 2
    return run(order, flags, kernel, ins, outs, [], "fold", grid=(steps,))


def shards(
    block_input,
    out_grad,
    triple_weight,
    output_weight,
    expand_weight,
    contract_weight,
    norm_gains,
    norm_biases,
):
    section = lax.axis_index("pipe")
    span = lax.axis_index("ctx")
    lane = lax.axis_index("tp")
    spans = lax.axis_size("ctx")
    lanes = lax.axis_size("tp")
    micros, rows, width = block_input.shape
    span_rows = rows * lanes
    heads = triple_weight.shape[2]
    head_dim = triple_weight.shape[4]
    across_units = heads * head_dim
    scale = head_dim ** (-0.5)
    first_section = section == 0
    both = (0, 1)

    def hop(array, axis, step, sections):
        size = lax.axis_size(axis)
        pairs = [(s * size + a, s * size + (a ^ step)) for s in sections for a in range(size)]
        return lax.ppermute(array, ("pipe", axis), pairs)

    order = Order()

    def flags_for(wanted):
        return jnp.stack([jnp.asarray(wanted), span, section]).astype(jnp.int32)

    flags = [flags_for(section == s) for s in both]
    always = flags_for(1)

    kept = [[SimpleNamespace() for _ in range(micros)] for _ in both]
    due = {}
    slot_index = [0]

    def slot(hops, kernels=()):
        now = slot_index[0]
        slot_index[0] += 1
        ready = due.pop(now, [])
        hops = [h if len(h) == 3 else h + (1,) for h in hops]
        if hops:
            gated = fence([operand for operand, _, _ in hops], order.last + ready)
            order.last = [min(gated, key=lambda array: array.size)]
            for passed, (_, go, slots) in zip(gated, hops):
                results = go(passed)
                results = results if isinstance(results, list) else [results]
                due.setdefault(now + slots, []).extend(results)
        else:
            order.last = order.last + ready
        for kernel in kernels:
            kernel()

    def halved(keep, came, dim):
        middle = keep.shape[dim] // 2
        total = keep.astype(f32) + came.astype(f32)
        return (
            lax.slice_in_dim(total, 0, middle, axis=dim).astype(bf16),
            lax.slice_in_dim(total, middle, 2 * middle, axis=dim).astype(bf16),
        )

    def spread_hops(pieces, axis, axis_name, sections, first):
        step = lax.axis_size(axis_name) // 4
        going = first
        while step:
            pieces.append(hop(going, axis_name, step, sections))
            going = jnp.concatenate(pieces, axis=axis)
            step //= 2
        return pieces[-1]

    def fold_hops(k, first, axis_name, dim, sections):
        step, size = 1, lax.axis_size(axis_name)
        while 2 * step < size:
            came = hop(first, axis_name, step, sections)
            k.keep, k.send = halved(k.keep, came, dim)
            first = k.send
            step *= 2
        return came

    depth = width // spans
    far = spans // 2
    assert depth == across_units
    small = jnp.concatenate([norm_gains[0], norm_biases[0]], axis=0)
    packed = jnp.concatenate(
        [triple_weight[0].reshape(depth, -1), output_weight[0].reshape(-1, depth)],
        axis=1,
    )
    packed = jnp.pad(packed, ((0, 16), (0, 0)))
    packed = lax.dynamic_update_slice(packed, small, (depth, 0))
    own_expand, own_contract = expand_weight[0], contract_weight[0]
    hidden = own_expand.shape[1]
    inputs = xor_blocks(block_input, span, spans)
    cotangent = xor_blocks(out_grad, span, spans)
    early = jnp.where(first_section, inputs, cotangent)

    in_row = jnp.arange(rows, dtype=jnp.int32)
    in_span = jnp.concatenate([(lane ^ j) * rows + in_row for j in doubling(lanes)])
    positions = span * span_rows + in_span
    key_positions = jnp.stack([(span ^ k) * span_rows + in_span for k in doubling(spans)])
    tables = rope_tables(positions)
    position_column = positions[:, None]
    key_positions = key_positions[:, None, :]

    def blocks_of(own, came):
        held, step = {0: own, far: came}, far // 2
        while step:
            for k in list(held):
                held[k ^ step] = hop(held[k], "ctx", step, both)
            step //= 2
        return [held[k] for k in doubling(spans)]

    lane_offsets = doubling(lanes)

    def across(array, j, source):
        pairs = [(source * lanes + a, (1 - source) * lanes + (a ^ j)) for a in range(lanes)]
        return lax.ppermute(array, ("pipe", "tp"), pairs)

    def rows_far(s, m):
        k = kept[s][m]

        def go(passed):
            k.rows = passed
            k.pieces = [passed, hop(passed, "tp", lanes // 2, (s,))]
            return k.pieces[1]

        return k.rows, go

    def rows_near(s, m):
        k = kept[s][m]

        def go(passed):
            last_piece = spread_hops(k.pieces, 0, "tp", (s,), passed)
            k.row_pieces = [piece[None] for piece in k.pieces]
            return last_piece

        return jnp.concatenate(k.pieces, axis=0), go

    def one_way(array, direction, s):
        pairs = [
            (s * spans + a, s * spans + (a ^ far))
            for a in range(spans)
            if direction * ((a ^ far) - a) > 0
        ]
        return lax.ppermute(array, ("pipe", "ctx"), pairs)

    def pair_far(s, m):
        k = kept[s][m]

        def go(passed):
            k.pairs = [passed, one_way(passed, 1, s)]
            return k.pairs[1]

        return k.pair, go

    def pair_near(s, m):
        k = kept[s][m]

        def go(passed):
            return spread_hops(k.pairs, 0, "ctx", (s,), passed)

        return jnp.concatenate(k.pairs, axis=0), go

    def pair_grad_near(s, m):
        k = kept[s][m].pair_grad
        return k.send, lambda passed: fold_hops(k, passed, "ctx", 0, (s,))

    def pair_grad_both(s, m):
        k = kept[s][m].pair_grad

        def go(passed):
            fold_hops(k, passed, "ctx", 0, (s,))
            k.came = one_way(k.send, -1, s)
            return k.came

        return k.send, go

    def pair_grad_far(s, m):
        k = kept[s][m].pair_grad

        def go(passed):
            k.came = one_way(passed, -1, s)
            return k.came

        return k.send, go

    def sum_near(s, k):
        k.keep, going = k.blocks
        return going, lambda passed: fold_hops(k, passed, "tp", 0, (s,))

    def sum_far(s, k):
        def go(passed):
            k.blocks, k.arrived = [k.keep], [hop(passed, "tp", lanes // 2, (s,))]
            return k.arrived[0]

        return k.send, go

    def total_of(k):
        return sum(array.astype(f32) for array in [k.blocks[0], *k.arrived])

    def norm_back(upstream, combined, entering):
        normalized, inverse = normalize(entering.astype(f32))
        return (
            upstream.astype(f32)
            + inverse
            * (
                combined
                - jnp.mean(combined, axis=-1, keepdims=True)
                - normalized * jnp.mean(combined * normalized, axis=-1, keepdims=True)
            )
        ).astype(bf16)

    def middle_of(m):
        return (inputs[m].astype(f32) + total_of(kept[0][m])).astype(bf16)

    def entry_of(m):
        k = kept[1][m]
        return norm_back(cotangent[m], total_of(k), k.rows)

    def hand_one(s, m):
        k, other = kept[s][m], kept[1 - s][m]
        k.given = middle_of(m) if s == 0 else entry_of(m)

        def go(passed):
            k.given = passed
            other.rows = across(passed, 0, s)
            return other.rows

        return k.given, go

    def run_project(s, m):
        k = kept[s][m]
        pieces, place = (early_pieces, m) if s == 0 else (k.row_pieces, 0)
        k.first, k.second, k.normal, k.queries, pair = project(
            order, flags[s], pieces, place, gains, biases, tables, packed, heads, head_dim
        )
        k.pair = pair[None]

    def run_expand(m):
        k = kept[0][m]
        k.active, k.slope = expand_up(order, flags[0], k.second, weights.expand, span_rows)

    def run_attend(m):
        k = kept[0][m]
        k.attended, k.probs = attend(
            order, flags[0], k.queries, k.pairs, position_column, key_positions, scale
        )

    def run_branch(m):
        k = kept[0][m]
        k.blocks = branch_out(
            order, flags[0], [(k.active, k.attended)], contract, packed
        )

    def run_hidden_both(m):
        k = kept[1][m]
        k.upstream, k.active, k.hidden, k.part, k.side_second = hidden_both(
            order,
            flags[1],
            k.second,
            early_pieces,
            m,
            weights.expand,
            contract,
            k.normal,
            gains,
        )

    def run_attend_both(m):
        k = kept[1][m]
        k.attended, k.turned_back, keep, send = attend_both(
            order,
            flags[1],
            k.upstream,
            packed,
            k.queries,
            k.pairs,
            position_column,
            key_positions,
            tables,
            scale,
        )
        k.pair_grad = SimpleNamespace(keep=keep, send=send)

    def run_attend_back(m):
        k = kept[0][m]
        k.upstream, k.turned_back, keep, send = attend_back(
            order,
            flags[0],
            k.row_pieces,
            packed,
            k.queries,
            k.pairs,
            k.probs,
            tables,
            scale,
        )
        k.pair_grad = SimpleNamespace(keep=keep, send=send)

    def run_hidden_back(m):
        k = kept[0][m]
        k.hidden, k.part, k.side_second = hidden_back(
            order,
            flags[0],
            k.upstream,
            contract,
            weights.expand,
            k.slope,
            k.normal,
            gains,
        )

    def run_project_back(s, m):
        k = kept[s][m]
        own, arrived = k.pair_grad.keep, k.pair_grad.came
        k.stacked, k.side_first, *k.blocks = project_back(
            order,
            flags[s],
            k.turned_back,
            own.reshape(own.shape[1:]),
            arrived.reshape(arrived.shape[1:]),
            packed,
            k.part,
            k.normal,
            gains,
            tables,
        )

    def of(name, s, count=micros):
        return [getattr(kept[s][m], name) for m in range(count)]

    branch_sums, expand_sums, triple_sums = (SimpleNamespace(parts=[]) for _ in range(3))

    def run_sums(w, lefts, rights, by_rows):
        w.dim = 0 if by_rows else 1
        w.keep, w.send = weight_sums(order, always, lefts, rights, by_rows, spans)

    def wide_near(w):
        def go(passed):
            w.came = hop(passed, "ctx", 1, both)
            return w.came

        return w.send, go

    def run_fold(w):
        step = 2
        w.keep, w.send = fold(order, always, w.keep, w.came, w.dim)
        while 2 * step < spans:
            w.came = hop(w.send, "ctx", step, both)
            w.keep, w.send = fold(order, always, w.keep, w.came, w.dim)
            step *= 2

    def wide_far(w, start, stop):
        def go(passed):
            w.parts.append(hop(passed, "ctx", far, both))
            return w.parts[-1]

        return w.send[start:stop], go

    weights = SimpleNamespace(expand_came=[], contract_came=[])
    half_depth = depth // 2

    def expand_far(start, stop):
        def go(passed):
            weights.expand_came.append(hop(passed, "ctx", far, both))
            return weights.expand_came[-1]

        return own_expand[start:stop], go

    def packed_far(passed):
        weights.packed_came = hop(passed, "ctx", far, both)
        return weights.packed_came

    def packed_near(passed):
        weights.packed = blocks_of(packed, passed)
        return weights.packed[1:]

    def expand_near(passed):
        weights.expand = blocks_of(own_expand, passed)
        return weights.expand[1:]

    def contract_far(start, stop):
        def go(passed):
            weights.contract_came.append(hop(passed, "ctx", far, both))
            return weights.contract_came[-1]

        return own_contract[start:stop], go

    def contract_near(passed):
        weights.contract = blocks_of(own_contract, passed)
        return weights.contract[1:]

    def early_hops(passed):
        weights.early = [passed] + [hop(passed, "tp", j, both) for j in lane_offsets[1:]]
        return weights.early[1:]

    due[0] = [expand_far(0, half_depth)[1](own_expand[:half_depth])]
    slot([(packed, packed_far), expand_far(half_depth, depth), (early, early_hops)])
    early_pieces = weights.early
    cuts = [0, hidden // 4, 11 * hidden // 16, hidden]
    expand_came = jnp.concatenate(weights.expand_came, axis=0)
    slot(
        [
            (weights.packed_came, packed_near),
            (expand_came, expand_near),
            contract_far(cuts[0], cuts[1]),
        ]
    )
    packed = weights.packed
    small_full = jnp.concatenate(
        [piece[depth : depth + 4, :depth] for piece in packed], axis=1
    ).astype(f32)
    gains, biases = small_full[:2], small_full[2:]
    slot(
        [contract_far(cuts[1], cuts[2])],
        [lambda m=m: run_project(0, m) for m in range(micros)],
    )
    a, b = kept
    slot(
        [pair_far(0, 0), contract_far(cuts[2], cuts[3])],
        [lambda m=m: run_expand(m) for m in range(micros)],
    )
    contract_came = jnp.concatenate(weights.contract_came, axis=0)
    slot([(contract_came, contract_near), pair_near(0, 0)])
    contract = weights.contract
    slot([pair_far(0, 1)], [lambda: run_attend(0), lambda: run_branch(0)])
    slot([sum_near(0, a[0]), pair_near(0, 1)])
    slot([sum_far(0, a[0]), pair_far(0, 2)], [lambda: run_attend(1), lambda: run_branch(1)])
    slot([hand_one(0, 0), sum_near(0, a[1]), pair_near(0, 2)])
    slot(
        [rows_far(1, 0), sum_far(0, a[1])], [lambda: run_attend(2), lambda: run_branch(2)]
    )
    slot([rows_near(1, 0), hand_one(0, 1), sum_near(0, a[2])])
    slot([rows_far(1, 1), sum_far(0, a[2])], [lambda: run_project(1, 0)])
    slot(
        [pair_far(1, 0), rows_near(1, 1), hand_one(0, 2)], [lambda: run_hidden_both(0)]
    )
    slot([pair_near(1, 0), rows_far(1, 2)], [lambda: run_project(1, 1)])
    slot(
        [pair_far(1, 1), rows_near(1, 2)],
        [lambda: run_attend_both(0), lambda: run_hidden_both(1)],
    )
    slot([pair_grad_near(1, 0), pair_near(1, 1)], [lambda: run_project(1, 2)])
    slot(
        [pair_grad_far(1, 0), pair_far(1, 2)],
        [lambda: run_attend_both(1), lambda: run_hidden_both(2)],
    )
    slot([pair_grad_near(1, 1), pair_near(1, 2)], [lambda: run_project_back(1, 0)])
    slot([sum_near(1, b[0]), pair_grad_far(1, 1)], [lambda: run_attend_both(2)])
    slot([sum_far(1, b[0]), pair_grad_near(1, 2)], [lambda: run_project_back(1, 1)])
    slot([hand_one(1, 0), sum_near(1, b[1]), pair_grad_far(1, 2)])
    slot([sum_far(1, b[1]), rows_far(0, 0)], [lambda: run_project_back(1, 2)])
    slot([sum_near(1, b[2]), hand_one(1, 1), rows_near(0, 0)])
    slot([sum_far(1, b[2]), rows_far(0, 1)], [lambda: run_attend_back(0)])
    slot(
        [hand_one(1, 2), rows_near(0, 1), pair_grad_near(0, 0)],
        [lambda: run_hidden_back(0)],
    )
    slot([rows_far(0, 2), pair_grad_far(0, 0)], [lambda: run_attend_back(1)])
    slot(
        [rows_near(0, 2), pair_grad_near(0, 1)],
        [lambda: run_hidden_back(1), lambda: run_project_back(0, 0)],
    )
    last = micros - 1

    def run_branch_sums():
        run_sums(
            branch_sums,
            [[of("active", s), of("attended", s)] for s in both],
            [
                [of("upstream", 0, last) + [piece[0] for piece in a[last].row_pieces]],
                [of("upstream", 1)],
            ],
            False,
        )

    def run_expand_sums():
        run_sums(
            expand_sums,
            [[of("second", s)] for s in both],
            [[of("hidden", s)] for s in both],
            True,
        )

    def run_triple_sums():
        run_sums(
            triple_sums,
            [[of("first", s)] for s in both],
            [[of("stacked", s)] for s in both],
            True,
        )

    finals = SimpleNamespace()

    def run_final_branch():
        blocks = branch_out(
            order, flags[1], [(k.active, k.attended) for k in b], contract, packed
        )
        finals.keep = jnp.stack(blocks[0::2])
        finals.send = jnp.stack(blocks[1::2])

    def last_near(w, s):
        return w.send, lambda passed: fold_hops(w, passed, "tp", 1, (s,))

    def last_far(w, s):
        def go(passed):
            w.came = hop(passed, "tp", lanes // 2, (s,))
            return w.came

        return w.send, go

    slot([pair_grad_far(0, 1)], [run_branch_sums])
    slot(
        [wide_near(branch_sums)], [lambda: run_attend_back(2), lambda: run_project_back(0, 1)]
    )
    slot([], [lambda: run_fold(branch_sums)])
    cut = [0, 3 * hidden // 8, 7 * hidden // 8, hidden + across_units]
    slot(
        [wide_far(branch_sums, cut[0], cut[1]), pair_grad_both(0, 2)],
        [lambda: run_hidden_back(2)],
    )
    slot(
        [wide_far(branch_sums, cut[1], cut[2])],
        [lambda: run_project_back(0, 2), run_triple_sums],
    )
    outs = SimpleNamespace(
        keep=jnp.stack([k.blocks[0] for k in a]), send=jnp.stack([k.blocks[1] for k in a])
    )

    def side_of(mades):
        return sum(
            jnp.concatenate([k.side_first, k.side_second], axis=0) for k in mades
        )

    side = SimpleNamespace(all=jnp.where(first_section, side_of(a), side_of(b)))

    def side_ctx(passed):
        step = 1
        while step < spans:
            middle = passed.shape[1] // 2
            came = hop(passed[:, middle:], "ctx", step, both)
            passed = passed[:, :middle] + came
            step *= 2
        side.all = passed
        return came

    def side_near(passed):
        step = 1
        while 2 * step < lanes:
            came = hop(passed, "tp", step, both)
            passed = passed + came
            step *= 2
        side.all = passed
        return came

    def side_far(passed):
        came = hop(passed, "tp", lanes // 2, both)
        side.all = passed + came
        return came

    def held_back(w, j):
        def go(passed):
            w.parts[j] = passed
            return []

        return w.parts[j], go

    def wide_total(keep, parts):
        came = jnp.concatenate(parts, axis=0) if len(parts) > 1 else parts[0]
        return keep.astype(f32) + came.astype(f32)

    slot(
        [
            wide_near(triple_sums),
            wide_far(branch_sums, cut[2], cut[3]),
            (side.all, side_ctx),
        ],
        [run_expand_sums, run_final_branch],
    )
    slot([], [lambda: run_fold(triple_sums)])
    slot(
        [
            wide_far(triple_sums, 0, depth),
            wide_near(expand_sums),
            last_near(outs, 0),
            last_near(finals, 1),
            (side.all, side_near),
        ]
    )
    slot([], [lambda: run_fold(expand_sums)])
    slot(
        [
            wide_far(expand_sums, 0, depth),
            last_far(outs, 0),
            last_far(finals, 1),
            (side.all, side_far),
            held_back(triple_sums, 0),
            held_back(branch_sums, 2),
        ]
    )
    triple_grads = wide_total(triple_sums.keep, triple_sums.parts)
    triple_grads = triple_grads.reshape(triple_weight.shape)
    branch_grads = wide_total(branch_sums.keep, branch_sums.parts)
    contract_grads, output_grads = branch_grads[:hidden], branch_grads[hidden:]
    expand_grads = wide_total(expand_sums.keep, expand_sums.parts)
    layer_outputs = jnp.stack(
        [
            jnp.where(
                first_section,
                kept[0][m].given,
                (
                    b[m].rows.astype(f32)
                    + finals.keep[m].astype(f32)
                    + finals.came[m].astype(f32)
                ).astype(bf16),
            )
            for m in range(micros)
        ]
    )
    own_rows = jnp.stack(of("rows", 0))
    entry_grads = jnp.where(
        first_section,
        norm_back(own_rows, outs.keep.astype(f32) + outs.came.astype(f32), inputs),
        jnp.stack(of("given", 1)),
    )
    gain_grads = jnp.stack([side.all[0], side.all[2]])
    bias_grads = jnp.stack([side.all[1], side.all[3]])
    return (
        xor_blocks(layer_outputs, span, spans, inverse=True)[None],
        xor_blocks(entry_grads, span, spans, inverse=True)[None],
        triple_grads,
        output_grads.reshape(output_weight.shape),
        expand_grads[None],
        contract_grads[None],
        gain_grads[None],
        bias_grads[None],
    )


def solution(mesh):
    return jax.shard_map(
        shards,
        mesh=mesh,
        in_specs=(
            P(None, ("ctx", "tp"), None),
            P(None, ("ctx", "tp"), None),
            P("pipe", "ctx", "tp", None, None),
            P("pipe", "tp", None, "ctx"),
            P("pipe", "ctx", "tp"),
            P("pipe", "tp", "ctx"),
            P("pipe", None, "ctx"),
            P("pipe", None, "ctx"),
        ),
        out_specs=(
            P("pipe", None, ("ctx", "tp"), None),
            P("pipe", None, ("ctx", "tp"), None),
            P("pipe", "ctx", "tp", None, None),
            P("pipe", "tp", None, "ctx"),
            P("pipe", "ctx", "tp"),
            P("pipe", "tp", "ctx"),
            P("pipe", None, "ctx"),
            P("pipe", None, "ctx"),
        ),
        check_vma=False,
    )
```

```python
import functools
import math
from types import SimpleNamespace

import jax
import jax.numpy as jnp
from jax import lax
from jax.experimental import pallas as pl
from jax.experimental.pallas import tpu as pltpu
from jax.sharding import PartitionSpec as P

ROT = 64
LANES = 128
epsilon = 1e-05
masked_score = -1e30
f32 = jnp.float32
bf16 = jnp.bfloat16
mebibyte = 1024 * 1024
half_root = 0.7071067811865476
bell = 0.3989422804014327


def dot(a, b, dims):
    return lax.dot_general(a, b, (dims, ((), ())), preferred_element_type=f32)


def plain(a, b):
    return dot(a, b, ((1,), (0,)))


def turned(a, b):
    return dot(a, b, ((1,), (1,)))


def doubling(count):
    order, step = [0], count // 2
    while step:
        order += [k ^ step for k in order]
        step //= 2
    return order


def xor_blocks(values, index, count, inverse=False):
    width = values.shape[-1] // count
    order = doubling(count)

    def taken(places):
        return jnp.concatenate(
            [values[..., k * width : (k + 1) * width] for k in places], axis=-1
        )

    if inverse:
        values = taken([order.index(k) for k in range(count)])
    step = 1
    while step < count:
        swapped = taken([k ^ step for k in range(count)])
        values = jnp.where((index & step) != 0, swapped, values)
        step *= 2
    return values if inverse else taken(order)


def rope_tables(positions):
    half = ROT // 2
    frequency = 10000.0 ** (-jnp.arange(0, ROT, 2, dtype=f32) / ROT)
    angles = positions.astype(f32)[:, None] * frequency[None, :]
    cosine, sine = jnp.cos(angles), jnp.sin(angles)
    count = positions.shape[0]
    rest = jnp.zeros((count, LANES - ROT), f32)
    none = jnp.zeros((count, half), f32)
    return jnp.stack(
        [
            jnp.concatenate([cosine, cosine, rest + 1.0], axis=1),
            jnp.concatenate([-sine, none, rest], axis=1),
            jnp.concatenate([none, sine, rest], axis=1),
        ]
    )


def turn(values, tables, sign):
    half = ROT // 2
    part = values[:, :LANES]
    moved = (
        pltpu.roll(part, LANES - half, 1) * tables[1] + pltpu.roll(part, half, 1) * tables[2]
    )
    part = part * tables[0] + (moved if sign > 0 else -moved)
    return jnp.concatenate([part, values[:, LANES:]], axis=1)


def normalize(values):
    center = values - jnp.mean(values, axis=-1, keepdims=True)
    inverse = lax.rsqrt(jnp.mean(center * center, axis=-1, keepdims=True) + epsilon)
    return (center * inverse, inverse)


def whole(array):
    zeros = (0,) * array.ndim
    return pl.BlockSpec(array.shape, lambda *_: zeros)


def at(block, place):
    return pl.BlockSpec(block, lambda *_: place)


kept_out = pl.BlockSpec(memory_space=pl.ANY)


def shape(dims, dtype=bf16):
    return jax.ShapeDtypeStruct(dims, dtype)


class Order:
    def __init__(self):
        self.last = []

    def follow(self, results):
        self.last = [min(results, key=lambda array: array.size * array.dtype.itemsize)]

    def also(self, array):
        self.last = self.last + [array]


took = dict(
    project=7,
    expand=8,
    attend=5,
    branch=8,
    hidden_both=14,
    attend_both=11,
    attend_back=8,
    hidden_back=13,
    project_back=8,
    weight_sums=16,
    fold=7,
)
peak = 1.15e9


def run(order, flags, kernel, ins, outs, scratch, name, grid=(1,), work=0):
    taken = len(ins)
    ins = [(flags, pl.BlockSpec(memory_space=pltpu.SMEM))] + list(ins)
    ins += [(array, kept_out) for array in order.last]
    arrays = [array for array, _ in ins]
    once = grid == (1,)

    def sized(spec, dtype):
        if spec.block_shape is None:
            return spec, 0
        size = math.prod(spec.block_shape) * jnp.dtype(dtype).itemsize
        if not once:
            return spec, 2 * size
        single = pl.BlockSpec(
            spec.block_shape, spec.index_map, pipeline_mode=pl.Buffered(1)
        )
        return single, size

    in_specs = [sized(spec, array.dtype) for array, spec in ins]
    out_specs = [sized(spec, struct.dtype) for struct, spec in outs]
    held = sum(size for _, size in in_specs + out_specs)
    for buffer in scratch:
        if buffer.memory_space == pltpu.VMEM:
            held += math.prod(buffer.shape) * jnp.dtype(buffer.dtype).itemsize

    def body(flag_ref, *refs):
        @pl.when(flag_ref[0] == 1)
        def _():
            kernel(flag_ref, *refs[:taken], *refs[len(ins) - 1 :])

    results = pl.pallas_call(
        body,
        grid=grid,
        in_specs=[spec for spec, _ in in_specs],
        out_specs=[spec for spec, _ in out_specs],
        out_shape=[struct for struct, _ in outs],
        scratch_shapes=scratch,
        compiler_params=pltpu.CompilerParams(
            vmem_limit_bytes=int(held + (work + 1) * mebibyte)
        ),
        cost_estimate=pl.CostEstimate(
            flops=int(took[name] * peak), bytes_accessed=0, transcendentals=0
        ),
        name=name,
    )(*arrays)
    order.follow(results)
    return results


def fence(through, waits):
    count = len(through)

    def kernel(*refs):
        pass

    return pl.pallas_call(
        kernel,
        in_specs=[kept_out] * (count + len(waits)),
        out_specs=[kept_out] * count,
        out_shape=[shape(array.shape, array.dtype) for array in through],
        input_output_aliases={j: j for j in range(count)},
        compiler_params=pltpu.CompilerParams(vmem_limit_bytes=mebibyte),
        cost_estimate=pl.CostEstimate(flops=1, bytes_accessed=1, transcendentals=0),
        name="fence",
    )(*through, *waits)


def full_out(dims, dtype=bf16):
    zeros = (0,) * len(dims)
    return (shape(dims, dtype), pl.BlockSpec(dims, lambda *_: zeros))


def copies(sources, targets, sems):
    started = []
    for source, target, sem in zip(sources, targets, sems):
        copy = pltpu.make_async_copy(source, target, sem)
        copy.start()
        started.append(copy)
    return started


def project(order, flags, pieces, at_piece, gains, biases, tables, weights, heads, head_dim):
    count, width = 1, pieces[0].shape[2]
    span_rows = sum(piece.shape[1] for piece in pieces)
    rows = count * span_rows
    chunk = pieces[0].shape[1]
    spans = len(weights)
    depth = width // spans
    wide = 3 * head_dim
    columns = heads * wide

    def kernel(flag_ref, *refs):
        piece_refs = refs[: len(pieces)]
        gain_ref, bias_ref, table_ref = refs[len(pieces) : len(pieces) + 3]
        weight_refs = refs[len(pieces) + 3 : len(pieces) + 3 + spans]
        first, second, normal, queries, pair, held, sems = refs[len(pieces) + 3 + spans :]
        started = []
        for h in range(heads):
            started.append(
                copies(
                    [w.at[:depth, h * wide : (h + 1) * wide] for w in weight_refs],
                    [held.at[h, k * depth : (k + 1) * depth] for k in range(spans)],
                    [sems.at[h, k] for k in range(spans)],
                )
            )
        start = 0
        for piece_ref in piece_refs:
            chunks = piece_ref.shape[1] // chunk

            def one(i, _, piece_ref=piece_ref, start=start, chunks=chunks):
                m, c = i // chunks, i % chunks
                values = piece_ref[m, pl.ds(pl.multiple_of(c * chunk, chunk), chunk), :]
                normed, _ = normalize(values.astype(f32))
                to = pl.ds(
                    pl.multiple_of(m * span_rows + start + c * chunk, chunk), chunk
                )
                normal[to, :] = normed.astype(bf16)
                first[to, :] = (normed * gain_ref[0:1] + bias_ref[0:1]).astype(bf16)
                second[to, :] = (normed * gain_ref[1:2] + bias_ref[1:2]).astype(bf16)
                return 0

            lax.fori_loop(0, count * chunks, one, 0)
            start += piece_ref.shape[1]
        for h in range(heads):
            for copy in started[h]:
                copy.wait()

            def two(m, _, h=h):
                to = pl.ds(pl.multiple_of(m * span_rows, span_rows), span_rows)
                made = plain(first[to, :], held[h])
                queries[h, to, :] = turn(made[:, :head_dim], table_ref, 1).astype(bf16)
                pair[0, h, to, :] = turn(
                    made[:, head_dim : 2 * head_dim], table_ref, 1
                ).astype(bf16)
                pair[1, h, to, :] = made[:, 2 * head_dim :].astype(bf16)
                return 0

            lax.fori_loop(0, count, two, 0)

    ins = [(piece, at((1,) + piece.shape[1:], (at_piece, 0, 0))) for piece in pieces]
    ins += [(array, whole(array)) for array in (gains, biases, tables)]
    ins += [(w, kept_out) for w in weights]
    outs = [full_out((rows, width))] * 3 + [
        full_out((heads, rows, head_dim)),
        full_out((2, heads, rows, head_dim)),
    ]
    scratch = [
        pltpu.VMEM((heads, width, wide), bf16),
        pltpu.SemaphoreType.DMA((heads, spans)),
    ]
    return run(order, flags, kernel, ins, outs, scratch, "project")


def expand_up(order, flags, second, weights, span_rows):
    rows, width = second.shape
    depth, hidden = weights[0].shape
    spans = len(weights)
    tile = min(512, hidden)
    tiles = hidden // tile

    def kernel(flag_ref, *refs):
        second_ref, weight_refs = refs[0], refs[1 : 1 + spans]
        active, slope, held, sems = refs[1 + spans :]
        started = []
        for t in range(tiles):
            started.append(
                copies(
                    [w.at[:, t * tile : (t + 1) * tile] for w in weight_refs],
                    [held.at[t, k * depth : (k + 1) * depth] for k in range(spans)],
                    [sems.at[t, k] for k in range(spans)],
                )
            )
        for t in range(tiles):
            for copy in started[t]:
                copy.wait()

            def one(m, _, t=t):
                to = pl.ds(pl.multiple_of(m * span_rows, span_rows), span_rows)
                pre = plain(second_ref[to, :], held[t])
                risen = 0.5 * (1.0 + lax.erf(pre * half_root))
                columns = slice(t * tile, (t + 1) * tile)
                active[to, columns] = (pre * risen).astype(bf16)
                slope[to, columns] = (
                    risen + pre * jnp.exp(-0.5 * pre * pre) * bell
                ).astype(bf16)
                return 0

            lax.fori_loop(0, rows // span_rows, one, 0)

    ins = [(second, whole(second))] + [(w, kept_out) for w in weights]
    outs = [full_out((rows, hidden))] * 2
    scratch = [
        pltpu.VMEM((tiles, width, tile), bf16),
        pltpu.SemaphoreType.DMA((tiles, spans)),
    ]
    return run(order, flags, kernel, ins, outs, scratch, "expand")


def spread(refs):
    return [ref.at[j] for ref in refs for j in range(ref.shape[0])]


def attention(here, pairs, head, row_ref, key_ref, scale):
    scores = []
    for k, pair in enumerate(pairs):
        raw = turned(here, pair[0, head]) * scale
        scores.append(jnp.where(key_ref[k] <= row_ref[...], raw, masked_score))
    top = functools.reduce(
        jnp.maximum, [jnp.max(part, axis=1, keepdims=True) for part in scores]
    )
    scores = [jnp.exp(part - top) for part in scores]
    inverse = 1.0 / sum(jnp.sum(part, axis=1, keepdims=True) for part in scores)
    return [part * inverse for part in scores]


def attend(order, flags, queries, pairs, positions, key_positions, scale):
    heads, rows, head_dim = queries.shape
    spans = sum(pair.shape[0] for pair in pairs)

    def kernel(flag_ref, query_ref, *refs):
        views, refs = spread(refs[: len(pairs)]), refs[len(pairs) :]
        row_ref, key_ref, attended, probs = refs
        for h in range(heads):
            parts = attention(query_ref[h], views, h, row_ref, key_ref, scale)
            summed = None
            for k in range(spans):
                part = parts[k].astype(bf16)
                probs[k, h] = part
                term = plain(part, views[k][1, h])
                summed = term if summed is None else summed + term
            attended[:, h * head_dim : (h + 1) * head_dim] = summed.astype(bf16)

    ins = [
        (array, whole(array)) for array in (queries, *pairs, positions, key_positions)
    ]
    outs = [full_out((rows, heads * head_dim)), full_out((spans, heads, rows, rows))]
    work = spans * rows * rows * 4 * heads * 4 / mebibyte
    return run(order, flags, kernel, ins, outs, [], "attend", work=work)


def attention_grads(grad, here, parts, views, head, keep, send, scale):
    half = keep.shape[0]
    grad_probs = [turned(grad, view[1, head]) for view in views]
    delta = sum(
        jnp.sum(part.astype(f32) * slope, axis=1, keepdims=True)
        for part, slope in zip(parts, grad_probs)
    )
    query_grad = None
    for k, view in enumerate(views):
        slopes = (parts[k].astype(f32) * (grad_probs[k] - delta)).astype(bf16)
        term = plain(slopes, view[0, head])
        query_grad = term if query_grad is None else query_grad + term
        side = keep if k < half else send
        side[k % half, 0, head] = (dot(slopes, here, ((0,), (0,))) * scale).astype(bf16)
        side[k % half, 1, head] = dot(parts[k].astype(bf16), grad, ((0,), (0,))).astype(bf16)
    return query_grad * scale


def attend_both(
    order, flags, rows_in, packed, queries, pairs, positions, key_positions, tables, scale
):
    heads, rows, head_dim = queries.shape
    width = rows_in.shape[1]
    spans = len(packed)
    across, depth = heads * head_dim, width // spans
    half = spans // 2

    def kernel(flag_ref, rows_ref, *refs):
        packed_refs, refs = refs[:spans], refs[spans:]
        query_ref, refs = refs[0], refs[1:]
        views, refs = spread(refs[: len(pairs)]), refs[len(pairs) :]
        row_ref, key_ref, table_ref, attended, turned_back, keep, send, held, sems = refs
        started = copies(
            [w.at[:across, 3 * across : 3 * across + depth] for w in packed_refs],
            [held.at[:, k * depth : (k + 1) * depth] for k in range(spans)],
            [sems.at[k] for k in range(spans)],
        )
        all_parts = []
        for h in range(heads):
            parts = attention(query_ref[h], views, h, row_ref, key_ref, scale)
            summed = None
            for k in range(spans):
                term = plain(parts[k].astype(bf16), views[k][1, h])
                summed = term if summed is None else summed + term
            attended[:, h * head_dim : (h + 1) * head_dim] = summed.astype(bf16)
            all_parts.append(parts)
        for copy in started:
            copy.wait()
        grads = turned(rows_ref[...], held[...]).astype(bf16)
        for h in range(heads):
            made = attention_grads(
                grads[:, h * head_dim : (h + 1) * head_dim],
                query_ref[h],
                all_parts[h],
                views,
                h,
                keep,
                send,
                scale,
            )
            turned_back[h] = turn(made, table_ref, -1).astype(bf16)

    ins = [(rows_in, whole(rows_in))] + [(w, kept_out) for w in packed]
    ins += [
        (array, whole(array)) for array in (queries, *pairs, positions, key_positions, tables)
    ]
    outs = [full_out((rows, across)), full_out((heads, rows, head_dim))]
    outs += [full_out((half, 2, heads, rows, head_dim))] * 2
    scratch = [pltpu.VMEM((across, width), bf16), pltpu.SemaphoreType.DMA((spans,))]
    work = spans * rows * rows * 4 * (heads + 4) / mebibyte
    return run(order, flags, kernel, ins, outs, scratch, "attend_both", work=work)


def hidden_both(order, flags, second, pieces, at_piece, expand, contract, normal, gains):
    rows, width = second.shape
    hidden, depth = contract[0].shape
    spans = len(contract)
    tile = min(512, hidden)
    tiles = hidden // tile

    def kernel(flag_ref, second_ref, *refs):
        piece_refs, refs = refs[: len(pieces)], refs[len(pieces) :]
        expand_refs, refs = refs[:spans], refs[spans:]
        contract_refs, refs = refs[:spans], refs[spans:]
        normal_ref, gain_ref, rows_out, active, grads, part, side, *refs = refs
        held_up, held_down, sems_up, sems_down = refs
        started = []
        for t in range(tiles):
            block = slice(t * tile, (t + 1) * tile)
            places = [slice(k * depth, (k + 1) * depth) for k in range(spans)]
            up = copies(
                [w.at[:, block] for w in expand_refs],
                [held_up.at[place, block] for place in places],
                [sems_up.at[t, k] for k in range(spans)],
            )
            down = copies(
                [w.at[block, :] for w in contract_refs],
                [held_down.at[block, place] for place in places],
                [sems_down.at[t, k] for k in range(spans)],
            )
            started.append((up, down))
        start = 0
        for piece_ref in piece_refs:
            size = piece_ref.shape[1]
            rows_out[start : start + size, :] = piece_ref[0]
            start += size
        for t in range(tiles):
            block = slice(t * tile, (t + 1) * tile)
            for copy in started[t][0] + started[t][1]:
                copy.wait()
            pre = plain(second_ref[...], held_up[:, block])
            risen = 0.5 * (1.0 + lax.erf(pre * half_root))
            active[:, block] = (pre * risen).astype(bf16)
            slope = risen + pre * jnp.exp(-0.5 * pre * pre) * bell
            grads[:, block] = (turned(rows_out[...], held_down[block, :]) * slope).astype(bf16)
        for k in range(spans):
            place = slice(k * depth, (k + 1) * depth)
            made = turned(grads[...], held_up[place, :])
            side[0:1, place] = jnp.sum(
                made * normal_ref[:, place].astype(f32), axis=0, keepdims=True
            )
            side[1:2, place] = jnp.sum(made, axis=0, keepdims=True)
            part[:, place] = made * gain_ref[1:2, place]

    ins = [(second, whole(second))]
    ins += [(piece, at((1,) + piece.shape[1:], (at_piece, 0, 0))) for piece in pieces]
    ins += [(w, kept_out) for w in expand] + [(w, kept_out) for w in contract]
    ins += [(normal, whole(normal)), (gains, whole(gains))]
    outs = [
        full_out((rows, width)),
        full_out((rows, hidden)),
        full_out((rows, hidden)),
        full_out((rows, width), f32),
        full_out((2, width), f32),
    ]
    scratch = [
        pltpu.VMEM((width, hidden), bf16),
        pltpu.VMEM((hidden, width), bf16),
        pltpu.SemaphoreType.DMA((tiles, spans)),
        pltpu.SemaphoreType.DMA((tiles, spans)),
    ]
    return run(order, flags, kernel, ins, outs, scratch, "hidden_both")


def branch_out(order, flags, groups, contract, packed):
    hidden, depth = contract[0].shape
    across = groups[0][1].shape[1]
    spans = len(contract)
    width = depth * spans
    span_rows = groups[0][0].shape[0]
    block = span_rows // 2
    count = len(groups)

    def kernel(flag_ref, *refs):
        group_refs, refs = refs[: 2 * count], refs[2 * count :]
        contract_refs, packed_refs = refs[:spans], refs[spans : 2 * spans]
        blocks, refs = refs[2 * spans : 2 * (spans + count)], refs[2 * (spans + count) :]
        held, held_out, sems = refs
        outputs = [w.at[:across, 3 * across : 3 * across + depth] for w in packed_refs]
        started = copies(
            [ref for k in range(spans) for ref in (outputs[k], contract_refs[k])],
            [ref for k in range(spans) for ref in (held_out.at[k], held.at[k])],
            [sems.at[j] for j in range(2 * spans)],
        )
        for k in range(spans):
            started[2 * k].wait()
            started[2 * k + 1].wait()
            columns = slice(k * depth, (k + 1) * depth)
            for c in range(count):
                made = plain(group_refs[2 * c + 1][...], held_out[k])
                made = made + plain(group_refs[2 * c][...], held[k])
                blocks[2 * c][:, columns] = made[:block].astype(bf16)
                blocks[2 * c + 1][:, columns] = made[block:].astype(bf16)

    ins = []
    for active, attended in groups:
        ins += [(active, whole(active)), (attended, whole(attended))]
    ins += [(w, kept_out) for w in contract] + [(w, kept_out) for w in packed]
    outs = [full_out((block, width))] * (2 * count)
    scratch = [
        pltpu.VMEM((spans, hidden, depth), bf16),
        pltpu.VMEM((spans, across, depth), bf16),
        pltpu.SemaphoreType.DMA((2 * spans,)),
    ]
    return run(order, flags, kernel, ins, outs, scratch, "branch")


def attend_back(order, flags, pieces, packed, queries, pairs, probs, tables, scale):
    rows = sum(piece.shape[1] for piece in pieces)
    width = pieces[0].shape[2]
    heads, _, head_dim = queries.shape
    spans = len(packed)
    across, depth = heads * head_dim, width // spans
    half = spans // 2

    def kernel(flag_ref, *refs):
        piece_refs, refs = refs[: len(pieces)], refs[len(pieces) :]
        packed_refs, refs = refs[:spans], refs[spans:]
        query_ref, refs = refs[0], refs[1:]
        views, refs = spread(refs[: len(pairs)]), refs[len(pairs) :]
        prob_ref, table_ref, rows_out, turned_back, keep, send, held, sems = refs
        started = copies(
            [w.at[:across, 3 * across : 3 * across + depth] for w in packed_refs],
            [held.at[:, k * depth : (k + 1) * depth] for k in range(spans)],
            [sems.at[k] for k in range(spans)],
        )
        start = 0
        for piece_ref in piece_refs:
            size = piece_ref.shape[1]
            rows_out[start : start + size, :] = piece_ref[0]
            start += size
        for copy in started:
            copy.wait()
        grads = turned(rows_out[...], held[...]).astype(bf16)
        for h in range(heads):
            made = attention_grads(
                grads[:, h * head_dim : (h + 1) * head_dim],
                query_ref[h],
                [prob_ref[k, h] for k in range(spans)],
                views,
                h,
                keep,
                send,
                scale,
            )
            turned_back[h] = turn(made, table_ref, -1).astype(bf16)

    ins = [(piece, whole(piece)) for piece in pieces] + [(w, kept_out) for w in packed]
    ins += [(array, whole(array)) for array in (queries, *pairs, probs, tables)]
    outs = [full_out((rows, width)), full_out((heads, rows, head_dim))]
    outs += [full_out((half, 2, heads, rows, head_dim))] * 2
    scratch = [pltpu.VMEM((across, width), bf16), pltpu.SemaphoreType.DMA((spans,))]
    work = spans * rows * rows * 4 * 4 / mebibyte
    return run(order, flags, kernel, ins, outs, scratch, "attend_back", work=work)


def hidden_back(order, flags, upstream, contract, expand, slope, normal, gains):
    span_rows, width = upstream.shape
    hidden, depth = contract[0].shape
    spans = len(contract)
    tile = min(512, hidden)
    tiles = hidden // tile

    def kernel(flag_ref, *refs):
        upstream_ref, refs = refs[0], refs[1:]
        contract_refs, refs = refs[:spans], refs[spans:]
        expand_refs, refs = refs[:spans], refs[spans:]
        slope_ref, normal_ref, gain_ref, grads, part, side, held, held_up, sems, sems_up = refs
        started = [
            copies(
                [w.at[t * tile : (t + 1) * tile, :] for w in contract_refs],
                [held.at[t, :, k * depth : (k + 1) * depth] for k in range(spans)],
                [sems.at[t, k] for k in range(spans)],
            )
            for t in range(tiles)
        ]
        started_up = copies(
            expand_refs, [held_up.at[k] for k in range(spans)], [sems_up.at[k] for k in range(spans)]
        )
        for t in range(tiles):
            for copy in started[t]:
                copy.wait()
            columns = slice(t * tile, (t + 1) * tile)
            grads[:, columns] = (
                turned(upstream_ref[...], held[t]) * slope_ref[:, columns].astype(f32)
            ).astype(bf16)
        for k in range(spans):
            started_up[k].wait()
            made = turned(grads[...], held_up[k])
            columns = slice(k * depth, (k + 1) * depth)
            side[0:1, columns] = jnp.sum(
                made * normal_ref[:, columns].astype(f32), axis=0, keepdims=True
            )
            side[1:2, columns] = jnp.sum(made, axis=0, keepdims=True)
            part[:, columns] = made * gain_ref[1:2, columns]

    ins = [(upstream, whole(upstream))]
    ins += [(w, kept_out) for w in contract] + [(w, kept_out) for w in expand]
    ins += [
        (slope, whole(slope)),
        (normal, whole(normal)),
        (gains, whole(gains)),
    ]
    outs = [
        full_out((span_rows, hidden)),
        full_out((span_rows, width), f32),
        full_out((2, width), f32),
    ]
    scratch = [
        pltpu.VMEM((tiles, tile, width), bf16),
        pltpu.VMEM((spans, depth, hidden), bf16),
        pltpu.SemaphoreType.DMA((tiles, spans)),
        pltpu.SemaphoreType.DMA((spans,)),
    ]
    return run(order, flags, kernel, ins, outs, scratch, "hidden_back")


def project_back(
    order, flags, turned_back, own, came, weights, part, normal, gains, tables
):
    heads, span_rows, head_dim = turned_back.shape
    spans = len(weights)
    width = part.shape[1]
    depth, columns = width // spans, 3 * heads * head_dim
    block = span_rows // 2

    def kernel(flag_ref, *refs):
        query_ref, own_ref, came_ref, refs = refs[0], refs[1], refs[2], refs[3:]
        weight_refs, refs = refs[:spans], refs[spans:]
        part_ref, normal_ref, gain_ref, table_ref, grads, side, *refs = refs
        low, high, held, sems = refs
        started = copies(
            [w.at[:depth, :columns] for w in weight_refs],
            [held.at[k] for k in range(spans)],
            [sems.at[k] for k in range(spans)],
        )
        for h in range(heads):
            at_column = h * 3 * head_dim
            keys = own_ref[0, h].astype(f32) + came_ref[0, h].astype(f32)
            values = own_ref[1, h].astype(f32) + came_ref[1, h].astype(f32)
            grads[:, at_column : at_column + head_dim] = query_ref[h]
            grads[:, at_column + head_dim : at_column + 2 * head_dim] = turn(
                keys, table_ref, -1
            ).astype(bf16)
            grads[:, at_column + 2 * head_dim : at_column + 3 * head_dim] = values.astype(bf16)
        for k in range(spans):
            started[k].wait()
            made = turned(grads[...], held[k])
            span_columns = slice(k * depth, (k + 1) * depth)
            side[0:1, span_columns] = jnp.sum(
                made * normal_ref[:, span_columns].astype(f32), axis=0, keepdims=True
            )
            side[1:2, span_columns] = jnp.sum(made, axis=0, keepdims=True)
            both = (made * gain_ref[0:1, span_columns] + part_ref[:, span_columns]).astype(bf16)
            low[:, span_columns] = both[:block]
            high[:, span_columns] = both[block:]

    ins = [(array, whole(array)) for array in (turned_back, own, came)]
    ins += [(w, kept_out) for w in weights]
    ins += [(part, whole(part)), (normal, whole(normal))]
    ins += [(gains, whole(gains)), (tables, whole(tables))]
    outs = [full_out((span_rows, columns)), full_out((2, width), f32)]
    outs += [full_out((block, width))] * 2
    scratch = [pltpu.VMEM((spans, depth, columns), bf16), pltpu.SemaphoreType.DMA((spans,))]
    return run(order, flags, kernel, ins, outs, scratch, "project_back")


def weight_sums(order, flags, lefts, rights, by_rows, spans):
    rows = sum(piece.shape[0] for piece in lefts[0][0])
    left_width = sum(group[0].shape[1] for group in lefts[0])
    right_width = sum(group[0].shape[1] for group in rights[0])
    if by_rows:
        tile = left_width // spans
        steps, block = spans // 2, (tile, right_width)
    else:
        tile = min(512, left_width)
        while left_width % tile:
            tile //= 2
        steps, block = left_width // tile, (tile, right_width // 2)
    chunk = min(1024, block[1])
    while right_width % chunk:
        chunk //= 2
    pieces = [
        [piece for groups in (lefts[s], rights[s]) for group in groups for piece in group]
        for s in (0, 1)
    ]
    most = max(len(p) for p in pieces)

    def kernel(flag_ref, *refs):
        piece_refs = (refs[: len(pieces[0])], refs[len(pieces[0]) : len(pieces[0]) + len(pieces[1])])
        keep, send, left, right, flipped, sems = refs[len(pieces[0]) + len(pieces[1]) :]
        g = pl.program_id(0)
        for s in (0, 1):

            @pl.when((g == 0) & (flag_ref[2] == s))
            def _(s=s):
                targets = []
                for held, groups in ((left, lefts[s]), (right, rights[s])):
                    column = 0
                    for group in groups:
                        row, wide = 0, group[0].shape[1]
                        for piece in group:
                            targets.append(
                                held.at[row : row + piece.shape[0], column : column + wide]
                            )
                            row += piece.shape[0]
                        column += wide
                started = copies(
                    piece_refs[s], targets, [sems.at[j] for j in range(len(targets))]
                )
                for copy in started:
                    copy.wait()

        def product(column, store):
            flipped[...] = left[:, pl.ds(pl.multiple_of(column, LANES), tile)].T

            def one(c, _):
                columns = pl.ds(pl.multiple_of(c * chunk, chunk), chunk)
                store(c, plain(flipped[...], right[:, columns]).astype(bf16))
                return 0

            lax.fori_loop(0, right_width // chunk, one, 0)

        if by_rows:

            def to(target):
                def store(c, made):
                    target[:, pl.ds(pl.multiple_of(c * chunk, chunk), chunk)] = made

                return store

            product(g * tile, to(keep))
            product((g + steps) * tile, to(send))
        else:
            half = right_width // 2 // chunk

            def store(c, made):
                @pl.when(c < half)
                def _():
                    keep[:, pl.ds(pl.multiple_of(c * chunk, chunk), chunk)] = made

                @pl.when(c >= half)
                def _():
                    send[:, pl.ds(pl.multiple_of((c - half) * chunk, chunk), chunk)] = made

            product(g * tile, store)

    ins = [(piece, kept_out) for s in (0, 1) for piece in pieces[s]]
    dims = (steps * tile, block[1])
    outs = [(shape(dims), pl.BlockSpec(block, lambda g: (g, 0)))] * 2
    scratch = [
        pltpu.VMEM((rows, left_width), bf16),
        pltpu.VMEM((rows, right_width), bf16),
        pltpu.VMEM((tile, rows), bf16),
        pltpu.SemaphoreType.DMA((most,)),
    ]
    return run(
        order, flags, kernel, ins, outs, scratch, "weight_sums", grid=(steps,)
    )


def fold(order, flags, keep, came, dim):
    rows, columns = keep.shape
    if dim == 0:
        tile = rows // 4
        steps, block = rows // 2 // tile, (tile, columns)
        places = [lambda g: (g, 0), lambda g: (g + steps, 0)]
        half = (rows // 2, columns)
    else:
        tile = rows // 4
        steps, block = rows // tile, (tile, columns // 2)
        places = [lambda g: (g, 0), lambda g: (g, 1)]
        half = (rows, columns // 2)

    def kernel(flag_ref, keep_low, keep_high, came_low, came_high, low, high):
        low[...] = (keep_low[...].astype(f32) + came_low[...].astype(f32)).astype(bf16)
        high[...] = (keep_high[...].astype(f32) + came_high[...].astype(f32)).astype(bf16)

    ins = [(array, pl.BlockSpec(block, place)) for array in (keep, came) for place in places]
    outs = [(shape(half), pl.BlockSpec(block, lambda g: (g, 0)))] * 2
    return run(order, flags, kernel, ins, outs, [], "fold", grid=(steps,))


def shards(
    block_input,
    out_grad,
    triple_weight,
    output_weight,
    expand_weight,
    contract_weight,
    norm_gains,
    norm_biases,
):
    section = lax.axis_index("pipe")
    span = lax.axis_index("ctx")
    lane = lax.axis_index("tp")
    spans = lax.axis_size("ctx")
    lanes = lax.axis_size("tp")
    micros, rows, width = block_input.shape
    span_rows = rows * lanes
    heads = triple_weight.shape[2]
    head_dim = triple_weight.shape[4]
    across_units = heads * head_dim
    scale = head_dim ** (-0.5)
    first_section = section == 0
    both = (0, 1)

    def hop(array, axis, step, sections):
        size = lax.axis_size(axis)
        pairs = [(s * size + a, s * size + (a ^ step)) for s in sections for a in range(size)]
        return lax.ppermute(array, ("pipe", axis), pairs)

    order = Order()

    def flags_for(wanted):
        return jnp.stack([jnp.asarray(wanted), span, section]).astype(jnp.int32)

    flags = [flags_for(section == s) for s in both]
    always = flags_for(1)

    kept = [[SimpleNamespace() for _ in range(micros)] for _ in both]
    due = {}
    slot_index = [0]

    def slot(hops, kernels=()):
        now = slot_index[0]
        slot_index[0] += 1
        ready = due.pop(now, [])
        hops = [h if len(h) == 3 else h + (1,) for h in hops]
        if hops:
            gated = fence([operand for operand, _, _ in hops], order.last + ready)
            order.last = [min(gated, key=lambda array: array.size)]
            for passed, (_, go, slots) in zip(gated, hops):
                results = go(passed)
                results = results if isinstance(results, list) else [results]
                due.setdefault(now + slots, []).extend(results)
        else:
            order.last = order.last + ready
        for kernel in kernels:
            kernel()

    def halved(keep, came, dim):
        middle = keep.shape[dim] // 2
        total = keep.astype(f32) + came.astype(f32)
        return (
            lax.slice_in_dim(total, 0, middle, axis=dim).astype(bf16),
            lax.slice_in_dim(total, middle, 2 * middle, axis=dim).astype(bf16),
        )

    def spread_hops(pieces, axis, axis_name, sections, first):
        step = lax.axis_size(axis_name) // 4
        going = first
        while step:
            pieces.append(hop(going, axis_name, step, sections))
            going = jnp.concatenate(pieces, axis=axis)
            step //= 2
        return pieces[-1]

    def fold_hops(k, first, axis_name, dim, sections):
        step, size = 1, lax.axis_size(axis_name)
        while 2 * step < size:
            came = hop(first, axis_name, step, sections)
            k.keep, k.send = halved(k.keep, came, dim)
            first = k.send
            step *= 2
        return came

    depth = width // spans
    far = spans // 2
    assert depth == across_units
    small = jnp.concatenate([norm_gains[0], norm_biases[0]], axis=0)
    packed = jnp.concatenate(
        [triple_weight[0].reshape(depth, -1), output_weight[0].reshape(-1, depth)],
        axis=1,
    )
    packed = jnp.pad(packed, ((0, 16), (0, 0)))
    packed = lax.dynamic_update_slice(packed, small, (depth, 0))
    own_expand, own_contract = expand_weight[0], contract_weight[0]
    hidden = own_expand.shape[1]
    inputs = xor_blocks(block_input, span, spans)
    cotangent = xor_blocks(out_grad, span, spans)
    early = jnp.where(first_section, inputs, cotangent)

    in_row = jnp.arange(rows, dtype=jnp.int32)
    in_span = jnp.concatenate([(lane ^ j) * rows + in_row for j in doubling(lanes)])
    positions = span * span_rows + in_span
    key_positions = jnp.stack([(span ^ k) * span_rows + in_span for k in doubling(spans)])
    tables = rope_tables(positions)
    position_column = positions[:, None]
    key_positions = key_positions[:, None, :]

    def blocks_of(own, came):
        held, step = {0: own, far: came}, far // 2
        while step:
            for k in list(held):
                held[k ^ step] = hop(held[k], "ctx", step, both)
            step //= 2
        return [held[k] for k in doubling(spans)]

    lane_offsets = doubling(lanes)

    def across(array, j, source):
        pairs = [(source * lanes + a, (1 - source) * lanes + (a ^ j)) for a in range(lanes)]
        return lax.ppermute(array, ("pipe", "tp"), pairs)

    def rows_far(s, m):
        k = kept[s][m]

        def go(passed):
            k.rows = passed
            k.pieces = [passed, hop(passed, "tp", lanes // 2, (s,))]
            return k.pieces[1]

        return k.rows, go

    def rows_near(s, m):
        k = kept[s][m]

        def go(passed):
            last_piece = spread_hops(k.pieces, 0, "tp", (s,), passed)
            k.row_pieces = [piece[None] for piece in k.pieces]
            return last_piece

        return jnp.concatenate(k.pieces, axis=0), go

    def one_way(array, direction, s):
        pairs = [
            (s * spans + a, s * spans + (a ^ far))
            for a in range(spans)
            if direction * ((a ^ far) - a) > 0
        ]
        return lax.ppermute(array, ("pipe", "ctx"), pairs)

    def pair_far(s, m):
        k = kept[s][m]

        def go(passed):
            k.pairs = [passed, one_way(passed, 1, s)]
            return k.pairs[1]

        return k.pair, go

    def pair_near(s, m):
        k = kept[s][m]

        def go(passed):
            return spread_hops(k.pairs, 0, "ctx", (s,), passed)

        return jnp.concatenate(k.pairs, axis=0), go

    def pair_grad_near(s, m):
        k = kept[s][m].pair_grad
        return k.send, lambda passed: fold_hops(k, passed, "ctx", 0, (s,))

    def pair_grad_both(s, m):
        k = kept[s][m].pair_grad

        def go(passed):
            fold_hops(k, passed, "ctx", 0, (s,))
            k.came = one_way(k.send, -1, s)
            return k.came

        return k.send, go

    def pair_grad_far(s, m):
        k = kept[s][m].pair_grad

        def go(passed):
            k.came = one_way(passed, -1, s)
            return k.came

        return k.send, go

    def sum_near(s, k):
        k.keep, going = k.blocks
        return going, lambda passed: fold_hops(k, passed, "tp", 0, (s,))

    def sum_far(s, k):
        def go(passed):
            k.blocks, k.arrived = [k.keep], [hop(passed, "tp", lanes // 2, (s,))]
            return k.arrived[0]

        return k.send, go

    def total_of(k):
        return sum(array.astype(f32) for array in [k.blocks[0], *k.arrived])

    def norm_back(upstream, combined, entering):
        normalized, inverse = normalize(entering.astype(f32))
        return (
            upstream.astype(f32)
            + inverse
            * (
                combined
                - jnp.mean(combined, axis=-1, keepdims=True)
                - normalized * jnp.mean(combined * normalized, axis=-1, keepdims=True)
            )
        ).astype(bf16)

    def middle_of(m):
        return (inputs[m].astype(f32) + total_of(kept[0][m])).astype(bf16)

    def entry_of(m):
        k = kept[1][m]
        return norm_back(cotangent[m], total_of(k), k.rows)

    def hand_one(s, m):
        k, other = kept[s][m], kept[1 - s][m]
        k.given = middle_of(m) if s == 0 else entry_of(m)

        def go(passed):
            k.given = passed
            other.rows = across(passed, 0, s)
            return other.rows

        return k.given, go

    def run_project(s, m):
        k = kept[s][m]
        pieces, place = (early_pieces, m) if s == 0 else (k.row_pieces, 0)
        k.first, k.second, k.normal, k.queries, pair = project(
            order, flags[s], pieces, place, gains, biases, tables, packed, heads, head_dim
        )
        k.pair = pair[None]

    def run_expand(m):
        k = kept[0][m]
        k.active, k.slope = expand_up(order, flags[0], k.second, weights.expand, span_rows)

    def run_attend(m):
        k = kept[0][m]
        k.attended, k.probs = attend(
            order, flags[0], k.queries, k.pairs, position_column, key_positions, scale
        )

    def run_branch(m):
        k = kept[0][m]
        k.blocks = branch_out(
            order, flags[0], [(k.active, k.attended)], contract, packed
        )

    def run_hidden_both(m):
        k = kept[1][m]
        k.upstream, k.active, k.hidden, k.part, k.side_second = hidden_both(
            order,
            flags[1],
            k.second,
            early_pieces,
            m,
            weights.expand,
            contract,
            k.normal,
            gains,
        )

    def run_attend_both(m):
        k = kept[1][m]
        k.attended, k.turned_back, keep, send = attend_both(
            order,
            flags[1],
            k.upstream,
            packed,
            k.queries,
            k.pairs,
            position_column,
            key_positions,
            tables,
            scale,
        )
        k.pair_grad = SimpleNamespace(keep=keep, send=send)

    def run_attend_back(m):
        k = kept[0][m]
        k.upstream, k.turned_back, keep, send = attend_back(
            order,
            flags[0],
            k.row_pieces,
            packed,
            k.queries,
            k.pairs,
            k.probs,
            tables,
            scale,
        )
        k.pair_grad = SimpleNamespace(keep=keep, send=send)

    def run_hidden_back(m):
        k = kept[0][m]
        k.hidden, k.part, k.side_second = hidden_back(
            order,
            flags[0],
            k.upstream,
            contract,
            weights.expand,
            k.slope,
            k.normal,
            gains,
        )

    def run_project_back(s, m):
        k = kept[s][m]
        own, arrived = k.pair_grad.keep, k.pair_grad.came
        k.stacked, k.side_first, *k.blocks = project_back(
            order,
            flags[s],
            k.turned_back,
            own.reshape(own.shape[1:]),
            arrived.reshape(arrived.shape[1:]),
            packed,
            k.part,
            k.normal,
            gains,
            tables,
        )

    def of(name, s, count=micros):
        return [getattr(kept[s][m], name) for m in range(count)]

    branch_sums, expand_sums, triple_sums = (SimpleNamespace(parts=[]) for _ in range(3))

    def run_sums(w, lefts, rights, by_rows):
        w.dim = 0 if by_rows else 1
        w.keep, w.send = weight_sums(order, always, lefts, rights, by_rows, spans)

    def wide_near(w):
        def go(passed):
            w.came = hop(passed, "ctx", 1, both)
            return w.came

        return w.send, go

    def run_fold(w):
        step = 2
        w.keep, w.send = fold(order, always, w.keep, w.came, w.dim)
        while 2 * step < spans:
            w.came = hop(w.send, "ctx", step, both)
            w.keep, w.send = fold(order, always, w.keep, w.came, w.dim)
            step *= 2

    def wide_far(w, start, stop):
        def go(passed):
            w.parts.append(hop(passed, "ctx", far, both))
            return w.parts[-1]

        return w.send[start:stop], go

    weights = SimpleNamespace(expand_came=[], contract_came=[])
    half_depth = depth // 2

    def expand_far(start, stop):
        def go(passed):
            weights.expand_came.append(hop(passed, "ctx", far, both))
            return weights.expand_came[-1]

        return own_expand[start:stop], go

    def packed_far(passed):
        weights.packed_came = hop(passed, "ctx", far, both)
        return weights.packed_came

    def packed_near(passed):
        weights.packed = blocks_of(packed, passed)
        return weights.packed[1:]

    def expand_near(passed):
        weights.expand = blocks_of(own_expand, passed)
        return weights.expand[1:]

    def contract_far(start, stop):
        def go(passed):
            weights.contract_came.append(hop(passed, "ctx", far, both))
            return weights.contract_came[-1]

        return own_contract[start:stop], go

    def contract_near(passed):
        weights.contract = blocks_of(own_contract, passed)
        return weights.contract[1:]

    def early_hops(passed):
        weights.early = [passed] + [hop(passed, "tp", j, both) for j in lane_offsets[1:]]
        return weights.early[1:]

    due[0] = [expand_far(0, half_depth)[1](own_expand[:half_depth])]
    slot([(packed, packed_far), expand_far(half_depth, depth), (early, early_hops)])
    early_pieces = weights.early
    cuts = [0, hidden // 4, 11 * hidden // 16, hidden]
    expand_came = jnp.concatenate(weights.expand_came, axis=0)
    slot(
        [
            (weights.packed_came, packed_near),
            (expand_came, expand_near),
            contract_far(cuts[0], cuts[1]),
        ]
    )
    packed = weights.packed
    small_full = jnp.concatenate(
        [piece[depth : depth + 4, :depth] for piece in packed], axis=1
    ).astype(f32)
    gains, biases = small_full[:2], small_full[2:]
    slot(
        [contract_far(cuts[1], cuts[2])],
        [lambda m=m: run_project(0, m) for m in range(micros)],
    )
    a, b = kept
    slot(
        [pair_far(0, 0), contract_far(cuts[2], cuts[3])],
        [lambda m=m: run_expand(m) for m in range(micros)],
    )
    contract_came = jnp.concatenate(weights.contract_came, axis=0)
    slot([(contract_came, contract_near), pair_near(0, 0)])
    contract = weights.contract
    slot([pair_far(0, 1)], [lambda: run_attend(0), lambda: run_branch(0)])
    slot([sum_near(0, a[0]), pair_near(0, 1)])
    slot([sum_far(0, a[0]), pair_far(0, 2)], [lambda: run_attend(1), lambda: run_branch(1)])
    slot([hand_one(0, 0), sum_near(0, a[1]), pair_near(0, 2)])
    slot(
        [rows_far(1, 0), sum_far(0, a[1])], [lambda: run_attend(2), lambda: run_branch(2)]
    )
    slot([rows_near(1, 0), hand_one(0, 1), sum_near(0, a[2])])
    slot([rows_far(1, 1), sum_far(0, a[2])], [lambda: run_project(1, 0)])
    slot(
        [pair_far(1, 0), rows_near(1, 1), hand_one(0, 2)], [lambda: run_hidden_both(0)]
    )
    slot([pair_near(1, 0), rows_far(1, 2)], [lambda: run_project(1, 1)])
    slot(
        [pair_far(1, 1), rows_near(1, 2)],
        [lambda: run_attend_both(0), lambda: run_hidden_both(1)],
    )
    slot([pair_grad_near(1, 0), pair_near(1, 1)], [lambda: run_project(1, 2)])
    slot(
        [pair_grad_far(1, 0), pair_far(1, 2)],
        [lambda: run_attend_both(1), lambda: run_hidden_both(2)],
    )
    slot([pair_grad_near(1, 1), pair_near(1, 2)], [lambda: run_project_back(1, 0)])
    slot([sum_near(1, b[0]), pair_grad_far(1, 1)], [lambda: run_attend_both(2)])
    slot([sum_far(1, b[0]), pair_grad_near(1, 2)], [lambda: run_project_back(1, 1)])
    slot([hand_one(1, 0), sum_near(1, b[1]), pair_grad_far(1, 2)])
    slot([sum_far(1, b[1]), rows_far(0, 0)], [lambda: run_project_back(1, 2)])
    slot([sum_near(1, b[2]), hand_one(1, 1), rows_near(0, 0)])
    slot([sum_far(1, b[2]), rows_far(0, 1)], [lambda: run_attend_back(0)])
    slot(
        [hand_one(1, 2), rows_near(0, 1), pair_grad_near(0, 0)],
        [lambda: run_hidden_back(0)],
    )
    slot([rows_far(0, 2), pair_grad_far(0, 0)], [lambda: run_attend_back(1)])
    slot(
        [rows_near(0, 2), pair_grad_near(0, 1)],
        [lambda: run_hidden_back(1), lambda: run_project_back(0, 0)],
    )
    last = micros - 1

    def run_branch_sums():
        run_sums(
            branch_sums,
            [[of("active", s), of("attended", s)] for s in both],
            [
                [of("upstream", 0, last) + [piece[0] for piece in a[last].row_pieces]],
                [of("upstream", 1)],
            ],
            False,
        )

    def run_expand_sums():
        run_sums(
            expand_sums,
            [[of("second", s)] for s in both],
            [[of("hidden", s)] for s in both],
            True,
        )

    def run_triple_sums():
        run_sums(
            triple_sums,
            [[of("first", s)] for s in both],
            [[of("stacked", s)] for s in both],
            True,
        )

    finals = SimpleNamespace()

    def run_final_branch():
        blocks = branch_out(
            order, flags[1], [(k.active, k.attended) for k in b], contract, packed
        )
        finals.keep = jnp.stack(blocks[0::2])
        finals.send = jnp.stack(blocks[1::2])

    def last_near(w, s):
        return w.send, lambda passed: fold_hops(w, passed, "tp", 1, (s,))

    def last_far(w, s):
        def go(passed):
            w.came = hop(passed, "tp", lanes // 2, (s,))
            return w.came

        return w.send, go

    slot([pair_grad_far(0, 1)], [run_branch_sums])
    slot(
        [wide_near(branch_sums)], [lambda: run_attend_back(2), lambda: run_project_back(0, 1)]
    )
    slot([], [lambda: run_fold(branch_sums)])
    cut = [0, 3 * hidden // 8, 7 * hidden // 8, hidden + across_units]
    slot(
        [wide_far(branch_sums, cut[0], cut[1]), pair_grad_both(0, 2)],
        [lambda: run_hidden_back(2)],
    )
    slot(
        [wide_far(branch_sums, cut[1], cut[2])],
        [lambda: run_project_back(0, 2), run_triple_sums],
    )
    outs = SimpleNamespace(
        keep=jnp.stack([k.blocks[0] for k in a]), send=jnp.stack([k.blocks[1] for k in a])
    )

    def side_of(mades):
        return sum(
            jnp.concatenate([k.side_first, k.side_second], axis=0) for k in mades
        )

    side = SimpleNamespace(all=jnp.where(first_section, side_of(a), side_of(b)))

    def side_ctx(passed):
        step = 1
        while step < spans:
            middle = passed.shape[1] // 2
            came = hop(passed[:, middle:], "ctx", step, both)
            passed = passed[:, :middle] + came
            step *= 2
        side.all = passed
        return came

    def side_near(passed):
        step = 1
        while 2 * step < lanes:
            came = hop(passed, "tp", step, both)
            passed = passed + came
            step *= 2
        side.all = passed
        return came

    def side_far(passed):
        came = hop(passed, "tp", lanes // 2, both)
        side.all = passed + came
        return came

    def held_back(w, j):
        def go(passed):
            w.parts[j] = passed
            return []

        return w.parts[j], go

    def wide_total(keep, parts):
        came = jnp.concatenate(parts, axis=0) if len(parts) > 1 else parts[0]
        return keep.astype(f32) + came.astype(f32)

    slot(
        [
            wide_near(triple_sums),
            wide_far(branch_sums, cut[2], cut[3]),
            (side.all, side_ctx),
        ],
        [run_expand_sums, run_final_branch],
    )
    slot([], [lambda: run_fold(triple_sums)])
    slot(
        [
            wide_far(triple_sums, 0, depth),
            wide_near(expand_sums),
            last_near(outs, 0),
            last_near(finals, 1),
            (side.all, side_near),
        ]
    )
    slot([], [lambda: run_fold(expand_sums)])
    slot(
        [
            wide_far(expand_sums, 0, depth),
            last_far(outs, 0),
            last_far(finals, 1),
            (side.all, side_far),
            held_back(triple_sums, 0),
        ]
    )
    triple_grads = wide_total(triple_sums.keep, triple_sums.parts)
    triple_grads = triple_grads.reshape(triple_weight.shape)
    branch_grads = wide_total(branch_sums.keep, branch_sums.parts)
    contract_grads, output_grads = branch_grads[:hidden], branch_grads[hidden:]
    expand_grads = wide_total(expand_sums.keep, expand_sums.parts)
    layer_outputs = jnp.stack(
        [
            jnp.where(
                first_section,
                kept[0][m].given,
                (
                    b[m].rows.astype(f32)
                    + finals.keep[m].astype(f32)
                    + finals.came[m].astype(f32)
                ).astype(bf16),
            )
            for m in range(micros)
        ]
    )
    own_rows = jnp.stack(of("rows", 0))
    entry_grads = jnp.where(
        first_section,
        norm_back(own_rows, outs.keep.astype(f32) + outs.came.astype(f32), inputs),
        jnp.stack(of("given", 1)),
    )
    gain_grads = jnp.stack([side.all[0], side.all[2]])
    bias_grads = jnp.stack([side.all[1], side.all[3]])
    return (
        xor_blocks(layer_outputs, span, spans, inverse=True)[None],
        xor_blocks(entry_grads, span, spans, inverse=True)[None],
        triple_grads,
        output_grads.reshape(output_weight.shape),
        expand_grads[None],
        contract_grads[None],
        gain_grads[None],
        bias_grads[None],
    )


def solution(mesh):
    return jax.shard_map(
        shards,
        mesh=mesh,
        in_specs=(
            P(None, ("ctx", "tp"), None),
            P(None, ("ctx", "tp"), None),
            P("pipe", "ctx", "tp", None, None),
            P("pipe", "tp", None, "ctx"),
            P("pipe", "ctx", "tp"),
            P("pipe", "tp", "ctx"),
            P("pipe", None, "ctx"),
            P("pipe", None, "ctx"),
        ),
        out_specs=(
            P("pipe", None, ("ctx", "tp"), None),
            P("pipe", None, ("ctx", "tp"), None),
            P("pipe", "ctx", "tp", None, None),
            P("pipe", "tp", None, "ctx"),
            P("pipe", "ctx", "tp"),
            P("pipe", "tp", "ctx"),
            P("pipe", None, "ctx"),
            P("pipe", None, "ctx"),
        ),
        check_vma=False,
    )
```
